32 devices in a mesh: dp: 16 (over z, y, core), tensor: 2 (over x).
Axes of the slice: x: 2, y: 2, z: 4, core: 2. Of those that a mesh axis runs over, the one named last changes fastest.
Arguments:
- tokens: bfloat16 [7584, 768], P('dp'), may hold values from -6 to 6
- caption_lengths: int32 [32], P('dp'), may hold values from 8 to 40, as said below
- gain_attn: bfloat16 [768], P('dp'), may hold values from 0.5 to 1.5
- w_query: bfloat16 [768, 768], P('dp', 'tensor'), may hold values from -0.21875 to 0.21875
- w_key: bfloat16 [768, 768], P('dp', 'tensor'), may hold values from -0.21875 to 0.21875
- w_value: bfloat16 [768, 768], P('dp', 'tensor'), may hold values from -0.21875 to 0.21875
- w_out: bfloat16 [768, 768], P('tensor', 'dp'), may hold values from -1.75 to 1.75
- gain_ffn: bfloat16 [768], P('dp'), may hold values from 0.5 to 1.5
- vis_in: bfloat16 [768, 3072], P('dp', 'tensor'), may hold values from -0.21875 to 0.21875
- vis_out: bfloat16 [3072, 768], P('tensor', 'dp'), may hold values from -0.109375 to 0.109375
- txt_in: bfloat16 [768, 3072], P('dp', 'tensor'), may hold values from -0.21875 to 0.21875
- txt_out: bfloat16 [3072, 768], P('tensor', 'dp'), may hold values from -0.109375 to 0.109375
- cotangent: bfloat16 [7584, 768], P('dp'), may hold values from -6 to 6
Outputs:
- out_tokens: bfloat16 [7584, 768], P('dp')
- grad_tokens: float32 [7584, 768], P('dp')
- grad_gain_attn: float32 [768], P('dp')
- grad_w_query: float32 [768, 768], P('dp', 'tensor')
- grad_w_key: float32 [768, 768], P('dp', 'tensor')
- grad_w_value: float32 [768, 768], P('dp', 'tensor')
- grad_w_out: float32 [768, 768], P('tensor', 'dp')
- grad_gain_ffn: float32 [768], P('dp')
- grad_vis_in: float32 [768, 3072], P('dp', 'tensor')
- grad_vis_out: float32 [3072, 768], P('tensor', 'dp')
- grad_txt_in: float32 [768, 3072], P('dp', 'tensor')
- grad_txt_out: float32 [3072, 768], P('tensor', 'dp')
The draws below stay inside these ranges and needn't reach their ends.
Inputs may be any that keep to these rules, and one draw needn't show every extreme that they name: `caption_lengths`: each pair's caption holds 8 to 40 tokens; in every draw some pair holds 40.
All inputs are finite; a program needn't handle non-finite values.
Results may differ from the reference program's by a relative error of at most 0.015.
Values may be sent and summed in bfloat16 or wider, within the bound.
A program may use at most 128 MiB of HBM per device.

```python
import jax
import jax.numpy as jnp
from jax import lax

D = 768
HEAD_DIM = 64
FF = 3072
PATCHES = 197
CAPTION = 40
PAIRS = 32
TOKENS = 7584


def draw_caption_lengths(key, part):
    key = jax.random.fold_in(key, 7)
    first, second = jax.random.split(key)
    lengths = jax.random.randint(first, (PAIRS,), 8, CAPTION + 1)
    chosen = jax.random.randint(second, (), 0, PAIRS)
    return lengths.at[chosen].set(CAPTION).astype(jnp.int32)


def strengthened(array, stream_key, source, target, blocks, factor):
    owner, partner = [(jnp.arange(array.shape[dim]) // (array.shape[dim] // blocks)).reshape([-1 if axis == dim else 1 for axis in range(array.ndim)]) for dim in (source, target)]
    chosen = jax.random.permutation(stream_key, blocks)[partner]
    strong = (owner == chosen) | (owner == (partner + blocks // 2) % blocks)
    return jnp.where(strong, factor * array, array)


def block_scale(rng, extent, cuts, least, top_value):
    factor_of, own = 1.0, jax.random.fold_in(rng, 6)
    for dim, blocks in cuts:
        draws = jnp.exp(jax.random.uniform(jax.random.fold_in(own, dim), (blocks,), jnp.float32, least / len(cuts), top_value / len(cuts)))
        factor_of = factor_of * jnp.repeat(draws, extent[dim] // blocks).reshape([-1 if axis == dim else 1 for axis in range(len(extent))])
    return factor_of


def bell_draw(own_key, dims, scale, limit, cuts=(), kind=jnp.bfloat16):
    entries = scale * jax.random.normal(own_key, dims, jnp.float32)
    if cuts:
        entries = entries * block_scale(own_key, dims, cuts, -0.22, 0.18)
    return jnp.clip(entries, -limit, limit).astype(kind)


def noise_with(own_key, shape, scale, most, cuts, heavy, kind=jnp.bfloat16):
    array = scale * jax.random.normal(own_key, shape, jnp.float32)
    if cuts:
        array = array * block_scale(own_key, shape, cuts, -0.22, 0.18)
    return jnp.clip(strengthened(array, jax.random.fold_in(own_key, 3), *heavy), -most, most).astype(kind)


def setup_inputs(seed: int = 0) -> dict:
    key_of = jax.random.split(jax.random.key(seed), 14)
    return {
        "tokens": bell_draw(key_of[0], (TOKENS, D), 1.0, 6.0, ((0, 16),)),
        "caption_lengths": draw_caption_lengths(jax.random.fold_in(key_of[13], 71), 0),
        "gain_attn": jnp.clip(1.0 + 0.1 * jax.random.normal(key_of[2], (D,), jnp.float32), 0.5, 1.5).astype(jnp.bfloat16),
        "w_query": bell_draw(key_of[3], (D, D), D ** -0.5, 0.21875, ((0, 16), (1, 2))),
        "w_key": bell_draw(key_of[4], (D, D), D ** -0.5, 0.21875, ((0, 16), (1, 2))),
        "w_value": bell_draw(key_of[5], (D, D), D ** -0.5, 0.21875, ((0, 16), (1, 2))),
        "w_out": bell_draw(key_of[6], (D, D), (D // 64) ** -0.5, 1.75, ((0, 2), (1, 16))),
        "gain_ffn": jnp.clip(1.0 + 0.1 * jax.random.normal(key_of[7], (D,), jnp.float32), 0.5, 1.5).astype(jnp.bfloat16),
        "vis_in": bell_draw(key_of[8], (D, FF), D ** -0.5, 0.21875, ((0, 16), (1, 2))),
        "vis_out": bell_draw(key_of[9], (FF, D), FF ** -0.5, 0.109375, ((0, 2), (1, 16))),
        "txt_in": bell_draw(key_of[10], (D, FF), D ** -0.5, 0.21875, ((0, 16), (1, 2))),
        "txt_out": bell_draw(key_of[11], (FF, D), FF ** -0.5, 0.109375, ((0, 2), (1, 16))),
        "cotangent": noise_with(key_of[12], (TOKENS, D), 1.0, 6.0, ((0, 16),), (0, 1, 16, 2.0)),
    }


@jax.custom_vjp
def low(v):
    return lax.optimization_barrier(v.astype(jnp.bfloat16)).astype(jnp.float32)

@jax.custom_vjp
def low_back(v):
    return v

def low_keep(v):
    return (low(v), None)

def low_pass(kept, grad):
    return (grad,)

def back_keep(v):
    return (v, None)

def back_low(kept, grad):
    return (low(grad),)
low.defvjp(low_keep, low_pass)
low_back.defvjp(back_keep, back_low)
epsilon = 1e-05
highest = lax.Precision.HIGHEST

def layer_norm(values, gain):
    center = values - lax.optimization_barrier(jnp.mean(values, axis=-1, keepdims=True))
    spread = lax.optimization_barrier(jnp.mean(center * center, axis=-1, keepdims=True))
    return center * lax.rsqrt(spread + epsilon) * gain

def expert(rows, weight_in, weight_out):
    hidden_pre = low_back(jnp.einsum('gsd,df->gsf', rows, weight_in, precision=highest))
    hidden = low(jax.nn.gelu(hidden_pre, approximate=False))
    return jnp.einsum('gsf,fd->gsd', hidden, weight_out, precision=highest)

def forward(inputs, valid_rows, params):
    gain_one, query_w, key_w, value_w, out_w, gain_two, vis_in_w, vis_out_w, txt_in_w, txt_out_w = params
    group_pairs, seq_len, width = inputs.shape
    head_count = width // HEAD_DIM
    normed = low(layer_norm(inputs, gain_one))

    def project(weight):
        result = low(low_back(jnp.einsum('gsd,de->gse', normed, weight, precision=highest)))
        return result.reshape(group_pairs, seq_len, head_count, HEAD_DIM)
    queries = project(query_w)
    keys_all = project(key_w)
    values_all = project(value_w)
    scores = low_back(jnp.einsum('gqhe,gkhe->ghqk', queries, keys_all, precision=highest) * HEAD_DIM ** (-0.5))
    key_live = valid_rows[:, None, None, :] > 0.5
    scores = jnp.where(key_live, scores, -1e+30)
    shifted = scores - lax.optimization_barrier(jnp.max(scores, axis=-1, keepdims=True))
    weights = jnp.exp(shifted)
    probs = low(weights / lax.optimization_barrier(jnp.sum(weights, axis=-1, keepdims=True)))
    context = low(low_back(jnp.einsum('ghqk,gkhe->gqhe', probs, values_all, precision=highest)))
    context = context.reshape(group_pairs, seq_len, width)
    attended = low_back(jnp.einsum('gsd,de->gse', context, out_w, precision=highest))
    mask_col = valid_rows[..., None]
    middle = inputs + mask_col * attended
    second = low(layer_norm(middle, gain_two))
    image_out = expert(second[:, :PATCHES], vis_in_w, vis_out_w)
    text_out = expert(second[:, PATCHES:], txt_in_w, txt_out_w)
    branch = low_back(jnp.concatenate([image_out, text_out], axis=1))
    return middle + mask_col * branch

def reference(tokens, caption_lengths, gain_attn, w_query, w_key, w_value, w_out, gain_ffn, vis_in, vis_out, txt_in, txt_out, cotangent):
    seq_len = PATCHES + CAPTION
    group_pairs = 16
    group_count = PAIRS // group_pairs
    params = tuple((weight.astype(jnp.float32) for weight in (gain_attn, w_query, w_key, w_value, w_out, gain_ffn, vis_in, vis_out, txt_in, txt_out)))
    position = jnp.arange(seq_len, dtype=jnp.int32)
    live = (position[None, :] < PATCHES) | (position[None, :] - PATCHES < caption_lengths.astype(jnp.int32)[:, None])
    valid_all = live.astype(jnp.float32).reshape(group_count, group_pairs, seq_len)
    inputs = tokens.astype(jnp.float32).reshape(group_count, group_pairs, seq_len, D)
    upstream = cotangent.astype(jnp.float32).reshape(group_count, group_pairs, seq_len, D)
    zeros = tuple((jnp.zeros_like(weight) for weight in params))

    def step(totals, block):
        block_in, block_valid, block_up = block

        def run(values, weights):
            return forward(values, block_valid, weights)
        output, pullback = jax.vjp(run, block_in, params)
        grad_in, grad_params = pullback(block_up)
        totals = tuple((before + added for before, added in zip(totals, grad_params)))
        return (totals, (output.astype(jnp.bfloat16), grad_in))
    totals, outcome = lax.scan(step, zeros, (inputs, valid_all, upstream))
    outputs, grad_inputs = outcome
    return (outputs.reshape(TOKENS, D), grad_inputs.reshape(TOKENS, D), totals[0], totals[1], totals[2], totals[3], totals[4], totals[5], totals[6], totals[7], totals[8], totals[9])
```

```python
import functools
import math

import jax
import jax.numpy as jnp
from jax import lax
from jax.experimental import pallas as pl
from jax.experimental.pallas import tpu as pltpu
from jax.sharding import PartitionSpec as P

HEAD_DIM = 64
PATCHES = 197
CAPTION = 40
VIS = 208
TXT = 48
SEQ = VIS + TXT

MESH = pl.DeviceIdType.MESH
BF = jnp.bfloat16
F32 = jnp.float32

ATT, TIN, TOUT, VIN, VOUT = range(5)

epsilon = 1e-05
inv_root_two = 1.0 / math.sqrt(2.0)
inv_root_tau = 1.0 / math.sqrt(2.0 * math.pi)


def mm(left, right):
    return jnp.dot(left, right, preferred_element_type=F32)


def mm_nt(left, right):
    return lax.dot_general(left, right, (((1,), (1,)), ((), ())), preferred_element_type=F32)


def mm_tn(left, right):
    return lax.dot_general(left, right, (((0,), (0,)), ((), ())), preferred_element_type=F32)


def normalize(values):
    center = values - jnp.mean(values, axis=-1, keepdims=True)
    spread = jnp.mean(center * center, axis=-1, keepdims=True)
    inverse = lax.rsqrt(spread + epsilon)
    return center * inverse, inverse


def normalize_back(grad_normed, normed, inverse):
    return inverse * (
        grad_normed
        - jnp.mean(grad_normed, axis=-1, keepdims=True)
        - normed * jnp.mean(grad_normed * normed, axis=-1, keepdims=True)
    )


class Events:
    def __init__(self):
        self.todo = []

    def add(self, *steps):
        self.todo.extend(steps)

    def advance(self, count):
        for _ in range(min(count, len(self.todo))):
            self.todo.pop(0)()

    def drain(self):
        self.advance(len(self.todo))


def layer_kernel(n, names, *refs):
    R = dict(zip(names, refs))
    for later, earlier in (
        ("pb", "pa"), ("pf", "pg"), ("ga", "x4"), ("rf", "ra"), ("rb", "rg"), ("n2", "n1"),
    ):
        R[later] = R[earlier]
    S, X, DY, MASK, BIAS = (R[k] for k in ("shard", "x", "dy", "mask", "bias"))
    OUT, GTOK, GW, GG = (R[k] for k in ("out", "gtok", "gw", "gg"))
    G, PART, LAND = R["gathered"], R["part"], R["land"]
    width = G.shape[2]
    own = width // (2 * n)

    x = lax.axis_index("tensor")
    d = lax.axis_index("dp")
    c = lax.rem(d, 2)
    other = 1 - c
    chip = d // 2
    y, z = lax.rem(chip, 2), chip // 2
    r = z + y * (n - 1 - 2 * z)
    half = n // 2

    def chip_at(pos):
        pos = lax.rem(pos + 2 * n, n)
        upper = pos // half
        return 2 * (pos + upper * (n - 1 - 2 * pos)) + upper

    mate = {"dp": d + 1 - 2 * c}
    across = {"tensor": 1 - x}
    ahead = {"dp": 2 * chip_at(r + 1) + c}
    behind = {"dp": 2 * chip_at(r - 1) + c}
    way = (ahead, behind)

    def rows_at(pos, side):
        return pl.ds(pl.multiple_of(2 * own * chip_at(pos) + own * side, 16), own)

    my_rows = pl.ds(pl.multiple_of(own * d, 16), own)

    barrier = pltpu.get_barrier_semaphore()
    for device in (mate, across, ahead, behind):
        pl.semaphore_signal(barrier, inc=1, device_id=device, device_id_type=MESH)

    mine, theirs = pl.multiple_of(2 * c, 2), pl.multiple_of(2 * other, 2)
    pair_own = 2 * c + x
    pair_across = 2 * c + 1 - x

    started = []
    counter = [0]

    def remote(source, target, device, index=None):
        if index is None:
            index = counter[0]
            counter[0] += 1
        return pltpu.make_async_remote_copy(
            src_ref=source,
            dst_ref=target,
            send_sem=R["sent"].at[index],
            recv_sem=R["came"].at[index],
            device_id=device,
            device_id_type=MESH,
        )

    def start(source, target, device):
        copy = remote(source, target, device)
        copy.start()
        started.append(copy)
        return copy

    for k in range(5):
        G[k, my_rows, :] = S[k, c]
    for t in range(2):
        R["x4"][2 * c + t] = X[t]
        R["bias4"][2 * c + t] = BIAS[t]

        @pl.loop(0, SEQ // 64)
        def _(i, t=t):
            rows = pl.ds(pl.multiple_of(i * 64, 64), 64)
            live = MASK[t, rows, :][:, :1]
            R["gz"][2 * c + t, rows, :] = (DY[t, rows, :].astype(F32) * live).astype(BF)

    pl.semaphore_wait(barrier, 4)
    shard_a = start(S.at[pl.ds(0, 1), other], G.at[pl.ds(0, 1), my_rows, :], mate)
    send_x = start(X, R["x4"].at[pl.ds(mine, 2)], mate)
    shard_b = start(S.at[pl.ds(1, 4), other], G.at[pl.ds(1, 4), my_rows, :], mate)
    send_bias = start(BIAS, R["bias4"].at[pl.ds(mine, 2)], mate)
    send_gz = start(R["gz"].at[pl.ds(mine, 2)], R["gz"].at[pl.ds(mine, 2)], mate)

    def gather_index(k, side, s):
        return (k * 2 + side) * (n - 1) + s

    def gather_copy(k, side, s):
        pos = r - s if side == 0 else r + s
        block = G.at[k, rows_at(pos, side), :]
        i = gather_index(k, side, s)
        return pltpu.make_async_remote_copy(
            src_ref=block,
            dst_ref=block,
            send_sem=R["ring_sent"].at[i],
            recv_sem=R["ring_came"].at[i],
            device_id=way[side],
            device_id_type=MESH,
        )

    def gather_came(k, side, s):
        pos = r - 1 - s if side == 0 else r + 1 + s
        block = G.at[k, rows_at(pos, side), :]
        i = gather_index(k, side, s)
        pltpu.make_async_remote_copy(
            src_ref=block,
            dst_ref=block,
            send_sem=R["ring_sent"].at[i],
            recv_sem=R["ring_came"].at[i],
            device_id=way[side],
            device_id_type=MESH,
        ).wait_recv()

    def gather_step(k, s):
        for side in range(2):
            if not (isinstance(s, int) and s == 0):
                gather_came(k, side, s - 1)
            if not (isinstance(s, int) and s == n - 1):
                gather_copy(k, side, s).start()

    sum_base = 5 * 2 * (n - 1)

    def sum_copy(k, side, s, source):
        i = sum_base + gather_index(k, side, s)
        return pltpu.make_async_remote_copy(
            src_ref=source,
            dst_ref=LAND.at[k, side, s],
            send_sem=R["ring_sent"].at[i],
            recv_sem=R["ring_came"].at[i],
            device_id=way[side],
            device_id_type=MESH,
        )

    def sum_step(k, s):
        for side in range(2):
            pos = r - 1 - s if side == 0 else r + 1 + s
            if isinstance(s, int) and s == 0:
                source = PART.at[k, rows_at(pos, side), :]
            else:
                source = LAND.at[k, side, s - 1]
                sum_copy(k, side, s - 1, source).wait_recv()
                LAND[k, side, s - 1] = (
                    LAND[k, side, s - 1].astype(F32) + PART[k, rows_at(pos, side), :].astype(F32)
                ).astype(BF)
            sum_copy(k, side, s, source).start()

    finals = []

    def sum_last(k):
        for side in range(2):
            sum_copy(k, side, n - 2, LAND.at[k, side, n - 2]).wait_recv()

        def total(core):
            rows = pl.ds(pl.multiple_of(2 * own * chip + own * core, 16), own)
            return LAND[k, core, n - 2].astype(F32) + PART[k, rows, :].astype(F32)

        R["give"][k] = total(other)
        finals.append(start(R["give"].at[k], GW.at[k, c], mate))
        GW[k, c] = total(c)

    shard_a.wait_recv()
    gather_step(ATT, 0)
    shard_b.wait_recv()
    gather_step(TIN, 0)
    send_x.wait_recv()

    ring = Events()
    for s in range(1, n - 1):
        ring.add(functools.partial(gather_step, ATT, s), functools.partial(gather_step, TIN, s))

    for i in range(4):

        @pl.loop(0, SEQ // 64)
        def _(j, i=i):
            rows = pl.ds(pl.multiple_of(j * 64, 64), 64)
            normed, _ = normalize(R["x4"][i, rows, :].astype(F32))
            R["n1"][i, rows, :] = normed.astype(BF)

        R["n1t"][:, i * SEQ : (i + 1) * SEQ] = R["n1"][i].T
        ring.advance(1)
    send_gz.wait_recv()
    send_bias.wait_recv()
    ring.advance(1)

    @pl.loop(0, width // 256)
    def _(j):
        cols = pl.ds(pl.multiple_of(j * 256, 256), 256)
        R["gzvt"][cols, :] = R["gz"][:, :VIS, cols].reshape(4 * VIS, 256).T
        R["gztt"][cols, :] = R["gz"][:, VIS:, cols].reshape(4 * TXT, 256).T

    ring.drain()
    gather_step(ATT, n - 1)
    gather_step(TIN, n - 1)
    for k in (TOUT, VIN, VOUT):
        gather_step(k, 0)

    heads = width // HEAD_DIM // 4
    span = heads * HEAD_DIM
    R["wo"][...] = G[ATT][:, 3 * span :]

    @pl.loop(0, 4)
    def _(i):
        projected = mm(R["n1"][i], G[ATT][:, : 3 * span]).astype(BF)
        R["q"][i] = projected[:, :span]
        R["k"][i] = projected[:, span : 2 * span]
        R["v"][i] = projected[:, 2 * span :]

    lane = lax.broadcasted_iota(jnp.int32, (1, span), 1) // HEAD_DIM

    def only(head, values):
        return values * (lane == head).astype(F32).astype(BF)

    for k in (TOUT, VIN, VOUT):
        gather_step(k, 1)

    base = counter[0]
    counter[0] += 2

    def pair_order(j):
        core = other + (j // 2) * (c - other)
        turn = (1 - x) + lax.rem(j, 2) * (2 * x - 1)
        return core, turn, 2 * core + turn

    def forward_copy(j, turn, i):
        return remote(R["pa"].at[i], R["ra"].at[turn], mate, base + j)

    cross_a = remote(R["xs"], R["xr"], across)

    @pl.loop(0, 4)
    def _(j):
        core, turn, i = pair_order(j)
        q, k, v = R["q"][i], R["k"][i], R["v"][i]
        context = jnp.zeros((SEQ, span), F32)
        for h in range(heads):
            scores = mm_nt(q, only(h, k)) + R["bias4"][i][:1, :]
            top = jnp.max(scores, axis=-1, keepdims=True)
            weights = jnp.exp(scores - top)
            total = jnp.sum(weights, axis=-1, keepdims=True)
            probs = (weights * (1.0 / total)).astype(BF)
            R["probs"][i * heads + h] = probs
            context += mm(probs, only(h, v))
        context = context.astype(BF)
        R["c"][i] = context
        R["pa"][i] = mm_nt(context, R["wo"][...]).astype(BF)

        @pl.when(j < 2)
        def _():
            forward_copy(j, turn, i).start()

        @pl.when(j == 2)
        def _():
            forward_copy(0, 1 - x, pair_across).wait_recv()
            R["xs"][...] = (
                R["pa"][pair_across].astype(F32) + R["ra"][1 - x].astype(F32)
            ).astype(BF)
            cross_a.start()

        for k in (TOUT, VIN, VOUT):
            gather_step(k, 2 + j)

    started.append(cross_a)
    for j in range(2):
        core, turn, i = pair_order(j)
        forward_copy(j, turn, i).wait_send()
    forward_copy(1, x, pair_own).wait_recv()
    for k in (TOUT, VIN, VOUT):
        gather_step(k, n - 2)
    cross_a.wait_recv()

    @pl.loop(0, SEQ // 64)
    def _(j):
        rows = pl.ds(pl.multiple_of(j * 64, 64), 64)
        attended = (
            R["pa"][pair_own, rows, :].astype(F32)
            + R["ra"][x, rows, :].astype(F32)
            + R["xr"][rows, :].astype(F32)
        )
        live = MASK[x, rows, :][:, :1]
        middle = X[x, rows, :].astype(F32) + live * attended
        R["y1"][rows, :] = middle
        normed, _ = normalize(middle)
        R["n2"][pair_own, rows, :] = normed.astype(BF)

    def spread(name):
        block = R[name].at[pair_own]
        to_across = start(block, block, across)
        to_mate = start(block, block, mate)
        return to_across, to_mate

    to_across, to_mate = spread("n2")
    to_across.wait_recv()
    block = R["n2"].at[pair_across]
    passed = start(block, block, mate)
    to_mate.wait_recv()
    passed.wait_recv()

    for k in (TOUT, VIN, VOUT):
        gather_step(k, n - 1)

    def expert(low, high, w_in, w_out, h_ref, gu_ref, after):
        per = high - low
        total_rows = 4 * per
        step = 64

        def run(j):
            cols = pl.ds(pl.multiple_of(j * 256, 256), 256)
            R["u"][:total_rows, :] = mm(
                R["n2"][:, low:high, :].reshape(total_rows, width), G[w_in, :, cols]
            )
            R["gh"][:total_rows, :] = mm(
                R["gz"][:, low:high, :].reshape(total_rows, width), G[w_out, :, cols]
            )

            @pl.loop(0, total_rows // step)
            def _(i):
                rows = pl.ds(pl.multiple_of(i * step, step), step)
                pre = R["u"][rows, :]
                cumulative = 0.5 * (1.0 + lax.erf(pre * inv_root_two))
                density = jnp.exp(-0.5 * pre * pre) * inv_root_tau
                h_ref[rows, cols] = (pre * cumulative).astype(BF)
                gu_ref[rows, cols] = (R["gh"][rows, :] * (cumulative + pre * density)).astype(BF)

            after(j)

        pl.loop(0, width // 256)(run)

    def weight_grad(k, turned, ref):
        @pl.loop(0, width // 256)
        def _(j):
            cols = pl.ds(pl.multiple_of(j * 256, 256), 256)
            PART[k, :, cols] = mm(turned, ref[:, cols]).astype(BF)

    expert(VIS, SEQ, TIN, TOUT, R["ht"], R["gut"], lambda j: None)
    weight_grad(TOUT, R["gztt"][...], R["ht"])
    sum_step(TOUT, 0)

    @pl.loop(0, width // 256)
    def _(j):
        cols = pl.ds(pl.multiple_of(j * 256, 256), 256)
        R["n2vt"][cols, :] = R["n2"][:, :VIS, cols].reshape(4 * VIS, 256).T
        R["n2tt"][cols, :] = R["n2"][:, VIS:, cols].reshape(4 * TXT, 256).T

    weight_grad(TIN, R["n2tt"][...], R["gut"])
    sum_step(TIN, 0)

    def vis_after(j):
        sum_step(TOUT, 1 + j)
        sum_step(TIN, 1 + j)

    expert(0, VIS, VIN, VOUT, R["hv"], R["guv"], vis_after)

    def terms(target, hv, ht, w_vis, w_txt, first):
        vis_rows = pl.ds(pl.multiple_of(first * VIS, 16), 2 * VIS)
        txt_rows = pl.ds(pl.multiple_of(first * TXT, 16), 2 * TXT)
        vis_part = mm_nt(hv[vis_rows, :], G[w_vis]).astype(BF)
        target[pl.ds(first, 2), :VIS, :] = vis_part.reshape(2, VIS, width)
        txt_part = mm_nt(ht[txt_rows, :], G[w_txt]).astype(BF)
        target[pl.ds(first, 2), VIS:, :] = txt_part.reshape(2, TXT, width)

    terms(R["pg"], R["guv"], R["gut"], VIN, TIN, theirs)
    mate_g = start(R["pg"].at[pl.ds(theirs, 2)], R["rg"], mate)
    sum_step(TOUT, 4)
    sum_step(TIN, 4)
    terms(R["pg"], R["guv"], R["gut"], VIN, TIN, mine)
    mate_g.wait_recv()
    R["xsg"][...] = (R["pg"][pair_across].astype(F32) + R["rg"][1 - x].astype(F32)).astype(BF)
    cross_g = start(R["xsg"], R["xrg"], across)
    sum_step(TOUT, 5)
    sum_step(TIN, 5)
    weight_grad(VOUT, R["gzvt"][...], R["hv"])
    sum_step(VOUT, 0)
    sum_step(TOUT, 6)
    sum_step(TIN, 6)
    weight_grad(VIN, R["n2vt"][...], R["guv"])
    sum_step(VIN, 0)
    cross_g.wait_recv()

    @pl.loop(0, SEQ // 64)
    def _(j):
        rows = pl.ds(pl.multiple_of(j * 64, 64), 64)
        grad_normed = (
            R["pg"][pair_own, rows, :].astype(F32)
            + R["rg"][x, rows, :].astype(F32)
            + R["xrg"][rows, :].astype(F32)
        )
        normed, inverse = normalize(R["y1"][rows, :])
        grad = DY[x, rows, :].astype(F32) + normalize_back(grad_normed, normed, inverse)
        R["gy"][x, rows, :] = grad.astype(BF)
        live = MASK[x, rows, :][:, :1]
        R["ga"][pair_own, rows, :] = (grad * live).astype(BF)

    gy_across = start(R["gy"].at[x], R["gy"].at[x], across)
    gy_mate = start(R["ga"].at[pair_own], R["ga"].at[pair_own], mate)
    sum_last(TOUT)
    sum_last(TIN)
    sum_step(VOUT, 1)
    sum_step(VIN, 1)

    mate_g.wait_send()
    started[:] = [copy for copy in started if copy is not mate_g]
    terms(R["pf"], R["hv"], R["ht"], VOUT, TOUT, theirs)
    mate_f = start(R["pf"].at[pl.ds(theirs, 2)], R["rf"], mate)
    sum_step(VOUT, 2)
    sum_step(VIN, 2)
    gy_across.wait_recv()

    @pl.loop(0, SEQ // 64)
    def _(j):
        rows = pl.ds(pl.multiple_of(j * 64, 64), 64)
        live = MASK[1 - x, rows, :][:, :1]
        R["ga"][pair_across, rows, :] = (R["gy"][1 - x, rows, :].astype(F32) * live).astype(BF)

    block = R["ga"].at[pair_across]
    gy_passed = start(block, block, mate)
    terms(R["pf"], R["hv"], R["ht"], VOUT, TOUT, mine)
    mate_f.wait_recv()
    R["xsf"][...] = (R["pf"][pair_across].astype(F32) + R["rf"][1 - x].astype(F32)).astype(BF)
    cross_f = start(R["xsf"], R["xrf"], across)
    gy_mate.wait_recv()
    gy_passed.wait_recv()

    base_back = counter[0]
    counter[0] += 2

    def back_copy(j, turn, i):
        return remote(R["pb"].at[i], R["rb"].at[turn], mate, base_back + j)

    base_cross = counter[0]
    counter[0] += 2

    def back_cross(j, turn):
        return remote(R["xsb"].at[turn], R["xrb"].at[turn], across, base_cross + j)

    @pl.loop(0, 4)
    def _(j):
        core, turn, i = pair_order(j)
        grad_context = mm(R["ga"][i], R["wo"][...]).astype(BF)
        R["gat"][:, pl.ds(pl.multiple_of(i * SEQ, SEQ), SEQ)] = R["ga"][i].T
        q, k, v = R["q"][i], R["k"][i], R["v"][i]
        grad_q = jnp.zeros((SEQ, span), F32)
        grad_k = jnp.zeros((SEQ, span), F32)
        grad_v = jnp.zeros((SEQ, span), F32)
        for h in range(heads):
            probs = R["probs"][i * heads + h]
            grad_probs = mm_nt(grad_context, only(h, v))
            exact = probs.astype(F32)
            inner = jnp.sum(grad_probs * exact, axis=-1, keepdims=True)
            grad_scores = (exact * (grad_probs - inner)).astype(BF)
            grad_q += mm(grad_scores, only(h, k))
            grad_k += mm_tn(grad_scores, only(h, q))
            grad_v += mm_tn(probs, only(h, grad_context))
        joined = jnp.concatenate([grad_q, grad_k, grad_v], axis=1).astype(BF)
        R["gqkv"][i] = joined
        R["pb"][i] = mm_nt(joined, G[ATT][:, : 3 * span]).astype(BF)

        @pl.when(j < 2)
        def _():
            back_copy(j, turn, i).start()

        @pl.when(j >= 2)
        def _():
            back_copy(j - 2, turn, i).wait_recv()
            R["xsb"][turn] = (
                R["pb"][i].astype(F32) + R["rb"][turn].astype(F32)
            ).astype(BF)
            back_cross(j - 2, turn).start()

        sum_step(VOUT, 3 + j)
        sum_step(VIN, 3 + j)

    for j in range(2):
        core, turn, i = pair_order(j)
        started.append(back_copy(j, turn, i))
        started.append(back_cross(j, turn))

    @pl.loop(0, 3)
    def _(j):
        cols = pl.ds(pl.multiple_of(j * 256, 256), 256)
        rows = pl.ds(pl.multiple_of(j * 256, 256), 256)
        grads = mm(R["n1t"][rows, :], R["gqkv"][...].reshape(4 * SEQ, 3 * span))
        grad_o = mm(R["gat"][rows, :], R["c"][...].reshape(4 * SEQ, span))
        PART[ATT, rows, :] = jnp.concatenate([grads, grad_o], axis=1).astype(BF)

    sum_step(ATT, 0)
    sum_last(VOUT)
    sum_last(VIN)

    cross_f.wait_recv()

    @pl.loop(0, SEQ // 64)
    def _(j):
        rows = pl.ds(pl.multiple_of(j * 64, 64), 64)
        branch = (
            R["pf"][pair_own, rows, :].astype(F32)
            + R["rf"][x, rows, :].astype(F32)
            + R["xrf"][rows, :].astype(F32)
        )
        live = MASK[x, rows, :][:, :1]
        OUT[x, rows, :] = (R["y1"][rows, :] + live * branch).astype(BF)

    out_across = start(OUT.at[x], OUT.at[x], across)
    for s in range(1, 3):
        sum_step(ATT, s)

    for j in range(2):
        back_cross(j, x if j == 0 else 1 - x).wait_recv()
    for t in range(2):

        @pl.loop(0, SEQ // 64)
        def _(j, t=t):
            rows = pl.ds(pl.multiple_of(j * 64, 64), 64)
            grad_normed = R["xsb"][t, rows, :].astype(F32) + R["xrb"][t, rows, :].astype(F32)
            normed, inverse = normalize(X[t, rows, :].astype(F32))
            GTOK[t, rows, :] = R["gy"][t, rows, :].astype(F32) + normalize_back(
                grad_normed, normed, inverse
            )

        sum_step(ATT, 3 + 2 * t)
        sum_step(ATT, 4 + 2 * t)
    sum_last(ATT)
    for copy in finals:
        copy.wait_recv()

    def row_sums(k, last):
        return sum(
            jnp.sum(
                S[k, core][:, :last].astype(F32) * GW[k, core][:, :last], axis=-1, keepdims=True
            )
            for core in range(2)
        )

    R["gs"][0] = jnp.broadcast_to(row_sums(ATT, 3 * span), (own, 128))
    R["gs"][1] = jnp.broadcast_to(row_sums(TIN, width) + row_sums(VIN, width), (own, 128))
    cross_gain = start(R["gs"], R["gr"], across)
    cross_gain.wait_recv()
    GG[...] = R["gs"][...] + R["gr"][...]
    out_across.wait_recv()

    for copy in started:
        copy.wait_send()
    for k in range(5):
        for side in range(2):
            for s in range(n - 1):
                gather_copy(k, side, s).wait_send()
                source = (
                    PART.at[k, rows_at(r, side), :] if s == 0 else LAND.at[k, side, s - 1]
                )
                sum_copy(k, side, s, source).wait_send()


def fused_layer(
    tokens,
    caption_lengths,
    gain_attn,
    w_query,
    w_key,
    w_value,
    w_out,
    gain_ffn,
    vis_in,
    vis_out,
    txt_in,
    txt_out,
    cotangent,
):
    n = lax.axis_size("dp") // 2
    own, columns = w_query.shape
    width = tokens.shape[1]
    heads = width // HEAD_DIM // 4
    span = heads * HEAD_DIM
    gain_one = gain_attn.astype(F32)[:, None]
    gain_two = gain_ffn.astype(F32)[:, None]

    def scaled(weight, gain):
        return (weight.astype(F32) * gain).astype(BF)

    def by_core(weight):
        return weight.reshape(own, 2, -1).transpose(1, 0, 2)

    shard = jnp.stack(
        [
            jnp.concatenate(
                [
                    by_core(scaled(w_query, gain_one * HEAD_DIM**-0.5)),
                    by_core(scaled(w_key, gain_one)),
                    by_core(scaled(w_value, gain_one)),
                    by_core(w_out.T),
                ],
                axis=2,
            ),
            by_core(scaled(txt_in, gain_two)),
            by_core(txt_out.T),
            by_core(scaled(vis_in, gain_two)),
            by_core(vis_out.T),
        ]
    )

    def padded(values):
        values = values.reshape(2, PATCHES + CAPTION, width)
        return jnp.concatenate(
            [
                jnp.pad(values[:, :PATCHES], ((0, 0), (0, VIS - PATCHES), (0, 0))),
                jnp.pad(values[:, PATCHES:], ((0, 0), (0, TXT - CAPTION), (0, 0))),
            ],
            axis=1,
        )

    def trimmed(values):
        return jnp.concatenate(
            [values[:, :PATCHES], values[:, VIS : VIS + CAPTION]], axis=1
        ).reshape(-1, width)

    slot = jnp.arange(SEQ, dtype=jnp.int32)[None, :]
    live = (slot < PATCHES) | ((slot >= VIS) & (slot - VIS < caption_lengths[:, None]))
    bias = jnp.broadcast_to(jnp.where(live, 0.0, -1e30).astype(F32)[:, None, :], (2, 8, SEQ))
    mask = jnp.broadcast_to(live.astype(F32)[:, :, None], (2, SEQ, 128))

    rows = 4 * SEQ
    scratch = {
        "gathered": pltpu.VMEM((5, width, width), BF),
        "part": pltpu.VMEM((5, width, width), BF),
        "land": pltpu.VMEM((5, 2, n - 1, own, width), BF),
        "give": pltpu.VMEM((5, own, width), F32),
        "x4": pltpu.VMEM((4, SEQ, width), BF),
        "bias4": pltpu.VMEM((4, 8, SEQ), F32),
        "n1": pltpu.VMEM((4, SEQ, width), BF),
        "n1t": pltpu.VMEM((width, rows), BF),
        "gz": pltpu.VMEM((4, SEQ, width), BF),
        "gzvt": pltpu.VMEM((width, 4 * VIS), BF),
        "gztt": pltpu.VMEM((width, 4 * TXT), BF),
        "wo": pltpu.VMEM((width, span), BF),
        "q": pltpu.VMEM((4, SEQ, span), BF),
        "k": pltpu.VMEM((4, SEQ, span), BF),
        "v": pltpu.VMEM((4, SEQ, span), BF),
        "c": pltpu.VMEM((4, SEQ, span), BF),
        "probs": pltpu.VMEM((4 * heads, SEQ, SEQ), BF),
        "pa": pltpu.VMEM((4, SEQ, width), BF),
        "ra": pltpu.VMEM((2, SEQ, width), BF),
        "xs": pltpu.VMEM((SEQ, width), BF),
        "xr": pltpu.VMEM((SEQ, width), BF),
        "y1": pltpu.VMEM((SEQ, width), F32),
        "n2vt": pltpu.VMEM((width, 4 * VIS), BF),
        "n2tt": pltpu.VMEM((width, 4 * TXT), BF),
        "u": pltpu.VMEM((4 * VIS, 256), F32),
        "gh": pltpu.VMEM((4 * VIS, 256), F32),
        "hv": pltpu.VMEM((4 * VIS, width), BF),
        "guv": pltpu.VMEM((4 * VIS, width), BF),
        "ht": pltpu.VMEM((4 * TXT, width), BF),
        "gut": pltpu.VMEM((4 * TXT, width), BF),
        "pg": pltpu.VMEM((4, SEQ, width), BF),
        "rg": pltpu.VMEM((2, SEQ, width), BF),
        "xsg": pltpu.VMEM((SEQ, width), BF),
        "xrg": pltpu.VMEM((SEQ, width), BF),
        "gy": pltpu.VMEM((2, SEQ, width), BF),
        "gat": pltpu.VMEM((width, rows), BF),
        "xsf": pltpu.VMEM((SEQ, width), BF),
        "xrf": pltpu.VMEM((SEQ, width), BF),
        "gqkv": pltpu.VMEM((4, SEQ, 3 * span), BF),
        "xsb": pltpu.VMEM((2, SEQ, width), BF),
        "xrb": pltpu.VMEM((2, SEQ, width), BF),
        "gs": pltpu.VMEM((2, own, 128), F32),
        "gr": pltpu.VMEM((2, own, 128), F32),
        "sent": pltpu.SemaphoreType.DMA((40,)),
        "came": pltpu.SemaphoreType.DMA((40,)),
        "ring_sent": pltpu.SemaphoreType.DMA((5 * 2 * (n - 1) * 2,)),
        "ring_came": pltpu.SemaphoreType.DMA((5 * 2 * (n - 1) * 2,)),
    }
    names = ("shard", "x", "dy", "mask", "bias", "out", "gtok", "gw", "gg") + tuple(scratch)
    out, gtok, gw, gg = pl.pallas_call(
        functools.partial(layer_kernel, n, names),
        out_shape=(
            jax.ShapeDtypeStruct((2, SEQ, width), BF),
            jax.ShapeDtypeStruct((2, SEQ, width), F32),
            jax.ShapeDtypeStruct((5, 2, own, width), F32),
            jax.ShapeDtypeStruct((2, own, 128), F32),
        ),
        in_specs=[pl.BlockSpec(memory_space=pltpu.VMEM)] * 5,
        out_specs=[pl.BlockSpec(memory_space=pltpu.VMEM)] * 4,
        scratch_shapes=list(scratch.values()),
        compiler_params=pltpu.CompilerParams(
            collective_id=0, has_side_effects=True, vmem_limit_bytes=60 * 2**20
        ),
    )(shard, padded(tokens), padded(cotangent), mask, bias)

    def joined(block):
        return block.transpose(1, 0, 2).reshape(own, -1)

    attn = gw[ATT]
    grads = [joined(attn[:, :, i * span : (i + 1) * span]) for i in range(4)]
    return (
        trimmed(out),
        trimmed(gtok),
        gg[0, :, 0] / gain_one[:, 0],
        grads[0] * (gain_one * HEAD_DIM**-0.5),
        grads[1] * gain_one,
        grads[2] * gain_one,
        grads[3].T,
        gg[1, :, 0] / gain_two[:, 0],
        joined(gw[VIN]) * gain_two,
        joined(gw[VOUT]).T,
        joined(gw[TIN]) * gain_two,
        joined(gw[TOUT]).T,
    )


def norm_parts(values):
    center = values - jnp.mean(values, axis=-1, keepdims=True)
    spread = jnp.mean(center * center, axis=-1, keepdims=True)
    inverse = lax.rsqrt(spread + epsilon)
    return (center * inverse, inverse)


def norm_back(grad_out, normed, inverse, gain):
    grad_normed = grad_out * gain
    grad_gain = jnp.sum(grad_out * normed, axis=0)
    inner = (
        grad_normed
        - jnp.mean(grad_normed, axis=-1, keepdims=True)
        - normed * jnp.mean(grad_normed * normed, axis=-1, keepdims=True)
    )
    return (inverse * inner, grad_gain)


def matmul(left, right):
    return jnp.dot(left, right, preferred_element_type=jnp.float32)


def matmul_tn(left, right):
    return lax.dot_general(
        left, right, (((0,), (0,)), ((), ())), preferred_element_type=jnp.float32
    )


def matmul_nt(left, right):
    return lax.dot_general(
        left, right, (((1,), (1,)), ((), ())), preferred_element_type=jnp.float32
    )


def gelu_slope(pre):
    cumulative = 0.5 * (1.0 + lax.erf(pre * inv_root_two))
    density = jnp.exp(-0.5 * pre * pre) * inv_root_tau
    return cumulative + pre * density


def expert_forward(rows, weight_in, weight_out):
    pre = matmul(rows, weight_in)
    hidden = jax.nn.gelu(pre, approximate=False).astype(jnp.bfloat16)
    return (pre, hidden, matmul(hidden, weight_out))


def expert_backward(rows, pre, hidden, grad_out, weight_in, weight_out):
    grad_weight_out = matmul_tn(hidden, grad_out)
    grad_hidden = matmul_nt(grad_out, weight_out)
    grad_pre = (grad_hidden * gelu_slope(pre)).astype(jnp.bfloat16)
    return (matmul_tn(rows, grad_pre), grad_weight_out, matmul_nt(grad_pre, weight_in))


def join_experts(image_rows, text_rows, pair_count, width):
    joined = jnp.concatenate(
        [
            image_rows.reshape(pair_count, PATCHES, width),
            text_rows.reshape(pair_count, CAPTION, width),
        ],
        axis=1,
    )
    return joined.reshape(-1, width)


def plain_layer(
    tokens,
    caption_lengths,
    gain_attn,
    w_query,
    w_key,
    w_value,
    w_out,
    gain_ffn,
    vis_in,
    vis_out,
    txt_in,
    txt_out,
    cotangent,
):
    seq_len = PATCHES + CAPTION
    width = tokens.shape[1]
    pair_count = tokens.shape[0] // seq_len
    half_pairs = pair_count // lax.axis_size("tensor")
    half_rows = half_pairs * seq_len
    row_start = lax.axis_index("tensor") * half_rows
    gain_one, query_w, key_w, value_w, out_w = (
        lax.all_gather(gain_attn, "dp", axis=0, tiled=True),
        lax.all_gather(w_query, "dp", axis=0, tiled=True),
        lax.all_gather(w_key, "dp", axis=0, tiled=True),
        lax.all_gather(w_value, "dp", axis=0, tiled=True),
        lax.all_gather(w_out, "dp", axis=1, tiled=True),
    )
    gain_two, vis_in_w, vis_out_w, txt_in_w, txt_out_w = (
        lax.all_gather(gain_ffn, "dp", axis=0, tiled=True),
        lax.all_gather(vis_in, "dp", axis=0, tiled=True),
        lax.all_gather(vis_out, "dp", axis=1, tiled=True),
        lax.all_gather(txt_in, "dp", axis=0, tiled=True),
        lax.all_gather(txt_out, "dp", axis=1, tiled=True),
    )
    gain_one = gain_one.astype(jnp.float32)
    gain_two = gain_two.astype(jnp.float32)
    head_local = query_w.shape[1] // HEAD_DIM
    score_scale = HEAD_DIM ** (-0.5)
    position = jnp.arange(seq_len, dtype=jnp.int32)
    live = (position[None, :] < PATCHES) | (position[None, :] - PATCHES < caption_lengths[:, None])
    valid_rows = live.astype(jnp.float32)
    mask_col = valid_rows.reshape(-1, 1)
    key_live = valid_rows[:, None, None, :] > 0.5

    def own_rows(values):
        return lax.dynamic_slice_in_dim(values, row_start, half_rows, 0)

    inputs = tokens.astype(jnp.float32)
    normed_one, inverse_one = norm_parts(inputs)
    first_in = (normed_one * gain_one).astype(jnp.bfloat16)

    def project(weight):
        return (
            matmul(first_in, weight)
            .astype(jnp.bfloat16)
            .reshape(pair_count, seq_len, head_local, HEAD_DIM)
        )

    queries = project(query_w)
    keys_all = project(key_w)
    values_all = project(value_w)

    def score_block():
        raw = (
            jnp.einsum("pqhe,pkhe->phqk", queries, keys_all, preferred_element_type=jnp.float32)
            * score_scale
        )
        return jnp.where(key_live, raw, -1e30)

    scores = score_block()
    top = jnp.max(scores, axis=-1, keepdims=True)
    weights = jnp.exp(scores - top)
    total = jnp.sum(weights, axis=-1, keepdims=True)
    probs = (weights / total).astype(jnp.bfloat16)
    log_total = top + jnp.log(total)
    context = jnp.einsum("phqk,pkhe->pqhe", probs, values_all, preferred_element_type=jnp.float32)
    context = context.astype(jnp.bfloat16).reshape(-1, head_local * HEAD_DIM)
    attn_terms = matmul(context, out_w)
    attended_own = lax.psum_scatter(
        attn_terms.astype(jnp.bfloat16), "tensor", scatter_dimension=0, tiled=True
    ).astype(jnp.float32)
    mask_own = own_rows(mask_col)
    middle_own = own_rows(inputs) + mask_own * attended_own
    normed_two, inverse_two = norm_parts(middle_own)
    second_own = (normed_two * gain_two).astype(jnp.bfloat16)
    grid = lax.all_gather(second_own, "tensor", axis=0, tiled=True).reshape(
        pair_count, seq_len, width
    )
    image_rows = grid[:, :PATCHES].reshape(-1, width)
    text_rows = grid[:, PATCHES:].reshape(-1, width)
    image_pre, image_hidden, image_part = expert_forward(image_rows, vis_in_w, vis_out_w)
    text_pre, text_hidden, text_part = expert_forward(text_rows, txt_in_w, txt_out_w)
    image_own, text_own = (
        lax.psum_scatter(
            image_part.astype(jnp.bfloat16), "tensor", scatter_dimension=0, tiled=True
        ).astype(jnp.float32),
        lax.psum_scatter(
            text_part.astype(jnp.bfloat16), "tensor", scatter_dimension=0, tiled=True
        ).astype(jnp.float32),
    )
    branch_own = join_experts(image_own, text_own, half_pairs, width)
    output_own = (middle_own + mask_own * branch_own).astype(jnp.bfloat16)
    upstream = cotangent.astype(jnp.float32)
    grad_branch = (upstream * mask_col).astype(jnp.bfloat16).reshape(pair_count, seq_len, width)
    image_grads = expert_backward(
        image_rows,
        image_pre,
        image_hidden,
        grad_branch[:, :PATCHES].reshape(-1, width),
        vis_in_w,
        vis_out_w,
    )
    text_grads = expert_backward(
        text_rows,
        text_pre,
        text_hidden,
        grad_branch[:, PATCHES:].reshape(-1, width),
        txt_in_w,
        txt_out_w,
    )
    back_image_own, back_text_own = (
        lax.psum_scatter(
            image_grads[2].astype(jnp.bfloat16), "tensor", scatter_dimension=0, tiled=True
        ).astype(jnp.float32),
        lax.psum_scatter(
            text_grads[2].astype(jnp.bfloat16), "tensor", scatter_dimension=0, tiled=True
        ).astype(jnp.float32),
    )
    grad_second_own = join_experts(back_image_own, back_text_own, half_pairs, width)
    grad_norm_own, gain_part = norm_back(grad_second_own, normed_two, inverse_two, gain_two)
    grad_middle_own = own_rows(upstream) + grad_norm_own
    output_wide, grad_middle, gain_parts = (
        lax.all_gather(
            output_own.astype(jnp.float32).astype(jnp.bfloat16), "tensor", axis=0, tiled=True
        ).astype(jnp.float32),
        lax.all_gather(grad_middle_own.astype(jnp.bfloat16), "tensor", axis=0, tiled=True).astype(
            grad_middle_own.dtype
        ),
        lax.all_gather(gain_part.astype(jnp.bfloat16), "tensor", axis=0, tiled=True).astype(
            gain_part.dtype
        ),
    )
    output = output_wide.astype(jnp.bfloat16)
    grad_gain_two = jnp.sum(gain_parts.reshape(-1, width), axis=0)
    grad_attended = (grad_middle * mask_col).astype(jnp.bfloat16)
    grad_out_w = matmul_tn(context, grad_attended)
    grad_context = (
        matmul_nt(grad_attended, out_w)
        .astype(jnp.bfloat16)
        .reshape(pair_count, seq_len, head_local, HEAD_DIM)
    )
    scores_again = score_block()
    probs_exact = jnp.exp(scores_again - log_total)
    grad_probs = jnp.einsum(
        "pqhe,pkhe->phqk", grad_context, values_all, preferred_element_type=jnp.float32
    )
    inner = jnp.sum(grad_probs * probs_exact, axis=-1, keepdims=True)
    grad_scores = (probs_exact * (grad_probs - inner)).astype(jnp.bfloat16)
    grad_values = jnp.einsum(
        "phqk,pqhe->pkhe", probs, grad_context, preferred_element_type=jnp.float32
    )
    grad_values = grad_values.astype(jnp.bfloat16).reshape(-1, head_local * HEAD_DIM)
    grad_queries = (
        jnp.einsum("phqk,pkhe->pqhe", grad_scores, keys_all, preferred_element_type=jnp.float32)
        * score_scale
    )
    grad_queries = grad_queries.astype(jnp.bfloat16).reshape(-1, head_local * HEAD_DIM)
    grad_keys = (
        jnp.einsum("phqk,pqhe->pkhe", grad_scores, queries, preferred_element_type=jnp.float32)
        * score_scale
    )
    grad_keys = grad_keys.astype(jnp.bfloat16).reshape(-1, head_local * HEAD_DIM)
    grad_query_w = matmul_tn(first_in, grad_queries)
    grad_key_w = matmul_tn(first_in, grad_keys)
    grad_value_w = matmul_tn(first_in, grad_values)
    first_part = (
        matmul_nt(grad_queries, query_w)
        + matmul_nt(grad_keys, key_w)
        + matmul_nt(grad_values, value_w)
    )
    grad_first = lax.psum(first_part.astype(jnp.bfloat16), "tensor").astype(jnp.float32)
    grad_norm_one, grad_gain_one = norm_back(grad_first, normed_one, inverse_one, gain_one)
    grad_inputs = grad_middle + grad_norm_one
    attn_sent = (
        lax.psum_scatter(grad_gain_one, "dp", scatter_dimension=0, tiled=True),
        lax.psum_scatter(grad_query_w, "dp", scatter_dimension=0, tiled=True),
        lax.psum_scatter(grad_key_w, "dp", scatter_dimension=0, tiled=True),
        lax.psum_scatter(grad_value_w, "dp", scatter_dimension=0, tiled=True),
        lax.psum_scatter(grad_out_w, "dp", scatter_dimension=1, tiled=True),
    )
    final_expert = (
        lax.psum_scatter(grad_gain_two, "dp", scatter_dimension=0, tiled=True),
        lax.psum_scatter(image_grads[0], "dp", scatter_dimension=0, tiled=True),
        lax.psum_scatter(image_grads[1], "dp", scatter_dimension=1, tiled=True),
        lax.psum_scatter(text_grads[0], "dp", scatter_dimension=0, tiled=True),
        lax.psum_scatter(text_grads[1], "dp", scatter_dimension=1, tiled=True),
    )
    return (
        output,
        grad_inputs,
        attn_sent[0],
        attn_sent[1],
        attn_sent[2],
        attn_sent[3],
        attn_sent[4],
        final_expert[0],
        final_expert[1],
        final_expert[2],
        final_expert[3],
        final_expert[4],
    )


def solution(mesh):
    def local(tokens, lengths, gain, w_query, *rest):
        ring = mesh.shape["dp"] // 2
        fits = (
            mesh.shape["tensor"] == 2
            and ring == 8
            and lengths.shape[0] == 2
            and w_query.shape[0] % 16 == 0
        )
        layer = fused_layer if fits else plain_layer
        return layer(tokens, lengths, gain, w_query, *rest)

    return jax.shard_map(
        local,
        mesh=mesh,
        in_specs=(
            P("dp", None),
            P("dp"),
            P("dp"),
            P("dp", "tensor"),
            P("dp", "tensor"),
            P("dp", "tensor"),
            P("tensor", "dp"),
            P("dp"),
            P("dp", "tensor"),
            P("tensor", "dp"),
            P("dp", "tensor"),
            P("tensor", "dp"),
            P("dp", None),
        ),
        out_specs=(
            P("dp", None),
            P("dp", None),
            P("dp"),
            P("dp", "tensor"),
            P("dp", "tensor"),
            P("dp", "tensor"),
            P("tensor", "dp"),
            P("dp"),
            P("dp", "tensor"),
            P("tensor", "dp"),
            P("dp", "tensor"),
            P("tensor", "dp"),
        ),
        check_vma=False,
    )
```

```python
import functools
import math
import types

import jax
import jax.numpy as jnp
from jax import lax
from jax.experimental import pallas as pl
from jax.experimental.pallas import tpu as pltpu
from jax.sharding import PartitionSpec as P

HEAD_DIM = 64
PATCHES = 197
CAPTION = 40
VIS = 208
TXT = 48
SEQ = VIS + TXT

MESH = pl.DeviceIdType.MESH
BF = jnp.bfloat16
F32 = jnp.float32

ATT, TIN, TOUT, VIN, VOUT = range(5)

epsilon = 1e-05
inv_root_two = 1.0 / math.sqrt(2.0)
inv_root_tau = 1.0 / math.sqrt(2.0 * math.pi)


def mm(left, right):
    return jnp.dot(left, right, preferred_element_type=F32)


def mm_nt(left, right):
    return lax.dot_general(left, right, (((1,), (1,)), ((), ())), preferred_element_type=F32)


def mm_tn(left, right):
    return lax.dot_general(left, right, (((0,), (0,)), ((), ())), preferred_element_type=F32)


def normalize(values):
    center = values - jnp.mean(values, axis=-1, keepdims=True)
    spread = jnp.mean(center * center, axis=-1, keepdims=True)
    inverse = lax.rsqrt(spread + epsilon)
    return center * inverse, inverse


def normalize_back(grad_normed, normed, inverse):
    return inverse * (
        grad_normed
        - jnp.mean(grad_normed, axis=-1, keepdims=True)
        - normed * jnp.mean(grad_normed * normed, axis=-1, keepdims=True)
    )


def unit(size):
    rows = lax.broadcasted_iota(jnp.int32, (size, size), 0)
    return (rows == lax.broadcasted_iota(jnp.int32, (size, size), 1)).astype(F32).astype(BF)


def column(ref):
    size = ref.shape[1]
    return jnp.sum(unit(size).astype(F32) * ref[...].astype(F32), axis=1, keepdims=True)


class Events:
    def __init__(self):
        self.todo = []

    def add(self, *steps):
        self.todo.extend(steps)

    def advance(self, count):
        for _ in range(min(count, len(self.todo))):
            self.todo.pop(0)()

    def drain(self):
        self.advance(len(self.todo))


def layer_kernel(n, names, *refs):
    R = types.SimpleNamespace(**dict(zip(names, refs)))
    R.pb, R.pf, R.ga, R.rf, R.rb, R.n2 = R.pa, R.pg, R.x4, R.ra, R.rg, R.n1
    R.gat, R.gzvt, R.gqkv = R.turned, R.turned, R.n2
    S, BIAS = R.shard, R.bias
    OUT, GW, GG = R.padded_out, R.gw, R.gg
    G, PART, LAND = R.gathered, R.part, R.land
    width = G.shape[2]
    own = width // (2 * n)

    x = lax.axis_index("tensor")
    d = lax.axis_index("dp")
    c = lax.rem(d, 2)
    other = 1 - c
    chip = d // 2
    y, z = lax.rem(chip, 2), chip // 2
    r = z + y * (n - 1 - 2 * z)
    half = n // 2

    def chip_at(pos):
        pos = lax.rem(pos + 2 * n, n)
        upper = pos // half
        return 2 * (pos + upper * (n - 1 - 2 * pos)) + upper

    mate = {"dp": d + 1 - 2 * c}
    across = {"tensor": 1 - x}
    ahead = {"dp": 2 * chip_at(r + 1) + c}
    behind = {"dp": 2 * chip_at(r - 1) + c}
    way = (ahead, behind)

    def rows_at(pos, side):
        return pl.ds(pl.multiple_of(2 * own * chip_at(pos) + own * side, 16), own)

    my_rows = pl.ds(pl.multiple_of(own * d, 16), own)

    barrier = pltpu.get_barrier_semaphore()
    for device in (mate, across, ahead, behind):
        pl.semaphore_signal(barrier, inc=1, device_id=device, device_id_type=MESH)

    mine, theirs = pl.multiple_of(2 * c, 2), pl.multiple_of(2 * other, 2)
    pair_own = 2 * c + x
    pair_across = 2 * c + 1 - x

    started = []
    counter = [0]

    def remote(source, target, device, index=None):
        if index is None:
            index = counter[0]
            counter[0] += 1
        return pltpu.make_async_remote_copy(
            src_ref=source,
            dst_ref=target,
            send_sem=R.sent.at[index],
            recv_sem=R.came.at[index],
            device_id=device,
            device_id_type=MESH,
        )

    def start(source, target, device):
        copy = remote(source, target, device)
        copy.start()
        started.append(copy)
        return copy

    def sent(copy):
        copy.wait_send()
        started[:] = [one for one in started if one is not copy]

    span = width // 4

    def shard_part(k, value):
        for core in range(2):
            S[k, core] = value(core).astype(BF)

    gain_one, gain_two = column(R.gain_attn), column(R.gain_ffn)
    square = unit(own)

    def attention_part(core):
        cols = slice(core * span, (core + 1) * span)
        return jnp.concatenate(
            [
                R.w_query[:, cols].astype(F32) * (gain_one * HEAD_DIM**-0.5),
                R.w_key[:, cols].astype(F32) * gain_one,
                R.w_value[:, cols].astype(F32) * gain_one,
                mm_nt(square, R.w_out[cols, :]),
            ],
            axis=1,
        )

    def half_of(ref, core):
        return ref[:, core * width : (core + 1) * width].astype(F32) * gain_two

    def turned_half(ref, core):
        return mm_nt(square, ref[core * width : (core + 1) * width, :])

    shard_part(ATT, attention_part)
    pl.semaphore_wait(barrier, 4)
    shard_a = start(S.at[pl.ds(0, 1), other], G.at[pl.ds(0, 1), my_rows, :], mate)
    G[ATT, my_rows, :] = S[ATT, c]
    shard_part(TIN, functools.partial(half_of, R.txt_in))
    shard_part(TOUT, functools.partial(turned_half, R.txt_out))
    shard_part(VIN, functools.partial(half_of, R.vis_in))
    shard_part(VOUT, functools.partial(turned_half, R.vis_out))
    shard_b = start(S.at[pl.ds(1, 4), other], G.at[pl.ds(1, 4), my_rows, :], mate)
    for k in (TIN, TOUT, VIN, VOUT):
        G[k, my_rows, :] = S[k, c]

    lengths = R.lengths

    def live(t, slots):
        return (slots < PATCHES) | ((slots >= VIS) & (slots < VIS + lengths[t]))

    def live_rows(t, j, count=64):
        slots = lax.broadcasted_iota(jnp.int32, (count, 1), 0) + j * count
        return live(t, slots).astype(F32)

    row_count = R.tokens.shape[0]

    def placed(t, slots, rows, kept):
        source = t * (PATCHES + CAPTION) + slots - (slots >= VIS).astype(jnp.int32) * (VIS - PATCHES)
        return ((rows == source) & kept).astype(F32).astype(BF)

    def chooser(t, only_live):
        slots = lax.broadcasted_iota(jnp.int32, (SEQ, row_count), 0)
        rows = lax.broadcasted_iota(jnp.int32, (SEQ, row_count), 1)
        filled = (slots < PATCHES) | ((slots >= VIS) & (slots < VIS + CAPTION))
        return placed(t, slots, rows, live(t, slots) if only_live else filled)

    for t in range(2):
        R.x4[2 * c + t] = mm(chooser(t, False), R.tokens[...]).astype(BF)
        slots = lax.broadcasted_iota(jnp.int32, (8, SEQ), 1)
        BIAS[t] = jnp.where(live(t, slots), 0.0, -1e30)
        R.bias4[2 * c + t] = BIAS[t]
    send_x = start(R.x4.at[pl.ds(mine, 2)], R.x4.at[pl.ds(mine, 2)], mate)
    send_bias = start(BIAS, R.bias4.at[pl.ds(mine, 2)], mate)

    def gather_index(k, side, s):
        return (k * 2 + side) * (n - 1) + s

    def gather_copy(k, side, s):
        pos = r - s if side == 0 else r + s
        block = G.at[k, rows_at(pos, side), :]
        i = gather_index(k, side, s)
        return pltpu.make_async_remote_copy(
            src_ref=block,
            dst_ref=block,
            send_sem=R.ring_sent.at[i],
            recv_sem=R.ring_came.at[i],
            device_id=way[side],
            device_id_type=MESH,
        )

    def gather_came(k, side, s):
        pos = r - 1 - s if side == 0 else r + 1 + s
        block = G.at[k, rows_at(pos, side), :]
        i = gather_index(k, side, s)
        pltpu.make_async_remote_copy(
            src_ref=block,
            dst_ref=block,
            send_sem=R.ring_sent.at[i],
            recv_sem=R.ring_came.at[i],
            device_id=way[side],
            device_id_type=MESH,
        ).wait_recv()

    def gather_step(k, s):
        for side in range(2):
            if not (isinstance(s, int) and s == 0):
                gather_came(k, side, s - 1)
            if not (isinstance(s, int) and s == n - 1):
                gather_copy(k, side, s).start()

    sum_base = 5 * 2 * (n - 1)

    def sum_copy(k, side, s, source):
        i = sum_base + gather_index(k, side, s)
        return pltpu.make_async_remote_copy(
            src_ref=source,
            dst_ref=LAND.at[k, side, s],
            send_sem=R.ring_sent.at[i],
            recv_sem=R.ring_came.at[i],
            device_id=way[side],
            device_id_type=MESH,
        )

    def sum_step(k, s):
        for side in range(2):
            pos = r - 1 - s if side == 0 else r + 1 + s
            if isinstance(s, int) and s == 0:
                source = PART.at[k, rows_at(pos, side), :]
            else:
                source = LAND.at[k, side, s - 1]
                sum_copy(k, side, s - 1, source).wait_recv()
                LAND[k, side, s - 1] = (
                    LAND[k, side, s - 1].astype(F32) + PART[k, rows_at(pos, side), :].astype(F32)
                ).astype(BF)
            sum_copy(k, side, s, source).start()

    finals = []

    def sum_last(k):
        for side in range(2):
            sum_copy(k, side, n - 2, LAND.at[k, side, n - 2]).wait_recv()

        def total(core):
            rows = pl.ds(pl.multiple_of(2 * own * chip + own * core, 16), own)
            return LAND[k, core, n - 2].astype(F32) + PART[k, rows, :].astype(F32)

        R.give[k] = total(other)
        finals.append(start(R.give.at[k], GW.at[k, c], mate))
        GW[k, c] = total(c)

    shard_a.wait_recv()
    gather_step(ATT, 0)
    for t in range(2):
        R.gz[2 * c + t] = mm(chooser(t, True), R.cotangent[...]).astype(BF)
    send_gz = start(R.gz.at[pl.ds(mine, 2)], R.gz.at[pl.ds(mine, 2)], mate)
    R.dy[...] = mm(chooser(x, False), R.cotangent[...]).astype(BF)
    for t in range(2):
        R.x[t] = R.x4[2 * c + t]
    shard_b.wait_recv()
    gather_step(TIN, 0)
    send_x.wait_recv()

    ring = Events()
    for s in range(1, n - 1):
        ring.add(functools.partial(gather_step, ATT, s), functools.partial(gather_step, TIN, s))

    for i in range(4):

        @pl.loop(0, SEQ // 64)
        def _(j, i=i):
            rows = pl.ds(pl.multiple_of(j * 64, 64), 64)
            normed, _ = normalize(R.x4[i, rows, :].astype(F32))
            R.n1[i, rows, :] = normed.astype(BF)

        R.n1t[:, i * SEQ : (i + 1) * SEQ] = R.n1[i].T
        ring.advance(1)
    send_gz.wait_recv()
    send_bias.wait_recv()
    ring.advance(1)

    @pl.loop(0, width // 256)
    def _(j):
        cols = pl.ds(pl.multiple_of(j * 256, 256), 256)
        R.gzvt[cols, : 4 * VIS] = R.gz[:, :VIS, cols].reshape(4 * VIS, 256).T
        R.gztt[cols, :] = R.gz[:, VIS:, cols].reshape(4 * TXT, 256).T

    ring.drain()
    gather_step(ATT, n - 1)
    gather_step(TIN, n - 1)
    for k in (TOUT, VIN, VOUT):
        gather_step(k, 0)

    heads = span // HEAD_DIM
    R.wo[...] = G[ATT][:, 3 * span :]

    @pl.loop(0, 4)
    def _(i):
        projected = mm(R.n1[i], G[ATT][:, : 3 * span]).astype(BF)
        R.q[i] = projected[:, :span]
        R.k[i] = projected[:, span : 2 * span]
        R.v[i] = projected[:, 2 * span :]

    lane = lax.broadcasted_iota(jnp.int32, (1, span), 1) // HEAD_DIM

    def only(head, values):
        return values * (lane == head).astype(F32).astype(BF)

    for k in (TOUT, VIN, VOUT):
        gather_step(k, 1)

    base = counter[0]
    counter[0] += 2

    def pair_order(j):
        core = other + (j // 2) * (c - other)
        turn = (1 - x) + lax.rem(j, 2) * (2 * x - 1)
        return core, turn, 2 * core + turn

    def forward_copy(j, turn, i):
        return remote(R.pa.at[i], R.ra.at[turn], mate, base + j)

    cross_a = remote(R.xs, R.xr, across)

    @pl.loop(0, 4)
    def _(j):
        core, turn, i = pair_order(j)
        q, k, v = R.q[i], R.k[i], R.v[i]
        context = jnp.zeros((SEQ, span), F32)
        for h in range(heads):
            scores = mm_nt(q, only(h, k)) + R.bias4[i][:1, :]
            top = jnp.max(scores, axis=-1, keepdims=True)
            weights = jnp.exp(scores - top)
            total = jnp.sum(weights, axis=-1, keepdims=True)
            probs = (weights * (1.0 / total)).astype(BF)
            R.probs[i * heads + h] = probs
            context += mm(probs, only(h, v))
        context = context.astype(BF)
        R.c[i] = context
        R.pa[i] = mm_nt(context, R.wo[...]).astype(BF)

        @pl.when(j < 2)
        def _():
            forward_copy(j, turn, i).start()

        @pl.when(j == 2)
        def _():
            forward_copy(0, 1 - x, pair_across).wait_recv()
            R.xs[...] = (
                R.pa[pair_across].astype(F32) + R.ra[1 - x].astype(F32)
            ).astype(BF)
            cross_a.start()

        for k in (TOUT, VIN, VOUT):
            gather_step(k, 2 + j)

    started.append(cross_a)
    for j in range(2):
        core, turn, i = pair_order(j)
        forward_copy(j, turn, i).wait_send()
    forward_copy(1, x, pair_own).wait_recv()
    for k in (TOUT, VIN, VOUT):
        gather_step(k, n - 2)
    cross_a.wait_recv()

    @pl.loop(0, SEQ // 64)
    def _(j):
        rows = pl.ds(pl.multiple_of(j * 64, 64), 64)
        attended = (
            R.pa[pair_own, rows, :].astype(F32)
            + R.ra[x, rows, :].astype(F32)
            + R.xr[rows, :].astype(F32)
        )
        alive = live_rows(x, j)
        middle = R.x[x, rows, :].astype(F32) + alive * attended
        R.y1[rows, :] = middle
        normed, _ = normalize(middle)
        R.n2[pair_own, rows, :] = normed.astype(BF)

    def spread(ref):
        block = ref.at[pair_own]
        to_across = start(block, block, across)
        to_mate = start(block, block, mate)
        return to_across, to_mate

    to_across, to_mate = spread(R.n2)
    to_across.wait_recv()
    block = R.n2.at[pair_across]
    passed = start(block, block, mate)
    to_mate.wait_recv()
    passed.wait_recv()

    for k in (TOUT, VIN, VOUT):
        gather_step(k, n - 1)

    def expert(low, high, w_in, w_out, h_ref, gu_ref, after):
        per = high - low
        total_rows = 4 * per
        step = 64

        def run(j):
            cols = pl.ds(pl.multiple_of(j * 256, 256), 256)
            R.u[:total_rows, :] = mm(
                R.n2[:, low:high, :].reshape(total_rows, width), G[w_in, :, cols]
            )
            R.gh[:total_rows, :] = mm(
                R.gz[:, low:high, :].reshape(total_rows, width), G[w_out, :, cols]
            )

            @pl.loop(0, total_rows // step)
            def _(i):
                rows = pl.ds(pl.multiple_of(i * step, step), step)
                pre = R.u[rows, :]
                cumulative = 0.5 * (1.0 + lax.erf(pre * inv_root_two))
                density = jnp.exp(-0.5 * pre * pre) * inv_root_tau
                h_ref[rows, cols] = (pre * cumulative).astype(BF)
                gu_ref[rows, cols] = (R.gh[rows, :] * (cumulative + pre * density)).astype(BF)

            after(j)

        pl.loop(0, width // 256)(run)

    def weight_grad(k, turned, ref):
        @pl.loop(0, width // 256)
        def _(j):
            cols = pl.ds(pl.multiple_of(j * 256, 256), 256)
            PART[k, :, cols] = mm(turned, ref[:, cols]).astype(BF)

    expert(VIS, SEQ, TIN, TOUT, R.ht, R.gut, lambda j: None)
    weight_grad(TOUT, R.gztt[...], R.ht)
    sum_step(TOUT, 0)

    @pl.loop(0, width // 256)
    def _(j):
        cols = pl.ds(pl.multiple_of(j * 256, 256), 256)
        R.n2vt[cols, :] = R.n2[:, :VIS, cols].reshape(4 * VIS, 256).T
        R.n2tt[cols, :] = R.n2[:, VIS:, cols].reshape(4 * TXT, 256).T

    weight_grad(TIN, R.n2tt[...], R.gut)
    sum_step(TIN, 0)

    def vis_after(j):
        sum_step(TOUT, 1 + j)
        sum_step(TIN, 1 + j)

    expert(0, VIS, VIN, VOUT, R.hv, R.guv, vis_after)

    def terms(target, hv, ht, w_vis, w_txt, first):
        vis_rows = pl.ds(pl.multiple_of(first * VIS, 16), 2 * VIS)
        txt_rows = pl.ds(pl.multiple_of(first * TXT, 16), 2 * TXT)
        vis_part = mm_nt(hv[vis_rows, :], G[w_vis]).astype(BF)
        target[pl.ds(first, 2), :VIS, :] = vis_part.reshape(2, VIS, width)
        txt_part = mm_nt(ht[txt_rows, :], G[w_txt]).astype(BF)
        target[pl.ds(first, 2), VIS:, :] = txt_part.reshape(2, TXT, width)

    terms(R.pg, R.guv, R.gut, VIN, TIN, theirs)
    mate_g = start(R.pg.at[pl.ds(theirs, 2)], R.rg, mate)
    sum_step(TOUT, 4)
    sum_step(TIN, 4)
    terms(R.pg, R.guv, R.gut, VIN, TIN, mine)
    mate_g.wait_recv()
    R.xsg[...] = (R.pg[pair_across].astype(F32) + R.rg[1 - x].astype(F32)).astype(BF)
    cross_g = start(R.xsg, R.xrg, across)
    sum_step(TOUT, 5)
    sum_step(TIN, 5)
    weight_grad(VOUT, R.gzvt[:, : 4 * VIS], R.hv)
    sum_step(VOUT, 0)
    sum_step(TOUT, 6)
    sum_step(TIN, 6)
    weight_grad(VIN, R.n2vt[...], R.guv)
    sum_step(VIN, 0)
    cross_g.wait_recv()
    for copy in (send_x, to_across, to_mate, passed):
        sent(copy)

    @pl.loop(0, SEQ // 64)
    def _(j):
        rows = pl.ds(pl.multiple_of(j * 64, 64), 64)
        grad_normed = (
            R.pg[pair_own, rows, :].astype(F32)
            + R.rg[x, rows, :].astype(F32)
            + R.xrg[rows, :].astype(F32)
        )
        normed, inverse = normalize(R.y1[rows, :])
        grad = R.dy[rows, :].astype(F32) + normalize_back(grad_normed, normed, inverse)
        R.gy[x, rows, :] = grad.astype(BF)
        alive = live_rows(x, j)
        R.ga[pair_own, rows, :] = (grad * alive).astype(BF)

    gy_across = start(R.gy.at[x], R.gy.at[x], across)
    gy_mate = start(R.ga.at[pair_own], R.ga.at[pair_own], mate)
    sum_last(TOUT)
    sum_last(TIN)
    sum_step(VOUT, 1)
    sum_step(VIN, 1)

    sent(mate_g)
    terms(R.pf, R.hv, R.ht, VOUT, TOUT, theirs)
    mate_f = start(R.pf.at[pl.ds(theirs, 2)], R.rf, mate)
    sum_step(VOUT, 2)
    sum_step(VIN, 2)
    gy_across.wait_recv()

    @pl.loop(0, SEQ // 64)
    def _(j):
        rows = pl.ds(pl.multiple_of(j * 64, 64), 64)
        alive = live_rows(1 - x, j)
        R.ga[pair_across, rows, :] = (R.gy[1 - x, rows, :].astype(F32) * alive).astype(BF)

    block = R.ga.at[pair_across]
    gy_passed = start(block, block, mate)
    terms(R.pf, R.hv, R.ht, VOUT, TOUT, mine)
    mate_f.wait_recv()
    R.xsf[...] = (R.pf[pair_across].astype(F32) + R.rf[1 - x].astype(F32)).astype(BF)
    cross_f = start(R.xsf, R.xrf, across)
    gy_mate.wait_recv()
    gy_passed.wait_recv()

    base_back = counter[0]
    counter[0] += 2

    def back_copy(j, turn, i):
        return remote(R.pb.at[i], R.rb.at[turn], mate, base_back + j)

    base_cross = counter[0]
    counter[0] += 2

    def back_cross(j, turn):
        return remote(R.xsb.at[turn], R.xrb.at[turn], across, base_cross + j)

    @pl.loop(0, 4)
    def _(j):
        core, turn, i = pair_order(j)
        grad_context = mm(R.ga[i], R.wo[...]).astype(BF)
        R.gat[:, pl.ds(pl.multiple_of(i * SEQ, SEQ), SEQ)] = R.ga[i].T
        q, k, v = R.q[i], R.k[i], R.v[i]
        grad_q = jnp.zeros((SEQ, span), F32)
        grad_k = jnp.zeros((SEQ, span), F32)
        grad_v = jnp.zeros((SEQ, span), F32)
        for h in range(heads):
            probs = R.probs[i * heads + h]
            grad_probs = mm_nt(grad_context, only(h, v))
            exact = probs.astype(F32)
            inner = jnp.sum(grad_probs * exact, axis=-1, keepdims=True)
            grad_scores = (exact * (grad_probs - inner)).astype(BF)
            grad_q += mm(grad_scores, only(h, k))
            grad_k += mm_tn(grad_scores, only(h, q))
            grad_v += mm_tn(probs, only(h, grad_context))
        joined = jnp.concatenate([grad_q, grad_k, grad_v], axis=1).astype(BF)
        R.gqkv[i, :, : 3 * span] = joined
        R.pb[i] = mm_nt(joined, G[ATT][:, : 3 * span]).astype(BF)

        @pl.when(j < 2)
        def _():
            back_copy(j, turn, i).start()

        @pl.when(j >= 2)
        def _():
            back_copy(j - 2, turn, i).wait_recv()
            R.xsb[turn] = (
                R.pb[i].astype(F32) + R.rb[turn].astype(F32)
            ).astype(BF)
            back_cross(j - 2, turn).start()

        sum_step(VOUT, 3 + j)
        sum_step(VIN, 3 + j)

    for j in range(2):
        core, turn, i = pair_order(j)
        started.append(back_copy(j, turn, i))
        started.append(back_cross(j, turn))

    @pl.loop(0, 3)
    def _(j):
        cols = pl.ds(pl.multiple_of(j * 256, 256), 256)
        rows = pl.ds(pl.multiple_of(j * 256, 256), 256)
        grads = mm(R.n1t[rows, :], R.gqkv[:, :, : 3 * span].reshape(4 * SEQ, 3 * span))
        grad_o = mm(R.gat[rows, :], R.c[...].reshape(4 * SEQ, span))
        PART[ATT, rows, :] = jnp.concatenate([grads, grad_o], axis=1).astype(BF)

    sum_step(ATT, 0)
    sum_last(VOUT)
    sum_last(VIN)

    cross_f.wait_recv()

    @pl.loop(0, SEQ // 64)
    def _(j):
        rows = pl.ds(pl.multiple_of(j * 64, 64), 64)
        branch = (
            R.pf[pair_own, rows, :].astype(F32)
            + R.rf[x, rows, :].astype(F32)
            + R.xrf[rows, :].astype(F32)
        )
        alive = live_rows(x, j)
        OUT[x, rows, :] = (R.y1[rows, :] + alive * branch).astype(BF)

    out_across = start(OUT.at[x], OUT.at[x], across)
    for s in range(1, 3):
        sum_step(ATT, s)

    for j in range(2):
        back_cross(j, x if j == 0 else 1 - x).wait_recv()
    for t in range(2):

        @pl.loop(0, SEQ // 64)
        def _(j, t=t):
            rows = pl.ds(pl.multiple_of(j * 64, 64), 64)
            grad_normed = R.xsb[t, rows, :].astype(F32) + R.xrb[t, rows, :].astype(F32)
            normed, inverse = normalize(R.x[t, rows, :].astype(F32))
            grad = R.gy[t, rows, :].astype(F32) + normalize_back(grad_normed, normed, inverse)
            high = grad.astype(BF)
            rows = pl.ds(pl.multiple_of(t * SEQ + j * 64, 64), 64)
            R.hv[rows, :] = high
            R.guv[rows, :] = (grad - high.astype(F32)).astype(BF)

        sum_step(ATT, 3 + 2 * t)
        sum_step(ATT, 4 + 2 * t)

    slots = lax.broadcasted_iota(jnp.int32, (row_count, 2 * SEQ), 1)
    rows = lax.broadcasted_iota(jnp.int32, (row_count, 2 * SEQ), 0)
    turn = slots // SEQ
    back = placed(turn, slots - turn * SEQ, rows, slots >= 0)
    out_across.wait_recv()
    R.out_tokens[...] = mm(back, OUT[...].reshape(2 * SEQ, width)).astype(BF)
    R.grad_tokens[...] = mm(back, R.hv[: 2 * SEQ, :]) + mm(back, R.guv[: 2 * SEQ, :])
    sum_last(ATT)
    for copy in finals:
        copy.wait_recv()

    def row_sums(k, last):
        return sum(
            jnp.sum(
                S[k, core][:, :last].astype(F32) * GW[k, core][:, :last], axis=-1, keepdims=True
            )
            for core in range(2)
        )

    R.gs[0] = jnp.broadcast_to(row_sums(ATT, 3 * span), (own, 128))
    R.gs[1] = jnp.broadcast_to(row_sums(TIN, width) + row_sums(VIN, width), (own, 128))
    cross_gain = start(R.gs, R.gr, across)
    cross_gain.wait_recv()
    GG[...] = R.gs[...] + R.gr[...]

    for copy in started:
        copy.wait_send()
    for k in range(5):
        for side in range(2):
            for s in range(n - 1):
                gather_copy(k, side, s).wait_send()
                source = (
                    PART.at[k, rows_at(r, side), :] if s == 0 else LAND.at[k, side, s - 1]
                )
                sum_copy(k, side, s, source).wait_send()


def finish_kernel(out, gtok, gw, gg, gain_attn, gain_ffn, *rest):
    (
        out_tokens,
        grad_tokens,
        grad_gain_attn,
        grad_query,
        grad_key,
        grad_value,
        grad_out,
        grad_gain_ffn,
        grad_vis_in,
        grad_vis_out,
        grad_txt_in,
        grad_txt_out,
        sems,
    ) = rest
    copies = [
        pltpu.make_async_copy(out, out_tokens, sems.at[0]),
        pltpu.make_async_copy(gtok, grad_tokens, sems.at[1]),
    ]
    for copy in copies:
        copy.start()
    width = gw.shape[3]
    own = gw.shape[2]
    span = width // 4
    gain_one, gain_two = column(gain_attn), column(gain_ffn)
    square = unit(own).astype(F32)
    grad_gain_attn[...] = jnp.sum(square * (gg[0][:, :1] / gain_one), axis=0, keepdims=True)
    grad_gain_ffn[...] = jnp.sum(square * (gg[1][:, :1] / gain_two), axis=0, keepdims=True)

    def both(part):
        return jnp.concatenate([gw[ATT, core][:, part * span : (part + 1) * span] for core in range(2)], axis=1)

    grad_query[...] = both(0) * (gain_one * HEAD_DIM**-0.5)
    grad_key[...] = both(1) * gain_one
    grad_value[...] = both(2) * gain_one
    grad_out[...] = both(3).T
    for core in range(2):
        part = slice(core * width, (core + 1) * width)
        grad_vis_in[:, part] = gw[VIN, core] * gain_two
        grad_txt_in[:, part] = gw[TIN, core] * gain_two
        grad_vis_out[part, :] = gw[VOUT, core].T
        grad_txt_out[part, :] = gw[TOUT, core].T
    for copy in copies:
        copy.wait()


def fused_layer(
    tokens,
    caption_lengths,
    gain_attn,
    w_query,
    w_key,
    w_value,
    w_out,
    gain_ffn,
    vis_in,
    vis_out,
    txt_in,
    txt_out,
    cotangent,
):
    n = lax.axis_size("dp") // 2
    own = w_query.shape[0]
    row_count, width = tokens.shape
    span = width // 4
    heads = span // HEAD_DIM
    gain_one, gain_two = gain_attn.reshape(1, own), gain_ffn.reshape(1, own)

    rows = 4 * SEQ
    scratch = dict(
        shard=pltpu.VMEM((5, 2, own, width), BF),
        bias=pltpu.VMEM((2, 8, SEQ), F32),
        x=pltpu.VMEM((2, SEQ, width), BF),
        dy=pltpu.VMEM((SEQ, width), BF),
        padded_out=pltpu.VMEM((2, SEQ, width), BF),
        gathered=pltpu.VMEM((5, width, width), BF),
        part=pltpu.VMEM((5, width, width), BF),
        land=pltpu.VMEM((5, 2, n - 1, own, width), BF),
        give=pltpu.VMEM((5, own, width), F32),
        x4=pltpu.VMEM((4, SEQ, width), BF),
        bias4=pltpu.VMEM((4, 8, SEQ), F32),
        n1=pltpu.VMEM((4, SEQ, width), BF),
        n1t=pltpu.VMEM((width, rows), BF),
        gz=pltpu.VMEM((4, SEQ, width), BF),
        turned=pltpu.VMEM((width, rows), BF),
        gztt=pltpu.VMEM((width, 4 * TXT), BF),
        wo=pltpu.VMEM((width, span), BF),
        q=pltpu.VMEM((4, SEQ, span), BF),
        k=pltpu.VMEM((4, SEQ, span), BF),
        v=pltpu.VMEM((4, SEQ, span), BF),
        c=pltpu.VMEM((4, SEQ, span), BF),
        probs=pltpu.VMEM((4 * heads, SEQ, SEQ), BF),
        pa=pltpu.VMEM((4, SEQ, width), BF),
        ra=pltpu.VMEM((2, SEQ, width), BF),
        xs=pltpu.VMEM((SEQ, width), BF),
        xr=pltpu.VMEM((SEQ, width), BF),
        y1=pltpu.VMEM((SEQ, width), F32),
        n2vt=pltpu.VMEM((width, 4 * VIS), BF),
        n2tt=pltpu.VMEM((width, 4 * TXT), BF),
        u=pltpu.VMEM((4 * VIS, 256), F32),
        gh=pltpu.VMEM((4 * VIS, 256), F32),
        hv=pltpu.VMEM((4 * VIS, width), BF),
        guv=pltpu.VMEM((4 * VIS, width), BF),
        ht=pltpu.VMEM((4 * TXT, width), BF),
        gut=pltpu.VMEM((4 * TXT, width), BF),
        pg=pltpu.VMEM((4, SEQ, width), BF),
        rg=pltpu.VMEM((2, SEQ, width), BF),
        xsg=pltpu.VMEM((SEQ, width), BF),
        xrg=pltpu.VMEM((SEQ, width), BF),
        gy=pltpu.VMEM((2, SEQ, width), BF),
        xsf=pltpu.VMEM((SEQ, width), BF),
        xrf=pltpu.VMEM((SEQ, width), BF),
        xsb=pltpu.VMEM((2, SEQ, width), BF),
        xrb=pltpu.VMEM((2, SEQ, width), BF),
        gs=pltpu.VMEM((2, own, 128), F32),
        gr=pltpu.VMEM((2, own, 128), F32),
        sent=pltpu.SemaphoreType.DMA((40,)),
        came=pltpu.SemaphoreType.DMA((40,)),
        ring_sent=pltpu.SemaphoreType.DMA((5 * 2 * (n - 1) * 2,)),
        ring_came=pltpu.SemaphoreType.DMA((5 * 2 * (n - 1) * 2,)),
    )
    inputs = dict(
        lengths=caption_lengths,
        tokens=tokens,
        cotangent=cotangent,
        gain_attn=gain_one,
        gain_ffn=gain_two,
        w_query=w_query,
        w_key=w_key,
        w_value=w_value,
        w_out=w_out,
        vis_in=vis_in,
        vis_out=vis_out,
        txt_in=txt_in,
        txt_out=txt_out,
    )
    results = dict(
        out_tokens=jax.ShapeDtypeStruct((row_count, width), BF),
        grad_tokens=jax.ShapeDtypeStruct((row_count, width), F32),
        gw=jax.ShapeDtypeStruct((5, 2, own, width), F32),
        gg=jax.ShapeDtypeStruct((2, own, 128), F32),
    )
    vmem = pl.BlockSpec(memory_space=pltpu.VMEM)
    names = tuple(inputs) + tuple(results) + tuple(scratch)
    out, gtok, gw, gg = pl.pallas_call(
        functools.partial(layer_kernel, n, names),
        out_shape=tuple(results.values()),
        in_specs=[pl.BlockSpec(memory_space=pltpu.SMEM)] + [vmem] * (len(inputs) - 1),
        out_specs=[vmem] * len(results),
        scratch_shapes=list(scratch.values()),
        compiler_params=pltpu.CompilerParams(
            collective_id=0, has_side_effects=True, vmem_limit_bytes=60 * 2**20
        ),
    )(*inputs.values())

    final = pl.pallas_call(
        finish_kernel,
        out_shape=(
            jax.ShapeDtypeStruct((row_count, width), BF),
            jax.ShapeDtypeStruct((row_count, width), F32),
            jax.ShapeDtypeStruct((1, own), F32),
            jax.ShapeDtypeStruct((own, 2 * span), F32),
            jax.ShapeDtypeStruct((own, 2 * span), F32),
            jax.ShapeDtypeStruct((own, 2 * span), F32),
            jax.ShapeDtypeStruct((2 * span, own), F32),
            jax.ShapeDtypeStruct((1, own), F32),
            jax.ShapeDtypeStruct((own, 2 * width), F32),
            jax.ShapeDtypeStruct((2 * width, own), F32),
            jax.ShapeDtypeStruct((own, 2 * width), F32),
            jax.ShapeDtypeStruct((2 * width, own), F32),
        ),
        in_specs=[pl.BlockSpec(memory_space=pl.ANY)] * 2 + [vmem] * 4,
        out_specs=[pl.BlockSpec(memory_space=pl.ANY)] * 2 + [vmem] * 10,
        scratch_shapes=[pltpu.SemaphoreType.DMA((2,))],
        compiler_params=pltpu.CompilerParams(vmem_limit_bytes=48 * 2**20),
    )(out, gtok, gw, gg, gain_one, gain_two)
    final = list(final)
    final[2] = final[2].reshape(own)
    final[7] = final[7].reshape(own)
    return tuple(final)


def norm_parts(values):
    center = values - jnp.mean(values, axis=-1, keepdims=True)
    spread = jnp.mean(center * center, axis=-1, keepdims=True)
    inverse = lax.rsqrt(spread + epsilon)
    return (center * inverse, inverse)


def norm_back(grad_out, normed, inverse, gain):
    grad_normed = grad_out * gain
    grad_gain = jnp.sum(grad_out * normed, axis=0)
    inner = (
        grad_normed
        - jnp.mean(grad_normed, axis=-1, keepdims=True)
        - normed * jnp.mean(grad_normed * normed, axis=-1, keepdims=True)
    )
    return (inverse * inner, grad_gain)


def matmul(left, right):
    return jnp.dot(left, right, preferred_element_type=jnp.float32)


def matmul_tn(left, right):
    return lax.dot_general(
        left, right, (((0,), (0,)), ((), ())), preferred_element_type=jnp.float32
    )


def matmul_nt(left, right):
    return lax.dot_general(
        left, right, (((1,), (1,)), ((), ())), preferred_element_type=jnp.float32
    )


def gelu_slope(pre):
    cumulative = 0.5 * (1.0 + lax.erf(pre * inv_root_two))
    density = jnp.exp(-0.5 * pre * pre) * inv_root_tau
    return cumulative + pre * density


def expert_forward(rows, weight_in, weight_out):
    pre = matmul(rows, weight_in)
    hidden = jax.nn.gelu(pre, approximate=False).astype(jnp.bfloat16)
    return (pre, hidden, matmul(hidden, weight_out))


def expert_backward(rows, pre, hidden, grad_out, weight_in, weight_out):
    grad_weight_out = matmul_tn(hidden, grad_out)
    grad_hidden = matmul_nt(grad_out, weight_out)
    grad_pre = (grad_hidden * gelu_slope(pre)).astype(jnp.bfloat16)
    return (matmul_tn(rows, grad_pre), grad_weight_out, matmul_nt(grad_pre, weight_in))


def join_experts(image_rows, text_rows, pair_count, width):
    joined = jnp.concatenate(
        [
            image_rows.reshape(pair_count, PATCHES, width),
            text_rows.reshape(pair_count, CAPTION, width),
        ],
        axis=1,
    )
    return joined.reshape(-1, width)


def plain_layer(
    tokens,
    caption_lengths,
    gain_attn,
    w_query,
    w_key,
    w_value,
    w_out,
    gain_ffn,
    vis_in,
    vis_out,
    txt_in,
    txt_out,
    cotangent,
):
    seq_len = PATCHES + CAPTION
    width = tokens.shape[1]
    pair_count = tokens.shape[0] // seq_len
    half_pairs = pair_count // lax.axis_size("tensor")
    half_rows = half_pairs * seq_len
    row_start = lax.axis_index("tensor") * half_rows
    gain_one, query_w, key_w, value_w, out_w = (
        lax.all_gather(gain_attn, "dp", axis=0, tiled=True),
        lax.all_gather(w_query, "dp", axis=0, tiled=True),
        lax.all_gather(w_key, "dp", axis=0, tiled=True),
        lax.all_gather(w_value, "dp", axis=0, tiled=True),
        lax.all_gather(w_out, "dp", axis=1, tiled=True),
    )
    gain_two, vis_in_w, vis_out_w, txt_in_w, txt_out_w = (
        lax.all_gather(gain_ffn, "dp", axis=0, tiled=True),
        lax.all_gather(vis_in, "dp", axis=0, tiled=True),
        lax.all_gather(vis_out, "dp", axis=1, tiled=True),
        lax.all_gather(txt_in, "dp", axis=0, tiled=True),
        lax.all_gather(txt_out, "dp", axis=1, tiled=True),
    )
    gain_one = gain_one.astype(jnp.float32)
    gain_two = gain_two.astype(jnp.float32)
    head_local = query_w.shape[1] // HEAD_DIM
    score_scale = HEAD_DIM ** (-0.5)
    position = jnp.arange(seq_len, dtype=jnp.int32)
    live = (position[None, :] < PATCHES) | (position[None, :] - PATCHES < caption_lengths[:, None])
    valid_rows = live.astype(jnp.float32)
    mask_col = valid_rows.reshape(-1, 1)
    key_live = valid_rows[:, None, None, :] > 0.5

    def own_rows(values):
        return lax.dynamic_slice_in_dim(values, row_start, half_rows, 0)

    inputs = tokens.astype(jnp.float32)
    normed_one, inverse_one = norm_parts(inputs)
    first_in = (normed_one * gain_one).astype(jnp.bfloat16)

    def project(weight):
        return (
            matmul(first_in, weight)
            .astype(jnp.bfloat16)
            .reshape(pair_count, seq_len, head_local, HEAD_DIM)
        )

    queries = project(query_w)
    keys_all = project(key_w)
    values_all = project(value_w)

    def score_block():
        raw = (
            jnp.einsum("pqhe,pkhe->phqk", queries, keys_all, preferred_element_type=jnp.float32)
            * score_scale
        )
        return jnp.where(key_live, raw, -1e30)

    scores = score_block()
    top = jnp.max(scores, axis=-1, keepdims=True)
    weights = jnp.exp(scores - top)
    total = jnp.sum(weights, axis=-1, keepdims=True)
    probs = (weights / total).astype(jnp.bfloat16)
    log_total = top + jnp.log(total)
    context = jnp.einsum("phqk,pkhe->pqhe", probs, values_all, preferred_element_type=jnp.float32)
    context = context.astype(jnp.bfloat16).reshape(-1, head_local * HEAD_DIM)
    attn_terms = matmul(context, out_w)
    attended_own = lax.psum_scatter(
        attn_terms.astype(jnp.bfloat16), "tensor", scatter_dimension=0, tiled=True
    ).astype(jnp.float32)
    mask_own = own_rows(mask_col)
    middle_own = own_rows(inputs) + mask_own * attended_own
    normed_two, inverse_two = norm_parts(middle_own)
    second_own = (normed_two * gain_two).astype(jnp.bfloat16)
    grid = lax.all_gather(second_own, "tensor", axis=0, tiled=True).reshape(
        pair_count, seq_len, width
    )
    image_rows = grid[:, :PATCHES].reshape(-1, width)
    text_rows = grid[:, PATCHES:].reshape(-1, width)
    image_pre, image_hidden, image_part = expert_forward(image_rows, vis_in_w, vis_out_w)
    text_pre, text_hidden, text_part = expert_forward(text_rows, txt_in_w, txt_out_w)
    image_own, text_own = (
        lax.psum_scatter(
            image_part.astype(jnp.bfloat16), "tensor", scatter_dimension=0, tiled=True
        ).astype(jnp.float32),
        lax.psum_scatter(
            text_part.astype(jnp.bfloat16), "tensor", scatter_dimension=0, tiled=True
        ).astype(jnp.float32),
    )
    branch_own = join_experts(image_own, text_own, half_pairs, width)
    output_own = (middle_own + mask_own * branch_own).astype(jnp.bfloat16)
    upstream = cotangent.astype(jnp.float32)
    grad_branch = (upstream * mask_col).astype(jnp.bfloat16).reshape(pair_count, seq_len, width)
    image_grads = expert_backward(
        image_rows,
        image_pre,
        image_hidden,
        grad_branch[:, :PATCHES].reshape(-1, width),
        vis_in_w,
        vis_out_w,
    )
    text_grads = expert_backward(
        text_rows,
        text_pre,
        text_hidden,
        grad_branch[:, PATCHES:].reshape(-1, width),
        txt_in_w,
        txt_out_w,
    )
    back_image_own, back_text_own = (
        lax.psum_scatter(
            image_grads[2].astype(jnp.bfloat16), "tensor", scatter_dimension=0, tiled=True
        ).astype(jnp.float32),
        lax.psum_scatter(
            text_grads[2].astype(jnp.bfloat16), "tensor", scatter_dimension=0, tiled=True
        ).astype(jnp.float32),
    )
    grad_second_own = join_experts(back_image_own, back_text_own, half_pairs, width)
    grad_norm_own, gain_part = norm_back(grad_second_own, normed_two, inverse_two, gain_two)
    grad_middle_own = own_rows(upstream) + grad_norm_own
    output_wide, grad_middle, gain_parts = (
        lax.all_gather(
            output_own.astype(jnp.float32).astype(jnp.bfloat16), "tensor", axis=0, tiled=True
        ).astype(jnp.float32),
        lax.all_gather(grad_middle_own.astype(jnp.bfloat16), "tensor", axis=0, tiled=True).astype(
            grad_middle_own.dtype
        ),
        lax.all_gather(gain_part.astype(jnp.bfloat16), "tensor", axis=0, tiled=True).astype(
            gain_part.dtype
        ),
    )
    output = output_wide.astype(jnp.bfloat16)
    grad_gain_two = jnp.sum(gain_parts.reshape(-1, width), axis=0)
    grad_attended = (grad_middle * mask_col).astype(jnp.bfloat16)
    grad_out_w = matmul_tn(context, grad_attended)
    grad_context = (
        matmul_nt(grad_attended, out_w)
        .astype(jnp.bfloat16)
        .reshape(pair_count, seq_len, head_local, HEAD_DIM)
    )
    scores_again = score_block()
    probs_exact = jnp.exp(scores_again - log_total)
    grad_probs = jnp.einsum(
        "pqhe,pkhe->phqk", grad_context, values_all, preferred_element_type=jnp.float32
    )
    inner = jnp.sum(grad_probs * probs_exact, axis=-1, keepdims=True)
    grad_scores = (probs_exact * (grad_probs - inner)).astype(jnp.bfloat16)
    grad_values = jnp.einsum(
        "phqk,pqhe->pkhe", probs, grad_context, preferred_element_type=jnp.float32
    )
    grad_values = grad_values.astype(jnp.bfloat16).reshape(-1, head_local * HEAD_DIM)
    grad_queries = (
        jnp.einsum("phqk,pkhe->pqhe", grad_scores, keys_all, preferred_element_type=jnp.float32)
        * score_scale
    )
    grad_queries = grad_queries.astype(jnp.bfloat16).reshape(-1, head_local * HEAD_DIM)
    grad_keys = (
        jnp.einsum("phqk,pqhe->pkhe", grad_scores, queries, preferred_element_type=jnp.float32)
        * score_scale
    )
    grad_keys = grad_keys.astype(jnp.bfloat16).reshape(-1, head_local * HEAD_DIM)
    grad_query_w = matmul_tn(first_in, grad_queries)
    grad_key_w = matmul_tn(first_in, grad_keys)
    grad_value_w = matmul_tn(first_in, grad_values)
    first_part = (
        matmul_nt(grad_queries, query_w)
        + matmul_nt(grad_keys, key_w)
        + matmul_nt(grad_values, value_w)
    )
    grad_first = lax.psum(first_part.astype(jnp.bfloat16), "tensor").astype(jnp.float32)
    grad_norm_one, grad_gain_one = norm_back(grad_first, normed_one, inverse_one, gain_one)
    grad_inputs = grad_middle + grad_norm_one
    attn_sent = (
        lax.psum_scatter(grad_gain_one, "dp", scatter_dimension=0, tiled=True),
        lax.psum_scatter(grad_query_w, "dp", scatter_dimension=0, tiled=True),
        lax.psum_scatter(grad_key_w, "dp", scatter_dimension=0, tiled=True),
        lax.psum_scatter(grad_value_w, "dp", scatter_dimension=0, tiled=True),
        lax.psum_scatter(grad_out_w, "dp", scatter_dimension=1, tiled=True),
    )
    final_expert = (
        lax.psum_scatter(grad_gain_two, "dp", scatter_dimension=0, tiled=True),
        lax.psum_scatter(image_grads[0], "dp", scatter_dimension=0, tiled=True),
        lax.psum_scatter(image_grads[1], "dp", scatter_dimension=1, tiled=True),
        lax.psum_scatter(text_grads[0], "dp", scatter_dimension=0, tiled=True),
        lax.psum_scatter(text_grads[1], "dp", scatter_dimension=1, tiled=True),
    )
    return (
        output,
        grad_inputs,
        attn_sent[0],
        attn_sent[1],
        attn_sent[2],
        attn_sent[3],
        attn_sent[4],
        final_expert[0],
        final_expert[1],
        final_expert[2],
        final_expert[3],
        final_expert[4],
    )


def solution(mesh):
    def local(tokens, lengths, gain, w_query, *rest):
        ring = mesh.shape["dp"] // 2
        fits = (
            mesh.shape["tensor"] == 2
            and ring == 8
            and lengths.shape[0] == 2
            and w_query.shape[0] % 16 == 0
        )
        layer = fused_layer if fits else plain_layer
        return layer(tokens, lengths, gain, w_query, *rest)

    return jax.shard_map(
        local,
        mesh=mesh,
        in_specs=(
            P("dp", None),
            P("dp"),
            P("dp"),
            P("dp", "tensor"),
            P("dp", "tensor"),
            P("dp", "tensor"),
            P("tensor", "dp"),
            P("dp"),
            P("dp", "tensor"),
            P("tensor", "dp"),
            P("dp", "tensor"),
            P("tensor", "dp"),
            P("dp", None),
        ),
        out_specs=(
            P("dp", None),
            P("dp", None),
            P("dp"),
            P("dp", "tensor"),
            P("dp", "tensor"),
            P("dp", "tensor"),
            P("tensor", "dp"),
            P("dp"),
            P("dp", "tensor"),
            P("tensor", "dp"),
            P("dp", "tensor"),
            P("tensor", "dp"),
        ),
        check_vma=False,
    )
```

```python
import functools
import math
import types

import jax
import jax.numpy as jnp
from jax import lax
from jax.experimental import pallas as pl
from jax.experimental.pallas import tpu as pltpu
from jax.sharding import PartitionSpec as P

HEAD_DIM = 64
PATCHES = 197
CAPTION = 40
VIS = 208
TXT = 48
SEQ = VIS + TXT

MESH = pl.DeviceIdType.MESH
BF = jnp.bfloat16
F32 = jnp.float32

ATT, TIN, TOUT, VIN, VOUT = range(5)

epsilon = 1e-05
inv_root_two = 1.0 / math.sqrt(2.0)
inv_root_tau = 1.0 / math.sqrt(2.0 * math.pi)


def mm(left, right):
    return jnp.dot(left, right, preferred_element_type=F32)


def mm_nt(left, right):
    return lax.dot_general(left, right, (((1,), (1,)), ((), ())), preferred_element_type=F32)


def mm_tn(left, right):
    return lax.dot_general(left, right, (((0,), (0,)), ((), ())), preferred_element_type=F32)


def normalize(values):
    center = values - jnp.mean(values, axis=-1, keepdims=True)
    spread = jnp.mean(center * center, axis=-1, keepdims=True)
    inverse = lax.rsqrt(spread + epsilon)
    return center * inverse, inverse


def normalize_back(grad_normed, normed, inverse):
    return inverse * (
        grad_normed
        - jnp.mean(grad_normed, axis=-1, keepdims=True)
        - normed * jnp.mean(grad_normed * normed, axis=-1, keepdims=True)
    )


def unit(size):
    rows = lax.broadcasted_iota(jnp.int32, (size, size), 0)
    return (rows == lax.broadcasted_iota(jnp.int32, (size, size), 1)).astype(F32).astype(BF)


def column(ref):
    size = ref.shape[1]
    return jnp.sum(unit(size).astype(F32) * ref[...].astype(F32), axis=1, keepdims=True)


class Events:
    def __init__(self):
        self.todo = []

    def add(self, *steps):
        self.todo.extend(steps)

    def advance(self, count):
        for _ in range(min(count, len(self.todo))):
            self.todo.pop(0)()

    def drain(self):
        self.advance(len(self.todo))


def layer_kernel(n, names, *refs):
    R = types.SimpleNamespace(**dict(zip(names, refs)))
    R.pb, R.pf, R.ga, R.rf, R.rb, R.n2 = R.pa, R.pg, R.x4, R.ra, R.rg, R.n1
    R.gat, R.gzvt, R.gqkv = R.turned, R.turned, R.n2
    S, BIAS = R.shard, R.bias
    OUT, GW, GG = R.padded_out, R.gw, R.gg
    G, PART, LAND = R.gathered, R.part, R.land
    width = G.shape[2]
    own = width // (2 * n)

    x = lax.axis_index("tensor")
    d = lax.axis_index("dp")
    c = lax.rem(d, 2)
    other = 1 - c
    chip = d // 2
    y, z = lax.rem(chip, 2), chip // 2
    r = z + y * (n - 1 - 2 * z)
    half = n // 2

    def chip_at(pos):
        pos = lax.rem(pos + 2 * n, n)
        upper = pos // half
        return 2 * (pos + upper * (n - 1 - 2 * pos)) + upper

    mate = {"dp": d + 1 - 2 * c}
    across = {"tensor": 1 - x}
    ahead = {"dp": 2 * chip_at(r + 1) + c}
    behind = {"dp": 2 * chip_at(r - 1) + c}
    way = (ahead, behind)

    def rows_at(pos, side):
        return pl.ds(pl.multiple_of(2 * own * chip_at(pos) + own * side, 16), own)

    my_rows = pl.ds(pl.multiple_of(own * d, 16), own)

    barrier = pltpu.get_barrier_semaphore()
    for device in (mate, across, ahead, behind):
        pl.semaphore_signal(barrier, inc=1, device_id=device, device_id_type=MESH)

    mine, theirs = pl.multiple_of(2 * c, 2), pl.multiple_of(2 * other, 2)
    pair_own = 2 * c + x
    pair_across = 2 * c + 1 - x

    started = []
    counter = [0]

    def remote(source, target, device, index=None):
        if index is None:
            index = counter[0]
            counter[0] += 1
        return pltpu.make_async_remote_copy(
            src_ref=source,
            dst_ref=target,
            send_sem=R.sent.at[index],
            recv_sem=R.came.at[index],
            device_id=device,
            device_id_type=MESH,
        )

    def start(source, target, device):
        copy = remote(source, target, device)
        copy.start()
        started.append(copy)
        return copy

    def sent(copy):
        copy.wait_send()
        started[:] = [one for one in started if one is not copy]

    span = width // 4

    def shard_part(k, value):
        for core in range(2):
            S[k, core] = value(core).astype(BF)

    gain_one, gain_two = column(R.gain_attn), column(R.gain_ffn)

    def attention_part(core):
        cols = slice(core * span, (core + 1) * span)
        return jnp.concatenate(
            [
                R.w_query[:, cols].astype(F32) * (gain_one * HEAD_DIM**-0.5),
                R.w_key[:, cols].astype(F32) * gain_one,
                R.w_value[:, cols].astype(F32) * gain_one,
                R.w_out[:, cols].astype(F32),
            ],
            axis=1,
        )

    def half_of(ref, core):
        return ref[:, core * width : (core + 1) * width].astype(F32) * gain_two

    def turned_half(ref, core):
        return ref[:, core * width : (core + 1) * width]

    shard_part(ATT, attention_part)
    pl.semaphore_wait(barrier, 4)
    shard_a = start(S.at[pl.ds(0, 1), other], G.at[pl.ds(0, 1), my_rows, :], mate)
    G[ATT, my_rows, :] = S[ATT, c]
    shard_part(TIN, functools.partial(half_of, R.txt_in))
    shard_part(TOUT, functools.partial(turned_half, R.txt_out))
    shard_part(VIN, functools.partial(half_of, R.vis_in))
    shard_part(VOUT, functools.partial(turned_half, R.vis_out))
    shard_b = start(S.at[pl.ds(1, 4), other], G.at[pl.ds(1, 4), my_rows, :], mate)
    for k in (TIN, TOUT, VIN, VOUT):
        G[k, my_rows, :] = S[k, c]

    lengths = R.lengths

    def live(t, slots):
        return (slots < PATCHES) | ((slots >= VIS) & (slots < VIS + lengths[t]))

    def live_rows(t, j, count=64):
        slots = lax.broadcasted_iota(jnp.int32, (count, 1), 0) + j * count
        return live(t, slots).astype(F32)

    row_count = R.tokens.shape[0]

    def placed(t, slots, rows, kept):
        source = t * (PATCHES + CAPTION) + slots - (slots >= VIS).astype(jnp.int32) * (VIS - PATCHES)
        return ((rows == source) & kept).astype(F32).astype(BF)

    def chooser(t, only_live):
        slots = lax.broadcasted_iota(jnp.int32, (SEQ, row_count), 0)
        rows = lax.broadcasted_iota(jnp.int32, (SEQ, row_count), 1)
        filled = (slots < PATCHES) | ((slots >= VIS) & (slots < VIS + CAPTION))
        return placed(t, slots, rows, live(t, slots) if only_live else filled)

    for t in range(2):
        R.x4[2 * c + t] = mm(chooser(t, False), R.tokens[...]).astype(BF)
        slots = lax.broadcasted_iota(jnp.int32, (8, SEQ), 1)
        BIAS[t] = jnp.where(live(t, slots), 0.0, -1e30)
        R.bias4[2 * c + t] = BIAS[t]
    send_x = start(R.x4.at[pl.ds(mine, 2)], R.x4.at[pl.ds(mine, 2)], mate)
    send_bias = start(BIAS, R.bias4.at[pl.ds(mine, 2)], mate)

    near, far = (ATT, 0, width // 2), (ATT, width // 2, width // 2)
    parts = [near, far] + [(k, 0, width) for k in (TIN, TOUT, VIN, VOUT)]
    attention = (near, far)
    text, image = parts[2:4], parts[4:]

    def gather_index(part, side, s):
        return (parts.index(part) * 2 + side) * (n - 1) + s

    def view(ref, part, rows):
        k, first, count = part
        return ref.at[k, rows, pl.ds(first, count)]

    def gather_copy(part, side, s, pos):
        block = view(G, part, rows_at(pos, side))
        i = gather_index(part, side, s)
        return pltpu.make_async_remote_copy(
            src_ref=block,
            dst_ref=block,
            send_sem=R.ring_sent.at[i],
            recv_sem=R.ring_came.at[i],
            device_id=way[side],
            device_id_type=MESH,
        )

    def gather_step(group, s):
        for part in group:
            for side in range(2):
                pos = r - s if side == 0 else r + s
                if not (isinstance(s, int) and s == 0):
                    gather_copy(part, side, s - 1, pos).wait_recv()
                if not (isinstance(s, int) and s == n - 1):
                    gather_copy(part, side, s, pos).start()

    sum_base = len(parts) * 2 * (n - 1)

    def landed(part, side, s):
        k, first, count = part
        return LAND.at[k, side, s, :, pl.ds(first, count)]

    def sum_copy(part, side, s, source):
        i = sum_base + gather_index(part, side, s)
        return pltpu.make_async_remote_copy(
            src_ref=source,
            dst_ref=landed(part, side, s),
            send_sem=R.ring_sent.at[i],
            recv_sem=R.ring_came.at[i],
            device_id=way[side],
            device_id_type=MESH,
        )

    def sum_step(group, s):
        for part in group:
            for side in range(2):
                pos = r - 1 - s if side == 0 else r + 1 + s
                term = view(PART, part, rows_at(pos, side))
                if isinstance(s, int) and s == 0:
                    source = term
                else:
                    source = landed(part, side, s - 1)
                    sum_copy(part, side, s - 1, source).wait_recv()
                    source[...] = (source[...].astype(F32) + term[...].astype(F32)).astype(BF)
                sum_copy(part, side, s, source).start()

    finals = []

    def sum_last(group):
        for part in group:
            for side in range(2):
                sum_copy(part, side, n - 2, landed(part, side, n - 2)).wait_recv()
        for k in sorted({part[0] for part in group}):

            def total(core):
                rows = pl.ds(pl.multiple_of(2 * own * chip + own * core, 16), own)
                return LAND[k, core, n - 2].astype(F32) + PART[k, rows, :].astype(F32)

            R.give[k] = total(other)
            finals.append(start(R.give.at[k], GW.at[k, c], mate))
            GW[k, c] = total(c)

    shard_a.wait_recv()
    gather_step(attention, 0)
    for t in range(2):
        R.gz[2 * c + t] = mm(chooser(t, True), R.cotangent[...]).astype(BF)
    send_gz = start(R.gz.at[pl.ds(mine, 2)], R.gz.at[pl.ds(mine, 2)], mate)
    R.dy[...] = mm(chooser(x, False), R.cotangent[...]).astype(BF)
    for t in range(2):
        R.x[t] = R.x4[2 * c + t]
    send_x.wait_recv()

    ring = Events()
    for s in range(1, n - 1):
        ring.add(functools.partial(gather_step, attention, s))

    for i in range(4):

        @pl.loop(0, SEQ // 64, unroll=True)
        def _(j, i=i):
            rows = pl.ds(pl.multiple_of(j * 64, 64), 64)
            normed, _ = normalize(R.x4[i, rows, :].astype(F32))
            R.n1[i, rows, :] = normed.astype(BF)

        R.n1t[:, i * SEQ : (i + 1) * SEQ] = R.n1[i].T
        ring.advance(1)
    send_gz.wait_recv()
    send_bias.wait_recv()
    ring.advance(1)

    @pl.loop(0, width // 256)
    def _(j):
        cols = pl.ds(pl.multiple_of(j * 256, 256), 256)
        R.gzvt[cols, : 4 * VIS] = R.gz[:, :VIS, cols].reshape(4 * VIS, 256).T
        R.gztt[cols, :] = R.gz[:, VIS:, cols].reshape(4 * TXT, 256).T

    ring.drain()
    shard_b.wait_recv()
    gather_step(text, 0)
    gather_step(attention, n - 1)

    heads = span // HEAD_DIM
    R.wo[...] = G[ATT][:, 3 * span :]

    @pl.loop(0, 4)
    def _(i):
        projected = mm(R.n1[i], G[ATT][:, : 3 * span]).astype(BF)
        R.q[i] = projected[:, :span]
        R.k[i] = projected[:, span : 2 * span]
        R.v[i] = projected[:, 2 * span :]

    lane = lax.broadcasted_iota(jnp.int32, (1, span), 1) // HEAD_DIM

    def only(head, values):
        return values * (lane == head).astype(F32).astype(BF)

    gather_step(text, 1)

    base = counter[0]
    counter[0] += 2

    def pair_order(j):
        core = other + (j // 2) * (c - other)
        turn = (1 - x) + lax.rem(j, 2) * (2 * x - 1)
        return core, turn, 2 * core + turn

    def forward_copy(j, turn, i):
        return remote(R.pa.at[i], R.ra.at[turn], mate, base + j)

    cross_a = remote(R.xs, R.xr, across)

    @pl.loop(0, 4)
    def _(j):
        core, turn, i = pair_order(j)
        q, k, v = R.q[i], R.k[i], R.v[i]
        context = jnp.zeros((SEQ, span), F32)
        for h in range(heads):
            scores = mm_nt(q, only(h, k)) + R.bias4[i][:1, :]
            top = jnp.max(scores, axis=-1, keepdims=True)
            weights = jnp.exp(scores - top)
            total = jnp.sum(weights, axis=-1, keepdims=True)
            probs = (weights * (1.0 / total)).astype(BF)
            R.probs[i * heads + h] = probs
            context += mm(probs, only(h, v))
        context = context.astype(BF)
        R.c[i] = context
        R.pa[i] = mm_nt(context, R.wo[...]).astype(BF)

        @pl.when(j < 2)
        def _():
            forward_copy(j, turn, i).start()

        @pl.when(j == 2)
        def _():
            forward_copy(0, 1 - x, pair_across).wait_recv()
            R.xs[...] = (
                R.pa[pair_across].astype(F32) + R.ra[1 - x].astype(F32)
            ).astype(BF)
            cross_a.start()

        gather_step(text, 2 + j)

    started.append(cross_a)
    for j in range(2):
        core, turn, i = pair_order(j)
        forward_copy(j, turn, i).wait_send()
    forward_copy(1, x, pair_own).wait_recv()
    gather_step(text, n - 2)
    gather_step(image, 0)
    cross_a.wait_recv()

    @pl.loop(0, SEQ // 64, unroll=True)
    def _(j):
        rows = pl.ds(pl.multiple_of(j * 64, 64), 64)
        attended = (
            R.pa[pair_own, rows, :].astype(F32)
            + R.ra[x, rows, :].astype(F32)
            + R.xr[rows, :].astype(F32)
        )
        alive = live_rows(x, j)
        middle = R.x[x, rows, :].astype(F32) + alive * attended
        R.y1[rows, :] = middle
        normed, _ = normalize(middle)
        R.n2[pair_own, rows, :] = normed.astype(BF)

    def spread(ref):
        block = ref.at[pair_own]
        to_across = start(block, block, across)
        to_mate = start(block, block, mate)
        return to_across, to_mate

    to_across, to_mate = spread(R.n2)
    gather_step(text, n - 1)
    gather_step(image, 1)
    gather_step(image, 2)
    gather_step(image, 3)
    to_across.wait_recv()
    block = R.n2.at[pair_across]
    passed = start(block, block, mate)
    to_mate.wait_recv()
    passed.wait_recv()

    gather_step(image, 4)

    def expert(low, high, w_in, w_out, h_ref, gu_ref, after):
        per = high - low
        total_rows = 4 * per
        step = 64

        def run(j):
            cols = pl.ds(pl.multiple_of(j * 256, 256), 256)
            R.u[:total_rows, :] = mm(
                R.n2[:, low:high, :].reshape(total_rows, width), G[w_in, :, cols]
            )
            R.gh[:total_rows, :] = mm(
                R.gz[:, low:high, :].reshape(total_rows, width), G[w_out, :, cols]
            )

            @pl.loop(0, total_rows // step, unroll=2 if total_rows % 128 == 0 else 1)
            def _(i):
                rows = pl.ds(pl.multiple_of(i * step, step), step)
                pre = R.u[rows, :]
                cumulative = 0.5 * (1.0 + lax.erf(pre * inv_root_two))
                density = jnp.exp(-0.5 * pre * pre) * inv_root_tau
                h_ref[rows, cols] = (pre * cumulative).astype(BF)
                gu_ref[rows, cols] = (R.gh[rows, :] * (cumulative + pre * density)).astype(BF)

            after(j)

        pl.loop(0, width // 256)(run)

    def weight_grad(k, turned, ref):
        @pl.loop(0, width // 256)
        def _(j):
            cols = pl.ds(pl.multiple_of(j * 256, 256), 256)
            PART[k, :, cols] = mm(turned, ref[:, cols]).astype(BF)

    expert(VIS, SEQ, TIN, TOUT, R.ht, R.gut, lambda j: None)
    gather_step(image, 5)
    weight_grad(TOUT, R.gztt[...], R.ht)
    sum_step(text[1:], 0)

    @pl.loop(0, width // 256)
    def _(j):
        cols = pl.ds(pl.multiple_of(j * 256, 256), 256)
        R.n2vt[cols, :] = R.n2[:, :VIS, cols].reshape(4 * VIS, 256).T
        R.n2tt[cols, :] = R.n2[:, VIS:, cols].reshape(4 * TXT, 256).T

    gather_step(image, n - 2)
    weight_grad(TIN, R.n2tt[...], R.gut)
    sum_step(text[:1], 0)
    gather_step(image, n - 1)

    def vis_after(j):
        sum_step(text, 1 + j)

    expert(0, VIS, VIN, VOUT, R.hv, R.guv, vis_after)

    def terms(target, hv, ht, w_vis, w_txt, first):
        vis_rows = pl.ds(pl.multiple_of(first * VIS, 16), 2 * VIS)
        txt_rows = pl.ds(pl.multiple_of(first * TXT, 16), 2 * TXT)
        vis_part = mm_nt(hv[vis_rows, :], G[w_vis]).astype(BF)
        target[pl.ds(first, 2), :VIS, :] = vis_part.reshape(2, VIS, width)
        txt_part = mm_nt(ht[txt_rows, :], G[w_txt]).astype(BF)
        target[pl.ds(first, 2), VIS:, :] = txt_part.reshape(2, TXT, width)

    terms(R.pg, R.guv, R.gut, VIN, TIN, theirs)
    mate_g = start(R.pg.at[pl.ds(theirs, 2)], R.rg, mate)
    sum_step(text, 4)
    terms(R.pg, R.guv, R.gut, VIN, TIN, mine)
    mate_g.wait_recv()
    R.xsg[...] = (R.pg[pair_across].astype(F32) + R.rg[1 - x].astype(F32)).astype(BF)
    cross_g = start(R.xsg, R.xrg, across)
    sum_step(text, 5)
    weight_grad(VOUT, R.gzvt[:, : 4 * VIS], R.hv)
    sum_step(image[1:], 0)
    sum_step(text, 6)
    weight_grad(VIN, R.n2vt[...], R.guv)
    sum_step(image[:1], 0)
    cross_g.wait_recv()
    for copy in (send_x, to_across, to_mate, passed):
        sent(copy)

    @pl.loop(0, SEQ // 64, unroll=True)
    def _(j):
        rows = pl.ds(pl.multiple_of(j * 64, 64), 64)
        grad_normed = (
            R.pg[pair_own, rows, :].astype(F32)
            + R.rg[x, rows, :].astype(F32)
            + R.xrg[rows, :].astype(F32)
        )
        normed, inverse = normalize(R.y1[rows, :])
        grad = R.dy[rows, :].astype(F32) + normalize_back(grad_normed, normed, inverse)
        R.gy[x, rows, :] = grad.astype(BF)
        alive = live_rows(x, j)
        R.ga[pair_own, rows, :] = (grad * alive).astype(BF)

    gy_across = start(R.gy.at[x], R.gy.at[x], across)
    gy_mate = start(R.ga.at[pair_own], R.ga.at[pair_own], mate)
    sum_last(text)
    sum_step(image, 1)

    sent(mate_g)
    terms(R.pf, R.hv, R.ht, VOUT, TOUT, theirs)
    mate_f = start(R.pf.at[pl.ds(theirs, 2)], R.rf, mate)
    sum_step(image, 2)
    gy_across.wait_recv()

    @pl.loop(0, SEQ // 64, unroll=True)
    def _(j):
        rows = pl.ds(pl.multiple_of(j * 64, 64), 64)
        alive = live_rows(1 - x, j)
        R.ga[pair_across, rows, :] = (R.gy[1 - x, rows, :].astype(F32) * alive).astype(BF)

    block = R.ga.at[pair_across]
    gy_passed = start(block, block, mate)
    terms(R.pf, R.hv, R.ht, VOUT, TOUT, mine)
    mate_f.wait_recv()
    R.xsf[...] = (R.pf[pair_across].astype(F32) + R.rf[1 - x].astype(F32)).astype(BF)
    cross_f = start(R.xsf, R.xrf, across)
    gy_mate.wait_recv()
    gy_passed.wait_recv()

    base_back = counter[0]
    counter[0] += 2

    def back_copy(j, turn, i):
        return remote(R.pb.at[i], R.rb.at[turn], mate, base_back + j)

    base_cross = counter[0]
    counter[0] += 2

    def back_cross(j, turn):
        return remote(R.xsb.at[turn], R.xrb.at[turn], across, base_cross + j)

    @pl.loop(0, 4)
    def _(j):
        core, turn, i = pair_order(j)
        grad_context = mm(R.ga[i], R.wo[...]).astype(BF)
        R.gat[:, pl.ds(pl.multiple_of(i * SEQ, SEQ), SEQ)] = R.ga[i].T
        q, k, v = R.q[i], R.k[i], R.v[i]
        grad_q = jnp.zeros((SEQ, span), F32)
        grad_k = jnp.zeros((SEQ, span), F32)
        grad_v = jnp.zeros((SEQ, span), F32)
        for h in range(heads):
            probs = R.probs[i * heads + h]
            grad_probs = mm_nt(grad_context, only(h, v))
            exact = probs.astype(F32)
            inner = jnp.sum(grad_probs * exact, axis=-1, keepdims=True)
            grad_scores = (exact * (grad_probs - inner)).astype(BF)
            grad_q += mm(grad_scores, only(h, k))
            grad_k += mm_tn(grad_scores, only(h, q))
            grad_v += mm_tn(probs, only(h, grad_context))
        joined = jnp.concatenate([grad_q, grad_k, grad_v], axis=1).astype(BF)
        R.gqkv[i, :, : 3 * span] = joined
        R.pb[i] = mm_nt(joined, G[ATT][:, : 3 * span]).astype(BF)

        @pl.when(j < 2)
        def _():
            back_copy(j, turn, i).start()

        @pl.when(j >= 2)
        def _():
            back_copy(j - 2, turn, i).wait_recv()
            R.xsb[turn] = (
                R.pb[i].astype(F32) + R.rb[turn].astype(F32)
            ).astype(BF)
            back_cross(j - 2, turn).start()

        sum_step(image, 3 + j)

    for j in range(2):
        core, turn, i = pair_order(j)
        started.append(back_copy(j, turn, i))
        started.append(back_cross(j, turn))

    @pl.loop(0, 3)
    def _(j):
        cols = pl.ds(pl.multiple_of(j * 256, 256), 256)
        rows = pl.ds(pl.multiple_of(j * 256, 256), 256)
        grads = mm(R.n1t[rows, :], R.gqkv[:, :, : 3 * span].reshape(4 * SEQ, 3 * span))
        grad_o = mm(R.gat[rows, :], R.c[...].reshape(4 * SEQ, span))
        PART[ATT, rows, :] = jnp.concatenate([grads, grad_o], axis=1).astype(BF)

    sum_step(attention, 0)
    sum_last(image)

    cross_f.wait_recv()

    @pl.loop(0, SEQ // 64, unroll=True)
    def _(j):
        rows = pl.ds(pl.multiple_of(j * 64, 64), 64)
        branch = (
            R.pf[pair_own, rows, :].astype(F32)
            + R.rf[x, rows, :].astype(F32)
            + R.xrf[rows, :].astype(F32)
        )
        alive = live_rows(x, j)
        OUT[x, rows, :] = (R.y1[rows, :] + alive * branch).astype(BF)

    out_across = start(OUT.at[x], OUT.at[x], across)
    for s in range(1, 3):
        sum_step(attention, s)

    for j in range(2):
        back_cross(j, x if j == 0 else 1 - x).wait_recv()
    for t in range(2):

        @pl.loop(0, SEQ // 64, unroll=True)
        def _(j, t=t):
            rows = pl.ds(pl.multiple_of(j * 64, 64), 64)
            grad_normed = R.xsb[t, rows, :].astype(F32) + R.xrb[t, rows, :].astype(F32)
            normed, inverse = normalize(R.x[t, rows, :].astype(F32))
            grad = R.gy[t, rows, :].astype(F32) + normalize_back(grad_normed, normed, inverse)
            high = grad.astype(BF)
            rows = pl.ds(pl.multiple_of(t * SEQ + j * 64, 64), 64)
            R.hv[rows, :] = high
            R.guv[rows, :] = (grad - high.astype(F32)).astype(BF)

        sum_step(attention, 3 + 2 * t)
        sum_step(attention, 4 + 2 * t)

    slots = lax.broadcasted_iota(jnp.int32, (row_count, 2 * SEQ), 1)
    rows = lax.broadcasted_iota(jnp.int32, (row_count, 2 * SEQ), 0)
    turn = slots // SEQ
    back = placed(turn, slots - turn * SEQ, rows, slots >= 0)
    out_across.wait_recv()
    R.out_tokens[...] = mm(back, OUT[...].reshape(2 * SEQ, width)).astype(BF)
    R.grad_tokens[...] = mm(back, R.hv[: 2 * SEQ, :]) + mm(back, R.guv[: 2 * SEQ, :])
    sum_last(attention)
    for copy in finals:
        copy.wait_recv()

    def row_sums(k, last):
        return sum(
            jnp.sum(
                S[k, core][:, :last].astype(F32) * GW[k, core][:, :last], axis=-1, keepdims=True
            )
            for core in range(2)
        )

    R.gs[0] = jnp.broadcast_to(row_sums(ATT, 3 * span), (own, 128))
    R.gs[1] = jnp.broadcast_to(row_sums(TIN, width) + row_sums(VIN, width), (own, 128))
    cross_gain = start(R.gs, R.gr, across)
    cross_gain.wait_recv()
    GG[...] = R.gs[...] + R.gr[...]

    for copy in started:
        copy.wait_send()
    for part in parts:
        for side in range(2):
            for s in range(n - 1):
                gather_copy(part, side, s, r).wait_send()
                sum_copy(part, side, s, landed(part, side, s)).wait_send()


def finish_kernel(out, gtok, gw, gg, gain_attn, gain_ffn, *rest):
    (
        out_tokens,
        grad_tokens,
        grad_gain_attn,
        grad_query,
        grad_key,
        grad_value,
        grad_out,
        grad_gain_ffn,
        grad_vis_in,
        grad_vis_out,
        grad_txt_in,
        grad_txt_out,
        sems,
    ) = rest
    copies = [
        pltpu.make_async_copy(out, out_tokens, sems.at[0]),
        pltpu.make_async_copy(gtok, grad_tokens, sems.at[1]),
    ]
    for copy in copies:
        copy.start()
    width = gw.shape[3]
    own = gw.shape[2]
    span = width // 4
    gain_one, gain_two = column(gain_attn), column(gain_ffn)
    square = unit(own).astype(F32)
    grad_gain_attn[...] = jnp.sum(square * (gg[0][:, :1] / gain_one), axis=0, keepdims=True)
    grad_gain_ffn[...] = jnp.sum(square * (gg[1][:, :1] / gain_two), axis=0, keepdims=True)

    def both(part):
        return jnp.concatenate([gw[ATT, core][:, part * span : (part + 1) * span] for core in range(2)], axis=1)

    grad_query[...] = both(0) * (gain_one * HEAD_DIM**-0.5)
    grad_key[...] = both(1) * gain_one
    grad_value[...] = both(2) * gain_one
    grad_out[...] = both(3)
    for core in range(2):
        part = slice(core * width, (core + 1) * width)
        grad_vis_in[:, part] = gw[VIN, core] * gain_two
        grad_txt_in[:, part] = gw[TIN, core] * gain_two
        grad_vis_out[:, part] = gw[VOUT, core]
        grad_txt_out[:, part] = gw[TOUT, core]
    for copy in copies:
        copy.wait()


def fused_layer(
    tokens,
    caption_lengths,
    gain_attn,
    w_query,
    w_key,
    w_value,
    w_out,
    gain_ffn,
    vis_in,
    vis_out,
    txt_in,
    txt_out,
    cotangent,
):
    n = lax.axis_size("dp") // 2
    own = w_query.shape[0]
    row_count, width = tokens.shape
    span = width // 4
    heads = span // HEAD_DIM
    gain_one, gain_two = gain_attn.reshape(1, own), gain_ffn.reshape(1, own)

    rows = 4 * SEQ
    scratch = dict(
        shard=pltpu.VMEM((5, 2, own, width), BF),
        bias=pltpu.VMEM((2, 8, SEQ), F32),
        x=pltpu.VMEM((2, SEQ, width), BF),
        dy=pltpu.VMEM((SEQ, width), BF),
        padded_out=pltpu.VMEM((2, SEQ, width), BF),
        gathered=pltpu.VMEM((5, width, width), BF),
        part=pltpu.VMEM((5, width, width), BF),
        land=pltpu.VMEM((5, 2, n - 1, own, width), BF),
        give=pltpu.VMEM((5, own, width), F32),
        x4=pltpu.VMEM((4, SEQ, width), BF),
        bias4=pltpu.VMEM((4, 8, SEQ), F32),
        n1=pltpu.VMEM((4, SEQ, width), BF),
        n1t=pltpu.VMEM((width, rows), BF),
        gz=pltpu.VMEM((4, SEQ, width), BF),
        turned=pltpu.VMEM((width, rows), BF),
        gztt=pltpu.VMEM((width, 4 * TXT), BF),
        wo=pltpu.VMEM((width, span), BF),
        q=pltpu.VMEM((4, SEQ, span), BF),
        k=pltpu.VMEM((4, SEQ, span), BF),
        v=pltpu.VMEM((4, SEQ, span), BF),
        c=pltpu.VMEM((4, SEQ, span), BF),
        probs=pltpu.VMEM((4 * heads, SEQ, SEQ), BF),
        pa=pltpu.VMEM((4, SEQ, width), BF),
        ra=pltpu.VMEM((2, SEQ, width), BF),
        xs=pltpu.VMEM((SEQ, width), BF),
        xr=pltpu.VMEM((SEQ, width), BF),
        y1=pltpu.VMEM((SEQ, width), F32),
        n2vt=pltpu.VMEM((width, 4 * VIS), BF),
        n2tt=pltpu.VMEM((width, 4 * TXT), BF),
        u=pltpu.VMEM((4 * VIS, 256), F32),
        gh=pltpu.VMEM((4 * VIS, 256), F32),
        hv=pltpu.VMEM((4 * VIS, width), BF),
        guv=pltpu.VMEM((4 * VIS, width), BF),
        ht=pltpu.VMEM((4 * TXT, width), BF),
        gut=pltpu.VMEM((4 * TXT, width), BF),
        pg=pltpu.VMEM((4, SEQ, width), BF),
        rg=pltpu.VMEM((2, SEQ, width), BF),
        xsg=pltpu.VMEM((SEQ, width), BF),
        xrg=pltpu.VMEM((SEQ, width), BF),
        gy=pltpu.VMEM((2, SEQ, width), BF),
        xsf=pltpu.VMEM((SEQ, width), BF),
        xrf=pltpu.VMEM((SEQ, width), BF),
        xsb=pltpu.VMEM((2, SEQ, width), BF),
        xrb=pltpu.VMEM((2, SEQ, width), BF),
        gs=pltpu.VMEM((2, own, 128), F32),
        gr=pltpu.VMEM((2, own, 128), F32),
        sent=pltpu.SemaphoreType.DMA((40,)),
        came=pltpu.SemaphoreType.DMA((40,)),
        ring_sent=pltpu.SemaphoreType.DMA((6 * 2 * (n - 1) * 2,)),
        ring_came=pltpu.SemaphoreType.DMA((6 * 2 * (n - 1) * 2,)),
    )
    inputs = dict(
        lengths=caption_lengths,
        tokens=tokens,
        cotangent=cotangent,
        gain_attn=gain_one,
        gain_ffn=gain_two,
        w_query=w_query,
        w_key=w_key,
        w_value=w_value,
        w_out=w_out.T,
        vis_in=vis_in,
        vis_out=vis_out.T,
        txt_in=txt_in,
        txt_out=txt_out.T,
    )
    results = dict(
        out_tokens=jax.ShapeDtypeStruct((row_count, width), BF),
        grad_tokens=jax.ShapeDtypeStruct((row_count, width), F32),
        gw=jax.ShapeDtypeStruct((5, 2, own, width), F32),
        gg=jax.ShapeDtypeStruct((2, own, 128), F32),
    )
    vmem = pl.BlockSpec(memory_space=pltpu.VMEM)
    names = tuple(inputs) + tuple(results) + tuple(scratch)
    out, gtok, gw, gg = pl.pallas_call(
        functools.partial(layer_kernel, n, names),
        out_shape=tuple(results.values()),
        in_specs=[pl.BlockSpec(memory_space=pltpu.SMEM)] + [vmem] * (len(inputs) - 1),
        out_specs=[vmem] * len(results),
        scratch_shapes=list(scratch.values()),
        compiler_params=pltpu.CompilerParams(
            collective_id=0, has_side_effects=True, vmem_limit_bytes=60 * 2**20
        ),
    )(*inputs.values())

    final = pl.pallas_call(
        finish_kernel,
        out_shape=(
            jax.ShapeDtypeStruct((row_count, width), BF),
            jax.ShapeDtypeStruct((row_count, width), F32),
            jax.ShapeDtypeStruct((1, own), F32),
            jax.ShapeDtypeStruct((own, 2 * span), F32),
            jax.ShapeDtypeStruct((own, 2 * span), F32),
            jax.ShapeDtypeStruct((own, 2 * span), F32),
            jax.ShapeDtypeStruct((own, 2 * span), F32),
            jax.ShapeDtypeStruct((1, own), F32),
            jax.ShapeDtypeStruct((own, 2 * width), F32),
            jax.ShapeDtypeStruct((own, 2 * width), F32),
            jax.ShapeDtypeStruct((own, 2 * width), F32),
            jax.ShapeDtypeStruct((own, 2 * width), F32),
        ),
        in_specs=[pl.BlockSpec(memory_space=pl.ANY)] * 2 + [vmem] * 4,
        out_specs=[pl.BlockSpec(memory_space=pl.ANY)] * 2 + [vmem] * 10,
        scratch_shapes=[pltpu.SemaphoreType.DMA((2,))],
        compiler_params=pltpu.CompilerParams(vmem_limit_bytes=60 * 2**20),
    )(out, gtok, gw, gg, gain_one, gain_two)
    final = list(final)
    final[2] = final[2].reshape(own)
    final[7] = final[7].reshape(own)
    for turned in (6, 9, 11):
        final[turned] = final[turned].T
    return tuple(final)


def norm_parts(values):
    center = values - jnp.mean(values, axis=-1, keepdims=True)
    spread = jnp.mean(center * center, axis=-1, keepdims=True)
    inverse = lax.rsqrt(spread + epsilon)
    return (center * inverse, inverse)


def norm_back(grad_out, normed, inverse, gain):
    grad_normed = grad_out * gain
    grad_gain = jnp.sum(grad_out * normed, axis=0)
    inner = (
        grad_normed
        - jnp.mean(grad_normed, axis=-1, keepdims=True)
        - normed * jnp.mean(grad_normed * normed, axis=-1, keepdims=True)
    )
    return (inverse * inner, grad_gain)


def matmul(left, right):
    return jnp.dot(left, right, preferred_element_type=jnp.float32)


def matmul_tn(left, right):
    return lax.dot_general(
        left, right, (((0,), (0,)), ((), ())), preferred_element_type=jnp.float32
    )


def matmul_nt(left, right):
    return lax.dot_general(
        left, right, (((1,), (1,)), ((), ())), preferred_element_type=jnp.float32
    )


def gelu_slope(pre):
    cumulative = 0.5 * (1.0 + lax.erf(pre * inv_root_two))
    density = jnp.exp(-0.5 * pre * pre) * inv_root_tau
    return cumulative + pre * density


def expert_forward(rows, weight_in, weight_out):
    pre = matmul(rows, weight_in)
    hidden = jax.nn.gelu(pre, approximate=False).astype(jnp.bfloat16)
    return (pre, hidden, matmul(hidden, weight_out))


def expert_backward(rows, pre, hidden, grad_out, weight_in, weight_out):
    grad_weight_out = matmul_tn(hidden, grad_out)
    grad_hidden = matmul_nt(grad_out, weight_out)
    grad_pre = (grad_hidden * gelu_slope(pre)).astype(jnp.bfloat16)
    return (matmul_tn(rows, grad_pre), grad_weight_out, matmul_nt(grad_pre, weight_in))


def join_experts(image_rows, text_rows, pair_count, width):
    joined = jnp.concatenate(
        [
            image_rows.reshape(pair_count, PATCHES, width),
            text_rows.reshape(pair_count, CAPTION, width),
        ],
        axis=1,
    )
    return joined.reshape(-1, width)


def plain_layer(
    tokens,
    caption_lengths,
    gain_attn,
    w_query,
    w_key,
    w_value,
    w_out,
    gain_ffn,
    vis_in,
    vis_out,
    txt_in,
    txt_out,
    cotangent,
):
    seq_len = PATCHES + CAPTION
    width = tokens.shape[1]
    pair_count = tokens.shape[0] // seq_len
    half_pairs = pair_count // lax.axis_size("tensor")
    half_rows = half_pairs * seq_len
    row_start = lax.axis_index("tensor") * half_rows
    gain_one, query_w, key_w, value_w, out_w = (
        lax.all_gather(gain_attn, "dp", axis=0, tiled=True),
        lax.all_gather(w_query, "dp", axis=0, tiled=True),
        lax.all_gather(w_key, "dp", axis=0, tiled=True),
        lax.all_gather(w_value, "dp", axis=0, tiled=True),
        lax.all_gather(w_out, "dp", axis=1, tiled=True),
    )
    gain_two, vis_in_w, vis_out_w, txt_in_w, txt_out_w = (
        lax.all_gather(gain_ffn, "dp", axis=0, tiled=True),
        lax.all_gather(vis_in, "dp", axis=0, tiled=True),
        lax.all_gather(vis_out, "dp", axis=1, tiled=True),
        lax.all_gather(txt_in, "dp", axis=0, tiled=True),
        lax.all_gather(txt_out, "dp", axis=1, tiled=True),
    )
    gain_one = gain_one.astype(jnp.float32)
    gain_two = gain_two.astype(jnp.float32)
    head_local = query_w.shape[1] // HEAD_DIM
    score_scale = HEAD_DIM ** (-0.5)
    position = jnp.arange(seq_len, dtype=jnp.int32)
    live = (position[None, :] < PATCHES) | (position[None, :] - PATCHES < caption_lengths[:, None])
    valid_rows = live.astype(jnp.float32)
    mask_col = valid_rows.reshape(-1, 1)
    key_live = valid_rows[:, None, None, :] > 0.5

    def own_rows(values):
        return lax.dynamic_slice_in_dim(values, row_start, half_rows, 0)

    inputs = tokens.astype(jnp.float32)
    normed_one, inverse_one = norm_parts(inputs)
    first_in = (normed_one * gain_one).astype(jnp.bfloat16)

    def project(weight):
        return (
            matmul(first_in, weight)
            .astype(jnp.bfloat16)
            .reshape(pair_count, seq_len, head_local, HEAD_DIM)
        )

    queries = project(query_w)
    keys_all = project(key_w)
    values_all = project(value_w)

    def score_block():
        raw = (
            jnp.einsum("pqhe,pkhe->phqk", queries, keys_all, preferred_element_type=jnp.float32)
            * score_scale
        )
        return jnp.where(key_live, raw, -1e30)

    scores = score_block()
    top = jnp.max(scores, axis=-1, keepdims=True)
    weights = jnp.exp(scores - top)
    total = jnp.sum(weights, axis=-1, keepdims=True)
    probs = (weights / total).astype(jnp.bfloat16)
    log_total = top + jnp.log(total)
    context = jnp.einsum("phqk,pkhe->pqhe", probs, values_all, preferred_element_type=jnp.float32)
    context = context.astype(jnp.bfloat16).reshape(-1, head_local * HEAD_DIM)
    attn_terms = matmul(context, out_w)
    attended_own = lax.psum_scatter(
        attn_terms.astype(jnp.bfloat16), "tensor", scatter_dimension=0, tiled=True
    ).astype(jnp.float32)
    mask_own = own_rows(mask_col)
    middle_own = own_rows(inputs) + mask_own * attended_own
    normed_two, inverse_two = norm_parts(middle_own)
    second_own = (normed_two * gain_two).astype(jnp.bfloat16)
    grid = lax.all_gather(second_own, "tensor", axis=0, tiled=True).reshape(
        pair_count, seq_len, width
    )
    image_rows = grid[:, :PATCHES].reshape(-1, width)
    text_rows = grid[:, PATCHES:].reshape(-1, width)
    image_pre, image_hidden, image_part = expert_forward(image_rows, vis_in_w, vis_out_w)
    text_pre, text_hidden, text_part = expert_forward(text_rows, txt_in_w, txt_out_w)
    image_own, text_own = (
        lax.psum_scatter(
            image_part.astype(jnp.bfloat16), "tensor", scatter_dimension=0, tiled=True
        ).astype(jnp.float32),
        lax.psum_scatter(
            text_part.astype(jnp.bfloat16), "tensor", scatter_dimension=0, tiled=True
        ).astype(jnp.float32),
    )
    branch_own = join_experts(image_own, text_own, half_pairs, width)
    output_own = (middle_own + mask_own * branch_own).astype(jnp.bfloat16)
    upstream = cotangent.astype(jnp.float32)
    grad_branch = (upstream * mask_col).astype(jnp.bfloat16).reshape(pair_count, seq_len, width)
    image_grads = expert_backward(
        image_rows,
        image_pre,
        image_hidden,
        grad_branch[:, :PATCHES].reshape(-1, width),
        vis_in_w,
        vis_out_w,
    )
    text_grads = expert_backward(
        text_rows,
        text_pre,
        text_hidden,
        grad_branch[:, PATCHES:].reshape(-1, width),
        txt_in_w,
        txt_out_w,
    )
    back_image_own, back_text_own = (
        lax.psum_scatter(
            image_grads[2].astype(jnp.bfloat16), "tensor", scatter_dimension=0, tiled=True
        ).astype(jnp.float32),
        lax.psum_scatter(
            text_grads[2].astype(jnp.bfloat16), "tensor", scatter_dimension=0, tiled=True
        ).astype(jnp.float32),
    )
    grad_second_own = join_experts(back_image_own, back_text_own, half_pairs, width)
    grad_norm_own, gain_part = norm_back(grad_second_own, normed_two, inverse_two, gain_two)
    grad_middle_own = own_rows(upstream) + grad_norm_own
    output_wide, grad_middle, gain_parts = (
        lax.all_gather(
            output_own.astype(jnp.float32).astype(jnp.bfloat16), "tensor", axis=0, tiled=True
        ).astype(jnp.float32),
        lax.all_gather(grad_middle_own.astype(jnp.bfloat16), "tensor", axis=0, tiled=True).astype(
            grad_middle_own.dtype
        ),
        lax.all_gather(gain_part.astype(jnp.bfloat16), "tensor", axis=0, tiled=True).astype(
            gain_part.dtype
        ),
    )
    output = output_wide.astype(jnp.bfloat16)
    grad_gain_two = jnp.sum(gain_parts.reshape(-1, width), axis=0)
    grad_attended = (grad_middle * mask_col).astype(jnp.bfloat16)
    grad_out_w = matmul_tn(context, grad_attended)
    grad_context = (
        matmul_nt(grad_attended, out_w)
        .astype(jnp.bfloat16)
        .reshape(pair_count, seq_len, head_local, HEAD_DIM)
    )
    scores_again = score_block()
    probs_exact = jnp.exp(scores_again - log_total)
    grad_probs = jnp.einsum(
        "pqhe,pkhe->phqk", grad_context, values_all, preferred_element_type=jnp.float32
    )
    inner = jnp.sum(grad_probs * probs_exact, axis=-1, keepdims=True)
    grad_scores = (probs_exact * (grad_probs - inner)).astype(jnp.bfloat16)
    grad_values = jnp.einsum(
        "phqk,pqhe->pkhe", probs, grad_context, preferred_element_type=jnp.float32
    )
    grad_values = grad_values.astype(jnp.bfloat16).reshape(-1, head_local * HEAD_DIM)
    grad_queries = (
        jnp.einsum("phqk,pkhe->pqhe", grad_scores, keys_all, preferred_element_type=jnp.float32)
        * score_scale
    )
    grad_queries = grad_queries.astype(jnp.bfloat16).reshape(-1, head_local * HEAD_DIM)
    grad_keys = (
        jnp.einsum("phqk,pqhe->pkhe", grad_scores, queries, preferred_element_type=jnp.float32)
        * score_scale
    )
    grad_keys = grad_keys.astype(jnp.bfloat16).reshape(-1, head_local * HEAD_DIM)
    grad_query_w = matmul_tn(first_in, grad_queries)
    grad_key_w = matmul_tn(first_in, grad_keys)
    grad_value_w = matmul_tn(first_in, grad_values)
    first_part = (
        matmul_nt(grad_queries, query_w)
        + matmul_nt(grad_keys, key_w)
        + matmul_nt(grad_values, value_w)
    )
    grad_first = lax.psum(first_part.astype(jnp.bfloat16), "tensor").astype(jnp.float32)
    grad_norm_one, grad_gain_one = norm_back(grad_first, normed_one, inverse_one, gain_one)
    grad_inputs = grad_middle + grad_norm_one
    attn_sent = (
        lax.psum_scatter(grad_gain_one, "dp", scatter_dimension=0, tiled=True),
        lax.psum_scatter(grad_query_w, "dp", scatter_dimension=0, tiled=True),
        lax.psum_scatter(grad_key_w, "dp", scatter_dimension=0, tiled=True),
        lax.psum_scatter(grad_value_w, "dp", scatter_dimension=0, tiled=True),
        lax.psum_scatter(grad_out_w, "dp", scatter_dimension=1, tiled=True),
    )
    final_expert = (
        lax.psum_scatter(grad_gain_two, "dp", scatter_dimension=0, tiled=True),
        lax.psum_scatter(image_grads[0], "dp", scatter_dimension=0, tiled=True),
        lax.psum_scatter(image_grads[1], "dp", scatter_dimension=1, tiled=True),
        lax.psum_scatter(text_grads[0], "dp", scatter_dimension=0, tiled=True),
        lax.psum_scatter(text_grads[1], "dp", scatter_dimension=1, tiled=True),
    )
    return (
        output,
        grad_inputs,
        attn_sent[0],
        attn_sent[1],
        attn_sent[2],
        attn_sent[3],
        attn_sent[4],
        final_expert[0],
        final_expert[1],
        final_expert[2],
        final_expert[3],
        final_expert[4],
    )


def solution(mesh):
    def local(tokens, lengths, gain, w_query, *rest):
        ring = mesh.shape["dp"] // 2
        fits = (
            mesh.shape["tensor"] == 2
            and ring == 8
            and lengths.shape[0] == 2
            and w_query.shape[0] % 16 == 0
        )
        layer = fused_layer if fits else plain_layer
        return layer(tokens, lengths, gain, w_query, *rest)

    return jax.shard_map(
        local,
        mesh=mesh,
        in_specs=(
            P("dp", None),
            P("dp"),
            P("dp"),
            P("dp", "tensor"),
            P("dp", "tensor"),
            P("dp", "tensor"),
            P("tensor", "dp"),
            P("dp"),
            P("dp", "tensor"),
            P("tensor", "dp"),
            P("dp", "tensor"),
            P("tensor", "dp"),
            P("dp", None),
        ),
        out_specs=(
            P("dp", None),
            P("dp", None),
            P("dp"),
            P("dp", "tensor"),
            P("dp", "tensor"),
            P("dp", "tensor"),
            P("tensor", "dp"),
            P("dp"),
            P("dp", "tensor"),
            P("tensor", "dp"),
            P("dp", "tensor"),
            P("tensor", "dp"),
        ),
        check_vma=False,
    )
```

```python
import functools
import math
import types

import jax
import jax.numpy as jnp
from jax import lax
from jax.experimental import pallas as pl
from jax.experimental.pallas import tpu as pltpu
from jax.sharding import PartitionSpec as P

HEAD_DIM = 64
PATCHES = 197
CAPTION = 40
VIS = 208
TXT = 48
SEQ = VIS + TXT

MESH = pl.DeviceIdType.MESH
BF = jnp.bfloat16
F32 = jnp.float32

ATT, TIN, TOUT, VIN, VOUT = range(5)

epsilon = 1e-05
inv_root_two = 1.0 / math.sqrt(2.0)
inv_root_tau = 1.0 / math.sqrt(2.0 * math.pi)


def mm(left, right):
    return jnp.dot(left, right, preferred_element_type=F32)


def mm_nt(left, right):
    return lax.dot_general(left, right, (((1,), (1,)), ((), ())), preferred_element_type=F32)


def mm_tn(left, right):
    return lax.dot_general(left, right, (((0,), (0,)), ((), ())), preferred_element_type=F32)


def normalize(values):
    center = values - jnp.mean(values, axis=-1, keepdims=True)
    spread = jnp.mean(center * center, axis=-1, keepdims=True)
    inverse = lax.rsqrt(spread + epsilon)
    return center * inverse, inverse


def normalize_back(grad_normed, normed, inverse):
    return inverse * (
        grad_normed
        - jnp.mean(grad_normed, axis=-1, keepdims=True)
        - normed * jnp.mean(grad_normed * normed, axis=-1, keepdims=True)
    )


def unit(size):
    rows = lax.broadcasted_iota(jnp.int32, (size, size), 0)
    return (rows == lax.broadcasted_iota(jnp.int32, (size, size), 1)).astype(F32).astype(BF)


def column(ref):
    size = ref.shape[1]
    return jnp.sum(unit(size).astype(F32) * ref[...].astype(F32), axis=1, keepdims=True)


def layer_kernel(n, names, *refs):
    R = types.SimpleNamespace(**dict(zip(names, refs)))
    R.pb, R.pf, R.ga, R.rf, R.rb, R.n2 = R.pa, R.pg, R.x4, R.ra, R.rg, R.n1
    R.gat, R.gzvt, R.gqkv = R.turned, R.turned, R.n2
    S, G, PART, LAND = R.shard, R.gathered, R.part, R.land
    OUT, GW, GG = R.padded_out, R.gw, R.gg
    width = G.shape[2]
    own = width // (2 * n)
    span = width // 4
    heads = span // HEAD_DIM

    x = lax.axis_index("tensor")
    d = lax.axis_index("dp")
    c = lax.rem(d, 2)
    other = 1 - c
    chip = d // 2
    y, z = lax.rem(chip, 2), chip // 2
    r = z + y * (n - 1 - 2 * z)
    half = n // 2

    def chip_at(pos):
        pos = lax.rem(pos + 2 * n, n)
        upper = pos // half
        return 2 * (pos + upper * (n - 1 - 2 * pos)) + upper

    mate = {"dp": d + 1 - 2 * c}
    across = {"tensor": 1 - x}
    ahead = {"dp": 2 * chip_at(r + 1) + c}
    behind = {"dp": 2 * chip_at(r - 1) + c}
    way = (ahead, behind)

    def rows_at(pos):
        return pl.ds(pl.multiple_of(2 * own * chip_at(pos), 16), 2 * own)

    my_rows = pl.ds(pl.multiple_of(own * d, 16), own)

    barrier = pltpu.get_barrier_semaphore()
    for device in (mate, across, ahead, behind):
        pl.semaphore_signal(barrier, inc=1, device_id=device, device_id_type=MESH)

    mine, theirs = pl.multiple_of(2 * c, 2), pl.multiple_of(2 * other, 2)
    pair_own = 2 * c + x
    pair_across = 2 * c + 1 - x

    started = []
    counter = [0]

    def remote(source, target, device):
        index = counter[0]
        counter[0] += 1
        return pltpu.make_async_remote_copy(
            src_ref=source,
            dst_ref=target,
            send_sem=R.sent.at[index],
            recv_sem=R.came.at[index],
            device_id=device,
            device_id_type=MESH,
        )

    def start(source, target, device):
        copy = remote(source, target, device)
        copy.start()
        started.append(copy)
        return copy

    def sent(copy):
        copy.wait_send()
        started[:] = [one for one in started if one is not copy]

    near, far = (ATT, 0, width // 2), (ATT, width // 2, width // 2)
    parts = [near, far] + [(k, 0, width) for k in (TIN, TOUT, VIN, VOUT)]
    attention, text, image = parts[:2], parts[2:4], parts[4:]
    longest = half

    def hops(part, side):
        return half if (parts.index(part) + side) % 2 == 0 else n - 1 - half

    def ring_index(part, side, s):
        return (parts.index(part) * 2 + side) * longest + s

    def view(ref, part, rows):
        k, first, count = part
        return ref.at[k, rows, pl.ds(first, count)]

    def gather_copy(part, side, s, pos):
        block = view(G, part, rows_at(pos))
        i = ring_index(part, side, s)
        return pltpu.make_async_remote_copy(
            src_ref=block,
            dst_ref=block,
            send_sem=R.ring_sent.at[i],
            recv_sem=R.ring_came.at[i],
            device_id=way[side],
            device_id_type=MESH,
        )

    def gather_step(group, s):
        for part in group:
            for side in range(2):
                pos = r - s if side == 0 else r + s
                if 0 < s <= hops(part, side):
                    gather_copy(part, side, s - 1, pos).wait_recv()
                if s < hops(part, side):
                    gather_copy(part, side, s, pos).start()

    sum_base = len(parts) * 2 * longest

    def landed(part, side, s):
        k, first, count = part
        return LAND.at[k, side * hops(part, 0) + s, :, pl.ds(first, count)]

    def sum_copy(part, side, s, source):
        i = sum_base + ring_index(part, side, s)
        return pltpu.make_async_remote_copy(
            src_ref=source,
            dst_ref=landed(part, side, s),
            send_sem=R.ring_sent.at[i],
            recv_sem=R.ring_came.at[i],
            device_id=way[side],
            device_id_type=MESH,
        )

    def sum_step(group, s):
        for part in group:
            for side in range(2):
                reach = hops(part, side)
                if s >= reach:
                    continue
                pos = r + (reach - s) if side == 0 else r - (reach - s)
                term = view(PART, part, rows_at(pos))
                if s == 0:
                    source = term
                else:
                    source = landed(part, side, s - 1)
                    sum_copy(part, side, s - 1, source).wait_recv()
                    source[...] = (source[...].astype(F32) + term[...].astype(F32)).astype(BF)
                sum_copy(part, side, s, source).start()

    finals = []

    def sum_last(group):
        for part in group:
            k, first, count = part
            ends = []
            for side in range(2):
                end = landed(part, side, hops(part, side) - 1)
                sum_copy(part, side, hops(part, side) - 1, end).wait_recv()
                ends.append(end)

            def total(core):
                rows = pl.ds(pl.multiple_of(own * core, 16), own)
                mine_rows = pl.ds(pl.multiple_of(2 * own * chip + own * core, 16), own)
                return (
                    ends[0][rows, :].astype(F32)
                    + ends[1][rows, :].astype(F32)
                    + PART[k, mine_rows, first : first + count].astype(F32)
                )

            cols = slice(first, first + count)
            away, home = total(other), total(c)
            R.give[k, :, cols] = away
            finals.append(
                start(R.give.at[k, :, pl.ds(first, count)], GW.at[k, c, :, pl.ds(first, count)], mate)
            )
            GW[k, c, :, cols] = home

    def shard_part(k, value):
        for core in range(2):
            S[k, core] = value(core).astype(BF)

    gain_one, gain_two = column(R.gain_attn), column(R.gain_ffn)

    def attention_part(core):
        cols = slice(core * span, (core + 1) * span)
        return jnp.concatenate(
            [
                R.w_query[:, cols].astype(F32) * (gain_one * HEAD_DIM**-0.5),
                R.w_key[:, cols].astype(F32) * gain_one,
                R.w_value[:, cols].astype(F32) * gain_one,
                R.w_out[:, cols].astype(F32),
            ],
            axis=1,
        )

    def half_of(ref, core):
        return ref[:, core * width : (core + 1) * width].astype(F32) * gain_two

    def turned_half(ref, core):
        return ref[:, core * width : (core + 1) * width]

    lengths = R.lengths

    def live(t, slots):
        return (slots < PATCHES) | ((slots >= VIS) & (slots < VIS + lengths[t]))

    def live_rows(t, j, count=64):
        slots = lax.broadcasted_iota(jnp.int32, (count, 1), 0) + j * count
        return live(t, slots).astype(F32)

    row_count = R.tokens.shape[0]

    def placed(t, slots, rows, kept):
        source = t * (PATCHES + CAPTION) + slots - (slots >= VIS).astype(jnp.int32) * (VIS - PATCHES)
        return ((rows == source) & kept).astype(F32).astype(BF)

    def chooser(t, only_live):
        slots = lax.broadcasted_iota(jnp.int32, (SEQ, row_count), 0)
        rows = lax.broadcasted_iota(jnp.int32, (SEQ, row_count), 1)
        filled = (slots < PATCHES) | ((slots >= VIS) & (slots < VIS + CAPTION))
        return placed(t, slots, rows, live(t, slots) if only_live else filled)

    shard_part(ATT, attention_part)
    G[ATT, my_rows, :] = S[ATT, c]
    for t in range(2):
        R.lens[t] = jnp.full((8, 128), lengths[t], jnp.int32).astype(F32)
    pl.semaphore_wait(barrier, 4)
    shard_a = start(S.at[pl.ds(0, 1), other], G.at[pl.ds(0, 1), my_rows, :], mate)
    send_lens = start(R.lens, R.lens4.at[pl.ds(mine, 2)], mate)
    for t in range(2):
        R.x4[2 * c + t] = mm(chooser(t, False), R.tokens[...]).astype(BF)
        R.lens4[2 * c + t] = R.lens[t]
    send_x = start(R.x4.at[pl.ds(mine, 2)], R.x4.at[pl.ds(mine, 2)], mate)
    shard_a.wait_recv()
    gather_step(attention, 0)

    shard_part(TIN, functools.partial(half_of, R.txt_in))
    shard_part(TOUT, functools.partial(turned_half, R.txt_out))
    shard_part(VIN, functools.partial(half_of, R.vis_in))
    shard_part(VOUT, functools.partial(turned_half, R.vis_out))
    shard_b = start(S.at[pl.ds(1, 4), other], G.at[pl.ds(1, 4), my_rows, :], mate)
    for k in (TIN, TOUT, VIN, VOUT):
        G[k, my_rows, :] = S[k, c]
    gather_step(attention, 1)
    for t in range(2):
        R.gz[2 * c + t] = mm(chooser(t, True), R.cotangent[...]).astype(BF)
    send_gz = start(R.gz.at[pl.ds(mine, 2)], R.gz.at[pl.ds(mine, 2)], mate)
    R.dy[...] = mm(chooser(x, False), R.cotangent[...]).astype(BF)
    for t in range(2):
        R.x[t] = R.x4[2 * c + t]
    send_x.wait_recv()

    for i in range(4):

        @pl.loop(0, SEQ // 64, unroll=True)
        def _(j, i=i):
            rows = pl.ds(pl.multiple_of(j * 64, 64), 64)
            normed, _ = normalize(R.x4[i, rows, :].astype(F32))
            R.n1[i, rows, :] = normed.astype(BF)

        R.n1t[:, i * SEQ : (i + 1) * SEQ] = R.n1[i].T
        if i == 1:
            gather_step(attention, 2)
    gather_step(attention, 3)
    shard_b.wait_recv()
    gather_step(text, 0)
    send_gz.wait_recv()
    send_lens.wait_recv()

    @pl.loop(0, width // 256)
    def _(j):
        cols = pl.ds(pl.multiple_of(j * 256, 256), 256)
        R.gzvt[cols, : 4 * VIS] = R.gz[:, :VIS, cols].reshape(4 * VIS, 256).T
        R.gztt[cols, :] = R.gz[:, VIS:, cols].reshape(4 * TXT, 256).T

    gather_step(attention, 4)

    R.wo[...] = G[ATT][:, 3 * span :]

    @pl.loop(0, 4)
    def _(i):
        projected = mm(R.n1[i], G[ATT][:, : 3 * span]).astype(BF)
        R.q[i] = projected[:, :span]
        R.k[i] = projected[:, span : 2 * span]
        R.v[i] = projected[:, 2 * span :]

    lane = lax.broadcasted_iota(jnp.int32, (1, span), 1) // HEAD_DIM

    def only(head, values):
        return values * (lane == head).astype(F32).astype(BF)

    def head_rows(values, head):
        return values[head * HEAD_DIM : (head + 1) * HEAD_DIM, :]

    order = []
    for j in range(4):
        core = other if j < 2 else c
        turn = 1 - x if j % 2 == 0 else x
        order.append((turn, 2 * core + turn))
    attn_mate = [remote(R.pa.at[i], R.ra.at[turn], mate) for turn, i in order[:2]]
    cross_a = remote(R.xs, R.xr, across)
    started.append(cross_a)

    for j, (turn, i) in enumerate(order):
        q, k, v = R.q[i], R.k[i], R.v[i]
        turned_v = v.T
        slots = lax.broadcasted_iota(jnp.int32, (SEQ, 1), 0)
        caption = (slots - VIS).astype(F32) < R.lens4[i][:1, :1]
        bias = jnp.where((slots < PATCHES) | ((slots >= VIS) & caption), 0.0, -1e30)
        contexts = []
        for h in range(heads):
            scores = mm_nt(only(h, k), q) + bias
            top = jnp.max(scores, axis=0, keepdims=True)
            weights = jnp.exp(scores - top)
            total = jnp.sum(weights, axis=0, keepdims=True)
            probs = (weights * (1.0 / total)).astype(BF)
            R.probs[i * heads + h] = probs
            contexts.append(mm(head_rows(turned_v, h), probs))
        context = jnp.concatenate(contexts, axis=0).T.astype(BF)
        R.c[i] = context
        R.pa[i] = mm_nt(context, R.wo[...]).astype(BF)
        if j < 2:
            attn_mate[j].start()
        if j == 2:
            attn_mate[0].wait_recv()
            R.xs[...] = (R.pa[pair_across].astype(F32) + R.ra[1 - x].astype(F32)).astype(BF)
            cross_a.start()
        if j == 0:
            gather_step(text, 1)
        if j == 2:
            gather_step(text, 2)

    for copy in attn_mate:
        copy.wait_send()
    attn_mate[1].wait_recv()
    gather_step(text, 3)
    gather_step(image, 0)
    cross_a.wait_recv()

    @pl.loop(0, SEQ // 64, unroll=True)
    def _(j):
        rows = pl.ds(pl.multiple_of(j * 64, 64), 64)
        attended = (
            R.pa[pair_own, rows, :].astype(F32)
            + R.ra[x, rows, :].astype(F32)
            + R.xr[rows, :].astype(F32)
        )
        middle = R.x[x, rows, :].astype(F32) + live_rows(x, j) * attended
        R.y1[rows, :] = middle
        normed, _ = normalize(middle)
        R.n2[pair_own, rows, :] = normed.astype(BF)

    block = R.n2.at[pair_own]
    to_across = start(block, block, across)
    to_mate = start(block, block, mate)
    gather_step(text, 4)
    gather_step(image, 1)
    to_across.wait_recv()
    block = R.n2.at[pair_across]
    passed = start(block, block, mate)
    gather_step(image, 2)
    to_mate.wait_recv()
    passed.wait_recv()

    def expert(pairs, low, high, w_in, w_out, h_ref, gu_ref, j):
        first, count = pairs
        per = high - low
        total_rows = count * per
        cols = slice(j * 256, (j + 1) * 256)
        inside = slice(first, first + count)
        R.u[:total_rows, :] = mm(
            R.n2[inside, low:high, :].reshape(total_rows, width), G[w_in, :, cols]
        )
        R.gh[:total_rows, :] = mm(
            R.gz[inside, low:high, :].reshape(total_rows, width), G[w_out, :, cols]
        )
        step = 16
        steps = total_rows // step

        @pl.loop(0, steps, unroll=steps // 2)
        def _(i):
            rows = pl.ds(pl.multiple_of(i * step, step), step)
            into = pl.ds(pl.multiple_of(first * per + i * step, step), step)
            pre = R.u[rows, :]
            cumulative = 0.5 * (1.0 + lax.erf(pre * inv_root_two))
            density = jnp.exp(-0.5 * pre * pre) * inv_root_tau
            h_ref[into, cols] = (pre * cumulative).astype(BF)
            gu_ref[into, cols] = (R.gh[rows, :] * (cumulative + pre * density)).astype(BF)

    def weight_grad(k, turned, ref, j):
        cols = slice(j * 256, (j + 1) * 256)
        PART[k, :, cols] = mm(turned, ref[:, cols]).astype(BF)

    tiles = range(width // 256)
    for j in tiles:
        expert((0, 4), VIS, SEQ, TIN, TOUT, R.ht, R.gut, j)
    for j in tiles:
        weight_grad(TOUT, R.gztt[...], R.ht, j)
    gather_step(image, 3)

    @pl.loop(0, width // 256)
    def _(j):
        cols = pl.ds(pl.multiple_of(j * 256, 256), 256)
        R.n2vt[cols, :] = R.n2[:, :VIS, cols].reshape(4 * VIS, 256).T
        R.n2tt[cols, :] = R.n2[:, VIS:, cols].reshape(4 * TXT, 256).T

    for j in tiles:
        weight_grad(TIN, R.n2tt[...], R.gut, j)
    sum_step(text, 0)
    gather_step(image, 4)

    def terms(target, hv, ht, w_vis, w_txt, m):
        vis_rows = slice(2 * m * VIS, 2 * (m + 1) * VIS)
        txt_rows = slice(2 * m * TXT, 2 * (m + 1) * TXT)
        vis_part = mm_nt(hv[vis_rows, :], G[w_vis]).astype(BF)
        target[2 * m : 2 * m + 2, :VIS, :] = vis_part.reshape(2, VIS, width)
        txt_part = mm_nt(ht[txt_rows, :], G[w_txt]).astype(BF)
        target[2 * m : 2 * m + 2, VIS:, :] = txt_part.reshape(2, TXT, width)

    mate_g = remote(R.pg.at[pl.ds(theirs, 2)], R.rg, mate)
    cross_g = remote(R.xsg, R.xrg, across)
    gy_across = remote(R.gy.at[x], R.gy.at[x], across)
    gy_mate = remote(R.ga.at[pair_own], R.ga.at[pair_own], mate)
    gy_passed = remote(R.ga.at[pair_across], R.ga.at[pair_across], mate)
    started.extend([cross_g, gy_across, gy_mate, gy_passed])

    def image_terms(m):
        terms(R.pg, R.guv, R.gut, VIN, TIN, m)
        pl.when(c != m)(mate_g.start)

    def sum_cores(m):
        @pl.when(c == m)
        def _():
            mate_g.wait_recv()
            R.xsg[...] = (R.pg[pair_across].astype(F32) + R.rg[1 - x].astype(F32)).astype(BF)
            cross_g.start()

    def middle_back(m):
        @pl.when(c == m)
        def _():
            cross_g.wait_recv()

            @pl.loop(0, SEQ // 64, unroll=True)
            def _(j):
                rows = pl.ds(pl.multiple_of(j * 64, 64), 64)
                grad_normed = (
                    R.pg[pair_own, rows, :].astype(F32)
                    + R.rg[x, rows, :].astype(F32)
                    + R.xrg[rows, :].astype(F32)
                )
                normed, inverse = normalize(R.y1[rows, :])
                grad = R.dy[rows, :].astype(F32) + normalize_back(grad_normed, normed, inverse)
                R.gy[x, rows, :] = grad.astype(BF)
                R.ga[pair_own, rows, :] = (grad * live_rows(x, j)).astype(BF)

            gy_across.start()
            gy_mate.start()

    def middle_pass(m):
        @pl.when(c == m)
        def _():
            gy_across.wait_recv()

            @pl.loop(0, SEQ // 64, unroll=True)
            def _(j):
                rows = pl.ds(pl.multiple_of(j * 64, 64), 64)
                R.ga[pair_across, rows, :] = (
                    R.gy[1 - x, rows, :].astype(F32) * live_rows(1 - x, j)
                ).astype(BF)

            gy_passed.start()

    def middle_came(m):
        @pl.when(c != m)
        def _():
            gy_mate.wait_recv()
            gy_passed.wait_recv()

    sent(send_x)
    for j in tiles:
        expert((0, 2), 0, VIS, VIN, VOUT, R.hv, R.guv, j)
    sum_step(text, 1)
    image_terms(0)
    expert((2, 2), 0, VIS, VIN, VOUT, R.hv, R.guv, 0)
    sum_cores(0)
    for j in tiles[1:]:
        expert((2, 2), 0, VIS, VIN, VOUT, R.hv, R.guv, j)
    sum_step(text, 2)
    image_terms(1)
    for copy in (to_across, to_mate, passed):
        sent(copy)
    weight_grad(VOUT, R.gzvt[:, : 4 * VIS], R.hv, 0)
    sum_cores(1)
    middle_back(0)
    for j in tiles[1:]:
        weight_grad(VOUT, R.gzvt[:, : 4 * VIS], R.hv, j)
    for j in tiles:
        weight_grad(VIN, R.n2vt[...], R.guv, j)
    sum_step(text, 3)
    sum_step(image, 0)

    mate_g.wait_send()
    terms(R.pf, R.hv, R.ht, VOUT, TOUT, 0)
    middle_pass(0)
    middle_back(1)
    terms(R.pf, R.hv, R.ht, VOUT, TOUT, 1)
    mate_f = start(R.pf.at[pl.ds(theirs, 2)], R.rf, mate)
    cross_f = remote(R.xsf, R.xrf, across)
    started.append(cross_f)
    sum_last(text)
    sum_step(image, 1)
    middle_came(0)

    back_mate = [remote(R.pb.at[theirs + t], R.rb.at[t], mate) for t in range(2)]
    back_cross = [remote(R.xsb.at[t], R.xrb.at[t], across) for t in range(2)]
    started.extend(back_mate + back_cross)

    def attention_back(m, t):
        i = 2 * m + t
        grad_context = mm(R.ga[i], R.wo[...]).astype(BF)
        R.gat[:, i * SEQ : (i + 1) * SEQ] = R.ga[i].T
        q, k, v = R.q[i], R.k[i], R.v[i]
        turned_k = k.T
        grad_q = []
        grad_k = jnp.zeros((SEQ, span), F32)
        grad_v = jnp.zeros((SEQ, span), F32)
        for h in range(heads):
            probs = R.probs[i * heads + h]
            grad_probs = mm_nt(only(h, v), grad_context)
            exact = probs.astype(F32)
            inner = jnp.sum(grad_probs * exact, axis=0, keepdims=True)
            grad_scores = (exact * (grad_probs - inner)).astype(BF)
            grad_q.append(mm(head_rows(turned_k, h), grad_scores))
            grad_k += mm(grad_scores, only(h, q))
            grad_v += mm(probs, only(h, grad_context))
        grad_q = jnp.concatenate(grad_q, axis=0).T
        joined = jnp.concatenate([grad_q, grad_k, grad_v], axis=1).astype(BF)
        R.gqkv[i, :, : 3 * span] = joined
        R.pb[i] = mm_nt(joined, G[ATT][:, : 3 * span]).astype(BF)
        pl.when(c != m)(back_mate[t].start)

    def back_sum(m):
        @pl.when(c == m)
        def _():
            for t in range(2):
                back_mate[t].wait_recv()
                R.xsb[t] = (R.pb[2 * m + t].astype(F32) + R.rb[t].astype(F32)).astype(BF)
                back_cross[t].start()

    attention_back(0, 0)
    mate_f.wait_recv()
    R.xsf[...] = (R.pf[pair_across].astype(F32) + R.rf[1 - x].astype(F32)).astype(BF)
    middle_pass(1)
    cross_f.start()
    attention_back(0, 1)
    sum_step(image, 2)
    middle_came(1)
    attention_back(1, 0)
    back_sum(0)
    attention_back(1, 1)
    sum_step(image, 3)

    @pl.loop(0, 3)
    def _(j):
        rows = pl.ds(pl.multiple_of(j * 256, 256), 256)
        grads = mm(R.n1t[rows, :], R.gqkv[:, :, : 3 * span].reshape(4 * SEQ, 3 * span))
        grad_o = mm(R.gat[rows, :], R.c[...].reshape(4 * SEQ, span))
        PART[ATT, rows, :] = jnp.concatenate([grads, grad_o], axis=1).astype(BF)

    sum_step(attention, 0)
    back_sum(1)
    sum_last(image)

    cross_f.wait_recv()

    @pl.loop(0, SEQ // 64, unroll=True)
    def _(j):
        rows = pl.ds(pl.multiple_of(j * 64, 64), 64)
        branch = (
            R.pf[pair_own, rows, :].astype(F32)
            + R.rf[x, rows, :].astype(F32)
            + R.xrf[rows, :].astype(F32)
        )
        OUT[x, rows, :] = (R.y1[rows, :] + live_rows(x, j) * branch).astype(BF)

    out_across = start(OUT.at[x], OUT.at[x], across)
    sum_step(attention, 1)

    for t in range(2):
        back_cross[t].wait_recv()

        @pl.loop(0, SEQ // 64, unroll=True)
        def _(j, t=t):
            rows = pl.ds(pl.multiple_of(j * 64, 64), 64)
            grad_normed = R.xsb[t, rows, :].astype(F32) + R.xrb[t, rows, :].astype(F32)
            normed, inverse = normalize(R.x[t, rows, :].astype(F32))
            grad = R.gy[t, rows, :].astype(F32) + normalize_back(grad_normed, normed, inverse)
            high = grad.astype(BF)
            rows = pl.ds(pl.multiple_of(t * SEQ + j * 64, 64), 64)
            R.hv[rows, :] = high
            R.guv[rows, :] = (grad - high.astype(F32)).astype(BF)

        sum_step(attention, 2 + t)

    slots = lax.broadcasted_iota(jnp.int32, (row_count, 2 * SEQ), 1)
    rows = lax.broadcasted_iota(jnp.int32, (row_count, 2 * SEQ), 0)
    turn = slots // SEQ
    back = placed(turn, slots - turn * SEQ, rows, slots >= 0)
    out_across.wait_recv()
    R.out_tokens[...] = mm(back, OUT[...].reshape(2 * SEQ, width)).astype(BF)
    R.grad_tokens[...] = mm(back, R.hv[: 2 * SEQ, :]) + mm(back, R.guv[: 2 * SEQ, :])
    sum_last(attention)
    for copy in finals:
        copy.wait_recv()

    def row_sums(k, last):
        return sum(
            jnp.sum(S[k, core][:, :last].astype(F32) * GW[k, core][:, :last], axis=-1, keepdims=True)
            for core in range(2)
        )

    R.gs[0] = jnp.broadcast_to(row_sums(ATT, 3 * span), (own, 128))
    R.gs[1] = jnp.broadcast_to(row_sums(TIN, width) + row_sums(VIN, width), (own, 128))
    cross_gain = start(R.gs, R.gr, across)
    cross_gain.wait_recv()
    GG[...] = R.gs[...] + R.gr[...]

    for copy in started:
        copy.wait_send()
    for part in parts:
        for side in range(2):
            for s in range(hops(part, side)):
                gather_copy(part, side, s, r).wait_send()
                sum_copy(part, side, s, landed(part, side, s)).wait_send()


def finish_kernel(out, gtok, gw, gg, gain_attn, gain_ffn, *rest):
    (
        out_tokens,
        grad_tokens,
        grad_gain_attn,
        grad_query,
        grad_key,
        grad_value,
        grad_out,
        grad_gain_ffn,
        grad_vis_in,
        grad_vis_out,
        grad_txt_in,
        grad_txt_out,
    ) = rest
    out_tokens[...] = out[...]
    grad_tokens[...] = gtok[...]
    width = gw.shape[3]
    own = gw.shape[2]
    span = width // 4
    gain_one, gain_two = column(gain_attn), column(gain_ffn)
    square = unit(own).astype(F32)
    grad_gain_attn[...] = jnp.sum(square * (gg[0][:, :1] / gain_one), axis=0, keepdims=True)
    grad_gain_ffn[...] = jnp.sum(square * (gg[1][:, :1] / gain_two), axis=0, keepdims=True)

    def both(part):
        return jnp.concatenate([gw[ATT, core][:, part * span : (part + 1) * span] for core in range(2)], axis=1)

    grad_query[...] = both(0) * (gain_one * HEAD_DIM**-0.5)
    grad_key[...] = both(1) * gain_one
    grad_value[...] = both(2) * gain_one
    grad_out[...] = both(3)
    for core in range(2):
        part = slice(core * width, (core + 1) * width)
        grad_vis_in[:, part] = gw[VIN, core] * gain_two
        grad_txt_in[:, part] = gw[TIN, core] * gain_two
        grad_vis_out[:, part] = gw[VOUT, core]
        grad_txt_out[:, part] = gw[TOUT, core]


def fused_layer(
    tokens,
    caption_lengths,
    gain_attn,
    w_query,
    w_key,
    w_value,
    w_out,
    gain_ffn,
    vis_in,
    vis_out,
    txt_in,
    txt_out,
    cotangent,
):
    n = lax.axis_size("dp") // 2
    own = w_query.shape[0]
    row_count, width = tokens.shape
    span = width // 4
    heads = span // HEAD_DIM
    gain_one, gain_two = gain_attn.reshape(1, own), gain_ffn.reshape(1, own)

    rows = 4 * SEQ
    scratch = dict(
        shard=pltpu.VMEM((5, 2, own, width), BF),
        lens=pltpu.VMEM((2, 8, 128), F32),
        x=pltpu.VMEM((2, SEQ, width), BF),
        dy=pltpu.VMEM((SEQ, width), BF),
        padded_out=pltpu.VMEM((2, SEQ, width), BF),
        gathered=pltpu.VMEM((5, width, width), BF),
        part=pltpu.VMEM((5, width, width), BF),
        land=pltpu.VMEM((5, n - 1, 2 * own, width), BF),
        give=pltpu.VMEM((5, own, width), F32),
        x4=pltpu.VMEM((4, SEQ, width), BF),
        lens4=pltpu.VMEM((4, 8, 128), F32),
        n1=pltpu.VMEM((4, SEQ, width), BF),
        n1t=pltpu.VMEM((width, rows), BF),
        gz=pltpu.VMEM((4, SEQ, width), BF),
        turned=pltpu.VMEM((width, rows), BF),
        gztt=pltpu.VMEM((width, 4 * TXT), BF),
        wo=pltpu.VMEM((width, span), BF),
        q=pltpu.VMEM((4, SEQ, span), BF),
        k=pltpu.VMEM((4, SEQ, span), BF),
        v=pltpu.VMEM((4, SEQ, span), BF),
        c=pltpu.VMEM((4, SEQ, span), BF),
        probs=pltpu.VMEM((4 * heads, SEQ, SEQ), BF),
        pa=pltpu.VMEM((4, SEQ, width), BF),
        ra=pltpu.VMEM((2, SEQ, width), BF),
        xs=pltpu.VMEM((SEQ, width), BF),
        xr=pltpu.VMEM((SEQ, width), BF),
        y1=pltpu.VMEM((SEQ, width), F32),
        n2vt=pltpu.VMEM((width, 4 * VIS), BF),
        n2tt=pltpu.VMEM((width, 4 * TXT), BF),
        u=pltpu.VMEM((4 * VIS, 256), F32),
        gh=pltpu.VMEM((4 * VIS, 256), F32),
        hv=pltpu.VMEM((4 * VIS, width), BF),
        guv=pltpu.VMEM((4 * VIS, width), BF),
        ht=pltpu.VMEM((4 * TXT, width), BF),
        gut=pltpu.VMEM((4 * TXT, width), BF),
        pg=pltpu.VMEM((4, SEQ, width), BF),
        rg=pltpu.VMEM((2, SEQ, width), BF),
        xsg=pltpu.VMEM((SEQ, width), BF),
        xrg=pltpu.VMEM((SEQ, width), BF),
        gy=pltpu.VMEM((2, SEQ, width), BF),
        xsf=pltpu.VMEM((SEQ, width), BF),
        xrf=pltpu.VMEM((SEQ, width), BF),
        xsb=pltpu.VMEM((2, SEQ, width), BF),
        xrb=pltpu.VMEM((2, SEQ, width), BF),
        gs=pltpu.VMEM((2, own, 128), F32),
        gr=pltpu.VMEM((2, own, 128), F32),
        sent=pltpu.SemaphoreType.DMA((40,)),
        came=pltpu.SemaphoreType.DMA((40,)),
        ring_sent=pltpu.SemaphoreType.DMA((6 * 2 * (n // 2) * 2,)),
        ring_came=pltpu.SemaphoreType.DMA((6 * 2 * (n // 2) * 2,)),
    )
    inputs = dict(
        lengths=caption_lengths,
        tokens=tokens,
        cotangent=cotangent,
        gain_attn=gain_one,
        gain_ffn=gain_two,
        w_query=w_query,
        w_key=w_key,
        w_value=w_value,
        w_out=w_out.T,
        vis_in=vis_in,
        vis_out=vis_out.T,
        txt_in=txt_in,
        txt_out=txt_out.T,
    )
    results = dict(
        out_tokens=jax.ShapeDtypeStruct((row_count, width), BF),
        grad_tokens=jax.ShapeDtypeStruct((row_count, width), F32),
        gw=jax.ShapeDtypeStruct((5, 2, own, width), F32),
        gg=jax.ShapeDtypeStruct((2, own, 128), F32),
    )
    vmem = pl.BlockSpec(memory_space=pltpu.VMEM)
    names = tuple(inputs) + tuple(results) + tuple(scratch)
    out, gtok, gw, gg = pl.pallas_call(
        functools.partial(layer_kernel, n, names),
        out_shape=tuple(results.values()),
        in_specs=[pl.BlockSpec(memory_space=pltpu.SMEM)] + [vmem] * (len(inputs) - 1),
        out_specs=[vmem] * len(results),
        scratch_shapes=list(scratch.values()),
        compiler_params=pltpu.CompilerParams(
            collective_id=0, has_side_effects=True, vmem_limit_bytes=60 * 2**20
        ),
    )(*inputs.values())

    final = pl.pallas_call(
        finish_kernel,
        out_shape=(
            jax.ShapeDtypeStruct((row_count, width), BF),
            jax.ShapeDtypeStruct((row_count, width), F32),
            jax.ShapeDtypeStruct((1, own), F32),
            jax.ShapeDtypeStruct((own, 2 * span), F32),
            jax.ShapeDtypeStruct((own, 2 * span), F32),
            jax.ShapeDtypeStruct((own, 2 * span), F32),
            jax.ShapeDtypeStruct((own, 2 * span), F32),
            jax.ShapeDtypeStruct((1, own), F32),
            jax.ShapeDtypeStruct((own, 2 * width), F32),
            jax.ShapeDtypeStruct((own, 2 * width), F32),
            jax.ShapeDtypeStruct((own, 2 * width), F32),
            jax.ShapeDtypeStruct((own, 2 * width), F32),
        ),
        in_specs=[vmem] * 6,
        out_specs=[vmem] * 12,
        compiler_params=pltpu.CompilerParams(vmem_limit_bytes=60 * 2**20),
    )(out, gtok, gw, gg, gain_one, gain_two)
    final = list(final)
    final[2] = final[2].reshape(own)
    final[7] = final[7].reshape(own)
    for turned in (6, 9, 11):
        final[turned] = final[turned].T
    return tuple(final)


def norm_parts(values):
    center = values - jnp.mean(values, axis=-1, keepdims=True)
    spread = jnp.mean(center * center, axis=-1, keepdims=True)
    inverse = lax.rsqrt(spread + epsilon)
    return (center * inverse, inverse)


def norm_back(grad_out, normed, inverse, gain):
    grad_normed = grad_out * gain
    grad_gain = jnp.sum(grad_out * normed, axis=0)
    inner = (
        grad_normed
        - jnp.mean(grad_normed, axis=-1, keepdims=True)
        - normed * jnp.mean(grad_normed * normed, axis=-1, keepdims=True)
    )
    return (inverse * inner, grad_gain)


def matmul(left, right):
    return jnp.dot(left, right, preferred_element_type=jnp.float32)


def matmul_tn(left, right):
    return lax.dot_general(
        left, right, (((0,), (0,)), ((), ())), preferred_element_type=jnp.float32
    )


def matmul_nt(left, right):
    return lax.dot_general(
        left, right, (((1,), (1,)), ((), ())), preferred_element_type=jnp.float32
    )


def gelu_slope(pre):
    cumulative = 0.5 * (1.0 + lax.erf(pre * inv_root_two))
    density = jnp.exp(-0.5 * pre * pre) * inv_root_tau
    return cumulative + pre * density


def expert_forward(rows, weight_in, weight_out):
    pre = matmul(rows, weight_in)
    hidden = jax.nn.gelu(pre, approximate=False).astype(jnp.bfloat16)
    return (pre, hidden, matmul(hidden, weight_out))


def expert_backward(rows, pre, hidden, grad_out, weight_in, weight_out):
    grad_weight_out = matmul_tn(hidden, grad_out)
    grad_hidden = matmul_nt(grad_out, weight_out)
    grad_pre = (grad_hidden * gelu_slope(pre)).astype(jnp.bfloat16)
    return (matmul_tn(rows, grad_pre), grad_weight_out, matmul_nt(grad_pre, weight_in))


def join_experts(image_rows, text_rows, pair_count, width):
    joined = jnp.concatenate(
        [
            image_rows.reshape(pair_count, PATCHES, width),
            text_rows.reshape(pair_count, CAPTION, width),
        ],
        axis=1,
    )
    return joined.reshape(-1, width)


def plain_layer(
    tokens,
    caption_lengths,
    gain_attn,
    w_query,
    w_key,
    w_value,
    w_out,
    gain_ffn,
    vis_in,
    vis_out,
    txt_in,
    txt_out,
    cotangent,
):
    seq_len = PATCHES + CAPTION
    width = tokens.shape[1]
    pair_count = tokens.shape[0] // seq_len
    half_pairs = pair_count // lax.axis_size("tensor")
    half_rows = half_pairs * seq_len
    row_start = lax.axis_index("tensor") * half_rows
    gain_one, query_w, key_w, value_w, out_w = (
        lax.all_gather(gain_attn, "dp", axis=0, tiled=True),
        lax.all_gather(w_query, "dp", axis=0, tiled=True),
        lax.all_gather(w_key, "dp", axis=0, tiled=True),
        lax.all_gather(w_value, "dp", axis=0, tiled=True),
        lax.all_gather(w_out, "dp", axis=1, tiled=True),
    )
    gain_two, vis_in_w, vis_out_w, txt_in_w, txt_out_w = (
        lax.all_gather(gain_ffn, "dp", axis=0, tiled=True),
        lax.all_gather(vis_in, "dp", axis=0, tiled=True),
        lax.all_gather(vis_out, "dp", axis=1, tiled=True),
        lax.all_gather(txt_in, "dp", axis=0, tiled=True),
        lax.all_gather(txt_out, "dp", axis=1, tiled=True),
    )
    gain_one = gain_one.astype(jnp.float32)
    gain_two = gain_two.astype(jnp.float32)
    head_local = query_w.shape[1] // HEAD_DIM
    score_scale = HEAD_DIM ** (-0.5)
    position = jnp.arange(seq_len, dtype=jnp.int32)
    live = (position[None, :] < PATCHES) | (position[None, :] - PATCHES < caption_lengths[:, None])
    valid_rows = live.astype(jnp.float32)
    mask_col = valid_rows.reshape(-1, 1)
    key_live = valid_rows[:, None, None, :] > 0.5

    def own_rows(values):
        return lax.dynamic_slice_in_dim(values, row_start, half_rows, 0)

    inputs = tokens.astype(jnp.float32)
    normed_one, inverse_one = norm_parts(inputs)
    first_in = (normed_one * gain_one).astype(jnp.bfloat16)

    def project(weight):
        return (
            matmul(first_in, weight)
            .astype(jnp.bfloat16)
            .reshape(pair_count, seq_len, head_local, HEAD_DIM)
        )

    queries = project(query_w)
    keys_all = project(key_w)
    values_all = project(value_w)

    def score_block():
        raw = (
            jnp.einsum("pqhe,pkhe->phqk", queries, keys_all, preferred_element_type=jnp.float32)
            * score_scale
        )
        return jnp.where(key_live, raw, -1e30)

    scores = score_block()
    top = jnp.max(scores, axis=-1, keepdims=True)
    weights = jnp.exp(scores - top)
    total = jnp.sum(weights, axis=-1, keepdims=True)
    probs = (weights / total).astype(jnp.bfloat16)
    log_total = top + jnp.log(total)
    context = jnp.einsum("phqk,pkhe->pqhe", probs, values_all, preferred_element_type=jnp.float32)
    context = context.astype(jnp.bfloat16).reshape(-1, head_local * HEAD_DIM)
    attn_terms = matmul(context, out_w)
    attended_own = lax.psum_scatter(
        attn_terms.astype(jnp.bfloat16), "tensor", scatter_dimension=0, tiled=True
    ).astype(jnp.float32)
    mask_own = own_rows(mask_col)
    middle_own = own_rows(inputs) + mask_own * attended_own
    normed_two, inverse_two = norm_parts(middle_own)
    second_own = (normed_two * gain_two).astype(jnp.bfloat16)
    grid = lax.all_gather(second_own, "tensor", axis=0, tiled=True).reshape(
        pair_count, seq_len, width
    )
    image_rows = grid[:, :PATCHES].reshape(-1, width)
    text_rows = grid[:, PATCHES:].reshape(-1, width)
    image_pre, image_hidden, image_part = expert_forward(image_rows, vis_in_w, vis_out_w)
    text_pre, text_hidden, text_part = expert_forward(text_rows, txt_in_w, txt_out_w)
    image_own, text_own = (
        lax.psum_scatter(
            image_part.astype(jnp.bfloat16), "tensor", scatter_dimension=0, tiled=True
        ).astype(jnp.float32),
        lax.psum_scatter(
            text_part.astype(jnp.bfloat16), "tensor", scatter_dimension=0, tiled=True
        ).astype(jnp.float32),
    )
    branch_own = join_experts(image_own, text_own, half_pairs, width)
    output_own = (middle_own + mask_own * branch_own).astype(jnp.bfloat16)
    upstream = cotangent.astype(jnp.float32)
    grad_branch = (upstream * mask_col).astype(jnp.bfloat16).reshape(pair_count, seq_len, width)
    image_grads = expert_backward(
        image_rows,
        image_pre,
        image_hidden,
        grad_branch[:, :PATCHES].reshape(-1, width),
        vis_in_w,
        vis_out_w,
    )
    text_grads = expert_backward(
        text_rows,
        text_pre,
        text_hidden,
        grad_branch[:, PATCHES:].reshape(-1, width),
        txt_in_w,
        txt_out_w,
    )
    back_image_own, back_text_own = (
        lax.psum_scatter(
            image_grads[2].astype(jnp.bfloat16), "tensor", scatter_dimension=0, tiled=True
        ).astype(jnp.float32),
        lax.psum_scatter(
            text_grads[2].astype(jnp.bfloat16), "tensor", scatter_dimension=0, tiled=True
        ).astype(jnp.float32),
    )
    grad_second_own = join_experts(back_image_own, back_text_own, half_pairs, width)
    grad_norm_own, gain_part = norm_back(grad_second_own, normed_two, inverse_two, gain_two)
    grad_middle_own = own_rows(upstream) + grad_norm_own
    output_wide, grad_middle, gain_parts = (
        lax.all_gather(
            output_own.astype(jnp.float32).astype(jnp.bfloat16), "tensor", axis=0, tiled=True
        ).astype(jnp.float32),
        lax.all_gather(grad_middle_own.astype(jnp.bfloat16), "tensor", axis=0, tiled=True).astype(
            grad_middle_own.dtype
        ),
        lax.all_gather(gain_part.astype(jnp.bfloat16), "tensor", axis=0, tiled=True).astype(
            gain_part.dtype
        ),
    )
    output = output_wide.astype(jnp.bfloat16)
    grad_gain_two = jnp.sum(gain_parts.reshape(-1, width), axis=0)
    grad_attended = (grad_middle * mask_col).astype(jnp.bfloat16)
    grad_out_w = matmul_tn(context, grad_attended)
    grad_context = (
        matmul_nt(grad_attended, out_w)
        .astype(jnp.bfloat16)
        .reshape(pair_count, seq_len, head_local, HEAD_DIM)
    )
    scores_again = score_block()
    probs_exact = jnp.exp(scores_again - log_total)
    grad_probs = jnp.einsum(
        "pqhe,pkhe->phqk", grad_context, values_all, preferred_element_type=jnp.float32
    )
    inner = jnp.sum(grad_probs * probs_exact, axis=-1, keepdims=True)
    grad_scores = (probs_exact * (grad_probs - inner)).astype(jnp.bfloat16)
    grad_values = jnp.einsum(
        "phqk,pqhe->pkhe", probs, grad_context, preferred_element_type=jnp.float32
    )
    grad_values = grad_values.astype(jnp.bfloat16).reshape(-1, head_local * HEAD_DIM)
    grad_queries = (
        jnp.einsum("phqk,pkhe->pqhe", grad_scores, keys_all, preferred_element_type=jnp.float32)
        * score_scale
    )
    grad_queries = grad_queries.astype(jnp.bfloat16).reshape(-1, head_local * HEAD_DIM)
    grad_keys = (
        jnp.einsum("phqk,pqhe->pkhe", grad_scores, queries, preferred_element_type=jnp.float32)
        * score_scale
    )
    grad_keys = grad_keys.astype(jnp.bfloat16).reshape(-1, head_local * HEAD_DIM)
    grad_query_w = matmul_tn(first_in, grad_queries)
    grad_key_w = matmul_tn(first_in, grad_keys)
    grad_value_w = matmul_tn(first_in, grad_values)
    first_part = (
        matmul_nt(grad_queries, query_w)
        + matmul_nt(grad_keys, key_w)
        + matmul_nt(grad_values, value_w)
    )
    grad_first = lax.psum(first_part.astype(jnp.bfloat16), "tensor").astype(jnp.float32)
    grad_norm_one, grad_gain_one = norm_back(grad_first, normed_one, inverse_one, gain_one)
    grad_inputs = grad_middle + grad_norm_one
    attn_sent = (
        lax.psum_scatter(grad_gain_one, "dp", scatter_dimension=0, tiled=True),
        lax.psum_scatter(grad_query_w, "dp", scatter_dimension=0, tiled=True),
        lax.psum_scatter(grad_key_w, "dp", scatter_dimension=0, tiled=True),
        lax.psum_scatter(grad_value_w, "dp", scatter_dimension=0, tiled=True),
        lax.psum_scatter(grad_out_w, "dp", scatter_dimension=1, tiled=True),
    )
    final_expert = (
        lax.psum_scatter(grad_gain_two, "dp", scatter_dimension=0, tiled=True),
        lax.psum_scatter(image_grads[0], "dp", scatter_dimension=0, tiled=True),
        lax.psum_scatter(image_grads[1], "dp", scatter_dimension=1, tiled=True),
        lax.psum_scatter(text_grads[0], "dp", scatter_dimension=0, tiled=True),
        lax.psum_scatter(text_grads[1], "dp", scatter_dimension=1, tiled=True),
    )
    return (
        output,
        grad_inputs,
        attn_sent[0],
        attn_sent[1],
        attn_sent[2],
        attn_sent[3],
        attn_sent[4],
        final_expert[0],
        final_expert[1],
        final_expert[2],
        final_expert[3],
        final_expert[4],
    )


def solution(mesh):
    def local(tokens, lengths, gain, w_query, *rest):
        ring = mesh.shape["dp"] // 2
        fits = (
            mesh.shape["tensor"] == 2
            and ring == 8
            and lengths.shape[0] == 2
            and w_query.shape[0] % 16 == 0
        )
        layer = fused_layer if fits else plain_layer
        return layer(tokens, lengths, gain, w_query, *rest)

    return jax.shard_map(
        local,
        mesh=mesh,
        in_specs=(
            P("dp", None),
            P("dp"),
            P("dp"),
            P("dp", "tensor"),
            P("dp", "tensor"),
            P("dp", "tensor"),
            P("tensor", "dp"),
            P("dp"),
            P("dp", "tensor"),
            P("tensor", "dp"),
            P("dp", "tensor"),
            P("tensor", "dp"),
            P("dp", None),
        ),
        out_specs=(
            P("dp", None),
            P("dp", None),
            P("dp"),
            P("dp", "tensor"),
            P("dp", "tensor"),
            P("dp", "tensor"),
            P("tensor", "dp"),
            P("dp"),
            P("dp", "tensor"),
            P("tensor", "dp"),
            P("dp", "tensor"),
            P("tensor", "dp"),
        ),
        check_vma=False,
    )
```

```python
import functools
import math
import types

import jax
import jax.numpy as jnp
from jax import lax
from jax.experimental import pallas as pl
from jax.experimental.pallas import tpu as pltpu
from jax.sharding import PartitionSpec as P

HEAD_DIM = 64
PATCHES = 197
CAPTION = 40
VIS = 208
TXT = 48
SEQ = VIS + TXT

MESH = pl.DeviceIdType.MESH
BF = jnp.bfloat16
F32 = jnp.float32

ATT, TIN, TOUT, VIN, VOUT = range(5)

epsilon = 1e-05
inv_root_two = 1.0 / math.sqrt(2.0)
inv_root_tau = 1.0 / math.sqrt(2.0 * math.pi)


def mm(left, right):
    return jnp.dot(left, right, preferred_element_type=F32)


def mm_nt(left, right):
    return lax.dot_general(left, right, (((1,), (1,)), ((), ())), preferred_element_type=F32)


def mm_tn(left, right):
    return lax.dot_general(left, right, (((0,), (0,)), ((), ())), preferred_element_type=F32)


def normalize(values):
    center = values - jnp.mean(values, axis=-1, keepdims=True)
    spread = jnp.mean(center * center, axis=-1, keepdims=True)
    inverse = lax.rsqrt(spread + epsilon)
    return center * inverse, inverse


def normalize_back(grad_normed, normed, inverse):
    return inverse * (
        grad_normed
        - jnp.mean(grad_normed, axis=-1, keepdims=True)
        - normed * jnp.mean(grad_normed * normed, axis=-1, keepdims=True)
    )


def unit(size):
    rows = lax.broadcasted_iota(jnp.int32, (size, size), 0)
    return (rows == lax.broadcasted_iota(jnp.int32, (size, size), 1)).astype(F32).astype(BF)


def column(ref):
    size = ref.shape[1]
    return jnp.sum(unit(size).astype(F32) * ref[...].astype(F32), axis=1, keepdims=True)


def layer_kernel(n, names, *refs):
    R = types.SimpleNamespace(**dict(zip(names, refs)))
    R.pb, R.pf, R.ga, R.rf, R.rb, R.n2 = R.pa, R.pg, R.x4, R.ra, R.rg, R.n1
    R.gat, R.gzvt, R.gqkv = R.turned, R.turned, R.n2
    S, G, PART, LAND = R.shard, R.gathered, R.part, R.land
    OUT, GW, GG = R.padded_out, R.gw, R.gg
    width = G.shape[2]
    own = width // (2 * n)
    span = width // 4
    heads = span // HEAD_DIM

    x = lax.axis_index("tensor")
    d = lax.axis_index("dp")
    c = lax.rem(d, 2)
    other = 1 - c
    chip = d // 2
    y, z = lax.rem(chip, 2), chip // 2
    r = z + y * (n - 1 - 2 * z)
    half = n // 2

    def chip_at(pos):
        pos = lax.rem(pos + 2 * n, n)
        upper = pos // half
        return 2 * (pos + upper * (n - 1 - 2 * pos)) + upper

    mate = {"dp": d + 1 - 2 * c}
    across = {"tensor": 1 - x}
    ahead = {"dp": 2 * chip_at(r + 1) + c}
    behind = {"dp": 2 * chip_at(r - 1) + c}
    way = (ahead, behind)

    def rows_at(pos):
        return pl.ds(pl.multiple_of(2 * own * chip_at(pos), 16), 2 * own)

    my_rows = pl.ds(pl.multiple_of(own * d, 16), own)

    barrier = pltpu.get_barrier_semaphore()
    for device in (mate, across, ahead, behind):
        pl.semaphore_signal(barrier, inc=1, device_id=device, device_id_type=MESH)

    mine, theirs = pl.multiple_of(2 * c, 2), pl.multiple_of(2 * other, 2)
    pair_own = 2 * c + x
    pair_across = 2 * c + 1 - x

    started = []
    counter = [0]

    def remote(source, target, device):
        index = counter[0]
        counter[0] += 1
        return pltpu.make_async_remote_copy(
            src_ref=source,
            dst_ref=target,
            send_sem=R.sent.at[index],
            recv_sem=R.came.at[index],
            device_id=device,
            device_id_type=MESH,
        )

    def start(source, target, device):
        copy = remote(source, target, device)
        copy.start()
        started.append(copy)
        return copy

    def sent(copy):
        copy.wait_send()
        started[:] = [one for one in started if one is not copy]

    near, far = (ATT, 0, width // 2), (ATT, width // 2, width // 2)
    parts = [near, far] + [(k, 0, width) for k in (TIN, TOUT, VIN, VOUT)]
    tin, tout, vin, vout = parts[2:]
    longest = half

    def hops(part, side):
        return half if (parts.index(part) + side) % 2 == 0 else n - 1 - half

    def ring_index(part, side, s):
        return (parts.index(part) * 2 + side) * longest + s

    def view(ref, part, rows):
        k, first, count = part
        return ref.at[k, rows, pl.ds(first, count)]

    def gather_copy(part, side, s, pos):
        block = view(G, part, rows_at(pos))
        i = ring_index(part, side, s)
        return pltpu.make_async_remote_copy(
            src_ref=block,
            dst_ref=block,
            send_sem=R.ring_sent.at[i],
            recv_sem=R.ring_came.at[i],
            device_id=way[side],
            device_id_type=MESH,
        )

    def gather(part, s):
        for side in range(2):
            pos = r - s if side == 0 else r + s
            if 0 < s <= hops(part, side):
                gather_copy(part, side, s - 1, pos).wait_recv()
            if s < hops(part, side):
                gather_copy(part, side, s, pos).start()

    sum_base = len(parts) * 2 * longest

    def landed(part, side, s):
        k, first, count = part
        return LAND.at[k, side * hops(part, 0) + s, :, pl.ds(first, count)]

    def sum_copy(part, side, s, source):
        i = sum_base + ring_index(part, side, s)
        return pltpu.make_async_remote_copy(
            src_ref=source,
            dst_ref=landed(part, side, s),
            send_sem=R.ring_sent.at[i],
            recv_sem=R.ring_came.at[i],
            device_id=way[side],
            device_id_type=MESH,
        )

    def pass_sum(part, s):
        for side in range(2):
            reach = hops(part, side)
            if s >= reach:
                continue
            pos = r + (reach - s) if side == 0 else r - (reach - s)
            term = view(PART, part, rows_at(pos))
            if s == 0:
                source = term
            else:
                source = landed(part, side, s - 1)
                sum_copy(part, side, s - 1, source).wait_recv()
                source[...] = (source[...].astype(F32) + term[...].astype(F32)).astype(BF)
            sum_copy(part, side, s, source).start()

    finals = []

    def end_sum(*group):
        for part in group:
            k, first, count = part
            ends = []
            for side in range(2):
                end = landed(part, side, hops(part, side) - 1)
                sum_copy(part, side, hops(part, side) - 1, end).wait_recv()
                ends.append(end)

            def total(core):
                rows = pl.ds(pl.multiple_of(own * core, 16), own)
                mine_rows = pl.ds(pl.multiple_of(2 * own * chip + own * core, 16), own)
                return (
                    ends[0][rows, :].astype(F32)
                    + ends[1][rows, :].astype(F32)
                    + PART[k, mine_rows, first : first + count].astype(F32)
                )

            cols = slice(first, first + count)
            away, home = total(other), total(c)
            R.give[k, :, cols] = away
            finals.append(
                start(R.give.at[k, :, pl.ds(first, count)], GW.at[k, c, :, pl.ds(first, count)], mate)
            )
            GW[k, c, :, cols] = home

    def shard_part(k, value):
        for core in range(2):
            S[k, core] = value(core).astype(BF)

    gain_one, gain_two = column(R.gain_attn), column(R.gain_ffn)

    def attention_part(core):
        cols = slice(core * span, (core + 1) * span)
        return jnp.concatenate(
            [
                R.w_query[:, cols].astype(F32) * (gain_one * HEAD_DIM**-0.5),
                R.w_key[:, cols].astype(F32) * gain_one,
                R.w_value[:, cols].astype(F32) * gain_one,
                R.w_out[:, cols].astype(F32),
            ],
            axis=1,
        )

    def half_of(ref, core):
        return ref[:, core * width : (core + 1) * width].astype(F32) * gain_two

    def turned_half(ref, core):
        return ref[:, core * width : (core + 1) * width]

    lengths = R.lengths

    def live(t, slots):
        return (slots < PATCHES) | ((slots >= VIS) & (slots < VIS + lengths[t]))

    def live_rows(t, j, count=64):
        slots = lax.broadcasted_iota(jnp.int32, (count, 1), 0) + j * count
        return live(t, slots).astype(F32)

    row_count = R.tokens.shape[0]

    def placed(t, slots, rows, kept):
        source = t * (PATCHES + CAPTION) + slots - (slots >= VIS).astype(jnp.int32) * (VIS - PATCHES)
        return ((rows == source) & kept).astype(F32).astype(BF)

    def chooser(t, only_live):
        slots = lax.broadcasted_iota(jnp.int32, (SEQ, row_count), 0)
        rows = lax.broadcasted_iota(jnp.int32, (SEQ, row_count), 1)
        filled = (slots < PATCHES) | ((slots >= VIS) & (slots < VIS + CAPTION))
        return placed(t, slots, rows, live(t, slots) if only_live else filled)

    shard_part(ATT, attention_part)
    G[ATT, my_rows, :] = S[ATT, c]
    for t in range(2):
        R.lens[t] = jnp.full((8, 128), lengths[t], jnp.int32).astype(F32)
    pl.semaphore_wait(barrier, 4)
    shard_a = start(S.at[pl.ds(0, 1), other], G.at[pl.ds(0, 1), my_rows, :], mate)
    send_lens = start(R.lens, R.lens4.at[pl.ds(mine, 2)], mate)
    for t in range(2):
        R.x4[2 * c + t] = mm(chooser(t, False), R.tokens[...]).astype(BF)
        R.lens4[2 * c + t] = R.lens[t]
    send_x = start(R.x4.at[pl.ds(mine, 2)], R.x4.at[pl.ds(mine, 2)], mate)
    shard_a.wait_recv()
    gather(near, 0)
    gather(far, 0)

    shard_part(TIN, functools.partial(half_of, R.txt_in))
    shard_part(TOUT, functools.partial(turned_half, R.txt_out))
    shard_part(VIN, functools.partial(half_of, R.vis_in))
    shard_part(VOUT, functools.partial(turned_half, R.vis_out))
    shard_b = start(S.at[pl.ds(1, 4), other], G.at[pl.ds(1, 4), my_rows, :], mate)
    for k in (TIN, TOUT, VIN, VOUT):
        G[k, my_rows, :] = S[k, c]
    gather(near, 1)
    for t in range(2):
        R.gz[2 * c + t] = mm(chooser(t, True), R.cotangent[...]).astype(BF)
        if t == 0:
            gather(far, 1)
    send_gz = start(R.gz.at[pl.ds(mine, 2)], R.gz.at[pl.ds(mine, 2)], mate)
    R.dy[...] = mm(chooser(x, False), R.cotangent[...]).astype(BF)
    for t in range(2):
        R.x[t] = R.x4[2 * c + t]
    gather(near, 2)
    send_x.wait_recv()

    for i in range(4):

        @pl.loop(0, SEQ // 64, unroll=True)
        def _(j, i=i):
            rows = pl.ds(pl.multiple_of(j * 64, 64), 64)
            normed, _ = normalize(R.x4[i, rows, :].astype(F32))
            R.n1[i, rows, :] = normed.astype(BF)

        R.n1t[:, i * SEQ : (i + 1) * SEQ] = R.n1[i].T
        if i == 0:
            gather(far, 2)
        if i == 1:
            gather(near, 3)
        if i == 2:
            gather(far, 3)
            shard_b.wait_recv()
            gather(tin, 0)
            gather(tout, 0)
    send_gz.wait_recv()
    send_lens.wait_recv()
    gather(near, 4)
    gather(far, 4)

    R.wo[...] = G[ATT][:, 3 * span :]

    @pl.loop(0, 4)
    def _(i):
        projected = mm(R.n1[i], G[ATT][:, : 3 * span]).astype(BF)
        R.q[i] = projected[:, :span]
        R.k[i] = projected[:, span : 2 * span]
        R.v[i] = projected[:, 2 * span :]

    lane = lax.broadcasted_iota(jnp.int32, (1, span), 1) // HEAD_DIM

    def only(head, values):
        return values * (lane == head).astype(F32).astype(BF)

    def head_rows(values, head):
        return values[head * HEAD_DIM : (head + 1) * HEAD_DIM, :]

    order = []
    for j in range(4):
        core = other if j < 2 else c
        turn = 1 - x if j % 2 == 0 else x
        order.append((turn, 2 * core + turn))
    attn_mate = [remote(R.pa.at[i], R.ra.at[turn], mate) for turn, i in order[:2]]
    cross_a = remote(R.xs, R.xr, across)
    started.append(cross_a)

    for j, (turn, i) in enumerate(order):
        q, k, v = R.q[i], R.k[i], R.v[i]
        turned_v = v.T
        slots = lax.broadcasted_iota(jnp.int32, (SEQ, 1), 0)
        caption = (slots - VIS).astype(F32) < R.lens4[i][:1, :1]
        bias = jnp.where((slots < PATCHES) | ((slots >= VIS) & caption), 0.0, -1e30)
        contexts = []
        for h in range(heads):
            scores = mm_nt(only(h, k), q) + bias
            top = jnp.max(scores, axis=0, keepdims=True)
            weights = jnp.exp(scores - top)
            total = jnp.sum(weights, axis=0, keepdims=True)
            probs = (weights * (1.0 / total)).astype(BF)
            R.probs[i * heads + h] = probs
            contexts.append(mm(head_rows(turned_v, h), probs))
        context = jnp.concatenate(contexts, axis=0).T.astype(BF)
        R.c[i] = context
        R.pa[i] = mm_nt(context, R.wo[...]).astype(BF)
        if j < 2:
            attn_mate[j].start()
        if j == 2:
            attn_mate[0].wait_recv()
            R.xs[...] = (R.pa[pair_across].astype(F32) + R.ra[1 - x].astype(F32)).astype(BF)
            cross_a.start()
        if j == 0:
            gather(tin, 1)
        if j == 1:
            gather(tout, 1)
        if j == 3:
            gather(tin, 2)

    for copy in attn_mate:
        copy.wait_send()
    attn_mate[1].wait_recv()

    @pl.loop(0, width // 256)
    def _(j):
        cols = pl.ds(pl.multiple_of(j * 256, 256), 256)
        R.gzvt[cols, : 4 * VIS] = R.gz[:, :VIS, cols].reshape(4 * VIS, 256).T
        R.gztt[cols, :] = R.gz[:, VIS:, cols].reshape(4 * TXT, 256).T

    gather(tout, 2)
    cross_a.wait_recv()

    @pl.loop(0, SEQ // 64, unroll=True)
    def _(j):
        rows = pl.ds(pl.multiple_of(j * 64, 64), 64)
        attended = (
            R.pa[pair_own, rows, :].astype(F32)
            + R.ra[x, rows, :].astype(F32)
            + R.xr[rows, :].astype(F32)
        )
        middle = R.x[x, rows, :].astype(F32) + live_rows(x, j) * attended
        R.y1[rows, :] = middle
        normed, _ = normalize(middle)
        R.n2[pair_own, rows, :] = normed.astype(BF)

    block = R.n2.at[pair_own]
    to_across = start(block, block, across)
    to_mate = start(block, block, mate)
    gather(tin, 3)
    gather(tout, 3)
    gather(vin, 0)
    gather(vout, 0)
    to_across.wait_recv()
    block = R.n2.at[pair_across]
    passed = start(block, block, mate)
    gather(tin, 4)
    gather(tout, 4)
    gather(vin, 1)
    to_mate.wait_recv()
    passed.wait_recv()

    def expert(pairs, low, high, w_in, w_out, h_ref, gu_ref, j):
        first, count = pairs
        per = high - low
        total_rows = count * per
        cols = slice(j * 256, (j + 1) * 256)
        inside = slice(first, first + count)
        R.u[:total_rows, :] = mm(
            R.n2[inside, low:high, :].reshape(total_rows, width), G[w_in, :, cols]
        )
        R.gh[:total_rows, :] = mm(
            R.gz[inside, low:high, :].reshape(total_rows, width), G[w_out, :, cols]
        )
        step = 16
        steps = total_rows // step

        @pl.loop(0, steps, unroll=steps // 2)
        def _(i):
            rows = pl.ds(pl.multiple_of(i * step, step), step)
            into = pl.ds(pl.multiple_of(first * per + i * step, step), step)
            pre = R.u[rows, :]
            cumulative = 0.5 * (1.0 + lax.erf(pre * inv_root_two))
            density = jnp.exp(-0.5 * pre * pre) * inv_root_tau
            h_ref[into, cols] = (pre * cumulative).astype(BF)
            gu_ref[into, cols] = (R.gh[rows, :] * (cumulative + pre * density)).astype(BF)

    def weight_grad(k, turned, ref, j):
        cols = slice(j * 256, (j + 1) * 256)
        PART[k, :, cols] = mm(turned, ref[:, cols]).astype(BF)

    tiles = range(width // 256)
    for j in tiles:
        expert((0, 4), VIS, SEQ, TIN, TOUT, R.ht, R.gut, j)
    gather(vout, 1)
    for j in tiles:
        weight_grad(TOUT, R.gztt[...], R.ht, j)

    @pl.loop(0, width // 256)
    def _(j):
        cols = pl.ds(pl.multiple_of(j * 256, 256), 256)
        R.n2vt[cols, :] = R.n2[:, :VIS, cols].reshape(4 * VIS, 256).T
        R.n2tt[cols, :] = R.n2[:, VIS:, cols].reshape(4 * TXT, 256).T

    gather(vin, 2)
    for j in tiles:
        weight_grad(TIN, R.n2tt[...], R.gut, j)
    gather(vout, 2)
    gather(vin, 3)
    gather(vout, 3)
    pass_sum(tout, 0)
    pass_sum(tin, 0)
    gather(vin, 4)
    gather(vout, 4)

    def terms(target, hv, ht, w_vis, w_txt, m):
        vis_rows = slice(2 * m * VIS, 2 * (m + 1) * VIS)
        txt_rows = slice(2 * m * TXT, 2 * (m + 1) * TXT)
        vis_part = mm_nt(hv[vis_rows, :], G[w_vis]).astype(BF)
        target[2 * m : 2 * m + 2, :VIS, :] = vis_part.reshape(2, VIS, width)
        txt_part = mm_nt(ht[txt_rows, :], G[w_txt]).astype(BF)
        target[2 * m : 2 * m + 2, VIS:, :] = txt_part.reshape(2, TXT, width)

    mate_g = remote(R.pg.at[pl.ds(theirs, 2)], R.rg, mate)
    cross_g = remote(R.xsg, R.xrg, across)
    gy_across = remote(R.gy.at[x], R.gy.at[x], across)
    gy_mate = remote(R.ga.at[pair_own], R.ga.at[pair_own], mate)
    gy_passed = remote(R.ga.at[pair_across], R.ga.at[pair_across], mate)
    started.extend([cross_g, gy_across, gy_mate, gy_passed])

    def image_terms(m):
        terms(R.pg, R.guv, R.gut, VIN, TIN, m)
        pl.when(c != m)(mate_g.start)

    def sum_cores(m):
        @pl.when(c == m)
        def _():
            mate_g.wait_recv()
            R.xsg[...] = (R.pg[pair_across].astype(F32) + R.rg[1 - x].astype(F32)).astype(BF)
            cross_g.start()

    def middle_back(m):
        @pl.when(c == m)
        def _():
            cross_g.wait_recv()

            @pl.loop(0, SEQ // 64, unroll=True)
            def _(j):
                rows = pl.ds(pl.multiple_of(j * 64, 64), 64)
                grad_normed = (
                    R.pg[pair_own, rows, :].astype(F32)
                    + R.rg[x, rows, :].astype(F32)
                    + R.xrg[rows, :].astype(F32)
                )
                normed, inverse = normalize(R.y1[rows, :])
                grad = R.dy[rows, :].astype(F32) + normalize_back(grad_normed, normed, inverse)
                R.gy[x, rows, :] = grad.astype(BF)
                R.ga[pair_own, rows, :] = (grad * live_rows(x, j)).astype(BF)

            gy_across.start()
            gy_mate.start()

    def middle_pass(m):
        @pl.when(c == m)
        def _():
            gy_across.wait_recv()

            @pl.loop(0, SEQ // 64, unroll=True)
            def _(j):
                rows = pl.ds(pl.multiple_of(j * 64, 64), 64)
                R.ga[pair_across, rows, :] = (
                    R.gy[1 - x, rows, :].astype(F32) * live_rows(1 - x, j)
                ).astype(BF)

            gy_passed.start()

    def middle_came(m):
        @pl.when(c != m)
        def _():
            gy_mate.wait_recv()
            gy_passed.wait_recv()

    sent(send_x)
    for j in tiles:
        expert((0, 2), 0, VIS, VIN, VOUT, R.hv, R.guv, j)
        if j == 1:
            pass_sum(tout, 1)
    image_terms(0)
    pass_sum(tin, 1)
    expert((2, 2), 0, VIS, VIN, VOUT, R.hv, R.guv, 0)
    sum_cores(0)
    expert((2, 2), 0, VIS, VIN, VOUT, R.hv, R.guv, 1)
    pass_sum(tout, 2)
    for j in tiles[2:]:
        expert((2, 2), 0, VIS, VIN, VOUT, R.hv, R.guv, j)
    image_terms(1)
    pass_sum(tin, 2)
    for copy in (to_across, to_mate, passed):
        sent(copy)
    weight_grad(VOUT, R.gzvt[:, : 4 * VIS], R.hv, 0)
    sum_cores(1)
    middle_back(0)
    for j in tiles[1:]:
        weight_grad(VOUT, R.gzvt[:, : 4 * VIS], R.hv, j)
    pass_sum(tout, 3)
    pass_sum(vout, 0)
    for j in tiles:
        weight_grad(VIN, R.n2vt[...], R.guv, j)
    pass_sum(tin, 3)
    pass_sum(vin, 0)

    mate_g.wait_send()
    terms(R.pf, R.hv, R.ht, VOUT, TOUT, 0)
    middle_pass(0)
    middle_back(1)
    end_sum(tout, tin)
    terms(R.pf, R.hv, R.ht, VOUT, TOUT, 1)
    mate_f = start(R.pf.at[pl.ds(theirs, 2)], R.rf, mate)
    cross_f = remote(R.xsf, R.xrf, across)
    started.append(cross_f)
    pass_sum(vout, 1)
    middle_came(0)

    back_mate = [remote(R.pb.at[theirs + t], R.rb.at[t], mate) for t in range(2)]
    back_cross = [remote(R.xsb.at[t], R.xrb.at[t], across) for t in range(2)]
    started.extend(back_mate + back_cross)

    def attention_back(m, t):
        i = 2 * m + t
        grad_context = mm(R.ga[i], R.wo[...]).astype(BF)
        R.gat[:, i * SEQ : (i + 1) * SEQ] = R.ga[i].T
        q, k, v = R.q[i], R.k[i], R.v[i]
        turned_k = k.T
        grad_q = []
        grad_k = jnp.zeros((SEQ, span), F32)
        grad_v = jnp.zeros((SEQ, span), F32)
        for h in range(heads):
            probs = R.probs[i * heads + h]
            grad_probs = mm_nt(only(h, v), grad_context)
            exact = probs.astype(F32)
            inner = jnp.sum(grad_probs * exact, axis=0, keepdims=True)
            grad_scores = (exact * (grad_probs - inner)).astype(BF)
            grad_q.append(mm(head_rows(turned_k, h), grad_scores))
            grad_k += mm(grad_scores, only(h, q))
            grad_v += mm(probs, only(h, grad_context))
        grad_q = jnp.concatenate(grad_q, axis=0).T
        joined = jnp.concatenate([grad_q, grad_k, grad_v], axis=1).astype(BF)
        R.gqkv[i, :, : 3 * span] = joined
        R.pb[i] = mm_nt(joined, G[ATT][:, : 3 * span]).astype(BF)
        pl.when(c != m)(back_mate[t].start)

    def back_sum(m):
        @pl.when(c == m)
        def _():
            for t in range(2):
                back_mate[t].wait_recv()
                R.xsb[t] = (R.pb[2 * m + t].astype(F32) + R.rb[t].astype(F32)).astype(BF)
                back_cross[t].start()

    attention_back(0, 0)
    pass_sum(vin, 1)
    mate_f.wait_recv()
    R.xsf[...] = (R.pf[pair_across].astype(F32) + R.rf[1 - x].astype(F32)).astype(BF)
    middle_pass(1)
    cross_f.start()
    attention_back(0, 1)
    pass_sum(vout, 2)
    middle_came(1)
    attention_back(1, 0)
    pass_sum(vin, 2)
    back_sum(0)
    attention_back(1, 1)
    pass_sum(vout, 3)
    pass_sum(vin, 3)

    @pl.loop(0, 3)
    def _(j):
        rows = pl.ds(pl.multiple_of(j * 256, 256), 256)
        grads = mm(R.n1t[rows, :], R.gqkv[:, :, : 3 * span].reshape(4 * SEQ, 3 * span))
        grad_o = mm(R.gat[rows, :], R.c[...].reshape(4 * SEQ, span))
        PART[ATT, rows, :] = jnp.concatenate([grads, grad_o], axis=1).astype(BF)

    pass_sum(near, 0)
    pass_sum(far, 0)
    back_sum(1)
    end_sum(vout, vin)

    cross_f.wait_recv()

    @pl.loop(0, SEQ // 64, unroll=True)
    def _(j):
        rows = pl.ds(pl.multiple_of(j * 64, 64), 64)
        branch = (
            R.pf[pair_own, rows, :].astype(F32)
            + R.rf[x, rows, :].astype(F32)
            + R.xrf[rows, :].astype(F32)
        )
        OUT[x, rows, :] = (R.y1[rows, :] + live_rows(x, j) * branch).astype(BF)

    out_across = start(OUT.at[x], OUT.at[x], across)
    pass_sum(near, 1)
    pass_sum(far, 1)

    for t in range(2):
        back_cross[t].wait_recv()

        @pl.loop(0, SEQ // 64, unroll=True)
        def _(j, t=t):
            rows = pl.ds(pl.multiple_of(j * 64, 64), 64)
            grad_normed = R.xsb[t, rows, :].astype(F32) + R.xrb[t, rows, :].astype(F32)
            normed, inverse = normalize(R.x[t, rows, :].astype(F32))
            grad = R.gy[t, rows, :].astype(F32) + normalize_back(grad_normed, normed, inverse)
            high = grad.astype(BF)
            rows = pl.ds(pl.multiple_of(t * SEQ + j * 64, 64), 64)
            R.hv[rows, :] = high
            R.guv[rows, :] = (grad - high.astype(F32)).astype(BF)

        pass_sum(near, 2 + t)
        pass_sum(far, 2 + t)

    slots = lax.broadcasted_iota(jnp.int32, (row_count, 2 * SEQ), 1)
    rows = lax.broadcasted_iota(jnp.int32, (row_count, 2 * SEQ), 0)
    turn = slots // SEQ
    back = placed(turn, slots - turn * SEQ, rows, slots >= 0)
    out_across.wait_recv()
    R.out_tokens[...] = mm(back, OUT[...].reshape(2 * SEQ, width)).astype(BF)
    R.grad_tokens[...] = mm(back, R.hv[: 2 * SEQ, :]) + mm(back, R.guv[: 2 * SEQ, :])
    end_sum(near, far)
    for copy in finals:
        copy.wait_recv()

    def row_sums(k, last):
        return sum(
            jnp.sum(S[k, core][:, :last].astype(F32) * GW[k, core][:, :last], axis=-1, keepdims=True)
            for core in range(2)
        )

    R.gs[0] = jnp.broadcast_to(row_sums(ATT, 3 * span), (own, 128))
    R.gs[1] = jnp.broadcast_to(row_sums(TIN, width) + row_sums(VIN, width), (own, 128))
    cross_gain = start(R.gs, R.gr, across)
    cross_gain.wait_recv()
    GG[...] = R.gs[...] + R.gr[...]

    for copy in started:
        copy.wait_send()
    for part in parts:
        for side in range(2):
            for s in range(hops(part, side)):
                gather_copy(part, side, s, r).wait_send()
                sum_copy(part, side, s, landed(part, side, s)).wait_send()


def finish_kernel(out, gtok, gw, gg, gain_attn, gain_ffn, *rest):
    (
        out_tokens,
        grad_tokens,
        grad_gain_attn,
        grad_query,
        grad_key,
        grad_value,
        grad_out,
        grad_gain_ffn,
        grad_vis_in,
        grad_vis_out,
        grad_txt_in,
        grad_txt_out,
    ) = rest
    out_tokens[...] = out[...]
    grad_tokens[...] = gtok[...]
    width = gw.shape[3]
    own = gw.shape[2]
    span = width // 4
    gain_one, gain_two = column(gain_attn), column(gain_ffn)
    square = unit(own).astype(F32)
    grad_gain_attn[...] = jnp.sum(square * (gg[0][:, :1] / gain_one), axis=0, keepdims=True)
    grad_gain_ffn[...] = jnp.sum(square * (gg[1][:, :1] / gain_two), axis=0, keepdims=True)

    def both(part):
        return jnp.concatenate([gw[ATT, core][:, part * span : (part + 1) * span] for core in range(2)], axis=1)

    grad_query[...] = both(0) * (gain_one * HEAD_DIM**-0.5)
    grad_key[...] = both(1) * gain_one
    grad_value[...] = both(2) * gain_one
    grad_out[...] = both(3)
    for core in range(2):
        part = slice(core * width, (core + 1) * width)
        grad_vis_in[:, part] = gw[VIN, core] * gain_two
        grad_txt_in[:, part] = gw[TIN, core] * gain_two
        grad_vis_out[:, part] = gw[VOUT, core]
        grad_txt_out[:, part] = gw[TOUT, core]


def fused_layer(
    tokens,
    caption_lengths,
    gain_attn,
    w_query,
    w_key,
    w_value,
    w_out,
    gain_ffn,
    vis_in,
    vis_out,
    txt_in,
    txt_out,
    cotangent,
):
    n = lax.axis_size("dp") // 2
    own = w_query.shape[0]
    row_count, width = tokens.shape
    span = width // 4
    heads = span // HEAD_DIM
    gain_one, gain_two = gain_attn.reshape(1, own), gain_ffn.reshape(1, own)

    rows = 4 * SEQ
    scratch = dict(
        shard=pltpu.VMEM((5, 2, own, width), BF),
        lens=pltpu.VMEM((2, 8, 128), F32),
        x=pltpu.VMEM((2, SEQ, width), BF),
        dy=pltpu.VMEM((SEQ, width), BF),
        padded_out=pltpu.VMEM((2, SEQ, width), BF),
        gathered=pltpu.VMEM((5, width, width), BF),
        part=pltpu.VMEM((5, width, width), BF),
        land=pltpu.VMEM((5, n - 1, 2 * own, width), BF),
        give=pltpu.VMEM((5, own, width), F32),
        x4=pltpu.VMEM((4, SEQ, width), BF),
        lens4=pltpu.VMEM((4, 8, 128), F32),
        n1=pltpu.VMEM((4, SEQ, width), BF),
        n1t=pltpu.VMEM((width, rows), BF),
        gz=pltpu.VMEM((4, SEQ, width), BF),
        turned=pltpu.VMEM((width, rows), BF),
        gztt=pltpu.VMEM((width, 4 * TXT), BF),
        wo=pltpu.VMEM((width, span), BF),
        q=pltpu.VMEM((4, SEQ, span), BF),
        k=pltpu.VMEM((4, SEQ, span), BF),
        v=pltpu.VMEM((4, SEQ, span), BF),
        c=pltpu.VMEM((4, SEQ, span), BF),
        probs=pltpu.VMEM((4 * heads, SEQ, SEQ), BF),
        pa=pltpu.VMEM((4, SEQ, width), BF),
        ra=pltpu.VMEM((2, SEQ, width), BF),
        xs=pltpu.VMEM((SEQ, width), BF),
        xr=pltpu.VMEM((SEQ, width), BF),
        y1=pltpu.VMEM((SEQ, width), F32),
        n2vt=pltpu.VMEM((width, 4 * VIS), BF),
        n2tt=pltpu.VMEM((width, 4 * TXT), BF),
        u=pltpu.VMEM((4 * VIS, 256), F32),
        gh=pltpu.VMEM((4 * VIS, 256), F32),
        hv=pltpu.VMEM((4 * VIS, width), BF),
        guv=pltpu.VMEM((4 * VIS, width), BF),
        ht=pltpu.VMEM((4 * TXT, width), BF),
        gut=pltpu.VMEM((4 * TXT, width), BF),
        pg=pltpu.VMEM((4, SEQ, width), BF),
        rg=pltpu.VMEM((2, SEQ, width), BF),
        xsg=pltpu.VMEM((SEQ, width), BF),
        xrg=pltpu.VMEM((SEQ, width), BF),
        gy=pltpu.VMEM((2, SEQ, width), BF),
        xsf=pltpu.VMEM((SEQ, width), BF),
        xrf=pltpu.VMEM((SEQ, width), BF),
        xsb=pltpu.VMEM((2, SEQ, width), BF),
        xrb=pltpu.VMEM((2, SEQ, width), BF),
        gs=pltpu.VMEM((2, own, 128), F32),
        gr=pltpu.VMEM((2, own, 128), F32),
        sent=pltpu.SemaphoreType.DMA((40,)),
        came=pltpu.SemaphoreType.DMA((40,)),
        ring_sent=pltpu.SemaphoreType.DMA((6 * 2 * (n // 2) * 2,)),
        ring_came=pltpu.SemaphoreType.DMA((6 * 2 * (n // 2) * 2,)),
    )
    inputs = dict(
        lengths=caption_lengths,
        tokens=tokens,
        cotangent=cotangent,
        gain_attn=gain_one,
        gain_ffn=gain_two,
        w_query=w_query,
        w_key=w_key,
        w_value=w_value,
        w_out=w_out.T,
        vis_in=vis_in,
        vis_out=vis_out.T,
        txt_in=txt_in,
        txt_out=txt_out.T,
    )
    results = dict(
        out_tokens=jax.ShapeDtypeStruct((row_count, width), BF),
        grad_tokens=jax.ShapeDtypeStruct((row_count, width), F32),
        gw=jax.ShapeDtypeStruct((5, 2, own, width), F32),
        gg=jax.ShapeDtypeStruct((2, own, 128), F32),
    )
    vmem = pl.BlockSpec(memory_space=pltpu.VMEM)
    names = tuple(inputs) + tuple(results) + tuple(scratch)
    out, gtok, gw, gg = pl.pallas_call(
        functools.partial(layer_kernel, n, names),
        out_shape=tuple(results.values()),
        in_specs=[pl.BlockSpec(memory_space=pltpu.SMEM)] + [vmem] * (len(inputs) - 1),
        out_specs=[vmem] * len(results),
        scratch_shapes=list(scratch.values()),
        compiler_params=pltpu.CompilerParams(
            collective_id=0, has_side_effects=True, vmem_limit_bytes=60 * 2**20
        ),
    )(*inputs.values())

    final = pl.pallas_call(
        finish_kernel,
        out_shape=(
            jax.ShapeDtypeStruct((row_count, width), BF),
            jax.ShapeDtypeStruct((row_count, width), F32),
            jax.ShapeDtypeStruct((1, own), F32),
            jax.ShapeDtypeStruct((own, 2 * span), F32),
            jax.ShapeDtypeStruct((own, 2 * span), F32),
            jax.ShapeDtypeStruct((own, 2 * span), F32),
            jax.ShapeDtypeStruct((own, 2 * span), F32),
            jax.ShapeDtypeStruct((1, own), F32),
            jax.ShapeDtypeStruct((own, 2 * width), F32),
            jax.ShapeDtypeStruct((own, 2 * width), F32),
            jax.ShapeDtypeStruct((own, 2 * width), F32),
            jax.ShapeDtypeStruct((own, 2 * width), F32),
        ),
        in_specs=[vmem] * 6,
        out_specs=[vmem] * 12,
        compiler_params=pltpu.CompilerParams(vmem_limit_bytes=60 * 2**20),
    )(out, gtok, gw, gg, gain_one, gain_two)
    final = list(final)
    final[2] = final[2].reshape(own)
    final[7] = final[7].reshape(own)
    for turned in (6, 9, 11):
        final[turned] = final[turned].T
    return tuple(final)


def norm_parts(values):
    center = values - jnp.mean(values, axis=-1, keepdims=True)
    spread = jnp.mean(center * center, axis=-1, keepdims=True)
    inverse = lax.rsqrt(spread + epsilon)
    return (center * inverse, inverse)


def norm_back(grad_out, normed, inverse, gain):
    grad_normed = grad_out * gain
    grad_gain = jnp.sum(grad_out * normed, axis=0)
    inner = (
        grad_normed
        - jnp.mean(grad_normed, axis=-1, keepdims=True)
        - normed * jnp.mean(grad_normed * normed, axis=-1, keepdims=True)
    )
    return (inverse * inner, grad_gain)


def matmul(left, right):
    return jnp.dot(left, right, preferred_element_type=jnp.float32)


def matmul_tn(left, right):
    return lax.dot_general(
        left, right, (((0,), (0,)), ((), ())), preferred_element_type=jnp.float32
    )


def matmul_nt(left, right):
    return lax.dot_general(
        left, right, (((1,), (1,)), ((), ())), preferred_element_type=jnp.float32
    )


def gelu_slope(pre):
    cumulative = 0.5 * (1.0 + lax.erf(pre * inv_root_two))
    density = jnp.exp(-0.5 * pre * pre) * inv_root_tau
    return cumulative + pre * density


def expert_forward(rows, weight_in, weight_out):
    pre = matmul(rows, weight_in)
    hidden = jax.nn.gelu(pre, approximate=False).astype(jnp.bfloat16)
    return (pre, hidden, matmul(hidden, weight_out))


def expert_backward(rows, pre, hidden, grad_out, weight_in, weight_out):
    grad_weight_out = matmul_tn(hidden, grad_out)
    grad_hidden = matmul_nt(grad_out, weight_out)
    grad_pre = (grad_hidden * gelu_slope(pre)).astype(jnp.bfloat16)
    return (matmul_tn(rows, grad_pre), grad_weight_out, matmul_nt(grad_pre, weight_in))


def join_experts(image_rows, text_rows, pair_count, width):
    joined = jnp.concatenate(
        [
            image_rows.reshape(pair_count, PATCHES, width),
            text_rows.reshape(pair_count, CAPTION, width),
        ],
        axis=1,
    )
    return joined.reshape(-1, width)


def plain_layer(
    tokens,
    caption_lengths,
    gain_attn,
    w_query,
    w_key,
    w_value,
    w_out,
    gain_ffn,
    vis_in,
    vis_out,
    txt_in,
    txt_out,
    cotangent,
):
    seq_len = PATCHES + CAPTION
    width = tokens.shape[1]
    pair_count = tokens.shape[0] // seq_len
    half_pairs = pair_count // lax.axis_size("tensor")
    half_rows = half_pairs * seq_len
    row_start = lax.axis_index("tensor") * half_rows
    gain_one, query_w, key_w, value_w, out_w = (
        lax.all_gather(gain_attn, "dp", axis=0, tiled=True),
        lax.all_gather(w_query, "dp", axis=0, tiled=True),
        lax.all_gather(w_key, "dp", axis=0, tiled=True),
        lax.all_gather(w_value, "dp", axis=0, tiled=True),
        lax.all_gather(w_out, "dp", axis=1, tiled=True),
    )
    gain_two, vis_in_w, vis_out_w, txt_in_w, txt_out_w = (
        lax.all_gather(gain_ffn, "dp", axis=0, tiled=True),
        lax.all_gather(vis_in, "dp", axis=0, tiled=True),
        lax.all_gather(vis_out, "dp", axis=1, tiled=True),
        lax.all_gather(txt_in, "dp", axis=0, tiled=True),
        lax.all_gather(txt_out, "dp", axis=1, tiled=True),
    )
    gain_one = gain_one.astype(jnp.float32)
    gain_two = gain_two.astype(jnp.float32)
    head_local = query_w.shape[1] // HEAD_DIM
    score_scale = HEAD_DIM ** (-0.5)
    position = jnp.arange(seq_len, dtype=jnp.int32)
    live = (position[None, :] < PATCHES) | (position[None, :] - PATCHES < caption_lengths[:, None])
    valid_rows = live.astype(jnp.float32)
    mask_col = valid_rows.reshape(-1, 1)
    key_live = valid_rows[:, None, None, :] > 0.5

    def own_rows(values):
        return lax.dynamic_slice_in_dim(values, row_start, half_rows, 0)

    inputs = tokens.astype(jnp.float32)
    normed_one, inverse_one = norm_parts(inputs)
    first_in = (normed_one * gain_one).astype(jnp.bfloat16)

    def project(weight):
        return (
            matmul(first_in, weight)
            .astype(jnp.bfloat16)
            .reshape(pair_count, seq_len, head_local, HEAD_DIM)
        )

    queries = project(query_w)
    keys_all = project(key_w)
    values_all = project(value_w)

    def score_block():
        raw = (
            jnp.einsum("pqhe,pkhe->phqk", queries, keys_all, preferred_element_type=jnp.float32)
            * score_scale
        )
        return jnp.where(key_live, raw, -1e30)

    scores = score_block()
    top = jnp.max(scores, axis=-1, keepdims=True)
    weights = jnp.exp(scores - top)
    total = jnp.sum(weights, axis=-1, keepdims=True)
    probs = (weights / total).astype(jnp.bfloat16)
    log_total = top + jnp.log(total)
    context = jnp.einsum("phqk,pkhe->pqhe", probs, values_all, preferred_element_type=jnp.float32)
    context = context.astype(jnp.bfloat16).reshape(-1, head_local * HEAD_DIM)
    attn_terms = matmul(context, out_w)
    attended_own = lax.psum_scatter(
        attn_terms.astype(jnp.bfloat16), "tensor", scatter_dimension=0, tiled=True
    ).astype(jnp.float32)
    mask_own = own_rows(mask_col)
    middle_own = own_rows(inputs) + mask_own * attended_own
    normed_two, inverse_two = norm_parts(middle_own)
    second_own = (normed_two * gain_two).astype(jnp.bfloat16)
    grid = lax.all_gather(second_own, "tensor", axis=0, tiled=True).reshape(
        pair_count, seq_len, width
    )
    image_rows = grid[:, :PATCHES].reshape(-1, width)
    text_rows = grid[:, PATCHES:].reshape(-1, width)
    image_pre, image_hidden, image_part = expert_forward(image_rows, vis_in_w, vis_out_w)
    text_pre, text_hidden, text_part = expert_forward(text_rows, txt_in_w, txt_out_w)
    image_own, text_own = (
        lax.psum_scatter(
            image_part.astype(jnp.bfloat16), "tensor", scatter_dimension=0, tiled=True
        ).astype(jnp.float32),
        lax.psum_scatter(
            text_part.astype(jnp.bfloat16), "tensor", scatter_dimension=0, tiled=True
        ).astype(jnp.float32),
    )
    branch_own = join_experts(image_own, text_own, half_pairs, width)
    output_own = (middle_own + mask_own * branch_own).astype(jnp.bfloat16)
    upstream = cotangent.astype(jnp.float32)
    grad_branch = (upstream * mask_col).astype(jnp.bfloat16).reshape(pair_count, seq_len, width)
    image_grads = expert_backward(
        image_rows,
        image_pre,
        image_hidden,
        grad_branch[:, :PATCHES].reshape(-1, width),
        vis_in_w,
        vis_out_w,
    )
    text_grads = expert_backward(
        text_rows,
        text_pre,
        text_hidden,
        grad_branch[:, PATCHES:].reshape(-1, width),
        txt_in_w,
        txt_out_w,
    )
    back_image_own, back_text_own = (
        lax.psum_scatter(
            image_grads[2].astype(jnp.bfloat16), "tensor", scatter_dimension=0, tiled=True
        ).astype(jnp.float32),
        lax.psum_scatter(
            text_grads[2].astype(jnp.bfloat16), "tensor", scatter_dimension=0, tiled=True
        ).astype(jnp.float32),
    )
    grad_second_own = join_experts(back_image_own, back_text_own, half_pairs, width)
    grad_norm_own, gain_part = norm_back(grad_second_own, normed_two, inverse_two, gain_two)
    grad_middle_own = own_rows(upstream) + grad_norm_own
    output_wide, grad_middle, gain_parts = (
        lax.all_gather(
            output_own.astype(jnp.float32).astype(jnp.bfloat16), "tensor", axis=0, tiled=True
        ).astype(jnp.float32),
        lax.all_gather(grad_middle_own.astype(jnp.bfloat16), "tensor", axis=0, tiled=True).astype(
            grad_middle_own.dtype
        ),
        lax.all_gather(gain_part.astype(jnp.bfloat16), "tensor", axis=0, tiled=True).astype(
            gain_part.dtype
        ),
    )
    output = output_wide.astype(jnp.bfloat16)
    grad_gain_two = jnp.sum(gain_parts.reshape(-1, width), axis=0)
    grad_attended = (grad_middle * mask_col).astype(jnp.bfloat16)
    grad_out_w = matmul_tn(context, grad_attended)
    grad_context = (
        matmul_nt(grad_attended, out_w)
        .astype(jnp.bfloat16)
        .reshape(pair_count, seq_len, head_local, HEAD_DIM)
    )
    scores_again = score_block()
    probs_exact = jnp.exp(scores_again - log_total)
    grad_probs = jnp.einsum(
        "pqhe,pkhe->phqk", grad_context, values_all, preferred_element_type=jnp.float32
    )
    inner = jnp.sum(grad_probs * probs_exact, axis=-1, keepdims=True)
    grad_scores = (probs_exact * (grad_probs - inner)).astype(jnp.bfloat16)
    grad_values = jnp.einsum(
        "phqk,pqhe->pkhe", probs, grad_context, preferred_element_type=jnp.float32
    )
    grad_values = grad_values.astype(jnp.bfloat16).reshape(-1, head_local * HEAD_DIM)
    grad_queries = (
        jnp.einsum("phqk,pkhe->pqhe", grad_scores, keys_all, preferred_element_type=jnp.float32)
        * score_scale
    )
    grad_queries = grad_queries.astype(jnp.bfloat16).reshape(-1, head_local * HEAD_DIM)
    grad_keys = (
        jnp.einsum("phqk,pqhe->pkhe", grad_scores, queries, preferred_element_type=jnp.float32)
        * score_scale
    )
    grad_keys = grad_keys.astype(jnp.bfloat16).reshape(-1, head_local * HEAD_DIM)
    grad_query_w = matmul_tn(first_in, grad_queries)
    grad_key_w = matmul_tn(first_in, grad_keys)
    grad_value_w = matmul_tn(first_in, grad_values)
    first_part = (
        matmul_nt(grad_queries, query_w)
        + matmul_nt(grad_keys, key_w)
        + matmul_nt(grad_values, value_w)
    )
    grad_first = lax.psum(first_part.astype(jnp.bfloat16), "tensor").astype(jnp.float32)
    grad_norm_one, grad_gain_one = norm_back(grad_first, normed_one, inverse_one, gain_one)
    grad_inputs = grad_middle + grad_norm_one
    attn_sent = (
        lax.psum_scatter(grad_gain_one, "dp", scatter_dimension=0, tiled=True),
        lax.psum_scatter(grad_query_w, "dp", scatter_dimension=0, tiled=True),
        lax.psum_scatter(grad_key_w, "dp", scatter_dimension=0, tiled=True),
        lax.psum_scatter(grad_value_w, "dp", scatter_dimension=0, tiled=True),
        lax.psum_scatter(grad_out_w, "dp", scatter_dimension=1, tiled=True),
    )
    final_expert = (
        lax.psum_scatter(grad_gain_two, "dp", scatter_dimension=0, tiled=True),
        lax.psum_scatter(image_grads[0], "dp", scatter_dimension=0, tiled=True),
        lax.psum_scatter(image_grads[1], "dp", scatter_dimension=1, tiled=True),
        lax.psum_scatter(text_grads[0], "dp", scatter_dimension=0, tiled=True),
        lax.psum_scatter(text_grads[1], "dp", scatter_dimension=1, tiled=True),
    )
    return (
        output,
        grad_inputs,
        attn_sent[0],
        attn_sent[1],
        attn_sent[2],
        attn_sent[3],
        attn_sent[4],
        final_expert[0],
        final_expert[1],
        final_expert[2],
        final_expert[3],
        final_expert[4],
    )


def solution(mesh):
    def local(tokens, lengths, gain, w_query, *rest):
        ring = mesh.shape["dp"] // 2
        fits = (
            mesh.shape["tensor"] == 2
            and ring == 8
            and lengths.shape[0] == 2
            and w_query.shape[0] % 16 == 0
        )
        layer = fused_layer if fits else plain_layer
        return layer(tokens, lengths, gain, w_query, *rest)

    return jax.shard_map(
        local,
        mesh=mesh,
        in_specs=(
            P("dp", None),
            P("dp"),
            P("dp"),
            P("dp", "tensor"),
            P("dp", "tensor"),
            P("dp", "tensor"),
            P("tensor", "dp"),
            P("dp"),
            P("dp", "tensor"),
            P("tensor", "dp"),
            P("dp", "tensor"),
            P("tensor", "dp"),
            P("dp", None),
        ),
        out_specs=(
            P("dp", None),
            P("dp", None),
            P("dp"),
            P("dp", "tensor"),
            P("dp", "tensor"),
            P("dp", "tensor"),
            P("tensor", "dp"),
            P("dp"),
            P("dp", "tensor"),
            P("tensor", "dp"),
            P("dp", "tensor"),
            P("tensor", "dp"),
        ),
        check_vma=False,
    )
```

```python
import functools
import math
import types

import jax
import jax.numpy as jnp
from jax import lax
from jax.experimental import pallas as pl
from jax.experimental.pallas import tpu as pltpu
from jax.sharding import PartitionSpec as P

HEAD_DIM = 64
PATCHES = 197
CAPTION = 40
VIS = 208
TXT = 48
SEQ = VIS + TXT

MESH = pl.DeviceIdType.MESH
BF = jnp.bfloat16
F32 = jnp.float32

ATT, TIN, TOUT, VIN, VOUT = range(5)

epsilon = 1e-05
inv_root_two = 1.0 / math.sqrt(2.0)
inv_root_tau = 1.0 / math.sqrt(2.0 * math.pi)


def mm(left, right):
    return jnp.dot(left, right, preferred_element_type=F32)


def mm_nt(left, right):
    return lax.dot_general(left, right, (((1,), (1,)), ((), ())), preferred_element_type=F32)


def mm_tn(left, right):
    return lax.dot_general(left, right, (((0,), (0,)), ((), ())), preferred_element_type=F32)


def normalize(values):
    center = values - jnp.mean(values, axis=-1, keepdims=True)
    spread = jnp.mean(center * center, axis=-1, keepdims=True)
    inverse = lax.rsqrt(spread + epsilon)
    return center * inverse, inverse


def normalize_back(grad_normed, normed, inverse):
    return inverse * (
        grad_normed
        - jnp.mean(grad_normed, axis=-1, keepdims=True)
        - normed * jnp.mean(grad_normed * normed, axis=-1, keepdims=True)
    )


def unit(size):
    rows = lax.broadcasted_iota(jnp.int32, (size, size), 0)
    return (rows == lax.broadcasted_iota(jnp.int32, (size, size), 1)).astype(F32).astype(BF)


def column(ref):
    size = ref.shape[1]
    return jnp.sum(unit(size).astype(F32) * ref[...].astype(F32), axis=1, keepdims=True)


def layer_kernel(n, names, *refs):
    R = types.SimpleNamespace(**dict(zip(names, refs)))
    R.pb, R.pf, R.ga, R.rf, R.rb, R.n2 = R.pa, R.pg, R.x4, R.ra, R.rg, R.n1
    R.gat, R.gzvt, R.gqkv = R.turned, R.turned, R.n2
    S, G, PART, LAND = R.shard, R.gathered, R.part, R.land
    OUT, GW, GG = R.padded_out, R.gw, R.gg
    width = G.shape[2]
    own = width // (2 * n)
    span = width // 4
    heads = span // HEAD_DIM

    x = lax.axis_index("tensor")
    d = lax.axis_index("dp")
    c = lax.rem(d, 2)
    other = 1 - c
    chip = d // 2
    y, z = lax.rem(chip, 2), chip // 2
    r = z + y * (n - 1 - 2 * z)
    half = n // 2

    def chip_at(pos):
        pos = lax.rem(pos + 2 * n, n)
        upper = pos // half
        return 2 * (pos + upper * (n - 1 - 2 * pos)) + upper

    mate = {"dp": d + 1 - 2 * c}
    across = {"tensor": 1 - x}
    ahead = {"dp": 2 * chip_at(r + 1) + c}
    behind = {"dp": 2 * chip_at(r - 1) + c}
    way = (ahead, behind)

    def rows_at(pos):
        return pl.ds(pl.multiple_of(2 * own * chip_at(pos), 16), 2 * own)

    my_rows = pl.ds(pl.multiple_of(own * d, 16), own)

    barrier = pltpu.get_barrier_semaphore()
    for device in (mate, across, ahead, behind):
        pl.semaphore_signal(barrier, inc=1, device_id=device, device_id_type=MESH)

    mine, theirs = pl.multiple_of(2 * c, 2), pl.multiple_of(2 * other, 2)
    pair_own = 2 * c + x
    pair_across = 2 * c + 1 - x

    started = []
    counter = [0]

    def remote(source, target, device):
        index = counter[0]
        counter[0] += 1
        return pltpu.make_async_remote_copy(
            src_ref=source,
            dst_ref=target,
            send_sem=R.sent.at[index],
            recv_sem=R.came.at[index],
            device_id=device,
            device_id_type=MESH,
        )

    def start(source, target, device):
        copy = remote(source, target, device)
        copy.start()
        started.append(copy)
        return copy

    def sent(copy):
        copy.wait_send()
        started[:] = [one for one in started if one is not copy]

    near, far = (ATT, 0, width // 2), (ATT, width // 2, width // 2)
    parts = [near, far] + [(k, 0, width) for k in (TIN, TOUT, VIN, VOUT)]
    tin, tout, vin, vout = parts[2:]
    longest = half

    def hops(part, side):
        return half if (parts.index(part) + side) % 2 == 0 else n - 1 - half

    def ring_index(part, side, s):
        return (parts.index(part) * 2 + side) * longest + s

    def view(ref, part, rows):
        k, first, count = part
        return ref.at[k, rows, pl.ds(first, count)]

    def gather_copy(part, side, s, pos):
        block = view(G, part, rows_at(pos))
        i = ring_index(part, side, s)
        return pltpu.make_async_remote_copy(
            src_ref=block,
            dst_ref=block,
            send_sem=R.ring_sent.at[i],
            recv_sem=R.ring_came.at[i],
            device_id=way[side],
            device_id_type=MESH,
        )

    def gather(part, s):
        for side in range(2):
            pos = r - s if side == 0 else r + s
            if 0 < s <= hops(part, side):
                gather_copy(part, side, s - 1, pos).wait_recv()
            if s < hops(part, side):
                gather_copy(part, side, s, pos).start()

    sum_base = len(parts) * 2 * longest

    def landed(part, side, s):
        k, first, count = part
        return LAND.at[k, side * hops(part, 0) + s, :, pl.ds(first, count)]

    def sum_copy(part, side, s, source):
        i = sum_base + ring_index(part, side, s)
        return pltpu.make_async_remote_copy(
            src_ref=source,
            dst_ref=landed(part, side, s),
            send_sem=R.ring_sent.at[i],
            recv_sem=R.ring_came.at[i],
            device_id=way[side],
            device_id_type=MESH,
        )

    def pass_sum(part, s):
        for side in range(2):
            reach = hops(part, side)
            if s >= reach:
                continue
            pos = r + (reach - s) if side == 0 else r - (reach - s)
            term = view(PART, part, rows_at(pos))
            if s == 0:
                source = term
            else:
                source = landed(part, side, s - 1)
                sum_copy(part, side, s - 1, source).wait_recv()
                source[...] = (source[...].astype(F32) + term[...].astype(F32)).astype(BF)
            sum_copy(part, side, s, source).start()

    finals = []

    def end_sum(*group):
        for part in group:
            k, first, count = part
            ends = []
            for side in range(2):
                end = landed(part, side, hops(part, side) - 1)
                sum_copy(part, side, hops(part, side) - 1, end).wait_recv()
                ends.append(end)

            def total(core):
                rows = pl.ds(pl.multiple_of(own * core, 16), own)
                mine_rows = pl.ds(pl.multiple_of(2 * own * chip + own * core, 16), own)
                return (
                    ends[0][rows, :].astype(F32)
                    + ends[1][rows, :].astype(F32)
                    + PART[k, mine_rows, first : first + count].astype(F32)
                )

            cols = slice(first, first + count)
            away, home = total(other), total(c)
            R.give[k, :, cols] = away
            finals.append(
                start(R.give.at[k, :, pl.ds(first, count)], GW.at[k, c, :, pl.ds(first, count)], mate)
            )
            GW[k, c, :, cols] = home

    def shard_part(k, value):
        for core in range(2):
            S[k, core] = value(core).astype(BF)

    gain_one, gain_two = column(R.gain_attn), column(R.gain_ffn)

    def attention_part(core):
        cols = slice(core * span, (core + 1) * span)
        return jnp.concatenate(
            [
                R.w_query[:, cols].astype(F32) * (gain_one * HEAD_DIM**-0.5),
                R.w_key[:, cols].astype(F32) * gain_one,
                R.w_value[:, cols].astype(F32) * gain_one,
                R.w_out[:, cols].astype(F32),
            ],
            axis=1,
        )

    def half_of(ref, core):
        return ref[:, core * width : (core + 1) * width].astype(F32) * gain_two

    def turned_half(ref, core):
        return ref[:, core * width : (core + 1) * width]

    lengths = R.lengths

    def live(t, slots):
        return (slots < PATCHES) | ((slots >= VIS) & (slots < VIS + lengths[t]))

    def live_rows(t, j, count=64):
        slots = lax.broadcasted_iota(jnp.int32, (count, 1), 0) + j * count
        return live(t, slots).astype(F32)

    row_count = R.tokens.shape[0]

    def placed(t, slots, rows, kept):
        source = t * (PATCHES + CAPTION) + slots - (slots >= VIS).astype(jnp.int32) * (VIS - PATCHES)
        return ((rows == source) & kept).astype(F32).astype(BF)

    def chooser(t, only_live):
        slots = lax.broadcasted_iota(jnp.int32, (SEQ, row_count), 0)
        rows = lax.broadcasted_iota(jnp.int32, (SEQ, row_count), 1)
        filled = (slots < PATCHES) | ((slots >= VIS) & (slots < VIS + CAPTION))
        return placed(t, slots, rows, live(t, slots) if only_live else filled)

    shard_part(ATT, attention_part)
    G[ATT, my_rows, :] = S[ATT, c]
    for t in range(2):
        R.lens[t] = jnp.full((8, 128), lengths[t], jnp.int32).astype(F32)
    pl.semaphore_wait(barrier, 4)
    shard_a = start(S.at[pl.ds(0, 1), other], G.at[pl.ds(0, 1), my_rows, :], mate)
    send_lens = start(R.lens, R.lens4.at[pl.ds(mine, 2)], mate)
    for t in range(2):
        R.x4[2 * c + t] = mm(chooser(t, False), R.tokens[...]).astype(BF)
        R.lens4[2 * c + t] = R.lens[t]
    send_x = start(R.x4.at[pl.ds(mine, 2)], R.x4.at[pl.ds(mine, 2)], mate)
    shard_a.wait_recv()
    gather(near, 0)
    gather(far, 0)

    shard_part(TIN, functools.partial(half_of, R.txt_in))
    shard_part(TOUT, functools.partial(turned_half, R.txt_out))
    shard_part(VIN, functools.partial(half_of, R.vis_in))
    shard_part(VOUT, functools.partial(turned_half, R.vis_out))
    shard_b = start(S.at[pl.ds(1, 4), other], G.at[pl.ds(1, 4), my_rows, :], mate)
    for k in (TIN, TOUT, VIN, VOUT):
        G[k, my_rows, :] = S[k, c]
    gather(near, 1)
    for t in range(2):
        R.gz[2 * c + t] = mm(chooser(t, True), R.cotangent[...]).astype(BF)
        if t == 0:
            gather(far, 1)
    send_gz = start(R.gz.at[pl.ds(mine, 2)], R.gz.at[pl.ds(mine, 2)], mate)
    R.dy[...] = mm(chooser(x, False), R.cotangent[...]).astype(BF)
    for t in range(2):
        R.x[t] = R.x4[2 * c + t]
    gather(near, 2)
    send_x.wait_recv()

    for i in range(4):

        @pl.loop(0, SEQ // 64)
        def _(j, i=i):
            rows = pl.ds(pl.multiple_of(j * 64, 64), 64)
            normed, _ = normalize(R.x4[i, rows, :].astype(F32))
            R.n1[i, rows, :] = normed.astype(BF)

        R.n1t[:, i * SEQ : (i + 1) * SEQ] = R.n1[i].T
        if i == 0:
            gather(far, 2)
        if i == 1:
            gather(near, 3)
        if i == 2:
            gather(far, 3)
            shard_b.wait_recv()
            gather(tin, 0)
            gather(tout, 0)
    send_gz.wait_recv()
    send_lens.wait_recv()
    gather(near, 4)
    gather(far, 4)

    R.wo[...] = G[ATT][:, 3 * span :]

    @pl.loop(0, 4)
    def _(i):
        projected = mm(R.n1[i], G[ATT][:, : 3 * span]).astype(BF)
        R.q[i] = projected[:, :span]
        R.k[i] = projected[:, span : 2 * span]
        R.v[i] = projected[:, 2 * span :]

    lane = lax.broadcasted_iota(jnp.int32, (1, span), 1) // HEAD_DIM

    def only(head, values):
        return values * (lane == head).astype(F32).astype(BF)

    def head_rows(values, head):
        return values[head * HEAD_DIM : (head + 1) * HEAD_DIM, :]

    order = []
    for j in range(4):
        core = other if j < 2 else c
        turn = 1 - x if j % 2 == 0 else x
        order.append((turn, 2 * core + turn))
    attn_mate = [remote(R.pa.at[i], R.ra.at[turn], mate) for turn, i in order[:2]]
    cross_a = remote(R.xs, R.xr, across)
    started.append(cross_a)

    for j, (turn, i) in enumerate(order):
        q, k, v = R.q[i], R.k[i], R.v[i]
        turned_v = v.T
        slots = lax.broadcasted_iota(jnp.int32, (SEQ, 1), 0)
        caption = (slots - VIS).astype(F32) < R.lens4[i][:1, :1]
        bias = jnp.where((slots < PATCHES) | ((slots >= VIS) & caption), 0.0, -1e30)
        contexts = []
        for h in range(heads):
            scores = mm_nt(only(h, k), q) + bias
            top = jnp.max(scores, axis=0, keepdims=True)
            weights = jnp.exp(scores - top)
            total = jnp.sum(weights, axis=0, keepdims=True)
            probs = (weights * (1.0 / total)).astype(BF)
            R.probs[i * heads + h] = probs
            contexts.append(mm(head_rows(turned_v, h), probs))
        context = jnp.concatenate(contexts, axis=0).T.astype(BF)
        R.c[i] = context
        R.pa[i] = mm_nt(context, R.wo[...]).astype(BF)
        if j < 2:
            attn_mate[j].start()
        if j == 2:
            attn_mate[0].wait_recv()
            R.xs[...] = (R.pa[pair_across].astype(F32) + R.ra[1 - x].astype(F32)).astype(BF)
            cross_a.start()
        if j == 0:
            gather(tin, 1)
        if j == 1:
            gather(tout, 1)
        if j == 3:
            gather(tin, 2)

    for copy in attn_mate:
        copy.wait_send()
    attn_mate[1].wait_recv()

    @pl.loop(0, width // 256)
    def _(j):
        cols = pl.ds(pl.multiple_of(j * 256, 256), 256)
        R.gzvt[cols, : 4 * VIS] = R.gz[:, :VIS, cols].reshape(4 * VIS, 256).T
        R.gztt[cols, :] = R.gz[:, VIS:, cols].reshape(4 * TXT, 256).T

    gather(tout, 2)
    cross_a.wait_recv()

    @pl.loop(0, SEQ // 64)
    def _(j):
        rows = pl.ds(pl.multiple_of(j * 64, 64), 64)
        attended = (
            R.pa[pair_own, rows, :].astype(F32)
            + R.ra[x, rows, :].astype(F32)
            + R.xr[rows, :].astype(F32)
        )
        middle = R.x[x, rows, :].astype(F32) + live_rows(x, j) * attended
        R.y1[rows, :] = middle
        normed, _ = normalize(middle)
        R.n2[pair_own, rows, :] = normed.astype(BF)

    block = R.n2.at[pair_own]
    to_across = start(block, block, across)
    to_mate = start(block, block, mate)
    gather(tin, 3)
    gather(tout, 3)
    gather(vin, 0)
    gather(vout, 0)
    to_across.wait_recv()
    block = R.n2.at[pair_across]
    passed = start(block, block, mate)
    gather(tin, 4)
    gather(tout, 4)
    gather(vin, 1)
    to_mate.wait_recv()
    passed.wait_recv()

    def expert(pairs, low, high, w_in, w_out, h_ref, gu_ref, j):
        first, count = pairs
        per = high - low
        total_rows = count * per
        cols = slice(j * 256, (j + 1) * 256)
        inside = slice(first, first + count)
        R.u[:total_rows, :] = mm(
            R.n2[inside, low:high, :].reshape(total_rows, width), G[w_in, :, cols]
        )
        R.gh[:total_rows, :] = mm(
            R.gz[inside, low:high, :].reshape(total_rows, width), G[w_out, :, cols]
        )
        step = min(total_rows, VIS)

        @pl.loop(0, 2 * (total_rows // step))
        def _(i):
            lanes = lax.rem(i, 2) * 128
            rows = pl.ds(pl.multiple_of(i // 2 * step, 16), step)
            into = pl.ds(pl.multiple_of(first * per + i // 2 * step, 16), step)
            side = pl.ds(pl.multiple_of(lanes, 128), 128)
            pre = R.u[rows, side]
            cumulative = 0.5 * (1.0 + lax.erf(pre * inv_root_two))
            density = jnp.exp(-0.5 * pre * pre) * inv_root_tau
            onto = pl.ds(pl.multiple_of(j * 256 + lanes, 128), 128)
            h_ref[into, onto] = (pre * cumulative).astype(BF)
            gu_ref[into, onto] = (R.gh[rows, side] * (cumulative + pre * density)).astype(BF)

    def weight_grad(k, turned, ref, j):
        cols = slice(j * 256, (j + 1) * 256)
        PART[k, :, cols] = mm(turned, ref[:, cols]).astype(BF)

    tiles = range(width // 256)
    for j in tiles:
        expert((0, 4), VIS, SEQ, TIN, TOUT, R.ht, R.gut, j)
    gather(vout, 1)
    for j in tiles:
        weight_grad(TOUT, R.gztt[...], R.ht, j)

    @pl.loop(0, width // 256)
    def _(j):
        cols = pl.ds(pl.multiple_of(j * 256, 256), 256)
        R.n2vt[cols, :] = R.n2[:, :VIS, cols].reshape(4 * VIS, 256).T
        R.n2tt[cols, :] = R.n2[:, VIS:, cols].reshape(4 * TXT, 256).T

    gather(vin, 2)
    for j in tiles:
        weight_grad(TIN, R.n2tt[...], R.gut, j)
    gather(vout, 2)
    gather(vin, 3)
    gather(vout, 3)
    pass_sum(tout, 0)
    pass_sum(tin, 0)
    gather(vin, 4)
    gather(vout, 4)

    def terms(target, hv, ht, w_vis, w_txt, m):
        vis_rows = slice(2 * m * VIS, 2 * (m + 1) * VIS)
        txt_rows = slice(2 * m * TXT, 2 * (m + 1) * TXT)
        vis_part = mm_nt(hv[vis_rows, :], G[w_vis]).astype(BF)
        target[2 * m : 2 * m + 2, :VIS, :] = vis_part.reshape(2, VIS, width)
        txt_part = mm_nt(ht[txt_rows, :], G[w_txt]).astype(BF)
        target[2 * m : 2 * m + 2, VIS:, :] = txt_part.reshape(2, TXT, width)

    mate_g = remote(R.pg.at[pl.ds(theirs, 2)], R.rg, mate)
    cross_g = remote(R.xsg, R.xrg, across)
    gy_across = remote(R.gy.at[x], R.gy.at[x], across)
    gy_mate = remote(R.ga.at[pair_own], R.ga.at[pair_own], mate)
    gy_passed = remote(R.ga.at[pair_across], R.ga.at[pair_across], mate)
    started.extend([cross_g, gy_across, gy_mate, gy_passed])

    def image_terms(m):
        terms(R.pg, R.guv, R.gut, VIN, TIN, m)
        pl.when(c != m)(mate_g.start)

    def sum_cores(m):
        @pl.when(c == m)
        def _():
            mate_g.wait_recv()
            R.xsg[...] = (R.pg[pair_across].astype(F32) + R.rg[1 - x].astype(F32)).astype(BF)
            cross_g.start()

    def middle_back(m):
        @pl.when(c == m)
        def _():
            cross_g.wait_recv()

            @pl.loop(0, SEQ // 64)
            def _(j):
                rows = pl.ds(pl.multiple_of(j * 64, 64), 64)
                grad_normed = (
                    R.pg[pair_own, rows, :].astype(F32)
                    + R.rg[x, rows, :].astype(F32)
                    + R.xrg[rows, :].astype(F32)
                )
                normed, inverse = normalize(R.y1[rows, :])
                grad = R.dy[rows, :].astype(F32) + normalize_back(grad_normed, normed, inverse)
                R.gy[x, rows, :] = grad.astype(BF)
                R.ga[pair_own, rows, :] = (grad * live_rows(x, j)).astype(BF)

            gy_across.start()
            gy_mate.start()

    def middle_pass(m):
        @pl.when(c == m)
        def _():
            gy_across.wait_recv()

            @pl.loop(0, SEQ // 64)
            def _(j):
                rows = pl.ds(pl.multiple_of(j * 64, 64), 64)
                R.ga[pair_across, rows, :] = (
                    R.gy[1 - x, rows, :].astype(F32) * live_rows(1 - x, j)
                ).astype(BF)

            gy_passed.start()

    def middle_came(m):
        @pl.when(c != m)
        def _():
            gy_mate.wait_recv()
            gy_passed.wait_recv()

    sent(send_x)
    for j in tiles:
        expert((0, 2), 0, VIS, VIN, VOUT, R.hv, R.guv, j)
        if j == 1:
            pass_sum(tout, 1)
    image_terms(0)
    pass_sum(tin, 1)
    expert((2, 2), 0, VIS, VIN, VOUT, R.hv, R.guv, 0)
    sum_cores(0)
    expert((2, 2), 0, VIS, VIN, VOUT, R.hv, R.guv, 1)
    pass_sum(tout, 2)
    for j in tiles[2:]:
        expert((2, 2), 0, VIS, VIN, VOUT, R.hv, R.guv, j)
    image_terms(1)
    pass_sum(tin, 2)
    for copy in (to_across, to_mate, passed):
        sent(copy)
    weight_grad(VOUT, R.gzvt[:, : 4 * VIS], R.hv, 0)
    sum_cores(1)
    middle_back(0)
    for j in tiles[1:]:
        weight_grad(VOUT, R.gzvt[:, : 4 * VIS], R.hv, j)
    pass_sum(tout, 3)
    pass_sum(vout, 0)
    for j in tiles:
        weight_grad(VIN, R.n2vt[...], R.guv, j)
    pass_sum(tin, 3)
    pass_sum(vin, 0)

    mate_g.wait_send()
    terms(R.pf, R.hv, R.ht, VOUT, TOUT, 0)
    middle_pass(0)
    middle_back(1)
    end_sum(tout, tin)
    terms(R.pf, R.hv, R.ht, VOUT, TOUT, 1)
    mate_f = start(R.pf.at[pl.ds(theirs, 2)], R.rf, mate)
    cross_f = remote(R.xsf, R.xrf, across)
    started.append(cross_f)
    pass_sum(vout, 1)
    middle_came(0)

    back_mate = [remote(R.pb.at[theirs + t], R.rb.at[t], mate) for t in range(2)]
    back_cross = [remote(R.xsb.at[t], R.xrb.at[t], across) for t in range(2)]
    started.extend(back_mate + back_cross)

    def attention_back(m, t):
        i = 2 * m + t
        grad_context = mm(R.ga[i], R.wo[...]).astype(BF)
        R.gat[:, i * SEQ : (i + 1) * SEQ] = R.ga[i].T
        q, k, v = R.q[i], R.k[i], R.v[i]
        turned_k = k.T
        grad_q = []
        grad_k = jnp.zeros((SEQ, span), F32)
        grad_v = jnp.zeros((SEQ, span), F32)
        for h in range(heads):
            probs = R.probs[i * heads + h]
            grad_probs = mm_nt(only(h, v), grad_context)
            exact = probs.astype(F32)
            inner = jnp.sum(grad_probs * exact, axis=0, keepdims=True)
            grad_scores = (exact * (grad_probs - inner)).astype(BF)
            grad_q.append(mm(head_rows(turned_k, h), grad_scores))
            grad_k += mm(grad_scores, only(h, q))
            grad_v += mm(probs, only(h, grad_context))
        grad_q = jnp.concatenate(grad_q, axis=0).T
        joined = jnp.concatenate([grad_q, grad_k, grad_v], axis=1).astype(BF)
        R.gqkv[i, :, : 3 * span] = joined
        R.pb[i] = mm_nt(joined, G[ATT][:, : 3 * span]).astype(BF)
        pl.when(c != m)(back_mate[t].start)

    def back_sum(m):
        @pl.when(c == m)
        def _():
            for t in range(2):
                back_mate[t].wait_recv()
                R.xsb[t] = (R.pb[2 * m + t].astype(F32) + R.rb[t].astype(F32)).astype(BF)
                back_cross[t].start()

    attention_back(0, 0)
    pass_sum(vin, 1)
    mate_f.wait_recv()
    R.xsf[...] = (R.pf[pair_across].astype(F32) + R.rf[1 - x].astype(F32)).astype(BF)
    middle_pass(1)
    cross_f.start()
    attention_back(0, 1)
    pass_sum(vout, 2)
    middle_came(1)
    attention_back(1, 0)
    pass_sum(vin, 2)
    back_sum(0)
    attention_back(1, 1)
    pass_sum(vout, 3)
    pass_sum(vin, 3)

    @pl.loop(0, 3)
    def _(j):
        rows = pl.ds(pl.multiple_of(j * 256, 256), 256)
        grads = mm(R.n1t[rows, :], R.gqkv[:, :, : 3 * span].reshape(4 * SEQ, 3 * span))
        grad_o = mm(R.gat[rows, :], R.c[...].reshape(4 * SEQ, span))
        PART[ATT, rows, :] = jnp.concatenate([grads, grad_o], axis=1).astype(BF)

    pass_sum(near, 0)
    pass_sum(far, 0)
    back_sum(1)
    end_sum(vout, vin)

    cross_f.wait_recv()

    @pl.loop(0, SEQ // 64)
    def _(j):
        rows = pl.ds(pl.multiple_of(j * 64, 64), 64)
        branch = (
            R.pf[pair_own, rows, :].astype(F32)
            + R.rf[x, rows, :].astype(F32)
            + R.xrf[rows, :].astype(F32)
        )
        OUT[x, rows, :] = (R.y1[rows, :] + live_rows(x, j) * branch).astype(BF)

    out_across = start(OUT.at[x], OUT.at[x], across)
    pass_sum(near, 1)
    pass_sum(far, 1)

    for t in range(2):
        back_cross[t].wait_recv()

        @pl.loop(0, SEQ // 64)
        def _(j, t=t):
            rows = pl.ds(pl.multiple_of(j * 64, 64), 64)
            grad_normed = R.xsb[t, rows, :].astype(F32) + R.xrb[t, rows, :].astype(F32)
            normed, inverse = normalize(R.x[t, rows, :].astype(F32))
            grad = R.gy[t, rows, :].astype(F32) + normalize_back(grad_normed, normed, inverse)
            high = grad.astype(BF)
            rows = pl.ds(pl.multiple_of(t * SEQ + j * 64, 64), 64)
            R.hv[rows, :] = high
            R.guv[rows, :] = (grad - high.astype(F32)).astype(BF)

        pass_sum(near, 2 + t)
        pass_sum(far, 2 + t)

    slots = lax.broadcasted_iota(jnp.int32, (row_count, 2 * SEQ), 1)
    rows = lax.broadcasted_iota(jnp.int32, (row_count, 2 * SEQ), 0)
    turn = slots // SEQ
    back = placed(turn, slots - turn * SEQ, rows, slots >= 0)
    out_across.wait_recv()
    R.out_tokens[...] = mm(back, OUT[...].reshape(2 * SEQ, width)).astype(BF)
    R.grad_tokens[...] = mm(back, R.hv[: 2 * SEQ, :]) + mm(back, R.guv[: 2 * SEQ, :])
    end_sum(near, far)
    for copy in finals:
        copy.wait_recv()

    def row_sums(k, last):
        return sum(
            jnp.sum(S[k, core][:, :last].astype(F32) * GW[k, core][:, :last], axis=-1, keepdims=True)
            for core in range(2)
        )

    R.gs[0] = jnp.broadcast_to(row_sums(ATT, 3 * span), (own, 128))
    R.gs[1] = jnp.broadcast_to(row_sums(TIN, width) + row_sums(VIN, width), (own, 128))
    cross_gain = start(R.gs, R.gr, across)
    cross_gain.wait_recv()
    GG[...] = R.gs[...] + R.gr[...]

    for copy in started:
        copy.wait_send()
    for part in parts:
        for side in range(2):
            for s in range(hops(part, side)):
                gather_copy(part, side, s, r).wait_send()
                sum_copy(part, side, s, landed(part, side, s)).wait_send()


def finish_kernel(out, gtok, gw, gg, gain_attn, gain_ffn, *rest):
    (
        out_tokens,
        grad_tokens,
        grad_gain_attn,
        grad_query,
        grad_key,
        grad_value,
        grad_out,
        grad_gain_ffn,
        grad_vis_in,
        grad_vis_out,
        grad_txt_in,
        grad_txt_out,
    ) = rest
    out_tokens[...] = out[...]
    grad_tokens[...] = gtok[...]
    width = gw.shape[3]
    own = gw.shape[2]
    span = width // 4
    gain_one, gain_two = column(gain_attn), column(gain_ffn)
    square = unit(own).astype(F32)
    grad_gain_attn[...] = jnp.sum(square * (gg[0][:, :1] / gain_one), axis=0, keepdims=True)
    grad_gain_ffn[...] = jnp.sum(square * (gg[1][:, :1] / gain_two), axis=0, keepdims=True)

    def both(part):
        return jnp.concatenate([gw[ATT, core][:, part * span : (part + 1) * span] for core in range(2)], axis=1)

    grad_query[...] = both(0) * (gain_one * HEAD_DIM**-0.5)
    grad_key[...] = both(1) * gain_one
    grad_value[...] = both(2) * gain_one
    grad_out[...] = both(3)
    for core in range(2):
        part = slice(core * width, (core + 1) * width)
        grad_vis_in[:, part] = gw[VIN, core] * gain_two
        grad_txt_in[:, part] = gw[TIN, core] * gain_two
        grad_vis_out[:, part] = gw[VOUT, core]
        grad_txt_out[:, part] = gw[TOUT, core]


def fused_layer(
    tokens,
    caption_lengths,
    gain_attn,
    w_query,
    w_key,
    w_value,
    w_out,
    gain_ffn,
    vis_in,
    vis_out,
    txt_in,
    txt_out,
    cotangent,
):
    n = lax.axis_size("dp") // 2
    own = w_query.shape[0]
    row_count, width = tokens.shape
    span = width // 4
    heads = span // HEAD_DIM
    gain_one, gain_two = gain_attn.reshape(1, own), gain_ffn.reshape(1, own)

    rows = 4 * SEQ
    scratch = dict(
        shard=pltpu.VMEM((5, 2, own, width), BF),
        lens=pltpu.VMEM((2, 8, 128), F32),
        x=pltpu.VMEM((2, SEQ, width), BF),
        dy=pltpu.VMEM((SEQ, width), BF),
        padded_out=pltpu.VMEM((2, SEQ, width), BF),
        gathered=pltpu.VMEM((5, width, width), BF),
        part=pltpu.VMEM((5, width, width), BF),
        land=pltpu.VMEM((5, n - 1, 2 * own, width), BF),
        give=pltpu.VMEM((5, own, width), F32),
        x4=pltpu.VMEM((4, SEQ, width), BF),
        lens4=pltpu.VMEM((4, 8, 128), F32),
        n1=pltpu.VMEM((4, SEQ, width), BF),
        n1t=pltpu.VMEM((width, rows), BF),
        gz=pltpu.VMEM((4, SEQ, width), BF),
        turned=pltpu.VMEM((width, rows), BF),
        gztt=pltpu.VMEM((width, 4 * TXT), BF),
        wo=pltpu.VMEM((width, span), BF),
        q=pltpu.VMEM((4, SEQ, span), BF),
        k=pltpu.VMEM((4, SEQ, span), BF),
        v=pltpu.VMEM((4, SEQ, span), BF),
        c=pltpu.VMEM((4, SEQ, span), BF),
        probs=pltpu.VMEM((4 * heads, SEQ, SEQ), BF),
        pa=pltpu.VMEM((4, SEQ, width), BF),
        ra=pltpu.VMEM((2, SEQ, width), BF),
        xs=pltpu.VMEM((SEQ, width), BF),
        xr=pltpu.VMEM((SEQ, width), BF),
        y1=pltpu.VMEM((SEQ, width), F32),
        n2vt=pltpu.VMEM((width, 4 * VIS), BF),
        n2tt=pltpu.VMEM((width, 4 * TXT), BF),
        u=pltpu.VMEM((4 * VIS, 256), F32),
        gh=pltpu.VMEM((4 * VIS, 256), F32),
        hv=pltpu.VMEM((4 * VIS, width), BF),
        guv=pltpu.VMEM((4 * VIS, width), BF),
        ht=pltpu.VMEM((4 * TXT, width), BF),
        gut=pltpu.VMEM((4 * TXT, width), BF),
        pg=pltpu.VMEM((4, SEQ, width), BF),
        rg=pltpu.VMEM((2, SEQ, width), BF),
        xsg=pltpu.VMEM((SEQ, width), BF),
        xrg=pltpu.VMEM((SEQ, width), BF),
        gy=pltpu.VMEM((2, SEQ, width), BF),
        xsf=pltpu.VMEM((SEQ, width), BF),
        xrf=pltpu.VMEM((SEQ, width), BF),
        xsb=pltpu.VMEM((2, SEQ, width), BF),
        xrb=pltpu.VMEM((2, SEQ, width), BF),
        gs=pltpu.VMEM((2, own, 128), F32),
        gr=pltpu.VMEM((2, own, 128), F32),
        sent=pltpu.SemaphoreType.DMA((40,)),
        came=pltpu.SemaphoreType.DMA((40,)),
        ring_sent=pltpu.SemaphoreType.DMA((6 * 2 * (n // 2) * 2,)),
        ring_came=pltpu.SemaphoreType.DMA((6 * 2 * (n // 2) * 2,)),
    )
    inputs = dict(
        lengths=caption_lengths,
        tokens=tokens,
        cotangent=cotangent,
        gain_attn=gain_one,
        gain_ffn=gain_two,
        w_query=w_query,
        w_key=w_key,
        w_value=w_value,
        w_out=w_out.T,
        vis_in=vis_in,
        vis_out=vis_out.T,
        txt_in=txt_in,
        txt_out=txt_out.T,
    )
    results = dict(
        out_tokens=jax.ShapeDtypeStruct((row_count, width), BF),
        grad_tokens=jax.ShapeDtypeStruct((row_count, width), F32),
        gw=jax.ShapeDtypeStruct((5, 2, own, width), F32),
        gg=jax.ShapeDtypeStruct((2, own, 128), F32),
    )
    vmem = pl.BlockSpec(memory_space=pltpu.VMEM)
    names = tuple(inputs) + tuple(results) + tuple(scratch)
    out, gtok, gw, gg = pl.pallas_call(
        functools.partial(layer_kernel, n, names),
        out_shape=tuple(results.values()),
        in_specs=[pl.BlockSpec(memory_space=pltpu.SMEM)] + [vmem] * (len(inputs) - 1),
        out_specs=[vmem] * len(results),
        scratch_shapes=list(scratch.values()),
        compiler_params=pltpu.CompilerParams(
            collective_id=0, has_side_effects=True, vmem_limit_bytes=60 * 2**20
        ),
    )(*inputs.values())

    final = pl.pallas_call(
        finish_kernel,
        out_shape=(
            jax.ShapeDtypeStruct((row_count, width), BF),
            jax.ShapeDtypeStruct((row_count, width), F32),
            jax.ShapeDtypeStruct((1, own), F32),
            jax.ShapeDtypeStruct((own, 2 * span), F32),
            jax.ShapeDtypeStruct((own, 2 * span), F32),
            jax.ShapeDtypeStruct((own, 2 * span), F32),
            jax.ShapeDtypeStruct((own, 2 * span), F32),
            jax.ShapeDtypeStruct((1, own), F32),
            jax.ShapeDtypeStruct((own, 2 * width), F32),
            jax.ShapeDtypeStruct((own, 2 * width), F32),
            jax.ShapeDtypeStruct((own, 2 * width), F32),
            jax.ShapeDtypeStruct((own, 2 * width), F32),
        ),
        in_specs=[vmem] * 6,
        out_specs=[vmem] * 12,
        compiler_params=pltpu.CompilerParams(vmem_limit_bytes=60 * 2**20),
    )(out, gtok, gw, gg, gain_one, gain_two)
    final = list(final)
    final[2] = final[2].reshape(own)
    final[7] = final[7].reshape(own)
    for turned in (6, 9, 11):
        final[turned] = final[turned].T
    return tuple(final)


def norm_parts(values):
    center = values - jnp.mean(values, axis=-1, keepdims=True)
    spread = jnp.mean(center * center, axis=-1, keepdims=True)
    inverse = lax.rsqrt(spread + epsilon)
    return (center * inverse, inverse)


def norm_back(grad_out, normed, inverse, gain):
    grad_normed = grad_out * gain
    grad_gain = jnp.sum(grad_out * normed, axis=0)
    inner = (
        grad_normed
        - jnp.mean(grad_normed, axis=-1, keepdims=True)
        - normed * jnp.mean(grad_normed * normed, axis=-1, keepdims=True)
    )
    return (inverse * inner, grad_gain)


def matmul(left, right):
    return jnp.dot(left, right, preferred_element_type=jnp.float32)


def matmul_tn(left, right):
    return lax.dot_general(
        left, right, (((0,), (0,)), ((), ())), preferred_element_type=jnp.float32
    )


def matmul_nt(left, right):
    return lax.dot_general(
        left, right, (((1,), (1,)), ((), ())), preferred_element_type=jnp.float32
    )


def gelu_slope(pre):
    cumulative = 0.5 * (1.0 + lax.erf(pre * inv_root_two))
    density = jnp.exp(-0.5 * pre * pre) * inv_root_tau
    return cumulative + pre * density


def expert_forward(rows, weight_in, weight_out):
    pre = matmul(rows, weight_in)
    hidden = jax.nn.gelu(pre, approximate=False).astype(jnp.bfloat16)
    return (pre, hidden, matmul(hidden, weight_out))


def expert_backward(rows, pre, hidden, grad_out, weight_in, weight_out):
    grad_weight_out = matmul_tn(hidden, grad_out)
    grad_hidden = matmul_nt(grad_out, weight_out)
    grad_pre = (grad_hidden * gelu_slope(pre)).astype(jnp.bfloat16)
    return (matmul_tn(rows, grad_pre), grad_weight_out, matmul_nt(grad_pre, weight_in))


def join_experts(image_rows, text_rows, pair_count, width):
    joined = jnp.concatenate(
        [
            image_rows.reshape(pair_count, PATCHES, width),
            text_rows.reshape(pair_count, CAPTION, width),
        ],
        axis=1,
    )
    return joined.reshape(-1, width)


def plain_layer(
    tokens,
    caption_lengths,
    gain_attn,
    w_query,
    w_key,
    w_value,
    w_out,
    gain_ffn,
    vis_in,
    vis_out,
    txt_in,
    txt_out,
    cotangent,
):
    seq_len = PATCHES + CAPTION
    width = tokens.shape[1]
    pair_count = tokens.shape[0] // seq_len
    half_pairs = pair_count // lax.axis_size("tensor")
    half_rows = half_pairs * seq_len
    row_start = lax.axis_index("tensor") * half_rows
    gain_one, query_w, key_w, value_w, out_w = (
        lax.all_gather(gain_attn, "dp", axis=0, tiled=True),
        lax.all_gather(w_query, "dp", axis=0, tiled=True),
        lax.all_gather(w_key, "dp", axis=0, tiled=True),
        lax.all_gather(w_value, "dp", axis=0, tiled=True),
        lax.all_gather(w_out, "dp", axis=1, tiled=True),
    )
    gain_two, vis_in_w, vis_out_w, txt_in_w, txt_out_w = (
        lax.all_gather(gain_ffn, "dp", axis=0, tiled=True),
        lax.all_gather(vis_in, "dp", axis=0, tiled=True),
        lax.all_gather(vis_out, "dp", axis=1, tiled=True),
        lax.all_gather(txt_in, "dp", axis=0, tiled=True),
        lax.all_gather(txt_out, "dp", axis=1, tiled=True),
    )
    gain_one = gain_one.astype(jnp.float32)
    gain_two = gain_two.astype(jnp.float32)
    head_local = query_w.shape[1] // HEAD_DIM
    score_scale = HEAD_DIM ** (-0.5)
    position = jnp.arange(seq_len, dtype=jnp.int32)
    live = (position[None, :] < PATCHES) | (position[None, :] - PATCHES < caption_lengths[:, None])
    valid_rows = live.astype(jnp.float32)
    mask_col = valid_rows.reshape(-1, 1)
    key_live = valid_rows[:, None, None, :] > 0.5

    def own_rows(values):
        return lax.dynamic_slice_in_dim(values, row_start, half_rows, 0)

    inputs = tokens.astype(jnp.float32)
    normed_one, inverse_one = norm_parts(inputs)
    first_in = (normed_one * gain_one).astype(jnp.bfloat16)

    def project(weight):
        return (
            matmul(first_in, weight)
            .astype(jnp.bfloat16)
            .reshape(pair_count, seq_len, head_local, HEAD_DIM)
        )

    queries = project(query_w)
    keys_all = project(key_w)
    values_all = project(value_w)

    def score_block():
        raw = (
            jnp.einsum("pqhe,pkhe->phqk", queries, keys_all, preferred_element_type=jnp.float32)
            * score_scale
        )
        return jnp.where(key_live, raw, -1e30)

    scores = score_block()
    top = jnp.max(scores, axis=-1, keepdims=True)
    weights = jnp.exp(scores - top)
    total = jnp.sum(weights, axis=-1, keepdims=True)
    probs = (weights / total).astype(jnp.bfloat16)
    log_total = top + jnp.log(total)
    context = jnp.einsum("phqk,pkhe->pqhe", probs, values_all, preferred_element_type=jnp.float32)
    context = context.astype(jnp.bfloat16).reshape(-1, head_local * HEAD_DIM)
    attn_terms = matmul(context, out_w)
    attended_own = lax.psum_scatter(
        attn_terms.astype(jnp.bfloat16), "tensor", scatter_dimension=0, tiled=True
    ).astype(jnp.float32)
    mask_own = own_rows(mask_col)
    middle_own = own_rows(inputs) + mask_own * attended_own
    normed_two, inverse_two = norm_parts(middle_own)
    second_own = (normed_two * gain_two).astype(jnp.bfloat16)
    grid = lax.all_gather(second_own, "tensor", axis=0, tiled=True).reshape(
        pair_count, seq_len, width
    )
    image_rows = grid[:, :PATCHES].reshape(-1, width)
    text_rows = grid[:, PATCHES:].reshape(-1, width)
    image_pre, image_hidden, image_part = expert_forward(image_rows, vis_in_w, vis_out_w)
    text_pre, text_hidden, text_part = expert_forward(text_rows, txt_in_w, txt_out_w)
    image_own, text_own = (
        lax.psum_scatter(
            image_part.astype(jnp.bfloat16), "tensor", scatter_dimension=0, tiled=True
        ).astype(jnp.float32),
        lax.psum_scatter(
            text_part.astype(jnp.bfloat16), "tensor", scatter_dimension=0, tiled=True
        ).astype(jnp.float32),
    )
    branch_own = join_experts(image_own, text_own, half_pairs, width)
    output_own = (middle_own + mask_own * branch_own).astype(jnp.bfloat16)
    upstream = cotangent.astype(jnp.float32)
    grad_branch = (upstream * mask_col).astype(jnp.bfloat16).reshape(pair_count, seq_len, width)
    image_grads = expert_backward(
        image_rows,
        image_pre,
        image_hidden,
        grad_branch[:, :PATCHES].reshape(-1, width),
        vis_in_w,
        vis_out_w,
    )
    text_grads = expert_backward(
        text_rows,
        text_pre,
        text_hidden,
        grad_branch[:, PATCHES:].reshape(-1, width),
        txt_in_w,
        txt_out_w,
    )
    back_image_own, back_text_own = (
        lax.psum_scatter(
            image_grads[2].astype(jnp.bfloat16), "tensor", scatter_dimension=0, tiled=True
        ).astype(jnp.float32),
        lax.psum_scatter(
            text_grads[2].astype(jnp.bfloat16), "tensor", scatter_dimension=0, tiled=True
        ).astype(jnp.float32),
    )
    grad_second_own = join_experts(back_image_own, back_text_own, half_pairs, width)
    grad_norm_own, gain_part = norm_back(grad_second_own, normed_two, inverse_two, gain_two)
    grad_middle_own = own_rows(upstream) + grad_norm_own
    output_wide, grad_middle, gain_parts = (
        lax.all_gather(
            output_own.astype(jnp.float32).astype(jnp.bfloat16), "tensor", axis=0, tiled=True
        ).astype(jnp.float32),
        lax.all_gather(grad_middle_own.astype(jnp.bfloat16), "tensor", axis=0, tiled=True).astype(
            grad_middle_own.dtype
        ),
        lax.all_gather(gain_part.astype(jnp.bfloat16), "tensor", axis=0, tiled=True).astype(
            gain_part.dtype
        ),
    )
    output = output_wide.astype(jnp.bfloat16)
    grad_gain_two = jnp.sum(gain_parts.reshape(-1, width), axis=0)
    grad_attended = (grad_middle * mask_col).astype(jnp.bfloat16)
    grad_out_w = matmul_tn(context, grad_attended)
    grad_context = (
        matmul_nt(grad_attended, out_w)
        .astype(jnp.bfloat16)
        .reshape(pair_count, seq_len, head_local, HEAD_DIM)
    )
    scores_again = score_block()
    probs_exact = jnp.exp(scores_again - log_total)
    grad_probs = jnp.einsum(
        "pqhe,pkhe->phqk", grad_context, values_all, preferred_element_type=jnp.float32
    )
    inner = jnp.sum(grad_probs * probs_exact, axis=-1, keepdims=True)
    grad_scores = (probs_exact * (grad_probs - inner)).astype(jnp.bfloat16)
    grad_values = jnp.einsum(
        "phqk,pqhe->pkhe", probs, grad_context, preferred_element_type=jnp.float32
    )
    grad_values = grad_values.astype(jnp.bfloat16).reshape(-1, head_local * HEAD_DIM)
    grad_queries = (
        jnp.einsum("phqk,pkhe->pqhe", grad_scores, keys_all, preferred_element_type=jnp.float32)
        * score_scale
    )
    grad_queries = grad_queries.astype(jnp.bfloat16).reshape(-1, head_local * HEAD_DIM)
    grad_keys = (
        jnp.einsum("phqk,pqhe->pkhe", grad_scores, queries, preferred_element_type=jnp.float32)
        * score_scale
    )
    grad_keys = grad_keys.astype(jnp.bfloat16).reshape(-1, head_local * HEAD_DIM)
    grad_query_w = matmul_tn(first_in, grad_queries)
    grad_key_w = matmul_tn(first_in, grad_keys)
    grad_value_w = matmul_tn(first_in, grad_values)
    first_part = (
        matmul_nt(grad_queries, query_w)
        + matmul_nt(grad_keys, key_w)
        + matmul_nt(grad_values, value_w)
    )
    grad_first = lax.psum(first_part.astype(jnp.bfloat16), "tensor").astype(jnp.float32)
    grad_norm_one, grad_gain_one = norm_back(grad_first, normed_one, inverse_one, gain_one)
    grad_inputs = grad_middle + grad_norm_one
    attn_sent = (
        lax.psum_scatter(grad_gain_one, "dp", scatter_dimension=0, tiled=True),
        lax.psum_scatter(grad_query_w, "dp", scatter_dimension=0, tiled=True),
        lax.psum_scatter(grad_key_w, "dp", scatter_dimension=0, tiled=True),
        lax.psum_scatter(grad_value_w, "dp", scatter_dimension=0, tiled=True),
        lax.psum_scatter(grad_out_w, "dp", scatter_dimension=1, tiled=True),
    )
    final_expert = (
        lax.psum_scatter(grad_gain_two, "dp", scatter_dimension=0, tiled=True),
        lax.psum_scatter(image_grads[0], "dp", scatter_dimension=0, tiled=True),
        lax.psum_scatter(image_grads[1], "dp", scatter_dimension=1, tiled=True),
        lax.psum_scatter(text_grads[0], "dp", scatter_dimension=0, tiled=True),
        lax.psum_scatter(text_grads[1], "dp", scatter_dimension=1, tiled=True),
    )
    return (
        output,
        grad_inputs,
        attn_sent[0],
        attn_sent[1],
        attn_sent[2],
        attn_sent[3],
        attn_sent[4],
        final_expert[0],
        final_expert[1],
        final_expert[2],
        final_expert[3],
        final_expert[4],
    )


def solution(mesh):
    def local(tokens, lengths, gain, w_query, *rest):
        ring = mesh.shape["dp"] // 2
        fits = (
            mesh.shape["tensor"] == 2
            and ring == 8
            and lengths.shape[0] == 2
            and w_query.shape[0] % 16 == 0
        )
        layer = fused_layer if fits else plain_layer
        return layer(tokens, lengths, gain, w_query, *rest)

    return jax.shard_map(
        local,
        mesh=mesh,
        in_specs=(
            P("dp", None),
            P("dp"),
            P("dp"),
            P("dp", "tensor"),
            P("dp", "tensor"),
            P("dp", "tensor"),
            P("tensor", "dp"),
            P("dp"),
            P("dp", "tensor"),
            P("tensor", "dp"),
            P("dp", "tensor"),
            P("tensor", "dp"),
            P("dp", None),
        ),
        out_specs=(
            P("dp", None),
            P("dp", None),
            P("dp"),
            P("dp", "tensor"),
            P("dp", "tensor"),
            P("dp", "tensor"),
            P("tensor", "dp"),
            P("dp"),
            P("dp", "tensor"),
            P("tensor", "dp"),
            P("dp", "tensor"),
            P("tensor", "dp"),
        ),
        check_vma=False,
    )
```

```python
import functools
import math
import types

import jax
import jax.numpy as jnp
from jax import lax
from jax.experimental import pallas as pl
from jax.experimental.pallas import tpu as pltpu
from jax.sharding import PartitionSpec as P

HEAD_DIM = 64
PATCHES = 197
CAPTION = 40
VIS = 208
TXT = 48
SEQ = VIS + TXT

MESH = pl.DeviceIdType.MESH
BF = jnp.bfloat16
F32 = jnp.float32

ATT, TIN, TOUT, VIN, VOUT = range(5)

epsilon = 1e-05
inv_root_two = 1.0 / math.sqrt(2.0)
inv_root_tau = 1.0 / math.sqrt(2.0 * math.pi)


def mm(left, right):
    return jnp.dot(left, right, preferred_element_type=F32)


def mm_nt(left, right):
    return lax.dot_general(left, right, (((1,), (1,)), ((), ())), preferred_element_type=F32)


def mm_tn(left, right):
    return lax.dot_general(left, right, (((0,), (0,)), ((), ())), preferred_element_type=F32)


def normalize(values):
    center = values - jnp.mean(values, axis=-1, keepdims=True)
    spread = jnp.mean(center * center, axis=-1, keepdims=True)
    inverse = lax.rsqrt(spread + epsilon)
    return center * inverse, inverse


def normalize_back(grad_normed, normed, inverse):
    return inverse * (
        grad_normed
        - jnp.mean(grad_normed, axis=-1, keepdims=True)
        - normed * jnp.mean(grad_normed * normed, axis=-1, keepdims=True)
    )


def unit(size):
    rows = lax.broadcasted_iota(jnp.int32, (size, size), 0)
    return (rows == lax.broadcasted_iota(jnp.int32, (size, size), 1)).astype(F32).astype(BF)


def column(ref):
    size = ref.shape[1]
    return jnp.sum(unit(size).astype(F32) * ref[...].astype(F32), axis=1, keepdims=True)


def layer_kernel(n, names, *refs):
    R = types.SimpleNamespace(**dict(zip(names, refs)))
    R.pb, R.pf, R.ga, R.rf, R.rb, R.n2 = R.pa, R.pg, R.x4, R.ra, R.rg, R.n1
    R.gat, R.gzvt, R.gqkv = R.turned, R.turned, R.n2
    S, G, PART, LAND = R.shard, R.gathered, R.part, R.land
    OUT, GW, GG = R.padded_out, R.gw, R.gg
    width = G.shape[2]
    own = width // (2 * n)
    span = width // 4
    heads = span // HEAD_DIM

    x = lax.axis_index("tensor")
    d = lax.axis_index("dp")
    c = lax.rem(d, 2)
    other = 1 - c
    chip = d // 2
    y, z = lax.rem(chip, 2), chip // 2
    r = z + y * (n - 1 - 2 * z)
    half = n // 2

    def chip_at(pos):
        pos = lax.rem(pos + 2 * n, n)
        upper = pos // half
        return 2 * (pos + upper * (n - 1 - 2 * pos)) + upper

    mate = {"dp": d + 1 - 2 * c}
    across = {"tensor": 1 - x}
    ahead = {"dp": 2 * chip_at(r + 1) + c}
    behind = {"dp": 2 * chip_at(r - 1) + c}
    way = (ahead, behind)

    def rows_at(pos):
        return pl.ds(pl.multiple_of(2 * own * chip_at(pos), 16), 2 * own)

    my_rows = pl.ds(pl.multiple_of(own * d, 16), own)

    barrier = pltpu.get_barrier_semaphore()
    for device in (mate, across, ahead, behind):
        pl.semaphore_signal(barrier, inc=1, device_id=device, device_id_type=MESH)

    mine, theirs = pl.multiple_of(2 * c, 2), pl.multiple_of(2 * other, 2)
    pair_own = 2 * c + x
    pair_across = 2 * c + 1 - x

    started = []
    counter = [0]

    def remote(source, target, device):
        index = counter[0]
        counter[0] += 1
        return pltpu.make_async_remote_copy(
            src_ref=source,
            dst_ref=target,
            send_sem=R.sent.at[index],
            recv_sem=R.came.at[index],
            device_id=device,
            device_id_type=MESH,
        )

    def start(source, target, device):
        copy = remote(source, target, device)
        copy.start()
        started.append(copy)
        return copy

    def sent(copy):
        copy.wait_send()
        started[:] = [one for one in started if one is not copy]

    near, far = (ATT, 0, width // 2), (ATT, width // 2, width // 2)
    parts = [near, far] + [(k, 0, width) for k in (TIN, TOUT, VIN, VOUT)]
    tin, tout, vin, vout = parts[2:]
    longest = half

    def hops(part, side):
        return half if (parts.index(part) + side) % 2 == 0 else n - 1 - half

    def ring_index(part, side, s):
        return (parts.index(part) * 2 + side) * longest + s

    def view(ref, part, rows):
        k, first, count = part
        return ref.at[k, rows, pl.ds(first, count)]

    def gather_copy(part, side, s, pos):
        block = view(G, part, rows_at(pos))
        i = ring_index(part, side, s)
        return pltpu.make_async_remote_copy(
            src_ref=block,
            dst_ref=block,
            send_sem=R.ring_sent.at[i],
            recv_sem=R.ring_came.at[i],
            device_id=way[side],
            device_id_type=MESH,
        )

    def gather(part, s):
        for side in range(2):
            pos = r - s if side == 0 else r + s
            if 0 < s <= hops(part, side):
                gather_copy(part, side, s - 1, pos).wait_recv()
            if s < hops(part, side):
                gather_copy(part, side, s, pos).start()

    sum_base = len(parts) * 2 * longest

    def landed(part, side, s):
        k, first, count = part
        return LAND.at[k, side * hops(part, 0) + s, :, pl.ds(first, count)]

    def sum_copy(part, side, s, source):
        i = sum_base + ring_index(part, side, s)
        return pltpu.make_async_remote_copy(
            src_ref=source,
            dst_ref=landed(part, side, s),
            send_sem=R.ring_sent.at[i],
            recv_sem=R.ring_came.at[i],
            device_id=way[side],
            device_id_type=MESH,
        )

    def pass_sum(part, s):
        for side in range(2):
            reach = hops(part, side)
            if s >= reach:
                continue
            pos = r + (reach - s) if side == 0 else r - (reach - s)
            term = view(PART, part, rows_at(pos))
            if s == 0:
                source = term
            else:
                source = landed(part, side, s - 1)
                sum_copy(part, side, s - 1, source).wait_recv()
                source[...] = (source[...].astype(F32) + term[...].astype(F32)).astype(BF)
            sum_copy(part, side, s, source).start()

    finals = []

    def end_sum(*group):
        for part in group:
            k, first, count = part
            ends = []
            for side in range(2):
                end = landed(part, side, hops(part, side) - 1)
                sum_copy(part, side, hops(part, side) - 1, end).wait_recv()
                ends.append(end)

            def total(core):
                rows = pl.ds(pl.multiple_of(own * core, 16), own)
                mine_rows = pl.ds(pl.multiple_of(2 * own * chip + own * core, 16), own)
                return (
                    ends[0][rows, :].astype(F32)
                    + ends[1][rows, :].astype(F32)
                    + PART[k, mine_rows, first : first + count].astype(F32)
                )

            cols = slice(first, first + count)
            away, home = total(other), total(c)
            R.give[k, :, cols] = away
            finals.append(
                start(R.give.at[k, :, pl.ds(first, count)], GW.at[k, c, :, pl.ds(first, count)], mate)
            )
            GW[k, c, :, cols] = home

    def shard_part(k, value):
        for core in range(2):
            S[k, core] = value(core).astype(BF)

    gain_one, gain_two = column(R.gain_attn), column(R.gain_ffn)

    def attention_part(core):
        cols = slice(core * span, (core + 1) * span)
        return jnp.concatenate(
            [
                R.w_query[:, cols].astype(F32) * (gain_one * HEAD_DIM**-0.5),
                R.w_key[:, cols].astype(F32) * gain_one,
                R.w_value[:, cols].astype(F32) * gain_one,
                R.w_out[:, cols].astype(F32),
            ],
            axis=1,
        )

    def half_of(ref, core):
        return ref[:, core * width : (core + 1) * width].astype(F32) * gain_two

    def turned_half(ref, core):
        return ref[:, core * width : (core + 1) * width]

    lengths = R.lengths

    def live(t, slots):
        return (slots < PATCHES) | ((slots >= VIS) & (slots < VIS + lengths[t]))

    def live_rows(t, j, count=64):
        slots = lax.broadcasted_iota(jnp.int32, (count, 1), 0) + j * count
        return live(t, slots).astype(F32)

    row_count = R.tokens.shape[0]

    def placed(t, slots, rows, kept):
        source = t * (PATCHES + CAPTION) + slots - (slots >= VIS).astype(jnp.int32) * (VIS - PATCHES)
        return ((rows == source) & kept).astype(F32).astype(BF)

    def chooser(t, only_live):
        slots = lax.broadcasted_iota(jnp.int32, (SEQ, row_count), 0)
        rows = lax.broadcasted_iota(jnp.int32, (SEQ, row_count), 1)
        filled = (slots < PATCHES) | ((slots >= VIS) & (slots < VIS + CAPTION))
        return placed(t, slots, rows, live(t, slots) if only_live else filled)

    shard_part(ATT, attention_part)
    G[ATT, my_rows, :] = S[ATT, c]
    for t in range(2):
        R.lens[t] = jnp.full((8, 128), lengths[t], jnp.int32).astype(F32)
    pl.semaphore_wait(barrier, 4)
    shard_a = start(S.at[pl.ds(0, 1), other], G.at[pl.ds(0, 1), my_rows, :], mate)
    send_lens = start(R.lens, R.lens4.at[pl.ds(mine, 2)], mate)
    for t in range(2):
        R.x4[2 * c + t] = mm(chooser(t, False), R.tokens[...]).astype(BF)
        R.lens4[2 * c + t] = R.lens[t]
    send_x = start(R.x4.at[pl.ds(mine, 2)], R.x4.at[pl.ds(mine, 2)], mate)
    shard_a.wait_recv()
    gather(near, 0)
    gather(far, 0)

    shard_part(TIN, functools.partial(half_of, R.txt_in))
    shard_part(TOUT, functools.partial(turned_half, R.txt_out))
    shard_part(VIN, functools.partial(half_of, R.vis_in))
    shard_part(VOUT, functools.partial(turned_half, R.vis_out))
    shard_b = start(S.at[pl.ds(1, 4), other], G.at[pl.ds(1, 4), my_rows, :], mate)
    for k in (TIN, TOUT, VIN, VOUT):
        G[k, my_rows, :] = S[k, c]
    gather(near, 1)
    for t in range(2):
        R.gz[2 * c + t] = mm(chooser(t, True), R.cotangent[...]).astype(BF)
        if t == 0:
            gather(far, 1)
    send_gz = start(R.gz.at[pl.ds(mine, 2)], R.gz.at[pl.ds(mine, 2)], mate)
    R.dy[...] = mm(chooser(x, False), R.cotangent[...]).astype(BF)
    for t in range(2):
        R.x[t] = R.x4[2 * c + t]
    shard_b.wait_recv()
    gather(tin, 0)
    gather(near, 2)
    send_x.wait_recv()

    for i in range(4):

        @pl.loop(0, SEQ // 64)
        def _(j, i=i):
            rows = pl.ds(pl.multiple_of(j * 64, 64), 64)
            normed, _ = normalize(R.x4[i, rows, :].astype(F32))
            R.n1[i, rows, :] = normed.astype(BF)

        R.n1t[:, i * SEQ : (i + 1) * SEQ] = R.n1[i].T
        if i == 0:
            gather(far, 2)
        if i == 1:
            gather(tout, 0)
            gather(near, 3)
        if i == 2:
            gather(far, 3)
            gather(vin, 0)
            gather(vout, 0)
    send_gz.wait_recv()
    send_lens.wait_recv()
    gather(near, 4)
    gather(far, 4)

    R.wo[...] = G[ATT][:, 3 * span :]

    @pl.loop(0, 4)
    def _(i):
        projected = mm(R.n1[i], G[ATT][:, : 3 * span]).astype(BF)
        R.q[i] = projected[:, :span]
        R.k[i] = projected[:, span : 2 * span]
        R.v[i] = projected[:, 2 * span :]

    lane = lax.broadcasted_iota(jnp.int32, (1, span), 1) // HEAD_DIM

    def only(head, values):
        return values * (lane == head).astype(F32).astype(BF)

    def head_rows(values, head):
        return values[head * HEAD_DIM : (head + 1) * HEAD_DIM, :]

    order = []
    for j in range(4):
        core = other if j < 2 else c
        turn = 1 - x if j % 2 == 0 else x
        order.append((turn, 2 * core + turn))
    attn_mate = [remote(R.pa.at[i], R.ra.at[turn], mate) for turn, i in order[:2]]
    cross_a = remote(R.xs, R.xr, across)
    started.append(cross_a)

    for j, (turn, i) in enumerate(order):
        q, k, v = R.q[i], R.k[i], R.v[i]
        turned_v = v.T
        slots = lax.broadcasted_iota(jnp.int32, (SEQ, 1), 0)
        caption = (slots - VIS).astype(F32) < R.lens4[i][:1, :1]
        bias = jnp.where((slots < PATCHES) | ((slots >= VIS) & caption), 0.0, -1e30)
        contexts = []
        for h in range(heads):
            scores = mm_nt(only(h, k), q) + bias
            top = jnp.max(scores, axis=0, keepdims=True)
            weights = jnp.exp(scores - top)
            total = jnp.sum(weights, axis=0, keepdims=True)
            probs = (weights * (1.0 / total)).astype(BF)
            R.probs[i * heads + h] = probs
            contexts.append(mm(head_rows(turned_v, h), probs))
        context = jnp.concatenate(contexts, axis=0).T.astype(BF)
        R.c[i] = context
        R.pa[i] = mm_nt(context, R.wo[...]).astype(BF)
        if j < 2:
            attn_mate[j].start()
        if j == 2:
            attn_mate[0].wait_recv()
            R.xs[...] = (R.pa[pair_across].astype(F32) + R.ra[1 - x].astype(F32)).astype(BF)
            cross_a.start()
        if j == 0:
            gather(tin, 1)
        if j == 1:
            gather(tout, 1)
        if j == 3:
            gather(tin, 2)
            gather(tout, 2)

    for copy in attn_mate:
        copy.wait_send()
    attn_mate[1].wait_recv()

    @pl.loop(0, width // 256)
    def _(j):
        cols = pl.ds(pl.multiple_of(j * 256, 256), 256)
        R.gzvt[cols, : 4 * VIS] = R.gz[:, :VIS, cols].reshape(4 * VIS, 256).T
        R.gztt[cols, :] = R.gz[:, VIS:, cols].reshape(4 * TXT, 256).T

    gather(vin, 1)
    cross_a.wait_recv()

    @pl.loop(0, SEQ // 64)
    def _(j):
        rows = pl.ds(pl.multiple_of(j * 64, 64), 64)
        attended = (
            R.pa[pair_own, rows, :].astype(F32)
            + R.ra[x, rows, :].astype(F32)
            + R.xr[rows, :].astype(F32)
        )
        middle = R.x[x, rows, :].astype(F32) + live_rows(x, j) * attended
        R.y1[rows, :] = middle
        normed, _ = normalize(middle)
        R.n2[pair_own, rows, :] = normed.astype(BF)

    block = R.n2.at[pair_own]
    to_across = start(block, block, across)
    to_mate = start(block, block, mate)
    gather(vout, 1)
    gather(tin, 3)
    gather(tout, 3)
    to_across.wait_recv()
    block = R.n2.at[pair_across]
    passed = start(block, block, mate)
    gather(vin, 2)
    gather(vout, 2)
    gather(tin, 4)
    gather(tout, 4)
    to_mate.wait_recv()
    passed.wait_recv()

    def expert(pairs, low, high, w_in, w_out, h_ref, gu_ref, j):
        first, count = pairs
        per = high - low
        total_rows = count * per
        cols = slice(j * 256, (j + 1) * 256)
        inside = slice(first, first + count)
        R.u[:total_rows, :] = mm(
            R.n2[inside, low:high, :].reshape(total_rows, width), G[w_in, :, cols]
        )
        R.gh[:total_rows, :] = mm(
            R.gz[inside, low:high, :].reshape(total_rows, width), G[w_out, :, cols]
        )
        step = min(total_rows, VIS)

        @pl.loop(0, 2 * (total_rows // step))
        def _(i):
            lanes = lax.rem(i, 2) * 128
            rows = pl.ds(pl.multiple_of(i // 2 * step, 16), step)
            into = pl.ds(pl.multiple_of(first * per + i // 2 * step, 16), step)
            side = pl.ds(pl.multiple_of(lanes, 128), 128)
            pre = R.u[rows, side]
            cumulative = 0.5 * (1.0 + lax.erf(pre * inv_root_two))
            density = jnp.exp(-0.5 * pre * pre) * inv_root_tau
            onto = pl.ds(pl.multiple_of(j * 256 + lanes, 128), 128)
            h_ref[into, onto] = (pre * cumulative).astype(BF)
            gu_ref[into, onto] = (R.gh[rows, side] * (cumulative + pre * density)).astype(BF)

    def weight_grad(k, turned, ref, j):
        cols = slice(j * 256, (j + 1) * 256)
        PART[k, :, cols] = mm(turned, ref[:, cols]).astype(BF)

    tiles = range(width // 256)
    for j in tiles:
        expert((0, 4), VIS, SEQ, TIN, TOUT, R.ht, R.gut, j)
    gather(vin, 3)
    for j in tiles:
        weight_grad(TOUT, R.gztt[...], R.ht, j)

    @pl.loop(0, width // 256)
    def _(j):
        cols = pl.ds(pl.multiple_of(j * 256, 256), 256)
        R.n2vt[cols, :] = R.n2[:, :VIS, cols].reshape(4 * VIS, 256).T
        R.n2tt[cols, :] = R.n2[:, VIS:, cols].reshape(4 * TXT, 256).T

    gather(vout, 3)
    for j in tiles:
        weight_grad(TIN, R.n2tt[...], R.gut, j)
    pass_sum(tout, 0)
    pass_sum(tin, 0)
    gather(vin, 4)
    gather(vout, 4)

    def terms(target, hv, ht, w_vis, w_txt, m):
        vis_rows = slice(2 * m * VIS, 2 * (m + 1) * VIS)
        txt_rows = slice(2 * m * TXT, 2 * (m + 1) * TXT)
        vis_part = mm_nt(hv[vis_rows, :], G[w_vis]).astype(BF)
        target[2 * m : 2 * m + 2, :VIS, :] = vis_part.reshape(2, VIS, width)
        txt_part = mm_nt(ht[txt_rows, :], G[w_txt]).astype(BF)
        target[2 * m : 2 * m + 2, VIS:, :] = txt_part.reshape(2, TXT, width)

    mate_g = remote(R.pg.at[pl.ds(theirs, 2)], R.rg, mate)
    cross_g = remote(R.xsg, R.xrg, across)
    gy_across = remote(R.gy.at[x], R.gy.at[x], across)
    gy_mate = remote(R.ga.at[pair_own], R.ga.at[pair_own], mate)
    gy_passed = remote(R.ga.at[pair_across], R.ga.at[pair_across], mate)
    started.extend([cross_g, gy_across, gy_mate, gy_passed])

    def image_terms(m):
        terms(R.pg, R.guv, R.gut, VIN, TIN, m)
        pl.when(c != m)(mate_g.start)

    def sum_cores(m):
        @pl.when(c == m)
        def _():
            mate_g.wait_recv()
            R.xsg[...] = (R.pg[pair_across].astype(F32) + R.rg[1 - x].astype(F32)).astype(BF)
            cross_g.start()

    def middle_back(m):
        @pl.when(c == m)
        def _():
            cross_g.wait_recv()

            @pl.loop(0, SEQ // 64)
            def _(j):
                rows = pl.ds(pl.multiple_of(j * 64, 64), 64)
                grad_normed = (
                    R.pg[pair_own, rows, :].astype(F32)
                    + R.rg[x, rows, :].astype(F32)
                    + R.xrg[rows, :].astype(F32)
                )
                normed, inverse = normalize(R.y1[rows, :])
                grad = R.dy[rows, :].astype(F32) + normalize_back(grad_normed, normed, inverse)
                R.gy[x, rows, :] = grad.astype(BF)
                R.ga[pair_own, rows, :] = (grad * live_rows(x, j)).astype(BF)

            gy_across.start()
            gy_mate.start()

    def middle_pass(m):
        @pl.when(c == m)
        def _():
            gy_across.wait_recv()

            @pl.loop(0, SEQ // 64)
            def _(j):
                rows = pl.ds(pl.multiple_of(j * 64, 64), 64)
                R.ga[pair_across, rows, :] = (
                    R.gy[1 - x, rows, :].astype(F32) * live_rows(1 - x, j)
                ).astype(BF)

            gy_passed.start()

    def middle_came(m):
        @pl.when(c != m)
        def _():
            gy_mate.wait_recv()
            gy_passed.wait_recv()

    sent(send_x)
    for j in tiles:
        expert((0, 2), 0, VIS, VIN, VOUT, R.hv, R.guv, j)
        if j == 1:
            pass_sum(tout, 1)
    image_terms(0)
    pass_sum(tin, 1)
    expert((2, 2), 0, VIS, VIN, VOUT, R.hv, R.guv, 0)
    sum_cores(0)
    expert((2, 2), 0, VIS, VIN, VOUT, R.hv, R.guv, 1)
    pass_sum(tout, 2)
    for j in tiles[2:]:
        expert((2, 2), 0, VIS, VIN, VOUT, R.hv, R.guv, j)
    image_terms(1)
    pass_sum(tin, 2)
    for copy in (to_across, to_mate, passed):
        sent(copy)
    weight_grad(VOUT, R.gzvt[:, : 4 * VIS], R.hv, 0)
    sum_cores(1)
    middle_back(0)
    for j in tiles[1:]:
        weight_grad(VOUT, R.gzvt[:, : 4 * VIS], R.hv, j)
    pass_sum(tout, 3)
    pass_sum(vout, 0)
    for j in tiles:
        weight_grad(VIN, R.n2vt[...], R.guv, j)
    pass_sum(tin, 3)
    pass_sum(vin, 0)

    mate_g.wait_send()
    terms(R.pf, R.hv, R.ht, VOUT, TOUT, 0)
    middle_pass(0)
    middle_back(1)
    end_sum(tout, tin)
    terms(R.pf, R.hv, R.ht, VOUT, TOUT, 1)
    mate_f = start(R.pf.at[pl.ds(theirs, 2)], R.rf, mate)
    cross_f = remote(R.xsf, R.xrf, across)
    started.append(cross_f)
    pass_sum(vout, 1)
    middle_came(0)

    back_mate = [remote(R.pb.at[theirs + t], R.rb.at[t], mate) for t in range(2)]
    back_cross = [remote(R.xsb.at[t], R.xrb.at[t], across) for t in range(2)]
    started.extend(back_mate + back_cross)

    def attention_back(m, t):
        i = 2 * m + t
        grad_context = mm(R.ga[i], R.wo[...]).astype(BF)
        R.gat[:, i * SEQ : (i + 1) * SEQ] = R.ga[i].T
        q, k, v = R.q[i], R.k[i], R.v[i]
        turned_k = k.T
        grad_q = []
        grad_k = jnp.zeros((SEQ, span), F32)
        grad_v = jnp.zeros((SEQ, span), F32)
        for h in range(heads):
            probs = R.probs[i * heads + h]
            grad_probs = mm_nt(only(h, v), grad_context)
            exact = probs.astype(F32)
            inner = jnp.sum(grad_probs * exact, axis=0, keepdims=True)
            grad_scores = (exact * (grad_probs - inner)).astype(BF)
            grad_q.append(mm(head_rows(turned_k, h), grad_scores))
            grad_k += mm(grad_scores, only(h, q))
            grad_v += mm(probs, only(h, grad_context))
        grad_q = jnp.concatenate(grad_q, axis=0).T
        joined = jnp.concatenate([grad_q, grad_k, grad_v], axis=1).astype(BF)
        R.gqkv[i, :, : 3 * span] = joined
        R.pb[i] = mm_nt(joined, G[ATT][:, : 3 * span]).astype(BF)
        pl.when(c != m)(back_mate[t].start)

    def back_sum(m):
        @pl.when(c == m)
        def _():
            for t in range(2):
                back_mate[t].wait_recv()
                R.xsb[t] = (R.pb[2 * m + t].astype(F32) + R.rb[t].astype(F32)).astype(BF)
                back_cross[t].start()

    attention_back(0, 0)
    pass_sum(vin, 1)
    mate_f.wait_recv()
    R.xsf[...] = (R.pf[pair_across].astype(F32) + R.rf[1 - x].astype(F32)).astype(BF)
    middle_pass(1)
    cross_f.start()
    attention_back(0, 1)
    pass_sum(vout, 2)
    middle_came(1)
    attention_back(1, 0)
    pass_sum(vin, 2)
    back_sum(0)
    attention_back(1, 1)
    pass_sum(vout, 3)
    pass_sum(vin, 3)

    @pl.loop(0, 3)
    def _(j):
        rows = pl.ds(pl.multiple_of(j * 256, 256), 256)
        grads = mm(R.n1t[rows, :], R.gqkv[:, :, : 3 * span].reshape(4 * SEQ, 3 * span))
        grad_o = mm(R.gat[rows, :], R.c[...].reshape(4 * SEQ, span))
        PART[ATT, rows, :] = jnp.concatenate([grads, grad_o], axis=1).astype(BF)

    pass_sum(near, 0)
    pass_sum(far, 0)
    back_sum(1)
    end_sum(vout, vin)

    cross_f.wait_recv()

    @pl.loop(0, SEQ // 64)
    def _(j):
        rows = pl.ds(pl.multiple_of(j * 64, 64), 64)
        branch = (
            R.pf[pair_own, rows, :].astype(F32)
            + R.rf[x, rows, :].astype(F32)
            + R.xrf[rows, :].astype(F32)
        )
        OUT[x, rows, :] = (R.y1[rows, :] + live_rows(x, j) * branch).astype(BF)

    out_across = start(OUT.at[x], OUT.at[x], across)
    pass_sum(near, 1)
    pass_sum(far, 1)

    for t in range(2):
        back_cross[t].wait_recv()

        @pl.loop(0, SEQ // 64)
        def _(j, t=t):
            rows = pl.ds(pl.multiple_of(j * 64, 64), 64)
            grad_normed = R.xsb[t, rows, :].astype(F32) + R.xrb[t, rows, :].astype(F32)
            normed, inverse = normalize(R.x[t, rows, :].astype(F32))
            grad = R.gy[t, rows, :].astype(F32) + normalize_back(grad_normed, normed, inverse)
            high = grad.astype(BF)
            rows = pl.ds(pl.multiple_of(t * SEQ + j * 64, 64), 64)
            R.hv[rows, :] = high
            R.guv[rows, :] = (grad - high.astype(F32)).astype(BF)

        pass_sum(near, 2 + t)
        pass_sum(far, 2 + t)

    slots = lax.broadcasted_iota(jnp.int32, (row_count, 2 * SEQ), 1)
    rows = lax.broadcasted_iota(jnp.int32, (row_count, 2 * SEQ), 0)
    turn = slots // SEQ
    back = placed(turn, slots - turn * SEQ, rows, slots >= 0)
    out_across.wait_recv()
    R.out_tokens[...] = mm(back, OUT[...].reshape(2 * SEQ, width)).astype(BF)
    R.grad_tokens[...] = mm(back, R.hv[: 2 * SEQ, :]) + mm(back, R.guv[: 2 * SEQ, :])
    end_sum(near, far)
    for copy in finals:
        copy.wait_recv()

    def row_sums(k, last):
        return sum(
            jnp.sum(S[k, core][:, :last].astype(F32) * GW[k, core][:, :last], axis=-1, keepdims=True)
            for core in range(2)
        )

    R.gs[0] = jnp.broadcast_to(row_sums(ATT, 3 * span), (own, 128))
    R.gs[1] = jnp.broadcast_to(row_sums(TIN, width) + row_sums(VIN, width), (own, 128))
    cross_gain = start(R.gs, R.gr, across)
    cross_gain.wait_recv()
    GG[...] = R.gs[...] + R.gr[...]

    for copy in started:
        copy.wait_send()
    for part in parts:
        for side in range(2):
            for s in range(hops(part, side)):
                gather_copy(part, side, s, r).wait_send()
                sum_copy(part, side, s, landed(part, side, s)).wait_send()


def finish_kernel(out, gtok, gw, gg, gain_attn, gain_ffn, *rest):
    (
        out_tokens,
        grad_tokens,
        grad_gain_attn,
        grad_query,
        grad_key,
        grad_value,
        grad_out,
        grad_gain_ffn,
        grad_vis_in,
        grad_vis_out,
        grad_txt_in,
        grad_txt_out,
    ) = rest
    out_tokens[...] = out[...]
    grad_tokens[...] = gtok[...]
    width = gw.shape[3]
    own = gw.shape[2]
    span = width // 4
    gain_one, gain_two = column(gain_attn), column(gain_ffn)
    square = unit(own).astype(F32)
    grad_gain_attn[...] = jnp.sum(square * (gg[0][:, :1] / gain_one), axis=0, keepdims=True)
    grad_gain_ffn[...] = jnp.sum(square * (gg[1][:, :1] / gain_two), axis=0, keepdims=True)

    def both(part):
        return jnp.concatenate([gw[ATT, core][:, part * span : (part + 1) * span] for core in range(2)], axis=1)

    grad_query[...] = both(0) * (gain_one * HEAD_DIM**-0.5)
    grad_key[...] = both(1) * gain_one
    grad_value[...] = both(2) * gain_one
    grad_out[...] = both(3)
    for core in range(2):
        part = slice(core * width, (core + 1) * width)
        grad_vis_in[:, part] = gw[VIN, core] * gain_two
        grad_txt_in[:, part] = gw[TIN, core] * gain_two
        grad_vis_out[:, part] = gw[VOUT, core]
        grad_txt_out[:, part] = gw[TOUT, core]


def fused_layer(
    tokens,
    caption_lengths,
    gain_attn,
    w_query,
    w_key,
    w_value,
    w_out,
    gain_ffn,
    vis_in,
    vis_out,
    txt_in,
    txt_out,
    cotangent,
):
    n = lax.axis_size("dp") // 2
    own = w_query.shape[0]
    row_count, width = tokens.shape
    span = width // 4
    heads = span // HEAD_DIM
    gain_one, gain_two = gain_attn.reshape(1, own), gain_ffn.reshape(1, own)

    rows = 4 * SEQ
    scratch = dict(
        shard=pltpu.VMEM((5, 2, own, width), BF),
        lens=pltpu.VMEM((2, 8, 128), F32),
        x=pltpu.VMEM((2, SEQ, width), BF),
        dy=pltpu.VMEM((SEQ, width), BF),
        padded_out=pltpu.VMEM((2, SEQ, width), BF),
        gathered=pltpu.VMEM((5, width, width), BF),
        part=pltpu.VMEM((5, width, width), BF),
        land=pltpu.VMEM((5, n - 1, 2 * own, width), BF),
        give=pltpu.VMEM((5, own, width), F32),
        x4=pltpu.VMEM((4, SEQ, width), BF),
        lens4=pltpu.VMEM((4, 8, 128), F32),
        n1=pltpu.VMEM((4, SEQ, width), BF),
        n1t=pltpu.VMEM((width, rows), BF),
        gz=pltpu.VMEM((4, SEQ, width), BF),
        turned=pltpu.VMEM((width, rows), BF),
        gztt=pltpu.VMEM((width, 4 * TXT), BF),
        wo=pltpu.VMEM((width, span), BF),
        q=pltpu.VMEM((4, SEQ, span), BF),
        k=pltpu.VMEM((4, SEQ, span), BF),
        v=pltpu.VMEM((4, SEQ, span), BF),
        c=pltpu.VMEM((4, SEQ, span), BF),
        probs=pltpu.VMEM((4 * heads, SEQ, SEQ), BF),
        pa=pltpu.VMEM((4, SEQ, width), BF),
        ra=pltpu.VMEM((2, SEQ, width), BF),
        xs=pltpu.VMEM((SEQ, width), BF),
        xr=pltpu.VMEM((SEQ, width), BF),
        y1=pltpu.VMEM((SEQ, width), F32),
        n2vt=pltpu.VMEM((width, 4 * VIS), BF),
        n2tt=pltpu.VMEM((width, 4 * TXT), BF),
        u=pltpu.VMEM((4 * VIS, 256), F32),
        gh=pltpu.VMEM((4 * VIS, 256), F32),
        hv=pltpu.VMEM((4 * VIS, width), BF),
        guv=pltpu.VMEM((4 * VIS, width), BF),
        ht=pltpu.VMEM((4 * TXT, width), BF),
        gut=pltpu.VMEM((4 * TXT, width), BF),
        pg=pltpu.VMEM((4, SEQ, width), BF),
        rg=pltpu.VMEM((2, SEQ, width), BF),
        xsg=pltpu.VMEM((SEQ, width), BF),
        xrg=pltpu.VMEM((SEQ, width), BF),
        gy=pltpu.VMEM((2, SEQ, width), BF),
        xsf=pltpu.VMEM((SEQ, width), BF),
        xrf=pltpu.VMEM((SEQ, width), BF),
        xsb=pltpu.VMEM((2, SEQ, width), BF),
        xrb=pltpu.VMEM((2, SEQ, width), BF),
        gs=pltpu.VMEM((2, own, 128), F32),
        gr=pltpu.VMEM((2, own, 128), F32),
        sent=pltpu.SemaphoreType.DMA((40,)),
        came=pltpu.SemaphoreType.DMA((40,)),
        ring_sent=pltpu.SemaphoreType.DMA((6 * 2 * (n // 2) * 2,)),
        ring_came=pltpu.SemaphoreType.DMA((6 * 2 * (n // 2) * 2,)),
    )
    inputs = dict(
        lengths=caption_lengths,
        tokens=tokens,
        cotangent=cotangent,
        gain_attn=gain_one,
        gain_ffn=gain_two,
        w_query=w_query,
        w_key=w_key,
        w_value=w_value,
        w_out=w_out.T,
        vis_in=vis_in,
        vis_out=vis_out.T,
        txt_in=txt_in,
        txt_out=txt_out.T,
    )
    results = dict(
        out_tokens=jax.ShapeDtypeStruct((row_count, width), BF),
        grad_tokens=jax.ShapeDtypeStruct((row_count, width), F32),
        gw=jax.ShapeDtypeStruct((5, 2, own, width), F32),
        gg=jax.ShapeDtypeStruct((2, own, 128), F32),
    )
    vmem = pl.BlockSpec(memory_space=pltpu.VMEM)
    names = tuple(inputs) + tuple(results) + tuple(scratch)
    out, gtok, gw, gg = pl.pallas_call(
        functools.partial(layer_kernel, n, names),
        out_shape=tuple(results.values()),
        in_specs=[pl.BlockSpec(memory_space=pltpu.SMEM)] + [vmem] * (len(inputs) - 1),
        out_specs=[vmem] * len(results),
        scratch_shapes=list(scratch.values()),
        compiler_params=pltpu.CompilerParams(
            collective_id=0, has_side_effects=True, vmem_limit_bytes=60 * 2**20
        ),
    )(*inputs.values())

    final = pl.pallas_call(
        finish_kernel,
        out_shape=(
            jax.ShapeDtypeStruct((row_count, width), BF),
            jax.ShapeDtypeStruct((row_count, width), F32),
            jax.ShapeDtypeStruct((1, own), F32),
            jax.ShapeDtypeStruct((own, 2 * span), F32),
            jax.ShapeDtypeStruct((own, 2 * span), F32),
            jax.ShapeDtypeStruct((own, 2 * span), F32),
            jax.ShapeDtypeStruct((own, 2 * span), F32),
            jax.ShapeDtypeStruct((1, own), F32),
            jax.ShapeDtypeStruct((own, 2 * width), F32),
            jax.ShapeDtypeStruct((own, 2 * width), F32),
            jax.ShapeDtypeStruct((own, 2 * width), F32),
            jax.ShapeDtypeStruct((own, 2 * width), F32),
        ),
        in_specs=[vmem] * 6,
        out_specs=[vmem] * 12,
        compiler_params=pltpu.CompilerParams(vmem_limit_bytes=60 * 2**20),
    )(out, gtok, gw, gg, gain_one, gain_two)
    final = list(final)
    final[2] = final[2].reshape(own)
    final[7] = final[7].reshape(own)
    for turned in (6, 9, 11):
        final[turned] = final[turned].T
    return tuple(final)


def norm_parts(values):
    center = values - jnp.mean(values, axis=-1, keepdims=True)
    spread = jnp.mean(center * center, axis=-1, keepdims=True)
    inverse = lax.rsqrt(spread + epsilon)
    return (center * inverse, inverse)


def norm_back(grad_out, normed, inverse, gain):
    grad_normed = grad_out * gain
    grad_gain = jnp.sum(grad_out * normed, axis=0)
    inner = (
        grad_normed
        - jnp.mean(grad_normed, axis=-1, keepdims=True)
        - normed * jnp.mean(grad_normed * normed, axis=-1, keepdims=True)
    )
    return (inverse * inner, grad_gain)


def matmul(left, right):
    return jnp.dot(left, right, preferred_element_type=jnp.float32)


def matmul_tn(left, right):
    return lax.dot_general(
        left, right, (((0,), (0,)), ((), ())), preferred_element_type=jnp.float32
    )


def matmul_nt(left, right):
    return lax.dot_general(
        left, right, (((1,), (1,)), ((), ())), preferred_element_type=jnp.float32
    )


def gelu_slope(pre):
    cumulative = 0.5 * (1.0 + lax.erf(pre * inv_root_two))
    density = jnp.exp(-0.5 * pre * pre) * inv_root_tau
    return cumulative + pre * density


def expert_forward(rows, weight_in, weight_out):
    pre = matmul(rows, weight_in)
    hidden = jax.nn.gelu(pre, approximate=False).astype(jnp.bfloat16)
    return (pre, hidden, matmul(hidden, weight_out))


def expert_backward(rows, pre, hidden, grad_out, weight_in, weight_out):
    grad_weight_out = matmul_tn(hidden, grad_out)
    grad_hidden = matmul_nt(grad_out, weight_out)
    grad_pre = (grad_hidden * gelu_slope(pre)).astype(jnp.bfloat16)
    return (matmul_tn(rows, grad_pre), grad_weight_out, matmul_nt(grad_pre, weight_in))


def join_experts(image_rows, text_rows, pair_count, width):
    joined = jnp.concatenate(
        [
            image_rows.reshape(pair_count, PATCHES, width),
            text_rows.reshape(pair_count, CAPTION, width),
        ],
        axis=1,
    )
    return joined.reshape(-1, width)


def plain_layer(
    tokens,
    caption_lengths,
    gain_attn,
    w_query,
    w_key,
    w_value,
    w_out,
    gain_ffn,
    vis_in,
    vis_out,
    txt_in,
    txt_out,
    cotangent,
):
    seq_len = PATCHES + CAPTION
    width = tokens.shape[1]
    pair_count = tokens.shape[0] // seq_len
    half_pairs = pair_count // lax.axis_size("tensor")
    half_rows = half_pairs * seq_len
    row_start = lax.axis_index("tensor") * half_rows
    gain_one, query_w, key_w, value_w, out_w = (
        lax.all_gather(gain_attn, "dp", axis=0, tiled=True),
        lax.all_gather(w_query, "dp", axis=0, tiled=True),
        lax.all_gather(w_key, "dp", axis=0, tiled=True),
        lax.all_gather(w_value, "dp", axis=0, tiled=True),
        lax.all_gather(w_out, "dp", axis=1, tiled=True),
    )
    gain_two, vis_in_w, vis_out_w, txt_in_w, txt_out_w = (
        lax.all_gather(gain_ffn, "dp", axis=0, tiled=True),
        lax.all_gather(vis_in, "dp", axis=0, tiled=True),
        lax.all_gather(vis_out, "dp", axis=1, tiled=True),
        lax.all_gather(txt_in, "dp", axis=0, tiled=True),
        lax.all_gather(txt_out, "dp", axis=1, tiled=True),
    )
    gain_one = gain_one.astype(jnp.float32)
    gain_two = gain_two.astype(jnp.float32)
    head_local = query_w.shape[1] // HEAD_DIM
    score_scale = HEAD_DIM ** (-0.5)
    position = jnp.arange(seq_len, dtype=jnp.int32)
    live = (position[None, :] < PATCHES) | (position[None, :] - PATCHES < caption_lengths[:, None])
    valid_rows = live.astype(jnp.float32)
    mask_col = valid_rows.reshape(-1, 1)
    key_live = valid_rows[:, None, None, :] > 0.5

    def own_rows(values):
        return lax.dynamic_slice_in_dim(values, row_start, half_rows, 0)

    inputs = tokens.astype(jnp.float32)
    normed_one, inverse_one = norm_parts(inputs)
    first_in = (normed_one * gain_one).astype(jnp.bfloat16)

    def project(weight):
        return (
            matmul(first_in, weight)
            .astype(jnp.bfloat16)
            .reshape(pair_count, seq_len, head_local, HEAD_DIM)
        )

    queries = project(query_w)
    keys_all = project(key_w)
    values_all = project(value_w)

    def score_block():
        raw = (
            jnp.einsum("pqhe,pkhe->phqk", queries, keys_all, preferred_element_type=jnp.float32)
            * score_scale
        )
        return jnp.where(key_live, raw, -1e30)

    scores = score_block()
    top = jnp.max(scores, axis=-1, keepdims=True)
    weights = jnp.exp(scores - top)
    total = jnp.sum(weights, axis=-1, keepdims=True)
    probs = (weights / total).astype(jnp.bfloat16)
    log_total = top + jnp.log(total)
    context = jnp.einsum("phqk,pkhe->pqhe", probs, values_all, preferred_element_type=jnp.float32)
    context = context.astype(jnp.bfloat16).reshape(-1, head_local * HEAD_DIM)
    attn_terms = matmul(context, out_w)
    attended_own = lax.psum_scatter(
        attn_terms.astype(jnp.bfloat16), "tensor", scatter_dimension=0, tiled=True
    ).astype(jnp.float32)
    mask_own = own_rows(mask_col)
    middle_own = own_rows(inputs) + mask_own * attended_own
    normed_two, inverse_two = norm_parts(middle_own)
    second_own = (normed_two * gain_two).astype(jnp.bfloat16)
    grid = lax.all_gather(second_own, "tensor", axis=0, tiled=True).reshape(
        pair_count, seq_len, width
    )
    image_rows = grid[:, :PATCHES].reshape(-1, width)
    text_rows = grid[:, PATCHES:].reshape(-1, width)
    image_pre, image_hidden, image_part = expert_forward(image_rows, vis_in_w, vis_out_w)
    text_pre, text_hidden, text_part = expert_forward(text_rows, txt_in_w, txt_out_w)
    image_own, text_own = (
        lax.psum_scatter(
            image_part.astype(jnp.bfloat16), "tensor", scatter_dimension=0, tiled=True
        ).astype(jnp.float32),
        lax.psum_scatter(
            text_part.astype(jnp.bfloat16), "tensor", scatter_dimension=0, tiled=True
        ).astype(jnp.float32),
    )
    branch_own = join_experts(image_own, text_own, half_pairs, width)
    output_own = (middle_own + mask_own * branch_own).astype(jnp.bfloat16)
    upstream = cotangent.astype(jnp.float32)
    grad_branch = (upstream * mask_col).astype(jnp.bfloat16).reshape(pair_count, seq_len, width)
    image_grads = expert_backward(
        image_rows,
        image_pre,
        image_hidden,
        grad_branch[:, :PATCHES].reshape(-1, width),
        vis_in_w,
        vis_out_w,
    )
    text_grads = expert_backward(
        text_rows,
        text_pre,
        text_hidden,
        grad_branch[:, PATCHES:].reshape(-1, width),
        txt_in_w,
        txt_out_w,
    )
    back_image_own, back_text_own = (
        lax.psum_scatter(
            image_grads[2].astype(jnp.bfloat16), "tensor", scatter_dimension=0, tiled=True
        ).astype(jnp.float32),
        lax.psum_scatter(
            text_grads[2].astype(jnp.bfloat16), "tensor", scatter_dimension=0, tiled=True
        ).astype(jnp.float32),
    )
    grad_second_own = join_experts(back_image_own, back_text_own, half_pairs, width)
    grad_norm_own, gain_part = norm_back(grad_second_own, normed_two, inverse_two, gain_two)
    grad_middle_own = own_rows(upstream) + grad_norm_own
    output_wide, grad_middle, gain_parts = (
        lax.all_gather(
            output_own.astype(jnp.float32).astype(jnp.bfloat16), "tensor", axis=0, tiled=True
        ).astype(jnp.float32),
        lax.all_gather(grad_middle_own.astype(jnp.bfloat16), "tensor", axis=0, tiled=True).astype(
            grad_middle_own.dtype
        ),
        lax.all_gather(gain_part.astype(jnp.bfloat16), "tensor", axis=0, tiled=True).astype(
            gain_part.dtype
        ),
    )
    output = output_wide.astype(jnp.bfloat16)
    grad_gain_two = jnp.sum(gain_parts.reshape(-1, width), axis=0)
    grad_attended = (grad_middle * mask_col).astype(jnp.bfloat16)
    grad_out_w = matmul_tn(context, grad_attended)
    grad_context = (
        matmul_nt(grad_attended, out_w)
        .astype(jnp.bfloat16)
        .reshape(pair_count, seq_len, head_local, HEAD_DIM)
    )
    scores_again = score_block()
    probs_exact = jnp.exp(scores_again - log_total)
    grad_probs = jnp.einsum(
        "pqhe,pkhe->phqk", grad_context, values_all, preferred_element_type=jnp.float32
    )
    inner = jnp.sum(grad_probs * probs_exact, axis=-1, keepdims=True)
    grad_scores = (probs_exact * (grad_probs - inner)).astype(jnp.bfloat16)
    grad_values = jnp.einsum(
        "phqk,pqhe->pkhe", probs, grad_context, preferred_element_type=jnp.float32
    )
    grad_values = grad_values.astype(jnp.bfloat16).reshape(-1, head_local * HEAD_DIM)
    grad_queries = (
        jnp.einsum("phqk,pkhe->pqhe", grad_scores, keys_all, preferred_element_type=jnp.float32)
        * score_scale
    )
    grad_queries = grad_queries.astype(jnp.bfloat16).reshape(-1, head_local * HEAD_DIM)
    grad_keys = (
        jnp.einsum("phqk,pqhe->pkhe", grad_scores, queries, preferred_element_type=jnp.float32)
        * score_scale
    )
    grad_keys = grad_keys.astype(jnp.bfloat16).reshape(-1, head_local * HEAD_DIM)
    grad_query_w = matmul_tn(first_in, grad_queries)
    grad_key_w = matmul_tn(first_in, grad_keys)
    grad_value_w = matmul_tn(first_in, grad_values)
    first_part = (
        matmul_nt(grad_queries, query_w)
        + matmul_nt(grad_keys, key_w)
        + matmul_nt(grad_values, value_w)
    )
    grad_first = lax.psum(first_part.astype(jnp.bfloat16), "tensor").astype(jnp.float32)
    grad_norm_one, grad_gain_one = norm_back(grad_first, normed_one, inverse_one, gain_one)
    grad_inputs = grad_middle + grad_norm_one
    attn_sent = (
        lax.psum_scatter(grad_gain_one, "dp", scatter_dimension=0, tiled=True),
        lax.psum_scatter(grad_query_w, "dp", scatter_dimension=0, tiled=True),
        lax.psum_scatter(grad_key_w, "dp", scatter_dimension=0, tiled=True),
        lax.psum_scatter(grad_value_w, "dp", scatter_dimension=0, tiled=True),
        lax.psum_scatter(grad_out_w, "dp", scatter_dimension=1, tiled=True),
    )
    final_expert = (
        lax.psum_scatter(grad_gain_two, "dp", scatter_dimension=0, tiled=True),
        lax.psum_scatter(image_grads[0], "dp", scatter_dimension=0, tiled=True),
        lax.psum_scatter(image_grads[1], "dp", scatter_dimension=1, tiled=True),
        lax.psum_scatter(text_grads[0], "dp", scatter_dimension=0, tiled=True),
        lax.psum_scatter(text_grads[1], "dp", scatter_dimension=1, tiled=True),
    )
    return (
        output,
        grad_inputs,
        attn_sent[0],
        attn_sent[1],
        attn_sent[2],
        attn_sent[3],
        attn_sent[4],
        final_expert[0],
        final_expert[1],
        final_expert[2],
        final_expert[3],
        final_expert[4],
    )


def solution(mesh):
    def local(tokens, lengths, gain, w_query, *rest):
        ring = mesh.shape["dp"] // 2
        fits = (
            mesh.shape["tensor"] == 2
            and ring == 8
            and lengths.shape[0] == 2
            and w_query.shape[0] % 16 == 0
        )
        layer = fused_layer if fits else plain_layer
        return layer(tokens, lengths, gain, w_query, *rest)

    return jax.shard_map(
        local,
        mesh=mesh,
        in_specs=(
            P("dp", None),
            P("dp"),
            P("dp"),
            P("dp", "tensor"),
            P("dp", "tensor"),
            P("dp", "tensor"),
            P("tensor", "dp"),
            P("dp"),
            P("dp", "tensor"),
            P("tensor", "dp"),
            P("dp", "tensor"),
            P("tensor", "dp"),
            P("dp", None),
        ),
        out_specs=(
            P("dp", None),
            P("dp", None),
            P("dp"),
            P("dp", "tensor"),
            P("dp", "tensor"),
            P("dp", "tensor"),
            P("tensor", "dp"),
            P("dp"),
            P("dp", "tensor"),
            P("tensor", "dp"),
            P("dp", "tensor"),
            P("tensor", "dp"),
        ),
        check_vma=False,
    )
```

```python
import functools
import math
import types

import jax
import jax.numpy as jnp
from jax import lax
from jax.experimental import pallas as pl
from jax.experimental.pallas import tpu as pltpu
from jax.sharding import PartitionSpec as P

HEAD_DIM = 64
PATCHES = 197
CAPTION = 40
VIS = 208
TXT = 48
SEQ = VIS + TXT

MESH = pl.DeviceIdType.MESH
BF = jnp.bfloat16
F32 = jnp.float32

ATT, TIN, TOUT, VIN, VOUT = range(5)

epsilon = 1e-05
inv_root_two = 1.0 / math.sqrt(2.0)
inv_root_tau = 1.0 / math.sqrt(2.0 * math.pi)


def mm(left, right):
    return jnp.dot(left, right, preferred_element_type=F32)


def mm_nt(left, right):
    return lax.dot_general(left, right, (((1,), (1,)), ((), ())), preferred_element_type=F32)


def mm_tn(left, right):
    return lax.dot_general(left, right, (((0,), (0,)), ((), ())), preferred_element_type=F32)


def normalize(values):
    center = values - jnp.mean(values, axis=-1, keepdims=True)
    spread = jnp.mean(center * center, axis=-1, keepdims=True)
    inverse = lax.rsqrt(spread + epsilon)
    return center * inverse, inverse


def normalize_back(grad_normed, normed, inverse):
    return inverse * (
        grad_normed
        - jnp.mean(grad_normed, axis=-1, keepdims=True)
        - normed * jnp.mean(grad_normed * normed, axis=-1, keepdims=True)
    )


def unit(size):
    rows = lax.broadcasted_iota(jnp.int32, (size, size), 0)
    return (rows == lax.broadcasted_iota(jnp.int32, (size, size), 1)).astype(F32).astype(BF)


def column(ref):
    size = ref.shape[1]
    return jnp.sum(unit(size).astype(F32) * ref[...].astype(F32), axis=1, keepdims=True)


def layer_kernel(n, names, *refs):
    R = types.SimpleNamespace(**dict(zip(names, refs)))
    R.pb, R.pf, R.ga, R.rf, R.rb, R.n2 = R.pg, R.pa, R.x4, R.ra, R.rg, R.n1
    R.gqkv, R.xsg, R.xrg = R.n2, R.xs, R.xr
    S, G, PART, LAND = R.shard, R.gathered, R.part, R.land
    OUT, GW, GG = R.padded_out, R.gw, R.gg
    width = G.shape[2]
    own = width // (2 * n)
    span = width // 4
    heads = span // HEAD_DIM

    x = lax.axis_index("tensor")
    d = lax.axis_index("dp")
    c = lax.rem(d, 2)
    other = 1 - c
    chip = d // 2
    y, z = lax.rem(chip, 2), chip // 2
    r = z + y * (n - 1 - 2 * z)
    half = n // 2

    def chip_at(pos):
        pos = lax.rem(pos + 2 * n, n)
        upper = pos // half
        return 2 * (pos + upper * (n - 1 - 2 * pos)) + upper

    mate = {"dp": d + 1 - 2 * c}
    across = {"tensor": 1 - x}
    diagonal = {"dp": d + 1 - 2 * c, "tensor": 1 - x}
    ahead = {"dp": 2 * chip_at(r + 1) + c}
    behind = {"dp": 2 * chip_at(r - 1) + c}
    way = (ahead, behind)

    def rows_at(pos):
        return pl.ds(pl.multiple_of(2 * own * chip_at(pos), 16), 2 * own)

    my_rows = pl.ds(pl.multiple_of(own * d, 16), own)

    barrier = pltpu.get_barrier_semaphore()
    for device in (mate, across, diagonal, ahead, behind):
        pl.semaphore_signal(barrier, inc=1, device_id=device, device_id_type=MESH)

    mine, theirs = pl.multiple_of(2 * c, 2), pl.multiple_of(2 * other, 2)
    pair_own = 2 * c + x
    pair_across = 2 * c + 1 - x

    started = []
    counter = [0]

    def remote(source, target, device):
        index = counter[0]
        counter[0] += 1
        return pltpu.make_async_remote_copy(
            src_ref=source,
            dst_ref=target,
            send_sem=R.sent.at[index],
            recv_sem=R.came.at[index],
            device_id=device,
            device_id_type=MESH,
        )

    def start(source, target, device):
        copy = remote(source, target, device)
        copy.start()
        started.append(copy)
        return copy

    def sent(copy):
        copy.wait_send()
        started[:] = [one for one in started if one is not copy]

    near, far = (ATT, 0, width // 2), (ATT, width // 2, width // 2)
    parts = [near, far] + [(k, 0, width) for k in (TIN, TOUT, VIN, VOUT)]
    tin, tout, vin, vout = parts[2:]
    longest = half

    def hops(part, side):
        return half if (parts.index(part) + side) % 2 == 0 else n - 1 - half

    def ring_index(part, side, s):
        return (parts.index(part) * 2 + side) * longest + s

    def view(ref, part, rows):
        k, first, count = part
        return ref.at[k, rows, pl.ds(first, count)]

    def gather_copy(part, side, s, pos):
        block = view(G, part, rows_at(pos))
        i = ring_index(part, side, s)
        return pltpu.make_async_remote_copy(
            src_ref=block,
            dst_ref=block,
            send_sem=R.ring_sent.at[i],
            recv_sem=R.ring_came.at[i],
            device_id=way[side],
            device_id_type=MESH,
        )

    def gather(part, s):
        for side in range(2):
            pos = r - s if side == 0 else r + s
            if 0 < s <= hops(part, side):
                gather_copy(part, side, s - 1, pos).wait_recv()
            if s < hops(part, side):
                gather_copy(part, side, s, pos).start()

    sum_base = len(parts) * 2 * longest

    def landed(part, side, s):
        k, first, count = part
        return LAND.at[k, side * hops(part, 0) + s, :, pl.ds(first, count)]

    def sum_copy(part, side, s, source):
        i = sum_base + ring_index(part, side, s)
        return pltpu.make_async_remote_copy(
            src_ref=source,
            dst_ref=landed(part, side, s),
            send_sem=R.ring_sent.at[i],
            recv_sem=R.ring_came.at[i],
            device_id=way[side],
            device_id_type=MESH,
        )

    def pass_sum(part, s):
        for side in range(2):
            reach = hops(part, side)
            if s >= reach:
                continue
            pos = r + (reach - s) if side == 0 else r - (reach - s)
            term = view(PART, part, rows_at(pos))
            if s == 0:
                source = term
            else:
                source = landed(part, side, s - 1)
                sum_copy(part, side, s - 1, source).wait_recv()
                source[...] = (source[...].astype(F32) + term[...].astype(F32)).astype(BF)
            sum_copy(part, side, s, source).start()

    finals = []
    row_sums = [[], []]

    def end_sum(*group):
        for part in group:
            k, first, count = part
            ends = []
            for side in range(2):
                end = landed(part, side, hops(part, side) - 1)
                sum_copy(part, side, hops(part, side) - 1, end).wait_recv()
                ends.append(end)
            cols = slice(first, first + count)
            counted = min(3 * span - first, count) if k == ATT else count

            def total(core):
                rows = pl.ds(pl.multiple_of(own * core, 16), own)
                chip_rows = pl.ds(pl.multiple_of(2 * own * chip + own * core, 16), own)
                block = (
                    ends[0][rows, :].astype(F32)
                    + ends[1][rows, :].astype(F32)
                    + PART[k, chip_rows, cols].astype(F32)
                )
                if k in (ATT, TIN, VIN):
                    weighted = G[k, chip_rows, cols].astype(F32)[:, :counted] * block[:, :counted]
                    total = jnp.sum(weighted, axis=-1, keepdims=True)
                    row_sums[0 if core is c else 1].append((k, total))
                return block

            R.give[k, :, cols] = total(other)
            finals.append(
                start(R.give.at[k, :, pl.ds(first, count)], GW.at[k, c, :, pl.ds(first, count)], mate)
            )
            GW[k, c, :, cols] = total(c)

    def shard_part(k, value):
        for core in range(2):
            S[k, core] = value(core).astype(BF)

    gain_one, gain_two = column(R.gain_attn), column(R.gain_ffn)

    def attention_part(core):
        cols = slice(core * span, (core + 1) * span)
        return jnp.concatenate(
            [
                R.w_query[:, cols].astype(F32) * (gain_one * HEAD_DIM**-0.5),
                R.w_key[:, cols].astype(F32) * gain_one,
                R.w_value[:, cols].astype(F32) * gain_one,
                R.w_out[:, cols].astype(F32),
            ],
            axis=1,
        )

    def half_of(ref, core):
        return ref[:, core * width : (core + 1) * width].astype(F32) * gain_two

    def turned_half(ref, core):
        return ref[:, core * width : (core + 1) * width]

    lengths = R.lengths

    def live(t, slots):
        return (slots < PATCHES) | ((slots >= VIS) & (slots < VIS + lengths[t]))

    def live_rows(t, j, count=64):
        slots = lax.broadcasted_iota(jnp.int32, (count, 1), 0) + j * count
        return live(t, slots).astype(F32)

    row_count = R.tokens.shape[0]

    def placed(t, slots, rows, kept):
        source = t * (PATCHES + CAPTION) + slots - (slots >= VIS).astype(jnp.int32) * (VIS - PATCHES)
        return ((rows == source) & kept).astype(F32).astype(BF)

    def chooser(t, only_live):
        slots = lax.broadcasted_iota(jnp.int32, (SEQ, row_count), 0)
        rows = lax.broadcasted_iota(jnp.int32, (SEQ, row_count), 1)
        filled = (slots < PATCHES) | ((slots >= VIS) & (slots < VIS + CAPTION))
        return placed(t, slots, rows, live(t, slots) if only_live else filled)

    shard_part(ATT, attention_part)
    G[ATT, my_rows, :] = S[ATT, c]
    for t in range(2):
        R.lens[t] = jnp.full((8, 128), lengths[t], jnp.int32).astype(F32)
    pl.semaphore_wait(barrier, 5)
    shard_a = start(S.at[pl.ds(0, 1), other], G.at[pl.ds(0, 1), my_rows, :], mate)
    send_lens = start(R.lens, R.lens4.at[pl.ds(mine, 2)], mate)
    for t in range(2):
        R.x4[2 * c + t] = mm(chooser(t, False), R.tokens[...]).astype(BF)
        R.lens4[2 * c + t] = R.lens[t]
    send_x = start(R.x4.at[pl.ds(mine, 2)], R.x4.at[pl.ds(mine, 2)], mate)
    shard_a.wait_recv()
    gather(near, 0)
    gather(far, 0)

    shard_part(TIN, functools.partial(half_of, R.txt_in))
    shard_part(TOUT, functools.partial(turned_half, R.txt_out))
    shard_part(VIN, functools.partial(half_of, R.vis_in))
    shard_part(VOUT, functools.partial(turned_half, R.vis_out))
    shard_b = start(S.at[pl.ds(1, 4), other], G.at[pl.ds(1, 4), my_rows, :], mate)
    for k in (TIN, TOUT, VIN, VOUT):
        G[k, my_rows, :] = S[k, c]
    gather(near, 1)
    for t in range(2):
        R.gz[2 * c + t] = mm(chooser(t, True), R.cotangent[...]).astype(BF)
        if t == 0:
            gather(far, 1)
    send_gz = start(R.gz.at[pl.ds(mine, 2)], R.gz.at[pl.ds(mine, 2)], mate)
    R.dy[...] = mm(chooser(x, False), R.cotangent[...]).astype(BF)
    for t in range(2):
        R.x[t] = R.x4[2 * c + t]
    shard_b.wait_recv()
    gather(tin, 0)
    gather(near, 2)
    send_x.wait_recv()

    for i in range(4):

        @pl.loop(0, SEQ // 64)
        def _(j, i=i):
            rows = pl.ds(pl.multiple_of(j * 64, 64), 64)
            normed, _ = normalize(R.x4[i, rows, :].astype(F32))
            R.n1[i, rows, :] = normed.astype(BF)

        R.n1t[:, i * SEQ : (i + 1) * SEQ] = R.n1[i].T
        if i == 0:
            gather(far, 2)
        if i == 1:
            gather(tout, 0)
            gather(near, 3)
        if i == 2:
            gather(far, 3)
            gather(vin, 0)
            gather(vout, 0)
    send_gz.wait_recv()
    send_lens.wait_recv()
    gather(near, 4)
    gather(far, 4)

    R.wo[...] = G[ATT][:, 3 * span :]

    @pl.loop(0, 4)
    def _(i):
        projected = mm(R.n1[i], G[ATT][:, : 3 * span]).astype(BF)
        R.q[i] = projected[:, :span]
        R.k[i] = projected[:, span : 2 * span]
        R.v[i] = projected[:, 2 * span :]

    lane = lax.broadcasted_iota(jnp.int32, (1, span), 1) // HEAD_DIM

    def only(head, values):
        return values * (lane == head).astype(F32).astype(BF)

    def head_rows(values, head):
        return values[head * HEAD_DIM : (head + 1) * HEAD_DIM, :]

    order = []
    for j in range(4):
        core = other if j < 2 else c
        turn = 1 - x if j % 2 == 0 else x
        order.append((turn, 2 * core + turn))
    attn_mate = [remote(R.pa.at[i], R.ra.at[turn], mate) for turn, i in order[:2]]
    cross_a = remote(R.xs, R.xr, across)

    for j, (turn, i) in enumerate(order):
        q, k, v = R.q[i], R.k[i], R.v[i]
        turned_v = v.T
        slots = lax.broadcasted_iota(jnp.int32, (SEQ, 1), 0)
        caption = (slots - VIS).astype(F32) < R.lens4[i][:1, :1]
        bias = jnp.where((slots < PATCHES) | ((slots >= VIS) & caption), 0.0, -1e30)
        contexts = []
        for h in range(heads):
            scores = mm_nt(only(h, k), q) + bias
            top = jnp.max(scores, axis=0, keepdims=True)
            weights = jnp.exp(scores - top)
            total = jnp.sum(weights, axis=0, keepdims=True)
            probs = (weights * (1.0 / total)).astype(BF)
            R.probs[i * heads + h] = probs
            contexts.append(mm(head_rows(turned_v, h), probs))
        contexts = jnp.concatenate(contexts, axis=0)
        R.ct[:, pl.ds(pl.multiple_of(i * SEQ, SEQ), SEQ)] = contexts.astype(BF)
        context = contexts.T.astype(BF)
        R.pa[i] = mm_nt(context, R.wo[...]).astype(BF)
        if j < 2:
            attn_mate[j].start()
        if j == 2:
            attn_mate[0].wait_recv()
            R.xs[...] = (R.pa[pair_across].astype(F32) + R.ra[1 - x].astype(F32)).astype(BF)
            cross_a.start()
        if j == 0:
            gather(tin, 1)
        if j == 1:
            gather(tout, 1)
        if j == 3:
            gather(tin, 2)
            gather(tout, 2)

    for copy in attn_mate:
        copy.wait_send()
    attn_mate[1].wait_recv()

    @pl.loop(0, width // 256)
    def _(j):
        cols = pl.ds(pl.multiple_of(j * 256, 256), 256)
        R.gzvt[cols, :] = R.gz[:, :VIS, cols].reshape(4 * VIS, 256).T
        R.gztt[cols, :] = R.gz[:, VIS:, cols].reshape(4 * TXT, 256).T

    gather(vin, 1)
    cross_a.wait_recv()

    @pl.loop(0, SEQ // 64)
    def _(j):
        rows = pl.ds(pl.multiple_of(j * 64, 64), 64)
        attended = (
            R.pa[pair_own, rows, :].astype(F32)
            + R.ra[x, rows, :].astype(F32)
            + R.xr[rows, :].astype(F32)
        )
        middle = R.x[x, rows, :].astype(F32) + live_rows(x, j) * attended
        R.y1[rows, :] = middle
        normed, _ = normalize(middle)
        R.n2[pair_own, rows, :] = normed.astype(BF)

    block = R.n2.at[pair_own]
    to_across = start(block, block, across)
    to_mate = start(block, block, mate)
    gather(vout, 1)
    gather(tin, 3)
    gather(tout, 3)
    to_across.wait_recv()
    block = R.n2.at[pair_across]
    passed = start(block, block, mate)
    gather(vin, 2)
    gather(vout, 2)
    gather(tin, 4)
    gather(tout, 4)
    to_mate.wait_recv()
    passed.wait_recv()

    def expert(pairs, low, high, w_in, w_out, h_ref, gu_ref, j):
        first, count = pairs
        per = high - low
        total_rows = count * per
        cols = slice(j * 256, (j + 1) * 256)
        inside = slice(first, first + count)
        R.u[:total_rows, :] = mm(
            R.n2[inside, low:high, :].reshape(total_rows, width), G[w_in, :, cols]
        )
        R.gh[:total_rows, :] = mm(
            R.gz[inside, low:high, :].reshape(total_rows, width), G[w_out, :, cols]
        )
        step = min(total_rows, VIS)

        @pl.loop(0, 2 * (total_rows // step))
        def _(i):
            lanes = lax.rem(i, 2) * 128
            rows = pl.ds(pl.multiple_of(i // 2 * step, 16), step)
            into = pl.ds(pl.multiple_of(first * per + i // 2 * step, 16), step)
            side = pl.ds(pl.multiple_of(lanes, 128), 128)
            pre = R.u[rows, side]
            cumulative = 0.5 * (1.0 + lax.erf(pre * inv_root_two))
            density = jnp.exp(-0.5 * pre * pre) * inv_root_tau
            onto = pl.ds(pl.multiple_of(j * 256 + lanes, 128), 128)
            h_ref[into, onto] = (pre * cumulative).astype(BF)
            gu_ref[into, onto] = (R.gh[rows, side] * (cumulative + pre * density)).astype(BF)

    def weight_grad(k, turned, ref, j):
        cols = slice(j * 256, (j + 1) * 256)
        PART[k, :, cols] = mm(turned, ref[:, cols]).astype(BF)

    tiles = range(width // 256)
    for j in tiles:
        expert((0, 4), VIS, SEQ, TIN, TOUT, R.ht, R.gut, j)
    gather(vin, 3)
    for j in tiles:
        weight_grad(TOUT, R.gztt[...], R.ht, j)

    @pl.loop(0, width // 256)
    def _(j):
        cols = pl.ds(pl.multiple_of(j * 256, 256), 256)
        R.n2vt[cols, :] = R.n2[:, :VIS, cols].reshape(4 * VIS, 256).T
        R.n2tt[cols, :] = R.n2[:, VIS:, cols].reshape(4 * TXT, 256).T

    gather(vout, 3)
    for j in tiles:
        weight_grad(TIN, R.n2tt[...], R.gut, j)
    pass_sum(tout, 0)
    pass_sum(tin, 0)
    gather(vin, 4)
    gather(vout, 4)

    def terms(target, hv, ht, w_vis, w_txt, m):
        vis_rows = slice(2 * m * VIS, 2 * (m + 1) * VIS)
        txt_rows = slice(2 * m * TXT, 2 * (m + 1) * TXT)
        vis_part = mm_nt(hv[vis_rows, :], G[w_vis]).astype(BF)
        target[2 * m : 2 * m + 2, :VIS, :] = vis_part.reshape(2, VIS, width)
        txt_part = mm_nt(ht[txt_rows, :], G[w_txt]).astype(BF)
        target[2 * m : 2 * m + 2, VIS:, :] = txt_part.reshape(2, TXT, width)

    mate_g = remote(R.pg.at[pl.ds(theirs, 2)], R.rg, mate)
    cross_g = remote(R.xsg, R.xrg, across)
    gy_across = remote(R.gy.at[x], R.gy.at[x], across)
    gy_mate = remote(R.ga.at[pair_own], R.ga.at[pair_own], mate)
    gy_passed = remote(R.ga.at[pair_across], R.ga.at[pair_across], mate)
    started.extend([cross_g, gy_across, gy_mate, gy_passed])

    def image_terms(m):
        terms(R.pg, R.guv, R.gut, VIN, TIN, m)
        pl.when(c != m)(mate_g.start)

    def sum_cores(m):
        @pl.when(c == m)
        def _():
            mate_g.wait_recv()
            R.xsg[...] = (R.pg[pair_across].astype(F32) + R.rg[1 - x].astype(F32)).astype(BF)
            cross_g.start()

    def middle_back(m):
        @pl.when(c == m)
        def _():
            cross_g.wait_recv()

            @pl.loop(0, SEQ // 64)
            def _(j):
                rows = pl.ds(pl.multiple_of(j * 64, 64), 64)
                grad_normed = (
                    R.pg[pair_own, rows, :].astype(F32)
                    + R.rg[x, rows, :].astype(F32)
                    + R.xrg[rows, :].astype(F32)
                )
                normed, inverse = normalize(R.y1[rows, :])
                grad = R.dy[rows, :].astype(F32) + normalize_back(grad_normed, normed, inverse)
                R.gy[x, rows, :] = grad.astype(BF)
                R.ga[pair_own, rows, :] = (grad * live_rows(x, j)).astype(BF)

            gy_across.start()
            gy_mate.start()

    def middle_pass(m):
        @pl.when(c == m)
        def _():
            gy_across.wait_recv()

            @pl.loop(0, SEQ // 64)
            def _(j):
                rows = pl.ds(pl.multiple_of(j * 64, 64), 64)
                R.ga[pair_across, rows, :] = (
                    R.gy[1 - x, rows, :].astype(F32) * live_rows(1 - x, j)
                ).astype(BF)

            gy_passed.start()

    def middle_came(m):
        @pl.when(c != m)
        def _():
            gy_mate.wait_recv()
            gy_passed.wait_recv()

    sent(send_x)
    cross_a.wait_send()
    for j in tiles:
        expert((0, 2), 0, VIS, VIN, VOUT, R.hv, R.guv, j)
        if j == 1:
            pass_sum(tout, 1)
    image_terms(0)
    pass_sum(tin, 1)
    expert((2, 2), 0, VIS, VIN, VOUT, R.hv, R.guv, 0)
    sum_cores(0)
    expert((2, 2), 0, VIS, VIN, VOUT, R.hv, R.guv, 1)
    pass_sum(tout, 2)
    for j in tiles[2:]:
        expert((2, 2), 0, VIS, VIN, VOUT, R.hv, R.guv, j)
    image_terms(1)
    for copy in (to_across, to_mate, passed):
        sent(copy)
    sum_cores(1)
    pass_sum(tin, 2)

    for m in range(2):
        terms(R.pf, R.hv, R.ht, VOUT, TOUT, m)
    mate_f = start(R.pf.at[pl.ds(theirs, 2)], R.rf, mate)
    cross_f = remote(R.xsf, R.xrf, across)
    started.append(cross_f)
    middle_back(0)
    for j in tiles:
        weight_grad(VOUT, R.gzvt[...], R.hv, j)
    pass_sum(tout, 3)
    pass_sum(vout, 0)
    for j in tiles:
        weight_grad(VIN, R.n2vt[...], R.guv, j)
    pass_sum(tin, 3)
    pass_sum(vin, 0)
    middle_pass(0)
    middle_back(1)
    mate_f.wait_recv()
    R.xsf[...] = (R.pf[pair_across].astype(F32) + R.rf[1 - x].astype(F32)).astype(BF)
    R.fown[...] = (R.pf[pair_own].astype(F32) + R.rf[x].astype(F32)).astype(BF)
    cross_f.start()
    end_sum(tout, tin)
    pass_sum(vout, 1)
    mate_g.wait_send()
    middle_came(0)

    back_mate = [remote(R.pb.at[theirs + t], R.rb.at[t], mate) for t in range(2)]
    back_cross = [remote(R.xsb.at[t], R.xrb.at[t], across) for t in range(2)]
    started.extend(back_mate + back_cross)

    def attention_back(m, t):
        i = 2 * m + t
        grad_context = mm(R.ga[i], R.wo[...]).astype(BF)
        q, k, v = R.q[i], R.k[i], R.v[i]
        turned_k = k.T
        grad_q = []
        grad_k = jnp.zeros((SEQ, span), F32)
        grad_v = jnp.zeros((SEQ, span), F32)
        for h in range(heads):
            probs = R.probs[i * heads + h]
            grad_probs = mm_nt(only(h, v), grad_context)
            exact = probs.astype(F32)
            inner = jnp.sum(grad_probs * exact, axis=0, keepdims=True)
            grad_scores = (exact * (grad_probs - inner)).astype(BF)
            grad_q.append(mm(head_rows(turned_k, h), grad_scores))
            grad_k += mm(grad_scores, only(h, q))
            grad_v += mm(probs, only(h, grad_context))
        grad_q = jnp.concatenate(grad_q, axis=0).T
        joined = jnp.concatenate([grad_q, grad_k, grad_v], axis=1).astype(BF)
        R.gqkv[i, :, : 3 * span] = joined
        R.pb[i] = mm_nt(joined, G[ATT][:, : 3 * span]).astype(BF)
        pl.when(c != m)(back_mate[t].start)

    def back_sum(m, t):
        @pl.when(c == m)
        def _():
            back_mate[t].wait_recv()
            R.xsb[t] = (R.pb[2 * m + t].astype(F32) + R.rb[t].astype(F32)).astype(BF)
            back_cross[t].start()

    attention_back(0, 0)
    middle_pass(1)
    pass_sum(vin, 1)
    attention_back(0, 1)
    back_sum(0, 0)

    cross_f.wait_recv()

    @pl.loop(0, SEQ // 64)
    def _(j):
        rows = pl.ds(pl.multiple_of(j * 64, 64), 64)
        branch = R.fown[rows, :].astype(F32) + R.xrf[rows, :].astype(F32)
        OUT[x, rows, :] = (R.y1[rows, :] + live_rows(x, j) * branch).astype(BF)

    out_across = start(OUT.at[x], OUT.at[x], across)
    pass_sum(vout, 2)
    middle_came(1)
    attention_back(1, 0)
    back_sum(0, 1)
    pass_sum(vin, 2)
    attention_back(1, 1)
    back_sum(1, 0)
    pass_sum(vout, 3)
    pass_sum(vin, 3)

    lanes = width // 2

    @pl.loop(0, width // 256)
    def _(j):
        rows = pl.ds(pl.multiple_of(j * 256, 256), 256)
        grad_v = mm(R.n1t[rows, :], R.gqkv[:, :, lanes : 3 * span].reshape(4 * SEQ, span))
        grad_o = mm(R.ct[...], R.ga[:, :, rows].reshape(4 * SEQ, 256)).T
        PART[ATT, rows, lanes:] = jnp.concatenate([grad_v, grad_o], axis=1).astype(BF)

    pass_sum(far, 0)

    @pl.loop(0, width // 256)
    def _(j):
        rows = pl.ds(pl.multiple_of(j * 256, 256), 256)
        grads = mm(R.n1t[rows, :], R.gqkv[:, :, :lanes].reshape(4 * SEQ, lanes))
        PART[ATT, rows, :lanes] = grads.astype(BF)

    pass_sum(near, 0)
    back_sum(1, 1)

    def input_back(m, t):
        @pl.when(c == m)
        def _():
            back_cross[t].wait_recv()

            @pl.loop(0, SEQ // 64)
            def _(j):
                rows = pl.ds(pl.multiple_of(j * 64, 64), 64)
                grad_normed = R.xsb[t, rows, :].astype(F32) + R.xrb[t, rows, :].astype(F32)
                normed, inverse = normalize(R.x[t, rows, :].astype(F32))
                grad = R.gy[t, rows, :].astype(F32) + normalize_back(grad_normed, normed, inverse)
                high = grad.astype(BF)
                rows = pl.ds(pl.multiple_of(t * SEQ + j * 64, 64), 64)
                R.hv[rows, :] = high
                R.guv[rows, :] = (grad - high.astype(F32)).astype(BF)

    pass_sum(far, 1)
    input_back(0, 0)
    pass_sum(near, 1)
    input_back(0, 1)
    end_sum(vout, vin)
    pass_sum(far, 2)
    pass_sum(near, 2)

    slots = lax.broadcasted_iota(jnp.int32, (row_count, 2 * SEQ), 1)
    rows = lax.broadcasted_iota(jnp.int32, (row_count, 2 * SEQ), 0)
    turn = slots // SEQ
    back = placed(turn, slots - turn * SEQ, rows, slots >= 0)
    out_across.wait_recv()
    R.out_tokens[...] = mm(back, OUT[...].reshape(2 * SEQ, width)).astype(BF)
    pass_sum(far, 3)
    pass_sum(near, 3)
    input_back(1, 0)
    input_back(1, 1)
    R.grad_tokens[...] = mm(back, R.hv[: 2 * SEQ, :]) + mm(back, R.guv[: 2 * SEQ, :])
    end_sum(far, near)

    first_lane = lax.broadcasted_iota(jnp.int32, (own, 128), 1) == 0
    for place in range(2):
        attn = sum(total for k, total in row_sums[place] if k == ATT)
        experts = sum(total for k, total in row_sums[place] if k != ATT)
        R.gs[place] = jnp.where(first_lane, attn, experts)
    peers = [
        start(R.gs.at[place], R.gr.at[slot], device)
        for slot, (place, device) in enumerate(((1, mate), (0, across), (1, diagonal)))
    ]
    for copy in finals + peers:
        copy.wait_recv()
    GG[...] = (R.gs[0] + R.gr[1]) + (R.gr[0] + R.gr[2])

    for copy in started:
        copy.wait_send()
    for part in parts:
        for side in range(2):
            for s in range(hops(part, side)):
                gather_copy(part, side, s, r).wait_send()
                sum_copy(part, side, s, landed(part, side, s)).wait_send()


def finish_kernel(out, gtok, gw, gg, gain_attn, gain_ffn, *rest):
    (
        out_tokens,
        grad_tokens,
        grad_gain_attn,
        grad_query,
        grad_key,
        grad_value,
        grad_out,
        grad_gain_ffn,
        grad_vis_in,
        grad_vis_out,
        grad_txt_in,
        grad_txt_out,
    ) = rest
    out_tokens[...] = out[...]
    grad_tokens[...] = gtok[...]
    width = gw.shape[3]
    own = gw.shape[2]
    span = width // 4
    gain_one, gain_two = column(gain_attn), column(gain_ffn)
    square = unit(own).astype(F32)
    grad_gain_attn[...] = jnp.sum(square * (gg[:, :1] / gain_one), axis=0, keepdims=True)
    grad_gain_ffn[...] = jnp.sum(square * (gg[:, 1:2] / gain_two), axis=0, keepdims=True)

    def both(part):
        return jnp.concatenate([gw[ATT, core][:, part * span : (part + 1) * span] for core in range(2)], axis=1)

    grad_query[...] = both(0) * (gain_one * HEAD_DIM**-0.5)
    grad_key[...] = both(1) * gain_one
    grad_value[...] = both(2) * gain_one
    grad_out[...] = both(3)
    for core in range(2):
        part = slice(core * width, (core + 1) * width)
        grad_vis_in[:, part] = gw[VIN, core] * gain_two
        grad_txt_in[:, part] = gw[TIN, core] * gain_two
        grad_vis_out[:, part] = gw[VOUT, core]
        grad_txt_out[:, part] = gw[TOUT, core]


def fused_layer(
    tokens,
    caption_lengths,
    gain_attn,
    w_query,
    w_key,
    w_value,
    w_out,
    gain_ffn,
    vis_in,
    vis_out,
    txt_in,
    txt_out,
    cotangent,
):
    n = lax.axis_size("dp") // 2
    own = w_query.shape[0]
    row_count, width = tokens.shape
    span = width // 4
    heads = span // HEAD_DIM
    gain_one, gain_two = gain_attn.reshape(1, own), gain_ffn.reshape(1, own)

    rows = 4 * SEQ
    scratch = dict(
        shard=pltpu.VMEM((5, 2, own, width), BF),
        lens=pltpu.VMEM((2, 8, 128), F32),
        x=pltpu.VMEM((2, SEQ, width), BF),
        dy=pltpu.VMEM((SEQ, width), BF),
        padded_out=pltpu.VMEM((2, SEQ, width), BF),
        gathered=pltpu.VMEM((5, width, width), BF),
        part=pltpu.VMEM((5, width, width), BF),
        land=pltpu.VMEM((5, n - 1, 2 * own, width), BF),
        give=pltpu.VMEM((5, own, width), F32),
        x4=pltpu.VMEM((4, SEQ, width), BF),
        lens4=pltpu.VMEM((4, 8, 128), F32),
        n1=pltpu.VMEM((4, SEQ, width), BF),
        n1t=pltpu.VMEM((width, rows), BF),
        gz=pltpu.VMEM((4, SEQ, width), BF),
        gzvt=pltpu.VMEM((width, 4 * VIS), BF),
        ct=pltpu.VMEM((span, rows), BF),
        fown=pltpu.VMEM((SEQ, width), BF),
        gztt=pltpu.VMEM((width, 4 * TXT), BF),
        wo=pltpu.VMEM((width, span), BF),
        q=pltpu.VMEM((4, SEQ, span), BF),
        k=pltpu.VMEM((4, SEQ, span), BF),
        v=pltpu.VMEM((4, SEQ, span), BF),
        probs=pltpu.VMEM((4 * heads, SEQ, SEQ), BF),
        pa=pltpu.VMEM((4, SEQ, width), BF),
        ra=pltpu.VMEM((2, SEQ, width), BF),
        xs=pltpu.VMEM((SEQ, width), BF),
        xr=pltpu.VMEM((SEQ, width), BF),
        y1=pltpu.VMEM((SEQ, width), F32),
        n2vt=pltpu.VMEM((width, 4 * VIS), BF),
        n2tt=pltpu.VMEM((width, 4 * TXT), BF),
        u=pltpu.VMEM((4 * VIS, 256), F32),
        gh=pltpu.VMEM((4 * VIS, 256), F32),
        hv=pltpu.VMEM((4 * VIS, width), BF),
        guv=pltpu.VMEM((4 * VIS, width), BF),
        ht=pltpu.VMEM((4 * TXT, width), BF),
        gut=pltpu.VMEM((4 * TXT, width), BF),
        pg=pltpu.VMEM((4, SEQ, width), BF),
        rg=pltpu.VMEM((2, SEQ, width), BF),
        gy=pltpu.VMEM((2, SEQ, width), BF),
        xsf=pltpu.VMEM((SEQ, width), BF),
        xrf=pltpu.VMEM((SEQ, width), BF),
        xsb=pltpu.VMEM((2, SEQ, width), BF),
        xrb=pltpu.VMEM((2, SEQ, width), BF),
        gs=pltpu.VMEM((2, own, 128), F32),
        gr=pltpu.VMEM((3, own, 128), F32),
        sent=pltpu.SemaphoreType.DMA((40,)),
        came=pltpu.SemaphoreType.DMA((40,)),
        ring_sent=pltpu.SemaphoreType.DMA((6 * 2 * (n // 2) * 2,)),
        ring_came=pltpu.SemaphoreType.DMA((6 * 2 * (n // 2) * 2,)),
    )
    inputs = dict(
        lengths=caption_lengths,
        tokens=tokens,
        cotangent=cotangent,
        gain_attn=gain_one,
        gain_ffn=gain_two,
        w_query=w_query,
        w_key=w_key,
        w_value=w_value,
        w_out=w_out.T,
        vis_in=vis_in,
        vis_out=vis_out.T,
        txt_in=txt_in,
        txt_out=txt_out.T,
    )
    results = dict(
        out_tokens=jax.ShapeDtypeStruct((row_count, width), BF),
        grad_tokens=jax.ShapeDtypeStruct((row_count, width), F32),
        gw=jax.ShapeDtypeStruct((5, 2, own, width), F32),
        gg=jax.ShapeDtypeStruct((own, 128), F32),
    )
    vmem = pl.BlockSpec(memory_space=pltpu.VMEM)
    names = tuple(inputs) + tuple(results) + tuple(scratch)
    out, gtok, gw, gg = pl.pallas_call(
        functools.partial(layer_kernel, n, names),
        out_shape=tuple(results.values()),
        in_specs=[pl.BlockSpec(memory_space=pltpu.SMEM)] + [vmem] * (len(inputs) - 1),
        out_specs=[vmem] * len(results),
        scratch_shapes=list(scratch.values()),
        compiler_params=pltpu.CompilerParams(
            collective_id=0, has_side_effects=True, vmem_limit_bytes=60 * 2**20
        ),
    )(*inputs.values())

    final = pl.pallas_call(
        finish_kernel,
        out_shape=(
            jax.ShapeDtypeStruct((row_count, width), BF),
            jax.ShapeDtypeStruct((row_count, width), F32),
            jax.ShapeDtypeStruct((1, own), F32),
            jax.ShapeDtypeStruct((own, 2 * span), F32),
            jax.ShapeDtypeStruct((own, 2 * span), F32),
            jax.ShapeDtypeStruct((own, 2 * span), F32),
            jax.ShapeDtypeStruct((own, 2 * span), F32),
            jax.ShapeDtypeStruct((1, own), F32),
            jax.ShapeDtypeStruct((own, 2 * width), F32),
            jax.ShapeDtypeStruct((own, 2 * width), F32),
            jax.ShapeDtypeStruct((own, 2 * width), F32),
            jax.ShapeDtypeStruct((own, 2 * width), F32),
        ),
        in_specs=[vmem] * 6,
        out_specs=[vmem] * 12,
        compiler_params=pltpu.CompilerParams(vmem_limit_bytes=60 * 2**20),
    )(out, gtok, gw, gg, gain_one, gain_two)
    final = list(final)
    final[2] = final[2].reshape(own)
    final[7] = final[7].reshape(own)
    for turned in (6, 9, 11):
        final[turned] = final[turned].T
    return tuple(final)


def norm_parts(values):
    center = values - jnp.mean(values, axis=-1, keepdims=True)
    spread = jnp.mean(center * center, axis=-1, keepdims=True)
    inverse = lax.rsqrt(spread + epsilon)
    return (center * inverse, inverse)


def norm_back(grad_out, normed, inverse, gain):
    grad_normed = grad_out * gain
    grad_gain = jnp.sum(grad_out * normed, axis=0)
    inner = (
        grad_normed
        - jnp.mean(grad_normed, axis=-1, keepdims=True)
        - normed * jnp.mean(grad_normed * normed, axis=-1, keepdims=True)
    )
    return (inverse * inner, grad_gain)


def matmul(left, right):
    return jnp.dot(left, right, preferred_element_type=jnp.float32)


def matmul_tn(left, right):
    return lax.dot_general(
        left, right, (((0,), (0,)), ((), ())), preferred_element_type=jnp.float32
    )


def matmul_nt(left, right):
    return lax.dot_general(
        left, right, (((1,), (1,)), ((), ())), preferred_element_type=jnp.float32
    )


def gelu_slope(pre):
    cumulative = 0.5 * (1.0 + lax.erf(pre * inv_root_two))
    density = jnp.exp(-0.5 * pre * pre) * inv_root_tau
    return cumulative + pre * density


def expert_forward(rows, weight_in, weight_out):
    pre = matmul(rows, weight_in)
    hidden = jax.nn.gelu(pre, approximate=False).astype(jnp.bfloat16)
    return (pre, hidden, matmul(hidden, weight_out))


def expert_backward(rows, pre, hidden, grad_out, weight_in, weight_out):
    grad_weight_out = matmul_tn(hidden, grad_out)
    grad_hidden = matmul_nt(grad_out, weight_out)
    grad_pre = (grad_hidden * gelu_slope(pre)).astype(jnp.bfloat16)
    return (matmul_tn(rows, grad_pre), grad_weight_out, matmul_nt(grad_pre, weight_in))


def join_experts(image_rows, text_rows, pair_count, width):
    joined = jnp.concatenate(
        [
            image_rows.reshape(pair_count, PATCHES, width),
            text_rows.reshape(pair_count, CAPTION, width),
        ],
        axis=1,
    )
    return joined.reshape(-1, width)


def plain_layer(
    tokens,
    caption_lengths,
    gain_attn,
    w_query,
    w_key,
    w_value,
    w_out,
    gain_ffn,
    vis_in,
    vis_out,
    txt_in,
    txt_out,
    cotangent,
):
    seq_len = PATCHES + CAPTION
    width = tokens.shape[1]
    pair_count = tokens.shape[0] // seq_len
    half_pairs = pair_count // lax.axis_size("tensor")
    half_rows = half_pairs * seq_len
    row_start = lax.axis_index("tensor") * half_rows
    gain_one, query_w, key_w, value_w, out_w = (
        lax.all_gather(gain_attn, "dp", axis=0, tiled=True),
        lax.all_gather(w_query, "dp", axis=0, tiled=True),
        lax.all_gather(w_key, "dp", axis=0, tiled=True),
        lax.all_gather(w_value, "dp", axis=0, tiled=True),
        lax.all_gather(w_out, "dp", axis=1, tiled=True),
    )
    gain_two, vis_in_w, vis_out_w, txt_in_w, txt_out_w = (
        lax.all_gather(gain_ffn, "dp", axis=0, tiled=True),
        lax.all_gather(vis_in, "dp", axis=0, tiled=True),
        lax.all_gather(vis_out, "dp", axis=1, tiled=True),
        lax.all_gather(txt_in, "dp", axis=0, tiled=True),
        lax.all_gather(txt_out, "dp", axis=1, tiled=True),
    )
    gain_one = gain_one.astype(jnp.float32)
    gain_two = gain_two.astype(jnp.float32)
    head_local = query_w.shape[1] // HEAD_DIM
    score_scale = HEAD_DIM ** (-0.5)
    position = jnp.arange(seq_len, dtype=jnp.int32)
    live = (position[None, :] < PATCHES) | (position[None, :] - PATCHES < caption_lengths[:, None])
    valid_rows = live.astype(jnp.float32)
    mask_col = valid_rows.reshape(-1, 1)
    key_live = valid_rows[:, None, None, :] > 0.5

    def own_rows(values):
        return lax.dynamic_slice_in_dim(values, row_start, half_rows, 0)

    inputs = tokens.astype(jnp.float32)
    normed_one, inverse_one = norm_parts(inputs)
    first_in = (normed_one * gain_one).astype(jnp.bfloat16)

    def project(weight):
        return (
            matmul(first_in, weight)
            .astype(jnp.bfloat16)
            .reshape(pair_count, seq_len, head_local, HEAD_DIM)
        )

    queries = project(query_w)
    keys_all = project(key_w)
    values_all = project(value_w)

    def score_block():
        raw = (
            jnp.einsum("pqhe,pkhe->phqk", queries, keys_all, preferred_element_type=jnp.float32)
            * score_scale
        )
        return jnp.where(key_live, raw, -1e30)

    scores = score_block()
    top = jnp.max(scores, axis=-1, keepdims=True)
    weights = jnp.exp(scores - top)
    total = jnp.sum(weights, axis=-1, keepdims=True)
    probs = (weights / total).astype(jnp.bfloat16)
    log_total = top + jnp.log(total)
    context = jnp.einsum("phqk,pkhe->pqhe", probs, values_all, preferred_element_type=jnp.float32)
    context = context.astype(jnp.bfloat16).reshape(-1, head_local * HEAD_DIM)
    attn_terms = matmul(context, out_w)
    attended_own = lax.psum_scatter(
        attn_terms.astype(jnp.bfloat16), "tensor", scatter_dimension=0, tiled=True
    ).astype(jnp.float32)
    mask_own = own_rows(mask_col)
    middle_own = own_rows(inputs) + mask_own * attended_own
    normed_two, inverse_two = norm_parts(middle_own)
    second_own = (normed_two * gain_two).astype(jnp.bfloat16)
    grid = lax.all_gather(second_own, "tensor", axis=0, tiled=True).reshape(
        pair_count, seq_len, width
    )
    image_rows = grid[:, :PATCHES].reshape(-1, width)
    text_rows = grid[:, PATCHES:].reshape(-1, width)
    image_pre, image_hidden, image_part = expert_forward(image_rows, vis_in_w, vis_out_w)
    text_pre, text_hidden, text_part = expert_forward(text_rows, txt_in_w, txt_out_w)
    image_own, text_own = (
        lax.psum_scatter(
            image_part.astype(jnp.bfloat16), "tensor", scatter_dimension=0, tiled=True
        ).astype(jnp.float32),
        lax.psum_scatter(
            text_part.astype(jnp.bfloat16), "tensor", scatter_dimension=0, tiled=True
        ).astype(jnp.float32),
    )
    branch_own = join_experts(image_own, text_own, half_pairs, width)
    output_own = (middle_own + mask_own * branch_own).astype(jnp.bfloat16)
    upstream = cotangent.astype(jnp.float32)
    grad_branch = (upstream * mask_col).astype(jnp.bfloat16).reshape(pair_count, seq_len, width)
    image_grads = expert_backward(
        image_rows,
        image_pre,
        image_hidden,
        grad_branch[:, :PATCHES].reshape(-1, width),
        vis_in_w,
        vis_out_w,
    )
    text_grads = expert_backward(
        text_rows,
        text_pre,
        text_hidden,
        grad_branch[:, PATCHES:].reshape(-1, width),
        txt_in_w,
        txt_out_w,
    )
    back_image_own, back_text_own = (
        lax.psum_scatter(
            image_grads[2].astype(jnp.bfloat16), "tensor", scatter_dimension=0, tiled=True
        ).astype(jnp.float32),
        lax.psum_scatter(
            text_grads[2].astype(jnp.bfloat16), "tensor", scatter_dimension=0, tiled=True
        ).astype(jnp.float32),
    )
    grad_second_own = join_experts(back_image_own, back_text_own, half_pairs, width)
    grad_norm_own, gain_part = norm_back(grad_second_own, normed_two, inverse_two, gain_two)
    grad_middle_own = own_rows(upstream) + grad_norm_own
    output_wide, grad_middle, gain_parts = (
        lax.all_gather(
            output_own.astype(jnp.float32).astype(jnp.bfloat16), "tensor", axis=0, tiled=True
        ).astype(jnp.float32),
        lax.all_gather(grad_middle_own.astype(jnp.bfloat16), "tensor", axis=0, tiled=True).astype(
            grad_middle_own.dtype
        ),
        lax.all_gather(gain_part.astype(jnp.bfloat16), "tensor", axis=0, tiled=True).astype(
            gain_part.dtype
        ),
    )
    output = output_wide.astype(jnp.bfloat16)
    grad_gain_two = jnp.sum(gain_parts.reshape(-1, width), axis=0)
    grad_attended = (grad_middle * mask_col).astype(jnp.bfloat16)
    grad_out_w = matmul_tn(context, grad_attended)
    grad_context = (
        matmul_nt(grad_attended, out_w)
        .astype(jnp.bfloat16)
        .reshape(pair_count, seq_len, head_local, HEAD_DIM)
    )
    scores_again = score_block()
    probs_exact = jnp.exp(scores_again - log_total)
    grad_probs = jnp.einsum(
        "pqhe,pkhe->phqk", grad_context, values_all, preferred_element_type=jnp.float32
    )
    inner = jnp.sum(grad_probs * probs_exact, axis=-1, keepdims=True)
    grad_scores = (probs_exact * (grad_probs - inner)).astype(jnp.bfloat16)
    grad_values = jnp.einsum(
        "phqk,pqhe->pkhe", probs, grad_context, preferred_element_type=jnp.float32
    )
    grad_values = grad_values.astype(jnp.bfloat16).reshape(-1, head_local * HEAD_DIM)
    grad_queries = (
        jnp.einsum("phqk,pkhe->pqhe", grad_scores, keys_all, preferred_element_type=jnp.float32)
        * score_scale
    )
    grad_queries = grad_queries.astype(jnp.bfloat16).reshape(-1, head_local * HEAD_DIM)
    grad_keys = (
        jnp.einsum("phqk,pqhe->pkhe", grad_scores, queries, preferred_element_type=jnp.float32)
        * score_scale
    )
    grad_keys = grad_keys.astype(jnp.bfloat16).reshape(-1, head_local * HEAD_DIM)
    grad_query_w = matmul_tn(first_in, grad_queries)
    grad_key_w = matmul_tn(first_in, grad_keys)
    grad_value_w = matmul_tn(first_in, grad_values)
    first_part = (
        matmul_nt(grad_queries, query_w)
        + matmul_nt(grad_keys, key_w)
        + matmul_nt(grad_values, value_w)
    )
    grad_first = lax.psum(first_part.astype(jnp.bfloat16), "tensor").astype(jnp.float32)
    grad_norm_one, grad_gain_one = norm_back(grad_first, normed_one, inverse_one, gain_one)
    grad_inputs = grad_middle + grad_norm_one
    attn_sent = (
        lax.psum_scatter(grad_gain_one, "dp", scatter_dimension=0, tiled=True),
        lax.psum_scatter(grad_query_w, "dp", scatter_dimension=0, tiled=True),
        lax.psum_scatter(grad_key_w, "dp", scatter_dimension=0, tiled=True),
        lax.psum_scatter(grad_value_w, "dp", scatter_dimension=0, tiled=True),
        lax.psum_scatter(grad_out_w, "dp", scatter_dimension=1, tiled=True),
    )
    final_expert = (
        lax.psum_scatter(grad_gain_two, "dp", scatter_dimension=0, tiled=True),
        lax.psum_scatter(image_grads[0], "dp", scatter_dimension=0, tiled=True),
        lax.psum_scatter(image_grads[1], "dp", scatter_dimension=1, tiled=True),
        lax.psum_scatter(text_grads[0], "dp", scatter_dimension=0, tiled=True),
        lax.psum_scatter(text_grads[1], "dp", scatter_dimension=1, tiled=True),
    )
    return (
        output,
        grad_inputs,
        attn_sent[0],
        attn_sent[1],
        attn_sent[2],
        attn_sent[3],
        attn_sent[4],
        final_expert[0],
        final_expert[1],
        final_expert[2],
        final_expert[3],
        final_expert[4],
    )


def solution(mesh):
    def local(tokens, lengths, gain, w_query, *rest):
        ring = mesh.shape["dp"] // 2
        fits = (
            mesh.shape["tensor"] == 2
            and ring == 8
            and lengths.shape[0] == 2
            and w_query.shape[0] % 16 == 0
        )
        layer = fused_layer if fits else plain_layer
        return layer(tokens, lengths, gain, w_query, *rest)

    return jax.shard_map(
        local,
        mesh=mesh,
        in_specs=(
            P("dp", None),
            P("dp"),
            P("dp"),
            P("dp", "tensor"),
            P("dp", "tensor"),
            P("dp", "tensor"),
            P("tensor", "dp"),
            P("dp"),
            P("dp", "tensor"),
            P("tensor", "dp"),
            P("dp", "tensor"),
            P("tensor", "dp"),
            P("dp", None),
        ),
        out_specs=(
            P("dp", None),
            P("dp", None),
            P("dp"),
            P("dp", "tensor"),
            P("dp", "tensor"),
            P("dp", "tensor"),
            P("tensor", "dp"),
            P("dp"),
            P("dp", "tensor"),
            P("tensor", "dp"),
            P("dp", "tensor"),
            P("tensor", "dp"),
        ),
        check_vma=False,
    )
```

```python
import functools
import math
import types

import jax
import jax.numpy as jnp
from jax import lax
from jax.experimental import pallas as pl
from jax.experimental.pallas import tpu as pltpu
from jax.sharding import PartitionSpec as P

HEAD_DIM = 64
PATCHES = 197
CAPTION = 40
VIS = 208
TXT = 48
SEQ = VIS + TXT

MESH = pl.DeviceIdType.MESH
HBM = "_hbm"
BF = jnp.bfloat16
F32 = jnp.float32

ATT, TIN, TOUT, VIN, VOUT = range(5)

epsilon = 1e-05
inv_root_two = 1.0 / math.sqrt(2.0)
inv_root_tau = 1.0 / math.sqrt(2.0 * math.pi)


def mm(left, right):
    return jnp.dot(left, right, preferred_element_type=F32)


def mm_nt(left, right):
    return lax.dot_general(left, right, (((1,), (1,)), ((), ())), preferred_element_type=F32)


def mm_tn(left, right):
    return lax.dot_general(left, right, (((0,), (0,)), ((), ())), preferred_element_type=F32)


def normalize(values):
    center = values - jnp.mean(values, axis=-1, keepdims=True)
    spread = jnp.mean(center * center, axis=-1, keepdims=True)
    inverse = lax.rsqrt(spread + epsilon)
    return center * inverse, inverse


def normalize_back(grad_normed, normed, inverse):
    return inverse * (
        grad_normed
        - jnp.mean(grad_normed, axis=-1, keepdims=True)
        - normed * jnp.mean(grad_normed * normed, axis=-1, keepdims=True)
    )


def unit(size):
    rows = lax.broadcasted_iota(jnp.int32, (size, size), 0)
    return (rows == lax.broadcasted_iota(jnp.int32, (size, size), 1)).astype(F32).astype(BF)


def column(ref):
    size = ref.shape[1]
    return jnp.sum(unit(size).astype(F32) * ref[...].astype(F32), axis=1, keepdims=True)


def layer_kernel(n, names, *refs):
    R = types.SimpleNamespace(**dict(zip(names, refs)))
    R.pb, R.pf, R.ga, R.rf, R.rb, R.n2 = R.pg, R.pa, R.x4, R.ra, R.rg, R.n1
    R.gqkv, R.xsg, R.xrg = R.n2, R.xs, R.xr
    S, G, PART, LAND = R.shard, R.gathered, R.part, R.land
    OUT, GW, GG = R.padded_out, R.gw, R.gg
    width = G.shape[2]
    own = width // (2 * n)
    span = width // 4
    heads = span // HEAD_DIM

    x = lax.axis_index("tensor")
    d = lax.axis_index("dp")
    c = lax.rem(d, 2)
    other = 1 - c
    chip = d // 2
    y, z = lax.rem(chip, 2), chip // 2
    r = z + y * (n - 1 - 2 * z)
    half = n // 2

    def chip_at(pos):
        pos = lax.rem(pos + 2 * n, n)
        upper = pos // half
        return 2 * (pos + upper * (n - 1 - 2 * pos)) + upper

    mate = {"dp": d + 1 - 2 * c}
    across = {"tensor": 1 - x}
    diagonal = {"dp": d + 1 - 2 * c, "tensor": 1 - x}
    ahead = {"dp": 2 * chip_at(r + 1) + c}
    behind = {"dp": 2 * chip_at(r - 1) + c}
    way = (ahead, behind)

    def rows_at(pos):
        return pl.ds(pl.multiple_of(2 * own * chip_at(pos), 16), 2 * own)

    my_rows = pl.ds(pl.multiple_of(own * d, 16), own)

    def fetch(slot, source, target):
        copy = pltpu.make_async_copy(source, target, R.local.at[slot])
        copy.start()
        return copy

    fetched = [
        fetch(0, R.tokens_hbm, R.tokens),
        fetch(1, R.txt_in_hbm, R.txt_in),
        fetch(2, R.txt_out_hbm, R.txt_out),
        fetch(3, R.vis_in_hbm, R.vis_in),
        fetch(4, R.vis_out_hbm, R.vis_out),
        fetch(5, R.cotangent_hbm, R.cotangent),
    ]

    barrier = pltpu.get_barrier_semaphore()
    for device in (mate, across, diagonal, ahead, behind):
        pl.semaphore_signal(barrier, inc=1, device_id=device, device_id_type=MESH)

    mine, theirs = pl.multiple_of(2 * c, 2), pl.multiple_of(2 * other, 2)
    pair_own = 2 * c + x
    pair_across = 2 * c + 1 - x

    started = []
    counter = [0]

    def remote(source, target, device):
        index = counter[0]
        counter[0] += 1
        return pltpu.make_async_remote_copy(
            src_ref=source,
            dst_ref=target,
            send_sem=R.sent.at[index],
            recv_sem=R.came.at[index],
            device_id=device,
            device_id_type=MESH,
        )

    def start(source, target, device):
        copy = remote(source, target, device)
        copy.start()
        started.append(copy)
        return copy

    def sent(copy):
        copy.wait_send()
        started[:] = [one for one in started if one is not copy]

    near, far = (ATT, 0, width // 2), (ATT, width // 2, width // 2)
    parts = [near, far] + [(k, 0, width) for k in (TIN, TOUT, VIN, VOUT)]
    tin, tout, vin, vout = parts[2:]
    longest = half

    def hops(part, side):
        return half if (parts.index(part) + side) % 2 == 0 else n - 1 - half

    def ring_index(part, side, s):
        return (parts.index(part) * 2 + side) * longest + s

    def view(ref, part, rows):
        k, first, count = part
        return ref.at[k, rows, pl.ds(first, count)]

    sum_base = len(parts) * 2 * longest

    def gather_copy(part, side, s, pos):
        block = view(G, part, rows_at(pos))
        i = ring_index(part, side, s)
        return pltpu.make_async_remote_copy(
            src_ref=block,
            dst_ref=block,
            send_sem=R.ring_sent.at[i],
            recv_sem=R.ring_came.at[i],
            device_id=way[side],
            device_id_type=MESH,
        )

    def first_copy(part, side, core, pos):
        rows = pl.ds(pl.multiple_of(2 * own * chip_at(pos) + own * core, 16), own)
        block = view(G, part, rows)
        i = 2 * sum_base + 4 * parts.index(part) + 2 * side + core
        return pltpu.make_async_remote_copy(
            src_ref=block,
            dst_ref=block,
            send_sem=R.ring_sent.at[i],
            recv_sem=R.ring_came.at[i],
            device_id=way[side],
            device_id_type=MESH,
        )

    def gather_first(core):
        for part in (near, far):
            for side in range(2):
                first_copy(part, side, core, r).start()

    def gather(part, s):
        for side in range(2):
            pos = r - s if side == 0 else r + s
            if s == 1 and part in (near, far):
                for core in range(2):
                    first_copy(part, side, core, pos).wait_recv()
            elif 0 < s <= hops(part, side):
                gather_copy(part, side, s - 1, pos).wait_recv()
            if s < hops(part, side):
                gather_copy(part, side, s, pos).start()

    def landed(part, side, s):
        k, first, count = part
        return LAND.at[k, side * hops(part, 0) + s, :, pl.ds(first, count)]

    def sum_copy(part, side, s, source):
        i = sum_base + ring_index(part, side, s)
        return pltpu.make_async_remote_copy(
            src_ref=source,
            dst_ref=landed(part, side, s),
            send_sem=R.ring_sent.at[i],
            recv_sem=R.ring_came.at[i],
            device_id=way[side],
            device_id_type=MESH,
        )

    def pass_sum(part, s):
        for side in range(2):
            reach = hops(part, side)
            if s >= reach:
                continue
            pos = r + (reach - s) if side == 0 else r - (reach - s)
            term = view(PART, part, rows_at(pos))
            if s == 0:
                source = term
            else:
                source = landed(part, side, s - 1)
                sum_copy(part, side, s - 1, source).wait_recv()
                source[...] = (source[...].astype(F32) + term[...].astype(F32)).astype(BF)
            sum_copy(part, side, s, source).start()

    finals = []
    row_sums = [[], []]

    def end_sum(*group):
        for part in group:
            k, first, count = part
            ends = []
            for side in range(2):
                end = landed(part, side, hops(part, side) - 1)
                sum_copy(part, side, hops(part, side) - 1, end).wait_recv()
                ends.append(end)
            cols = slice(first, first + count)
            counted = min(3 * span - first, count) if k == ATT else count

            def total(core):
                rows = pl.ds(pl.multiple_of(own * core, 16), own)
                chip_rows = pl.ds(pl.multiple_of(2 * own * chip + own * core, 16), own)
                block = (
                    ends[0][rows, :].astype(F32)
                    + ends[1][rows, :].astype(F32)
                    + PART[k, chip_rows, cols].astype(F32)
                )
                if k in (ATT, TIN, VIN):
                    weighted = G[k, chip_rows, cols].astype(F32)[:, :counted] * block[:, :counted]
                    total = jnp.sum(weighted, axis=-1, keepdims=True)
                    row_sums[0 if core is c else 1].append((k, total))
                return block

            R.give[k, :, cols] = total(other)
            finals.append(
                start(R.give.at[k, :, pl.ds(first, count)], GW.at[k, c, :, pl.ds(first, count)], mate)
            )
            GW[k, c, :, cols] = total(c)

    def shard_part(k, value):
        for core in range(2):
            S[k, core] = value(core).astype(BF)

    gain_one, gain_two = column(R.gain_attn), column(R.gain_ffn)

    def attention_part(core):
        cols = slice(core * span, (core + 1) * span)
        return jnp.concatenate(
            [
                R.w_query[:, cols].astype(F32) * (gain_one * HEAD_DIM**-0.5),
                R.w_key[:, cols].astype(F32) * gain_one,
                R.w_value[:, cols].astype(F32) * gain_one,
                R.w_out[:, cols].astype(F32),
            ],
            axis=1,
        )

    def half_of(ref, core):
        return ref[:, core * width : (core + 1) * width].astype(F32) * gain_two

    def turned_half(ref, core):
        return ref[:, core * width : (core + 1) * width]

    lengths = R.lengths

    def live(t, slots):
        return (slots < PATCHES) | ((slots >= VIS) & (slots < VIS + lengths[t]))

    def live_rows(t, j, count=64):
        slots = lax.broadcasted_iota(jnp.int32, (count, 1), 0) + j * count
        return live(t, slots).astype(F32)

    row_count = R.tokens.shape[0]

    def placed(t, slots, rows, kept):
        source = t * (PATCHES + CAPTION) + slots - (slots >= VIS).astype(jnp.int32) * (VIS - PATCHES)
        return ((rows == source) & kept).astype(F32).astype(BF)

    def chooser(t, only_live):
        slots = lax.broadcasted_iota(jnp.int32, (SEQ, row_count), 0)
        rows = lax.broadcasted_iota(jnp.int32, (SEQ, row_count), 1)
        filled = (slots < PATCHES) | ((slots >= VIS) & (slots < VIS + CAPTION))
        return placed(t, slots, rows, live(t, slots) if only_live else filled)

    shard_part(ATT, attention_part)
    G[ATT, my_rows, :] = S[ATT, c]
    for t in range(2):
        R.lens[t] = jnp.full((8, 128), lengths[t], jnp.int32).astype(F32)
    pl.semaphore_wait(barrier, 5)
    shard_a = start(S.at[pl.ds(0, 1), other], G.at[pl.ds(0, 1), my_rows, :], mate)
    gather_first(c)
    send_lens = start(R.lens, R.lens4.at[pl.ds(mine, 2)], mate)
    fetched[0].wait()
    for t in range(2):
        R.x4[2 * c + t] = mm(chooser(t, False), R.tokens[...]).astype(BF)
        R.lens4[2 * c + t] = R.lens[t]
    send_x = start(R.x4.at[pl.ds(mine, 2)], R.x4.at[pl.ds(mine, 2)], mate)
    shard_a.wait_recv()
    gather_first(other)
    for copy in fetched[1:]:
        copy.wait()

    shard_part(TIN, functools.partial(half_of, R.txt_in))
    shard_part(TOUT, functools.partial(turned_half, R.txt_out))
    shard_part(VIN, functools.partial(half_of, R.vis_in))
    shard_part(VOUT, functools.partial(turned_half, R.vis_out))
    shard_b = start(S.at[pl.ds(1, 4), other], G.at[pl.ds(1, 4), my_rows, :], mate)
    for k in (TIN, TOUT, VIN, VOUT):
        G[k, my_rows, :] = S[k, c]
    gather(near, 1)
    for t in range(2):
        R.gz[2 * c + t] = mm(chooser(t, True), R.cotangent[...]).astype(BF)
        if t == 0:
            gather(far, 1)
    send_gz = start(R.gz.at[pl.ds(mine, 2)], R.gz.at[pl.ds(mine, 2)], mate)
    R.dy[...] = mm(chooser(x, False), R.cotangent[...]).astype(BF)
    for t in range(2):
        R.x[t] = R.x4[2 * c + t]
    shard_b.wait_recv()
    gather(tin, 0)
    gather(near, 2)
    send_x.wait_recv()

    for i in range(4):

        @pl.loop(0, SEQ // 64)
        def _(j, i=i):
            rows = pl.ds(pl.multiple_of(j * 64, 64), 64)
            normed, _ = normalize(R.x4[i, rows, :].astype(F32))
            R.n1[i, rows, :] = normed.astype(BF)

        R.n1t[:, i * SEQ : (i + 1) * SEQ] = R.n1[i].T
        if i == 0:
            gather(far, 2)
        if i == 1:
            gather(tout, 0)
            gather(near, 3)
        if i == 2:
            gather(far, 3)
            gather(vin, 0)
            gather(vout, 0)
    send_gz.wait_recv()
    send_lens.wait_recv()
    gather(near, 4)
    gather(far, 4)

    R.wo[...] = G[ATT][:, 3 * span :]

    @pl.loop(0, 4)
    def _(i):
        projected = mm(R.n1[i], G[ATT][:, : 3 * span]).astype(BF)
        R.q[i] = projected[:, :span]
        R.k[i] = projected[:, span : 2 * span]
        R.v[i] = projected[:, 2 * span :]

    lane = lax.broadcasted_iota(jnp.int32, (1, span), 1) // HEAD_DIM

    def only(head, values):
        return values * (lane == head).astype(F32).astype(BF)

    def head_rows(values, head):
        return values[head * HEAD_DIM : (head + 1) * HEAD_DIM, :]

    order = []
    for j in range(4):
        core = other if j < 2 else c
        turn = 1 - x if j % 2 == 0 else x
        order.append((turn, 2 * core + turn))
    attn_mate = [remote(R.pa.at[i], R.ra.at[turn], mate) for turn, i in order[:2]]
    cross_a = remote(R.xs, R.xr, across)

    for j, (turn, i) in enumerate(order):
        q, k, v = R.q[i], R.k[i], R.v[i]
        turned_v = v.T
        slots = lax.broadcasted_iota(jnp.int32, (SEQ, 1), 0)
        caption = (slots - VIS).astype(F32) < R.lens4[i][:1, :1]
        bias = jnp.where((slots < PATCHES) | ((slots >= VIS) & caption), 0.0, -1e30)
        contexts = []
        for h in range(heads):
            scores = mm_nt(only(h, k), q) + bias
            top = jnp.max(scores, axis=0, keepdims=True)
            weights = jnp.exp(scores - top)
            total = jnp.sum(weights, axis=0, keepdims=True)
            probs = (weights * (1.0 / total)).astype(BF)
            R.probs[i * heads + h] = probs
            contexts.append(mm(head_rows(turned_v, h), probs))
        contexts = jnp.concatenate(contexts, axis=0)
        R.ct[:, pl.ds(pl.multiple_of(i * SEQ, SEQ), SEQ)] = contexts.astype(BF)
        context = contexts.T.astype(BF)
        R.pa[i] = mm_nt(context, R.wo[...]).astype(BF)
        if j < 2:
            attn_mate[j].start()
        if j == 2:
            attn_mate[0].wait_recv()
            R.xs[...] = (R.pa[pair_across].astype(F32) + R.ra[1 - x].astype(F32)).astype(BF)
            cross_a.start()
        if j == 0:
            gather(tin, 1)
        if j == 1:
            gather(tout, 1)
        if j == 3:
            gather(tin, 2)
            gather(tout, 2)

    for copy in attn_mate:
        copy.wait_send()
    attn_mate[1].wait_recv()

    @pl.loop(0, width // 256)
    def _(j):
        cols = pl.ds(pl.multiple_of(j * 256, 256), 256)
        R.gzvt[cols, :] = R.gz[:, :VIS, cols].reshape(4 * VIS, 256).T
        R.gztt[cols, :] = R.gz[:, VIS:, cols].reshape(4 * TXT, 256).T

    gather(vin, 1)
    cross_a.wait_recv()

    @pl.loop(0, SEQ // 64)
    def _(j):
        rows = pl.ds(pl.multiple_of(j * 64, 64), 64)
        attended = (
            R.pa[pair_own, rows, :].astype(F32)
            + R.ra[x, rows, :].astype(F32)
            + R.xr[rows, :].astype(F32)
        )
        middle = R.x[x, rows, :].astype(F32) + live_rows(x, j) * attended
        R.y1[rows, :] = middle
        normed, _ = normalize(middle)
        R.n2[pair_own, rows, :] = normed.astype(BF)

    block = R.n2.at[pair_own]
    to_across = start(block, block, across)
    to_mate = start(block, block, mate)
    gather(vout, 1)
    gather(tin, 3)
    gather(tout, 3)
    to_across.wait_recv()
    block = R.n2.at[pair_across]
    passed = start(block, block, mate)
    gather(vin, 2)
    gather(vout, 2)
    gather(tin, 4)
    gather(tout, 4)
    to_mate.wait_recv()
    passed.wait_recv()

    def expert(pairs, low, high, w_in, w_out, h_ref, gu_ref, j):
        first, count = pairs
        per = high - low
        total_rows = count * per
        cols = slice(j * 256, (j + 1) * 256)
        inside = slice(first, first + count)
        R.u[:total_rows, :] = mm(
            R.n2[inside, low:high, :].reshape(total_rows, width), G[w_in, :, cols]
        )
        R.gh[:total_rows, :] = mm(
            R.gz[inside, low:high, :].reshape(total_rows, width), G[w_out, :, cols]
        )
        step = min(total_rows, VIS)

        @pl.loop(0, 2 * (total_rows // step))
        def _(i):
            lanes = lax.rem(i, 2) * 128
            rows = pl.ds(pl.multiple_of(i // 2 * step, 16), step)
            into = pl.ds(pl.multiple_of(first * per + i // 2 * step, 16), step)
            side = pl.ds(pl.multiple_of(lanes, 128), 128)
            pre = R.u[rows, side]
            cumulative = 0.5 * (1.0 + lax.erf(pre * inv_root_two))
            density = jnp.exp(-0.5 * pre * pre) * inv_root_tau
            onto = pl.ds(pl.multiple_of(j * 256 + lanes, 128), 128)
            h_ref[into, onto] = (pre * cumulative).astype(BF)
            gu_ref[into, onto] = (R.gh[rows, side] * (cumulative + pre * density)).astype(BF)

    def weight_grad(k, turned, ref, j):
        cols = slice(j * 256, (j + 1) * 256)
        PART[k, :, cols] = mm(turned, ref[:, cols]).astype(BF)

    tiles = range(width // 256)
    for j in tiles:
        expert((0, 4), VIS, SEQ, TIN, TOUT, R.ht, R.gut, j)
    gather(vin, 3)
    for j in tiles:
        weight_grad(TOUT, R.gztt[...], R.ht, j)

    @pl.loop(0, width // 256)
    def _(j):
        cols = pl.ds(pl.multiple_of(j * 256, 256), 256)
        R.n2vt[cols, :] = R.n2[:, :VIS, cols].reshape(4 * VIS, 256).T
        R.n2tt[cols, :] = R.n2[:, VIS:, cols].reshape(4 * TXT, 256).T

    gather(vout, 3)
    for j in tiles:
        weight_grad(TIN, R.n2tt[...], R.gut, j)
    pass_sum(tout, 0)
    pass_sum(tin, 0)
    gather(vin, 4)
    gather(vout, 4)

    def terms(target, hv, ht, w_vis, w_txt, m):
        vis_rows = slice(2 * m * VIS, 2 * (m + 1) * VIS)
        txt_rows = slice(2 * m * TXT, 2 * (m + 1) * TXT)
        vis_part = mm_nt(hv[vis_rows, :], G[w_vis]).astype(BF)
        target[2 * m : 2 * m + 2, :VIS, :] = vis_part.reshape(2, VIS, width)
        txt_part = mm_nt(ht[txt_rows, :], G[w_txt]).astype(BF)
        target[2 * m : 2 * m + 2, VIS:, :] = txt_part.reshape(2, TXT, width)

    mate_g = remote(R.pg.at[pl.ds(theirs, 2)], R.rg, mate)
    cross_g = remote(R.xsg, R.xrg, across)
    gy_across = remote(R.gy.at[x], R.gy.at[x], across)
    gy_mate = remote(R.ga.at[pair_own], R.ga.at[pair_own], mate)
    gy_passed = remote(R.ga.at[pair_across], R.ga.at[pair_across], mate)
    started.extend([cross_g, gy_across, gy_mate, gy_passed])

    def image_terms(m):
        terms(R.pg, R.guv, R.gut, VIN, TIN, m)
        pl.when(c != m)(mate_g.start)

    def sum_cores(m):
        @pl.when(c == m)
        def _():
            mate_g.wait_recv()
            R.xsg[...] = (R.pg[pair_across].astype(F32) + R.rg[1 - x].astype(F32)).astype(BF)
            cross_g.start()

    def middle_back(m):
        @pl.when(c == m)
        def _():
            cross_g.wait_recv()

            @pl.loop(0, SEQ // 64)
            def _(j):
                rows = pl.ds(pl.multiple_of(j * 64, 64), 64)
                grad_normed = (
                    R.pg[pair_own, rows, :].astype(F32)
                    + R.rg[x, rows, :].astype(F32)
                    + R.xrg[rows, :].astype(F32)
                )
                normed, inverse = normalize(R.y1[rows, :])
                grad = R.dy[rows, :].astype(F32) + normalize_back(grad_normed, normed, inverse)
                R.gy[x, rows, :] = grad.astype(BF)
                R.ga[pair_own, rows, :] = (grad * live_rows(x, j)).astype(BF)

            gy_across.start()
            gy_mate.start()

    def middle_pass(m):
        @pl.when(c == m)
        def _():
            gy_across.wait_recv()

            @pl.loop(0, SEQ // 64)
            def _(j):
                rows = pl.ds(pl.multiple_of(j * 64, 64), 64)
                R.ga[pair_across, rows, :] = (
                    R.gy[1 - x, rows, :].astype(F32) * live_rows(1 - x, j)
                ).astype(BF)

            gy_passed.start()

    def middle_came(m):
        @pl.when(c != m)
        def _():
            gy_mate.wait_recv()
            gy_passed.wait_recv()

    sent(send_x)
    cross_a.wait_send()
    for j in tiles:
        expert((0, 2), 0, VIS, VIN, VOUT, R.hv, R.guv, j)
        if j == 1:
            pass_sum(tout, 1)
    image_terms(0)
    pass_sum(tin, 1)
    expert((2, 2), 0, VIS, VIN, VOUT, R.hv, R.guv, 0)
    sum_cores(0)
    expert((2, 2), 0, VIS, VIN, VOUT, R.hv, R.guv, 1)
    pass_sum(tout, 2)
    for j in tiles[2:]:
        expert((2, 2), 0, VIS, VIN, VOUT, R.hv, R.guv, j)
    image_terms(1)
    for copy in (to_across, to_mate, passed):
        sent(copy)
    sum_cores(1)
    pass_sum(tin, 2)

    for m in range(2):
        terms(R.pf, R.hv, R.ht, VOUT, TOUT, m)
    mate_f = start(R.pf.at[pl.ds(theirs, 2)], R.rf, mate)
    cross_f = remote(R.xsf, R.xrf, across)
    started.append(cross_f)
    middle_back(0)
    for j in tiles:
        weight_grad(VOUT, R.gzvt[...], R.hv, j)
    pass_sum(tout, 3)
    pass_sum(vout, 0)
    for j in tiles:
        weight_grad(VIN, R.n2vt[...], R.guv, j)
    pass_sum(tin, 3)
    pass_sum(vin, 0)
    middle_pass(0)
    middle_back(1)
    mate_f.wait_recv()
    R.xsf[...] = (R.pf[pair_across].astype(F32) + R.rf[1 - x].astype(F32)).astype(BF)
    R.fown[...] = (R.pf[pair_own].astype(F32) + R.rf[x].astype(F32)).astype(BF)
    cross_f.start()
    end_sum(tout, tin)
    pass_sum(vout, 1)
    mate_g.wait_send()
    middle_came(0)

    back_mate = [remote(R.pb.at[theirs + t], R.rb.at[t], mate) for t in range(2)]
    back_cross = [remote(R.xsb.at[t], R.xrb.at[t], across) for t in range(2)]
    started.extend(back_mate + back_cross)

    def attention_back(m, t):
        i = 2 * m + t
        grad_context = mm(R.ga[i], R.wo[...]).astype(BF)
        q, k, v = R.q[i], R.k[i], R.v[i]
        turned_k = k.T
        grad_q = []
        grad_k = jnp.zeros((SEQ, span), F32)
        grad_v = jnp.zeros((SEQ, span), F32)
        for h in range(heads):
            probs = R.probs[i * heads + h]
            grad_probs = mm_nt(only(h, v), grad_context)
            exact = probs.astype(F32)
            inner = jnp.sum(grad_probs * exact, axis=0, keepdims=True)
            grad_scores = (exact * (grad_probs - inner)).astype(BF)
            grad_q.append(mm(head_rows(turned_k, h), grad_scores))
            grad_k += mm(grad_scores, only(h, q))
            grad_v += mm(probs, only(h, grad_context))
        grad_q = jnp.concatenate(grad_q, axis=0).T
        joined = jnp.concatenate([grad_q, grad_k, grad_v], axis=1).astype(BF)
        R.gqkv[i, :, : 3 * span] = joined
        R.pb[i] = mm_nt(joined, G[ATT][:, : 3 * span]).astype(BF)
        pl.when(c != m)(back_mate[t].start)

    def back_sum(m, t):
        @pl.when(c == m)
        def _():
            back_mate[t].wait_recv()
            R.xsb[t] = (R.pb[2 * m + t].astype(F32) + R.rb[t].astype(F32)).astype(BF)
            back_cross[t].start()

    attention_back(0, 0)
    middle_pass(1)
    pass_sum(vin, 1)
    attention_back(0, 1)
    back_sum(0, 0)

    cross_f.wait_recv()

    @pl.loop(0, SEQ // 64)
    def _(j):
        rows = pl.ds(pl.multiple_of(j * 64, 64), 64)
        branch = R.fown[rows, :].astype(F32) + R.xrf[rows, :].astype(F32)
        OUT[x, rows, :] = (R.y1[rows, :] + live_rows(x, j) * branch).astype(BF)

    out_across = start(OUT.at[x], OUT.at[x], across)
    pass_sum(vout, 2)
    middle_came(1)
    attention_back(1, 0)
    back_sum(0, 1)
    pass_sum(vin, 2)
    attention_back(1, 1)
    back_sum(1, 0)
    pass_sum(vout, 3)
    pass_sum(vin, 3)

    lanes = width // 2

    @pl.loop(0, width // 256)
    def _(j):
        rows = pl.ds(pl.multiple_of(j * 256, 256), 256)
        grad_v = mm(R.n1t[rows, :], R.gqkv[:, :, lanes : 3 * span].reshape(4 * SEQ, span))
        grad_o = mm(R.ct[...], R.ga[:, :, rows].reshape(4 * SEQ, 256)).T
        PART[ATT, rows, lanes:] = jnp.concatenate([grad_v, grad_o], axis=1).astype(BF)

    pass_sum(far, 0)

    @pl.loop(0, width // 256)
    def _(j):
        rows = pl.ds(pl.multiple_of(j * 256, 256), 256)
        grads = mm(R.n1t[rows, :], R.gqkv[:, :, :lanes].reshape(4 * SEQ, lanes))
        PART[ATT, rows, :lanes] = grads.astype(BF)

    pass_sum(near, 0)
    back_sum(1, 1)

    def input_back(m, t):
        @pl.when(c == m)
        def _():
            back_cross[t].wait_recv()

            @pl.loop(0, SEQ // 64)
            def _(j):
                rows = pl.ds(pl.multiple_of(j * 64, 64), 64)
                grad_normed = R.xsb[t, rows, :].astype(F32) + R.xrb[t, rows, :].astype(F32)
                normed, inverse = normalize(R.x[t, rows, :].astype(F32))
                grad = R.gy[t, rows, :].astype(F32) + normalize_back(grad_normed, normed, inverse)
                high = grad.astype(BF)
                rows = pl.ds(pl.multiple_of(t * SEQ + j * 64, 64), 64)
                R.hv[rows, :] = high
                R.guv[rows, :] = (grad - high.astype(F32)).astype(BF)

    pass_sum(far, 1)
    input_back(0, 0)
    pass_sum(near, 1)
    input_back(0, 1)
    end_sum(vout, vin)
    pass_sum(far, 2)
    pass_sum(near, 2)

    leaving = []

    def leave(slot, source, target):
        leaving.append(fetch(slot, source, target))

    slots = lax.broadcasted_iota(jnp.int32, (row_count, 2 * SEQ), 1)
    rows = lax.broadcasted_iota(jnp.int32, (row_count, 2 * SEQ), 0)
    turn = slots // SEQ
    back = placed(turn, slots - turn * SEQ, rows, slots >= 0)
    out_across.wait_recv()
    R.out_tokens[...] = mm(back, OUT[...].reshape(2 * SEQ, width)).astype(BF)
    leave(6, R.out_tokens, R.out_tokens_hbm)
    for copy in finals:
        copy.wait_recv()
    finals.clear()
    leave(7, GW.at[pl.ds(1, 4)], R.gw_hbm.at[pl.ds(1, 4)])
    pass_sum(far, 3)
    pass_sum(near, 3)
    input_back(1, 0)
    input_back(1, 1)
    R.grad_tokens[...] = mm(back, R.hv[: 2 * SEQ, :]) + mm(back, R.guv[: 2 * SEQ, :])
    leave(8, R.grad_tokens, R.grad_tokens_hbm)
    end_sum(far, near)

    first_lane = lax.broadcasted_iota(jnp.int32, (own, 128), 1) == 0
    for place in range(2):
        attn = sum(total for k, total in row_sums[place] if k == ATT)
        experts = sum(total for k, total in row_sums[place] if k != ATT)
        R.gs[place] = jnp.where(first_lane, attn, experts)
    peers = [
        start(R.gs.at[place], R.gr.at[slot], device)
        for slot, (place, device) in enumerate(((1, mate), (0, across), (1, diagonal)))
    ]
    for copy in finals + peers:
        copy.wait_recv()
    leave(9, GW.at[pl.ds(0, 1)], R.gw_hbm.at[pl.ds(0, 1)])
    GG[...] = (R.gs[0] + R.gr[1]) + (R.gr[0] + R.gr[2])

    for copy in started:
        copy.wait_send()
    for copy in leaving:
        copy.wait()
    for part in parts:
        for side in range(2):
            for s in range(hops(part, side)):
                if s == 0 and part in (near, far):
                    for core in range(2):
                        first_copy(part, side, core, r).wait_send()
                else:
                    gather_copy(part, side, s, r).wait_send()
                sum_copy(part, side, s, landed(part, side, s)).wait_send()


def finish_kernel(n_results, out, gtok, gw_hbm, gg, gain_attn, gain_ffn, *rest):
    results, scratch = rest[:n_results], rest[n_results:]
    buffers, (out_buffer, gtok_buffer, gw, came, gone) = scratch[:n_results], scratch[n_results:]
    arriving = [
        pltpu.make_async_copy(source, target, came.at[slot])
        for slot, (source, target) in enumerate(((gw_hbm, gw), (out, out_buffer), (gtok, gtok_buffer)))
    ]
    for copy in arriving:
        copy.start()
    width = gw.shape[3]
    own = gw.shape[2]
    span = width // 4
    gain_one, gain_two = column(gain_attn), column(gain_ffn)
    square = unit(own).astype(F32)
    leaving = []

    def leave(slot, source):
        copy = pltpu.make_async_copy(source, results[slot], gone.at[slot])
        copy.start()
        leaving.append(copy)

    def both(part):
        cols = slice(part * span, (part + 1) * span)
        return jnp.concatenate([gw[ATT, core][:, cols] for core in range(2)], axis=1)

    def put(slot, value):
        buffers[slot][...] = value
        leave(slot, buffers[slot])

    put(2, jnp.sum(square * (gg[:, :1] / gain_one), axis=0, keepdims=True))
    put(7, jnp.sum(square * (gg[:, 1:2] / gain_two), axis=0, keepdims=True))
    arriving[0].wait()
    for slot, k, scale in ((8, VIN, gain_two), (9, VOUT, 1.0), (10, TIN, gain_two), (11, TOUT, 1.0)):
        put(slot, jnp.concatenate([gw[k, 0], gw[k, 1]], axis=1) * scale)
    put(3, both(0) * (gain_one * HEAD_DIM**-0.5))
    put(4, both(1) * gain_one)
    put(5, both(2) * gain_one)
    put(6, both(3))
    arriving[1].wait()
    leave(0, out_buffer)
    arriving[2].wait()
    leave(1, gtok_buffer)
    for copy in leaving:
        copy.wait()


def fused_layer(
    tokens,
    caption_lengths,
    gain_attn,
    w_query,
    w_key,
    w_value,
    w_out,
    gain_ffn,
    vis_in,
    vis_out,
    txt_in,
    txt_out,
    cotangent,
):
    n = lax.axis_size("dp") // 2
    own = w_query.shape[0]
    row_count, width = tokens.shape
    span = width // 4
    heads = span // HEAD_DIM
    gain_one, gain_two = gain_attn.reshape(1, own), gain_ffn.reshape(1, own)

    rows = 4 * SEQ
    scratch = dict(
        tokens=pltpu.VMEM((row_count, width), BF),
        cotangent=pltpu.VMEM((row_count, width), BF),
        txt_in=pltpu.VMEM((own, 2 * width), BF),
        txt_out=pltpu.VMEM((own, 2 * width), BF),
        vis_in=pltpu.VMEM((own, 2 * width), BF),
        vis_out=pltpu.VMEM((own, 2 * width), BF),
        out_tokens=pltpu.VMEM((row_count, width), BF),
        grad_tokens=pltpu.VMEM((row_count, width), F32),
        gw=pltpu.VMEM((5, 2, own, width), F32),
        local=pltpu.SemaphoreType.DMA((10,)),
        shard=pltpu.VMEM((5, 2, own, width), BF),
        lens=pltpu.VMEM((2, 8, 128), F32),
        x=pltpu.VMEM((2, SEQ, width), BF),
        dy=pltpu.VMEM((SEQ, width), BF),
        padded_out=pltpu.VMEM((2, SEQ, width), BF),
        gathered=pltpu.VMEM((5, width, width), BF),
        part=pltpu.VMEM((5, width, width), BF),
        land=pltpu.VMEM((5, n - 1, 2 * own, width), BF),
        give=pltpu.VMEM((5, own, width), F32),
        x4=pltpu.VMEM((4, SEQ, width), BF),
        lens4=pltpu.VMEM((4, 8, 128), F32),
        n1=pltpu.VMEM((4, SEQ, width), BF),
        n1t=pltpu.VMEM((width, rows), BF),
        gz=pltpu.VMEM((4, SEQ, width), BF),
        gzvt=pltpu.VMEM((width, 4 * VIS), BF),
        ct=pltpu.VMEM((span, rows), BF),
        fown=pltpu.VMEM((SEQ, width), BF),
        gztt=pltpu.VMEM((width, 4 * TXT), BF),
        wo=pltpu.VMEM((width, span), BF),
        q=pltpu.VMEM((4, SEQ, span), BF),
        k=pltpu.VMEM((4, SEQ, span), BF),
        v=pltpu.VMEM((4, SEQ, span), BF),
        probs=pltpu.VMEM((4 * heads, SEQ, SEQ), BF),
        pa=pltpu.VMEM((4, SEQ, width), BF),
        ra=pltpu.VMEM((2, SEQ, width), BF),
        xs=pltpu.VMEM((SEQ, width), BF),
        xr=pltpu.VMEM((SEQ, width), BF),
        y1=pltpu.VMEM((SEQ, width), F32),
        n2vt=pltpu.VMEM((width, 4 * VIS), BF),
        n2tt=pltpu.VMEM((width, 4 * TXT), BF),
        u=pltpu.VMEM((4 * VIS, 256), F32),
        gh=pltpu.VMEM((4 * VIS, 256), F32),
        hv=pltpu.VMEM((4 * VIS, width), BF),
        guv=pltpu.VMEM((4 * VIS, width), BF),
        ht=pltpu.VMEM((4 * TXT, width), BF),
        gut=pltpu.VMEM((4 * TXT, width), BF),
        pg=pltpu.VMEM((4, SEQ, width), BF),
        rg=pltpu.VMEM((2, SEQ, width), BF),
        gy=pltpu.VMEM((2, SEQ, width), BF),
        xsf=pltpu.VMEM((SEQ, width), BF),
        xrf=pltpu.VMEM((SEQ, width), BF),
        xsb=pltpu.VMEM((2, SEQ, width), BF),
        xrb=pltpu.VMEM((2, SEQ, width), BF),
        gs=pltpu.VMEM((2, own, 128), F32),
        gr=pltpu.VMEM((3, own, 128), F32),
        sent=pltpu.SemaphoreType.DMA((40,)),
        came=pltpu.SemaphoreType.DMA((40,)),
        ring_sent=pltpu.SemaphoreType.DMA((6 * 2 * (n // 2) * 2 + 8,)),
        ring_came=pltpu.SemaphoreType.DMA((6 * 2 * (n // 2) * 2 + 8,)),
    )
    inputs = dict(
        lengths=caption_lengths,
        tokens_hbm=tokens,
        cotangent_hbm=cotangent,
        gain_attn=gain_one,
        gain_ffn=gain_two,
        w_query=w_query,
        w_key=w_key,
        w_value=w_value,
        w_out=w_out.T,
        vis_in_hbm=vis_in,
        vis_out_hbm=vis_out.T,
        txt_in_hbm=txt_in,
        txt_out_hbm=txt_out.T,
    )
    results = dict(
        out_tokens_hbm=jax.ShapeDtypeStruct((row_count, width), BF),
        grad_tokens_hbm=jax.ShapeDtypeStruct((row_count, width), F32),
        gw_hbm=jax.ShapeDtypeStruct((5, 2, own, width), F32),
        gg=jax.ShapeDtypeStruct((own, 128), F32),
    )
    vmem, hbm = pl.BlockSpec(memory_space=pltpu.VMEM), pl.BlockSpec(memory_space=pl.ANY)
    names = tuple(inputs) + tuple(results) + tuple(scratch)
    out, gtok, gw, gg = pl.pallas_call(
        functools.partial(layer_kernel, n, names),
        out_shape=tuple(results.values()),
        in_specs=[pl.BlockSpec(memory_space=pltpu.SMEM)] + [hbm if k.endswith(HBM) else vmem for k in names[1 : len(inputs)]],
        out_specs=[hbm if k.endswith(HBM) else vmem for k in results],
        scratch_shapes=list(scratch.values()),
        compiler_params=pltpu.CompilerParams(
            collective_id=0, has_side_effects=True, vmem_limit_bytes=60 * 2**20
        ),
    )(*inputs.values())

    shapes = (
        jax.ShapeDtypeStruct((row_count, width), BF),
        jax.ShapeDtypeStruct((row_count, width), F32),
        jax.ShapeDtypeStruct((1, own), F32),
        jax.ShapeDtypeStruct((own, 2 * span), F32),
        jax.ShapeDtypeStruct((own, 2 * span), F32),
        jax.ShapeDtypeStruct((own, 2 * span), F32),
        jax.ShapeDtypeStruct((own, 2 * span), F32),
        jax.ShapeDtypeStruct((1, own), F32),
        jax.ShapeDtypeStruct((own, 2 * width), F32),
        jax.ShapeDtypeStruct((own, 2 * width), F32),
        jax.ShapeDtypeStruct((own, 2 * width), F32),
        jax.ShapeDtypeStruct((own, 2 * width), F32),
    )
    buffers = [pltpu.VMEM(one.shape if slot > 1 else (8, 128), F32) for slot, one in enumerate(shapes)]
    final = pl.pallas_call(
        functools.partial(finish_kernel, len(shapes)),
        out_shape=shapes,
        in_specs=[hbm] * 3 + [vmem] * 3,
        out_specs=[hbm] * len(shapes),
        scratch_shapes=buffers
        + [
            pltpu.VMEM((row_count, width), BF),
            pltpu.VMEM((row_count, width), F32),
            pltpu.VMEM((5, 2, own, width), F32),
            pltpu.SemaphoreType.DMA((3,)),
            pltpu.SemaphoreType.DMA((len(shapes),)),
        ],
        compiler_params=pltpu.CompilerParams(vmem_limit_bytes=60 * 2**20),
    )(out, gtok, gw, gg, gain_one, gain_two)
    final = list(final)
    final[2] = final[2].reshape(own)
    final[7] = final[7].reshape(own)
    for turned in (6, 9, 11):
        final[turned] = final[turned].T
    return tuple(final)


def norm_parts(values):
    center = values - jnp.mean(values, axis=-1, keepdims=True)
    spread = jnp.mean(center * center, axis=-1, keepdims=True)
    inverse = lax.rsqrt(spread + epsilon)
    return (center * inverse, inverse)


def norm_back(grad_out, normed, inverse, gain):
    grad_normed = grad_out * gain
    grad_gain = jnp.sum(grad_out * normed, axis=0)
    inner = (
        grad_normed
        - jnp.mean(grad_normed, axis=-1, keepdims=True)
        - normed * jnp.mean(grad_normed * normed, axis=-1, keepdims=True)
    )
    return (inverse * inner, grad_gain)


def matmul(left, right):
    return jnp.dot(left, right, preferred_element_type=jnp.float32)


def matmul_tn(left, right):
    return lax.dot_general(
        left, right, (((0,), (0,)), ((), ())), preferred_element_type=jnp.float32
    )


def matmul_nt(left, right):
    return lax.dot_general(
        left, right, (((1,), (1,)), ((), ())), preferred_element_type=jnp.float32
    )


def gelu_slope(pre):
    cumulative = 0.5 * (1.0 + lax.erf(pre * inv_root_two))
    density = jnp.exp(-0.5 * pre * pre) * inv_root_tau
    return cumulative + pre * density


def expert_forward(rows, weight_in, weight_out):
    pre = matmul(rows, weight_in)
    hidden = jax.nn.gelu(pre, approximate=False).astype(jnp.bfloat16)
    return (pre, hidden, matmul(hidden, weight_out))


def expert_backward(rows, pre, hidden, grad_out, weight_in, weight_out):
    grad_weight_out = matmul_tn(hidden, grad_out)
    grad_hidden = matmul_nt(grad_out, weight_out)
    grad_pre = (grad_hidden * gelu_slope(pre)).astype(jnp.bfloat16)
    return (matmul_tn(rows, grad_pre), grad_weight_out, matmul_nt(grad_pre, weight_in))


def join_experts(image_rows, text_rows, pair_count, width):
    joined = jnp.concatenate(
        [
            image_rows.reshape(pair_count, PATCHES, width),
            text_rows.reshape(pair_count, CAPTION, width),
        ],
        axis=1,
    )
    return joined.reshape(-1, width)


def plain_layer(
    tokens,
    caption_lengths,
    gain_attn,
    w_query,
    w_key,
    w_value,
    w_out,
    gain_ffn,
    vis_in,
    vis_out,
    txt_in,
    txt_out,
    cotangent,
):
    seq_len = PATCHES + CAPTION
    width = tokens.shape[1]
    pair_count = tokens.shape[0] // seq_len
    half_pairs = pair_count // lax.axis_size("tensor")
    half_rows = half_pairs * seq_len
    row_start = lax.axis_index("tensor") * half_rows
    gain_one, query_w, key_w, value_w, out_w = (
        lax.all_gather(gain_attn, "dp", axis=0, tiled=True),
        lax.all_gather(w_query, "dp", axis=0, tiled=True),
        lax.all_gather(w_key, "dp", axis=0, tiled=True),
        lax.all_gather(w_value, "dp", axis=0, tiled=True),
        lax.all_gather(w_out, "dp", axis=1, tiled=True),
    )
    gain_two, vis_in_w, vis_out_w, txt_in_w, txt_out_w = (
        lax.all_gather(gain_ffn, "dp", axis=0, tiled=True),
        lax.all_gather(vis_in, "dp", axis=0, tiled=True),
        lax.all_gather(vis_out, "dp", axis=1, tiled=True),
        lax.all_gather(txt_in, "dp", axis=0, tiled=True),
        lax.all_gather(txt_out, "dp", axis=1, tiled=True),
    )
    gain_one = gain_one.astype(jnp.float32)
    gain_two = gain_two.astype(jnp.float32)
    head_local = query_w.shape[1] // HEAD_DIM
    score_scale = HEAD_DIM ** (-0.5)
    position = jnp.arange(seq_len, dtype=jnp.int32)
    live = (position[None, :] < PATCHES) | (position[None, :] - PATCHES < caption_lengths[:, None])
    valid_rows = live.astype(jnp.float32)
    mask_col = valid_rows.reshape(-1, 1)
    key_live = valid_rows[:, None, None, :] > 0.5

    def own_rows(values):
        return lax.dynamic_slice_in_dim(values, row_start, half_rows, 0)

    inputs = tokens.astype(jnp.float32)
    normed_one, inverse_one = norm_parts(inputs)
    first_in = (normed_one * gain_one).astype(jnp.bfloat16)

    def project(weight):
        return (
            matmul(first_in, weight)
            .astype(jnp.bfloat16)
            .reshape(pair_count, seq_len, head_local, HEAD_DIM)
        )

    queries = project(query_w)
    keys_all = project(key_w)
    values_all = project(value_w)

    def score_block():
        raw = (
            jnp.einsum("pqhe,pkhe->phqk", queries, keys_all, preferred_element_type=jnp.float32)
            * score_scale
        )
        return jnp.where(key_live, raw, -1e30)

    scores = score_block()
    top = jnp.max(scores, axis=-1, keepdims=True)
    weights = jnp.exp(scores - top)
    total = jnp.sum(weights, axis=-1, keepdims=True)
    probs = (weights / total).astype(jnp.bfloat16)
    log_total = top + jnp.log(total)
    context = jnp.einsum("phqk,pkhe->pqhe", probs, values_all, preferred_element_type=jnp.float32)
    context = context.astype(jnp.bfloat16).reshape(-1, head_local * HEAD_DIM)
    attn_terms = matmul(context, out_w)
    attended_own = lax.psum_scatter(
        attn_terms.astype(jnp.bfloat16), "tensor", scatter_dimension=0, tiled=True
    ).astype(jnp.float32)
    mask_own = own_rows(mask_col)
    middle_own = own_rows(inputs) + mask_own * attended_own
    normed_two, inverse_two = norm_parts(middle_own)
    second_own = (normed_two * gain_two).astype(jnp.bfloat16)
    grid = lax.all_gather(second_own, "tensor", axis=0, tiled=True).reshape(
        pair_count, seq_len, width
    )
    image_rows = grid[:, :PATCHES].reshape(-1, width)
    text_rows = grid[:, PATCHES:].reshape(-1, width)
    image_pre, image_hidden, image_part = expert_forward(image_rows, vis_in_w, vis_out_w)
    text_pre, text_hidden, text_part = expert_forward(text_rows, txt_in_w, txt_out_w)
    image_own, text_own = (
        lax.psum_scatter(
            image_part.astype(jnp.bfloat16), "tensor", scatter_dimension=0, tiled=True
        ).astype(jnp.float32),
        lax.psum_scatter(
            text_part.astype(jnp.bfloat16), "tensor", scatter_dimension=0, tiled=True
        ).astype(jnp.float32),
    )
    branch_own = join_experts(image_own, text_own, half_pairs, width)
    output_own = (middle_own + mask_own * branch_own).astype(jnp.bfloat16)
    upstream = cotangent.astype(jnp.float32)
    grad_branch = (upstream * mask_col).astype(jnp.bfloat16).reshape(pair_count, seq_len, width)
    image_grads = expert_backward(
        image_rows,
        image_pre,
        image_hidden,
        grad_branch[:, :PATCHES].reshape(-1, width),
        vis_in_w,
        vis_out_w,
    )
    text_grads = expert_backward(
        text_rows,
        text_pre,
        text_hidden,
        grad_branch[:, PATCHES:].reshape(-1, width),
        txt_in_w,
        txt_out_w,
    )
    back_image_own, back_text_own = (
        lax.psum_scatter(
            image_grads[2].astype(jnp.bfloat16), "tensor", scatter_dimension=0, tiled=True
        ).astype(jnp.float32),
        lax.psum_scatter(
            text_grads[2].astype(jnp.bfloat16), "tensor", scatter_dimension=0, tiled=True
        ).astype(jnp.float32),
    )
    grad_second_own = join_experts(back_image_own, back_text_own, half_pairs, width)
    grad_norm_own, gain_part = norm_back(grad_second_own, normed_two, inverse_two, gain_two)
    grad_middle_own = own_rows(upstream) + grad_norm_own
    output_wide, grad_middle, gain_parts = (
        lax.all_gather(
            output_own.astype(jnp.float32).astype(jnp.bfloat16), "tensor", axis=0, tiled=True
        ).astype(jnp.float32),
        lax.all_gather(grad_middle_own.astype(jnp.bfloat16), "tensor", axis=0, tiled=True).astype(
            grad_middle_own.dtype
        ),
        lax.all_gather(gain_part.astype(jnp.bfloat16), "tensor", axis=0, tiled=True).astype(
            gain_part.dtype
        ),
    )
    output = output_wide.astype(jnp.bfloat16)
    grad_gain_two = jnp.sum(gain_parts.reshape(-1, width), axis=0)
    grad_attended = (grad_middle * mask_col).astype(jnp.bfloat16)
    grad_out_w = matmul_tn(context, grad_attended)
    grad_context = (
        matmul_nt(grad_attended, out_w)
        .astype(jnp.bfloat16)
        .reshape(pair_count, seq_len, head_local, HEAD_DIM)
    )
    scores_again = score_block()
    probs_exact = jnp.exp(scores_again - log_total)
    grad_probs = jnp.einsum(
        "pqhe,pkhe->phqk", grad_context, values_all, preferred_element_type=jnp.float32
    )
    inner = jnp.sum(grad_probs * probs_exact, axis=-1, keepdims=True)
    grad_scores = (probs_exact * (grad_probs - inner)).astype(jnp.bfloat16)
    grad_values = jnp.einsum(
        "phqk,pqhe->pkhe", probs, grad_context, preferred_element_type=jnp.float32
    )
    grad_values = grad_values.astype(jnp.bfloat16).reshape(-1, head_local * HEAD_DIM)
    grad_queries = (
        jnp.einsum("phqk,pkhe->pqhe", grad_scores, keys_all, preferred_element_type=jnp.float32)
        * score_scale
    )
    grad_queries = grad_queries.astype(jnp.bfloat16).reshape(-1, head_local * HEAD_DIM)
    grad_keys = (
        jnp.einsum("phqk,pqhe->pkhe", grad_scores, queries, preferred_element_type=jnp.float32)
        * score_scale
    )
    grad_keys = grad_keys.astype(jnp.bfloat16).reshape(-1, head_local * HEAD_DIM)
    grad_query_w = matmul_tn(first_in, grad_queries)
    grad_key_w = matmul_tn(first_in, grad_keys)
    grad_value_w = matmul_tn(first_in, grad_values)
    first_part = (
        matmul_nt(grad_queries, query_w)
        + matmul_nt(grad_keys, key_w)
        + matmul_nt(grad_values, value_w)
    )
    grad_first = lax.psum(first_part.astype(jnp.bfloat16), "tensor").astype(jnp.float32)
    grad_norm_one, grad_gain_one = norm_back(grad_first, normed_one, inverse_one, gain_one)
    grad_inputs = grad_middle + grad_norm_one
    attn_sent = (
        lax.psum_scatter(grad_gain_one, "dp", scatter_dimension=0, tiled=True),
        lax.psum_scatter(grad_query_w, "dp", scatter_dimension=0, tiled=True),
        lax.psum_scatter(grad_key_w, "dp", scatter_dimension=0, tiled=True),
        lax.psum_scatter(grad_value_w, "dp", scatter_dimension=0, tiled=True),
        lax.psum_scatter(grad_out_w, "dp", scatter_dimension=1, tiled=True),
    )
    final_expert = (
        lax.psum_scatter(grad_gain_two, "dp", scatter_dimension=0, tiled=True),
        lax.psum_scatter(image_grads[0], "dp", scatter_dimension=0, tiled=True),
        lax.psum_scatter(image_grads[1], "dp", scatter_dimension=1, tiled=True),
        lax.psum_scatter(text_grads[0], "dp", scatter_dimension=0, tiled=True),
        lax.psum_scatter(text_grads[1], "dp", scatter_dimension=1, tiled=True),
    )
    return (
        output,
        grad_inputs,
        attn_sent[0],
        attn_sent[1],
        attn_sent[2],
        attn_sent[3],
        attn_sent[4],
        final_expert[0],
        final_expert[1],
        final_expert[2],
        final_expert[3],
        final_expert[4],
    )


def solution(mesh):
    def local(tokens, lengths, gain, w_query, *rest):
        ring = mesh.shape["dp"] // 2
        fits = (
            mesh.shape["tensor"] == 2
            and ring == 8
            and lengths.shape[0] == 2
            and w_query.shape[0] % 16 == 0
        )
        layer = fused_layer if fits else plain_layer
        return layer(tokens, lengths, gain, w_query, *rest)

    return jax.shard_map(
        local,
        mesh=mesh,
        in_specs=(
            P("dp", None),
            P("dp"),
            P("dp"),
            P("dp", "tensor"),
            P("dp", "tensor"),
            P("dp", "tensor"),
            P("tensor", "dp"),
            P("dp"),
            P("dp", "tensor"),
            P("tensor", "dp"),
            P("dp", "tensor"),
            P("tensor", "dp"),
            P("dp", None),
        ),
        out_specs=(
            P("dp", None),
            P("dp", None),
            P("dp"),
            P("dp", "tensor"),
            P("dp", "tensor"),
            P("dp", "tensor"),
            P("tensor", "dp"),
            P("dp"),
            P("dp", "tensor"),
            P("tensor", "dp"),
            P("dp", "tensor"),
            P("tensor", "dp"),
        ),
        check_vma=False,
    )
```

```python
import functools
import math
import types

import jax
import jax.numpy as jnp
from jax import lax
from jax.experimental import pallas as pl
from jax.experimental.pallas import tpu as pltpu
from jax.sharding import PartitionSpec as P

HEAD_DIM = 64
PATCHES = 197
CAPTION = 40
VIS = 208
TXT = 48
SEQ = VIS + TXT

MESH = pl.DeviceIdType.MESH
HBM = "_hbm"
BF = jnp.bfloat16
F32 = jnp.float32

ATT, TIN, TOUT, VIN, VOUT = range(5)

epsilon = 1e-05
inv_root_two = 1.0 / math.sqrt(2.0)
inv_root_tau = 1.0 / math.sqrt(2.0 * math.pi)


def mm(left, right):
    return jnp.dot(left, right, preferred_element_type=F32)


def mm_nt(left, right):
    return lax.dot_general(left, right, (((1,), (1,)), ((), ())), preferred_element_type=F32)


def mm_tn(left, right):
    return lax.dot_general(left, right, (((0,), (0,)), ((), ())), preferred_element_type=F32)


def normalize(values):
    center = values - jnp.mean(values, axis=-1, keepdims=True)
    spread = jnp.mean(center * center, axis=-1, keepdims=True)
    inverse = lax.rsqrt(spread + epsilon)
    return center * inverse, inverse


def normalize_back(grad_normed, normed, inverse):
    return inverse * (
        grad_normed
        - jnp.mean(grad_normed, axis=-1, keepdims=True)
        - normed * jnp.mean(grad_normed * normed, axis=-1, keepdims=True)
    )


def unit(size):
    rows = lax.broadcasted_iota(jnp.int32, (size, size), 0)
    return (rows == lax.broadcasted_iota(jnp.int32, (size, size), 1)).astype(F32).astype(BF)


def column(ref):
    size = ref.shape[1]
    return jnp.sum(unit(size).astype(F32) * ref[...].astype(F32), axis=1, keepdims=True)


def layer_kernel(n, names, *refs):
    R = types.SimpleNamespace(**dict(zip(names, refs)))
    R.pb, R.pf, R.ga, R.rf, R.rb, R.n2 = R.pg, R.pa, R.x4, R.ra, R.rg, R.n1
    R.gqkv, R.xsg, R.xrg = R.n2, R.xs, R.xr
    S, G, PART, LAND = R.shard, R.gathered, R.part, R.land
    OUT, GW, GG = R.padded_out, R.gw, R.gg
    width = G.shape[2]
    own = width // (2 * n)
    span = width // 4
    heads = span // HEAD_DIM

    x = lax.axis_index("tensor")
    d = lax.axis_index("dp")
    c = lax.rem(d, 2)
    other = 1 - c
    chip = d // 2
    y, z = lax.rem(chip, 2), chip // 2
    r = z + y * (n - 1 - 2 * z)
    half = n // 2

    def chip_at(pos):
        pos = lax.rem(pos + 2 * n, n)
        upper = pos // half
        return 2 * (pos + upper * (n - 1 - 2 * pos)) + upper

    near_mate = d + 1 - 2 * c
    mate, across, diagonal = (near_mate, x), (d, 1 - x), (near_mate, 1 - x)
    ahead = (2 * chip_at(r + 1) + c, x)
    behind = (2 * chip_at(r - 1) + c, x)
    way = (ahead, behind)

    offsets = {hop: 2 * own * chip_at(r + hop) for hop in range(-half, half + 1)}

    def rows_at(hop):
        return pl.ds(pl.multiple_of(offsets[hop], 16), 2 * own)

    my_rows = pl.ds(pl.multiple_of(own * d, 16), own)

    def fetch(slot, source, target):
        copy = pltpu.make_async_copy(source, target, R.local.at[slot])
        copy.start()
        return copy

    fetched = [
        fetch(0, R.tokens_hbm, R.tokens),
        fetch(1, R.txt_in_hbm, R.txt_in),
        fetch(2, R.txt_out_hbm, R.txt_out),
        fetch(3, R.vis_in_hbm, R.vis_in),
        fetch(4, R.vis_out_hbm, R.vis_out),
        fetch(5, R.cotangent_hbm, R.cotangent),
    ]

    barrier = pltpu.get_barrier_semaphore()
    for device in (mate, across, diagonal, ahead, behind):
        pl.semaphore_signal(barrier, inc=1, device_id=device, device_id_type=MESH)

    mine, theirs = pl.multiple_of(2 * c, 2), pl.multiple_of(2 * other, 2)
    pair_own = 2 * c + x
    pair_across = 2 * c + 1 - x

    started = []
    counter = [0]

    def remote(source, target, device):
        index = counter[0]
        counter[0] += 1
        return pltpu.make_async_remote_copy(
            src_ref=source,
            dst_ref=target,
            send_sem=R.sent.at[index],
            recv_sem=R.came.at[index],
            device_id=device,
            device_id_type=MESH,
        )

    def start(source, target, device):
        copy = remote(source, target, device)
        copy.start()
        started.append(copy)
        return copy

    def sent(copy):
        copy.wait_send()
        started[:] = [one for one in started if one is not copy]

    near, far = (ATT, 0, width // 2), (ATT, width // 2, width // 2)
    parts = [near, far] + [(k, 0, width) for k in (TIN, TOUT, VIN, VOUT)]
    tin, tout, vin, vout = parts[2:]
    longest = half

    def hops(part, side):
        return half if (parts.index(part) + side) % 2 == 0 else n - 1 - half

    def ring_index(part, side, s):
        return (parts.index(part) * 2 + side) * longest + s

    def view(ref, part, rows):
        k, first, count = part
        return ref.at[k, rows, pl.ds(first, count)]

    sum_base = len(parts) * 2 * longest

    def gather_copy(part, side, s, pos):
        block = view(G, part, rows_at(pos))
        i = ring_index(part, side, s)
        return pltpu.make_async_remote_copy(
            src_ref=block,
            dst_ref=block,
            send_sem=R.ring_sent.at[part[0]],
            recv_sem=R.ring_came.at[i],
            device_id=way[side],
            device_id_type=MESH,
        )

    def gather(part, s):
        for side in range(2):
            pos = -s if side == 0 else s
            if 0 < s <= hops(part, side):
                gather_copy(part, side, s - 1, pos).wait_recv()
            if s < hops(part, side):
                gather_copy(part, side, s, pos).start()

    def landed(part, side, s):
        k, first, count = part
        return LAND.at[k, side * hops(part, 0) + s, :, pl.ds(first, count)]

    def sum_copy(part, side, s, source):
        i = sum_base + ring_index(part, side, s)
        return pltpu.make_async_remote_copy(
            src_ref=source,
            dst_ref=landed(part, side, s),
            send_sem=R.ring_sent.at[5 + part[0]],
            recv_sem=R.ring_came.at[i],
            device_id=way[side],
            device_id_type=MESH,
        )

    def pass_sum(part, s):
        for side in range(2):
            reach = hops(part, side)
            if s >= reach:
                continue
            pos = reach - s if side == 0 else s - reach
            term = view(PART, part, rows_at(pos))
            if s == 0:
                source = term
            else:
                source = landed(part, side, s - 1)
                sum_copy(part, side, s - 1, source).wait_recv()
                source[...] = (source[...].astype(F32) + term[...].astype(F32)).astype(BF)
            sum_copy(part, side, s, source).start()

    finals = []
    row_sums = [[], []]

    def end_sum(*group):
        for part in group:
            k, first, count = part
            ends = []
            for side in range(2):
                end = landed(part, side, hops(part, side) - 1)
                sum_copy(part, side, hops(part, side) - 1, end).wait_recv()
                ends.append(end)
            cols = slice(first, first + count)
            counted = min(3 * span - first, count) if k == ATT else count

            def total(core):
                rows = pl.ds(pl.multiple_of(own * core, 16), own)
                chip_rows = pl.ds(pl.multiple_of(2 * own * chip + own * core, 16), own)
                block = (
                    ends[0][rows, :].astype(F32)
                    + ends[1][rows, :].astype(F32)
                    + PART[k, chip_rows, cols].astype(F32)
                )
                if k in (ATT, TIN, VIN):
                    weighted = G[k, chip_rows, cols].astype(F32)[:, :counted] * block[:, :counted]
                    total = jnp.sum(weighted, axis=-1, keepdims=True)
                    row_sums[0 if core is c else 1].append((k, total))
                return block

            R.give[k, :, cols] = total(other)
            finals.append(
                start(R.give.at[k, :, pl.ds(first, count)], GW.at[k, c, :, pl.ds(first, count)], mate)
            )
            GW[k, c, :, cols] = total(c)

    def shard_part(k, value):
        for core in range(2):
            S[k, core] = value(core).astype(BF)

    gain_one, gain_two = column(R.gain_attn), column(R.gain_ffn)

    def attention_part(core):
        cols = slice(core * span, (core + 1) * span)
        return jnp.concatenate(
            [
                R.w_query[:, cols].astype(F32) * (gain_one * HEAD_DIM**-0.5),
                R.w_key[:, cols].astype(F32) * gain_one,
                R.w_value[:, cols].astype(F32) * gain_one,
                R.w_out[:, cols].astype(F32),
            ],
            axis=1,
        )

    def half_of(ref, core):
        return ref[:, core * width : (core + 1) * width].astype(F32) * gain_two

    def turned_half(ref, core):
        return ref[:, core * width : (core + 1) * width]

    lengths = R.lengths

    def live(t, slots):
        return (slots < PATCHES) | ((slots >= VIS) & (slots < VIS + lengths[t]))

    def live_rows(t, j, count=64):
        slots = lax.broadcasted_iota(jnp.int32, (count, 1), 0) + j * count
        return live(t, slots).astype(F32)

    row_count = R.tokens.shape[0]

    def placed(t, slots, rows, kept):
        source = t * (PATCHES + CAPTION) + slots - (slots >= VIS).astype(jnp.int32) * (VIS - PATCHES)
        return ((rows == source) & kept).astype(F32).astype(BF)

    def chooser(t, only_live):
        slots = lax.broadcasted_iota(jnp.int32, (SEQ, row_count), 0)
        rows = lax.broadcasted_iota(jnp.int32, (SEQ, row_count), 1)
        filled = (slots < PATCHES) | ((slots >= VIS) & (slots < VIS + CAPTION))
        return placed(t, slots, rows, live(t, slots) if only_live else filled)

    shard_part(ATT, attention_part)
    G[ATT, my_rows, :] = S[ATT, c]
    for t in range(2):
        R.lens[t] = jnp.full((8, 128), lengths[t], jnp.int32).astype(F32)
    pl.semaphore_wait(barrier, 5)
    shard_a = start(S.at[pl.ds(0, 1), other], G.at[pl.ds(0, 1), my_rows, :], mate)
    send_lens = start(R.lens, R.lens4.at[pl.ds(mine, 2)], mate)
    fetched[0].wait()
    for t in range(2):
        R.x4[2 * c + t] = mm(chooser(t, False), R.tokens[...]).astype(BF)
        R.lens4[2 * c + t] = R.lens[t]
    send_x = start(R.x4.at[pl.ds(mine, 2)], R.x4.at[pl.ds(mine, 2)], mate)
    shard_a.wait_recv()
    gather(near, 0)
    gather(far, 0)
    for copy in fetched[1:]:
        copy.wait()

    shard_part(TIN, functools.partial(half_of, R.txt_in))
    shard_part(TOUT, functools.partial(turned_half, R.txt_out))
    shard_part(VIN, functools.partial(half_of, R.vis_in))
    shard_part(VOUT, functools.partial(turned_half, R.vis_out))
    shard_b = start(S.at[pl.ds(1, 4), other], G.at[pl.ds(1, 4), my_rows, :], mate)
    for k in (TIN, TOUT, VIN, VOUT):
        G[k, my_rows, :] = S[k, c]
    gather(near, 1)
    for t in range(2):
        R.gz[2 * c + t] = mm(chooser(t, True), R.cotangent[...]).astype(BF)
        if t == 0:
            gather(far, 1)
    send_gz = start(R.gz.at[pl.ds(mine, 2)], R.gz.at[pl.ds(mine, 2)], mate)
    R.dy[...] = mm(chooser(x, False), R.cotangent[...]).astype(BF)
    for t in range(2):
        R.x[t] = R.x4[2 * c + t]
    shard_b.wait_recv()
    gather(tin, 0)
    gather(near, 2)
    send_x.wait_recv()

    for i in range(4):

        @pl.loop(0, SEQ // 64)
        def _(j, i=i):
            rows = pl.ds(pl.multiple_of(j * 64, 64), 64)
            normed, _ = normalize(R.x4[i, rows, :].astype(F32))
            R.n1[i, rows, :] = normed.astype(BF)

        R.n1t[:, i * SEQ : (i + 1) * SEQ] = R.n1[i].T
        if i == 0:
            gather(far, 2)
        if i == 1:
            gather(tout, 0)
            gather(near, 3)
        if i == 2:
            gather(far, 3)
            gather(vin, 0)
            gather(vout, 0)
    send_gz.wait_recv()
    send_lens.wait_recv()
    gather(near, 4)
    gather(far, 4)

    R.wo[...] = G[ATT][:, 3 * span :]

    @pl.loop(0, 4)
    def _(i):
        projected = mm(R.n1[i], G[ATT][:, : 3 * span]).astype(BF)
        R.q[i] = projected[:, :span]
        R.k[i] = projected[:, span : 2 * span]
        R.v[i] = projected[:, 2 * span :]

    lane = lax.broadcasted_iota(jnp.int32, (1, span), 1) // HEAD_DIM

    def only(head, values):
        return values * (lane == head).astype(F32).astype(BF)

    def head_rows(values, head):
        return values[head * HEAD_DIM : (head + 1) * HEAD_DIM, :]

    order = []
    for j in range(4):
        core = other if j < 2 else c
        turn = 1 - x if j % 2 == 0 else x
        order.append((turn, 2 * core + turn))
    attn_mate = [remote(R.pa.at[i], R.ra.at[turn], mate) for turn, i in order[:2]]
    cross_a = remote(R.xs, R.xr, across)

    for j, (turn, i) in enumerate(order):
        q, k, v = R.q[i], R.k[i], R.v[i]
        turned_v = v.T
        slots = lax.broadcasted_iota(jnp.int32, (SEQ, 1), 0)
        caption = (slots - VIS).astype(F32) < R.lens4[i][:1, :1]
        bias = jnp.where((slots < PATCHES) | ((slots >= VIS) & caption), 0.0, -1e30)
        contexts = []
        for h in range(heads):
            scores = mm_nt(only(h, k), q) + bias
            top = jnp.max(scores, axis=0, keepdims=True)
            weights = jnp.exp(scores - top)
            total = jnp.sum(weights, axis=0, keepdims=True)
            probs = (weights * (1.0 / total)).astype(BF)
            R.probs[i * heads + h] = probs
            contexts.append(mm(head_rows(turned_v, h), probs))
        contexts = jnp.concatenate(contexts, axis=0)
        R.ct[:, pl.ds(pl.multiple_of(i * SEQ, SEQ), SEQ)] = contexts.astype(BF)
        context = contexts.T.astype(BF)
        R.pa[i] = mm_nt(context, R.wo[...]).astype(BF)
        if j < 2:
            attn_mate[j].start()
        if j == 2:
            attn_mate[0].wait_recv()
            R.xs[...] = (R.pa[pair_across].astype(F32) + R.ra[1 - x].astype(F32)).astype(BF)
            cross_a.start()
        if j == 0:
            gather(tin, 1)
        if j == 1:
            gather(tout, 1)
        if j == 3:
            gather(tin, 2)
            gather(tout, 2)

    for copy in attn_mate:
        copy.wait_send()
    attn_mate[1].wait_recv()

    @pl.loop(0, width // 256)
    def _(j):
        cols = pl.ds(pl.multiple_of(j * 256, 256), 256)
        R.gzvt[cols, :] = R.gz[:, :VIS, cols].reshape(4 * VIS, 256).T
        R.gztt[cols, :] = R.gz[:, VIS:, cols].reshape(4 * TXT, 256).T

    gather(vin, 1)
    cross_a.wait_recv()

    @pl.loop(0, SEQ // 64)
    def _(j):
        rows = pl.ds(pl.multiple_of(j * 64, 64), 64)
        attended = (
            R.pa[pair_own, rows, :].astype(F32)
            + R.ra[x, rows, :].astype(F32)
            + R.xr[rows, :].astype(F32)
        )
        middle = R.x[x, rows, :].astype(F32) + live_rows(x, j) * attended
        R.y1[rows, :] = middle
        normed, _ = normalize(middle)
        R.n2[pair_own, rows, :] = normed.astype(BF)

    block = R.n2.at[pair_own]
    to_across = start(block, block, across)
    to_mate = start(block, block, mate)
    gather(vout, 1)
    gather(tin, 3)
    gather(tout, 3)
    to_across.wait_recv()
    block = R.n2.at[pair_across]
    passed = start(block, block, mate)
    gather(vin, 2)
    gather(vout, 2)
    gather(tin, 4)
    gather(tout, 4)
    to_mate.wait_recv()
    passed.wait_recv()

    def expert(pairs, low, high, w_in, w_out, h_ref, gu_ref, j):
        first, count = pairs
        per = high - low
        total_rows = count * per
        cols = slice(j * 256, (j + 1) * 256)
        inside = slice(first, first + count)
        R.u[:total_rows, :] = mm(
            R.n2[inside, low:high, :].reshape(total_rows, width), G[w_in, :, cols]
        )
        R.gh[:total_rows, :] = mm(
            R.gz[inside, low:high, :].reshape(total_rows, width), G[w_out, :, cols]
        )
        step = min(total_rows, VIS)

        @pl.loop(0, 2 * (total_rows // step))
        def _(i):
            lanes = lax.rem(i, 2) * 128
            rows = pl.ds(pl.multiple_of(i // 2 * step, 16), step)
            into = pl.ds(pl.multiple_of(first * per + i // 2 * step, 16), step)
            side = pl.ds(pl.multiple_of(lanes, 128), 128)
            pre = R.u[rows, side]
            cumulative = 0.5 * (1.0 + lax.erf(pre * inv_root_two))
            density = jnp.exp(-0.5 * pre * pre) * inv_root_tau
            onto = pl.ds(pl.multiple_of(j * 256 + lanes, 128), 128)
            h_ref[into, onto] = (pre * cumulative).astype(BF)
            gu_ref[into, onto] = (R.gh[rows, side] * (cumulative + pre * density)).astype(BF)

    def weight_grad(k, turned, ref, j):
        cols = slice(j * 256, (j + 1) * 256)
        PART[k, :, cols] = mm(turned, ref[:, cols]).astype(BF)

    tiles = range(width // 256)
    for j in tiles:
        expert((0, 4), VIS, SEQ, TIN, TOUT, R.ht, R.gut, j)
    gather(vin, 3)
    for j in tiles:
        weight_grad(TOUT, R.gztt[...], R.ht, j)

    @pl.loop(0, width // 256)
    def _(j):
        cols = pl.ds(pl.multiple_of(j * 256, 256), 256)
        R.n2vt[cols, :] = R.n2[:, :VIS, cols].reshape(4 * VIS, 256).T
        R.n2tt[cols, :] = R.n2[:, VIS:, cols].reshape(4 * TXT, 256).T

    gather(vout, 3)
    for j in tiles:
        weight_grad(TIN, R.n2tt[...], R.gut, j)
    pass_sum(tout, 0)
    pass_sum(tin, 0)
    gather(vin, 4)
    gather(vout, 4)

    def terms(target, hv, ht, w_vis, w_txt, m):
        vis_rows = slice(2 * m * VIS, 2 * (m + 1) * VIS)
        txt_rows = slice(2 * m * TXT, 2 * (m + 1) * TXT)
        vis_part = mm_nt(hv[vis_rows, :], G[w_vis]).astype(BF)
        target[2 * m : 2 * m + 2, :VIS, :] = vis_part.reshape(2, VIS, width)
        txt_part = mm_nt(ht[txt_rows, :], G[w_txt]).astype(BF)
        target[2 * m : 2 * m + 2, VIS:, :] = txt_part.reshape(2, TXT, width)

    mate_g = remote(R.pg.at[pl.ds(theirs, 2)], R.rg, mate)
    cross_g = remote(R.xsg, R.xrg, across)
    gy_across = remote(R.gy.at[x], R.gy.at[x], across)
    gy_mate = remote(R.ga.at[pair_own], R.ga.at[pair_own], mate)
    gy_passed = remote(R.ga.at[pair_across], R.ga.at[pair_across], mate)
    started.extend([cross_g, gy_across, gy_mate, gy_passed])

    def image_terms(m):
        terms(R.pg, R.guv, R.gut, VIN, TIN, m)
        pl.when(c != m)(mate_g.start)

    def sum_cores(m):
        @pl.when(c == m)
        def _():
            mate_g.wait_recv()
            R.xsg[...] = (R.pg[pair_across].astype(F32) + R.rg[1 - x].astype(F32)).astype(BF)
            cross_g.start()

    def middle_back(m):
        @pl.when(c == m)
        def _():
            cross_g.wait_recv()

            @pl.loop(0, SEQ // 64)
            def _(j):
                rows = pl.ds(pl.multiple_of(j * 64, 64), 64)
                grad_normed = (
                    R.pg[pair_own, rows, :].astype(F32)
                    + R.rg[x, rows, :].astype(F32)
                    + R.xrg[rows, :].astype(F32)
                )
                normed, inverse = normalize(R.y1[rows, :])
                grad = R.dy[rows, :].astype(F32) + normalize_back(grad_normed, normed, inverse)
                R.gy[x, rows, :] = grad.astype(BF)
                R.ga[pair_own, rows, :] = (grad * live_rows(x, j)).astype(BF)

            gy_across.start()
            gy_mate.start()

    def middle_pass(m):
        @pl.when(c == m)
        def _():
            gy_across.wait_recv()

            @pl.loop(0, SEQ // 64)
            def _(j):
                rows = pl.ds(pl.multiple_of(j * 64, 64), 64)
                R.ga[pair_across, rows, :] = (
                    R.gy[1 - x, rows, :].astype(F32) * live_rows(1 - x, j)
                ).astype(BF)

            gy_passed.start()

    def middle_came(m):
        @pl.when(c != m)
        def _():
            gy_mate.wait_recv()
            gy_passed.wait_recv()

    sent(send_x)
    cross_a.wait_send()
    for j in tiles:
        expert((0, 2), 0, VIS, VIN, VOUT, R.hv, R.guv, j)
        if j == 1:
            pass_sum(tout, 1)
    image_terms(0)
    pass_sum(tin, 1)
    expert((2, 2), 0, VIS, VIN, VOUT, R.hv, R.guv, 0)
    sum_cores(0)
    expert((2, 2), 0, VIS, VIN, VOUT, R.hv, R.guv, 1)
    pass_sum(tout, 2)
    for j in tiles[2:]:
        expert((2, 2), 0, VIS, VIN, VOUT, R.hv, R.guv, j)
    image_terms(1)
    for copy in (to_across, to_mate, passed):
        sent(copy)
    sum_cores(1)
    pass_sum(tin, 2)

    weight_grad(VOUT, R.gzvt[...], R.hv, 0)
    middle_back(0)
    for j in tiles[1:]:
        weight_grad(VOUT, R.gzvt[...], R.hv, j)
    pass_sum(tout, 3)
    pass_sum(vout, 0)
    for j in tiles:
        weight_grad(VIN, R.n2vt[...], R.guv, j)
    pass_sum(tin, 3)
    pass_sum(vin, 0)

    terms(R.pf, R.hv, R.ht, VOUT, TOUT, 0)
    middle_pass(0)
    middle_back(1)
    end_sum(tout, tin)
    terms(R.pf, R.hv, R.ht, VOUT, TOUT, 1)
    mate_f = start(R.pf.at[pl.ds(theirs, 2)], R.rf, mate)
    cross_f = remote(R.xsf, R.xrf, across)
    started.append(cross_f)
    pass_sum(vout, 1)
    mate_g.wait_send()
    middle_came(0)

    back_mate = [remote(R.pb.at[theirs + t], R.rb.at[t], mate) for t in range(2)]
    back_cross = [remote(R.xsb.at[t], R.xrb.at[t], across) for t in range(2)]
    started.extend(back_mate + back_cross)

    def attention_back(m, t):
        i = 2 * m + t
        grad_context = mm(R.ga[i], R.wo[...]).astype(BF)
        q, k, v = R.q[i], R.k[i], R.v[i]
        turned_k = k.T
        grad_q = []
        grad_k = jnp.zeros((SEQ, span), F32)
        grad_v = jnp.zeros((SEQ, span), F32)
        for h in range(heads):
            probs = R.probs[i * heads + h]
            grad_probs = mm_nt(only(h, v), grad_context)
            exact = probs.astype(F32)
            inner = jnp.sum(grad_probs * exact, axis=0, keepdims=True)
            grad_scores = (exact * (grad_probs - inner)).astype(BF)
            grad_q.append(mm(head_rows(turned_k, h), grad_scores))
            grad_k += mm(grad_scores, only(h, q))
            grad_v += mm(probs, only(h, grad_context))
        grad_q = jnp.concatenate(grad_q, axis=0).T
        joined = jnp.concatenate([grad_q, grad_k, grad_v], axis=1).astype(BF)
        R.gqkv[i, :, : 3 * span] = joined
        R.pb[i] = mm_nt(joined, G[ATT][:, : 3 * span]).astype(BF)
        pl.when(c != m)(back_mate[t].start)

    def back_sum(m, t):
        @pl.when(c == m)
        def _():
            back_mate[t].wait_recv()
            R.xsb[t] = (R.pb[2 * m + t].astype(F32) + R.rb[t].astype(F32)).astype(BF)
            back_cross[t].start()

    attention_back(0, 0)
    pass_sum(vin, 1)
    mate_f.wait_recv()
    R.xsf[...] = (R.pf[pair_across].astype(F32) + R.rf[1 - x].astype(F32)).astype(BF)
    R.fown[...] = (R.pf[pair_own].astype(F32) + R.rf[x].astype(F32)).astype(BF)
    middle_pass(1)
    cross_f.start()
    attention_back(0, 1)
    back_sum(0, 0)

    pass_sum(vout, 2)
    middle_came(1)
    attention_back(1, 0)
    back_sum(0, 1)

    cross_f.wait_recv()

    @pl.loop(0, SEQ // 64)
    def _(j):
        rows = pl.ds(pl.multiple_of(j * 64, 64), 64)
        branch = R.fown[rows, :].astype(F32) + R.xrf[rows, :].astype(F32)
        OUT[x, rows, :] = (R.y1[rows, :] + live_rows(x, j) * branch).astype(BF)

    out_across = start(OUT.at[x], OUT.at[x], across)
    pass_sum(vin, 2)
    attention_back(1, 1)
    back_sum(1, 0)
    pass_sum(vout, 3)
    pass_sum(vin, 3)

    lanes = width // 2

    @pl.loop(0, width // 256)
    def _(j):
        rows = pl.ds(pl.multiple_of(j * 256, 256), 256)
        grad_v = mm(R.n1t[rows, :], R.gqkv[:, :, lanes : 3 * span].reshape(4 * SEQ, span))
        grad_o = mm(R.ct[...], R.ga[:, :, rows].reshape(4 * SEQ, 256)).T
        PART[ATT, rows, lanes:] = jnp.concatenate([grad_v, grad_o], axis=1).astype(BF)

    pass_sum(far, 0)

    @pl.loop(0, width // 256)
    def _(j):
        rows = pl.ds(pl.multiple_of(j * 256, 256), 256)
        grads = mm(R.n1t[rows, :], R.gqkv[:, :, :lanes].reshape(4 * SEQ, lanes))
        PART[ATT, rows, :lanes] = grads.astype(BF)

    pass_sum(near, 0)
    back_sum(1, 1)

    def input_back(m, t):
        @pl.when(c == m)
        def _():
            back_cross[t].wait_recv()

            @pl.loop(0, SEQ // 64)
            def _(j):
                rows = pl.ds(pl.multiple_of(j * 64, 64), 64)
                grad_normed = R.xsb[t, rows, :].astype(F32) + R.xrb[t, rows, :].astype(F32)
                normed, inverse = normalize(R.x[t, rows, :].astype(F32))
                grad = R.gy[t, rows, :].astype(F32) + normalize_back(grad_normed, normed, inverse)
                high = grad.astype(BF)
                rows = pl.ds(pl.multiple_of(t * SEQ + j * 64, 64), 64)
                R.hv[rows, :] = high
                R.guv[rows, :] = (grad - high.astype(F32)).astype(BF)

    pass_sum(far, 1)
    input_back(0, 0)
    pass_sum(near, 1)
    input_back(0, 1)
    end_sum(vout, vin)
    pass_sum(far, 2)
    pass_sum(near, 2)

    leaving = []

    def leave(slot, source, target):
        leaving.append(fetch(slot, source, target))

    slots = lax.broadcasted_iota(jnp.int32, (row_count, 2 * SEQ), 1)
    rows = lax.broadcasted_iota(jnp.int32, (row_count, 2 * SEQ), 0)
    turn = slots // SEQ
    back = placed(turn, slots - turn * SEQ, rows, slots >= 0)
    out_across.wait_recv()
    R.out_tokens[...] = mm(back, OUT[...].reshape(2 * SEQ, width)).astype(BF)
    leave(6, R.out_tokens, R.out_tokens_hbm)
    for copy in finals:
        copy.wait_recv()
    finals.clear()
    leave(7, GW.at[pl.ds(1, 4)], R.gw_hbm.at[pl.ds(1, 4)])
    pass_sum(far, 3)
    pass_sum(near, 3)
    input_back(1, 0)
    input_back(1, 1)
    R.grad_tokens[...] = mm(back, R.hv[: 2 * SEQ, :]) + mm(back, R.guv[: 2 * SEQ, :])
    leave(8, R.grad_tokens, R.grad_tokens_hbm)
    end_sum(far, near)

    first_lane = lax.broadcasted_iota(jnp.int32, (own, 128), 1) == 0
    for place in range(2):
        attn = sum(total for k, total in row_sums[place] if k == ATT)
        experts = sum(total for k, total in row_sums[place] if k != ATT)
        R.gs[place] = jnp.where(first_lane, attn, experts)
    peers = [
        start(R.gs.at[place], R.gr.at[slot], device)
        for slot, (place, device) in enumerate(((1, mate), (0, across), (1, diagonal)))
    ]
    for copy in finals + peers:
        copy.wait_recv()
    leave(9, GW.at[pl.ds(0, 1)], R.gw_hbm.at[pl.ds(0, 1)])
    GG[...] = (R.gs[0] + R.gr[1]) + (R.gr[0] + R.gr[2])

    for copy in started:
        copy.wait_send()
    for copy in leaving:
        copy.wait()
    for k in range(5):
        for semaphore in (k, 5 + k):
            pltpu.make_async_remote_copy(
                src_ref=LAND.at[k],
                dst_ref=LAND.at[k],
                send_sem=R.ring_sent.at[semaphore],
                recv_sem=R.ring_came.at[0],
                device_id=ahead,
                device_id_type=MESH,
            ).wait_send()


def finish_kernel(n_results, out, gtok, gw_hbm, gg, gain_attn, gain_ffn, *rest):
    results, scratch = rest[:n_results], rest[n_results:]
    buffers, (out_buffer, gtok_buffer, gw, came, gone) = scratch[:n_results], scratch[n_results:]
    arriving = [
        pltpu.make_async_copy(source, target, came.at[slot])
        for slot, (source, target) in enumerate(((gw_hbm, gw), (out, out_buffer), (gtok, gtok_buffer)))
    ]
    for copy in arriving:
        copy.start()
    width = gw.shape[3]
    own = gw.shape[2]
    span = width // 4
    gain_one, gain_two = column(gain_attn), column(gain_ffn)
    square = unit(own).astype(F32)
    leaving = []

    def leave(slot, source):
        copy = pltpu.make_async_copy(source, results[slot], gone.at[slot])
        copy.start()
        leaving.append(copy)

    def both(part):
        cols = slice(part * span, (part + 1) * span)
        return jnp.concatenate([gw[ATT, core][:, cols] for core in range(2)], axis=1)

    def put(slot, value):
        buffers[slot][...] = value
        leave(slot, buffers[slot])

    put(2, jnp.sum(square * (gg[:, :1] / gain_one), axis=0, keepdims=True))
    put(7, jnp.sum(square * (gg[:, 1:2] / gain_two), axis=0, keepdims=True))
    arriving[0].wait()
    for slot, k, scale in ((8, VIN, gain_two), (9, VOUT, 1.0), (10, TIN, gain_two), (11, TOUT, 1.0)):
        put(slot, jnp.concatenate([gw[k, 0], gw[k, 1]], axis=1) * scale)
    put(3, both(0) * (gain_one * HEAD_DIM**-0.5))
    put(4, both(1) * gain_one)
    put(5, both(2) * gain_one)
    put(6, both(3))
    arriving[1].wait()
    leave(0, out_buffer)
    arriving[2].wait()
    leave(1, gtok_buffer)
    for copy in leaving:
        copy.wait()


def fused_layer(
    tokens,
    caption_lengths,
    gain_attn,
    w_query,
    w_key,
    w_value,
    w_out,
    gain_ffn,
    vis_in,
    vis_out,
    txt_in,
    txt_out,
    cotangent,
):
    n = lax.axis_size("dp") // 2
    own = w_query.shape[0]
    row_count, width = tokens.shape
    span = width // 4
    heads = span // HEAD_DIM
    gain_one, gain_two = gain_attn.reshape(1, own), gain_ffn.reshape(1, own)

    rows = 4 * SEQ
    scratch = dict(
        tokens=pltpu.VMEM((row_count, width), BF),
        cotangent=pltpu.VMEM((row_count, width), BF),
        txt_in=pltpu.VMEM((own, 2 * width), BF),
        txt_out=pltpu.VMEM((own, 2 * width), BF),
        vis_in=pltpu.VMEM((own, 2 * width), BF),
        vis_out=pltpu.VMEM((own, 2 * width), BF),
        out_tokens=pltpu.VMEM((row_count, width), BF),
        grad_tokens=pltpu.VMEM((row_count, width), F32),
        gw=pltpu.VMEM((5, 2, own, width), F32),
        local=pltpu.SemaphoreType.DMA((10,)),
        shard=pltpu.VMEM((5, 2, own, width), BF),
        lens=pltpu.VMEM((2, 8, 128), F32),
        x=pltpu.VMEM((2, SEQ, width), BF),
        dy=pltpu.VMEM((SEQ, width), BF),
        padded_out=pltpu.VMEM((2, SEQ, width), BF),
        gathered=pltpu.VMEM((5, width, width), BF),
        part=pltpu.VMEM((5, width, width), BF),
        land=pltpu.VMEM((5, n - 1, 2 * own, width), BF),
        give=pltpu.VMEM((5, own, width), F32),
        x4=pltpu.VMEM((4, SEQ, width), BF),
        lens4=pltpu.VMEM((4, 8, 128), F32),
        n1=pltpu.VMEM((4, SEQ, width), BF),
        n1t=pltpu.VMEM((width, rows), BF),
        gz=pltpu.VMEM((4, SEQ, width), BF),
        gzvt=pltpu.VMEM((width, 4 * VIS), BF),
        ct=pltpu.VMEM((span, rows), BF),
        fown=pltpu.VMEM((SEQ, width), BF),
        gztt=pltpu.VMEM((width, 4 * TXT), BF),
        wo=pltpu.VMEM((width, span), BF),
        q=pltpu.VMEM((4, SEQ, span), BF),
        k=pltpu.VMEM((4, SEQ, span), BF),
        v=pltpu.VMEM((4, SEQ, span), BF),
        probs=pltpu.VMEM((4 * heads, SEQ, SEQ), BF),
        pa=pltpu.VMEM((4, SEQ, width), BF),
        ra=pltpu.VMEM((2, SEQ, width), BF),
        xs=pltpu.VMEM((SEQ, width), BF),
        xr=pltpu.VMEM((SEQ, width), BF),
        y1=pltpu.VMEM((SEQ, width), F32),
        n2vt=pltpu.VMEM((width, 4 * VIS), BF),
        n2tt=pltpu.VMEM((width, 4 * TXT), BF),
        u=pltpu.VMEM((4 * VIS, 256), F32),
        gh=pltpu.VMEM((4 * VIS, 256), F32),
        hv=pltpu.VMEM((4 * VIS, width), BF),
        guv=pltpu.VMEM((4 * VIS, width), BF),
        ht=pltpu.VMEM((4 * TXT, width), BF),
        gut=pltpu.VMEM((4 * TXT, width), BF),
        pg=pltpu.VMEM((4, SEQ, width), BF),
        rg=pltpu.VMEM((2, SEQ, width), BF),
        gy=pltpu.VMEM((2, SEQ, width), BF),
        xsf=pltpu.VMEM((SEQ, width), BF),
        xrf=pltpu.VMEM((SEQ, width), BF),
        xsb=pltpu.VMEM((2, SEQ, width), BF),
        xrb=pltpu.VMEM((2, SEQ, width), BF),
        gs=pltpu.VMEM((2, own, 128), F32),
        gr=pltpu.VMEM((3, own, 128), F32),
        sent=pltpu.SemaphoreType.DMA((40,)),
        came=pltpu.SemaphoreType.DMA((40,)),
        ring_sent=pltpu.SemaphoreType.DMA((10,)),
        ring_came=pltpu.SemaphoreType.DMA((6 * 2 * (n // 2) * 2,)),
    )
    inputs = dict(
        lengths=caption_lengths,
        tokens_hbm=tokens,
        cotangent_hbm=cotangent,
        gain_attn=gain_one,
        gain_ffn=gain_two,
        w_query=w_query,
        w_key=w_key,
        w_value=w_value,
        w_out=w_out.T,
        vis_in_hbm=vis_in,
        vis_out_hbm=vis_out.T,
        txt_in_hbm=txt_in,
        txt_out_hbm=txt_out.T,
    )
    results = dict(
        out_tokens_hbm=jax.ShapeDtypeStruct((row_count, width), BF),
        grad_tokens_hbm=jax.ShapeDtypeStruct((row_count, width), F32),
        gw_hbm=jax.ShapeDtypeStruct((5, 2, own, width), F32),
        gg=jax.ShapeDtypeStruct((own, 128), F32),
    )
    vmem, hbm = pl.BlockSpec(memory_space=pltpu.VMEM), pl.BlockSpec(memory_space=pl.ANY)
    names = tuple(inputs) + tuple(results) + tuple(scratch)
    out, gtok, gw, gg = pl.pallas_call(
        functools.partial(layer_kernel, n, names),
        out_shape=tuple(results.values()),
        in_specs=[pl.BlockSpec(memory_space=pltpu.SMEM)] + [hbm if k.endswith(HBM) else vmem for k in names[1 : len(inputs)]],
        out_specs=[hbm if k.endswith(HBM) else vmem for k in results],
        scratch_shapes=list(scratch.values()),
        compiler_params=pltpu.CompilerParams(
            collective_id=0, has_side_effects=True, vmem_limit_bytes=60 * 2**20
        ),
    )(*inputs.values())

    shapes = (
        jax.ShapeDtypeStruct((row_count, width), BF),
        jax.ShapeDtypeStruct((row_count, width), F32),
        jax.ShapeDtypeStruct((1, own), F32),
        jax.ShapeDtypeStruct((own, 2 * span), F32),
        jax.ShapeDtypeStruct((own, 2 * span), F32),
        jax.ShapeDtypeStruct((own, 2 * span), F32),
        jax.ShapeDtypeStruct((own, 2 * span), F32),
        jax.ShapeDtypeStruct((1, own), F32),
        jax.ShapeDtypeStruct((own, 2 * width), F32),
        jax.ShapeDtypeStruct((own, 2 * width), F32),
        jax.ShapeDtypeStruct((own, 2 * width), F32),
        jax.ShapeDtypeStruct((own, 2 * width), F32),
    )
    buffers = [pltpu.VMEM(one.shape if slot > 1 else (8, 128), F32) for slot, one in enumerate(shapes)]
    final = pl.pallas_call(
        functools.partial(finish_kernel, len(shapes)),
        out_shape=shapes,
        in_specs=[hbm] * 3 + [vmem] * 3,
        out_specs=[hbm] * len(shapes),
        scratch_shapes=buffers
        + [
            pltpu.VMEM((row_count, width), BF),
            pltpu.VMEM((row_count, width), F32),
            pltpu.VMEM((5, 2, own, width), F32),
            pltpu.SemaphoreType.DMA((3,)),
            pltpu.SemaphoreType.DMA((len(shapes),)),
        ],
        compiler_params=pltpu.CompilerParams(vmem_limit_bytes=60 * 2**20),
    )(out, gtok, gw, gg, gain_one, gain_two)
    final = list(final)
    final[2] = final[2].reshape(own)
    final[7] = final[7].reshape(own)
    for turned in (6, 9, 11):
        final[turned] = final[turned].T
    return tuple(final)


def norm_parts(values):
    center = values - jnp.mean(values, axis=-1, keepdims=True)
    spread = jnp.mean(center * center, axis=-1, keepdims=True)
    inverse = lax.rsqrt(spread + epsilon)
    return (center * inverse, inverse)


def norm_back(grad_out, normed, inverse, gain):
    grad_normed = grad_out * gain
    grad_gain = jnp.sum(grad_out * normed, axis=0)
    inner = (
        grad_normed
        - jnp.mean(grad_normed, axis=-1, keepdims=True)
        - normed * jnp.mean(grad_normed * normed, axis=-1, keepdims=True)
    )
    return (inverse * inner, grad_gain)


def matmul(left, right):
    return jnp.dot(left, right, preferred_element_type=jnp.float32)


def matmul_tn(left, right):
    return lax.dot_general(
        left, right, (((0,), (0,)), ((), ())), preferred_element_type=jnp.float32
    )


def matmul_nt(left, right):
    return lax.dot_general(
        left, right, (((1,), (1,)), ((), ())), preferred_element_type=jnp.float32
    )


def gelu_slope(pre):
    cumulative = 0.5 * (1.0 + lax.erf(pre * inv_root_two))
    density = jnp.exp(-0.5 * pre * pre) * inv_root_tau
    return cumulative + pre * density


def expert_forward(rows, weight_in, weight_out):
    pre = matmul(rows, weight_in)
    hidden = jax.nn.gelu(pre, approximate=False).astype(jnp.bfloat16)
    return (pre, hidden, matmul(hidden, weight_out))


def expert_backward(rows, pre, hidden, grad_out, weight_in, weight_out):
    grad_weight_out = matmul_tn(hidden, grad_out)
    grad_hidden = matmul_nt(grad_out, weight_out)
    grad_pre = (grad_hidden * gelu_slope(pre)).astype(jnp.bfloat16)
    return (matmul_tn(rows, grad_pre), grad_weight_out, matmul_nt(grad_pre, weight_in))


def join_experts(image_rows, text_rows, pair_count, width):
    joined = jnp.concatenate(
        [
            image_rows.reshape(pair_count, PATCHES, width),
            text_rows.reshape(pair_count, CAPTION, width),
        ],
        axis=1,
    )
    return joined.reshape(-1, width)


def plain_layer(
    tokens,
    caption_lengths,
    gain_attn,
    w_query,
    w_key,
    w_value,
    w_out,
    gain_ffn,
    vis_in,
    vis_out,
    txt_in,
    txt_out,
    cotangent,
):
    seq_len = PATCHES + CAPTION
    width = tokens.shape[1]
    pair_count = tokens.shape[0] // seq_len
    half_pairs = pair_count // lax.axis_size("tensor")
    half_rows = half_pairs * seq_len
    row_start = lax.axis_index("tensor") * half_rows
    gain_one, query_w, key_w, value_w, out_w = (
        lax.all_gather(gain_attn, "dp", axis=0, tiled=True),
        lax.all_gather(w_query, "dp", axis=0, tiled=True),
        lax.all_gather(w_key, "dp", axis=0, tiled=True),
        lax.all_gather(w_value, "dp", axis=0, tiled=True),
        lax.all_gather(w_out, "dp", axis=1, tiled=True),
    )
    gain_two, vis_in_w, vis_out_w, txt_in_w, txt_out_w = (
        lax.all_gather(gain_ffn, "dp", axis=0, tiled=True),
        lax.all_gather(vis_in, "dp", axis=0, tiled=True),
        lax.all_gather(vis_out, "dp", axis=1, tiled=True),
        lax.all_gather(txt_in, "dp", axis=0, tiled=True),
        lax.all_gather(txt_out, "dp", axis=1, tiled=True),
    )
    gain_one = gain_one.astype(jnp.float32)
    gain_two = gain_two.astype(jnp.float32)
    head_local = query_w.shape[1] // HEAD_DIM
    score_scale = HEAD_DIM ** (-0.5)
    position = jnp.arange(seq_len, dtype=jnp.int32)
    live = (position[None, :] < PATCHES) | (position[None, :] - PATCHES < caption_lengths[:, None])
    valid_rows = live.astype(jnp.float32)
    mask_col = valid_rows.reshape(-1, 1)
    key_live = valid_rows[:, None, None, :] > 0.5

    def own_rows(values):
        return lax.dynamic_slice_in_dim(values, row_start, half_rows, 0)

    inputs = tokens.astype(jnp.float32)
    normed_one, inverse_one = norm_parts(inputs)
    first_in = (normed_one * gain_one).astype(jnp.bfloat16)

    def project(weight):
        return (
            matmul(first_in, weight)
            .astype(jnp.bfloat16)
            .reshape(pair_count, seq_len, head_local, HEAD_DIM)
        )

    queries = project(query_w)
    keys_all = project(key_w)
    values_all = project(value_w)

    def score_block():
        raw = (
            jnp.einsum("pqhe,pkhe->phqk", queries, keys_all, preferred_element_type=jnp.float32)
            * score_scale
        )
        return jnp.where(key_live, raw, -1e30)

    scores = score_block()
    top = jnp.max(scores, axis=-1, keepdims=True)
    weights = jnp.exp(scores - top)
    total = jnp.sum(weights, axis=-1, keepdims=True)
    probs = (weights / total).astype(jnp.bfloat16)
    log_total = top + jnp.log(total)
    context = jnp.einsum("phqk,pkhe->pqhe", probs, values_all, preferred_element_type=jnp.float32)
    context = context.astype(jnp.bfloat16).reshape(-1, head_local * HEAD_DIM)
    attn_terms = matmul(context, out_w)
    attended_own = lax.psum_scatter(
        attn_terms.astype(jnp.bfloat16), "tensor", scatter_dimension=0, tiled=True
    ).astype(jnp.float32)
    mask_own = own_rows(mask_col)
    middle_own = own_rows(inputs) + mask_own * attended_own
    normed_two, inverse_two = norm_parts(middle_own)
    second_own = (normed_two * gain_two).astype(jnp.bfloat16)
    grid = lax.all_gather(second_own, "tensor", axis=0, tiled=True).reshape(
        pair_count, seq_len, width
    )
    image_rows = grid[:, :PATCHES].reshape(-1, width)
    text_rows = grid[:, PATCHES:].reshape(-1, width)
    image_pre, image_hidden, image_part = expert_forward(image_rows, vis_in_w, vis_out_w)
    text_pre, text_hidden, text_part = expert_forward(text_rows, txt_in_w, txt_out_w)
    image_own, text_own = (
        lax.psum_scatter(
            image_part.astype(jnp.bfloat16), "tensor", scatter_dimension=0, tiled=True
        ).astype(jnp.float32),
        lax.psum_scatter(
            text_part.astype(jnp.bfloat16), "tensor", scatter_dimension=0, tiled=True
        ).astype(jnp.float32),
    )
    branch_own = join_experts(image_own, text_own, half_pairs, width)
    output_own = (middle_own + mask_own * branch_own).astype(jnp.bfloat16)
    upstream = cotangent.astype(jnp.float32)
    grad_branch = (upstream * mask_col).astype(jnp.bfloat16).reshape(pair_count, seq_len, width)
    image_grads = expert_backward(
        image_rows,
        image_pre,
        image_hidden,
        grad_branch[:, :PATCHES].reshape(-1, width),
        vis_in_w,
        vis_out_w,
    )
    text_grads = expert_backward(
        text_rows,
        text_pre,
        text_hidden,
        grad_branch[:, PATCHES:].reshape(-1, width),
        txt_in_w,
        txt_out_w,
    )
    back_image_own, back_text_own = (
        lax.psum_scatter(
            image_grads[2].astype(jnp.bfloat16), "tensor", scatter_dimension=0, tiled=True
        ).astype(jnp.float32),
        lax.psum_scatter(
            text_grads[2].astype(jnp.bfloat16), "tensor", scatter_dimension=0, tiled=True
        ).astype(jnp.float32),
    )
    grad_second_own = join_experts(back_image_own, back_text_own, half_pairs, width)
    grad_norm_own, gain_part = norm_back(grad_second_own, normed_two, inverse_two, gain_two)
    grad_middle_own = own_rows(upstream) + grad_norm_own
    output_wide, grad_middle, gain_parts = (
        lax.all_gather(
            output_own.astype(jnp.float32).astype(jnp.bfloat16), "tensor", axis=0, tiled=True
        ).astype(jnp.float32),
        lax.all_gather(grad_middle_own.astype(jnp.bfloat16), "tensor", axis=0, tiled=True).astype(
            grad_middle_own.dtype
        ),
        lax.all_gather(gain_part.astype(jnp.bfloat16), "tensor", axis=0, tiled=True).astype(
            gain_part.dtype
        ),
    )
    output = output_wide.astype(jnp.bfloat16)
    grad_gain_two = jnp.sum(gain_parts.reshape(-1, width), axis=0)
    grad_attended = (grad_middle * mask_col).astype(jnp.bfloat16)
    grad_out_w = matmul_tn(context, grad_attended)
    grad_context = (
        matmul_nt(grad_attended, out_w)
        .astype(jnp.bfloat16)
        .reshape(pair_count, seq_len, head_local, HEAD_DIM)
    )
    scores_again = score_block()
    probs_exact = jnp.exp(scores_again - log_total)
    grad_probs = jnp.einsum(
        "pqhe,pkhe->phqk", grad_context, values_all, preferred_element_type=jnp.float32
    )
    inner = jnp.sum(grad_probs * probs_exact, axis=-1, keepdims=True)
    grad_scores = (probs_exact * (grad_probs - inner)).astype(jnp.bfloat16)
    grad_values = jnp.einsum(
        "phqk,pqhe->pkhe", probs, grad_context, preferred_element_type=jnp.float32
    )
    grad_values = grad_values.astype(jnp.bfloat16).reshape(-1, head_local * HEAD_DIM)
    grad_queries = (
        jnp.einsum("phqk,pkhe->pqhe", grad_scores, keys_all, preferred_element_type=jnp.float32)
        * score_scale
    )
    grad_queries = grad_queries.astype(jnp.bfloat16).reshape(-1, head_local * HEAD_DIM)
    grad_keys = (
        jnp.einsum("phqk,pqhe->pkhe", grad_scores, queries, preferred_element_type=jnp.float32)
        * score_scale
    )
    grad_keys = grad_keys.astype(jnp.bfloat16).reshape(-1, head_local * HEAD_DIM)
    grad_query_w = matmul_tn(first_in, grad_queries)
    grad_key_w = matmul_tn(first_in, grad_keys)
    grad_value_w = matmul_tn(first_in, grad_values)
    first_part = (
        matmul_nt(grad_queries, query_w)
        + matmul_nt(grad_keys, key_w)
        + matmul_nt(grad_values, value_w)
    )
    grad_first = lax.psum(first_part.astype(jnp.bfloat16), "tensor").astype(jnp.float32)
    grad_norm_one, grad_gain_one = norm_back(grad_first, normed_one, inverse_one, gain_one)
    grad_inputs = grad_middle + grad_norm_one
    attn_sent = (
        lax.psum_scatter(grad_gain_one, "dp", scatter_dimension=0, tiled=True),
        lax.psum_scatter(grad_query_w, "dp", scatter_dimension=0, tiled=True),
        lax.psum_scatter(grad_key_w, "dp", scatter_dimension=0, tiled=True),
        lax.psum_scatter(grad_value_w, "dp", scatter_dimension=0, tiled=True),
        lax.psum_scatter(grad_out_w, "dp", scatter_dimension=1, tiled=True),
    )
    final_expert = (
        lax.psum_scatter(grad_gain_two, "dp", scatter_dimension=0, tiled=True),
        lax.psum_scatter(image_grads[0], "dp", scatter_dimension=0, tiled=True),
        lax.psum_scatter(image_grads[1], "dp", scatter_dimension=1, tiled=True),
        lax.psum_scatter(text_grads[0], "dp", scatter_dimension=0, tiled=True),
        lax.psum_scatter(text_grads[1], "dp", scatter_dimension=1, tiled=True),
    )
    return (
        output,
        grad_inputs,
        attn_sent[0],
        attn_sent[1],
        attn_sent[2],
        attn_sent[3],
        attn_sent[4],
        final_expert[0],
        final_expert[1],
        final_expert[2],
        final_expert[3],
        final_expert[4],
    )


def solution(mesh):
    def local(tokens, lengths, gain, w_query, *rest):
        ring = mesh.shape["dp"] // 2
        fits = (
            mesh.shape["tensor"] == 2
            and ring == 8
            and lengths.shape[0] == 2
            and w_query.shape[0] % 16 == 0
        )
        layer = fused_layer if fits else plain_layer
        return layer(tokens, lengths, gain, w_query, *rest)

    return jax.shard_map(
        local,
        mesh=mesh,
        in_specs=(
            P("dp", None),
            P("dp"),
            P("dp"),
            P("dp", "tensor"),
            P("dp", "tensor"),
            P("dp", "tensor"),
            P("tensor", "dp"),
            P("dp"),
            P("dp", "tensor"),
            P("tensor", "dp"),
            P("dp", "tensor"),
            P("tensor", "dp"),
            P("dp", None),
        ),
        out_specs=(
            P("dp", None),
            P("dp", None),
            P("dp"),
            P("dp", "tensor"),
            P("dp", "tensor"),
            P("dp", "tensor"),
            P("tensor", "dp"),
            P("dp"),
            P("dp", "tensor"),
            P("tensor", "dp"),
            P("dp", "tensor"),
            P("tensor", "dp"),
        ),
        check_vma=False,
    )
```

```python
import functools
import math
import types

import jax
import jax.numpy as jnp
from jax import lax
from jax.experimental import pallas as pl
from jax.experimental.pallas import tpu as pltpu
from jax.sharding import PartitionSpec as P

HEAD_DIM = 64
PATCHES = 197
CAPTION = 40
VIS = 208
TXT = 48
SEQ = VIS + TXT

MESH = pl.DeviceIdType.MESH
HBM = "_hbm"
BF = jnp.bfloat16
F32 = jnp.float32

ATT, TIN, TOUT, VIN, VOUT = range(5)

epsilon = 1e-05
inv_root_two = 1.0 / math.sqrt(2.0)
inv_root_tau = 1.0 / math.sqrt(2.0 * math.pi)


def mm(left, right):
    return jnp.dot(left, right, preferred_element_type=F32)


def mm_nt(left, right):
    return lax.dot_general(left, right, (((1,), (1,)), ((), ())), preferred_element_type=F32)


def mm_tn(left, right):
    return lax.dot_general(left, right, (((0,), (0,)), ((), ())), preferred_element_type=F32)


def normalize(values):
    center = values - jnp.mean(values, axis=-1, keepdims=True)
    spread = jnp.mean(center * center, axis=-1, keepdims=True)
    inverse = lax.rsqrt(spread + epsilon)
    return center * inverse, inverse


def normalize_back(grad_normed, normed, inverse):
    return inverse * (
        grad_normed
        - jnp.mean(grad_normed, axis=-1, keepdims=True)
        - normed * jnp.mean(grad_normed * normed, axis=-1, keepdims=True)
    )


def unit(size):
    rows = lax.broadcasted_iota(jnp.int32, (size, size), 0)
    return (rows == lax.broadcasted_iota(jnp.int32, (size, size), 1)).astype(F32).astype(BF)


def column(ref):
    size = ref.shape[1]
    return jnp.sum(unit(size).astype(F32) * ref[...].astype(F32), axis=1, keepdims=True)


def layer_kernel(n, names, *refs):
    R = types.SimpleNamespace(**dict(zip(names, refs)))
    R.pb, R.pf, R.ga, R.rf, R.rb, R.n2 = R.pg, R.pa, R.x4, R.ra, R.rg, R.n1
    R.gqkv, R.xsg, R.xrg = R.n2, R.xs, R.xr
    S, G, PART, LAND = R.shard, R.gathered, R.part, R.land
    OUT, GW, GG = R.padded_out, R.gw, R.gg
    width = G.shape[2]
    own = width // (2 * n)
    span = width // 4
    heads = span // HEAD_DIM

    x = lax.axis_index("tensor")
    d = lax.axis_index("dp")
    c = lax.rem(d, 2)
    other = 1 - c
    chip = d // 2
    y, z = lax.rem(chip, 2), chip // 2
    r = z + y * (n - 1 - 2 * z)
    half = n // 2

    def chip_at(pos):
        pos = lax.rem(pos + 2 * n, n)
        upper = pos // half
        return 2 * (pos + upper * (n - 1 - 2 * pos)) + upper

    near_mate = d + 1 - 2 * c
    mate, across, diagonal = (near_mate, x), (d, 1 - x), (near_mate, 1 - x)
    ahead = (2 * chip_at(r + 1) + c, x)
    behind = (2 * chip_at(r - 1) + c, x)
    way = (ahead, behind)

    offsets = {hop: 2 * own * chip_at(r + hop) for hop in range(-half, half + 1)}

    def rows_at(hop):
        return pl.ds(pl.multiple_of(offsets[hop], 16), 2 * own)

    my_rows = pl.ds(pl.multiple_of(own * d, 16), own)

    def fetch(slot, source, target):
        copy = pltpu.make_async_copy(source, target, R.local.at[slot])
        copy.start()
        return copy

    fetched = [
        fetch(0, R.tokens_hbm, R.tokens),
        fetch(1, R.txt_in_hbm, R.txt_in),
        fetch(2, R.txt_out_hbm, R.txt_out),
        fetch(3, R.vis_in_hbm, R.vis_in),
        fetch(4, R.vis_out_hbm, R.vis_out),
        fetch(5, R.cotangent_hbm, R.cotangent),
    ]

    barrier = pltpu.get_barrier_semaphore()
    for device in (mate, across, diagonal, ahead, behind):
        pl.semaphore_signal(barrier, inc=1, device_id=device, device_id_type=MESH)

    mine, theirs = pl.multiple_of(2 * c, 2), pl.multiple_of(2 * other, 2)
    pair_own = 2 * c + x
    pair_across = 2 * c + 1 - x

    started = []
    counter = [0]

    def remote(source, target, device):
        index = counter[0]
        counter[0] += 1
        return pltpu.make_async_remote_copy(
            src_ref=source,
            dst_ref=target,
            send_sem=R.sent.at[index],
            recv_sem=R.came.at[index],
            device_id=device,
            device_id_type=MESH,
        )

    def start(source, target, device):
        copy = remote(source, target, device)
        copy.start()
        started.append(copy)
        return copy

    def sent(copy):
        copy.wait_send()
        started[:] = [one for one in started if one is not copy]

    near, far = (ATT, 0, width // 2), (ATT, width // 2, width // 2)
    parts = [near, far] + [(k, 0, width) for k in (TIN, TOUT, VIN, VOUT)]
    tin, tout, vin, vout = parts[2:]
    longest = half

    def hops(part, side):
        return half if (parts.index(part) + side) % 2 == 0 else n - 1 - half

    def ring_index(part, side, s):
        return (parts.index(part) * 2 + side) * longest + s

    def view(ref, part, rows):
        k, first, count = part
        return ref.at[k, rows, pl.ds(first, count)]

    sum_base = len(parts) * 2 * longest

    def gather_copy(part, side, s, pos):
        block = view(G, part, rows_at(pos))
        i = ring_index(part, side, s)
        return pltpu.make_async_remote_copy(
            src_ref=block,
            dst_ref=block,
            send_sem=R.ring_sent.at[part[0]],
            recv_sem=R.ring_came.at[i],
            device_id=way[side],
            device_id_type=MESH,
        )

    def gather(part, s):
        for side in range(2):
            pos = -s if side == 0 else s
            if 0 < s <= hops(part, side):
                gather_copy(part, side, s - 1, pos).wait_recv()
            if s < hops(part, side):
                gather_copy(part, side, s, pos).start()

    def landed(part, side, s):
        k, first, count = part
        return LAND.at[k, side * hops(part, 0) + s, :, pl.ds(first, count)]

    def sum_copy(part, side, s, source):
        i = sum_base + ring_index(part, side, s)
        return pltpu.make_async_remote_copy(
            src_ref=source,
            dst_ref=landed(part, side, s),
            send_sem=R.ring_sent.at[5 + part[0]],
            recv_sem=R.ring_came.at[i],
            device_id=way[side],
            device_id_type=MESH,
        )

    def pass_sum(part, s):
        for side in range(2):
            reach = hops(part, side)
            if s >= reach:
                continue
            pos = reach - s if side == 0 else s - reach
            term = view(PART, part, rows_at(pos))
            if s == 0:
                source = term
            else:
                source = landed(part, side, s - 1)
                sum_copy(part, side, s - 1, source).wait_recv()
                source[...] = (source[...].astype(F32) + term[...].astype(F32)).astype(BF)
            sum_copy(part, side, s, source).start()

    finals = []
    row_sums = [[], []]

    def end_sum(*group):
        for part in group:
            k, first, count = part
            ends = []
            for side in range(2):
                end = landed(part, side, hops(part, side) - 1)
                sum_copy(part, side, hops(part, side) - 1, end).wait_recv()
                ends.append(end)
            cols = slice(first, first + count)
            counted = min(3 * span - first, count) if k == ATT else count

            def total(core):
                rows = pl.ds(pl.multiple_of(own * core, 16), own)
                chip_rows = pl.ds(pl.multiple_of(2 * own * chip + own * core, 16), own)
                block = (
                    ends[0][rows, :].astype(F32)
                    + ends[1][rows, :].astype(F32)
                    + PART[k, chip_rows, cols].astype(F32)
                )
                if k in (ATT, TIN, VIN):
                    weighted = G[k, chip_rows, cols].astype(F32)[:, :counted] * block[:, :counted]
                    total = jnp.sum(weighted, axis=-1, keepdims=True)
                    row_sums[0 if core is c else 1].append((k, total))
                return block

            R.give[k, :, cols] = total(other)
            finals.append(
                start(R.give.at[k, :, pl.ds(first, count)], GW.at[k, c, :, pl.ds(first, count)], mate)
            )
            GW[k, c, :, cols] = total(c)

    def shard_part(k, value):
        for core in range(2):
            S[k, core] = value(core).astype(BF)

    gain_one, gain_two = column(R.gain_attn), column(R.gain_ffn)

    def attention_part(core):
        cols = slice(core * span, (core + 1) * span)
        return jnp.concatenate(
            [
                R.w_query[:, cols].astype(F32) * (gain_one * HEAD_DIM**-0.5),
                R.w_key[:, cols].astype(F32) * gain_one,
                R.w_value[:, cols].astype(F32) * gain_one,
                R.w_out[:, cols].astype(F32),
            ],
            axis=1,
        )

    def half_of(ref, core):
        return ref[:, core * width : (core + 1) * width].astype(F32) * gain_two

    def turned_half(ref, core):
        return ref[:, core * width : (core + 1) * width]

    lengths = R.lengths

    def live(t, slots):
        return (slots < PATCHES) | ((slots >= VIS) & (slots < VIS + lengths[t]))

    def live_rows(t, j, count=64):
        slots = lax.broadcasted_iota(jnp.int32, (count, 1), 0) + j * count
        return live(t, slots).astype(F32)

    row_count = R.tokens.shape[0]

    def placed(t, slots, rows, kept):
        source = t * (PATCHES + CAPTION) + slots - (slots >= VIS).astype(jnp.int32) * (VIS - PATCHES)
        return ((rows == source) & kept).astype(F32).astype(BF)

    def chooser(t, only_live):
        slots = lax.broadcasted_iota(jnp.int32, (SEQ, row_count), 0)
        rows = lax.broadcasted_iota(jnp.int32, (SEQ, row_count), 1)
        filled = (slots < PATCHES) | ((slots >= VIS) & (slots < VIS + CAPTION))
        return placed(t, slots, rows, live(t, slots) if only_live else filled)

    shard_part(ATT, attention_part)
    G[ATT, my_rows, :] = S[ATT, c]
    for t in range(2):
        R.lens[t] = jnp.full((8, 128), lengths[t], jnp.int32).astype(F32)
    pl.semaphore_wait(barrier, 5)
    shard_a = start(S.at[pl.ds(0, 1), other], G.at[pl.ds(0, 1), my_rows, :], mate)
    send_lens = start(R.lens, R.lens4.at[pl.ds(mine, 2)], mate)
    fetched[0].wait()
    for t in range(2):
        R.x4[2 * c + t] = mm(chooser(t, False), R.tokens[...]).astype(BF)
        R.lens4[2 * c + t] = R.lens[t]
    send_x = start(R.x4.at[pl.ds(mine, 2)], R.x4.at[pl.ds(mine, 2)], mate)
    shard_a.wait_recv()
    gather(near, 0)
    gather(far, 0)
    for copy in fetched[1:]:
        copy.wait()

    shard_part(TIN, functools.partial(half_of, R.txt_in))
    shard_part(TOUT, functools.partial(turned_half, R.txt_out))
    shard_part(VIN, functools.partial(half_of, R.vis_in))
    shard_part(VOUT, functools.partial(turned_half, R.vis_out))
    shard_b = start(S.at[pl.ds(1, 4), other], G.at[pl.ds(1, 4), my_rows, :], mate)
    for k in (TIN, TOUT, VIN, VOUT):
        G[k, my_rows, :] = S[k, c]
    gather(near, 1)
    for t in range(2):
        R.gz[2 * c + t] = mm(chooser(t, True), R.cotangent[...]).astype(BF)
        if t == 0:
            gather(far, 1)
    send_gz = start(R.gz.at[pl.ds(mine, 2)], R.gz.at[pl.ds(mine, 2)], mate)
    R.dy[...] = mm(chooser(x, False), R.cotangent[...]).astype(BF)
    for t in range(2):
        R.x[t] = R.x4[2 * c + t]
    shard_b.wait_recv()
    gather(tin, 0)
    gather(near, 2)
    send_x.wait_recv()

    for i in range(4):

        @pl.loop(0, SEQ // 64)
        def _(j, i=i):
            rows = pl.ds(pl.multiple_of(j * 64, 64), 64)
            normed, _ = normalize(R.x4[i, rows, :].astype(F32))
            R.n1[i, rows, :] = normed.astype(BF)

        R.n1t[:, i * SEQ : (i + 1) * SEQ] = R.n1[i].T
        if i == 0:
            gather(far, 2)
        if i == 1:
            gather(tout, 0)
            gather(near, 3)
        if i == 2:
            gather(far, 3)
            gather(vin, 0)
            gather(vout, 0)
    send_gz.wait_recv()
    send_lens.wait_recv()
    gather(near, 4)
    gather(far, 4)

    R.wo[...] = G[ATT][:, 3 * span :]

    @pl.loop(0, 4)
    def _(i):
        projected = mm(R.n1[i], G[ATT][:, : 3 * span]).astype(BF)
        R.q[i] = projected[:, :span]
        R.k[i] = projected[:, span : 2 * span]
        R.v[i] = projected[:, 2 * span :]

    lane = lax.broadcasted_iota(jnp.int32, (1, span), 1) // HEAD_DIM

    def only(head, values):
        return values * (lane == head).astype(F32).astype(BF)

    def head_rows(values, head):
        return values[head * HEAD_DIM : (head + 1) * HEAD_DIM, :]

    order = []
    for j in range(4):
        core = other if j < 2 else c
        turn = 1 - x if j % 2 == 0 else x
        order.append((turn, 2 * core + turn))
    attn_mate = [remote(R.pa.at[i], R.ra.at[turn], mate) for turn, i in order[:2]]
    cross_a = remote(R.xs, R.xr, across)

    for j, (turn, i) in enumerate(order):
        q, k, v = R.q[i], R.k[i], R.v[i]
        turned_v = v.T
        slots = lax.broadcasted_iota(jnp.int32, (SEQ, 1), 0)
        caption = (slots - VIS).astype(F32) < R.lens4[i][:1, :1]
        bias = jnp.where((slots < PATCHES) | ((slots >= VIS) & caption), 0.0, -1e30)
        contexts = []
        for h in range(heads):
            scores = mm_nt(only(h, k), q) + bias
            top = jnp.max(scores, axis=0, keepdims=True)
            weights = jnp.exp(scores - top)
            total = jnp.sum(weights, axis=0, keepdims=True)
            probs = (weights * (1.0 / total)).astype(BF)
            R.probs[i * heads + h] = probs
            contexts.append(mm(head_rows(turned_v, h), probs))
        contexts = jnp.concatenate(contexts, axis=0)
        R.ct[:, pl.ds(pl.multiple_of(i * SEQ, SEQ), SEQ)] = contexts.astype(BF)
        context = contexts.T.astype(BF)
        R.pa[i] = mm_nt(context, R.wo[...]).astype(BF)
        if j < 2:
            attn_mate[j].start()
        if j == 2:
            attn_mate[0].wait_recv()
            R.xs[...] = (R.pa[pair_across].astype(F32) + R.ra[1 - x].astype(F32)).astype(BF)
            cross_a.start()
        if j == 0:
            gather(tin, 1)
        if j == 1:
            gather(tout, 1)
        if j == 3:
            gather(tin, 2)
            gather(tout, 2)

    for copy in attn_mate:
        copy.wait_send()
    attn_mate[1].wait_recv()

    @pl.loop(0, width // 256)
    def _(j):
        cols = pl.ds(pl.multiple_of(j * 256, 256), 256)
        R.gzvt[cols, :] = R.gz[:, :VIS, cols].reshape(4 * VIS, 256).T
        R.gztt[cols, :] = R.gz[:, VIS:, cols].reshape(4 * TXT, 256).T

    gather(vin, 1)
    cross_a.wait_recv()

    @pl.loop(0, SEQ // 64)
    def _(j):
        rows = pl.ds(pl.multiple_of(j * 64, 64), 64)
        attended = (
            R.pa[pair_own, rows, :].astype(F32)
            + R.ra[x, rows, :].astype(F32)
            + R.xr[rows, :].astype(F32)
        )
        middle = R.x[x, rows, :].astype(F32) + live_rows(x, j) * attended
        R.y1[rows, :] = middle
        normed, _ = normalize(middle)
        R.n2[pair_own, rows, :] = normed.astype(BF)

    block = R.n2.at[pair_own]
    to_across = start(block, block, across)
    to_mate = start(block, block, mate)
    gather(vout, 1)
    gather(tin, 3)
    gather(tout, 3)
    to_across.wait_recv()
    block = R.n2.at[pair_across]
    passed = start(block, block, mate)
    gather(vin, 2)
    gather(vout, 2)
    gather(tin, 4)
    gather(tout, 4)
    to_mate.wait_recv()
    passed.wait_recv()

    def expert(pairs, low, high, w_in, w_out, h_ref, gu_ref, j):
        first, count = pairs
        per = high - low
        total_rows = count * per
        cols = slice(j * 256, (j + 1) * 256)
        inside = slice(first, first + count)
        R.u[:total_rows, :] = mm(
            R.n2[inside, low:high, :].reshape(total_rows, width), G[w_in, :, cols]
        )
        R.gh[:total_rows, :] = mm(
            R.gz[inside, low:high, :].reshape(total_rows, width), G[w_out, :, cols]
        )
        step = min(total_rows, VIS)

        @pl.loop(0, 2 * (total_rows // step))
        def _(i):
            lanes = lax.rem(i, 2) * 128
            rows = pl.ds(pl.multiple_of(i // 2 * step, 16), step)
            into = pl.ds(pl.multiple_of(first * per + i // 2 * step, 16), step)
            side = pl.ds(pl.multiple_of(lanes, 128), 128)
            pre = R.u[rows, side]
            cumulative = 0.5 * (1.0 + lax.erf(pre * inv_root_two))
            density = jnp.exp(-0.5 * pre * pre) * inv_root_tau
            onto = pl.ds(pl.multiple_of(j * 256 + lanes, 128), 128)
            h_ref[into, onto] = (pre * cumulative).astype(BF)
            gu_ref[into, onto] = (R.gh[rows, side] * (cumulative + pre * density)).astype(BF)

    def weight_grad(k, turned, ref, j):
        cols = slice(j * 256, (j + 1) * 256)
        PART[k, :, cols] = mm(turned, ref[:, cols]).astype(BF)

    tiles = range(width // 256)
    for j in tiles:
        expert((0, 4), VIS, SEQ, TIN, TOUT, R.ht, R.gut, j)
    gather(vin, 3)
    for j in tiles:
        weight_grad(TOUT, R.gztt[...], R.ht, j)

    @pl.loop(0, width // 256)
    def _(j):
        cols = pl.ds(pl.multiple_of(j * 256, 256), 256)
        R.n2vt[cols, :] = R.n2[:, :VIS, cols].reshape(4 * VIS, 256).T
        R.n2tt[cols, :] = R.n2[:, VIS:, cols].reshape(4 * TXT, 256).T

    gather(vout, 3)
    for j in tiles:
        weight_grad(TIN, R.n2tt[...], R.gut, j)
    pass_sum(tout, 0)
    pass_sum(tin, 0)
    gather(vin, 4)
    gather(vout, 4)

    def terms(target, hv, ht, w_vis, w_txt, m):
        vis_rows = slice(2 * m * VIS, 2 * (m + 1) * VIS)
        txt_rows = slice(2 * m * TXT, 2 * (m + 1) * TXT)
        vis_part = mm_nt(hv[vis_rows, :], G[w_vis]).astype(BF)
        target[2 * m : 2 * m + 2, :VIS, :] = vis_part.reshape(2, VIS, width)
        txt_part = mm_nt(ht[txt_rows, :], G[w_txt]).astype(BF)
        target[2 * m : 2 * m + 2, VIS:, :] = txt_part.reshape(2, TXT, width)

    mate_g = remote(R.pg.at[pl.ds(theirs, 2)], R.rg, mate)
    cross_g = remote(R.xsg, R.xrg, across)
    gy_across = remote(R.gy.at[x], R.gy.at[x], across)
    gy_mate = remote(R.ga.at[pair_own], R.ga.at[pair_own], mate)
    gy_passed = remote(R.ga.at[pair_across], R.ga.at[pair_across], mate)
    started.extend([cross_g, gy_across, gy_mate, gy_passed])

    def image_terms(m):
        terms(R.pg, R.guv, R.gut, VIN, TIN, m)
        pl.when(c != m)(mate_g.start)

    def sum_cores(m):
        @pl.when(c == m)
        def _():
            mate_g.wait_recv()
            R.xsg[...] = (R.pg[pair_across].astype(F32) + R.rg[1 - x].astype(F32)).astype(BF)
            cross_g.start()

    def middle_back(m):
        @pl.when(c == m)
        def _():
            cross_g.wait_recv()

            @pl.loop(0, SEQ // 64)
            def _(j):
                rows = pl.ds(pl.multiple_of(j * 64, 64), 64)
                grad_normed = (
                    R.pg[pair_own, rows, :].astype(F32)
                    + R.rg[x, rows, :].astype(F32)
                    + R.xrg[rows, :].astype(F32)
                )
                normed, inverse = normalize(R.y1[rows, :])
                grad = R.dy[rows, :].astype(F32) + normalize_back(grad_normed, normed, inverse)
                R.gy[x, rows, :] = grad.astype(BF)
                R.ga[pair_own, rows, :] = (grad * live_rows(x, j)).astype(BF)

            gy_across.start()
            gy_mate.start()

    def middle_pass(m):
        @pl.when(c == m)
        def _():
            gy_across.wait_recv()

            @pl.loop(0, SEQ // 64)
            def _(j):
                rows = pl.ds(pl.multiple_of(j * 64, 64), 64)
                R.ga[pair_across, rows, :] = (
                    R.gy[1 - x, rows, :].astype(F32) * live_rows(1 - x, j)
                ).astype(BF)

            gy_passed.start()

    def middle_came(m):
        @pl.when(c != m)
        def _():
            gy_mate.wait_recv()
            gy_passed.wait_recv()

    sent(send_x)
    cross_a.wait_send()
    for j in tiles:
        expert((0, 2), 0, VIS, VIN, VOUT, R.hv, R.guv, j)
    image_terms(0)
    expert((2, 2), 0, VIS, VIN, VOUT, R.hv, R.guv, 0)
    sum_cores(0)
    pass_sum(tout, 1)
    for j in tiles[1:]:
        expert((2, 2), 0, VIS, VIN, VOUT, R.hv, R.guv, j)
    image_terms(1)
    for copy in (to_across, to_mate, passed):
        sent(copy)
    sum_cores(1)
    pass_sum(tin, 1)
    weight_grad(VOUT, R.gzvt[...], R.hv, 0)
    middle_back(0)
    for j in tiles[1:]:
        weight_grad(VOUT, R.gzvt[...], R.hv, j)
    pass_sum(vout, 0)
    pass_sum(tout, 2)
    for j in tiles:
        weight_grad(VIN, R.n2vt[...], R.guv, j)
    pass_sum(vin, 0)
    pass_sum(tin, 2)

    terms(R.pf, R.hv, R.ht, VOUT, TOUT, 0)
    middle_pass(0)
    middle_back(1)
    pass_sum(tout, 3)
    terms(R.pf, R.hv, R.ht, VOUT, TOUT, 1)
    mate_f = start(R.pf.at[pl.ds(theirs, 2)], R.rf, mate)
    cross_f = remote(R.xsf, R.xrf, across)
    started.append(cross_f)
    pass_sum(tin, 3)
    mate_g.wait_send()
    middle_came(0)

    back_mate = [remote(R.pb.at[theirs + t], R.rb.at[t], mate) for t in range(2)]
    back_cross = [remote(R.xsb.at[t], R.xrb.at[t], across) for t in range(2)]
    started.extend(back_mate + back_cross)

    def attention_back(m, t):
        i = 2 * m + t
        grad_context = mm(R.ga[i], R.wo[...]).astype(BF)
        q, k, v = R.q[i], R.k[i], R.v[i]
        turned_k = k.T
        grad_q = []
        grad_k = jnp.zeros((SEQ, span), F32)
        grad_v = jnp.zeros((SEQ, span), F32)
        for h in range(heads):
            probs = R.probs[i * heads + h]
            grad_probs = mm_nt(only(h, v), grad_context)
            exact = probs.astype(F32)
            inner = jnp.sum(grad_probs * exact, axis=0, keepdims=True)
            grad_scores = (exact * (grad_probs - inner)).astype(BF)
            grad_q.append(mm(head_rows(turned_k, h), grad_scores))
            grad_k += mm(grad_scores, only(h, q))
            grad_v += mm(probs, only(h, grad_context))
        grad_q = jnp.concatenate(grad_q, axis=0).T
        joined = jnp.concatenate([grad_q, grad_k, grad_v], axis=1).astype(BF)
        R.gqkv[i, :, : 3 * span] = joined
        R.pb[i] = mm_nt(joined, G[ATT][:, : 3 * span]).astype(BF)
        pl.when(c != m)(back_mate[t].start)

    def back_sum(m, t):
        @pl.when(c == m)
        def _():
            back_mate[t].wait_recv()
            R.xsb[t] = (R.pb[2 * m + t].astype(F32) + R.rb[t].astype(F32)).astype(BF)
            back_cross[t].start()

    attention_back(0, 0)
    pass_sum(vout, 1)
    mate_f.wait_recv()
    R.xsf[...] = (R.pf[pair_across].astype(F32) + R.rf[1 - x].astype(F32)).astype(BF)
    R.fown[...] = (R.pf[pair_own].astype(F32) + R.rf[x].astype(F32)).astype(BF)
    middle_pass(1)
    cross_f.start()
    attention_back(0, 1)
    back_sum(0, 0)

    pass_sum(vin, 1)
    middle_came(1)
    attention_back(1, 0)
    back_sum(0, 1)

    pass_sum(vout, 2)
    attention_back(1, 1)
    back_sum(1, 0)
    pass_sum(vin, 2)

    lanes = width // 2

    @pl.loop(0, width // 256)
    def _(j):
        rows = pl.ds(pl.multiple_of(j * 256, 256), 256)
        grad_v = mm(R.n1t[rows, :], R.gqkv[:, :, lanes : 3 * span].reshape(4 * SEQ, span))
        grad_o = mm(R.ct[...], R.ga[:, :, rows].reshape(4 * SEQ, 256)).T
        PART[ATT, rows, lanes:] = jnp.concatenate([grad_v, grad_o], axis=1).astype(BF)

    pass_sum(far, 0)

    cross_f.wait_recv()

    @pl.loop(0, SEQ // 64)
    def _(j):
        rows = pl.ds(pl.multiple_of(j * 64, 64), 64)
        branch = R.fown[rows, :].astype(F32) + R.xrf[rows, :].astype(F32)
        OUT[x, rows, :] = (R.y1[rows, :] + live_rows(x, j) * branch).astype(BF)

    out_across = start(OUT.at[x], OUT.at[x], across)

    @pl.loop(0, width // 256)
    def _(j):
        rows = pl.ds(pl.multiple_of(j * 256, 256), 256)
        grads = mm(R.n1t[rows, :], R.gqkv[:, :, :lanes].reshape(4 * SEQ, lanes))
        PART[ATT, rows, :lanes] = grads.astype(BF)

    pass_sum(near, 0)
    back_sum(1, 1)
    pass_sum(vout, 3)
    pass_sum(vin, 3)

    def input_back(m, t):
        @pl.when(c == m)
        def _():
            back_cross[t].wait_recv()

            @pl.loop(0, SEQ // 64)
            def _(j):
                rows = pl.ds(pl.multiple_of(j * 64, 64), 64)
                grad_normed = R.xsb[t, rows, :].astype(F32) + R.xrb[t, rows, :].astype(F32)
                normed, inverse = normalize(R.x[t, rows, :].astype(F32))
                grad = R.gy[t, rows, :].astype(F32) + normalize_back(grad_normed, normed, inverse)
                high = grad.astype(BF)
                rows = pl.ds(pl.multiple_of(t * SEQ + j * 64, 64), 64)
                R.hv[rows, :] = high
                R.guv[rows, :] = (grad - high.astype(F32)).astype(BF)

    pass_sum(far, 1)
    input_back(0, 0)
    pass_sum(near, 1)
    input_back(0, 1)
    end_sum(tout, tin)
    pass_sum(far, 2)
    pass_sum(near, 2)
    end_sum(vout, vin)

    leaving = []

    def leave(slot, source, target):
        leaving.append(fetch(slot, source, target))

    slots = lax.broadcasted_iota(jnp.int32, (row_count, 2 * SEQ), 1)
    rows = lax.broadcasted_iota(jnp.int32, (row_count, 2 * SEQ), 0)
    turn = slots // SEQ
    back = placed(turn, slots - turn * SEQ, rows, slots >= 0)
    out_across.wait_recv()
    R.out_tokens[...] = mm(back, OUT[...].reshape(2 * SEQ, width)).astype(BF)
    leave(6, R.out_tokens, R.out_tokens_hbm)
    for copy in finals:
        copy.wait_recv()
    finals.clear()
    leave(7, GW.at[pl.ds(1, 4)], R.gw_hbm.at[pl.ds(1, 4)])
    pass_sum(far, 3)
    pass_sum(near, 3)
    input_back(1, 0)
    input_back(1, 1)
    R.grad_tokens[...] = mm(back, R.hv[: 2 * SEQ, :]) + mm(back, R.guv[: 2 * SEQ, :])
    leave(8, R.grad_tokens, R.grad_tokens_hbm)
    end_sum(far, near)

    first_lane = lax.broadcasted_iota(jnp.int32, (own, 128), 1) == 0
    for place in range(2):
        attn = sum(total for k, total in row_sums[place] if k == ATT)
        experts = sum(total for k, total in row_sums[place] if k != ATT)
        R.gs[place] = jnp.where(first_lane, attn, experts)
    peers = [
        start(R.gs.at[place], R.gr.at[slot], device)
        for slot, (place, device) in enumerate(((1, mate), (0, across), (1, diagonal)))
    ]
    for copy in finals + peers:
        copy.wait_recv()
    leave(9, GW.at[pl.ds(0, 1)], R.gw_hbm.at[pl.ds(0, 1)])
    GG[...] = (R.gs[0] + R.gr[1]) + (R.gr[0] + R.gr[2])

    for copy in started:
        copy.wait_send()
    for copy in leaving:
        copy.wait()
    for k in range(5):
        for semaphore in (k, 5 + k):
            pltpu.make_async_remote_copy(
                src_ref=LAND.at[k],
                dst_ref=LAND.at[k],
                send_sem=R.ring_sent.at[semaphore],
                recv_sem=R.ring_came.at[0],
                device_id=ahead,
                device_id_type=MESH,
            ).wait_send()


def finish_kernel(n_results, out, gtok, gw_hbm, gg, gain_attn, gain_ffn, *rest):
    results, scratch = rest[:n_results], rest[n_results:]
    buffers, (out_buffer, gtok_buffer, gw, came, gone) = scratch[:n_results], scratch[n_results:]
    arriving = [
        pltpu.make_async_copy(source, target, came.at[slot])
        for slot, (source, target) in enumerate(((gw_hbm, gw), (out, out_buffer), (gtok, gtok_buffer)))
    ]
    for copy in arriving:
        copy.start()
    width = gw.shape[3]
    own = gw.shape[2]
    span = width // 4
    gain_one, gain_two = column(gain_attn), column(gain_ffn)
    square = unit(own).astype(F32)
    leaving = []

    def leave(slot, source):
        copy = pltpu.make_async_copy(source, results[slot], gone.at[slot])
        copy.start()
        leaving.append(copy)

    def both(part):
        cols = slice(part * span, (part + 1) * span)
        return jnp.concatenate([gw[ATT, core][:, cols] for core in range(2)], axis=1)

    def put(slot, value):
        buffers[slot][...] = value
        leave(slot, buffers[slot])

    put(2, jnp.sum(square * (gg[:, :1] / gain_one), axis=0, keepdims=True))
    put(7, jnp.sum(square * (gg[:, 1:2] / gain_two), axis=0, keepdims=True))
    arriving[0].wait()
    for slot, k, scale in ((8, VIN, gain_two), (9, VOUT, 1.0), (10, TIN, gain_two), (11, TOUT, 1.0)):
        put(slot, jnp.concatenate([gw[k, 0], gw[k, 1]], axis=1) * scale)
    put(3, both(0) * (gain_one * HEAD_DIM**-0.5))
    put(4, both(1) * gain_one)
    put(5, both(2) * gain_one)
    put(6, both(3))
    arriving[1].wait()
    leave(0, out_buffer)
    arriving[2].wait()
    leave(1, gtok_buffer)
    for copy in leaving:
        copy.wait()


def fused_layer(
    tokens,
    caption_lengths,
    gain_attn,
    w_query,
    w_key,
    w_value,
    w_out,
    gain_ffn,
    vis_in,
    vis_out,
    txt_in,
    txt_out,
    cotangent,
):
    n = lax.axis_size("dp") // 2
    own = w_query.shape[0]
    row_count, width = tokens.shape
    span = width // 4
    heads = span // HEAD_DIM
    gain_one, gain_two = gain_attn.reshape(1, own), gain_ffn.reshape(1, own)

    rows = 4 * SEQ
    scratch = dict(
        tokens=pltpu.VMEM((row_count, width), BF),
        cotangent=pltpu.VMEM((row_count, width), BF),
        txt_in=pltpu.VMEM((own, 2 * width), BF),
        txt_out=pltpu.VMEM((own, 2 * width), BF),
        vis_in=pltpu.VMEM((own, 2 * width), BF),
        vis_out=pltpu.VMEM((own, 2 * width), BF),
        out_tokens=pltpu.VMEM((row_count, width), BF),
        grad_tokens=pltpu.VMEM((row_count, width), F32),
        gw=pltpu.VMEM((5, 2, own, width), F32),
        local=pltpu.SemaphoreType.DMA((10,)),
        shard=pltpu.VMEM((5, 2, own, width), BF),
        lens=pltpu.VMEM((2, 8, 128), F32),
        x=pltpu.VMEM((2, SEQ, width), BF),
        dy=pltpu.VMEM((SEQ, width), BF),
        padded_out=pltpu.VMEM((2, SEQ, width), BF),
        gathered=pltpu.VMEM((5, width, width), BF),
        part=pltpu.VMEM((5, width, width), BF),
        land=pltpu.VMEM((5, n - 1, 2 * own, width), BF),
        give=pltpu.VMEM((5, own, width), F32),
        x4=pltpu.VMEM((4, SEQ, width), BF),
        lens4=pltpu.VMEM((4, 8, 128), F32),
        n1=pltpu.VMEM((4, SEQ, width), BF),
        n1t=pltpu.VMEM((width, rows), BF),
        gz=pltpu.VMEM((4, SEQ, width), BF),
        gzvt=pltpu.VMEM((width, 4 * VIS), BF),
        ct=pltpu.VMEM((span, rows), BF),
        fown=pltpu.VMEM((SEQ, width), BF),
        gztt=pltpu.VMEM((width, 4 * TXT), BF),
        wo=pltpu.VMEM((width, span), BF),
        q=pltpu.VMEM((4, SEQ, span), BF),
        k=pltpu.VMEM((4, SEQ, span), BF),
        v=pltpu.VMEM((4, SEQ, span), BF),
        probs=pltpu.VMEM((4 * heads, SEQ, SEQ), BF),
        pa=pltpu.VMEM((4, SEQ, width), BF),
        ra=pltpu.VMEM((2, SEQ, width), BF),
        xs=pltpu.VMEM((SEQ, width), BF),
        xr=pltpu.VMEM((SEQ, width), BF),
        y1=pltpu.VMEM((SEQ, width), F32),
        n2vt=pltpu.VMEM((width, 4 * VIS), BF),
        n2tt=pltpu.VMEM((width, 4 * TXT), BF),
        u=pltpu.VMEM((4 * VIS, 256), F32),
        gh=pltpu.VMEM((4 * VIS, 256), F32),
        hv=pltpu.VMEM((4 * VIS, width), BF),
        guv=pltpu.VMEM((4 * VIS, width), BF),
        ht=pltpu.VMEM((4 * TXT, width), BF),
        gut=pltpu.VMEM((4 * TXT, width), BF),
        pg=pltpu.VMEM((4, SEQ, width), BF),
        rg=pltpu.VMEM((2, SEQ, width), BF),
        gy=pltpu.VMEM((2, SEQ, width), BF),
        xsf=pltpu.VMEM((SEQ, width), BF),
        xrf=pltpu.VMEM((SEQ, width), BF),
        xsb=pltpu.VMEM((2, SEQ, width), BF),
        xrb=pltpu.VMEM((2, SEQ, width), BF),
        gs=pltpu.VMEM((2, own, 128), F32),
        gr=pltpu.VMEM((3, own, 128), F32),
        sent=pltpu.SemaphoreType.DMA((40,)),
        came=pltpu.SemaphoreType.DMA((40,)),
        ring_sent=pltpu.SemaphoreType.DMA((10,)),
        ring_came=pltpu.SemaphoreType.DMA((6 * 2 * (n // 2) * 2,)),
    )
    inputs = dict(
        lengths=caption_lengths,
        tokens_hbm=tokens,
        cotangent_hbm=cotangent,
        gain_attn=gain_one,
        gain_ffn=gain_two,
        w_query=w_query,
        w_key=w_key,
        w_value=w_value,
        w_out=w_out.T,
        vis_in_hbm=vis_in,
        vis_out_hbm=vis_out.T,
        txt_in_hbm=txt_in,
        txt_out_hbm=txt_out.T,
    )
    results = dict(
        out_tokens_hbm=jax.ShapeDtypeStruct((row_count, width), BF),
        grad_tokens_hbm=jax.ShapeDtypeStruct((row_count, width), F32),
        gw_hbm=jax.ShapeDtypeStruct((5, 2, own, width), F32),
        gg=jax.ShapeDtypeStruct((own, 128), F32),
    )
    vmem, hbm = pl.BlockSpec(memory_space=pltpu.VMEM), pl.BlockSpec(memory_space=pl.ANY)
    names = tuple(inputs) + tuple(results) + tuple(scratch)
    out, gtok, gw, gg = pl.pallas_call(
        functools.partial(layer_kernel, n, names),
        out_shape=tuple(results.values()),
        in_specs=[pl.BlockSpec(memory_space=pltpu.SMEM)] + [hbm if k.endswith(HBM) else vmem for k in names[1 : len(inputs)]],
        out_specs=[hbm if k.endswith(HBM) else vmem for k in results],
        scratch_shapes=list(scratch.values()),
        compiler_params=pltpu.CompilerParams(
            collective_id=0, has_side_effects=True, vmem_limit_bytes=60 * 2**20
        ),
    )(*inputs.values())

    shapes = (
        jax.ShapeDtypeStruct((row_count, width), BF),
        jax.ShapeDtypeStruct((row_count, width), F32),
        jax.ShapeDtypeStruct((1, own), F32),
        jax.ShapeDtypeStruct((own, 2 * span), F32),
        jax.ShapeDtypeStruct((own, 2 * span), F32),
        jax.ShapeDtypeStruct((own, 2 * span), F32),
        jax.ShapeDtypeStruct((own, 2 * span), F32),
        jax.ShapeDtypeStruct((1, own), F32),
        jax.ShapeDtypeStruct((own, 2 * width), F32),
        jax.ShapeDtypeStruct((own, 2 * width), F32),
        jax.ShapeDtypeStruct((own, 2 * width), F32),
        jax.ShapeDtypeStruct((own, 2 * width), F32),
    )
    buffers = [pltpu.VMEM(one.shape if slot > 1 else (8, 128), F32) for slot, one in enumerate(shapes)]
    final = pl.pallas_call(
        functools.partial(finish_kernel, len(shapes)),
        out_shape=shapes,
        in_specs=[hbm] * 3 + [vmem] * 3,
        out_specs=[hbm] * len(shapes),
        scratch_shapes=buffers
        + [
            pltpu.VMEM((row_count, width), BF),
            pltpu.VMEM((row_count, width), F32),
            pltpu.VMEM((5, 2, own, width), F32),
            pltpu.SemaphoreType.DMA((3,)),
            pltpu.SemaphoreType.DMA((len(shapes),)),
        ],
        compiler_params=pltpu.CompilerParams(vmem_limit_bytes=60 * 2**20),
    )(out, gtok, gw, gg, gain_one, gain_two)
    final = list(final)
    final[2] = final[2].reshape(own)
    final[7] = final[7].reshape(own)
    for turned in (6, 9, 11):
        final[turned] = final[turned].T
    return tuple(final)


def norm_parts(values):
    center = values - jnp.mean(values, axis=-1, keepdims=True)
    spread = jnp.mean(center * center, axis=-1, keepdims=True)
    inverse = lax.rsqrt(spread + epsilon)
    return (center * inverse, inverse)


def norm_back(grad_out, normed, inverse, gain):
    grad_normed = grad_out * gain
    grad_gain = jnp.sum(grad_out * normed, axis=0)
    inner = (
        grad_normed
        - jnp.mean(grad_normed, axis=-1, keepdims=True)
        - normed * jnp.mean(grad_normed * normed, axis=-1, keepdims=True)
    )
    return (inverse * inner, grad_gain)


def matmul(left, right):
    return jnp.dot(left, right, preferred_element_type=jnp.float32)


def matmul_tn(left, right):
    return lax.dot_general(
        left, right, (((0,), (0,)), ((), ())), preferred_element_type=jnp.float32
    )


def matmul_nt(left, right):
    return lax.dot_general(
        left, right, (((1,), (1,)), ((), ())), preferred_element_type=jnp.float32
    )


def gelu_slope(pre):
    cumulative = 0.5 * (1.0 + lax.erf(pre * inv_root_two))
    density = jnp.exp(-0.5 * pre * pre) * inv_root_tau
    return cumulative + pre * density


def expert_forward(rows, weight_in, weight_out):
    pre = matmul(rows, weight_in)
    hidden = jax.nn.gelu(pre, approximate=False).astype(jnp.bfloat16)
    return (pre, hidden, matmul(hidden, weight_out))


def expert_backward(rows, pre, hidden, grad_out, weight_in, weight_out):
    grad_weight_out = matmul_tn(hidden, grad_out)
    grad_hidden = matmul_nt(grad_out, weight_out)
    grad_pre = (grad_hidden * gelu_slope(pre)).astype(jnp.bfloat16)
    return (matmul_tn(rows, grad_pre), grad_weight_out, matmul_nt(grad_pre, weight_in))


def join_experts(image_rows, text_rows, pair_count, width):
    joined = jnp.concatenate(
        [
            image_rows.reshape(pair_count, PATCHES, width),
            text_rows.reshape(pair_count, CAPTION, width),
        ],
        axis=1,
    )
    return joined.reshape(-1, width)


def plain_layer(
    tokens,
    caption_lengths,
    gain_attn,
    w_query,
    w_key,
    w_value,
    w_out,
    gain_ffn,
    vis_in,
    vis_out,
    txt_in,
    txt_out,
    cotangent,
):
    seq_len = PATCHES + CAPTION
    width = tokens.shape[1]
    pair_count = tokens.shape[0] // seq_len
    half_pairs = pair_count // lax.axis_size("tensor")
    half_rows = half_pairs * seq_len
    row_start = lax.axis_index("tensor") * half_rows
    gain_one, query_w, key_w, value_w, out_w = (
        lax.all_gather(gain_attn, "dp", axis=0, tiled=True),
        lax.all_gather(w_query, "dp", axis=0, tiled=True),
        lax.all_gather(w_key, "dp", axis=0, tiled=True),
        lax.all_gather(w_value, "dp", axis=0, tiled=True),
        lax.all_gather(w_out, "dp", axis=1, tiled=True),
    )
    gain_two, vis_in_w, vis_out_w, txt_in_w, txt_out_w = (
        lax.all_gather(gain_ffn, "dp", axis=0, tiled=True),
        lax.all_gather(vis_in, "dp", axis=0, tiled=True),
        lax.all_gather(vis_out, "dp", axis=1, tiled=True),
        lax.all_gather(txt_in, "dp", axis=0, tiled=True),
        lax.all_gather(txt_out, "dp", axis=1, tiled=True),
    )
    gain_one = gain_one.astype(jnp.float32)
    gain_two = gain_two.astype(jnp.float32)
    head_local = query_w.shape[1] // HEAD_DIM
    score_scale = HEAD_DIM ** (-0.5)
    position = jnp.arange(seq_len, dtype=jnp.int32)
    live = (position[None, :] < PATCHES) | (position[None, :] - PATCHES < caption_lengths[:, None])
    valid_rows = live.astype(jnp.float32)
    mask_col = valid_rows.reshape(-1, 1)
    key_live = valid_rows[:, None, None, :] > 0.5

    def own_rows(values):
        return lax.dynamic_slice_in_dim(values, row_start, half_rows, 0)

    inputs = tokens.astype(jnp.float32)
    normed_one, inverse_one = norm_parts(inputs)
    first_in = (normed_one * gain_one).astype(jnp.bfloat16)

    def project(weight):
        return (
            matmul(first_in, weight)
            .astype(jnp.bfloat16)
            .reshape(pair_count, seq_len, head_local, HEAD_DIM)
        )

    queries = project(query_w)
    keys_all = project(key_w)
    values_all = project(value_w)

    def score_block():
        raw = (
            jnp.einsum("pqhe,pkhe->phqk", queries, keys_all, preferred_element_type=jnp.float32)
            * score_scale
        )
        return jnp.where(key_live, raw, -1e30)

    scores = score_block()
    top = jnp.max(scores, axis=-1, keepdims=True)
    weights = jnp.exp(scores - top)
    total = jnp.sum(weights, axis=-1, keepdims=True)
    probs = (weights / total).astype(jnp.bfloat16)
    log_total = top + jnp.log(total)
    context = jnp.einsum("phqk,pkhe->pqhe", probs, values_all, preferred_element_type=jnp.float32)
    context = context.astype(jnp.bfloat16).reshape(-1, head_local * HEAD_DIM)
    attn_terms = matmul(context, out_w)
    attended_own = lax.psum_scatter(
        attn_terms.astype(jnp.bfloat16), "tensor", scatter_dimension=0, tiled=True
    ).astype(jnp.float32)
    mask_own = own_rows(mask_col)
    middle_own = own_rows(inputs) + mask_own * attended_own
    normed_two, inverse_two = norm_parts(middle_own)
    second_own = (normed_two * gain_two).astype(jnp.bfloat16)
    grid = lax.all_gather(second_own, "tensor", axis=0, tiled=True).reshape(
        pair_count, seq_len, width
    )
    image_rows = grid[:, :PATCHES].reshape(-1, width)
    text_rows = grid[:, PATCHES:].reshape(-1, width)
    image_pre, image_hidden, image_part = expert_forward(image_rows, vis_in_w, vis_out_w)
    text_pre, text_hidden, text_part = expert_forward(text_rows, txt_in_w, txt_out_w)
    image_own, text_own = (
        lax.psum_scatter(
            image_part.astype(jnp.bfloat16), "tensor", scatter_dimension=0, tiled=True
        ).astype(jnp.float32),
        lax.psum_scatter(
            text_part.astype(jnp.bfloat16), "tensor", scatter_dimension=0, tiled=True
        ).astype(jnp.float32),
    )
    branch_own = join_experts(image_own, text_own, half_pairs, width)
    output_own = (middle_own + mask_own * branch_own).astype(jnp.bfloat16)
    upstream = cotangent.astype(jnp.float32)
    grad_branch = (upstream * mask_col).astype(jnp.bfloat16).reshape(pair_count, seq_len, width)
    image_grads = expert_backward(
        image_rows,
        image_pre,
        image_hidden,
        grad_branch[:, :PATCHES].reshape(-1, width),
        vis_in_w,
        vis_out_w,
    )
    text_grads = expert_backward(
        text_rows,
        text_pre,
        text_hidden,
        grad_branch[:, PATCHES:].reshape(-1, width),
        txt_in_w,
        txt_out_w,
    )
    back_image_own, back_text_own = (
        lax.psum_scatter(
            image_grads[2].astype(jnp.bfloat16), "tensor", scatter_dimension=0, tiled=True
        ).astype(jnp.float32),
        lax.psum_scatter(
            text_grads[2].astype(jnp.bfloat16), "tensor", scatter_dimension=0, tiled=True
        ).astype(jnp.float32),
    )
    grad_second_own = join_experts(back_image_own, back_text_own, half_pairs, width)
    grad_norm_own, gain_part = norm_back(grad_second_own, normed_two, inverse_two, gain_two)
    grad_middle_own = own_rows(upstream) + grad_norm_own
    output_wide, grad_middle, gain_parts = (
        lax.all_gather(
            output_own.astype(jnp.float32).astype(jnp.bfloat16), "tensor", axis=0, tiled=True
        ).astype(jnp.float32),
        lax.all_gather(grad_middle_own.astype(jnp.bfloat16), "tensor", axis=0, tiled=True).astype(
            grad_middle_own.dtype
        ),
        lax.all_gather(gain_part.astype(jnp.bfloat16), "tensor", axis=0, tiled=True).astype(
            gain_part.dtype
        ),
    )
    output = output_wide.astype(jnp.bfloat16)
    grad_gain_two = jnp.sum(gain_parts.reshape(-1, width), axis=0)
    grad_attended = (grad_middle * mask_col).astype(jnp.bfloat16)
    grad_out_w = matmul_tn(context, grad_attended)
    grad_context = (
        matmul_nt(grad_attended, out_w)
        .astype(jnp.bfloat16)
        .reshape(pair_count, seq_len, head_local, HEAD_DIM)
    )
    scores_again = score_block()
    probs_exact = jnp.exp(scores_again - log_total)
    grad_probs = jnp.einsum(
        "pqhe,pkhe->phqk", grad_context, values_all, preferred_element_type=jnp.float32
    )
    inner = jnp.sum(grad_probs * probs_exact, axis=-1, keepdims=True)
    grad_scores = (probs_exact * (grad_probs - inner)).astype(jnp.bfloat16)
    grad_values = jnp.einsum(
        "phqk,pqhe->pkhe", probs, grad_context, preferred_element_type=jnp.float32
    )
    grad_values = grad_values.astype(jnp.bfloat16).reshape(-1, head_local * HEAD_DIM)
    grad_queries = (
        jnp.einsum("phqk,pkhe->pqhe", grad_scores, keys_all, preferred_element_type=jnp.float32)
        * score_scale
    )
    grad_queries = grad_queries.astype(jnp.bfloat16).reshape(-1, head_local * HEAD_DIM)
    grad_keys = (
        jnp.einsum("phqk,pqhe->pkhe", grad_scores, queries, preferred_element_type=jnp.float32)
        * score_scale
    )
    grad_keys = grad_keys.astype(jnp.bfloat16).reshape(-1, head_local * HEAD_DIM)
    grad_query_w = matmul_tn(first_in, grad_queries)
    grad_key_w = matmul_tn(first_in, grad_keys)
    grad_value_w = matmul_tn(first_in, grad_values)
    first_part = (
        matmul_nt(grad_queries, query_w)
        + matmul_nt(grad_keys, key_w)
        + matmul_nt(grad_values, value_w)
    )
    grad_first = lax.psum(first_part.astype(jnp.bfloat16), "tensor").astype(jnp.float32)
    grad_norm_one, grad_gain_one = norm_back(grad_first, normed_one, inverse_one, gain_one)
    grad_inputs = grad_middle + grad_norm_one
    attn_sent = (
        lax.psum_scatter(grad_gain_one, "dp", scatter_dimension=0, tiled=True),
        lax.psum_scatter(grad_query_w, "dp", scatter_dimension=0, tiled=True),
        lax.psum_scatter(grad_key_w, "dp", scatter_dimension=0, tiled=True),
        lax.psum_scatter(grad_value_w, "dp", scatter_dimension=0, tiled=True),
        lax.psum_scatter(grad_out_w, "dp", scatter_dimension=1, tiled=True),
    )
    final_expert = (
        lax.psum_scatter(grad_gain_two, "dp", scatter_dimension=0, tiled=True),
        lax.psum_scatter(image_grads[0], "dp", scatter_dimension=0, tiled=True),
        lax.psum_scatter(image_grads[1], "dp", scatter_dimension=1, tiled=True),
        lax.psum_scatter(text_grads[0], "dp", scatter_dimension=0, tiled=True),
        lax.psum_scatter(text_grads[1], "dp", scatter_dimension=1, tiled=True),
    )
    return (
        output,
        grad_inputs,
        attn_sent[0],
        attn_sent[1],
        attn_sent[2],
        attn_sent[3],
        attn_sent[4],
        final_expert[0],
        final_expert[1],
        final_expert[2],
        final_expert[3],
        final_expert[4],
    )


def solution(mesh):
    def local(tokens, lengths, gain, w_query, *rest):
        ring = mesh.shape["dp"] // 2
        fits = (
            mesh.shape["tensor"] == 2
            and ring == 8
            and lengths.shape[0] == 2
            and w_query.shape[0] % 16 == 0
        )
        layer = fused_layer if fits else plain_layer
        return layer(tokens, lengths, gain, w_query, *rest)

    return jax.shard_map(
        local,
        mesh=mesh,
        in_specs=(
            P("dp", None),
            P("dp"),
            P("dp"),
            P("dp", "tensor"),
            P("dp", "tensor"),
            P("dp", "tensor"),
            P("tensor", "dp"),
            P("dp"),
            P("dp", "tensor"),
            P("tensor", "dp"),
            P("dp", "tensor"),
            P("tensor", "dp"),
            P("dp", None),
        ),
        out_specs=(
            P("dp", None),
            P("dp", None),
            P("dp"),
            P("dp", "tensor"),
            P("dp", "tensor"),
            P("dp", "tensor"),
            P("tensor", "dp"),
            P("dp"),
            P("dp", "tensor"),
            P("tensor", "dp"),
            P("dp", "tensor"),
            P("tensor", "dp"),
        ),
        check_vma=False,
    )
```

```python
import functools
import math
import types

import jax
import jax.numpy as jnp
from jax import lax
from jax.experimental import pallas as pl
from jax.experimental.pallas import tpu as pltpu
from jax.sharding import PartitionSpec as P

HEAD_DIM = 64
PATCHES = 197
CAPTION = 40
VIS = 208
TXT = 48
SEQ = VIS + TXT

MESH = pl.DeviceIdType.MESH
HBM = "_hbm"
BF = jnp.bfloat16
F32 = jnp.float32

ATT, TIN, TOUT, VIN, VOUT = range(5)

epsilon = 1e-05
inv_root_two = 1.0 / math.sqrt(2.0)
inv_root_tau = 1.0 / math.sqrt(2.0 * math.pi)


def mm(left, right):
    return jnp.dot(left, right, preferred_element_type=F32)


def mm_nt(left, right):
    return lax.dot_general(left, right, (((1,), (1,)), ((), ())), preferred_element_type=F32)


def mm_tn(left, right):
    return lax.dot_general(left, right, (((0,), (0,)), ((), ())), preferred_element_type=F32)


def normalize(values):
    center = values - jnp.mean(values, axis=-1, keepdims=True)
    spread = jnp.mean(center * center, axis=-1, keepdims=True)
    inverse = lax.rsqrt(spread + epsilon)
    return center * inverse, inverse


def normalize_back(grad_normed, normed, inverse):
    return inverse * (
        grad_normed
        - jnp.mean(grad_normed, axis=-1, keepdims=True)
        - normed * jnp.mean(grad_normed * normed, axis=-1, keepdims=True)
    )


def unit(size):
    rows = lax.broadcasted_iota(jnp.int32, (size, size), 0)
    return (rows == lax.broadcasted_iota(jnp.int32, (size, size), 1)).astype(F32).astype(BF)


def column(ref):
    size = ref.shape[1]
    return jnp.sum(unit(size).astype(F32) * ref[...].astype(F32), axis=1, keepdims=True)


def layer_kernel(n, names, *refs):
    R = types.SimpleNamespace(**dict(zip(names, refs)))
    R.pb, R.pf, R.ga, R.rf, R.rb, R.n2 = R.pg, R.pa, R.x4, R.ra, R.rg, R.n1
    R.gqkv, R.xsg, R.xrg = R.n2, R.xs, R.xr
    S, G, PART, LAND = R.shard, R.gathered, R.part, R.land
    OUT, GW, GG = R.padded_out, R.gw, R.gg
    width = G.shape[2]
    own = width // (2 * n)
    span = width // 4
    heads = span // HEAD_DIM

    x = lax.axis_index("tensor")
    d = lax.axis_index("dp")
    c = lax.rem(d, 2)
    other = 1 - c
    chip = d // 2
    y, z = lax.rem(chip, 2), chip // 2
    r = z + y * (n - 1 - 2 * z)
    half = n // 2

    def chip_at(pos):
        pos = lax.rem(pos + 2 * n, n)
        upper = pos // half
        return 2 * (pos + upper * (n - 1 - 2 * pos)) + upper

    near_mate = d + 1 - 2 * c
    mate, across, diagonal = (near_mate, x), (d, 1 - x), (near_mate, 1 - x)
    ahead = (2 * chip_at(r + 1) + c, x)
    behind = (2 * chip_at(r - 1) + c, x)
    way = (ahead, behind)

    offsets = {hop: 2 * own * chip_at(r + hop) for hop in range(-half, half + 1)}

    def rows_at(hop):
        return pl.ds(pl.multiple_of(offsets[hop], 16), 2 * own)

    my_rows = pl.ds(pl.multiple_of(own * d, 16), own)

    def fetch(slot, source, target):
        copy = pltpu.make_async_copy(source, target, R.local.at[slot])
        copy.start()
        return copy

    fetched = [
        fetch(0, R.tokens_hbm, R.tokens),
        fetch(1, R.txt_in_hbm, R.txt_in),
        fetch(2, R.txt_out_hbm, R.txt_out),
        fetch(3, R.vis_in_hbm, R.vis_in),
        fetch(4, R.vis_out_hbm, R.vis_out),
        fetch(5, R.cotangent_hbm, R.cotangent),
    ]

    barrier = pltpu.get_barrier_semaphore()
    for device in (mate, across, diagonal, ahead, behind):
        pl.semaphore_signal(barrier, inc=1, device_id=device, device_id_type=MESH)

    mine, theirs = pl.multiple_of(2 * c, 2), pl.multiple_of(2 * other, 2)
    pair_own = 2 * c + x
    pair_across = 2 * c + 1 - x

    started = []
    counter = [0]

    def remote(source, target, device):
        index = counter[0]
        counter[0] += 1
        return pltpu.make_async_remote_copy(
            src_ref=source,
            dst_ref=target,
            send_sem=R.sent.at[index],
            recv_sem=R.came.at[index],
            device_id=device,
            device_id_type=MESH,
        )

    def start(source, target, device):
        copy = remote(source, target, device)
        copy.start()
        started.append(copy)
        return copy

    def sent(copy):
        copy.wait_send()
        started[:] = [one for one in started if one is not copy]

    near, far = (ATT, 1, 0, width // 2), (ATT, 1, width // 2, width // 2)
    tin, tout = (TIN, 1, 0, width), (TOUT, 1, 0, width)
    tiles = range(width // 256)
    image = [(VIN, 2, j * 256, 256) for j in tiles]
    parts = [near, far, tin, tout] + image
    longest = half

    def hops(part, side):
        return half if (parts.index(part) + side) % 2 == 0 else n - 1 - half

    def ring_index(part, side, s):
        return (parts.index(part) * 2 + side) * longest + s

    def view(ref, part, rows):
        k, blocks, first, count = part
        return ref.at[pl.ds(k, blocks), rows, pl.ds(first, count)]

    sum_base = len(parts) * 2 * longest

    def gather_copy(part, side, s, pos):
        block = view(G, part, rows_at(pos))
        i = ring_index(part, side, s)
        return pltpu.make_async_remote_copy(
            src_ref=block,
            dst_ref=block,
            send_sem=R.ring_sent.at[part[0]],
            recv_sem=R.ring_came.at[i],
            device_id=way[side],
            device_id_type=MESH,
        )

    def gather(part, s):
        for side in range(2):
            pos = -s if side == 0 else s
            if 0 < s <= hops(part, side):
                gather_copy(part, side, s - 1, pos).wait_recv()
            if s < hops(part, side):
                gather_copy(part, side, s, pos).start()

    def landed(part, side, s):
        k, blocks, first, count = part
        return LAND.at[pl.ds(k, blocks), side * hops(part, 0) + s, :, pl.ds(first, count)]

    def sum_copy(part, side, s, source):
        i = sum_base + ring_index(part, side, s)
        return pltpu.make_async_remote_copy(
            src_ref=source,
            dst_ref=landed(part, side, s),
            send_sem=R.ring_sent.at[5 + part[0]],
            recv_sem=R.ring_came.at[i],
            device_id=way[side],
            device_id_type=MESH,
        )

    def pass_sum(part, s):
        for side in range(2):
            reach = hops(part, side)
            if s >= reach:
                continue
            pos = reach - s if side == 0 else s - reach
            term = view(PART, part, rows_at(pos))
            if s == 0:
                source = term
            else:
                source = landed(part, side, s - 1)
                sum_copy(part, side, s - 1, source).wait_recv()
                source[...] = (source[...].astype(F32) + term[...].astype(F32)).astype(BF)
            sum_copy(part, side, s, source).start()

    finals = []
    row_sums = [[], []]

    def end_sum(*group):
        for part in group:
            k, blocks, first, count = part
            ends = []
            for side in range(2):
                end = landed(part, side, hops(part, side) - 1)
                sum_copy(part, side, hops(part, side) - 1, end).wait_recv()
                ends.append(end)
            cols = slice(first, first + count)
            inside = slice(k, k + blocks)
            counted = min(3 * span - first, count) if k == ATT else count

            def total(core):
                rows = pl.ds(pl.multiple_of(own * core, 16), own)
                chip_rows = pl.ds(pl.multiple_of(2 * own * chip + own * core, 16), own)
                block = (
                    ends[0][:, rows, :].astype(F32)
                    + ends[1][:, rows, :].astype(F32)
                    + PART[inside, chip_rows, cols].astype(F32)
                )
                if k in (ATT, TIN, VIN):
                    weighted = G[k, chip_rows, cols].astype(F32)[:, :counted] * block[0][:, :counted]
                    row_sum = jnp.sum(weighted, axis=-1, keepdims=True)
                    row_sums[0 if core is c else 1].append((k, row_sum))
                return block

            R.give[inside, :, cols] = total(other)
            span_of = pl.ds(k, blocks), pl.ds(first, count)
            finals.append(
                start(
                    R.give.at[span_of[0], :, span_of[1]],
                    GW.at[span_of[0], c, :, span_of[1]],
                    mate,
                )
            )
            GW[inside, c, :, cols] = total(c)

    def shard_part(k, value):
        for core in range(2):
            S[k, core] = value(core).astype(BF)

    gain_one, gain_two = column(R.gain_attn), column(R.gain_ffn)

    def attention_part(core):
        cols = slice(core * span, (core + 1) * span)
        return jnp.concatenate(
            [
                R.w_query[:, cols].astype(F32) * (gain_one * HEAD_DIM**-0.5),
                R.w_key[:, cols].astype(F32) * gain_one,
                R.w_value[:, cols].astype(F32) * gain_one,
                R.w_out[:, cols].astype(F32),
            ],
            axis=1,
        )

    def half_of(ref, core):
        return ref[:, core * width : (core + 1) * width].astype(F32) * gain_two

    def turned_half(ref, core):
        return ref[:, core * width : (core + 1) * width]

    lengths = R.lengths

    def live(t, slots):
        return (slots < PATCHES) | ((slots >= VIS) & (slots < VIS + lengths[t]))

    def live_rows(t, j, count=64):
        slots = lax.broadcasted_iota(jnp.int32, (count, 1), 0) + j * count
        return live(t, slots).astype(F32)

    row_count = R.tokens.shape[0]

    def placed(t, slots, rows, kept):
        source = t * (PATCHES + CAPTION) + slots - (slots >= VIS).astype(jnp.int32) * (VIS - PATCHES)
        return ((rows == source) & kept).astype(F32).astype(BF)

    def chooser(t, only_live):
        slots = lax.broadcasted_iota(jnp.int32, (SEQ, row_count), 0)
        rows = lax.broadcasted_iota(jnp.int32, (SEQ, row_count), 1)
        filled = (slots < PATCHES) | ((slots >= VIS) & (slots < VIS + CAPTION))
        return placed(t, slots, rows, live(t, slots) if only_live else filled)

    shard_part(ATT, attention_part)
    G[ATT, my_rows, :] = S[ATT, c]
    for t in range(2):
        R.lens[t] = jnp.full((8, 128), lengths[t], jnp.int32).astype(F32)
    pl.semaphore_wait(barrier, 5)
    shard_a = start(S.at[pl.ds(0, 1), other], G.at[pl.ds(0, 1), my_rows, :], mate)
    send_lens = start(R.lens, R.lens4.at[pl.ds(mine, 2)], mate)
    fetched[0].wait()
    for t in range(2):
        R.x4[2 * c + t] = mm(chooser(t, False), R.tokens[...]).astype(BF)
        R.lens4[2 * c + t] = R.lens[t]
    send_x = start(R.x4.at[pl.ds(mine, 2)], R.x4.at[pl.ds(mine, 2)], mate)
    shard_a.wait_recv()
    gather(near, 0)
    gather(far, 0)
    for copy in fetched[1:]:
        copy.wait()

    shard_part(TIN, functools.partial(half_of, R.txt_in))
    shard_part(TOUT, functools.partial(turned_half, R.txt_out))
    shard_part(VIN, functools.partial(half_of, R.vis_in))
    shard_part(VOUT, functools.partial(turned_half, R.vis_out))
    shard_b = start(S.at[pl.ds(1, 4), other], G.at[pl.ds(1, 4), my_rows, :], mate)
    for k in (TIN, TOUT, VIN, VOUT):
        G[k, my_rows, :] = S[k, c]
    gather(near, 1)
    for t in range(2):
        R.gz[2 * c + t] = mm(chooser(t, True), R.cotangent[...]).astype(BF)
        if t == 0:
            gather(far, 1)
    send_gz = start(R.gz.at[pl.ds(mine, 2)], R.gz.at[pl.ds(mine, 2)], mate)
    R.dy[...] = mm(chooser(x, False), R.cotangent[...]).astype(BF)
    for t in range(2):
        R.x[t] = R.x4[2 * c + t]
    shard_b.wait_recv()
    gather(tin, 0)
    gather(near, 2)
    send_x.wait_recv()

    for i in range(4):

        @pl.loop(0, SEQ // 64, unroll=True)
        def _(j, i=i):
            rows = pl.ds(pl.multiple_of(j * 64, 64), 64)
            normed, _ = normalize(R.x4[i, rows, :].astype(F32))
            R.n1[i, rows, :] = normed.astype(BF)

        R.n1t[:, i * SEQ : (i + 1) * SEQ] = R.n1[i].T
        if i == 0:
            gather(far, 2)
        if i == 1:
            gather(tout, 0)
            gather(near, 3)
        if i == 2:
            gather(far, 3)
            gather(image[0], 0)
    send_gz.wait_recv()
    send_lens.wait_recv()
    gather(near, 4)
    gather(far, 4)

    R.wo[...] = G[ATT][:, 3 * span :]

    @pl.loop(0, 4)
    def _(i):
        projected = mm(R.n1[i], G[ATT][:, : 3 * span]).astype(BF)
        R.q[i] = projected[:, :span]
        R.k[i] = projected[:, span : 2 * span]
        R.v[i] = projected[:, 2 * span :]

    lane = lax.broadcasted_iota(jnp.int32, (1, span), 1) // HEAD_DIM

    def only(head, values):
        return values * (lane == head).astype(F32).astype(BF)

    def head_rows(values, head):
        return values[head * HEAD_DIM : (head + 1) * HEAD_DIM, :]

    order = []
    for j in range(4):
        core = other if j < 2 else c
        turn = 1 - x if j % 2 == 0 else x
        order.append((turn, 2 * core + turn))
    attn_mate = [remote(R.pa.at[i], R.ra.at[turn], mate) for turn, i in order[:2]]
    cross_a = remote(R.xs, R.xr, across)

    for j, (turn, i) in enumerate(order):
        q, k, v = R.q[i], R.k[i], R.v[i]
        turned_v = v.T
        slots = lax.broadcasted_iota(jnp.int32, (SEQ, 1), 0)
        caption = (slots - VIS).astype(F32) < R.lens4[i][:1, :1]
        bias = jnp.where((slots < PATCHES) | ((slots >= VIS) & caption), 0.0, -1e30)
        contexts = []
        for h in range(heads):
            scores = mm_nt(only(h, k), q) + bias
            top = jnp.max(scores, axis=0, keepdims=True)
            weights = jnp.exp(scores - top)
            total = jnp.sum(weights, axis=0, keepdims=True)
            probs = (weights * (1.0 / total)).astype(BF)
            R.probs[i * heads + h] = probs
            contexts.append(mm(head_rows(turned_v, h), probs))
        contexts = jnp.concatenate(contexts, axis=0)
        R.ct[:, pl.ds(pl.multiple_of(i * SEQ, SEQ), SEQ)] = contexts.astype(BF)
        context = contexts.T.astype(BF)
        R.pa[i] = mm_nt(context, R.wo[...]).astype(BF)
        if j < 2:
            attn_mate[j].start()
        if j == 2:
            attn_mate[0].wait_recv()
            R.xs[...] = (R.pa[pair_across].astype(F32) + R.ra[1 - x].astype(F32)).astype(BF)
            cross_a.start()
        if j == 0:
            gather(tin, 1)
        if j == 1:
            gather(tout, 1)
        if j == 3:
            gather(tin, 2)
            gather(tout, 2)

    for copy in attn_mate:
        copy.wait_send()
    attn_mate[1].wait_recv()

    @pl.loop(0, width // 256)
    def _(j):
        cols = pl.ds(pl.multiple_of(j * 256, 256), 256)
        R.gzvt[cols, :] = R.gz[:, :VIS, cols].reshape(4 * VIS, 256).T
        R.gztt[cols, :] = R.gz[:, VIS:, cols].reshape(4 * TXT, 256).T

    gather(image[0], 1)
    cross_a.wait_recv()

    @pl.loop(0, SEQ // 64, unroll=True)
    def _(j):
        rows = pl.ds(pl.multiple_of(j * 64, 64), 64)
        attended = (
            R.pa[pair_own, rows, :].astype(F32)
            + R.ra[x, rows, :].astype(F32)
            + R.xr[rows, :].astype(F32)
        )
        middle = R.x[x, rows, :].astype(F32) + live_rows(x, j) * attended
        R.y1[rows, :] = middle
        normed, _ = normalize(middle)
        R.n2[pair_own, rows, :] = normed.astype(BF)

    block = R.n2.at[pair_own]
    to_across = start(block, block, across)
    to_mate = start(block, block, mate)
    gather(tin, 3)
    gather(tout, 3)
    gather(image[1], 0)
    gather(image[0], 2)
    to_across.wait_recv()
    block = R.n2.at[pair_across]
    passed = start(block, block, mate)
    gather(image[1], 1)
    gather(image[0], 3)
    gather(image[2], 0)
    gather(tin, 4)
    gather(tout, 4)
    to_mate.wait_recv()
    passed.wait_recv()

    def expert(pairs, low, high, w_in, w_out, h_ref, gu_ref, j):
        first, count = pairs
        per = high - low
        total_rows = count * per
        cols = slice(j * 256, (j + 1) * 256)
        inside = slice(first, first + count)
        R.u[:total_rows, :] = mm(
            R.n2[inside, low:high, :].reshape(total_rows, width), G[w_in, :, cols]
        )
        R.gh[:total_rows, :] = mm(
            R.gz[inside, low:high, :].reshape(total_rows, width), G[w_out, :, cols]
        )
        step = min(total_rows, VIS)

        @pl.loop(0, 2 * (total_rows // step))
        def _(i):
            lanes = lax.rem(i, 2) * 128
            rows = pl.ds(pl.multiple_of(i // 2 * step, 16), step)
            into = pl.ds(pl.multiple_of(first * per + i // 2 * step, 16), step)
            side = pl.ds(pl.multiple_of(lanes, 128), 128)
            pre = R.u[rows, side]
            cumulative = 0.5 * (1.0 + lax.erf(pre * inv_root_two))
            density = jnp.exp(-0.5 * pre * pre) * inv_root_tau
            onto = pl.ds(pl.multiple_of(j * 256 + lanes, 128), 128)
            h_ref[into, onto] = (pre * cumulative).astype(BF)
            gu_ref[into, onto] = (R.gh[rows, side] * (cumulative + pre * density)).astype(BF)

    def weight_grad(k, turned, ref, j):
        cols = slice(j * 256, (j + 1) * 256)
        PART[k, :, cols] = mm(turned, ref[:, cols]).astype(BF)

    @pl.loop(0, width // 256)
    def _(j):
        cols = pl.ds(pl.multiple_of(j * 256, 256), 256)
        R.n2vt[cols, :] = R.n2[:, :VIS, cols].reshape(4 * VIS, 256).T
        R.n2tt[cols, :] = R.n2[:, VIS:, cols].reshape(4 * TXT, 256).T

    def image_expert(m, j):
        expert((2 * m, 2), 0, VIS, VIN, VOUT, R.hv, R.guv, j)

    def image_grad(j):
        weight_grad(VOUT, R.gzvt[...], R.hv, j)
        weight_grad(VIN, R.n2vt[...], R.guv, j)

    gather(image[1], 2)
    gather(image[0], 4)
    image_expert(0, 0)
    gather(image[2], 1)
    image_expert(1, 0)
    gather(image[1], 3)
    image_grad(0)
    gather(image[2], 2)
    gather(image[1], 4)
    image_expert(0, 1)
    image_expert(1, 1)
    gather(image[2], 3)
    image_grad(1)
    for j in tiles:
        expert((0, 4), VIS, SEQ, TIN, TOUT, R.ht, R.gut, j)
    pass_sum(image[0], 0)
    pass_sum(image[1], 0)

    def text_terms(target, rows, weight):
        target[:, VIS:, :] = mm_nt(rows, G[weight]).astype(BF).reshape(4, TXT, width)

    text_terms(R.pg, R.gut[...], TIN)
    text_terms(R.pf, R.ht[...], TOUT)
    gather(image[2], 4)

    def terms(target, rows, weight, m):
        part = mm_nt(rows[2 * m * VIS : 2 * (m + 1) * VIS, :], G[weight]).astype(BF)
        target[2 * m : 2 * m + 2, :VIS, :] = part.reshape(2, VIS, width)

    mate_g = remote(R.pg.at[pl.ds(theirs, 2)], R.rg, mate)
    cross_g = remote(R.xsg, R.xrg, across)
    gy_across = remote(R.gy.at[x], R.gy.at[x], across)
    gy_mate = remote(R.ga.at[pair_own], R.ga.at[pair_own], mate)
    gy_passed = remote(R.ga.at[pair_across], R.ga.at[pair_across], mate)
    started.extend([cross_g, gy_across, gy_mate, gy_passed])

    def image_terms(m):
        terms(R.pg, R.guv, VIN, m)
        pl.when(c != m)(mate_g.start)

    def sum_cores(m):
        @pl.when(c == m)
        def _():
            mate_g.wait_recv()
            R.xsg[...] = (R.pg[pair_across].astype(F32) + R.rg[1 - x].astype(F32)).astype(BF)
            cross_g.start()

    def middle_back(m):
        @pl.when(c == m)
        def _():
            cross_g.wait_recv()

            @pl.loop(0, SEQ // 64, unroll=True)
            def _(j):
                rows = pl.ds(pl.multiple_of(j * 64, 64), 64)
                grad_normed = (
                    R.pg[pair_own, rows, :].astype(F32)
                    + R.rg[x, rows, :].astype(F32)
                    + R.xrg[rows, :].astype(F32)
                )
                normed, inverse = normalize(R.y1[rows, :])
                grad = R.dy[rows, :].astype(F32) + normalize_back(grad_normed, normed, inverse)
                R.gy[x, rows, :] = grad.astype(BF)
                R.ga[pair_own, rows, :] = (grad * live_rows(x, j)).astype(BF)

            gy_across.start()
            gy_mate.start()

    def middle_pass(m):
        @pl.when(c == m)
        def _():
            gy_across.wait_recv()

            @pl.loop(0, SEQ // 64, unroll=True)
            def _(j):
                rows = pl.ds(pl.multiple_of(j * 64, 64), 64)
                R.ga[pair_across, rows, :] = (
                    R.gy[1 - x, rows, :].astype(F32) * live_rows(1 - x, j)
                ).astype(BF)

            gy_passed.start()

    def middle_came(m):
        @pl.when(c != m)
        def _():
            gy_mate.wait_recv()
            gy_passed.wait_recv()

    sent(send_x)
    cross_a.wait_send()
    image_expert(0, 2)
    image_terms(0)
    image_expert(1, 2)
    sum_cores(0)
    pass_sum(image[0], 1)
    image_terms(1)
    for copy in (to_across, to_mate, passed):
        sent(copy)
    sum_cores(1)
    pass_sum(image[1], 1)
    for j in tiles:
        weight_grad(TOUT, R.gztt[...], R.ht, j)
    pass_sum(tout, 0)
    middle_back(0)
    for j in tiles:
        weight_grad(TIN, R.n2tt[...], R.gut, j)
    pass_sum(tin, 0)
    pass_sum(image[0], 2)
    image_grad(2)
    pass_sum(image[2], 0)
    pass_sum(image[1], 2)

    terms(R.pf, R.hv, VOUT, 0)
    middle_pass(0)
    middle_back(1)
    pass_sum(tout, 1)
    terms(R.pf, R.hv, VOUT, 1)
    mate_f = start(R.pf.at[pl.ds(theirs, 2)], R.rf, mate)
    cross_f = remote(R.xsf, R.xrf, across)
    started.append(cross_f)
    pass_sum(image[0], 3)
    pass_sum(tin, 1)
    mate_g.wait_send()
    middle_came(0)

    back_mate = [remote(R.pb.at[theirs + t], R.rb.at[t], mate) for t in range(2)]
    back_cross = [remote(R.xsb.at[t], R.xrb.at[t], across) for t in range(2)]
    started.extend(back_mate + back_cross)

    def attention_back(m, t):
        i = 2 * m + t
        grad_context = mm(R.ga[i], R.wo[...]).astype(BF)
        q, k, v = R.q[i], R.k[i], R.v[i]
        turned_k = k.T
        grad_q = []
        grad_k = jnp.zeros((SEQ, span), F32)
        grad_v = jnp.zeros((SEQ, span), F32)
        for h in range(heads):
            probs = R.probs[i * heads + h]
            grad_probs = mm_nt(only(h, v), grad_context)
            exact = probs.astype(F32)
            inner = jnp.sum(grad_probs * exact, axis=0, keepdims=True)
            grad_scores = (exact * (grad_probs - inner)).astype(BF)
            grad_q.append(mm(head_rows(turned_k, h), grad_scores))
            grad_k += mm(grad_scores, only(h, q))
            grad_v += mm(probs, only(h, grad_context))
        grad_q = jnp.concatenate(grad_q, axis=0).T
        joined = jnp.concatenate([grad_q, grad_k, grad_v], axis=1).astype(BF)
        R.gqkv[i, :, : 3 * span] = joined
        R.pb[i] = mm_nt(joined, G[ATT][:, : 3 * span]).astype(BF)
        pl.when(c != m)(back_mate[t].start)

    def back_sum(m, t):
        @pl.when(c == m)
        def _():
            back_mate[t].wait_recv()
            R.xsb[t] = (R.pb[2 * m + t].astype(F32) + R.rb[t].astype(F32)).astype(BF)
            back_cross[t].start()

    attention_back(0, 0)
    pass_sum(image[1], 3)
    pass_sum(image[2], 1)
    mate_f.wait_recv()
    R.xsf[...] = (R.pf[pair_across].astype(F32) + R.rf[1 - x].astype(F32)).astype(BF)
    R.fown[...] = (R.pf[pair_own].astype(F32) + R.rf[x].astype(F32)).astype(BF)
    middle_pass(1)
    cross_f.start()
    attention_back(0, 1)
    back_sum(0, 0)

    pass_sum(tout, 2)
    middle_came(1)
    attention_back(1, 0)
    back_sum(0, 1)

    pass_sum(tin, 2)
    pass_sum(image[2], 2)
    attention_back(1, 1)
    back_sum(1, 0)
    pass_sum(tout, 3)

    lanes = width // 2

    @pl.loop(0, width // 256)
    def _(j):
        rows = pl.ds(pl.multiple_of(j * 256, 256), 256)
        grad_v = mm(R.n1t[rows, :], R.gqkv[:, :, lanes : 3 * span].reshape(4 * SEQ, span))
        grad_o = mm(R.ct[...], R.ga[:, :, rows].reshape(4 * SEQ, 256)).T
        PART[ATT, rows, lanes:] = jnp.concatenate([grad_v, grad_o], axis=1).astype(BF)

    pass_sum(far, 0)

    cross_f.wait_recv()

    @pl.loop(0, SEQ // 64, unroll=True)
    def _(j):
        rows = pl.ds(pl.multiple_of(j * 64, 64), 64)
        branch = R.fown[rows, :].astype(F32) + R.xrf[rows, :].astype(F32)
        OUT[x, rows, :] = (R.y1[rows, :] + live_rows(x, j) * branch).astype(BF)

    out_across = start(OUT.at[x], OUT.at[x], across)

    @pl.loop(0, width // 256)
    def _(j):
        rows = pl.ds(pl.multiple_of(j * 256, 256), 256)
        grads = mm(R.n1t[rows, :], R.gqkv[:, :, :lanes].reshape(4 * SEQ, lanes))
        PART[ATT, rows, :lanes] = grads.astype(BF)

    pass_sum(near, 0)
    back_sum(1, 1)
    pass_sum(tin, 3)
    pass_sum(image[2], 3)

    def input_back(m, t):
        @pl.when(c == m)
        def _():
            back_cross[t].wait_recv()

            @pl.loop(0, SEQ // 64, unroll=True)
            def _(j):
                rows = pl.ds(pl.multiple_of(j * 64, 64), 64)
                grad_normed = R.xsb[t, rows, :].astype(F32) + R.xrb[t, rows, :].astype(F32)
                normed, inverse = normalize(R.x[t, rows, :].astype(F32))
                grad = R.gy[t, rows, :].astype(F32) + normalize_back(grad_normed, normed, inverse)
                high = grad.astype(BF)
                rows = pl.ds(pl.multiple_of(t * SEQ + j * 64, 64), 64)
                R.hv[rows, :] = high
                R.guv[rows, :] = (grad - high.astype(F32)).astype(BF)

    pass_sum(far, 1)
    input_back(0, 0)
    pass_sum(near, 1)
    input_back(0, 1)
    end_sum(image[0], image[1])
    pass_sum(far, 2)
    pass_sum(near, 2)
    end_sum(tout, tin, image[2])

    leaving = []

    def leave(slot, source, target):
        leaving.append(fetch(slot, source, target))

    slots = lax.broadcasted_iota(jnp.int32, (row_count, 2 * SEQ), 1)
    rows = lax.broadcasted_iota(jnp.int32, (row_count, 2 * SEQ), 0)
    turn = slots // SEQ
    back = placed(turn, slots - turn * SEQ, rows, slots >= 0)
    out_across.wait_recv()
    R.out_tokens[...] = mm(back, OUT[...].reshape(2 * SEQ, width)).astype(BF)
    leave(6, R.out_tokens, R.out_tokens_hbm)
    for copy in finals:
        copy.wait_recv()
    finals.clear()
    leave(7, GW.at[pl.ds(1, 4)], R.gw_hbm.at[pl.ds(1, 4)])
    pass_sum(far, 3)
    pass_sum(near, 3)
    input_back(1, 0)
    input_back(1, 1)
    R.grad_tokens[...] = mm(back, R.hv[: 2 * SEQ, :]) + mm(back, R.guv[: 2 * SEQ, :])
    leave(8, R.grad_tokens, R.grad_tokens_hbm)
    end_sum(far, near)

    first_lane = lax.broadcasted_iota(jnp.int32, (own, 128), 1) == 0
    for place in range(2):
        attn = sum(total for k, total in row_sums[place] if k == ATT)
        experts = sum(total for k, total in row_sums[place] if k != ATT)
        R.gs[place] = jnp.where(first_lane, attn, experts)
    peers = [
        start(R.gs.at[place], R.gr.at[slot], device)
        for slot, (place, device) in enumerate(((1, mate), (0, across), (1, diagonal)))
    ]
    for copy in finals + peers:
        copy.wait_recv()
    leave(9, GW.at[pl.ds(0, 1)], R.gw_hbm.at[pl.ds(0, 1)])
    GG[...] = (R.gs[0] + R.gr[1]) + (R.gr[0] + R.gr[2])

    for copy in started:
        copy.wait_send()
    for copy in leaving:
        copy.wait()
    for k, blocks in ((ATT, 1), (TIN, 1), (TOUT, 1), (VIN, 2)):
        for semaphore in (k, 5 + k):
            places = LAND.at[pl.ds(k, blocks)]
            pltpu.make_async_remote_copy(
                src_ref=places,
                dst_ref=places,
                send_sem=R.ring_sent.at[semaphore],
                recv_sem=R.ring_came.at[0],
                device_id=ahead,
                device_id_type=MESH,
            ).wait_send()


def finish_kernel(n_results, out, gtok, gw_hbm, gg, gain_attn, gain_ffn, *rest):
    results, scratch = rest[:n_results], rest[n_results:]
    buffers, (out_buffer, gtok_buffer, gw, came, gone) = scratch[:n_results], scratch[n_results:]
    arriving = [
        pltpu.make_async_copy(source, target, came.at[slot])
        for slot, (source, target) in enumerate(((gw_hbm, gw), (out, out_buffer), (gtok, gtok_buffer)))
    ]
    for copy in arriving:
        copy.start()
    width = gw.shape[3]
    own = gw.shape[2]
    span = width // 4
    gain_one, gain_two = column(gain_attn), column(gain_ffn)
    square = unit(own).astype(F32)
    leaving = []

    def leave(slot, source):
        copy = pltpu.make_async_copy(source, results[slot], gone.at[slot])
        copy.start()
        leaving.append(copy)

    def both(part):
        cols = slice(part * span, (part + 1) * span)
        return jnp.concatenate([gw[ATT, core][:, cols] for core in range(2)], axis=1)

    def put(slot, value):
        buffers[slot][...] = value
        leave(slot, buffers[slot])

    put(2, jnp.sum(square * (gg[:, :1] / gain_one), axis=0, keepdims=True))
    put(7, jnp.sum(square * (gg[:, 1:2] / gain_two), axis=0, keepdims=True))
    arriving[0].wait()
    for slot, k, scale in ((8, VIN, gain_two), (9, VOUT, 1.0), (10, TIN, gain_two), (11, TOUT, 1.0)):
        put(slot, jnp.concatenate([gw[k, 0], gw[k, 1]], axis=1) * scale)
    put(3, both(0) * (gain_one * HEAD_DIM**-0.5))
    put(4, both(1) * gain_one)
    put(5, both(2) * gain_one)
    put(6, both(3))
    arriving[1].wait()
    leave(0, out_buffer)
    arriving[2].wait()
    leave(1, gtok_buffer)
    for copy in leaving:
        copy.wait()


def fused_layer(
    tokens,
    caption_lengths,
    gain_attn,
    w_query,
    w_key,
    w_value,
    w_out,
    gain_ffn,
    vis_in,
    vis_out,
    txt_in,
    txt_out,
    cotangent,
):
    n = lax.axis_size("dp") // 2
    own = w_query.shape[0]
    row_count, width = tokens.shape
    span = width // 4
    heads = span // HEAD_DIM
    gain_one, gain_two = gain_attn.reshape(1, own), gain_ffn.reshape(1, own)

    rows = 4 * SEQ
    scratch = dict(
        tokens=pltpu.VMEM((row_count, width), BF),
        cotangent=pltpu.VMEM((row_count, width), BF),
        txt_in=pltpu.VMEM((own, 2 * width), BF),
        txt_out=pltpu.VMEM((own, 2 * width), BF),
        vis_in=pltpu.VMEM((own, 2 * width), BF),
        vis_out=pltpu.VMEM((own, 2 * width), BF),
        out_tokens=pltpu.VMEM((row_count, width), BF),
        grad_tokens=pltpu.VMEM((row_count, width), F32),
        gw=pltpu.VMEM((5, 2, own, width), F32),
        local=pltpu.SemaphoreType.DMA((10,)),
        shard=pltpu.VMEM((5, 2, own, width), BF),
        lens=pltpu.VMEM((2, 8, 128), F32),
        x=pltpu.VMEM((2, SEQ, width), BF),
        dy=pltpu.VMEM((SEQ, width), BF),
        padded_out=pltpu.VMEM((2, SEQ, width), BF),
        gathered=pltpu.VMEM((5, width, width), BF),
        part=pltpu.VMEM((5, width, width), BF),
        land=pltpu.VMEM((5, n - 1, 2 * own, width), BF),
        give=pltpu.VMEM((5, own, width), F32),
        x4=pltpu.VMEM((4, SEQ, width), BF),
        lens4=pltpu.VMEM((4, 8, 128), F32),
        n1=pltpu.VMEM((4, SEQ, width), BF),
        n1t=pltpu.VMEM((width, rows), BF),
        gz=pltpu.VMEM((4, SEQ, width), BF),
        gzvt=pltpu.VMEM((width, 4 * VIS), BF),
        ct=pltpu.VMEM((span, rows), BF),
        fown=pltpu.VMEM((SEQ, width), BF),
        gztt=pltpu.VMEM((width, 4 * TXT), BF),
        wo=pltpu.VMEM((width, span), BF),
        q=pltpu.VMEM((4, SEQ, span), BF),
        k=pltpu.VMEM((4, SEQ, span), BF),
        v=pltpu.VMEM((4, SEQ, span), BF),
        probs=pltpu.VMEM((4 * heads, SEQ, SEQ), BF),
        pa=pltpu.VMEM((4, SEQ, width), BF),
        ra=pltpu.VMEM((2, SEQ, width), BF),
        xs=pltpu.VMEM((SEQ, width), BF),
        xr=pltpu.VMEM((SEQ, width), BF),
        y1=pltpu.VMEM((SEQ, width), F32),
        n2vt=pltpu.VMEM((width, 4 * VIS), BF),
        n2tt=pltpu.VMEM((width, 4 * TXT), BF),
        u=pltpu.VMEM((4 * VIS, 256), F32),
        gh=pltpu.VMEM((4 * VIS, 256), F32),
        hv=pltpu.VMEM((4 * VIS, width), BF),
        guv=pltpu.VMEM((4 * VIS, width), BF),
        ht=pltpu.VMEM((4 * TXT, width), BF),
        gut=pltpu.VMEM((4 * TXT, width), BF),
        pg=pltpu.VMEM((4, SEQ, width), BF),
        rg=pltpu.VMEM((2, SEQ, width), BF),
        gy=pltpu.VMEM((2, SEQ, width), BF),
        xsf=pltpu.VMEM((SEQ, width), BF),
        xrf=pltpu.VMEM((SEQ, width), BF),
        xsb=pltpu.VMEM((2, SEQ, width), BF),
        xrb=pltpu.VMEM((2, SEQ, width), BF),
        gs=pltpu.VMEM((2, own, 128), F32),
        gr=pltpu.VMEM((3, own, 128), F32),
        sent=pltpu.SemaphoreType.DMA((40,)),
        came=pltpu.SemaphoreType.DMA((40,)),
        ring_sent=pltpu.SemaphoreType.DMA((10,)),
        ring_came=pltpu.SemaphoreType.DMA((7 * 2 * (n // 2) * 2,)),
    )
    inputs = dict(
        lengths=caption_lengths,
        tokens_hbm=tokens,
        cotangent_hbm=cotangent,
        gain_attn=gain_one,
        gain_ffn=gain_two,
        w_query=w_query,
        w_key=w_key,
        w_value=w_value,
        w_out=w_out.T,
        vis_in_hbm=vis_in,
        vis_out_hbm=vis_out.T,
        txt_in_hbm=txt_in,
        txt_out_hbm=txt_out.T,
    )
    results = dict(
        out_tokens_hbm=jax.ShapeDtypeStruct((row_count, width), BF),
        grad_tokens_hbm=jax.ShapeDtypeStruct((row_count, width), F32),
        gw_hbm=jax.ShapeDtypeStruct((5, 2, own, width), F32),
        gg=jax.ShapeDtypeStruct((own, 128), F32),
    )
    vmem, hbm = pl.BlockSpec(memory_space=pltpu.VMEM), pl.BlockSpec(memory_space=pl.ANY)
    names = tuple(inputs) + tuple(results) + tuple(scratch)
    out, gtok, gw, gg = pl.pallas_call(
        functools.partial(layer_kernel, n, names),
        out_shape=tuple(results.values()),
        in_specs=[pl.BlockSpec(memory_space=pltpu.SMEM)] + [hbm if k.endswith(HBM) else vmem for k in names[1 : len(inputs)]],
        out_specs=[hbm if k.endswith(HBM) else vmem for k in results],
        scratch_shapes=list(scratch.values()),
        compiler_params=pltpu.CompilerParams(
            collective_id=0, has_side_effects=True, vmem_limit_bytes=60 * 2**20
        ),
    )(*inputs.values())

    shapes = (
        jax.ShapeDtypeStruct((row_count, width), BF),
        jax.ShapeDtypeStruct((row_count, width), F32),
        jax.ShapeDtypeStruct((1, own), F32),
        jax.ShapeDtypeStruct((own, 2 * span), F32),
        jax.ShapeDtypeStruct((own, 2 * span), F32),
        jax.ShapeDtypeStruct((own, 2 * span), F32),
        jax.ShapeDtypeStruct((own, 2 * span), F32),
        jax.ShapeDtypeStruct((1, own), F32),
        jax.ShapeDtypeStruct((own, 2 * width), F32),
        jax.ShapeDtypeStruct((own, 2 * width), F32),
        jax.ShapeDtypeStruct((own, 2 * width), F32),
        jax.ShapeDtypeStruct((own, 2 * width), F32),
    )
    buffers = [pltpu.VMEM(one.shape if slot > 1 else (8, 128), F32) for slot, one in enumerate(shapes)]
    final = pl.pallas_call(
        functools.partial(finish_kernel, len(shapes)),
        out_shape=shapes,
        in_specs=[hbm] * 3 + [vmem] * 3,
        out_specs=[hbm] * len(shapes),
        scratch_shapes=buffers
        + [
            pltpu.VMEM((row_count, width), BF),
            pltpu.VMEM((row_count, width), F32),
            pltpu.VMEM((5, 2, own, width), F32),
            pltpu.SemaphoreType.DMA((3,)),
            pltpu.SemaphoreType.DMA((len(shapes),)),
        ],
        compiler_params=pltpu.CompilerParams(vmem_limit_bytes=60 * 2**20),
    )(out, gtok, gw, gg, gain_one, gain_two)
    final = list(final)
    final[2] = final[2].reshape(own)
    final[7] = final[7].reshape(own)
    for turned in (6, 9, 11):
        final[turned] = final[turned].T
    return tuple(final)


def norm_parts(values):
    center = values - jnp.mean(values, axis=-1, keepdims=True)
    spread = jnp.mean(center * center, axis=-1, keepdims=True)
    inverse = lax.rsqrt(spread + epsilon)
    return (center * inverse, inverse)


def norm_back(grad_out, normed, inverse, gain):
    grad_normed = grad_out * gain
    grad_gain = jnp.sum(grad_out * normed, axis=0)
    inner = (
        grad_normed
        - jnp.mean(grad_normed, axis=-1, keepdims=True)
        - normed * jnp.mean(grad_normed * normed, axis=-1, keepdims=True)
    )
    return (inverse * inner, grad_gain)


def matmul(left, right):
    return jnp.dot(left, right, preferred_element_type=jnp.float32)


def matmul_tn(left, right):
    return lax.dot_general(
        left, right, (((0,), (0,)), ((), ())), preferred_element_type=jnp.float32
    )


def matmul_nt(left, right):
    return lax.dot_general(
        left, right, (((1,), (1,)), ((), ())), preferred_element_type=jnp.float32
    )


def gelu_slope(pre):
    cumulative = 0.5 * (1.0 + lax.erf(pre * inv_root_two))
    density = jnp.exp(-0.5 * pre * pre) * inv_root_tau
    return cumulative + pre * density


def expert_forward(rows, weight_in, weight_out):
    pre = matmul(rows, weight_in)
    hidden = jax.nn.gelu(pre, approximate=False).astype(jnp.bfloat16)
    return (pre, hidden, matmul(hidden, weight_out))


def expert_backward(rows, pre, hidden, grad_out, weight_in, weight_out):
    grad_weight_out = matmul_tn(hidden, grad_out)
    grad_hidden = matmul_nt(grad_out, weight_out)
    grad_pre = (grad_hidden * gelu_slope(pre)).astype(jnp.bfloat16)
    return (matmul_tn(rows, grad_pre), grad_weight_out, matmul_nt(grad_pre, weight_in))


def join_experts(image_rows, text_rows, pair_count, width):
    joined = jnp.concatenate(
        [
            image_rows.reshape(pair_count, PATCHES, width),
            text_rows.reshape(pair_count, CAPTION, width),
        ],
        axis=1,
    )
    return joined.reshape(-1, width)


def plain_layer(
    tokens,
    caption_lengths,
    gain_attn,
    w_query,
    w_key,
    w_value,
    w_out,
    gain_ffn,
    vis_in,
    vis_out,
    txt_in,
    txt_out,
    cotangent,
):
    seq_len = PATCHES + CAPTION
    width = tokens.shape[1]
    pair_count = tokens.shape[0] // seq_len
    half_pairs = pair_count // lax.axis_size("tensor")
    half_rows = half_pairs * seq_len
    row_start = lax.axis_index("tensor") * half_rows
    gain_one, query_w, key_w, value_w, out_w = (
        lax.all_gather(gain_attn, "dp", axis=0, tiled=True),
        lax.all_gather(w_query, "dp", axis=0, tiled=True),
        lax.all_gather(w_key, "dp", axis=0, tiled=True),
        lax.all_gather(w_value, "dp", axis=0, tiled=True),
        lax.all_gather(w_out, "dp", axis=1, tiled=True),
    )
    gain_two, vis_in_w, vis_out_w, txt_in_w, txt_out_w = (
        lax.all_gather(gain_ffn, "dp", axis=0, tiled=True),
        lax.all_gather(vis_in, "dp", axis=0, tiled=True),
        lax.all_gather(vis_out, "dp", axis=1, tiled=True),
        lax.all_gather(txt_in, "dp", axis=0, tiled=True),
        lax.all_gather(txt_out, "dp", axis=1, tiled=True),
    )
    gain_one = gain_one.astype(jnp.float32)
    gain_two = gain_two.astype(jnp.float32)
    head_local = query_w.shape[1] // HEAD_DIM
    score_scale = HEAD_DIM ** (-0.5)
    position = jnp.arange(seq_len, dtype=jnp.int32)
    live = (position[None, :] < PATCHES) | (position[None, :] - PATCHES < caption_lengths[:, None])
    valid_rows = live.astype(jnp.float32)
    mask_col = valid_rows.reshape(-1, 1)
    key_live = valid_rows[:, None, None, :] > 0.5

    def own_rows(values):
        return lax.dynamic_slice_in_dim(values, row_start, half_rows, 0)

    inputs = tokens.astype(jnp.float32)
    normed_one, inverse_one = norm_parts(inputs)
    first_in = (normed_one * gain_one).astype(jnp.bfloat16)

    def project(weight):
        return (
            matmul(first_in, weight)
            .astype(jnp.bfloat16)
            .reshape(pair_count, seq_len, head_local, HEAD_DIM)
        )

    queries = project(query_w)
    keys_all = project(key_w)
    values_all = project(value_w)

    def score_block():
        raw = (
            jnp.einsum("pqhe,pkhe->phqk", queries, keys_all, preferred_element_type=jnp.float32)
            * score_scale
        )
        return jnp.where(key_live, raw, -1e30)

    scores = score_block()
    top = jnp.max(scores, axis=-1, keepdims=True)
    weights = jnp.exp(scores - top)
    total = jnp.sum(weights, axis=-1, keepdims=True)
    probs = (weights / total).astype(jnp.bfloat16)
    log_total = top + jnp.log(total)
    context = jnp.einsum("phqk,pkhe->pqhe", probs, values_all, preferred_element_type=jnp.float32)
    context = context.astype(jnp.bfloat16).reshape(-1, head_local * HEAD_DIM)
    attn_terms = matmul(context, out_w)
    attended_own = lax.psum_scatter(
        attn_terms.astype(jnp.bfloat16), "tensor", scatter_dimension=0, tiled=True
    ).astype(jnp.float32)
    mask_own = own_rows(mask_col)
    middle_own = own_rows(inputs) + mask_own * attended_own
    normed_two, inverse_two = norm_parts(middle_own)
    second_own = (normed_two * gain_two).astype(jnp.bfloat16)
    grid = lax.all_gather(second_own, "tensor", axis=0, tiled=True).reshape(
        pair_count, seq_len, width
    )
    image_rows = grid[:, :PATCHES].reshape(-1, width)
    text_rows = grid[:, PATCHES:].reshape(-1, width)
    image_pre, image_hidden, image_part = expert_forward(image_rows, vis_in_w, vis_out_w)
    text_pre, text_hidden, text_part = expert_forward(text_rows, txt_in_w, txt_out_w)
    image_own, text_own = (
        lax.psum_scatter(
            image_part.astype(jnp.bfloat16), "tensor", scatter_dimension=0, tiled=True
        ).astype(jnp.float32),
        lax.psum_scatter(
            text_part.astype(jnp.bfloat16), "tensor", scatter_dimension=0, tiled=True
        ).astype(jnp.float32),
    )
    branch_own = join_experts(image_own, text_own, half_pairs, width)
    output_own = (middle_own + mask_own * branch_own).astype(jnp.bfloat16)
    upstream = cotangent.astype(jnp.float32)
    grad_branch = (upstream * mask_col).astype(jnp.bfloat16).reshape(pair_count, seq_len, width)
    image_grads = expert_backward(
        image_rows,
        image_pre,
        image_hidden,
        grad_branch[:, :PATCHES].reshape(-1, width),
        vis_in_w,
        vis_out_w,
    )
    text_grads = expert_backward(
        text_rows,
        text_pre,
        text_hidden,
        grad_branch[:, PATCHES:].reshape(-1, width),
        txt_in_w,
        txt_out_w,
    )
    back_image_own, back_text_own = (
        lax.psum_scatter(
            image_grads[2].astype(jnp.bfloat16), "tensor", scatter_dimension=0, tiled=True
        ).astype(jnp.float32),
        lax.psum_scatter(
            text_grads[2].astype(jnp.bfloat16), "tensor", scatter_dimension=0, tiled=True
        ).astype(jnp.float32),
    )
    grad_second_own = join_experts(back_image_own, back_text_own, half_pairs, width)
    grad_norm_own, gain_part = norm_back(grad_second_own, normed_two, inverse_two, gain_two)
    grad_middle_own = own_rows(upstream) + grad_norm_own
    output_wide, grad_middle, gain_parts = (
        lax.all_gather(
            output_own.astype(jnp.float32).astype(jnp.bfloat16), "tensor", axis=0, tiled=True
        ).astype(jnp.float32),
        lax.all_gather(grad_middle_own.astype(jnp.bfloat16), "tensor", axis=0, tiled=True).astype(
            grad_middle_own.dtype
        ),
        lax.all_gather(gain_part.astype(jnp.bfloat16), "tensor", axis=0, tiled=True).astype(
            gain_part.dtype
        ),
    )
    output = output_wide.astype(jnp.bfloat16)
    grad_gain_two = jnp.sum(gain_parts.reshape(-1, width), axis=0)
    grad_attended = (grad_middle * mask_col).astype(jnp.bfloat16)
    grad_out_w = matmul_tn(context, grad_attended)
    grad_context = (
        matmul_nt(grad_attended, out_w)
        .astype(jnp.bfloat16)
        .reshape(pair_count, seq_len, head_local, HEAD_DIM)
    )
    scores_again = score_block()
    probs_exact = jnp.exp(scores_again - log_total)
    grad_probs = jnp.einsum(
        "pqhe,pkhe->phqk", grad_context, values_all, preferred_element_type=jnp.float32
    )
    inner = jnp.sum(grad_probs * probs_exact, axis=-1, keepdims=True)
    grad_scores = (probs_exact * (grad_probs - inner)).astype(jnp.bfloat16)
    grad_values = jnp.einsum(
        "phqk,pqhe->pkhe", probs, grad_context, preferred_element_type=jnp.float32
    )
    grad_values = grad_values.astype(jnp.bfloat16).reshape(-1, head_local * HEAD_DIM)
    grad_queries = (
        jnp.einsum("phqk,pkhe->pqhe", grad_scores, keys_all, preferred_element_type=jnp.float32)
        * score_scale
    )
    grad_queries = grad_queries.astype(jnp.bfloat16).reshape(-1, head_local * HEAD_DIM)
    grad_keys = (
        jnp.einsum("phqk,pqhe->pkhe", grad_scores, queries, preferred_element_type=jnp.float32)
        * score_scale
    )
    grad_keys = grad_keys.astype(jnp.bfloat16).reshape(-1, head_local * HEAD_DIM)
    grad_query_w = matmul_tn(first_in, grad_queries)
    grad_key_w = matmul_tn(first_in, grad_keys)
    grad_value_w = matmul_tn(first_in, grad_values)
    first_part = (
        matmul_nt(grad_queries, query_w)
        + matmul_nt(grad_keys, key_w)
        + matmul_nt(grad_values, value_w)
    )
    grad_first = lax.psum(first_part.astype(jnp.bfloat16), "tensor").astype(jnp.float32)
    grad_norm_one, grad_gain_one = norm_back(grad_first, normed_one, inverse_one, gain_one)
    grad_inputs = grad_middle + grad_norm_one
    attn_sent = (
        lax.psum_scatter(grad_gain_one, "dp", scatter_dimension=0, tiled=True),
        lax.psum_scatter(grad_query_w, "dp", scatter_dimension=0, tiled=True),
        lax.psum_scatter(grad_key_w, "dp", scatter_dimension=0, tiled=True),
        lax.psum_scatter(grad_value_w, "dp", scatter_dimension=0, tiled=True),
        lax.psum_scatter(grad_out_w, "dp", scatter_dimension=1, tiled=True),
    )
    final_expert = (
        lax.psum_scatter(grad_gain_two, "dp", scatter_dimension=0, tiled=True),
        lax.psum_scatter(image_grads[0], "dp", scatter_dimension=0, tiled=True),
        lax.psum_scatter(image_grads[1], "dp", scatter_dimension=1, tiled=True),
        lax.psum_scatter(text_grads[0], "dp", scatter_dimension=0, tiled=True),
        lax.psum_scatter(text_grads[1], "dp", scatter_dimension=1, tiled=True),
    )
    return (
        output,
        grad_inputs,
        attn_sent[0],
        attn_sent[1],
        attn_sent[2],
        attn_sent[3],
        attn_sent[4],
        final_expert[0],
        final_expert[1],
        final_expert[2],
        final_expert[3],
        final_expert[4],
    )


def solution(mesh):
    def local(tokens, lengths, gain, w_query, *rest):
        ring = mesh.shape["dp"] // 2
        fits = (
            mesh.shape["tensor"] == 2
            and ring == 8
            and lengths.shape[0] == 2
            and w_query.shape[0] % 16 == 0
        )
        layer = fused_layer if fits else plain_layer
        return layer(tokens, lengths, gain, w_query, *rest)

    return jax.shard_map(
        local,
        mesh=mesh,
        in_specs=(
            P("dp", None),
            P("dp"),
            P("dp"),
            P("dp", "tensor"),
            P("dp", "tensor"),
            P("dp", "tensor"),
            P("tensor", "dp"),
            P("dp"),
            P("dp", "tensor"),
            P("tensor", "dp"),
            P("dp", "tensor"),
            P("tensor", "dp"),
            P("dp", None),
        ),
        out_specs=(
            P("dp", None),
            P("dp", None),
            P("dp"),
            P("dp", "tensor"),
            P("dp", "tensor"),
            P("dp", "tensor"),
            P("tensor", "dp"),
            P("dp"),
            P("dp", "tensor"),
            P("tensor", "dp"),
            P("dp", "tensor"),
            P("tensor", "dp"),
        ),
        check_vma=False,
    )
```

```python
import functools
import math
import types

import jax
import jax.numpy as jnp
from jax import lax
from jax.experimental import pallas as pl
from jax.experimental.pallas import tpu as pltpu
from jax.sharding import PartitionSpec as P

HEAD_DIM = 64
PATCHES = 197
CAPTION = 40
VIS = 208
TXT = 48
SEQ = VIS + TXT

MESH = pl.DeviceIdType.MESH
HBM = "_hbm"
BF = jnp.bfloat16
F32 = jnp.float32

ATT, TIN, TOUT, VIN, VOUT = range(5)

epsilon = 1e-05
inv_root_two = 1.0 / math.sqrt(2.0)
inv_root_tau = 1.0 / math.sqrt(2.0 * math.pi)


def mm(left, right):
    return jnp.dot(left, right, preferred_element_type=F32)


def mm_nt(left, right):
    return lax.dot_general(left, right, (((1,), (1,)), ((), ())), preferred_element_type=F32)


def mm_tn(left, right):
    return lax.dot_general(left, right, (((0,), (0,)), ((), ())), preferred_element_type=F32)


def normalize(values):
    center = values - jnp.mean(values, axis=-1, keepdims=True)
    spread = jnp.mean(center * center, axis=-1, keepdims=True)
    inverse = lax.rsqrt(spread + epsilon)
    return center * inverse, inverse


def normalize_back(grad_normed, normed, inverse):
    return inverse * (
        grad_normed
        - jnp.mean(grad_normed, axis=-1, keepdims=True)
        - normed * jnp.mean(grad_normed * normed, axis=-1, keepdims=True)
    )


def unit(size):
    rows = lax.broadcasted_iota(jnp.int32, (size, size), 0)
    return (rows == lax.broadcasted_iota(jnp.int32, (size, size), 1)).astype(F32).astype(BF)


def column(ref):
    size = ref.shape[1]
    return jnp.sum(unit(size).astype(F32) * ref[...].astype(F32), axis=1, keepdims=True)


def layer_kernel(n, names, *refs):
    R = types.SimpleNamespace(**dict(zip(names, refs)))
    R.pb, R.pf, R.ga, R.rf, R.rb, R.n2 = R.pg, R.pa, R.x4, R.ra, R.rg, R.n1
    R.gqkv, R.xsg, R.xrg = R.n2, R.xs, R.xr
    S, G, PART, LAND = R.shard, R.gathered, R.part, R.land
    OUT, GW, GG = R.padded_out, R.gw, R.gg
    width = G.shape[2]
    own = width // (2 * n)
    span = width // 4
    heads = span // HEAD_DIM

    x = lax.axis_index("tensor")
    d = lax.axis_index("dp")
    c = lax.rem(d, 2)
    other = 1 - c
    chip = d // 2
    y, z = lax.rem(chip, 2), chip // 2
    r = z + y * (n - 1 - 2 * z)
    half = n // 2

    def chip_at(pos):
        pos = lax.rem(pos + 2 * n, n)
        upper = pos // half
        return 2 * (pos + upper * (n - 1 - 2 * pos)) + upper

    near_mate = d + 1 - 2 * c
    mate, across, diagonal = (near_mate, x), (d, 1 - x), (near_mate, 1 - x)
    ahead = (2 * chip_at(r + 1) + c, x)
    behind = (2 * chip_at(r - 1) + c, x)
    way = (ahead, behind)

    offsets = {hop: 2 * own * chip_at(r + hop) for hop in range(-half, half + 1)}


    my_rows = pl.ds(pl.multiple_of(own * d, 16), own)

    def fetch(slot, source, target):
        copy = pltpu.make_async_copy(source, target, R.local.at[slot])
        copy.start()
        return copy

    fetched = [
        fetch(0, R.tokens_hbm, R.tokens),
        fetch(1, R.txt_in_hbm, R.txt_in),
        fetch(2, R.txt_out_hbm, R.txt_out),
        fetch(3, R.vis_in_hbm, R.vis_in),
        fetch(4, R.vis_out_hbm, R.vis_out),
        fetch(5, R.cotangent_hbm, R.cotangent),
    ]

    barrier = pltpu.get_barrier_semaphore()
    for device in (mate, across, diagonal, ahead, behind):
        pl.semaphore_signal(barrier, inc=1, device_id=device, device_id_type=MESH)

    mine, theirs = pl.multiple_of(2 * c, 2), pl.multiple_of(2 * other, 2)
    pair_own = 2 * c + x
    pair_across = 2 * c + 1 - x

    started = []
    counter = [0]

    def remote(source, target, device):
        index = counter[0]
        counter[0] += 1
        return pltpu.make_async_remote_copy(
            src_ref=source,
            dst_ref=target,
            send_sem=R.sent.at[index],
            recv_sem=R.came.at[index],
            device_id=device,
            device_id_type=MESH,
        )

    def start(source, target, device):
        copy = remote(source, target, device)
        copy.start()
        started.append(copy)
        return copy

    def sent(copy):
        copy.wait_send()
        started[:] = [one for one in started if one is not copy]

    near, far = (ATT, 0, own), (ATT, own, own)
    parts = [near, far] + [(k, 0, 2 * own) for k in (TIN, TOUT, VIN, VOUT)]
    tin, tout, vin, vout = parts[2:]
    longest = half

    def hops(part, side):
        return half if (parts.index(part) + side) % 2 == 0 else n - 1 - half

    def ring_index(part, side, s):
        return (parts.index(part) * 2 + side) * longest + s

    def view(ref, part, hop):
        k, first, count = part
        return ref.at[k, pl.ds(pl.multiple_of(offsets[hop] + first, 16), count), :]

    sum_base = len(parts) * 2 * longest

    def gather_copy(part, side, s, pos):
        block = view(G, part, pos)
        i = ring_index(part, side, s)
        return pltpu.make_async_remote_copy(
            src_ref=block,
            dst_ref=block,
            send_sem=R.ring_sent.at[part[0]],
            recv_sem=R.ring_came.at[i],
            device_id=way[side],
            device_id_type=MESH,
        )

    def gather(part, s):
        for side in range(2):
            pos = -s if side == 0 else s
            if 0 < s <= hops(part, side):
                gather_copy(part, side, s - 1, pos).wait_recv()
            if s < hops(part, side):
                gather_copy(part, side, s, pos).start()

    def landed(part, side, s):
        k, first, count = part
        return LAND.at[k, side * hops(part, 0) + s, pl.ds(first, count), :]

    def sum_copy(part, side, s, source):
        i = sum_base + ring_index(part, side, s)
        return pltpu.make_async_remote_copy(
            src_ref=source,
            dst_ref=landed(part, side, s),
            send_sem=R.ring_sent.at[5 + part[0]],
            recv_sem=R.ring_came.at[i],
            device_id=way[side],
            device_id_type=MESH,
        )

    def pass_sum(part, s):
        for side in range(2):
            reach = hops(part, side)
            if s >= reach:
                continue
            pos = reach - s if side == 0 else s - reach
            term = view(PART, part, pos)
            if s == 0:
                source = term
            else:
                source = landed(part, side, s - 1)
                sum_copy(part, side, s - 1, source).wait_recv()
                source[...] = (source[...].astype(F32) + term[...].astype(F32)).astype(BF)
            sum_copy(part, side, s, source).start()

    finals = []
    row_sums = [[], []]

    def end_sum(*group):
        for part in group:
            for side in range(2):
                last = hops(part, side) - 1
                sum_copy(part, side, last, landed(part, side, last)).wait_recv()
        for k in sorted({part[0] for part in group}):
            first = hops(near if k == ATT else parts[k + 1], 0) - 1
            earlier = 1 if k == ATT else 0
            counted = 3 * span if k == ATT else width

            def total(core):
                rows = pl.ds(pl.multiple_of(own * core, 16), own)
                chip_rows = pl.ds(pl.multiple_of(2 * own * chip + own * core, 16), own)
                block = (
                    LAND[k, first - earlier * core, rows, :].astype(F32)
                    + LAND[k, n - 2, rows, :].astype(F32)
                    + PART[k, chip_rows, :].astype(F32)
                )
                if k in (ATT, TIN, VIN):
                    weighted = G[k, chip_rows, :].astype(F32)[:, :counted] * block[:, :counted]
                    row_sum = jnp.sum(weighted, axis=-1, keepdims=True)
                    row_sums[0 if core is c else 1].append((k, row_sum))
                return block

            R.give[k] = total(other)
            finals.append(start(R.give.at[k], GW.at[k, c], mate))
            GW[k, c] = total(c)

    def shard_part(k, value):
        for core in range(2):
            S[k, core] = value(core).astype(BF)

    gain_one, gain_two = column(R.gain_attn), column(R.gain_ffn)

    def attention_part(core):
        cols = slice(core * span, (core + 1) * span)
        return jnp.concatenate(
            [
                R.w_query[:, cols].astype(F32) * (gain_one * HEAD_DIM**-0.5),
                R.w_key[:, cols].astype(F32) * gain_one,
                R.w_value[:, cols].astype(F32) * gain_one,
                R.w_out[:, cols].astype(F32),
            ],
            axis=1,
        )

    def half_of(ref, core):
        return ref[:, core * width : (core + 1) * width].astype(F32) * gain_two

    def turned_half(ref, core):
        return ref[:, core * width : (core + 1) * width]

    lengths = R.lengths

    def live(t, slots):
        return (slots < PATCHES) | ((slots >= VIS) & (slots < VIS + lengths[t]))

    def live_rows(t, j, count=64):
        slots = lax.broadcasted_iota(jnp.int32, (count, 1), 0) + j * count
        return live(t, slots).astype(F32)

    row_count = R.tokens.shape[0]

    def placed(t, slots, rows, kept):
        source = t * (PATCHES + CAPTION) + slots - (slots >= VIS).astype(jnp.int32) * (VIS - PATCHES)
        return ((rows == source) & kept).astype(F32).astype(BF)

    def chooser(t, only_live):
        slots = lax.broadcasted_iota(jnp.int32, (SEQ, row_count), 0)
        rows = lax.broadcasted_iota(jnp.int32, (SEQ, row_count), 1)
        filled = (slots < PATCHES) | ((slots >= VIS) & (slots < VIS + CAPTION))
        return placed(t, slots, rows, live(t, slots) if only_live else filled)

    shard_part(ATT, attention_part)
    G[ATT, my_rows, :] = S[ATT, c]
    for t in range(2):
        R.lens[t] = jnp.full((8, 128), lengths[t], jnp.int32).astype(F32)
    pl.semaphore_wait(barrier, 5)
    shard_a = start(S.at[pl.ds(0, 1), other], G.at[pl.ds(0, 1), my_rows, :], mate)
    send_lens = start(R.lens, R.lens4.at[pl.ds(mine, 2)], mate)
    fetched[0].wait()
    for t in range(2):
        R.x4[2 * c + t] = mm(chooser(t, False), R.tokens[...]).astype(BF)
        R.lens4[2 * c + t] = R.lens[t]
    send_x = start(R.x4.at[pl.ds(mine, 2)], R.x4.at[pl.ds(mine, 2)], mate)
    shard_a.wait_recv()
    gather(near, 0)
    gather(far, 0)
    for copy in fetched[1:]:
        copy.wait()

    shard_part(TIN, functools.partial(half_of, R.txt_in))
    shard_part(TOUT, functools.partial(turned_half, R.txt_out))
    shard_part(VIN, functools.partial(half_of, R.vis_in))
    shard_part(VOUT, functools.partial(turned_half, R.vis_out))
    shard_b = start(S.at[pl.ds(1, 4), other], G.at[pl.ds(1, 4), my_rows, :], mate)
    for k in (TIN, TOUT, VIN, VOUT):
        G[k, my_rows, :] = S[k, c]
    gather(near, 1)
    for t in range(2):
        R.gz[2 * c + t] = mm(chooser(t, True), R.cotangent[...]).astype(BF)
        if t == 0:
            gather(far, 1)
    send_gz = start(R.gz.at[pl.ds(mine, 2)], R.gz.at[pl.ds(mine, 2)], mate)
    R.dy[...] = mm(chooser(x, False), R.cotangent[...]).astype(BF)
    for t in range(2):
        R.x[t] = R.x4[2 * c + t]
    shard_b.wait_recv()
    gather(tin, 0)
    gather(near, 2)
    send_x.wait_recv()

    for i in range(4):

        @pl.loop(0, SEQ // 64, unroll=True)
        def _(j, i=i):
            rows = pl.ds(pl.multiple_of(j * 64, 64), 64)
            normed, _ = normalize(R.x4[i, rows, :].astype(F32))
            R.n1[i, rows, :] = normed.astype(BF)

        R.n1t[:, i * SEQ : (i + 1) * SEQ] = R.n1[i].T
        if i == 0:
            gather(far, 2)
        if i == 1:
            gather(tout, 0)
            gather(near, 3)
        if i == 2:
            gather(far, 3)
            gather(vin, 0)
            gather(vout, 0)
    send_gz.wait_recv()
    send_lens.wait_recv()
    gather(near, 4)
    gather(far, 4)

    R.wo[...] = G[ATT][:, 3 * span :]

    @pl.loop(0, 4)
    def _(i):
        projected = mm(R.n1[i], G[ATT][:, : 3 * span]).astype(BF)
        R.q[i] = projected[:, :span]
        R.k[i] = projected[:, span : 2 * span]
        R.v[i] = projected[:, 2 * span :]

    lane = lax.broadcasted_iota(jnp.int32, (1, span), 1) // HEAD_DIM

    def only(head, values):
        return values * (lane == head).astype(F32).astype(BF)

    def head_rows(values, head):
        return values[head * HEAD_DIM : (head + 1) * HEAD_DIM, :]

    order = []
    for j in range(4):
        core = other if j < 2 else c
        turn = 1 - x if j % 2 == 0 else x
        order.append((turn, 2 * core + turn))
    attn_mate = [remote(R.pa.at[i], R.ra.at[turn], mate) for turn, i in order[:2]]
    cross_a = remote(R.xs, R.xr, across)

    for j, (turn, i) in enumerate(order):
        q, k, v = R.q[i], R.k[i], R.v[i]
        turned_v = v.T
        slots = lax.broadcasted_iota(jnp.int32, (SEQ, 1), 0)
        caption = (slots - VIS).astype(F32) < R.lens4[i][:1, :1]
        bias = jnp.where((slots < PATCHES) | ((slots >= VIS) & caption), 0.0, -1e30)
        contexts = []
        for h in range(heads):
            scores = mm_nt(only(h, k), q) + bias
            top = jnp.max(scores, axis=0, keepdims=True)
            weights = jnp.exp(scores - top)
            total = jnp.sum(weights, axis=0, keepdims=True)
            probs = (weights * (1.0 / total)).astype(BF)
            R.probs[i * heads + h] = probs
            contexts.append(mm(head_rows(turned_v, h), probs))
        contexts = jnp.concatenate(contexts, axis=0)
        R.ct[:, pl.ds(pl.multiple_of(i * SEQ, SEQ), SEQ)] = contexts.astype(BF)
        context = contexts.T.astype(BF)
        R.pa[i] = mm_nt(context, R.wo[...]).astype(BF)
        if j < 2:
            attn_mate[j].start()
        if j == 2:
            attn_mate[0].wait_recv()
            R.xs[...] = (R.pa[pair_across].astype(F32) + R.ra[1 - x].astype(F32)).astype(BF)
            cross_a.start()
        if j == 0:
            gather(tin, 1)
        if j == 1:
            gather(tout, 1)
        if j == 3:
            gather(tin, 2)
            gather(tout, 2)

    for copy in attn_mate:
        copy.wait_send()
    attn_mate[1].wait_recv()

    @pl.loop(0, width // 256)
    def _(j):
        cols = pl.ds(pl.multiple_of(j * 256, 256), 256)
        R.gzvt[cols, :] = R.gz[:, :VIS, cols].reshape(4 * VIS, 256).T
        R.gztt[cols, :] = R.gz[:, VIS:, cols].reshape(4 * TXT, 256).T

    gather(vin, 1)
    cross_a.wait_recv()

    @pl.loop(0, SEQ // 64, unroll=True)
    def _(j):
        rows = pl.ds(pl.multiple_of(j * 64, 64), 64)
        attended = (
            R.pa[pair_own, rows, :].astype(F32)
            + R.ra[x, rows, :].astype(F32)
            + R.xr[rows, :].astype(F32)
        )
        middle = R.x[x, rows, :].astype(F32) + live_rows(x, j) * attended
        R.y1[rows, :] = middle
        normed, _ = normalize(middle)
        R.n2[pair_own, rows, :] = normed.astype(BF)

    block = R.n2.at[pair_own]
    to_across = start(block, block, across)
    to_mate = start(block, block, mate)
    gather(vout, 1)
    gather(tin, 3)
    gather(tout, 3)
    to_across.wait_recv()
    block = R.n2.at[pair_across]
    passed = start(block, block, mate)
    gather(vin, 2)
    gather(vout, 2)
    gather(tin, 4)
    gather(tout, 4)
    to_mate.wait_recv()
    passed.wait_recv()

    def expert(pairs, low, high, w_in, w_out, h_ref, gu_ref, j):
        first, count = pairs
        per = high - low
        total_rows = count * per
        cols = slice(j * 256, (j + 1) * 256)
        inside = slice(first, first + count)
        R.u[:total_rows, :] = mm(
            R.n2[inside, low:high, :].reshape(total_rows, width), G[w_in, :, cols]
        )
        R.gh[:total_rows, :] = mm(
            R.gz[inside, low:high, :].reshape(total_rows, width), G[w_out, :, cols]
        )
        step = min(total_rows, VIS)

        @pl.loop(0, 2 * (total_rows // step))
        def _(i):
            lanes = lax.rem(i, 2) * 128
            rows = pl.ds(pl.multiple_of(i // 2 * step, 16), step)
            into = pl.ds(pl.multiple_of(first * per + i // 2 * step, 16), step)
            side = pl.ds(pl.multiple_of(lanes, 128), 128)
            pre = R.u[rows, side]
            cumulative = 0.5 * (1.0 + lax.erf(pre * inv_root_two))
            density = jnp.exp(-0.5 * pre * pre) * inv_root_tau
            onto = pl.ds(pl.multiple_of(j * 256 + lanes, 128), 128)
            h_ref[into, onto] = (pre * cumulative).astype(BF)
            gu_ref[into, onto] = (R.gh[rows, side] * (cumulative + pre * density)).astype(BF)

    def weight_grad(k, turned, ref, j):
        cols = slice(j * 256, (j + 1) * 256)
        PART[k, :, cols] = mm(turned, ref[:, cols]).astype(BF)

    tiles = range(width // 256)
    for j in tiles:
        expert((0, 4), VIS, SEQ, TIN, TOUT, R.ht, R.gut, j)
    gather(vin, 3)
    for j in tiles:
        weight_grad(TOUT, R.gztt[...], R.ht, j)

    @pl.loop(0, width // 256)
    def _(j):
        cols = pl.ds(pl.multiple_of(j * 256, 256), 256)
        R.n2vt[cols, :] = R.n2[:, :VIS, cols].reshape(4 * VIS, 256).T
        R.n2tt[cols, :] = R.n2[:, VIS:, cols].reshape(4 * TXT, 256).T

    gather(vout, 3)
    for j in tiles:
        weight_grad(TIN, R.n2tt[...], R.gut, j)
    pass_sum(tout, 0)
    pass_sum(tin, 0)

    def text_terms(target, rows, weight):
        target[:, VIS:, :] = mm_nt(rows, G[weight]).astype(BF).reshape(4, TXT, width)

    text_terms(R.pg, R.gut[...], TIN)
    text_terms(R.pf, R.ht[...], TOUT)
    gather(vin, 4)
    gather(vout, 4)

    def terms(target, rows, weight, m):
        part = mm_nt(rows[2 * m * VIS : 2 * (m + 1) * VIS, :], G[weight]).astype(BF)
        target[2 * m : 2 * m + 2, :VIS, :] = part.reshape(2, VIS, width)

    mate_g = remote(R.pg.at[pl.ds(theirs, 2)], R.rg, mate)
    cross_g = remote(R.xsg, R.xrg, across)
    gy_across = remote(R.gy.at[x], R.gy.at[x], across)
    gy_mate = remote(R.ga.at[pair_own], R.ga.at[pair_own], mate)
    gy_passed = remote(R.ga.at[pair_across], R.ga.at[pair_across], mate)
    started.extend([cross_g, gy_across, gy_mate, gy_passed])

    def image_terms(m):
        terms(R.pg, R.guv, VIN, m)
        pl.when(c != m)(mate_g.start)

    def sum_cores(m):
        @pl.when(c == m)
        def _():
            mate_g.wait_recv()
            R.xsg[...] = (R.pg[pair_across].astype(F32) + R.rg[1 - x].astype(F32)).astype(BF)
            cross_g.start()

    def middle_back(m):
        @pl.when(c == m)
        def _():
            cross_g.wait_recv()

            @pl.loop(0, SEQ // 64, unroll=True)
            def _(j):
                rows = pl.ds(pl.multiple_of(j * 64, 64), 64)
                grad_normed = (
                    R.pg[pair_own, rows, :].astype(F32)
                    + R.rg[x, rows, :].astype(F32)
                    + R.xrg[rows, :].astype(F32)
                )
                normed, inverse = normalize(R.y1[rows, :])
                grad = R.dy[rows, :].astype(F32) + normalize_back(grad_normed, normed, inverse)
                R.gy[x, rows, :] = grad.astype(BF)
                R.ga[pair_own, rows, :] = (grad * live_rows(x, j)).astype(BF)

            gy_across.start()
            gy_mate.start()

    def middle_pass(m):
        @pl.when(c == m)
        def _():
            gy_across.wait_recv()

            @pl.loop(0, SEQ // 64, unroll=True)
            def _(j):
                rows = pl.ds(pl.multiple_of(j * 64, 64), 64)
                R.ga[pair_across, rows, :] = (
                    R.gy[1 - x, rows, :].astype(F32) * live_rows(1 - x, j)
                ).astype(BF)

            gy_passed.start()

    def middle_came(m):
        @pl.when(c != m)
        def _():
            gy_mate.wait_recv()
            gy_passed.wait_recv()

    sent(send_x)
    cross_a.wait_send()
    for j in tiles:
        expert((0, 2), 0, VIS, VIN, VOUT, R.hv, R.guv, j)
    image_terms(0)
    expert((2, 2), 0, VIS, VIN, VOUT, R.hv, R.guv, 0)
    sum_cores(0)
    pass_sum(tout, 1)
    for j in tiles[1:]:
        expert((2, 2), 0, VIS, VIN, VOUT, R.hv, R.guv, j)
    image_terms(1)
    for copy in (to_across, to_mate, passed):
        sent(copy)
    sum_cores(1)
    pass_sum(tin, 1)
    weight_grad(VOUT, R.gzvt[...], R.hv, 0)
    middle_back(0)
    for j in tiles[1:]:
        weight_grad(VOUT, R.gzvt[...], R.hv, j)
    pass_sum(vout, 0)
    pass_sum(tout, 2)
    for j in tiles:
        weight_grad(VIN, R.n2vt[...], R.guv, j)
    pass_sum(vin, 0)
    pass_sum(tin, 2)

    terms(R.pf, R.hv, VOUT, 0)
    middle_pass(0)
    middle_back(1)
    pass_sum(tout, 3)
    terms(R.pf, R.hv, VOUT, 1)
    mate_f = start(R.pf.at[pl.ds(theirs, 2)], R.rf, mate)
    cross_f = remote(R.xsf, R.xrf, across)
    started.append(cross_f)
    pass_sum(tin, 3)
    mate_g.wait_send()
    middle_came(0)

    back_mate = [remote(R.pb.at[theirs + t], R.rb.at[t], mate) for t in range(2)]
    back_cross = [remote(R.xsb.at[t], R.xrb.at[t], across) for t in range(2)]
    started.extend(back_mate + back_cross)

    def attention_back(m, t):
        i = 2 * m + t
        grad_context = mm(R.ga[i], R.wo[...]).astype(BF)
        q, k, v = R.q[i], R.k[i], R.v[i]
        turned_k = k.T
        grad_q = []
        grad_k = jnp.zeros((SEQ, span), F32)
        grad_v = jnp.zeros((SEQ, span), F32)
        for h in range(heads):
            probs = R.probs[i * heads + h]
            grad_probs = mm_nt(only(h, v), grad_context)
            exact = probs.astype(F32)
            inner = jnp.sum(grad_probs * exact, axis=0, keepdims=True)
            grad_scores = (exact * (grad_probs - inner)).astype(BF)
            grad_q.append(mm(head_rows(turned_k, h), grad_scores))
            grad_k += mm(grad_scores, only(h, q))
            grad_v += mm(probs, only(h, grad_context))
        grad_q = jnp.concatenate(grad_q, axis=0).T
        joined = jnp.concatenate([grad_q, grad_k, grad_v], axis=1).astype(BF)
        R.gqkv[i, :, : 3 * span] = joined
        R.pb[i] = mm_nt(joined, G[ATT][:, : 3 * span]).astype(BF)
        pl.when(c != m)(back_mate[t].start)

    def back_sum(m, t):
        @pl.when(c == m)
        def _():
            back_mate[t].wait_recv()
            R.xsb[t] = (R.pb[2 * m + t].astype(F32) + R.rb[t].astype(F32)).astype(BF)
            back_cross[t].start()

    attention_back(0, 0)
    pass_sum(vout, 1)
    mate_f.wait_recv()
    R.xsf[...] = (R.pf[pair_across].astype(F32) + R.rf[1 - x].astype(F32)).astype(BF)
    R.fown[...] = (R.pf[pair_own].astype(F32) + R.rf[x].astype(F32)).astype(BF)
    middle_pass(1)
    cross_f.start()
    attention_back(0, 1)
    back_sum(0, 0)

    pass_sum(vin, 1)
    middle_came(1)
    attention_back(1, 0)
    back_sum(0, 1)

    pass_sum(vout, 2)
    attention_back(1, 1)
    back_sum(1, 0)
    pass_sum(vin, 2)

    @pl.loop(0, width // 256)
    def _(j):
        rows = pl.ds(pl.multiple_of(j * 256, 256), 256)
        grads = mm(R.n1t[rows, :], R.gqkv[:, :, : 3 * span].reshape(4 * SEQ, 3 * span))
        grad_o = mm(R.ct[...], R.ga[:, :, rows].reshape(4 * SEQ, 256)).T
        PART[ATT, rows, :] = jnp.concatenate([grads, grad_o], axis=1).astype(BF)

    pass_sum(far, 0)
    pass_sum(near, 0)

    cross_f.wait_recv()

    @pl.loop(0, SEQ // 64, unroll=True)
    def _(j):
        rows = pl.ds(pl.multiple_of(j * 64, 64), 64)
        branch = R.fown[rows, :].astype(F32) + R.xrf[rows, :].astype(F32)
        OUT[x, rows, :] = (R.y1[rows, :] + live_rows(x, j) * branch).astype(BF)

    out_across = start(OUT.at[x], OUT.at[x], across)
    back_sum(1, 1)
    pass_sum(vout, 3)
    pass_sum(vin, 3)

    def input_back(m, t):
        @pl.when(c == m)
        def _():
            back_cross[t].wait_recv()

            @pl.loop(0, SEQ // 64, unroll=True)
            def _(j):
                rows = pl.ds(pl.multiple_of(j * 64, 64), 64)
                grad_normed = R.xsb[t, rows, :].astype(F32) + R.xrb[t, rows, :].astype(F32)
                normed, inverse = normalize(R.x[t, rows, :].astype(F32))
                grad = R.gy[t, rows, :].astype(F32) + normalize_back(grad_normed, normed, inverse)
                high = grad.astype(BF)
                rows = pl.ds(pl.multiple_of(t * SEQ + j * 64, 64), 64)
                R.hv[rows, :] = high
                R.guv[rows, :] = (grad - high.astype(F32)).astype(BF)

    pass_sum(far, 1)
    input_back(0, 0)
    pass_sum(near, 1)
    input_back(0, 1)
    end_sum(tout, tin)
    pass_sum(far, 2)
    pass_sum(near, 2)
    end_sum(vout, vin)

    leaving = []

    def leave(slot, source, target):
        leaving.append(fetch(slot, source, target))

    slots = lax.broadcasted_iota(jnp.int32, (row_count, 2 * SEQ), 1)
    rows = lax.broadcasted_iota(jnp.int32, (row_count, 2 * SEQ), 0)
    turn = slots // SEQ
    back = placed(turn, slots - turn * SEQ, rows, slots >= 0)
    out_across.wait_recv()
    R.out_tokens[...] = mm(back, OUT[...].reshape(2 * SEQ, width)).astype(BF)
    leave(6, R.out_tokens, R.out_tokens_hbm)
    for copy in finals:
        copy.wait_recv()
    finals.clear()
    leave(7, GW.at[pl.ds(1, 4)], R.gw_hbm.at[pl.ds(1, 4)])
    pass_sum(far, 3)
    pass_sum(near, 3)
    input_back(1, 0)
    input_back(1, 1)
    R.grad_tokens[...] = mm(back, R.hv[: 2 * SEQ, :]) + mm(back, R.guv[: 2 * SEQ, :])
    leave(8, R.grad_tokens, R.grad_tokens_hbm)
    end_sum(far, near)

    first_lane = lax.broadcasted_iota(jnp.int32, (own, 128), 1) == 0
    for place in range(2):
        attn = sum(total for k, total in row_sums[place] if k == ATT)
        experts = sum(total for k, total in row_sums[place] if k != ATT)
        R.gs[place] = jnp.where(first_lane, attn, experts)
    peers = [
        start(R.gs.at[place], R.gr.at[slot], device)
        for slot, (place, device) in enumerate(((1, mate), (0, across), (1, diagonal)))
    ]
    for copy in finals + peers:
        copy.wait_recv()
    leave(9, GW.at[pl.ds(0, 1)], R.gw_hbm.at[pl.ds(0, 1)])
    GG[...] = (R.gs[0] + R.gr[1]) + (R.gr[0] + R.gr[2])

    for copy in started:
        copy.wait_send()
    for copy in leaving:
        copy.wait()
    for k in range(5):
        for semaphore in (k, 5 + k):
            pltpu.make_async_remote_copy(
                src_ref=LAND.at[k],
                dst_ref=LAND.at[k],
                send_sem=R.ring_sent.at[semaphore],
                recv_sem=R.ring_came.at[0],
                device_id=ahead,
                device_id_type=MESH,
            ).wait_send()


def finish_kernel(n_results, out, gtok, gw_hbm, gg, gain_attn, gain_ffn, *rest):
    results, scratch = rest[:n_results], rest[n_results:]
    buffers, (out_buffer, gtok_buffer, gw, came, gone) = scratch[:n_results], scratch[n_results:]
    arriving = [
        pltpu.make_async_copy(source, target, came.at[slot])
        for slot, (source, target) in enumerate(((gw_hbm, gw), (out, out_buffer), (gtok, gtok_buffer)))
    ]
    for copy in arriving:
        copy.start()
    width = gw.shape[3]
    own = gw.shape[2]
    span = width // 4
    gain_one, gain_two = column(gain_attn), column(gain_ffn)
    square = unit(own).astype(F32)
    leaving = []

    def leave(slot, source):
        copy = pltpu.make_async_copy(source, results[slot], gone.at[slot])
        copy.start()
        leaving.append(copy)

    def both(part):
        cols = slice(part * span, (part + 1) * span)
        return jnp.concatenate([gw[ATT, core][:, cols] for core in range(2)], axis=1)

    def put(slot, value):
        buffers[slot][...] = value
        leave(slot, buffers[slot])

    put(2, jnp.sum(square * (gg[:, :1] / gain_one), axis=0, keepdims=True))
    put(7, jnp.sum(square * (gg[:, 1:2] / gain_two), axis=0, keepdims=True))
    arriving[0].wait()
    for slot, k, scale in ((8, VIN, gain_two), (9, VOUT, 1.0), (10, TIN, gain_two), (11, TOUT, 1.0)):
        put(slot, jnp.concatenate([gw[k, 0], gw[k, 1]], axis=1) * scale)
    put(3, both(0) * (gain_one * HEAD_DIM**-0.5))
    put(4, both(1) * gain_one)
    put(5, both(2) * gain_one)
    put(6, both(3))
    arriving[1].wait()
    leave(0, out_buffer)
    arriving[2].wait()
    leave(1, gtok_buffer)
    for copy in leaving:
        copy.wait()


def fused_layer(
    tokens,
    caption_lengths,
    gain_attn,
    w_query,
    w_key,
    w_value,
    w_out,
    gain_ffn,
    vis_in,
    vis_out,
    txt_in,
    txt_out,
    cotangent,
):
    n = lax.axis_size("dp") // 2
    own = w_query.shape[0]
    row_count, width = tokens.shape
    span = width // 4
    heads = span // HEAD_DIM
    gain_one, gain_two = gain_attn.reshape(1, own), gain_ffn.reshape(1, own)

    rows = 4 * SEQ
    scratch = dict(
        tokens=pltpu.VMEM((row_count, width), BF),
        cotangent=pltpu.VMEM((row_count, width), BF),
        txt_in=pltpu.VMEM((own, 2 * width), BF),
        txt_out=pltpu.VMEM((own, 2 * width), BF),
        vis_in=pltpu.VMEM((own, 2 * width), BF),
        vis_out=pltpu.VMEM((own, 2 * width), BF),
        out_tokens=pltpu.VMEM((row_count, width), BF),
        grad_tokens=pltpu.VMEM((row_count, width), F32),
        gw=pltpu.VMEM((5, 2, own, width), F32),
        local=pltpu.SemaphoreType.DMA((10,)),
        shard=pltpu.VMEM((5, 2, own, width), BF),
        lens=pltpu.VMEM((2, 8, 128), F32),
        x=pltpu.VMEM((2, SEQ, width), BF),
        dy=pltpu.VMEM((SEQ, width), BF),
        padded_out=pltpu.VMEM((2, SEQ, width), BF),
        gathered=pltpu.VMEM((5, width, width), BF),
        part=pltpu.VMEM((5, width, width), BF),
        land=pltpu.VMEM((5, n - 1, 2 * own, width), BF),
        give=pltpu.VMEM((5, own, width), F32),
        x4=pltpu.VMEM((4, SEQ, width), BF),
        lens4=pltpu.VMEM((4, 8, 128), F32),
        n1=pltpu.VMEM((4, SEQ, width), BF),
        n1t=pltpu.VMEM((width, rows), BF),
        gz=pltpu.VMEM((4, SEQ, width), BF),
        gzvt=pltpu.VMEM((width, 4 * VIS), BF),
        ct=pltpu.VMEM((span, rows), BF),
        fown=pltpu.VMEM((SEQ, width), BF),
        gztt=pltpu.VMEM((width, 4 * TXT), BF),
        wo=pltpu.VMEM((width, span), BF),
        q=pltpu.VMEM((4, SEQ, span), BF),
        k=pltpu.VMEM((4, SEQ, span), BF),
        v=pltpu.VMEM((4, SEQ, span), BF),
        probs=pltpu.VMEM((4 * heads, SEQ, SEQ), BF),
        pa=pltpu.VMEM((4, SEQ, width), BF),
        ra=pltpu.VMEM((2, SEQ, width), BF),
        xs=pltpu.VMEM((SEQ, width), BF),
        xr=pltpu.VMEM((SEQ, width), BF),
        y1=pltpu.VMEM((SEQ, width), F32),
        n2vt=pltpu.VMEM((width, 4 * VIS), BF),
        n2tt=pltpu.VMEM((width, 4 * TXT), BF),
        u=pltpu.VMEM((4 * VIS, 256), F32),
        gh=pltpu.VMEM((4 * VIS, 256), F32),
        hv=pltpu.VMEM((4 * VIS, width), BF),
        guv=pltpu.VMEM((4 * VIS, width), BF),
        ht=pltpu.VMEM((4 * TXT, width), BF),
        gut=pltpu.VMEM((4 * TXT, width), BF),
        pg=pltpu.VMEM((4, SEQ, width), BF),
        rg=pltpu.VMEM((2, SEQ, width), BF),
        gy=pltpu.VMEM((2, SEQ, width), BF),
        xsf=pltpu.VMEM((SEQ, width), BF),
        xrf=pltpu.VMEM((SEQ, width), BF),
        xsb=pltpu.VMEM((2, SEQ, width), BF),
        xrb=pltpu.VMEM((2, SEQ, width), BF),
        gs=pltpu.VMEM((2, own, 128), F32),
        gr=pltpu.VMEM((3, own, 128), F32),
        sent=pltpu.SemaphoreType.DMA((40,)),
        came=pltpu.SemaphoreType.DMA((40,)),
        ring_sent=pltpu.SemaphoreType.DMA((10,)),
        ring_came=pltpu.SemaphoreType.DMA((6 * 2 * (n // 2) * 2,)),
    )
    inputs = dict(
        lengths=caption_lengths,
        tokens_hbm=tokens,
        cotangent_hbm=cotangent,
        gain_attn=gain_one,
        gain_ffn=gain_two,
        w_query=w_query,
        w_key=w_key,
        w_value=w_value,
        w_out=w_out.T,
        vis_in_hbm=vis_in,
        vis_out_hbm=vis_out.T,
        txt_in_hbm=txt_in,
        txt_out_hbm=txt_out.T,
    )
    results = dict(
        out_tokens_hbm=jax.ShapeDtypeStruct((row_count, width), BF),
        grad_tokens_hbm=jax.ShapeDtypeStruct((row_count, width), F32),
        gw_hbm=jax.ShapeDtypeStruct((5, 2, own, width), F32),
        gg=jax.ShapeDtypeStruct((own, 128), F32),
    )
    vmem, hbm = pl.BlockSpec(memory_space=pltpu.VMEM), pl.BlockSpec(memory_space=pl.ANY)
    names = tuple(inputs) + tuple(results) + tuple(scratch)
    out, gtok, gw, gg = pl.pallas_call(
        functools.partial(layer_kernel, n, names),
        out_shape=tuple(results.values()),
        in_specs=[pl.BlockSpec(memory_space=pltpu.SMEM)] + [hbm if k.endswith(HBM) else vmem for k in names[1 : len(inputs)]],
        out_specs=[hbm if k.endswith(HBM) else vmem for k in results],
        scratch_shapes=list(scratch.values()),
        compiler_params=pltpu.CompilerParams(
            collective_id=0, has_side_effects=True, vmem_limit_bytes=60 * 2**20
        ),
    )(*inputs.values())

    shapes = (
        jax.ShapeDtypeStruct((row_count, width), BF),
        jax.ShapeDtypeStruct((row_count, width), F32),
        jax.ShapeDtypeStruct((1, own), F32),
        jax.ShapeDtypeStruct((own, 2 * span), F32),
        jax.ShapeDtypeStruct((own, 2 * span), F32),
        jax.ShapeDtypeStruct((own, 2 * span), F32),
        jax.ShapeDtypeStruct((own, 2 * span), F32),
        jax.ShapeDtypeStruct((1, own), F32),
        jax.ShapeDtypeStruct((own, 2 * width), F32),
        jax.ShapeDtypeStruct((own, 2 * width), F32),
        jax.ShapeDtypeStruct((own, 2 * width), F32),
        jax.ShapeDtypeStruct((own, 2 * width), F32),
    )
    buffers = [pltpu.VMEM(one.shape if slot > 1 else (8, 128), F32) for slot, one in enumerate(shapes)]
    final = pl.pallas_call(
        functools.partial(finish_kernel, len(shapes)),
        out_shape=shapes,
        in_specs=[hbm] * 3 + [vmem] * 3,
        out_specs=[hbm] * len(shapes),
        scratch_shapes=buffers
        + [
            pltpu.VMEM((row_count, width), BF),
            pltpu.VMEM((row_count, width), F32),
            pltpu.VMEM((5, 2, own, width), F32),
            pltpu.SemaphoreType.DMA((3,)),
            pltpu.SemaphoreType.DMA((len(shapes),)),
        ],
        compiler_params=pltpu.CompilerParams(vmem_limit_bytes=60 * 2**20),
    )(out, gtok, gw, gg, gain_one, gain_two)
    final = list(final)
    final[2] = final[2].reshape(own)
    final[7] = final[7].reshape(own)
    for turned in (6, 9, 11):
        final[turned] = final[turned].T
    return tuple(final)


def norm_parts(values):
    center = values - jnp.mean(values, axis=-1, keepdims=True)
    spread = jnp.mean(center * center, axis=-1, keepdims=True)
    inverse = lax.rsqrt(spread + epsilon)
    return (center * inverse, inverse)


def norm_back(grad_out, normed, inverse, gain):
    grad_normed = grad_out * gain
    grad_gain = jnp.sum(grad_out * normed, axis=0)
    inner = (
        grad_normed
        - jnp.mean(grad_normed, axis=-1, keepdims=True)
        - normed * jnp.mean(grad_normed * normed, axis=-1, keepdims=True)
    )
    return (inverse * inner, grad_gain)


def matmul(left, right):
    return jnp.dot(left, right, preferred_element_type=jnp.float32)


def matmul_tn(left, right):
    return lax.dot_general(
        left, right, (((0,), (0,)), ((), ())), preferred_element_type=jnp.float32
    )


def matmul_nt(left, right):
    return lax.dot_general(
        left, right, (((1,), (1,)), ((), ())), preferred_element_type=jnp.float32
    )


def gelu_slope(pre):
    cumulative = 0.5 * (1.0 + lax.erf(pre * inv_root_two))
    density = jnp.exp(-0.5 * pre * pre) * inv_root_tau
    return cumulative + pre * density


def expert_forward(rows, weight_in, weight_out):
    pre = matmul(rows, weight_in)
    hidden = jax.nn.gelu(pre, approximate=False).astype(jnp.bfloat16)
    return (pre, hidden, matmul(hidden, weight_out))


def expert_backward(rows, pre, hidden, grad_out, weight_in, weight_out):
    grad_weight_out = matmul_tn(hidden, grad_out)
    grad_hidden = matmul_nt(grad_out, weight_out)
    grad_pre = (grad_hidden * gelu_slope(pre)).astype(jnp.bfloat16)
    return (matmul_tn(rows, grad_pre), grad_weight_out, matmul_nt(grad_pre, weight_in))


def join_experts(image_rows, text_rows, pair_count, width):
    joined = jnp.concatenate(
        [
            image_rows.reshape(pair_count, PATCHES, width),
            text_rows.reshape(pair_count, CAPTION, width),
        ],
        axis=1,
    )
    return joined.reshape(-1, width)


def plain_layer(
    tokens,
    caption_lengths,
    gain_attn,
    w_query,
    w_key,
    w_value,
    w_out,
    gain_ffn,
    vis_in,
    vis_out,
    txt_in,
    txt_out,
    cotangent,
):
    seq_len = PATCHES + CAPTION
    width = tokens.shape[1]
    pair_count = tokens.shape[0] // seq_len
    half_pairs = pair_count // lax.axis_size("tensor")
    half_rows = half_pairs * seq_len
    row_start = lax.axis_index("tensor") * half_rows
    gain_one, query_w, key_w, value_w, out_w = (
        lax.all_gather(gain_attn, "dp", axis=0, tiled=True),
        lax.all_gather(w_query, "dp", axis=0, tiled=True),
        lax.all_gather(w_key, "dp", axis=0, tiled=True),
        lax.all_gather(w_value, "dp", axis=0, tiled=True),
        lax.all_gather(w_out, "dp", axis=1, tiled=True),
    )
    gain_two, vis_in_w, vis_out_w, txt_in_w, txt_out_w = (
        lax.all_gather(gain_ffn, "dp", axis=0, tiled=True),
        lax.all_gather(vis_in, "dp", axis=0, tiled=True),
        lax.all_gather(vis_out, "dp", axis=1, tiled=True),
        lax.all_gather(txt_in, "dp", axis=0, tiled=True),
        lax.all_gather(txt_out, "dp", axis=1, tiled=True),
    )
    gain_one = gain_one.astype(jnp.float32)
    gain_two = gain_two.astype(jnp.float32)
    head_local = query_w.shape[1] // HEAD_DIM
    score_scale = HEAD_DIM ** (-0.5)
    position = jnp.arange(seq_len, dtype=jnp.int32)
    live = (position[None, :] < PATCHES) | (position[None, :] - PATCHES < caption_lengths[:, None])
    valid_rows = live.astype(jnp.float32)
    mask_col = valid_rows.reshape(-1, 1)
    key_live = valid_rows[:, None, None, :] > 0.5

    def own_rows(values):
        return lax.dynamic_slice_in_dim(values, row_start, half_rows, 0)

    inputs = tokens.astype(jnp.float32)
    normed_one, inverse_one = norm_parts(inputs)
    first_in = (normed_one * gain_one).astype(jnp.bfloat16)

    def project(weight):
        return (
            matmul(first_in, weight)
            .astype(jnp.bfloat16)
            .reshape(pair_count, seq_len, head_local, HEAD_DIM)
        )

    queries = project(query_w)
    keys_all = project(key_w)
    values_all = project(value_w)

    def score_block():
        raw = (
            jnp.einsum("pqhe,pkhe->phqk", queries, keys_all, preferred_element_type=jnp.float32)
            * score_scale
        )
        return jnp.where(key_live, raw, -1e30)

    scores = score_block()
    top = jnp.max(scores, axis=-1, keepdims=True)
    weights = jnp.exp(scores - top)
    total = jnp.sum(weights, axis=-1, keepdims=True)
    probs = (weights / total).astype(jnp.bfloat16)
    log_total = top + jnp.log(total)
    context = jnp.einsum("phqk,pkhe->pqhe", probs, values_all, preferred_element_type=jnp.float32)
    context = context.astype(jnp.bfloat16).reshape(-1, head_local * HEAD_DIM)
    attn_terms = matmul(context, out_w)
    attended_own = lax.psum_scatter(
        attn_terms.astype(jnp.bfloat16), "tensor", scatter_dimension=0, tiled=True
    ).astype(jnp.float32)
    mask_own = own_rows(mask_col)
    middle_own = own_rows(inputs) + mask_own * attended_own
    normed_two, inverse_two = norm_parts(middle_own)
    second_own = (normed_two * gain_two).astype(jnp.bfloat16)
    grid = lax.all_gather(second_own, "tensor", axis=0, tiled=True).reshape(
        pair_count, seq_len, width
    )
    image_rows = grid[:, :PATCHES].reshape(-1, width)
    text_rows = grid[:, PATCHES:].reshape(-1, width)
    image_pre, image_hidden, image_part = expert_forward(image_rows, vis_in_w, vis_out_w)
    text_pre, text_hidden, text_part = expert_forward(text_rows, txt_in_w, txt_out_w)
    image_own, text_own = (
        lax.psum_scatter(
            image_part.astype(jnp.bfloat16), "tensor", scatter_dimension=0, tiled=True
        ).astype(jnp.float32),
        lax.psum_scatter(
            text_part.astype(jnp.bfloat16), "tensor", scatter_dimension=0, tiled=True
        ).astype(jnp.float32),
    )
    branch_own = join_experts(image_own, text_own, half_pairs, width)
    output_own = (middle_own + mask_own * branch_own).astype(jnp.bfloat16)
    upstream = cotangent.astype(jnp.float32)
    grad_branch = (upstream * mask_col).astype(jnp.bfloat16).reshape(pair_count, seq_len, width)
    image_grads = expert_backward(
        image_rows,
        image_pre,
        image_hidden,
        grad_branch[:, :PATCHES].reshape(-1, width),
        vis_in_w,
        vis_out_w,
    )
    text_grads = expert_backward(
        text_rows,
        text_pre,
        text_hidden,
        grad_branch[:, PATCHES:].reshape(-1, width),
        txt_in_w,
        txt_out_w,
    )
    back_image_own, back_text_own = (
        lax.psum_scatter(
            image_grads[2].astype(jnp.bfloat16), "tensor", scatter_dimension=0, tiled=True
        ).astype(jnp.float32),
        lax.psum_scatter(
            text_grads[2].astype(jnp.bfloat16), "tensor", scatter_dimension=0, tiled=True
        ).astype(jnp.float32),
    )
    grad_second_own = join_experts(back_image_own, back_text_own, half_pairs, width)
    grad_norm_own, gain_part = norm_back(grad_second_own, normed_two, inverse_two, gain_two)
    grad_middle_own = own_rows(upstream) + grad_norm_own
    output_wide, grad_middle, gain_parts = (
        lax.all_gather(
            output_own.astype(jnp.float32).astype(jnp.bfloat16), "tensor", axis=0, tiled=True
        ).astype(jnp.float32),
        lax.all_gather(grad_middle_own.astype(jnp.bfloat16), "tensor", axis=0, tiled=True).astype(
            grad_middle_own.dtype
        ),
        lax.all_gather(gain_part.astype(jnp.bfloat16), "tensor", axis=0, tiled=True).astype(
            gain_part.dtype
        ),
    )
    output = output_wide.astype(jnp.bfloat16)
    grad_gain_two = jnp.sum(gain_parts.reshape(-1, width), axis=0)
    grad_attended = (grad_middle * mask_col).astype(jnp.bfloat16)
    grad_out_w = matmul_tn(context, grad_attended)
    grad_context = (
        matmul_nt(grad_attended, out_w)
        .astype(jnp.bfloat16)
        .reshape(pair_count, seq_len, head_local, HEAD_DIM)
    )
    scores_again = score_block()
    probs_exact = jnp.exp(scores_again - log_total)
    grad_probs = jnp.einsum(
        "pqhe,pkhe->phqk", grad_context, values_all, preferred_element_type=jnp.float32
    )
    inner = jnp.sum(grad_probs * probs_exact, axis=-1, keepdims=True)
    grad_scores = (probs_exact * (grad_probs - inner)).astype(jnp.bfloat16)
    grad_values = jnp.einsum(
        "phqk,pqhe->pkhe", probs, grad_context, preferred_element_type=jnp.float32
    )
    grad_values = grad_values.astype(jnp.bfloat16).reshape(-1, head_local * HEAD_DIM)
    grad_queries = (
        jnp.einsum("phqk,pkhe->pqhe", grad_scores, keys_all, preferred_element_type=jnp.float32)
        * score_scale
    )
    grad_queries = grad_queries.astype(jnp.bfloat16).reshape(-1, head_local * HEAD_DIM)
    grad_keys = (
        jnp.einsum("phqk,pqhe->pkhe", grad_scores, queries, preferred_element_type=jnp.float32)
        * score_scale
    )
    grad_keys = grad_keys.astype(jnp.bfloat16).reshape(-1, head_local * HEAD_DIM)
    grad_query_w = matmul_tn(first_in, grad_queries)
    grad_key_w = matmul_tn(first_in, grad_keys)
    grad_value_w = matmul_tn(first_in, grad_values)
    first_part = (
        matmul_nt(grad_queries, query_w)
        + matmul_nt(grad_keys, key_w)
        + matmul_nt(grad_values, value_w)
    )
    grad_first = lax.psum(first_part.astype(jnp.bfloat16), "tensor").astype(jnp.float32)
    grad_norm_one, grad_gain_one = norm_back(grad_first, normed_one, inverse_one, gain_one)
    grad_inputs = grad_middle + grad_norm_one
    attn_sent = (
        lax.psum_scatter(grad_gain_one, "dp", scatter_dimension=0, tiled=True),
        lax.psum_scatter(grad_query_w, "dp", scatter_dimension=0, tiled=True),
        lax.psum_scatter(grad_key_w, "dp", scatter_dimension=0, tiled=True),
        lax.psum_scatter(grad_value_w, "dp", scatter_dimension=0, tiled=True),
        lax.psum_scatter(grad_out_w, "dp", scatter_dimension=1, tiled=True),
    )
    final_expert = (
        lax.psum_scatter(grad_gain_two, "dp", scatter_dimension=0, tiled=True),
        lax.psum_scatter(image_grads[0], "dp", scatter_dimension=0, tiled=True),
        lax.psum_scatter(image_grads[1], "dp", scatter_dimension=1, tiled=True),
        lax.psum_scatter(text_grads[0], "dp", scatter_dimension=0, tiled=True),
        lax.psum_scatter(text_grads[1], "dp", scatter_dimension=1, tiled=True),
    )
    return (
        output,
        grad_inputs,
        attn_sent[0],
        attn_sent[1],
        attn_sent[2],
        attn_sent[3],
        attn_sent[4],
        final_expert[0],
        final_expert[1],
        final_expert[2],
        final_expert[3],
        final_expert[4],
    )


def solution(mesh):
    def local(tokens, lengths, gain, w_query, *rest):
        ring = mesh.shape["dp"] // 2
        fits = (
            mesh.shape["tensor"] == 2
            and ring == 8
            and lengths.shape[0] == 2
            and w_query.shape[0] % 16 == 0
        )
        layer = fused_layer if fits else plain_layer
        return layer(tokens, lengths, gain, w_query, *rest)

    return jax.shard_map(
        local,
        mesh=mesh,
        in_specs=(
            P("dp", None),
            P("dp"),
            P("dp"),
            P("dp", "tensor"),
            P("dp", "tensor"),
            P("dp", "tensor"),
            P("tensor", "dp"),
            P("dp"),
            P("dp", "tensor"),
            P("tensor", "dp"),
            P("dp", "tensor"),
            P("tensor", "dp"),
            P("dp", None),
        ),
        out_specs=(
            P("dp", None),
            P("dp", None),
            P("dp"),
            P("dp", "tensor"),
            P("dp", "tensor"),
            P("dp", "tensor"),
            P("tensor", "dp"),
            P("dp"),
            P("dp", "tensor"),
            P("tensor", "dp"),
            P("dp", "tensor"),
            P("tensor", "dp"),
        ),
        check_vma=False,
    )
```

```python
import functools
import math
import types

import jax
import jax.numpy as jnp
from jax import lax
from jax.experimental import pallas as pl
from jax.experimental.pallas import tpu as pltpu
from jax.sharding import PartitionSpec as P

HEAD_DIM = 64
PATCHES = 197
CAPTION = 40
VIS = 208
TXT = 48
SEQ = VIS + TXT

MESH = pl.DeviceIdType.MESH
HBM = "_hbm"
BF = jnp.bfloat16
F32 = jnp.float32

ATT, TIN, TOUT, VIN, VOUT = range(5)

epsilon = 1e-05
inv_root_two = 1.0 / math.sqrt(2.0)
inv_root_tau = 1.0 / math.sqrt(2.0 * math.pi)


def mm(left, right):
    return jnp.dot(left, right, preferred_element_type=F32)


def mm_nt(left, right):
    return lax.dot_general(left, right, (((1,), (1,)), ((), ())), preferred_element_type=F32)


def mm_tn(left, right):
    return lax.dot_general(left, right, (((0,), (0,)), ((), ())), preferred_element_type=F32)


def normalize(values):
    center = values - jnp.mean(values, axis=-1, keepdims=True)
    spread = jnp.mean(center * center, axis=-1, keepdims=True)
    inverse = lax.rsqrt(spread + epsilon)
    return center * inverse, inverse


def normalize_back(grad_normed, normed, inverse):
    return inverse * (
        grad_normed
        - jnp.mean(grad_normed, axis=-1, keepdims=True)
        - normed * jnp.mean(grad_normed * normed, axis=-1, keepdims=True)
    )


def unit(size):
    rows = lax.broadcasted_iota(jnp.int32, (size, size), 0)
    return (rows == lax.broadcasted_iota(jnp.int32, (size, size), 1)).astype(F32).astype(BF)


def column(ref):
    size = ref.shape[1]
    return jnp.sum(unit(size).astype(F32) * ref[...].astype(F32), axis=1, keepdims=True)


def layer_kernel(n, names, *refs):
    R = types.SimpleNamespace(**dict(zip(names, refs)))
    R.pb, R.pf, R.ga, R.rf, R.rb, R.n2 = R.pg, R.pa, R.x4, R.ra, R.rg, R.n1
    R.gqkv, R.xsg, R.xrg = R.n2, R.xs, R.xr
    S, G, PART, LAND = R.shard, R.gathered, R.part, R.land
    OUT, GW, GG = R.padded_out, R.gw, R.gg
    width = G.shape[2]
    own = width // (2 * n)
    span = width // 4
    heads = span // HEAD_DIM

    x = lax.axis_index("tensor")
    d = lax.axis_index("dp")
    c = lax.rem(d, 2)
    other = 1 - c
    chip = d // 2
    y, z = lax.rem(chip, 2), chip // 2
    r = z + y * (n - 1 - 2 * z)
    half = n // 2

    def chip_at(pos):
        pos = lax.rem(pos + 2 * n, n)
        upper = pos // half
        return 2 * (pos + upper * (n - 1 - 2 * pos)) + upper

    near_mate = d + 1 - 2 * c
    mate, across, diagonal = (near_mate, x), (d, 1 - x), (near_mate, 1 - x)
    ahead = (2 * chip_at(r + 1) + c, x)
    behind = (2 * chip_at(r - 1) + c, x)
    way = (ahead, behind)

    offsets = {hop: 2 * own * chip_at(r + hop) for hop in range(-half, half + 1)}


    my_rows = pl.ds(pl.multiple_of(own * d, 16), own)

    def fetch(slot, source, target):
        copy = pltpu.make_async_copy(source, target, R.local.at[slot])
        copy.start()
        return copy

    fetched = [
        fetch(0, R.tokens_hbm, R.tokens),
        fetch(1, R.txt_in_hbm, R.txt_in),
        fetch(2, R.txt_out_hbm, R.txt_out),
        fetch(3, R.vis_in_hbm, R.vis_in),
        fetch(4, R.vis_out_hbm, R.vis_out),
        fetch(5, R.cotangent_hbm, R.cotangent),
    ]

    barrier = pltpu.get_barrier_semaphore()
    for device in (mate, across, diagonal, ahead, behind):
        pl.semaphore_signal(barrier, inc=1, device_id=device, device_id_type=MESH)

    mine, theirs = pl.multiple_of(2 * c, 2), pl.multiple_of(2 * other, 2)
    pair_own = 2 * c + x
    pair_across = 2 * c + 1 - x

    started = []
    counter = [0]

    def remote(source, target, device):
        index = counter[0]
        counter[0] += 1
        return pltpu.make_async_remote_copy(
            src_ref=source,
            dst_ref=target,
            send_sem=R.sent.at[index],
            recv_sem=R.came.at[index],
            device_id=device,
            device_id_type=MESH,
        )

    def start(source, target, device):
        copy = remote(source, target, device)
        copy.start()
        started.append(copy)
        return copy

    def sent(copy):
        copy.wait_send()
        started[:] = [one for one in started if one is not copy]

    near, far = (ATT, 0, own), (ATT, own, own)
    parts = [near, far] + [(k, 0, 2 * own) for k in (TIN, TOUT, VIN, VOUT)]
    tin, tout, vin, vout = parts[2:]
    longest = half

    def hops(part, side):
        return half if (parts.index(part) + side) % 2 == 0 else n - 1 - half

    def ring_index(part, side, s):
        return (parts.index(part) * 2 + side) * longest + s

    def view(ref, part, hop):
        k, first, count = part
        return ref.at[k, pl.ds(pl.multiple_of(offsets[hop] + first, 16), count), :]

    sum_base = len(parts) * 2 * longest

    def gather_copy(part, side, s, pos):
        block = view(G, part, pos)
        i = ring_index(part, side, s)
        return pltpu.make_async_remote_copy(
            src_ref=block,
            dst_ref=block,
            send_sem=R.ring_sent.at[part[0]],
            recv_sem=R.ring_came.at[i],
            device_id=way[side],
            device_id_type=MESH,
        )

    def gather(part, s):
        for side in range(2):
            pos = -s if side == 0 else s
            if 0 < s <= hops(part, side):
                gather_copy(part, side, s - 1, pos).wait_recv()
            if s < hops(part, side):
                gather_copy(part, side, s, pos).start()

    def landed(part, side, s):
        k, first, count = part
        return LAND.at[k, side * hops(part, 0) + s, pl.ds(first, count), :]

    def sum_copy(part, side, s, source):
        i = sum_base + ring_index(part, side, s)
        return pltpu.make_async_remote_copy(
            src_ref=source,
            dst_ref=landed(part, side, s),
            send_sem=R.ring_sent.at[5 + part[0]],
            recv_sem=R.ring_came.at[i],
            device_id=way[side],
            device_id_type=MESH,
        )

    def pass_sum(part, s):
        for side in range(2):
            reach = hops(part, side)
            if s >= reach:
                continue
            pos = reach - s if side == 0 else s - reach
            term = view(PART, part, pos)
            if s == 0:
                source = term
            else:
                source = landed(part, side, s - 1)
                sum_copy(part, side, s - 1, source).wait_recv()
                source[...] = (source[...].astype(F32) + term[...].astype(F32)).astype(BF)
            sum_copy(part, side, s, source).start()

    finals = []
    row_sums = [[], []]

    def end_sum(*group):
        for part in group:
            for side in range(2):
                last = hops(part, side) - 1
                sum_copy(part, side, last, landed(part, side, last)).wait_recv()
        for k in sorted({part[0] for part in group}):
            first = hops(near if k == ATT else parts[k + 1], 0) - 1
            earlier = 1 if k == ATT else 0
            counted = 3 * span if k == ATT else width

            def total(core):
                rows = pl.ds(pl.multiple_of(own * core, 16), own)
                chip_rows = pl.ds(pl.multiple_of(2 * own * chip + own * core, 16), own)
                block = (
                    LAND[k, first - earlier * core, rows, :].astype(F32)
                    + LAND[k, n - 2, rows, :].astype(F32)
                    + PART[k, chip_rows, :].astype(F32)
                )
                if k in (ATT, TIN, VIN):
                    weighted = G[k, chip_rows, :].astype(F32)[:, :counted] * block[:, :counted]
                    row_sum = jnp.sum(weighted, axis=-1, keepdims=True)
                    row_sums[0 if core is c else 1].append((k, row_sum))
                return block

            R.give[k] = total(other)
            finals.append(start(R.give.at[k], GW.at[k, c], mate))
            GW[k, c] = total(c)

    def shard_part(k, value):
        for core in range(2):
            S[k, core] = value(core).astype(BF)

    gain_one, gain_two = column(R.gain_attn), column(R.gain_ffn)

    def attention_part(core):
        cols = slice(core * span, (core + 1) * span)
        return jnp.concatenate(
            [
                R.w_query[:, cols].astype(F32) * (gain_one * HEAD_DIM**-0.5),
                R.w_key[:, cols].astype(F32) * gain_one,
                R.w_value[:, cols].astype(F32) * gain_one,
                R.w_out[:, cols].astype(F32),
            ],
            axis=1,
        )

    def half_of(ref, core):
        return ref[:, core * width : (core + 1) * width].astype(F32) * gain_two

    def turned_half(ref, core):
        return ref[:, core * width : (core + 1) * width]

    lengths = R.lengths

    def live(t, slots):
        return (slots < PATCHES) | ((slots >= VIS) & (slots < VIS + lengths[t]))

    def live_rows(t, j, count=64):
        slots = lax.broadcasted_iota(jnp.int32, (count, 1), 0) + j * count
        return live(t, slots).astype(F32)

    row_count = R.tokens.shape[0]

    def placed(t, slots, rows, kept):
        source = t * (PATCHES + CAPTION) + slots - (slots >= VIS).astype(jnp.int32) * (VIS - PATCHES)
        return ((rows == source) & kept).astype(F32).astype(BF)

    def chooser(t, only_live):
        slots = lax.broadcasted_iota(jnp.int32, (SEQ, row_count), 0)
        rows = lax.broadcasted_iota(jnp.int32, (SEQ, row_count), 1)
        filled = (slots < PATCHES) | ((slots >= VIS) & (slots < VIS + CAPTION))
        return placed(t, slots, rows, live(t, slots) if only_live else filled)

    shard_part(ATT, attention_part)
    G[ATT, my_rows, :] = S[ATT, c]
    for t in range(2):
        R.lens[t] = jnp.full((8, 128), lengths[t], jnp.int32).astype(F32)
    pl.semaphore_wait(barrier, 5)
    shard_a = start(S.at[pl.ds(0, 1), other], G.at[pl.ds(0, 1), my_rows, :], mate)
    send_lens = start(R.lens, R.lens4.at[pl.ds(mine, 2)], mate)
    fetched[0].wait()
    for t in range(2):
        R.x4[2 * c + t] = mm(chooser(t, False), R.tokens[...]).astype(BF)
        R.lens4[2 * c + t] = R.lens[t]
    send_x = start(R.x4.at[pl.ds(mine, 2)], R.x4.at[pl.ds(mine, 2)], mate)
    shard_a.wait_recv()
    gather(near, 0)
    gather(far, 0)
    for copy in fetched[1:]:
        copy.wait()

    shard_part(TIN, functools.partial(half_of, R.txt_in))
    shard_part(TOUT, functools.partial(turned_half, R.txt_out))
    shard_part(VIN, functools.partial(half_of, R.vis_in))
    shard_part(VOUT, functools.partial(turned_half, R.vis_out))
    shard_b = start(S.at[pl.ds(1, 4), other], G.at[pl.ds(1, 4), my_rows, :], mate)
    for k in (TIN, TOUT, VIN, VOUT):
        G[k, my_rows, :] = S[k, c]
    gather(near, 1)
    for t in range(2):
        R.gz[2 * c + t] = mm(chooser(t, True), R.cotangent[...]).astype(BF)
        if t == 0:
            gather(far, 1)
    send_gz = start(R.gz.at[pl.ds(mine, 2)], R.gz.at[pl.ds(mine, 2)], mate)
    R.dy[...] = mm(chooser(x, False), R.cotangent[...]).astype(BF)
    for t in range(2):
        R.x[t] = R.x4[2 * c + t]
    shard_b.wait_recv()
    gather(tin, 0)
    gather(near, 2)
    send_x.wait_recv()

    for i in range(4):

        @pl.loop(0, SEQ // 64)
        def _(j, i=i):
            rows = pl.ds(pl.multiple_of(j * 64, 64), 64)
            normed, _ = normalize(R.x4[i, rows, :].astype(F32))
            R.n1[i, rows, :] = normed.astype(BF)

        R.n1t[:, i * SEQ : (i + 1) * SEQ] = R.n1[i].T
        if i == 0:
            gather(far, 2)
        if i == 1:
            gather(tout, 0)
            gather(near, 3)
        if i == 2:
            gather(far, 3)
            gather(vin, 0)
            gather(vout, 0)
    send_gz.wait_recv()
    send_lens.wait_recv()
    gather(near, 4)
    gather(far, 4)

    R.wo[...] = G[ATT][:, 3 * span :]

    @pl.loop(0, 4)
    def _(i):
        projected = mm(R.n1[i], G[ATT][:, : 3 * span]).astype(BF)
        R.q[i] = projected[:, :span]
        R.k[i] = projected[:, span : 2 * span]
        R.v[i] = projected[:, 2 * span :]

    lane = lax.broadcasted_iota(jnp.int32, (1, span), 1) // HEAD_DIM

    def only(head, values):
        return values * (lane == head).astype(F32).astype(BF)

    def head_rows(values, head):
        return values[head * HEAD_DIM : (head + 1) * HEAD_DIM, :]

    order = []
    for j in range(4):
        core = other if j < 2 else c
        turn = 1 - x if j % 2 == 0 else x
        order.append((turn, 2 * core + turn))
    attn_mate = [remote(R.pa.at[i], R.ra.at[turn], mate) for turn, i in order[:2]]
    cross_a = remote(R.xs, R.xr, across)

    for j, (turn, i) in enumerate(order):
        q, k, v = R.q[i], R.k[i], R.v[i]
        turned_v = v.T
        slots = lax.broadcasted_iota(jnp.int32, (SEQ, 1), 0)
        caption = (slots - VIS).astype(F32) < R.lens4[i][:1, :1]
        bias = jnp.where((slots < PATCHES) | ((slots >= VIS) & caption), 0.0, -1e30)
        contexts = []
        for h in range(heads):
            scores = mm_nt(only(h, k), q) + bias
            top = jnp.max(scores, axis=0, keepdims=True)
            weights = jnp.exp(scores - top)
            total = jnp.sum(weights, axis=0, keepdims=True)
            probs = (weights * (1.0 / total)).astype(BF)
            R.probs[i * heads + h] = probs
            contexts.append(mm(head_rows(turned_v, h), probs))
        contexts = jnp.concatenate(contexts, axis=0)
        R.ct[:, pl.ds(pl.multiple_of(i * SEQ, SEQ), SEQ)] = contexts.astype(BF)
        context = contexts.T.astype(BF)
        R.pa[i] = mm_nt(context, R.wo[...]).astype(BF)
        if j < 2:
            attn_mate[j].start()
        if j == 2:
            attn_mate[0].wait_recv()
            R.xs[...] = (R.pa[pair_across].astype(F32) + R.ra[1 - x].astype(F32)).astype(BF)
            cross_a.start()
        if j == 0:
            gather(tin, 1)
        if j == 1:
            gather(tout, 1)
        if j == 3:
            gather(tin, 2)
            gather(tout, 2)

    for copy in attn_mate:
        copy.wait_send()
    attn_mate[1].wait_recv()

    @pl.loop(0, width // 256)
    def _(j):
        cols = pl.ds(pl.multiple_of(j * 256, 256), 256)
        R.gzvt[cols, :] = R.gz[:, :VIS, cols].reshape(4 * VIS, 256).T
        R.gztt[cols, :] = R.gz[:, VIS:, cols].reshape(4 * TXT, 256).T

    gather(vin, 1)
    cross_a.wait_recv()

    @pl.loop(0, SEQ // 64)
    def _(j):
        rows = pl.ds(pl.multiple_of(j * 64, 64), 64)
        attended = (
            R.pa[pair_own, rows, :].astype(F32)
            + R.ra[x, rows, :].astype(F32)
            + R.xr[rows, :].astype(F32)
        )
        middle = R.x[x, rows, :].astype(F32) + live_rows(x, j) * attended
        R.y1[rows, :] = middle
        normed, _ = normalize(middle)
        R.n2[pair_own, rows, :] = normed.astype(BF)

    block = R.n2.at[pair_own]
    to_across = start(block, block, across)
    to_mate = start(block, block, mate)
    gather(vout, 1)
    gather(tin, 3)
    gather(tout, 3)
    to_across.wait_recv()
    block = R.n2.at[pair_across]
    passed = start(block, block, mate)
    gather(vin, 2)
    gather(vout, 2)
    gather(tin, 4)
    gather(tout, 4)
    to_mate.wait_recv()
    passed.wait_recv()

    def expert(pairs, low, high, w_in, w_out, h_ref, gu_ref, j):
        first, count = pairs
        per = high - low
        total_rows = count * per
        cols = pl.ds(pl.multiple_of(j * 256, 256), 256)
        inside = slice(first, first + count)
        R.u[:total_rows, :] = mm(
            R.n2[inside, low:high, :].reshape(total_rows, width), G[w_in, :, cols]
        )
        R.gh[:total_rows, :] = mm(
            R.gz[inside, low:high, :].reshape(total_rows, width), G[w_out, :, cols]
        )
        step = min(total_rows, VIS)

        @pl.loop(0, 2 * (total_rows // step))
        def _(i):
            lanes = lax.rem(i, 2) * 128
            rows = pl.ds(pl.multiple_of(i // 2 * step, 16), step)
            into = pl.ds(pl.multiple_of(first * per + i // 2 * step, 16), step)
            side = pl.ds(pl.multiple_of(lanes, 128), 128)
            pre = R.u[rows, side]
            cumulative = 0.5 * (1.0 + lax.erf(pre * inv_root_two))
            density = jnp.exp(-0.5 * pre * pre) * inv_root_tau
            onto = pl.ds(pl.multiple_of(j * 256 + lanes, 128), 128)
            h_ref[into, onto] = (pre * cumulative).astype(BF)
            gu_ref[into, onto] = (R.gh[rows, side] * (cumulative + pre * density)).astype(BF)

    def weight_grad(k, turned, ref):
        @pl.loop(0, width // 256)
        def _(j):
            cols = pl.ds(pl.multiple_of(j * 256, 256), 256)
            PART[k, :, cols] = mm(turned[...], ref[:, cols]).astype(BF)

    tiles = width // 256

    @pl.loop(0, tiles)
    def _(j):
        expert((0, 4), VIS, SEQ, TIN, TOUT, R.ht, R.gut, j)

    gather(vin, 3)
    weight_grad(TOUT, R.gztt, R.ht)

    @pl.loop(0, width // 256)
    def _(j):
        cols = pl.ds(pl.multiple_of(j * 256, 256), 256)
        R.n2vt[cols, :] = R.n2[:, :VIS, cols].reshape(4 * VIS, 256).T
        R.n2tt[cols, :] = R.n2[:, VIS:, cols].reshape(4 * TXT, 256).T

    gather(vout, 3)
    weight_grad(TIN, R.n2tt, R.gut)
    pass_sum(tout, 0)
    pass_sum(tin, 0)

    def text_terms(target, rows, weight):
        target[:, VIS:, :] = mm_nt(rows, G[weight]).astype(BF).reshape(4, TXT, width)

    text_terms(R.pg, R.gut[...], TIN)
    text_terms(R.pf, R.ht[...], TOUT)
    gather(vin, 4)
    gather(vout, 4)

    def terms(target, rows, weight, m):
        part = mm_nt(rows[2 * m * VIS : 2 * (m + 1) * VIS, :], G[weight]).astype(BF)
        target[2 * m : 2 * m + 2, :VIS, :] = part.reshape(2, VIS, width)

    mate_g = remote(R.pg.at[pl.ds(theirs, 2)], R.rg, mate)
    cross_g = remote(R.xsg, R.xrg, across)
    gy_across = remote(R.gy.at[x], R.gy.at[x], across)
    gy_mate = remote(R.ga.at[pair_own], R.ga.at[pair_own], mate)
    gy_passed = remote(R.ga.at[pair_across], R.ga.at[pair_across], mate)
    started.extend([cross_g, gy_across, gy_mate, gy_passed])

    def image_terms(m):
        terms(R.pg, R.guv, VIN, m)
        pl.when(c != m)(mate_g.start)

    def sum_cores(m):
        @pl.when(c == m)
        def _():
            mate_g.wait_recv()
            R.xsg[...] = (R.pg[pair_across].astype(F32) + R.rg[1 - x].astype(F32)).astype(BF)
            cross_g.start()

    def middle_back(m):
        @pl.when(c == m)
        def _():
            cross_g.wait_recv()

            @pl.loop(0, SEQ // 64)
            def _(j):
                rows = pl.ds(pl.multiple_of(j * 64, 64), 64)
                grad_normed = (
                    R.pg[pair_own, rows, :].astype(F32)
                    + R.rg[x, rows, :].astype(F32)
                    + R.xrg[rows, :].astype(F32)
                )
                normed, inverse = normalize(R.y1[rows, :])
                grad = R.dy[rows, :].astype(F32) + normalize_back(grad_normed, normed, inverse)
                R.gy[x, rows, :] = grad.astype(BF)
                R.ga[pair_own, rows, :] = (grad * live_rows(x, j)).astype(BF)

            gy_across.start()
            gy_mate.start()

    def middle_pass(m):
        @pl.when(c == m)
        def _():
            gy_across.wait_recv()

            @pl.loop(0, SEQ // 64)
            def _(j):
                rows = pl.ds(pl.multiple_of(j * 64, 64), 64)
                R.ga[pair_across, rows, :] = (
                    R.gy[1 - x, rows, :].astype(F32) * live_rows(1 - x, j)
                ).astype(BF)

            gy_passed.start()

    def middle_came(m):
        @pl.when(c != m)
        def _():
            gy_mate.wait_recv()
            gy_passed.wait_recv()

    sent(send_x)
    cross_a.wait_send()

    @pl.loop(0, tiles)
    def _(j):
        expert((0, 2), 0, VIS, VIN, VOUT, R.hv, R.guv, j)

    image_terms(0)

    @pl.loop(0, tiles)
    def _(j):
        expert((2, 2), 0, VIS, VIN, VOUT, R.hv, R.guv, j)
        pl.when(j == 0)(functools.partial(sum_cores, 0))

    pass_sum(tout, 1)
    image_terms(1)
    for copy in (to_across, to_mate, passed):
        sent(copy)
    sum_cores(1)
    pass_sum(tin, 1)
    weight_grad(VOUT, R.gzvt, R.hv)
    middle_back(0)
    pass_sum(vout, 0)
    pass_sum(tout, 2)
    weight_grad(VIN, R.n2vt, R.guv)
    pass_sum(vin, 0)
    pass_sum(tin, 2)

    terms(R.pf, R.hv, VOUT, 0)
    middle_pass(0)
    middle_back(1)
    pass_sum(tout, 3)
    terms(R.pf, R.hv, VOUT, 1)
    mate_f = start(R.pf.at[pl.ds(theirs, 2)], R.rf, mate)
    cross_f = remote(R.xsf, R.xrf, across)
    started.append(cross_f)
    pass_sum(tin, 3)
    mate_g.wait_send()
    middle_came(0)

    back_mate = [remote(R.pb.at[theirs + t], R.rb.at[t], mate) for t in range(2)]
    back_cross = [remote(R.xsb.at[t], R.xrb.at[t], across) for t in range(2)]
    started.extend(back_mate + back_cross)

    def attention_back(m, t):
        i = 2 * m + t
        grad_context = mm(R.ga[i], R.wo[...]).astype(BF)
        q, k, v = R.q[i], R.k[i], R.v[i]
        turned_k = k.T
        grad_q = []
        grad_k = jnp.zeros((SEQ, span), F32)
        grad_v = jnp.zeros((SEQ, span), F32)
        for h in range(heads):
            probs = R.probs[i * heads + h]
            grad_probs = mm_nt(only(h, v), grad_context)
            exact = probs.astype(F32)
            inner = jnp.sum(grad_probs * exact, axis=0, keepdims=True)
            grad_scores = (exact * (grad_probs - inner)).astype(BF)
            grad_q.append(mm(head_rows(turned_k, h), grad_scores))
            grad_k += mm(grad_scores, only(h, q))
            grad_v += mm(probs, only(h, grad_context))
        grad_q = jnp.concatenate(grad_q, axis=0).T
        joined = jnp.concatenate([grad_q, grad_k, grad_v], axis=1).astype(BF)
        R.gqkv[i, :, : 3 * span] = joined
        R.pb[i] = mm_nt(joined, G[ATT][:, : 3 * span]).astype(BF)
        pl.when(c != m)(back_mate[t].start)

    def back_sum(m, t):
        @pl.when(c == m)
        def _():
            back_mate[t].wait_recv()
            R.xsb[t] = (R.pb[2 * m + t].astype(F32) + R.rb[t].astype(F32)).astype(BF)
            back_cross[t].start()

    attention_back(0, 0)
    pass_sum(vout, 1)
    mate_f.wait_recv()
    R.xsf[...] = (R.pf[pair_across].astype(F32) + R.rf[1 - x].astype(F32)).astype(BF)
    R.fown[...] = (R.pf[pair_own].astype(F32) + R.rf[x].astype(F32)).astype(BF)
    middle_pass(1)
    cross_f.start()
    attention_back(0, 1)
    back_sum(0, 0)

    pass_sum(vin, 1)
    middle_came(1)
    attention_back(1, 0)
    back_sum(0, 1)

    pass_sum(vout, 2)
    attention_back(1, 1)
    back_sum(1, 0)
    pass_sum(vin, 2)

    @pl.loop(0, width // 256)
    def _(j):
        rows = pl.ds(pl.multiple_of(j * 256, 256), 256)
        grads = mm(R.n1t[rows, :], R.gqkv[:, :, : 3 * span].reshape(4 * SEQ, 3 * span))
        grad_o = mm(R.ct[...], R.ga[:, :, rows].reshape(4 * SEQ, 256)).T
        PART[ATT, rows, :] = jnp.concatenate([grads, grad_o], axis=1).astype(BF)

    pass_sum(far, 0)
    pass_sum(near, 0)

    cross_f.wait_recv()

    @pl.loop(0, SEQ // 64)
    def _(j):
        rows = pl.ds(pl.multiple_of(j * 64, 64), 64)
        branch = R.fown[rows, :].astype(F32) + R.xrf[rows, :].astype(F32)
        OUT[x, rows, :] = (R.y1[rows, :] + live_rows(x, j) * branch).astype(BF)

    out_across = start(OUT.at[x], OUT.at[x], across)
    back_sum(1, 1)
    pass_sum(vout, 3)
    pass_sum(vin, 3)

    def input_back(m, t):
        @pl.when(c == m)
        def _():
            back_cross[t].wait_recv()

            @pl.loop(0, SEQ // 64)
            def _(j):
                rows = pl.ds(pl.multiple_of(j * 64, 64), 64)
                grad_normed = R.xsb[t, rows, :].astype(F32) + R.xrb[t, rows, :].astype(F32)
                normed, inverse = normalize(R.x[t, rows, :].astype(F32))
                grad = R.gy[t, rows, :].astype(F32) + normalize_back(grad_normed, normed, inverse)
                high = grad.astype(BF)
                rows = pl.ds(pl.multiple_of(t * SEQ + j * 64, 64), 64)
                R.hv[rows, :] = high
                R.guv[rows, :] = (grad - high.astype(F32)).astype(BF)

    pass_sum(far, 1)
    input_back(0, 0)
    pass_sum(near, 1)
    input_back(0, 1)
    end_sum(tout, tin)
    pass_sum(far, 2)
    pass_sum(near, 2)
    end_sum(vout, vin)

    leaving = []

    def leave(slot, source, target):
        leaving.append(fetch(slot, source, target))

    slots = lax.broadcasted_iota(jnp.int32, (row_count, 2 * SEQ), 1)
    rows = lax.broadcasted_iota(jnp.int32, (row_count, 2 * SEQ), 0)
    turn = slots // SEQ
    back = placed(turn, slots - turn * SEQ, rows, slots >= 0)
    out_across.wait_recv()
    R.out_tokens[...] = mm(back, OUT[...].reshape(2 * SEQ, width)).astype(BF)
    leave(6, R.out_tokens, R.out_tokens_hbm)
    for copy in finals:
        copy.wait_recv()
    finals.clear()
    leave(7, GW.at[pl.ds(1, 4)], R.gw_hbm.at[pl.ds(1, 4)])
    pass_sum(far, 3)
    pass_sum(near, 3)
    input_back(1, 0)
    input_back(1, 1)
    R.grad_tokens[...] = mm(back, R.hv[: 2 * SEQ, :]) + mm(back, R.guv[: 2 * SEQ, :])
    leave(8, R.grad_tokens, R.grad_tokens_hbm)
    end_sum(far, near)

    first_lane = lax.broadcasted_iota(jnp.int32, (own, 128), 1) == 0
    for place in range(2):
        attn = sum(total for k, total in row_sums[place] if k == ATT)
        experts = sum(total for k, total in row_sums[place] if k != ATT)
        R.gs[place] = jnp.where(first_lane, attn, experts)
    peers = [
        start(R.gs.at[place], R.gr.at[slot], device)
        for slot, (place, device) in enumerate(((1, mate), (0, across), (1, diagonal)))
    ]
    for copy in finals + peers:
        copy.wait_recv()
    leave(9, GW.at[pl.ds(0, 1)], R.gw_hbm.at[pl.ds(0, 1)])
    GG[...] = (R.gs[0] + R.gr[1]) + (R.gr[0] + R.gr[2])

    for copy in started:
        copy.wait_send()
    for copy in leaving:
        copy.wait()
    for k in range(5):
        for semaphore in (k, 5 + k):
            pltpu.make_async_remote_copy(
                src_ref=LAND.at[k],
                dst_ref=LAND.at[k],
                send_sem=R.ring_sent.at[semaphore],
                recv_sem=R.ring_came.at[0],
                device_id=ahead,
                device_id_type=MESH,
            ).wait_send()


def finish_kernel(n_results, out, gtok, gw_hbm, gg, gain_attn, gain_ffn, *rest):
    results, scratch = rest[:n_results], rest[n_results:]
    buffers, (out_buffer, gtok_buffer, gw, came, gone) = scratch[:n_results], scratch[n_results:]
    arriving = [
        pltpu.make_async_copy(source, target, came.at[slot])
        for slot, (source, target) in enumerate(((gw_hbm, gw), (out, out_buffer), (gtok, gtok_buffer)))
    ]
    for copy in arriving:
        copy.start()
    width = gw.shape[3]
    own = gw.shape[2]
    span = width // 4
    gain_one, gain_two = column(gain_attn), column(gain_ffn)
    square = unit(own).astype(F32)
    leaving = []

    def leave(slot, source):
        copy = pltpu.make_async_copy(source, results[slot], gone.at[slot])
        copy.start()
        leaving.append(copy)

    def both(part):
        cols = slice(part * span, (part + 1) * span)
        return jnp.concatenate([gw[ATT, core][:, cols] for core in range(2)], axis=1)

    def put(slot, value):
        buffers[slot][...] = value
        leave(slot, buffers[slot])

    put(2, jnp.sum(square * (gg[:, :1] / gain_one), axis=0, keepdims=True))
    put(7, jnp.sum(square * (gg[:, 1:2] / gain_two), axis=0, keepdims=True))
    arriving[0].wait()
    for slot, k, scale in ((8, VIN, gain_two), (9, VOUT, 1.0), (10, TIN, gain_two), (11, TOUT, 1.0)):
        put(slot, jnp.concatenate([gw[k, 0], gw[k, 1]], axis=1) * scale)
    put(3, both(0) * (gain_one * HEAD_DIM**-0.5))
    put(4, both(1) * gain_one)
    put(5, both(2) * gain_one)
    put(6, both(3))
    arriving[1].wait()
    leave(0, out_buffer)
    arriving[2].wait()
    leave(1, gtok_buffer)
    for copy in leaving:
        copy.wait()


def fused_layer(
    tokens,
    caption_lengths,
    gain_attn,
    w_query,
    w_key,
    w_value,
    w_out,
    gain_ffn,
    vis_in,
    vis_out,
    txt_in,
    txt_out,
    cotangent,
):
    n = lax.axis_size("dp") // 2
    own = w_query.shape[0]
    row_count, width = tokens.shape
    span = width // 4
    heads = span // HEAD_DIM
    gain_one, gain_two = gain_attn.reshape(1, own), gain_ffn.reshape(1, own)

    rows = 4 * SEQ
    scratch = dict(
        tokens=pltpu.VMEM((row_count, width), BF),
        cotangent=pltpu.VMEM((row_count, width), BF),
        txt_in=pltpu.VMEM((own, 2 * width), BF),
        txt_out=pltpu.VMEM((own, 2 * width), BF),
        vis_in=pltpu.VMEM((own, 2 * width), BF),
        vis_out=pltpu.VMEM((own, 2 * width), BF),
        out_tokens=pltpu.VMEM((row_count, width), BF),
        grad_tokens=pltpu.VMEM((row_count, width), F32),
        gw=pltpu.VMEM((5, 2, own, width), F32),
        local=pltpu.SemaphoreType.DMA((10,)),
        shard=pltpu.VMEM((5, 2, own, width), BF),
        lens=pltpu.VMEM((2, 8, 128), F32),
        x=pltpu.VMEM((2, SEQ, width), BF),
        dy=pltpu.VMEM((SEQ, width), BF),
        padded_out=pltpu.VMEM((2, SEQ, width), BF),
        gathered=pltpu.VMEM((5, width, width), BF),
        part=pltpu.VMEM((5, width, width), BF),
        land=pltpu.VMEM((5, n - 1, 2 * own, width), BF),
        give=pltpu.VMEM((5, own, width), F32),
        x4=pltpu.VMEM((4, SEQ, width), BF),
        lens4=pltpu.VMEM((4, 8, 128), F32),
        n1=pltpu.VMEM((4, SEQ, width), BF),
        n1t=pltpu.VMEM((width, rows), BF),
        gz=pltpu.VMEM((4, SEQ, width), BF),
        gzvt=pltpu.VMEM((width, 4 * VIS), BF),
        ct=pltpu.VMEM((span, rows), BF),
        fown=pltpu.VMEM((SEQ, width), BF),
        gztt=pltpu.VMEM((width, 4 * TXT), BF),
        wo=pltpu.VMEM((width, span), BF),
        q=pltpu.VMEM((4, SEQ, span), BF),
        k=pltpu.VMEM((4, SEQ, span), BF),
        v=pltpu.VMEM((4, SEQ, span), BF),
        probs=pltpu.VMEM((4 * heads, SEQ, SEQ), BF),
        pa=pltpu.VMEM((4, SEQ, width), BF),
        ra=pltpu.VMEM((2, SEQ, width), BF),
        xs=pltpu.VMEM((SEQ, width), BF),
        xr=pltpu.VMEM((SEQ, width), BF),
        y1=pltpu.VMEM((SEQ, width), F32),
        n2vt=pltpu.VMEM((width, 4 * VIS), BF),
        n2tt=pltpu.VMEM((width, 4 * TXT), BF),
        u=pltpu.VMEM((4 * VIS, 256), F32),
        gh=pltpu.VMEM((4 * VIS, 256), F32),
        hv=pltpu.VMEM((4 * VIS, width), BF),
        guv=pltpu.VMEM((4 * VIS, width), BF),
        ht=pltpu.VMEM((4 * TXT, width), BF),
        gut=pltpu.VMEM((4 * TXT, width), BF),
        pg=pltpu.VMEM((4, SEQ, width), BF),
        rg=pltpu.VMEM((2, SEQ, width), BF),
        gy=pltpu.VMEM((2, SEQ, width), BF),
        xsf=pltpu.VMEM((SEQ, width), BF),
        xrf=pltpu.VMEM((SEQ, width), BF),
        xsb=pltpu.VMEM((2, SEQ, width), BF),
        xrb=pltpu.VMEM((2, SEQ, width), BF),
        gs=pltpu.VMEM((2, own, 128), F32),
        gr=pltpu.VMEM((3, own, 128), F32),
        sent=pltpu.SemaphoreType.DMA((40,)),
        came=pltpu.SemaphoreType.DMA((40,)),
        ring_sent=pltpu.SemaphoreType.DMA((10,)),
        ring_came=pltpu.SemaphoreType.DMA((6 * 2 * (n // 2) * 2,)),
    )
    inputs = dict(
        lengths=caption_lengths,
        tokens_hbm=tokens,
        cotangent_hbm=cotangent,
        gain_attn=gain_one,
        gain_ffn=gain_two,
        w_query=w_query,
        w_key=w_key,
        w_value=w_value,
        w_out=w_out.T,
        vis_in_hbm=vis_in,
        vis_out_hbm=vis_out.T,
        txt_in_hbm=txt_in,
        txt_out_hbm=txt_out.T,
    )
    results = dict(
        out_tokens_hbm=jax.ShapeDtypeStruct((row_count, width), BF),
        grad_tokens_hbm=jax.ShapeDtypeStruct((row_count, width), F32),
        gw_hbm=jax.ShapeDtypeStruct((5, 2, own, width), F32),
        gg=jax.ShapeDtypeStruct((own, 128), F32),
    )
    vmem, hbm = pl.BlockSpec(memory_space=pltpu.VMEM), pl.BlockSpec(memory_space=pl.ANY)
    names = tuple(inputs) + tuple(results) + tuple(scratch)
    out, gtok, gw, gg = pl.pallas_call(
        functools.partial(layer_kernel, n, names),
        out_shape=tuple(results.values()),
        in_specs=[pl.BlockSpec(memory_space=pltpu.SMEM)] + [hbm if k.endswith(HBM) else vmem for k in names[1 : len(inputs)]],
        out_specs=[hbm if k.endswith(HBM) else vmem for k in results],
        scratch_shapes=list(scratch.values()),
        compiler_params=pltpu.CompilerParams(
            collective_id=0, has_side_effects=True, vmem_limit_bytes=60 * 2**20
        ),
    )(*inputs.values())

    shapes = (
        jax.ShapeDtypeStruct((row_count, width), BF),
        jax.ShapeDtypeStruct((row_count, width), F32),
        jax.ShapeDtypeStruct((1, own), F32),
        jax.ShapeDtypeStruct((own, 2 * span), F32),
        jax.ShapeDtypeStruct((own, 2 * span), F32),
        jax.ShapeDtypeStruct((own, 2 * span), F32),
        jax.ShapeDtypeStruct((own, 2 * span), F32),
        jax.ShapeDtypeStruct((1, own), F32),
        jax.ShapeDtypeStruct((own, 2 * width), F32),
        jax.ShapeDtypeStruct((own, 2 * width), F32),
        jax.ShapeDtypeStruct((own, 2 * width), F32),
        jax.ShapeDtypeStruct((own, 2 * width), F32),
    )
    buffers = [pltpu.VMEM(one.shape if slot > 1 else (8, 128), F32) for slot, one in enumerate(shapes)]
    final = pl.pallas_call(
        functools.partial(finish_kernel, len(shapes)),
        out_shape=shapes,
        in_specs=[hbm] * 3 + [vmem] * 3,
        out_specs=[hbm] * len(shapes),
        scratch_shapes=buffers
        + [
            pltpu.VMEM((row_count, width), BF),
            pltpu.VMEM((row_count, width), F32),
            pltpu.VMEM((5, 2, own, width), F32),
            pltpu.SemaphoreType.DMA((3,)),
            pltpu.SemaphoreType.DMA((len(shapes),)),
        ],
        compiler_params=pltpu.CompilerParams(vmem_limit_bytes=60 * 2**20),
    )(out, gtok, gw, gg, gain_one, gain_two)
    final = list(final)
    final[2] = final[2].reshape(own)
    final[7] = final[7].reshape(own)
    for turned in (6, 9, 11):
        final[turned] = final[turned].T
    return tuple(final)


def norm_parts(values):
    center = values - jnp.mean(values, axis=-1, keepdims=True)
    spread = jnp.mean(center * center, axis=-1, keepdims=True)
    inverse = lax.rsqrt(spread + epsilon)
    return (center * inverse, inverse)


def norm_back(grad_out, normed, inverse, gain):
    grad_normed = grad_out * gain
    grad_gain = jnp.sum(grad_out * normed, axis=0)
    inner = (
        grad_normed
        - jnp.mean(grad_normed, axis=-1, keepdims=True)
        - normed * jnp.mean(grad_normed * normed, axis=-1, keepdims=True)
    )
    return (inverse * inner, grad_gain)


def matmul(left, right):
    return jnp.dot(left, right, preferred_element_type=jnp.float32)


def matmul_tn(left, right):
    return lax.dot_general(
        left, right, (((0,), (0,)), ((), ())), preferred_element_type=jnp.float32
    )


def matmul_nt(left, right):
    return lax.dot_general(
        left, right, (((1,), (1,)), ((), ())), preferred_element_type=jnp.float32
    )


def gelu_slope(pre):
    cumulative = 0.5 * (1.0 + lax.erf(pre * inv_root_two))
    density = jnp.exp(-0.5 * pre * pre) * inv_root_tau
    return cumulative + pre * density


def expert_forward(rows, weight_in, weight_out):
    pre = matmul(rows, weight_in)
    hidden = jax.nn.gelu(pre, approximate=False).astype(jnp.bfloat16)
    return (pre, hidden, matmul(hidden, weight_out))


def expert_backward(rows, pre, hidden, grad_out, weight_in, weight_out):
    grad_weight_out = matmul_tn(hidden, grad_out)
    grad_hidden = matmul_nt(grad_out, weight_out)
    grad_pre = (grad_hidden * gelu_slope(pre)).astype(jnp.bfloat16)
    return (matmul_tn(rows, grad_pre), grad_weight_out, matmul_nt(grad_pre, weight_in))


def join_experts(image_rows, text_rows, pair_count, width):
    joined = jnp.concatenate(
        [
            image_rows.reshape(pair_count, PATCHES, width),
            text_rows.reshape(pair_count, CAPTION, width),
        ],
        axis=1,
    )
    return joined.reshape(-1, width)


def plain_layer(
    tokens,
    caption_lengths,
    gain_attn,
    w_query,
    w_key,
    w_value,
    w_out,
    gain_ffn,
    vis_in,
    vis_out,
    txt_in,
    txt_out,
    cotangent,
):
    seq_len = PATCHES + CAPTION
    width = tokens.shape[1]
    pair_count = tokens.shape[0] // seq_len
    half_pairs = pair_count // lax.axis_size("tensor")
    half_rows = half_pairs * seq_len
    row_start = lax.axis_index("tensor") * half_rows
    gain_one, query_w, key_w, value_w, out_w = (
        lax.all_gather(gain_attn, "dp", axis=0, tiled=True),
        lax.all_gather(w_query, "dp", axis=0, tiled=True),
        lax.all_gather(w_key, "dp", axis=0, tiled=True),
        lax.all_gather(w_value, "dp", axis=0, tiled=True),
        lax.all_gather(w_out, "dp", axis=1, tiled=True),
    )
    gain_two, vis_in_w, vis_out_w, txt_in_w, txt_out_w = (
        lax.all_gather(gain_ffn, "dp", axis=0, tiled=True),
        lax.all_gather(vis_in, "dp", axis=0, tiled=True),
        lax.all_gather(vis_out, "dp", axis=1, tiled=True),
        lax.all_gather(txt_in, "dp", axis=0, tiled=True),
        lax.all_gather(txt_out, "dp", axis=1, tiled=True),
    )
    gain_one = gain_one.astype(jnp.float32)
    gain_two = gain_two.astype(jnp.float32)
    head_local = query_w.shape[1] // HEAD_DIM
    score_scale = HEAD_DIM ** (-0.5)
    position = jnp.arange(seq_len, dtype=jnp.int32)
    live = (position[None, :] < PATCHES) | (position[None, :] - PATCHES < caption_lengths[:, None])
    valid_rows = live.astype(jnp.float32)
    mask_col = valid_rows.reshape(-1, 1)
    key_live = valid_rows[:, None, None, :] > 0.5

    def own_rows(values):
        return lax.dynamic_slice_in_dim(values, row_start, half_rows, 0)

    inputs = tokens.astype(jnp.float32)
    normed_one, inverse_one = norm_parts(inputs)
    first_in = (normed_one * gain_one).astype(jnp.bfloat16)

    def project(weight):
        return (
            matmul(first_in, weight)
            .astype(jnp.bfloat16)
            .reshape(pair_count, seq_len, head_local, HEAD_DIM)
        )

    queries = project(query_w)
    keys_all = project(key_w)
    values_all = project(value_w)

    def score_block():
        raw = (
            jnp.einsum("pqhe,pkhe->phqk", queries, keys_all, preferred_element_type=jnp.float32)
            * score_scale
        )
        return jnp.where(key_live, raw, -1e30)

    scores = score_block()
    top = jnp.max(scores, axis=-1, keepdims=True)
    weights = jnp.exp(scores - top)
    total = jnp.sum(weights, axis=-1, keepdims=True)
    probs = (weights / total).astype(jnp.bfloat16)
    log_total = top + jnp.log(total)
    context = jnp.einsum("phqk,pkhe->pqhe", probs, values_all, preferred_element_type=jnp.float32)
    context = context.astype(jnp.bfloat16).reshape(-1, head_local * HEAD_DIM)
    attn_terms = matmul(context, out_w)
    attended_own = lax.psum_scatter(
        attn_terms.astype(jnp.bfloat16), "tensor", scatter_dimension=0, tiled=True
    ).astype(jnp.float32)
    mask_own = own_rows(mask_col)
    middle_own = own_rows(inputs) + mask_own * attended_own
    normed_two, inverse_two = norm_parts(middle_own)
    second_own = (normed_two * gain_two).astype(jnp.bfloat16)
    grid = lax.all_gather(second_own, "tensor", axis=0, tiled=True).reshape(
        pair_count, seq_len, width
    )
    image_rows = grid[:, :PATCHES].reshape(-1, width)
    text_rows = grid[:, PATCHES:].reshape(-1, width)
    image_pre, image_hidden, image_part = expert_forward(image_rows, vis_in_w, vis_out_w)
    text_pre, text_hidden, text_part = expert_forward(text_rows, txt_in_w, txt_out_w)
    image_own, text_own = (
        lax.psum_scatter(
            image_part.astype(jnp.bfloat16), "tensor", scatter_dimension=0, tiled=True
        ).astype(jnp.float32),
        lax.psum_scatter(
            text_part.astype(jnp.bfloat16), "tensor", scatter_dimension=0, tiled=True
        ).astype(jnp.float32),
    )
    branch_own = join_experts(image_own, text_own, half_pairs, width)
    output_own = (middle_own + mask_own * branch_own).astype(jnp.bfloat16)
    upstream = cotangent.astype(jnp.float32)
    grad_branch = (upstream * mask_col).astype(jnp.bfloat16).reshape(pair_count, seq_len, width)
    image_grads = expert_backward(
        image_rows,
        image_pre,
        image_hidden,
        grad_branch[:, :PATCHES].reshape(-1, width),
        vis_in_w,
        vis_out_w,
    )
    text_grads = expert_backward(
        text_rows,
        text_pre,
        text_hidden,
        grad_branch[:, PATCHES:].reshape(-1, width),
        txt_in_w,
        txt_out_w,
    )
    back_image_own, back_text_own = (
        lax.psum_scatter(
            image_grads[2].astype(jnp.bfloat16), "tensor", scatter_dimension=0, tiled=True
        ).astype(jnp.float32),
        lax.psum_scatter(
            text_grads[2].astype(jnp.bfloat16), "tensor", scatter_dimension=0, tiled=True
        ).astype(jnp.float32),
    )
    grad_second_own = join_experts(back_image_own, back_text_own, half_pairs, width)
    grad_norm_own, gain_part = norm_back(grad_second_own, normed_two, inverse_two, gain_two)
    grad_middle_own = own_rows(upstream) + grad_norm_own
    output_wide, grad_middle, gain_parts = (
        lax.all_gather(
            output_own.astype(jnp.float32).astype(jnp.bfloat16), "tensor", axis=0, tiled=True
        ).astype(jnp.float32),
        lax.all_gather(grad_middle_own.astype(jnp.bfloat16), "tensor", axis=0, tiled=True).astype(
            grad_middle_own.dtype
        ),
        lax.all_gather(gain_part.astype(jnp.bfloat16), "tensor", axis=0, tiled=True).astype(
            gain_part.dtype
        ),
    )
    output = output_wide.astype(jnp.bfloat16)
    grad_gain_two = jnp.sum(gain_parts.reshape(-1, width), axis=0)
    grad_attended = (grad_middle * mask_col).astype(jnp.bfloat16)
    grad_out_w = matmul_tn(context, grad_attended)
    grad_context = (
        matmul_nt(grad_attended, out_w)
        .astype(jnp.bfloat16)
        .reshape(pair_count, seq_len, head_local, HEAD_DIM)
    )
    scores_again = score_block()
    probs_exact = jnp.exp(scores_again - log_total)
    grad_probs = jnp.einsum(
        "pqhe,pkhe->phqk", grad_context, values_all, preferred_element_type=jnp.float32
    )
    inner = jnp.sum(grad_probs * probs_exact, axis=-1, keepdims=True)
    grad_scores = (probs_exact * (grad_probs - inner)).astype(jnp.bfloat16)
    grad_values = jnp.einsum(
        "phqk,pqhe->pkhe", probs, grad_context, preferred_element_type=jnp.float32
    )
    grad_values = grad_values.astype(jnp.bfloat16).reshape(-1, head_local * HEAD_DIM)
    grad_queries = (
        jnp.einsum("phqk,pkhe->pqhe", grad_scores, keys_all, preferred_element_type=jnp.float32)
        * score_scale
    )
    grad_queries = grad_queries.astype(jnp.bfloat16).reshape(-1, head_local * HEAD_DIM)
    grad_keys = (
        jnp.einsum("phqk,pqhe->pkhe", grad_scores, queries, preferred_element_type=jnp.float32)
        * score_scale
    )
    grad_keys = grad_keys.astype(jnp.bfloat16).reshape(-1, head_local * HEAD_DIM)
    grad_query_w = matmul_tn(first_in, grad_queries)
    grad_key_w = matmul_tn(first_in, grad_keys)
    grad_value_w = matmul_tn(first_in, grad_values)
    first_part = (
        matmul_nt(grad_queries, query_w)
        + matmul_nt(grad_keys, key_w)
        + matmul_nt(grad_values, value_w)
    )
    grad_first = lax.psum(first_part.astype(jnp.bfloat16), "tensor").astype(jnp.float32)
    grad_norm_one, grad_gain_one = norm_back(grad_first, normed_one, inverse_one, gain_one)
    grad_inputs = grad_middle + grad_norm_one
    attn_sent = (
        lax.psum_scatter(grad_gain_one, "dp", scatter_dimension=0, tiled=True),
        lax.psum_scatter(grad_query_w, "dp", scatter_dimension=0, tiled=True),
        lax.psum_scatter(grad_key_w, "dp", scatter_dimension=0, tiled=True),
        lax.psum_scatter(grad_value_w, "dp", scatter_dimension=0, tiled=True),
        lax.psum_scatter(grad_out_w, "dp", scatter_dimension=1, tiled=True),
    )
    final_expert = (
        lax.psum_scatter(grad_gain_two, "dp", scatter_dimension=0, tiled=True),
        lax.psum_scatter(image_grads[0], "dp", scatter_dimension=0, tiled=True),
        lax.psum_scatter(image_grads[1], "dp", scatter_dimension=1, tiled=True),
        lax.psum_scatter(text_grads[0], "dp", scatter_dimension=0, tiled=True),
        lax.psum_scatter(text_grads[1], "dp", scatter_dimension=1, tiled=True),
    )
    return (
        output,
        grad_inputs,
        attn_sent[0],
        attn_sent[1],
        attn_sent[2],
        attn_sent[3],
        attn_sent[4],
        final_expert[0],
        final_expert[1],
        final_expert[2],
        final_expert[3],
        final_expert[4],
    )


def solution(mesh):
    def local(tokens, lengths, gain, w_query, *rest):
        ring = mesh.shape["dp"] // 2
        fits = (
            mesh.shape["tensor"] == 2
            and ring == 8
            and lengths.shape[0] == 2
            and w_query.shape[0] % 16 == 0
        )
        layer = fused_layer if fits else plain_layer
        return layer(tokens, lengths, gain, w_query, *rest)

    return jax.shard_map(
        local,
        mesh=mesh,
        in_specs=(
            P("dp", None),
            P("dp"),
            P("dp"),
            P("dp", "tensor"),
            P("dp", "tensor"),
            P("dp", "tensor"),
            P("tensor", "dp"),
            P("dp"),
            P("dp", "tensor"),
            P("tensor", "dp"),
            P("dp", "tensor"),
            P("tensor", "dp"),
            P("dp", None),
        ),
        out_specs=(
            P("dp", None),
            P("dp", None),
            P("dp"),
            P("dp", "tensor"),
            P("dp", "tensor"),
            P("dp", "tensor"),
            P("tensor", "dp"),
            P("dp"),
            P("dp", "tensor"),
            P("tensor", "dp"),
            P("dp", "tensor"),
            P("tensor", "dp"),
        ),
        check_vma=False,
    )
```

```python
import functools
import math
import types

import jax
import jax.numpy as jnp
from jax import lax
from jax.experimental import pallas as pl
from jax.experimental.pallas import tpu as pltpu
from jax.sharding import PartitionSpec as P

HEAD_DIM = 64
PATCHES = 197
CAPTION = 40
VIS = 208
TXT = 48
SEQ = VIS + TXT

MESH = pl.DeviceIdType.MESH
HBM = "_hbm"
BF = jnp.bfloat16
F32 = jnp.float32

ATT, TIN, TOUT, VIN, VOUT = range(5)

epsilon = 1e-05
inv_root_two = 1.0 / math.sqrt(2.0)
inv_root_tau = 1.0 / math.sqrt(2.0 * math.pi)


def mm(left, right):
    return jnp.dot(left, right, preferred_element_type=F32)


def mm_nt(left, right):
    return lax.dot_general(left, right, (((1,), (1,)), ((), ())), preferred_element_type=F32)


def mm_tn(left, right):
    return lax.dot_general(left, right, (((0,), (0,)), ((), ())), preferred_element_type=F32)


def normalize(values):
    center = values - jnp.mean(values, axis=-1, keepdims=True)
    spread = jnp.mean(center * center, axis=-1, keepdims=True)
    inverse = lax.rsqrt(spread + epsilon)
    return center * inverse, inverse


def normalize_back(grad_normed, normed, inverse):
    return inverse * (
        grad_normed
        - jnp.mean(grad_normed, axis=-1, keepdims=True)
        - normed * jnp.mean(grad_normed * normed, axis=-1, keepdims=True)
    )


def unit(size):
    rows = lax.broadcasted_iota(jnp.int32, (size, size), 0)
    return (rows == lax.broadcasted_iota(jnp.int32, (size, size), 1)).astype(F32).astype(BF)


def column(ref):
    size = ref.shape[1]
    return jnp.sum(unit(size).astype(F32) * ref[...].astype(F32), axis=1, keepdims=True)


def layer_kernel(n, names, *refs):
    R = types.SimpleNamespace(**dict(zip(names, refs)))
    R.pb, R.pf, R.ga, R.rf, R.rb, R.n2 = R.pg, R.pa, R.x4, R.ra, R.rg, R.n1
    R.gqkv, R.xsg, R.xrg = R.n2, R.xs, R.xr
    S, G, PART, LAND = R.shard, R.gathered, R.part, R.land
    OUT, GW, GG = R.padded_out, R.gw, R.gg
    width = G.shape[2]
    own = width // (2 * n)
    span = width // 4
    heads = span // HEAD_DIM

    x = lax.axis_index("tensor")
    d = lax.axis_index("dp")
    c = lax.rem(d, 2)
    other = 1 - c
    chip = d // 2
    y, z = lax.rem(chip, 2), chip // 2
    r = z + y * (n - 1 - 2 * z)
    half = n // 2

    def chip_at(pos):
        pos = lax.rem(pos + 2 * n, n)
        upper = pos // half
        return 2 * (pos + upper * (n - 1 - 2 * pos)) + upper

    near_mate = d + 1 - 2 * c
    mate, across, diagonal = (near_mate, x), (d, 1 - x), (near_mate, 1 - x)
    ahead = (2 * chip_at(r + 1) + c, x)
    behind = (2 * chip_at(r - 1) + c, x)
    way = (ahead, behind)

    offsets = {hop: 2 * own * chip_at(r + hop) for hop in range(-half, half + 1)}


    my_rows = pl.ds(pl.multiple_of(own * d, 16), own)

    def fetch(slot, source, target):
        copy = pltpu.make_async_copy(source, target, R.local.at[slot])
        copy.start()
        return copy

    fetched = [
        fetch(0, R.tokens_hbm, R.tokens),
        fetch(1, R.txt_in_hbm, R.txt_in),
        fetch(2, R.txt_out_hbm, R.txt_out),
        fetch(3, R.vis_in_hbm, R.vis_in),
        fetch(4, R.vis_out_hbm, R.vis_out),
        fetch(5, R.cotangent_hbm, R.cotangent),
    ]

    barrier = pltpu.get_barrier_semaphore()
    for device in (mate, across, diagonal, ahead, behind):
        pl.semaphore_signal(barrier, inc=1, device_id=device, device_id_type=MESH)

    mine, theirs = pl.multiple_of(2 * c, 2), pl.multiple_of(2 * other, 2)
    pair_own = 2 * c + x
    pair_across = 2 * c + 1 - x

    started = []
    counter = [0]

    def remote(source, target, device):
        index = counter[0]
        counter[0] += 1
        return pltpu.make_async_remote_copy(
            src_ref=source,
            dst_ref=target,
            send_sem=R.sent.at[index],
            recv_sem=R.came.at[index],
            device_id=device,
            device_id_type=MESH,
        )

    def start(source, target, device):
        copy = remote(source, target, device)
        copy.start()
        started.append(copy)
        return copy

    def sent(copy):
        copy.wait_send()
        started[:] = [one for one in started if one is not copy]

    def rows_at(hop):
        return pl.ds(pl.multiple_of(offsets[hop], 16), 2 * own)

    near, far = (ATT, 0, width // 2), (ATT, width // 2, width // 2)
    parts = [near, far] + [(k, 0, width) for k in (TIN, TOUT, VIN, VOUT)]
    tin, tout, vin, vout = parts[2:]
    longest = half

    def hops(part, side):
        return half if (parts.index(part) + side) % 2 == 0 else n - 1 - half

    def ring_index(part, side, s):
        return (parts.index(part) * 2 + side) * longest + s

    def view(ref, part, rows):
        k, first, count = part
        return ref.at[k, rows, pl.ds(first, count)]

    sum_base = len(parts) * 2 * longest

    def gather_copy(part, side, s, pos):
        block = view(G, part, rows_at(pos))
        i = ring_index(part, side, s)
        return pltpu.make_async_remote_copy(
            src_ref=block,
            dst_ref=block,
            send_sem=R.ring_sent.at[part[0]],
            recv_sem=R.ring_came.at[i],
            device_id=way[side],
            device_id_type=MESH,
        )

    def gather(part, s):
        for side in range(2):
            pos = -s if side == 0 else s
            if 0 < s <= hops(part, side):
                gather_copy(part, side, s - 1, pos).wait_recv()
            if s < hops(part, side):
                gather_copy(part, side, s, pos).start()

    def landed(part, side, s):
        k, first, count = part
        return LAND.at[k, side * hops(part, 0) + s, :, pl.ds(first, count)]

    def sum_copy(part, side, s, source):
        i = sum_base + ring_index(part, side, s)
        return pltpu.make_async_remote_copy(
            src_ref=source,
            dst_ref=landed(part, side, s),
            send_sem=R.ring_sent.at[5 + part[0]],
            recv_sem=R.ring_came.at[i],
            device_id=way[side],
            device_id_type=MESH,
        )

    def pass_sum(part, s):
        for side in range(2):
            reach = hops(part, side)
            if s >= reach:
                continue
            pos = reach - s if side == 0 else s - reach
            term = view(PART, part, rows_at(pos))
            if s == 0:
                source = term
            else:
                source = landed(part, side, s - 1)
                sum_copy(part, side, s - 1, source).wait_recv()
                source[...] = (source[...].astype(F32) + term[...].astype(F32)).astype(BF)
            sum_copy(part, side, s, source).start()

    finals = []
    row_sums = [[], []]

    def end_sum(*group):
        for part in group:
            k, first, count = part
            ends = []
            for side in range(2):
                end = landed(part, side, hops(part, side) - 1)
                sum_copy(part, side, hops(part, side) - 1, end).wait_recv()
                ends.append(end)
            cols = slice(first, first + count)
            counted = min(3 * span - first, count) if k == ATT else count

            def total(core):
                rows = pl.ds(pl.multiple_of(own * core, 16), own)
                chip_rows = pl.ds(pl.multiple_of(2 * own * chip + own * core, 16), own)
                block = (
                    ends[0][rows, :].astype(F32)
                    + ends[1][rows, :].astype(F32)
                    + PART[k, chip_rows, cols].astype(F32)
                )
                if k in (ATT, TIN, VIN):
                    weighted = G[k, chip_rows, cols].astype(F32)[:, :counted] * block[:, :counted]
                    total = jnp.sum(weighted, axis=-1, keepdims=True)
                    row_sums[0 if core is c else 1].append((k, total))
                return block

            R.give[k, :, cols] = total(other)
            finals.append(
                start(R.give.at[k, :, pl.ds(first, count)], GW.at[k, c, :, pl.ds(first, count)], mate)
            )
            GW[k, c, :, cols] = total(c)

    def shard_part(k, value):
        for core in range(2):
            S[k, core] = value(core).astype(BF)

    gain_one, gain_two = column(R.gain_attn), column(R.gain_ffn)

    def attention_part(core):
        cols = slice(core * span, (core + 1) * span)
        return jnp.concatenate(
            [
                R.w_query[:, cols].astype(F32) * (gain_one * HEAD_DIM**-0.5),
                R.w_key[:, cols].astype(F32) * gain_one,
                R.w_value[:, cols].astype(F32) * gain_one,
                R.w_out[:, cols].astype(F32),
            ],
            axis=1,
        )

    def half_of(ref, core):
        return ref[:, core * width : (core + 1) * width].astype(F32) * gain_two

    def turned_half(ref, core):
        return ref[:, core * width : (core + 1) * width]

    lengths = R.lengths

    def live(t, slots):
        return (slots < PATCHES) | ((slots >= VIS) & (slots < VIS + lengths[t]))

    def live_rows(t, j, count=64):
        slots = lax.broadcasted_iota(jnp.int32, (count, 1), 0) + j * count
        return live(t, slots).astype(F32)

    row_count = R.tokens.shape[0]

    def placed(t, slots, rows, kept):
        source = t * (PATCHES + CAPTION) + slots - (slots >= VIS).astype(jnp.int32) * (VIS - PATCHES)
        return ((rows == source) & kept).astype(F32).astype(BF)

    def chooser(t, only_live):
        slots = lax.broadcasted_iota(jnp.int32, (SEQ, row_count), 0)
        rows = lax.broadcasted_iota(jnp.int32, (SEQ, row_count), 1)
        filled = (slots < PATCHES) | ((slots >= VIS) & (slots < VIS + CAPTION))
        return placed(t, slots, rows, live(t, slots) if only_live else filled)

    shard_part(ATT, attention_part)
    G[ATT, my_rows, :] = S[ATT, c]
    for t in range(2):
        R.lens[t] = jnp.full((8, 128), lengths[t], jnp.int32).astype(F32)
    pl.semaphore_wait(barrier, 5)
    shard_a = start(S.at[pl.ds(0, 1), other], G.at[pl.ds(0, 1), my_rows, :], mate)
    send_lens = start(R.lens, R.lens4.at[pl.ds(mine, 2)], mate)
    fetched[0].wait()
    for t in range(2):
        R.x4[2 * c + t] = mm(chooser(t, False), R.tokens[...]).astype(BF)
        R.lens4[2 * c + t] = R.lens[t]
    send_x = start(R.x4.at[pl.ds(mine, 2)], R.x4.at[pl.ds(mine, 2)], mate)
    shard_a.wait_recv()
    gather(near, 0)
    gather(far, 0)
    for copy in fetched[1:]:
        copy.wait()

    shard_part(TIN, functools.partial(half_of, R.txt_in))
    shard_part(TOUT, functools.partial(turned_half, R.txt_out))
    shard_part(VIN, functools.partial(half_of, R.vis_in))
    shard_part(VOUT, functools.partial(turned_half, R.vis_out))
    shard_b = start(S.at[pl.ds(1, 4), other], G.at[pl.ds(1, 4), my_rows, :], mate)
    for k in (TIN, TOUT, VIN, VOUT):
        G[k, my_rows, :] = S[k, c]
    gather(near, 1)
    for t in range(2):
        R.gz[2 * c + t] = mm(chooser(t, True), R.cotangent[...]).astype(BF)
        if t == 0:
            gather(far, 1)
    send_gz = start(R.gz.at[pl.ds(mine, 2)], R.gz.at[pl.ds(mine, 2)], mate)
    R.dy[...] = mm(chooser(x, False), R.cotangent[...]).astype(BF)
    for t in range(2):
        R.x[t] = R.x4[2 * c + t]
    shard_b.wait_recv()
    gather(tin, 0)
    gather(near, 2)
    send_x.wait_recv()

    for i in range(4):

        @pl.loop(0, SEQ // 64)
        def _(j, i=i):
            rows = pl.ds(pl.multiple_of(j * 64, 64), 64)
            normed, _ = normalize(R.x4[i, rows, :].astype(F32))
            R.n1[i, rows, :] = normed.astype(BF)

        R.n1t[:, i * SEQ : (i + 1) * SEQ] = R.n1[i].T
        if i == 0:
            gather(far, 2)
        if i == 1:
            gather(tout, 0)
            gather(near, 3)
        if i == 2:
            gather(far, 3)
            gather(vin, 0)
            gather(vout, 0)
    send_gz.wait_recv()
    send_lens.wait_recv()
    gather(near, 4)
    gather(far, 4)

    R.wo[...] = G[ATT][:, 3 * span :]

    @pl.loop(0, 4)
    def _(i):
        projected = mm(R.n1[i], G[ATT][:, : 3 * span]).astype(BF)
        R.q[i] = projected[:, :span]
        R.k[i] = projected[:, span : 2 * span]
        R.v[i] = projected[:, 2 * span :]

    lane = lax.broadcasted_iota(jnp.int32, (1, span), 1) // HEAD_DIM

    def only(head, values):
        return values * (lane == head).astype(F32).astype(BF)

    def head_rows(values, head):
        return values[head * HEAD_DIM : (head + 1) * HEAD_DIM, :]

    order = []
    for j in range(4):
        core = other if j < 2 else c
        turn = 1 - x if j % 2 == 0 else x
        order.append((turn, 2 * core + turn))
    attn_mate = [remote(R.pa.at[i], R.ra.at[turn], mate) for turn, i in order[:2]]
    cross_a = remote(R.xs, R.xr, across)

    for j, (turn, i) in enumerate(order):
        q, k, v = R.q[i], R.k[i], R.v[i]
        turned_v = v.T
        slots = lax.broadcasted_iota(jnp.int32, (SEQ, 1), 0)
        caption = (slots - VIS).astype(F32) < R.lens4[i][:1, :1]
        bias = jnp.where((slots < PATCHES) | ((slots >= VIS) & caption), 0.0, -1e30)
        contexts = []
        for h in range(heads):
            scores = mm_nt(only(h, k), q) + bias
            top = jnp.max(scores, axis=0, keepdims=True)
            weights = jnp.exp(scores - top)
            total = jnp.sum(weights, axis=0, keepdims=True)
            probs = (weights * (1.0 / total)).astype(BF)
            R.probs[i * heads + h] = probs
            contexts.append(mm(head_rows(turned_v, h), probs))
        contexts = jnp.concatenate(contexts, axis=0)
        R.ct[:, pl.ds(pl.multiple_of(i * SEQ, SEQ), SEQ)] = contexts.astype(BF)
        context = contexts.T.astype(BF)
        R.pa[i] = mm_nt(context, R.wo[...]).astype(BF)
        if j < 2:
            attn_mate[j].start()
        if j == 2:
            attn_mate[0].wait_recv()
            R.xs[...] = (R.pa[pair_across].astype(F32) + R.ra[1 - x].astype(F32)).astype(BF)
            cross_a.start()
        if j == 0:
            gather(tin, 1)
        if j == 1:
            gather(tout, 1)
        if j == 3:
            gather(tin, 2)
            gather(tout, 2)

    for copy in attn_mate:
        copy.wait_send()
    attn_mate[1].wait_recv()

    @pl.loop(0, width // 256)
    def _(j):
        cols = pl.ds(pl.multiple_of(j * 256, 256), 256)
        R.gzvt[cols, :] = R.gz[:, :VIS, cols].reshape(4 * VIS, 256).T
        R.gztt[cols, :] = R.gz[:, VIS:, cols].reshape(4 * TXT, 256).T

    gather(vin, 1)
    cross_a.wait_recv()

    @pl.loop(0, SEQ // 64)
    def _(j):
        rows = pl.ds(pl.multiple_of(j * 64, 64), 64)
        attended = (
            R.pa[pair_own, rows, :].astype(F32)
            + R.ra[x, rows, :].astype(F32)
            + R.xr[rows, :].astype(F32)
        )
        middle = R.x[x, rows, :].astype(F32) + live_rows(x, j) * attended
        R.y1[rows, :] = middle
        normed, _ = normalize(middle)
        R.n2[pair_own, rows, :] = normed.astype(BF)

    block = R.n2.at[pair_own]
    to_across = start(block, block, across)
    to_mate = start(block, block, mate)
    gather(vout, 1)
    gather(tin, 3)
    gather(tout, 3)
    to_across.wait_recv()
    block = R.n2.at[pair_across]
    passed = start(block, block, mate)
    gather(vin, 2)
    gather(vout, 2)
    gather(tin, 4)
    gather(tout, 4)
    to_mate.wait_recv()
    passed.wait_recv()

    def expert(pairs, low, high, w_in, w_out, h_ref, gu_ref, j):
        first, count = pairs
        per = high - low
        total_rows = count * per
        cols = pl.ds(pl.multiple_of(j * 256, 256), 256)
        inside = slice(first, first + count)
        R.u[:total_rows, :] = mm(
            R.n2[inside, low:high, :].reshape(total_rows, width), G[w_in, :, cols]
        )
        R.gh[:total_rows, :] = mm(
            R.gz[inside, low:high, :].reshape(total_rows, width), G[w_out, :, cols]
        )
        step = min(total_rows, VIS)

        @pl.loop(0, 2 * (total_rows // step))
        def _(i):
            lanes = lax.rem(i, 2) * 128
            rows = pl.ds(pl.multiple_of(i // 2 * step, 16), step)
            into = pl.ds(pl.multiple_of(first * per + i // 2 * step, 16), step)
            side = pl.ds(pl.multiple_of(lanes, 128), 128)
            pre = R.u[rows, side]
            cumulative = 0.5 * (1.0 + lax.erf(pre * inv_root_two))
            density = jnp.exp(-0.5 * pre * pre) * inv_root_tau
            onto = pl.ds(pl.multiple_of(j * 256 + lanes, 128), 128)
            h_ref[into, onto] = (pre * cumulative).astype(BF)
            gu_ref[into, onto] = (R.gh[rows, side] * (cumulative + pre * density)).astype(BF)

    def weight_grad(k, turned, ref):
        @pl.loop(0, width // 256)
        def _(j):
            cols = pl.ds(pl.multiple_of(j * 256, 256), 256)
            PART[k, :, cols] = mm(turned[...], ref[:, cols]).astype(BF)

    tiles = width // 256

    @pl.loop(0, tiles)
    def _(j):
        expert((0, 4), VIS, SEQ, TIN, TOUT, R.ht, R.gut, j)

    gather(vin, 3)
    weight_grad(TOUT, R.gztt, R.ht)

    @pl.loop(0, width // 256)
    def _(j):
        cols = pl.ds(pl.multiple_of(j * 256, 256), 256)
        R.n2vt[cols, :] = R.n2[:, :VIS, cols].reshape(4 * VIS, 256).T
        R.n2tt[cols, :] = R.n2[:, VIS:, cols].reshape(4 * TXT, 256).T

    gather(vout, 3)
    weight_grad(TIN, R.n2tt, R.gut)
    pass_sum(tout, 0)
    pass_sum(tin, 0)

    def text_terms(target, rows, weight):
        target[:, VIS:, :] = mm_nt(rows, G[weight]).astype(BF).reshape(4, TXT, width)

    text_terms(R.pg, R.gut[...], TIN)
    text_terms(R.pf, R.ht[...], TOUT)
    gather(vin, 4)
    gather(vout, 4)

    def terms(target, rows, weight, m):
        part = mm_nt(rows[2 * m * VIS : 2 * (m + 1) * VIS, :], G[weight]).astype(BF)
        target[2 * m : 2 * m + 2, :VIS, :] = part.reshape(2, VIS, width)

    mate_g = remote(R.pg.at[pl.ds(theirs, 2)], R.rg, mate)
    pieces = [pl.ds(half_rows * (SEQ // 2), SEQ // 2) for half_rows in range(2)]
    cross_g = [remote(R.xsg.at[piece], R.xrg.at[piece], across) for piece in pieces]
    gy_across = [remote(R.gy.at[x, piece], R.gy.at[x, piece], across) for piece in pieces]
    gy_mate = remote(R.ga.at[pair_own], R.ga.at[pair_own], mate)
    gy_passed = remote(R.ga.at[pair_across], R.ga.at[pair_across], mate)
    started.extend(cross_g + gy_across + [gy_mate, gy_passed])

    def image_terms(m):
        terms(R.pg, R.guv, VIN, m)
        pl.when(c != m)(mate_g.start)

    def sum_cores(m):
        @pl.when(c == m)
        def _():
            mate_g.wait_recv()
            for piece, copy in zip(pieces, cross_g):
                R.xsg[piece, :] = (
                    R.pg[pair_across, piece, :].astype(F32) + R.rg[1 - x, piece, :].astype(F32)
                ).astype(BF)
                copy.start()

    def middle_back(m):
        @pl.when(c == m)
        def _():
            for half_rows in range(2):
                cross_g[half_rows].wait_recv()

                @pl.loop(0, SEQ // 128)
                def _(i):
                    j = i + half_rows * (SEQ // 128)
                    rows = pl.ds(pl.multiple_of(j * 64, 64), 64)
                    grad_normed = (
                        R.pg[pair_own, rows, :].astype(F32)
                        + R.rg[x, rows, :].astype(F32)
                        + R.xrg[rows, :].astype(F32)
                    )
                    normed, inverse = normalize(R.y1[rows, :])
                    grad = R.dy[rows, :].astype(F32) + normalize_back(grad_normed, normed, inverse)
                    R.gy[x, rows, :] = grad.astype(BF)
                    R.ga[pair_own, rows, :] = (grad * live_rows(x, j)).astype(BF)

                gy_across[half_rows].start()
            gy_mate.start()

    def middle_pass(m):
        @pl.when(c == m)
        def _():
            for half_rows in range(2):
                gy_across[half_rows].wait_recv()

                @pl.loop(0, SEQ // 128)
                def _(i):
                    j = i + half_rows * (SEQ // 128)
                    rows = pl.ds(pl.multiple_of(j * 64, 64), 64)
                    R.ga[pair_across, rows, :] = (
                        R.gy[1 - x, rows, :].astype(F32) * live_rows(1 - x, j)
                    ).astype(BF)

            gy_passed.start()

    def middle_came(m):
        @pl.when(c != m)
        def _():
            gy_mate.wait_recv()
            gy_passed.wait_recv()

    sent(send_x)
    cross_a.wait_send()

    @pl.loop(0, tiles)
    def _(j):
        expert((0, 2), 0, VIS, VIN, VOUT, R.hv, R.guv, j)

    image_terms(0)

    @pl.loop(0, tiles)
    def _(j):
        expert((2, 2), 0, VIS, VIN, VOUT, R.hv, R.guv, j)
        pl.when(j == 0)(functools.partial(sum_cores, 0))

    pass_sum(tout, 1)
    image_terms(1)
    for copy in (to_across, to_mate, passed):
        sent(copy)
    sum_cores(1)
    pass_sum(tin, 1)
    weight_grad(VOUT, R.gzvt, R.hv)
    middle_back(0)
    pass_sum(vout, 0)
    pass_sum(tout, 2)
    weight_grad(VIN, R.n2vt, R.guv)
    pass_sum(vin, 0)
    pass_sum(tin, 2)

    terms(R.pf, R.hv, VOUT, 0)
    middle_pass(0)
    middle_back(1)
    pass_sum(tout, 3)
    terms(R.pf, R.hv, VOUT, 1)
    mate_f = start(R.pf.at[pl.ds(theirs, 2)], R.rf, mate)
    cross_f = remote(R.xsf, R.xrf, across)
    started.append(cross_f)
    pass_sum(tin, 3)
    mate_g.wait_send()
    middle_came(0)

    back_mate = [remote(R.pb.at[theirs + t], R.rb.at[t], mate) for t in range(2)]
    back_cross = [remote(R.xsb.at[t], R.xrb.at[t], across) for t in range(2)]
    started.extend(back_mate + back_cross)

    def attention_back(m, t):
        i = 2 * m + t
        grad_context = mm(R.ga[i], R.wo[...]).astype(BF)
        q, k, v = R.q[i], R.k[i], R.v[i]
        turned_k = k.T
        grad_q = []
        grad_k = jnp.zeros((SEQ, span), F32)
        grad_v = jnp.zeros((SEQ, span), F32)
        for h in range(heads):
            probs = R.probs[i * heads + h]
            grad_probs = mm_nt(only(h, v), grad_context)
            exact = probs.astype(F32)
            inner = jnp.sum(grad_probs * exact, axis=0, keepdims=True)
            grad_scores = (exact * (grad_probs - inner)).astype(BF)
            grad_q.append(mm(head_rows(turned_k, h), grad_scores))
            grad_k += mm(grad_scores, only(h, q))
            grad_v += mm(probs, only(h, grad_context))
        grad_q = jnp.concatenate(grad_q, axis=0).T
        joined = jnp.concatenate([grad_q, grad_k, grad_v], axis=1).astype(BF)
        R.gqkv[i, :, : 3 * span] = joined
        R.pb[i] = mm_nt(joined, G[ATT][:, : 3 * span]).astype(BF)
        pl.when(c != m)(back_mate[t].start)

    def back_sum(m, t):
        @pl.when(c == m)
        def _():
            back_mate[t].wait_recv()
            R.xsb[t] = (R.pb[2 * m + t].astype(F32) + R.rb[t].astype(F32)).astype(BF)
            back_cross[t].start()

    attention_back(0, 0)
    pass_sum(vout, 1)
    mate_f.wait_recv()
    R.xsf[...] = (R.pf[pair_across].astype(F32) + R.rf[1 - x].astype(F32)).astype(BF)
    R.fown[...] = (R.pf[pair_own].astype(F32) + R.rf[x].astype(F32)).astype(BF)
    middle_pass(1)
    cross_f.start()
    attention_back(0, 1)
    back_sum(0, 0)

    pass_sum(vin, 1)
    middle_came(1)
    attention_back(1, 0)
    back_sum(0, 1)

    pass_sum(vout, 2)
    attention_back(1, 1)
    back_sum(1, 0)
    pass_sum(vin, 2)

    lanes = width // 2

    @pl.loop(0, width // 256)
    def _(j):
        rows = pl.ds(pl.multiple_of(j * 256, 256), 256)
        grad_v = mm(R.n1t[rows, :], R.gqkv[:, :, lanes : 3 * span].reshape(4 * SEQ, span))
        grad_o = mm(R.ct[...], R.ga[:, :, rows].reshape(4 * SEQ, 256)).T
        PART[ATT, rows, lanes:] = jnp.concatenate([grad_v, grad_o], axis=1).astype(BF)

    pass_sum(far, 0)

    cross_f.wait_recv()

    @pl.loop(0, SEQ // 64)
    def _(j):
        rows = pl.ds(pl.multiple_of(j * 64, 64), 64)
        branch = R.fown[rows, :].astype(F32) + R.xrf[rows, :].astype(F32)
        OUT[x, rows, :] = (R.y1[rows, :] + live_rows(x, j) * branch).astype(BF)

    out_across = start(OUT.at[x], OUT.at[x], across)

    @pl.loop(0, width // 256)
    def _(j):
        rows = pl.ds(pl.multiple_of(j * 256, 256), 256)
        grads = mm(R.n1t[rows, :], R.gqkv[:, :, :lanes].reshape(4 * SEQ, lanes))
        PART[ATT, rows, :lanes] = grads.astype(BF)

    pass_sum(near, 0)
    back_sum(1, 1)
    pass_sum(vout, 3)
    pass_sum(vin, 3)

    def input_back(m, t):
        @pl.when(c == m)
        def _():
            back_cross[t].wait_recv()

            @pl.loop(0, SEQ // 64)
            def _(j):
                rows = pl.ds(pl.multiple_of(j * 64, 64), 64)
                grad_normed = R.xsb[t, rows, :].astype(F32) + R.xrb[t, rows, :].astype(F32)
                normed, inverse = normalize(R.x[t, rows, :].astype(F32))
                grad = R.gy[t, rows, :].astype(F32) + normalize_back(grad_normed, normed, inverse)
                high = grad.astype(BF)
                rows = pl.ds(pl.multiple_of(t * SEQ + j * 64, 64), 64)
                R.hv[rows, :] = high
                R.guv[rows, :] = (grad - high.astype(F32)).astype(BF)

    pass_sum(far, 1)
    input_back(0, 0)
    pass_sum(near, 1)
    input_back(0, 1)
    end_sum(tout, tin)
    pass_sum(far, 2)
    pass_sum(near, 2)
    end_sum(vout, vin)

    leaving = []

    def leave(slot, source, target):
        leaving.append(fetch(slot, source, target))

    slots = lax.broadcasted_iota(jnp.int32, (row_count, 2 * SEQ), 1)
    rows = lax.broadcasted_iota(jnp.int32, (row_count, 2 * SEQ), 0)
    turn = slots // SEQ
    back = placed(turn, slots - turn * SEQ, rows, slots >= 0)
    out_across.wait_recv()
    R.out_tokens[...] = mm(back, OUT[...].reshape(2 * SEQ, width)).astype(BF)
    leave(6, R.out_tokens, R.out_tokens_hbm)
    for copy in finals:
        copy.wait_recv()
    finals.clear()
    leave(7, GW.at[pl.ds(1, 4)], R.gw_hbm.at[pl.ds(1, 4)])
    pass_sum(far, 3)
    pass_sum(near, 3)
    input_back(1, 0)
    input_back(1, 1)
    R.grad_tokens[...] = mm(back, R.hv[: 2 * SEQ, :]) + mm(back, R.guv[: 2 * SEQ, :])
    leave(8, R.grad_tokens, R.grad_tokens_hbm)
    end_sum(far, near)

    first_lane = lax.broadcasted_iota(jnp.int32, (own, 128), 1) == 0
    for place in range(2):
        attn = sum(total for k, total in row_sums[place] if k == ATT)
        experts = sum(total for k, total in row_sums[place] if k != ATT)
        R.gs[place] = jnp.where(first_lane, attn, experts)
    peers = [
        start(R.gs.at[place], R.gr.at[slot], device)
        for slot, (place, device) in enumerate(((1, mate), (0, across), (1, diagonal)))
    ]
    for copy in finals + peers:
        copy.wait_recv()
    leave(9, GW.at[pl.ds(0, 1)], R.gw_hbm.at[pl.ds(0, 1)])
    GG[...] = (R.gs[0] + R.gr[1]) + (R.gr[0] + R.gr[2])

    for copy in started:
        copy.wait_send()
    for copy in leaving:
        copy.wait()
    for k in range(5):
        for semaphore in (k, 5 + k):
            pltpu.make_async_remote_copy(
                src_ref=LAND.at[k],
                dst_ref=LAND.at[k],
                send_sem=R.ring_sent.at[semaphore],
                recv_sem=R.ring_came.at[0],
                device_id=ahead,
                device_id_type=MESH,
            ).wait_send()


def finish_kernel(n_results, out, gtok, gw_hbm, gg, gain_attn, gain_ffn, *rest):
    results, scratch = rest[:n_results], rest[n_results:]
    buffers, (out_buffer, gtok_buffer, gw, came, gone) = scratch[:n_results], scratch[n_results:]
    arriving = [
        pltpu.make_async_copy(source, target, came.at[slot])
        for slot, (source, target) in enumerate(((gw_hbm, gw), (out, out_buffer), (gtok, gtok_buffer)))
    ]
    for copy in arriving:
        copy.start()
    width = gw.shape[3]
    own = gw.shape[2]
    span = width // 4
    gain_one, gain_two = column(gain_attn), column(gain_ffn)
    square = unit(own).astype(F32)
    leaving = []

    def leave(slot, source):
        copy = pltpu.make_async_copy(source, results[slot], gone.at[slot])
        copy.start()
        leaving.append(copy)

    def both(part):
        cols = slice(part * span, (part + 1) * span)
        return jnp.concatenate([gw[ATT, core][:, cols] for core in range(2)], axis=1)

    def put(slot, value):
        buffers[slot][...] = value
        leave(slot, buffers[slot])

    put(2, jnp.sum(square * (gg[:, :1] / gain_one), axis=0, keepdims=True))
    put(7, jnp.sum(square * (gg[:, 1:2] / gain_two), axis=0, keepdims=True))
    arriving[0].wait()
    for slot, k, scale in ((8, VIN, gain_two), (9, VOUT, 1.0), (10, TIN, gain_two), (11, TOUT, 1.0)):
        put(slot, jnp.concatenate([gw[k, 0], gw[k, 1]], axis=1) * scale)
    put(3, both(0) * (gain_one * HEAD_DIM**-0.5))
    put(4, both(1) * gain_one)
    put(5, both(2) * gain_one)
    put(6, both(3))
    arriving[1].wait()
    leave(0, out_buffer)
    arriving[2].wait()
    leave(1, gtok_buffer)
    for copy in leaving:
        copy.wait()


def fused_layer(
    tokens,
    caption_lengths,
    gain_attn,
    w_query,
    w_key,
    w_value,
    w_out,
    gain_ffn,
    vis_in,
    vis_out,
    txt_in,
    txt_out,
    cotangent,
):
    n = lax.axis_size("dp") // 2
    own = w_query.shape[0]
    row_count, width = tokens.shape
    span = width // 4
    heads = span // HEAD_DIM
    gain_one, gain_two = gain_attn.reshape(1, own), gain_ffn.reshape(1, own)

    rows = 4 * SEQ
    scratch = dict(
        tokens=pltpu.VMEM((row_count, width), BF),
        cotangent=pltpu.VMEM((row_count, width), BF),
        txt_in=pltpu.VMEM((own, 2 * width), BF),
        txt_out=pltpu.VMEM((own, 2 * width), BF),
        vis_in=pltpu.VMEM((own, 2 * width), BF),
        vis_out=pltpu.VMEM((own, 2 * width), BF),
        out_tokens=pltpu.VMEM((row_count, width), BF),
        grad_tokens=pltpu.VMEM((row_count, width), F32),
        gw=pltpu.VMEM((5, 2, own, width), F32),
        local=pltpu.SemaphoreType.DMA((10,)),
        shard=pltpu.VMEM((5, 2, own, width), BF),
        lens=pltpu.VMEM((2, 8, 128), F32),
        x=pltpu.VMEM((2, SEQ, width), BF),
        dy=pltpu.VMEM((SEQ, width), BF),
        padded_out=pltpu.VMEM((2, SEQ, width), BF),
        gathered=pltpu.VMEM((5, width, width), BF),
        part=pltpu.VMEM((5, width, width), BF),
        land=pltpu.VMEM((5, n - 1, 2 * own, width), BF),
        give=pltpu.VMEM((5, own, width), F32),
        x4=pltpu.VMEM((4, SEQ, width), BF),
        lens4=pltpu.VMEM((4, 8, 128), F32),
        n1=pltpu.VMEM((4, SEQ, width), BF),
        n1t=pltpu.VMEM((width, rows), BF),
        gz=pltpu.VMEM((4, SEQ, width), BF),
        gzvt=pltpu.VMEM((width, 4 * VIS), BF),
        ct=pltpu.VMEM((span, rows), BF),
        fown=pltpu.VMEM((SEQ, width), BF),
        gztt=pltpu.VMEM((width, 4 * TXT), BF),
        wo=pltpu.VMEM((width, span), BF),
        q=pltpu.VMEM((4, SEQ, span), BF),
        k=pltpu.VMEM((4, SEQ, span), BF),
        v=pltpu.VMEM((4, SEQ, span), BF),
        probs=pltpu.VMEM((4 * heads, SEQ, SEQ), BF),
        pa=pltpu.VMEM((4, SEQ, width), BF),
        ra=pltpu.VMEM((2, SEQ, width), BF),
        xs=pltpu.VMEM((SEQ, width), BF),
        xr=pltpu.VMEM((SEQ, width), BF),
        y1=pltpu.VMEM((SEQ, width), F32),
        n2vt=pltpu.VMEM((width, 4 * VIS), BF),
        n2tt=pltpu.VMEM((width, 4 * TXT), BF),
        u=pltpu.VMEM((4 * VIS, 256), F32),
        gh=pltpu.VMEM((4 * VIS, 256), F32),
        hv=pltpu.VMEM((4 * VIS, width), BF),
        guv=pltpu.VMEM((4 * VIS, width), BF),
        ht=pltpu.VMEM((4 * TXT, width), BF),
        gut=pltpu.VMEM((4 * TXT, width), BF),
        pg=pltpu.VMEM((4, SEQ, width), BF),
        rg=pltpu.VMEM((2, SEQ, width), BF),
        gy=pltpu.VMEM((2, SEQ, width), BF),
        xsf=pltpu.VMEM((SEQ, width), BF),
        xrf=pltpu.VMEM((SEQ, width), BF),
        xsb=pltpu.VMEM((2, SEQ, width), BF),
        xrb=pltpu.VMEM((2, SEQ, width), BF),
        gs=pltpu.VMEM((2, own, 128), F32),
        gr=pltpu.VMEM((3, own, 128), F32),
        sent=pltpu.SemaphoreType.DMA((40,)),
        came=pltpu.SemaphoreType.DMA((40,)),
        ring_sent=pltpu.SemaphoreType.DMA((10,)),
        ring_came=pltpu.SemaphoreType.DMA((6 * 2 * (n // 2) * 2,)),
    )
    inputs = dict(
        lengths=caption_lengths,
        tokens_hbm=tokens,
        cotangent_hbm=cotangent,
        gain_attn=gain_one,
        gain_ffn=gain_two,
        w_query=w_query,
        w_key=w_key,
        w_value=w_value,
        w_out=w_out.T,
        vis_in_hbm=vis_in,
        vis_out_hbm=vis_out.T,
        txt_in_hbm=txt_in,
        txt_out_hbm=txt_out.T,
    )
    results = dict(
        out_tokens_hbm=jax.ShapeDtypeStruct((row_count, width), BF),
        grad_tokens_hbm=jax.ShapeDtypeStruct((row_count, width), F32),
        gw_hbm=jax.ShapeDtypeStruct((5, 2, own, width), F32),
        gg=jax.ShapeDtypeStruct((own, 128), F32),
    )
    vmem, hbm = pl.BlockSpec(memory_space=pltpu.VMEM), pl.BlockSpec(memory_space=pl.ANY)
    names = tuple(inputs) + tuple(results) + tuple(scratch)
    out, gtok, gw, gg = pl.pallas_call(
        functools.partial(layer_kernel, n, names),
        out_shape=tuple(results.values()),
        in_specs=[pl.BlockSpec(memory_space=pltpu.SMEM)] + [hbm if k.endswith(HBM) else vmem for k in names[1 : len(inputs)]],
        out_specs=[hbm if k.endswith(HBM) else vmem for k in results],
        scratch_shapes=list(scratch.values()),
        compiler_params=pltpu.CompilerParams(
            collective_id=0, has_side_effects=True, vmem_limit_bytes=60 * 2**20
        ),
    )(*inputs.values())

    shapes = (
        jax.ShapeDtypeStruct((row_count, width), BF),
        jax.ShapeDtypeStruct((row_count, width), F32),
        jax.ShapeDtypeStruct((1, own), F32),
        jax.ShapeDtypeStruct((own, 2 * span), F32),
        jax.ShapeDtypeStruct((own, 2 * span), F32),
        jax.ShapeDtypeStruct((own, 2 * span), F32),
        jax.ShapeDtypeStruct((own, 2 * span), F32),
        jax.ShapeDtypeStruct((1, own), F32),
        jax.ShapeDtypeStruct((own, 2 * width), F32),
        jax.ShapeDtypeStruct((own, 2 * width), F32),
        jax.ShapeDtypeStruct((own, 2 * width), F32),
        jax.ShapeDtypeStruct((own, 2 * width), F32),
    )
    buffers = [pltpu.VMEM(one.shape if slot > 1 else (8, 128), F32) for slot, one in enumerate(shapes)]
    final = pl.pallas_call(
        functools.partial(finish_kernel, len(shapes)),
        out_shape=shapes,
        in_specs=[hbm] * 3 + [vmem] * 3,
        out_specs=[hbm] * len(shapes),
        scratch_shapes=buffers
        + [
            pltpu.VMEM((row_count, width), BF),
            pltpu.VMEM((row_count, width), F32),
            pltpu.VMEM((5, 2, own, width), F32),
            pltpu.SemaphoreType.DMA((3,)),
            pltpu.SemaphoreType.DMA((len(shapes),)),
        ],
        compiler_params=pltpu.CompilerParams(vmem_limit_bytes=60 * 2**20),
    )(out, gtok, gw, gg, gain_one, gain_two)
    final = list(final)
    final[2] = final[2].reshape(own)
    final[7] = final[7].reshape(own)
    for turned in (6, 9, 11):
        final[turned] = final[turned].T
    return tuple(final)


def norm_parts(values):
    center = values - jnp.mean(values, axis=-1, keepdims=True)
    spread = jnp.mean(center * center, axis=-1, keepdims=True)
    inverse = lax.rsqrt(spread + epsilon)
    return (center * inverse, inverse)


def norm_back(grad_out, normed, inverse, gain):
    grad_normed = grad_out * gain
    grad_gain = jnp.sum(grad_out * normed, axis=0)
    inner = (
        grad_normed
        - jnp.mean(grad_normed, axis=-1, keepdims=True)
        - normed * jnp.mean(grad_normed * normed, axis=-1, keepdims=True)
    )
    return (inverse * inner, grad_gain)


def matmul(left, right):
    return jnp.dot(left, right, preferred_element_type=jnp.float32)


def matmul_tn(left, right):
    return lax.dot_general(
        left, right, (((0,), (0,)), ((), ())), preferred_element_type=jnp.float32
    )


def matmul_nt(left, right):
    return lax.dot_general(
        left, right, (((1,), (1,)), ((), ())), preferred_element_type=jnp.float32
    )


def gelu_slope(pre):
    cumulative = 0.5 * (1.0 + lax.erf(pre * inv_root_two))
    density = jnp.exp(-0.5 * pre * pre) * inv_root_tau
    return cumulative + pre * density


def expert_forward(rows, weight_in, weight_out):
    pre = matmul(rows, weight_in)
    hidden = jax.nn.gelu(pre, approximate=False).astype(jnp.bfloat16)
    return (pre, hidden, matmul(hidden, weight_out))


def expert_backward(rows, pre, hidden, grad_out, weight_in, weight_out):
    grad_weight_out = matmul_tn(hidden, grad_out)
    grad_hidden = matmul_nt(grad_out, weight_out)
    grad_pre = (grad_hidden * gelu_slope(pre)).astype(jnp.bfloat16)
    return (matmul_tn(rows, grad_pre), grad_weight_out, matmul_nt(grad_pre, weight_in))


def join_experts(image_rows, text_rows, pair_count, width):
    joined = jnp.concatenate(
        [
            image_rows.reshape(pair_count, PATCHES, width),
            text_rows.reshape(pair_count, CAPTION, width),
        ],
        axis=1,
    )
    return joined.reshape(-1, width)


def plain_layer(
    tokens,
    caption_lengths,
    gain_attn,
    w_query,
    w_key,
    w_value,
    w_out,
    gain_ffn,
    vis_in,
    vis_out,
    txt_in,
    txt_out,
    cotangent,
):
    seq_len = PATCHES + CAPTION
    width = tokens.shape[1]
    pair_count = tokens.shape[0] // seq_len
    half_pairs = pair_count // lax.axis_size("tensor")
    half_rows = half_pairs * seq_len
    row_start = lax.axis_index("tensor") * half_rows
    gain_one, query_w, key_w, value_w, out_w = (
        lax.all_gather(gain_attn, "dp", axis=0, tiled=True),
        lax.all_gather(w_query, "dp", axis=0, tiled=True),
        lax.all_gather(w_key, "dp", axis=0, tiled=True),
        lax.all_gather(w_value, "dp", axis=0, tiled=True),
        lax.all_gather(w_out, "dp", axis=1, tiled=True),
    )
    gain_two, vis_in_w, vis_out_w, txt_in_w, txt_out_w = (
        lax.all_gather(gain_ffn, "dp", axis=0, tiled=True),
        lax.all_gather(vis_in, "dp", axis=0, tiled=True),
        lax.all_gather(vis_out, "dp", axis=1, tiled=True),
        lax.all_gather(txt_in, "dp", axis=0, tiled=True),
        lax.all_gather(txt_out, "dp", axis=1, tiled=True),
    )
    gain_one = gain_one.astype(jnp.float32)
    gain_two = gain_two.astype(jnp.float32)
    head_local = query_w.shape[1] // HEAD_DIM
    score_scale = HEAD_DIM ** (-0.5)
    position = jnp.arange(seq_len, dtype=jnp.int32)
    live = (position[None, :] < PATCHES) | (position[None, :] - PATCHES < caption_lengths[:, None])
    valid_rows = live.astype(jnp.float32)
    mask_col = valid_rows.reshape(-1, 1)
    key_live = valid_rows[:, None, None, :] > 0.5

    def own_rows(values):
        return lax.dynamic_slice_in_dim(values, row_start, half_rows, 0)

    inputs = tokens.astype(jnp.float32)
    normed_one, inverse_one = norm_parts(inputs)
    first_in = (normed_one * gain_one).astype(jnp.bfloat16)

    def project(weight):
        return (
            matmul(first_in, weight)
            .astype(jnp.bfloat16)
            .reshape(pair_count, seq_len, head_local, HEAD_DIM)
        )

    queries = project(query_w)
    keys_all = project(key_w)
    values_all = project(value_w)

    def score_block():
        raw = (
            jnp.einsum("pqhe,pkhe->phqk", queries, keys_all, preferred_element_type=jnp.float32)
            * score_scale
        )
        return jnp.where(key_live, raw, -1e30)

    scores = score_block()
    top = jnp.max(scores, axis=-1, keepdims=True)
    weights = jnp.exp(scores - top)
    total = jnp.sum(weights, axis=-1, keepdims=True)
    probs = (weights / total).astype(jnp.bfloat16)
    log_total = top + jnp.log(total)
    context = jnp.einsum("phqk,pkhe->pqhe", probs, values_all, preferred_element_type=jnp.float32)
    context = context.astype(jnp.bfloat16).reshape(-1, head_local * HEAD_DIM)
    attn_terms = matmul(context, out_w)
    attended_own = lax.psum_scatter(
        attn_terms.astype(jnp.bfloat16), "tensor", scatter_dimension=0, tiled=True
    ).astype(jnp.float32)
    mask_own = own_rows(mask_col)
    middle_own = own_rows(inputs) + mask_own * attended_own
    normed_two, inverse_two = norm_parts(middle_own)
    second_own = (normed_two * gain_two).astype(jnp.bfloat16)
    grid = lax.all_gather(second_own, "tensor", axis=0, tiled=True).reshape(
        pair_count, seq_len, width
    )
    image_rows = grid[:, :PATCHES].reshape(-1, width)
    text_rows = grid[:, PATCHES:].reshape(-1, width)
    image_pre, image_hidden, image_part = expert_forward(image_rows, vis_in_w, vis_out_w)
    text_pre, text_hidden, text_part = expert_forward(text_rows, txt_in_w, txt_out_w)
    image_own, text_own = (
        lax.psum_scatter(
            image_part.astype(jnp.bfloat16), "tensor", scatter_dimension=0, tiled=True
        ).astype(jnp.float32),
        lax.psum_scatter(
            text_part.astype(jnp.bfloat16), "tensor", scatter_dimension=0, tiled=True
        ).astype(jnp.float32),
    )
    branch_own = join_experts(image_own, text_own, half_pairs, width)
    output_own = (middle_own + mask_own * branch_own).astype(jnp.bfloat16)
    upstream = cotangent.astype(jnp.float32)
    grad_branch = (upstream * mask_col).astype(jnp.bfloat16).reshape(pair_count, seq_len, width)
    image_grads = expert_backward(
        image_rows,
        image_pre,
        image_hidden,
        grad_branch[:, :PATCHES].reshape(-1, width),
        vis_in_w,
        vis_out_w,
    )
    text_grads = expert_backward(
        text_rows,
        text_pre,
        text_hidden,
        grad_branch[:, PATCHES:].reshape(-1, width),
        txt_in_w,
        txt_out_w,
    )
    back_image_own, back_text_own = (
        lax.psum_scatter(
            image_grads[2].astype(jnp.bfloat16), "tensor", scatter_dimension=0, tiled=True
        ).astype(jnp.float32),
        lax.psum_scatter(
            text_grads[2].astype(jnp.bfloat16), "tensor", scatter_dimension=0, tiled=True
        ).astype(jnp.float32),
    )
    grad_second_own = join_experts(back_image_own, back_text_own, half_pairs, width)
    grad_norm_own, gain_part = norm_back(grad_second_own, normed_two, inverse_two, gain_two)
    grad_middle_own = own_rows(upstream) + grad_norm_own
    output_wide, grad_middle, gain_parts = (
        lax.all_gather(
            output_own.astype(jnp.float32).astype(jnp.bfloat16), "tensor", axis=0, tiled=True
        ).astype(jnp.float32),
        lax.all_gather(grad_middle_own.astype(jnp.bfloat16), "tensor", axis=0, tiled=True).astype(
            grad_middle_own.dtype
        ),
        lax.all_gather(gain_part.astype(jnp.bfloat16), "tensor", axis=0, tiled=True).astype(
            gain_part.dtype
        ),
    )
    output = output_wide.astype(jnp.bfloat16)
    grad_gain_two = jnp.sum(gain_parts.reshape(-1, width), axis=0)
    grad_attended = (grad_middle * mask_col).astype(jnp.bfloat16)
    grad_out_w = matmul_tn(context, grad_attended)
    grad_context = (
        matmul_nt(grad_attended, out_w)
        .astype(jnp.bfloat16)
        .reshape(pair_count, seq_len, head_local, HEAD_DIM)
    )
    scores_again = score_block()
    probs_exact = jnp.exp(scores_again - log_total)
    grad_probs = jnp.einsum(
        "pqhe,pkhe->phqk", grad_context, values_all, preferred_element_type=jnp.float32
    )
    inner = jnp.sum(grad_probs * probs_exact, axis=-1, keepdims=True)
    grad_scores = (probs_exact * (grad_probs - inner)).astype(jnp.bfloat16)
    grad_values = jnp.einsum(
        "phqk,pqhe->pkhe", probs, grad_context, preferred_element_type=jnp.float32
    )
    grad_values = grad_values.astype(jnp.bfloat16).reshape(-1, head_local * HEAD_DIM)
    grad_queries = (
        jnp.einsum("phqk,pkhe->pqhe", grad_scores, keys_all, preferred_element_type=jnp.float32)
        * score_scale
    )
    grad_queries = grad_queries.astype(jnp.bfloat16).reshape(-1, head_local * HEAD_DIM)
    grad_keys = (
        jnp.einsum("phqk,pqhe->pkhe", grad_scores, queries, preferred_element_type=jnp.float32)
        * score_scale
    )
    grad_keys = grad_keys.astype(jnp.bfloat16).reshape(-1, head_local * HEAD_DIM)
    grad_query_w = matmul_tn(first_in, grad_queries)
    grad_key_w = matmul_tn(first_in, grad_keys)
    grad_value_w = matmul_tn(first_in, grad_values)
    first_part = (
        matmul_nt(grad_queries, query_w)
        + matmul_nt(grad_keys, key_w)
        + matmul_nt(grad_values, value_w)
    )
    grad_first = lax.psum(first_part.astype(jnp.bfloat16), "tensor").astype(jnp.float32)
    grad_norm_one, grad_gain_one = norm_back(grad_first, normed_one, inverse_one, gain_one)
    grad_inputs = grad_middle + grad_norm_one
    attn_sent = (
        lax.psum_scatter(grad_gain_one, "dp", scatter_dimension=0, tiled=True),
        lax.psum_scatter(grad_query_w, "dp", scatter_dimension=0, tiled=True),
        lax.psum_scatter(grad_key_w, "dp", scatter_dimension=0, tiled=True),
        lax.psum_scatter(grad_value_w, "dp", scatter_dimension=0, tiled=True),
        lax.psum_scatter(grad_out_w, "dp", scatter_dimension=1, tiled=True),
    )
    final_expert = (
        lax.psum_scatter(grad_gain_two, "dp", scatter_dimension=0, tiled=True),
        lax.psum_scatter(image_grads[0], "dp", scatter_dimension=0, tiled=True),
        lax.psum_scatter(image_grads[1], "dp", scatter_dimension=1, tiled=True),
        lax.psum_scatter(text_grads[0], "dp", scatter_dimension=0, tiled=True),
        lax.psum_scatter(text_grads[1], "dp", scatter_dimension=1, tiled=True),
    )
    return (
        output,
        grad_inputs,
        attn_sent[0],
        attn_sent[1],
        attn_sent[2],
        attn_sent[3],
        attn_sent[4],
        final_expert[0],
        final_expert[1],
        final_expert[2],
        final_expert[3],
        final_expert[4],
    )


def solution(mesh):
    def local(tokens, lengths, gain, w_query, *rest):
        ring = mesh.shape["dp"] // 2
        fits = (
            mesh.shape["tensor"] == 2
            and ring == 8
            and lengths.shape[0] == 2
            and w_query.shape[0] % 16 == 0
        )
        layer = fused_layer if fits else plain_layer
        return layer(tokens, lengths, gain, w_query, *rest)

    return jax.shard_map(
        local,
        mesh=mesh,
        in_specs=(
            P("dp", None),
            P("dp"),
            P("dp"),
            P("dp", "tensor"),
            P("dp", "tensor"),
            P("dp", "tensor"),
            P("tensor", "dp"),
            P("dp"),
            P("dp", "tensor"),
            P("tensor", "dp"),
            P("dp", "tensor"),
            P("tensor", "dp"),
            P("dp", None),
        ),
        out_specs=(
            P("dp", None),
            P("dp", None),
            P("dp"),
            P("dp", "tensor"),
            P("dp", "tensor"),
            P("dp", "tensor"),
            P("tensor", "dp"),
            P("dp"),
            P("dp", "tensor"),
            P("tensor", "dp"),
            P("dp", "tensor"),
            P("tensor", "dp"),
        ),
        check_vma=False,
    )
```

```python
import functools
import math
import types

import jax
import jax.numpy as jnp
from jax import lax
from jax.experimental import pallas as pl
from jax.experimental.pallas import tpu as pltpu
from jax.sharding import PartitionSpec as P

HEAD_DIM = 64
PATCHES = 197
CAPTION = 40
VIS = 208
TXT = 48
SEQ = VIS + TXT

MESH = pl.DeviceIdType.MESH
HBM = "_hbm"
BF = jnp.bfloat16
F32 = jnp.float32

ATT, TIN, TOUT, VIN, VOUT = range(5)

epsilon = 1e-05
inv_root_two = 1.0 / math.sqrt(2.0)
inv_root_tau = 1.0 / math.sqrt(2.0 * math.pi)


def mm(left, right):
    return jnp.dot(left, right, preferred_element_type=F32)


def mm_nt(left, right):
    return lax.dot_general(left, right, (((1,), (1,)), ((), ())), preferred_element_type=F32)


def mm_tn(left, right):
    return lax.dot_general(left, right, (((0,), (0,)), ((), ())), preferred_element_type=F32)


def normalize(values):
    center = values - jnp.mean(values, axis=-1, keepdims=True)
    spread = jnp.mean(center * center, axis=-1, keepdims=True)
    inverse = lax.rsqrt(spread + epsilon)
    return center * inverse, inverse


def normalize_back(grad_normed, normed, inverse):
    return inverse * (
        grad_normed
        - jnp.mean(grad_normed, axis=-1, keepdims=True)
        - normed * jnp.mean(grad_normed * normed, axis=-1, keepdims=True)
    )


def unit(size):
    rows = lax.broadcasted_iota(jnp.int32, (size, size), 0)
    return (rows == lax.broadcasted_iota(jnp.int32, (size, size), 1)).astype(F32).astype(BF)


def column(ref):
    size = ref.shape[1]
    return jnp.sum(unit(size).astype(F32) * ref[...].astype(F32), axis=1, keepdims=True)


def layer_kernel(n, names, *refs):
    R = types.SimpleNamespace(**dict(zip(names, refs)))
    R.pb, R.pf, R.ga, R.rf, R.rb, R.n2 = R.pg, R.pa, R.x4, R.ra, R.rg, R.n1
    R.gqkv, R.xsg, R.xrg = R.n2, R.xs, R.xr
    S, G, PART, LAND = R.shard, R.gathered, R.part, R.land
    OUT, GW, GG = R.padded_out, R.gw, R.gg
    width = G.shape[2]
    own = width // (2 * n)
    span = width // 4
    heads = span // HEAD_DIM

    x = lax.axis_index("tensor")
    d = lax.axis_index("dp")
    c = lax.rem(d, 2)
    other = 1 - c
    chip = d // 2
    y, z = lax.rem(chip, 2), chip // 2
    r = z + y * (n - 1 - 2 * z)
    half = n // 2

    def chip_at(pos):
        pos = lax.rem(pos + 2 * n, n)
        upper = pos // half
        return 2 * (pos + upper * (n - 1 - 2 * pos)) + upper

    near_mate = d + 1 - 2 * c
    mate, across, diagonal = (near_mate, x), (d, 1 - x), (near_mate, 1 - x)
    ahead = (2 * chip_at(r + 1) + c, x)
    behind = (2 * chip_at(r - 1) + c, x)
    way = (ahead, behind)

    offsets = {hop: 2 * own * chip_at(r + hop) for hop in range(-half, half + 1)}


    my_rows = pl.ds(pl.multiple_of(own * d, 16), own)

    def fetch(slot, source, target):
        copy = pltpu.make_async_copy(source, target, R.local.at[slot])
        copy.start()
        return copy

    fetched = [
        fetch(0, R.tokens_hbm, R.tokens),
        fetch(1, R.txt_in_hbm, R.txt_in),
        fetch(2, R.txt_out_hbm, R.txt_out),
        fetch(3, R.vis_in_hbm, R.vis_in),
        fetch(4, R.vis_out_hbm, R.vis_out),
        fetch(5, R.cotangent_hbm, R.cotangent),
    ]

    barrier = pltpu.get_barrier_semaphore()
    for device in (mate, across, diagonal, ahead, behind):
        pl.semaphore_signal(barrier, inc=1, device_id=device, device_id_type=MESH)

    mine, theirs = pl.multiple_of(2 * c, 2), pl.multiple_of(2 * other, 2)
    pair_own = 2 * c + x
    pair_across = 2 * c + 1 - x

    started = []
    counter = [0]

    def remote(source, target, device):
        index = counter[0]
        counter[0] += 1
        return pltpu.make_async_remote_copy(
            src_ref=source,
            dst_ref=target,
            send_sem=R.sent.at[index],
            recv_sem=R.came.at[index],
            device_id=device,
            device_id_type=MESH,
        )

    def start(source, target, device):
        copy = remote(source, target, device)
        copy.start()
        started.append(copy)
        return copy

    def sent(copy):
        copy.wait_send()
        started[:] = [one for one in started if one is not copy]

    def rows_at(hop):
        return pl.ds(pl.multiple_of(offsets[hop], 16), 2 * own)

    near, far = (ATT, 0, width // 2), (ATT, width // 2, width // 2)
    parts = [near, far] + [(k, 0, width) for k in (TIN, TOUT, VIN, VOUT)]
    tin, tout, vin, vout = parts[2:]
    longest = half

    def hops(part, side):
        return half if (parts.index(part) + side) % 2 == 0 else n - 1 - half

    def ring_index(part, side, s):
        return (parts.index(part) * 2 + side) * longest + s

    def view(ref, part, rows):
        k, first, count = part
        return ref.at[k, rows, pl.ds(first, count)]

    sum_base = len(parts) * 2 * longest

    def gather_copy(part, side, s, pos):
        block = view(G, part, rows_at(pos))
        i = ring_index(part, side, s)
        return pltpu.make_async_remote_copy(
            src_ref=block,
            dst_ref=block,
            send_sem=R.ring_sent.at[part[0]],
            recv_sem=R.ring_came.at[i],
            device_id=way[side],
            device_id_type=MESH,
        )

    def gather(part, s):
        for side in range(2):
            pos = -s if side == 0 else s
            if 0 < s <= hops(part, side):
                gather_copy(part, side, s - 1, pos).wait_recv()
            if s < hops(part, side):
                gather_copy(part, side, s, pos).start()

    def landed(part, side, s):
        k, first, count = part
        return LAND.at[k, side * hops(part, 0) + s, :, pl.ds(first, count)]

    def sum_copy(part, side, s, source):
        i = sum_base + ring_index(part, side, s)
        return pltpu.make_async_remote_copy(
            src_ref=source,
            dst_ref=landed(part, side, s),
            send_sem=R.ring_sent.at[5 + part[0]],
            recv_sem=R.ring_came.at[i],
            device_id=way[side],
            device_id_type=MESH,
        )

    def pass_sum(part, s):
        for side in range(2):
            reach = hops(part, side)
            if s >= reach:
                continue
            pos = reach - s if side == 0 else s - reach
            term = view(PART, part, rows_at(pos))
            if s == 0:
                source = term
            else:
                source = landed(part, side, s - 1)
                sum_copy(part, side, s - 1, source).wait_recv()
                source[...] = (source[...].astype(F32) + term[...].astype(F32)).astype(BF)
            sum_copy(part, side, s, source).start()

    finals = []
    row_sums = [[], []]

    def end_sum(*group):
        for part in group:
            k, first, count = part
            ends = []
            for side in range(2):
                end = landed(part, side, hops(part, side) - 1)
                sum_copy(part, side, hops(part, side) - 1, end).wait_recv()
                ends.append(end)
            cols = slice(first, first + count)
            counted = min(3 * span - first, count) if k == ATT else count

            def total(core):
                rows = pl.ds(pl.multiple_of(own * core, 16), own)
                chip_rows = pl.ds(pl.multiple_of(2 * own * chip + own * core, 16), own)
                block = (
                    ends[0][rows, :].astype(F32)
                    + ends[1][rows, :].astype(F32)
                    + PART[k, chip_rows, cols].astype(F32)
                )
                if k in (ATT, TIN, VIN):
                    weighted = G[k, chip_rows, cols].astype(F32)[:, :counted] * block[:, :counted]
                    total = jnp.sum(weighted, axis=-1, keepdims=True)
                    row_sums[0 if core is c else 1].append((k, total))
                return block

            R.give[k, :, cols] = total(other)
            finals.append(
                start(R.give.at[k, :, pl.ds(first, count)], GW.at[k, c, :, pl.ds(first, count)], mate)
            )
            GW[k, c, :, cols] = total(c)

    def shard_part(k, value):
        for core in range(2):
            S[k, core] = value(core).astype(BF)

    gain_one, gain_two = column(R.gain_attn), column(R.gain_ffn)

    def attention_part(core):
        cols = slice(core * span, (core + 1) * span)
        return jnp.concatenate(
            [
                R.w_query[:, cols].astype(F32) * (gain_one * HEAD_DIM**-0.5),
                R.w_key[:, cols].astype(F32) * gain_one,
                R.w_value[:, cols].astype(F32) * gain_one,
                R.w_out[:, cols].astype(F32),
            ],
            axis=1,
        )

    def half_of(ref, core):
        return ref[:, core * width : (core + 1) * width].astype(F32) * gain_two

    def turned_half(ref, core):
        return ref[:, core * width : (core + 1) * width]

    lengths = R.lengths

    def live(t, slots):
        return (slots < PATCHES) | ((slots >= VIS) & (slots < VIS + lengths[t]))

    def live_rows(t, j, count=64):
        slots = lax.broadcasted_iota(jnp.int32, (count, 1), 0) + j * count
        return live(t, slots).astype(F32)

    row_count = R.tokens.shape[0]

    def placed(t, slots, rows, kept):
        source = t * (PATCHES + CAPTION) + slots - (slots >= VIS).astype(jnp.int32) * (VIS - PATCHES)
        return ((rows == source) & kept).astype(F32).astype(BF)

    def chooser(t, only_live):
        slots = lax.broadcasted_iota(jnp.int32, (SEQ, row_count), 0)
        rows = lax.broadcasted_iota(jnp.int32, (SEQ, row_count), 1)
        filled = (slots < PATCHES) | ((slots >= VIS) & (slots < VIS + CAPTION))
        return placed(t, slots, rows, live(t, slots) if only_live else filled)

    shard_part(ATT, attention_part)
    G[ATT, my_rows, :] = S[ATT, c]
    for t in range(2):
        R.lens[t] = jnp.full((8, 128), lengths[t], jnp.int32).astype(F32)
    pl.semaphore_wait(barrier, 5)
    shard_a = start(S.at[pl.ds(0, 1), other], G.at[pl.ds(0, 1), my_rows, :], mate)
    send_lens = start(R.lens, R.lens4.at[pl.ds(mine, 2)], mate)
    fetched[0].wait()
    for t in range(2):
        R.x4[2 * c + t] = mm(chooser(t, False), R.tokens[...]).astype(BF)
        R.lens4[2 * c + t] = R.lens[t]
    send_x = start(R.x4.at[pl.ds(mine, 2)], R.x4.at[pl.ds(mine, 2)], mate)
    shard_a.wait_recv()
    gather(near, 0)
    gather(far, 0)
    for copy in fetched[1:]:
        copy.wait()

    shard_part(TIN, functools.partial(half_of, R.txt_in))
    shard_part(TOUT, functools.partial(turned_half, R.txt_out))
    shard_part(VIN, functools.partial(half_of, R.vis_in))
    shard_part(VOUT, functools.partial(turned_half, R.vis_out))
    shard_b = start(S.at[pl.ds(1, 4), other], G.at[pl.ds(1, 4), my_rows, :], mate)
    for k in (TIN, TOUT, VIN, VOUT):
        G[k, my_rows, :] = S[k, c]
    gather(near, 1)
    for t in range(2):
        R.gz[2 * c + t] = mm(chooser(t, True), R.cotangent[...]).astype(BF)
        if t == 0:
            gather(far, 1)
    send_gz = start(R.gz.at[pl.ds(mine, 2)], R.gz.at[pl.ds(mine, 2)], mate)
    R.dy[...] = mm(chooser(x, False), R.cotangent[...]).astype(BF)
    for t in range(2):
        R.x[t] = R.x4[2 * c + t]
    shard_b.wait_recv()
    gather(tin, 0)
    gather(near, 2)
    send_x.wait_recv()

    for i in range(4):

        @pl.loop(0, SEQ // 64)
        def _(j, i=i):
            rows = pl.ds(pl.multiple_of(j * 64, 64), 64)
            normed, _ = normalize(R.x4[i, rows, :].astype(F32))
            R.n1[i, rows, :] = normed.astype(BF)

        R.n1t[:, i * SEQ : (i + 1) * SEQ] = R.n1[i].T
        if i == 0:
            gather(far, 2)
        if i == 1:
            gather(tout, 0)
            gather(near, 3)
        if i == 2:
            gather(far, 3)
            gather(vin, 0)
            gather(vout, 0)
    send_gz.wait_recv()
    send_lens.wait_recv()
    gather(near, 4)
    gather(far, 4)

    R.wo[...] = G[ATT][:, 3 * span :]

    @pl.loop(0, 4)
    def _(i):
        projected = mm(R.n1[i], G[ATT][:, : 3 * span]).astype(BF)
        R.q[i] = projected[:, :span]
        R.k[i] = projected[:, span : 2 * span]
        R.v[i] = projected[:, 2 * span :]

    lane = lax.broadcasted_iota(jnp.int32, (1, span), 1) // HEAD_DIM

    def only(head, values):
        return values * (lane == head).astype(F32).astype(BF)

    def head_rows(values, head):
        return values[head * HEAD_DIM : (head + 1) * HEAD_DIM, :]

    order = []
    for j in range(4):
        core = other if j < 2 else c
        turn = 1 - x if j % 2 == 0 else x
        order.append((turn, 2 * core + turn))
    attn_mate = [remote(R.pa.at[i], R.ra.at[turn], mate) for turn, i in order[:2]]
    cross_a = remote(R.xs, R.xr, across)

    for j, (turn, i) in enumerate(order):
        q, k, v = R.q[i], R.k[i], R.v[i]
        turned_v = v.T
        slots = lax.broadcasted_iota(jnp.int32, (SEQ, 1), 0)
        caption = (slots - VIS).astype(F32) < R.lens4[i][:1, :1]
        bias = jnp.where((slots < PATCHES) | ((slots >= VIS) & caption), 0.0, -1e30)
        contexts = []
        for h in range(heads):
            scores = mm_nt(only(h, k), q) + bias
            top = jnp.max(scores, axis=0, keepdims=True)
            weights = jnp.exp(scores - top)
            total = jnp.sum(weights, axis=0, keepdims=True)
            probs = (weights * (1.0 / total)).astype(BF)
            R.probs[i * heads + h] = probs
            contexts.append(mm(head_rows(turned_v, h), probs))
        contexts = jnp.concatenate(contexts, axis=0)
        R.ct[:, pl.ds(pl.multiple_of(i * SEQ, SEQ), SEQ)] = contexts.astype(BF)
        context = contexts.T.astype(BF)
        R.pa[i] = mm_nt(context, R.wo[...]).astype(BF)
        if j < 2:
            attn_mate[j].start()
        if j == 2:
            attn_mate[0].wait_recv()
            R.xs[...] = (R.pa[pair_across].astype(F32) + R.ra[1 - x].astype(F32)).astype(BF)
            cross_a.start()
        if j == 0:
            gather(tin, 1)
        if j == 1:
            gather(tout, 1)
        if j == 3:
            gather(tin, 2)
            gather(tout, 2)

    for copy in attn_mate:
        copy.wait_send()
    attn_mate[1].wait_recv()

    @pl.loop(0, width // 256)
    def _(j):
        cols = pl.ds(pl.multiple_of(j * 256, 256), 256)
        R.gzvt[cols, :] = R.gz[:, :VIS, cols].reshape(4 * VIS, 256).T
        R.gztt[cols, :] = R.gz[:, VIS:, cols].reshape(4 * TXT, 256).T

    gather(vin, 1)
    cross_a.wait_recv()

    @pl.loop(0, SEQ // 64)
    def _(j):
        rows = pl.ds(pl.multiple_of(j * 64, 64), 64)
        attended = (
            R.pa[pair_own, rows, :].astype(F32)
            + R.ra[x, rows, :].astype(F32)
            + R.xr[rows, :].astype(F32)
        )
        middle = R.x[x, rows, :].astype(F32) + live_rows(x, j) * attended
        R.y1[rows, :] = middle
        normed, _ = normalize(middle)
        R.n2[pair_own, rows, :] = normed.astype(BF)

    block = R.n2.at[pair_own]
    to_across = start(block, block, across)
    to_mate = start(block, block, mate)
    gather(vout, 1)
    gather(tin, 3)
    gather(tout, 3)
    to_across.wait_recv()
    block = R.n2.at[pair_across]
    passed = start(block, block, mate)
    gather(vin, 2)
    gather(vout, 2)
    gather(tin, 4)
    gather(tout, 4)
    to_mate.wait_recv()
    passed.wait_recv()

    def expert(pairs, low, high, w_in, w_out, h_ref, gu_ref, j):
        first, count = pairs
        per = high - low
        total_rows = count * per
        cols = pl.ds(pl.multiple_of(j * 256, 256), 256)
        inside = slice(first, first + count)
        R.u[:total_rows, :] = mm(
            R.n2[inside, low:high, :].reshape(total_rows, width), G[w_in, :, cols]
        )
        R.gh[:total_rows, :] = mm(
            R.gz[inside, low:high, :].reshape(total_rows, width), G[w_out, :, cols]
        )
        step = min(total_rows, VIS)

        @pl.loop(0, 2 * (total_rows // step))
        def _(i):
            lanes = lax.rem(i, 2) * 128
            rows = pl.ds(pl.multiple_of(i // 2 * step, 16), step)
            into = pl.ds(pl.multiple_of(first * per + i // 2 * step, 16), step)
            side = pl.ds(pl.multiple_of(lanes, 128), 128)
            pre = R.u[rows, side]
            cumulative = 0.5 * (1.0 + lax.erf(pre * inv_root_two))
            density = jnp.exp(-0.5 * pre * pre) * inv_root_tau
            onto = pl.ds(pl.multiple_of(j * 256 + lanes, 128), 128)
            h_ref[into, onto] = (pre * cumulative).astype(BF)
            gu_ref[into, onto] = (R.gh[rows, side] * (cumulative + pre * density)).astype(BF)

    def weight_grad(k, turned, ref):
        @pl.loop(0, width // 256)
        def _(j):
            cols = pl.ds(pl.multiple_of(j * 256, 256), 256)
            PART[k, :, cols] = mm(turned[...], ref[:, cols]).astype(BF)

    tiles = width // 256

    @pl.loop(0, tiles)
    def _(j):
        expert((0, 4), VIS, SEQ, TIN, TOUT, R.ht, R.gut, j)

    gather(vin, 3)
    weight_grad(TOUT, R.gztt, R.ht)

    @pl.loop(0, width // 256)
    def _(j):
        cols = pl.ds(pl.multiple_of(j * 256, 256), 256)
        R.n2vt[cols, :] = R.n2[:, :VIS, cols].reshape(4 * VIS, 256).T
        R.n2tt[cols, :] = R.n2[:, VIS:, cols].reshape(4 * TXT, 256).T

    gather(vout, 3)
    weight_grad(TIN, R.n2tt, R.gut)
    pass_sum(tout, 0)
    pass_sum(tin, 0)

    def text_terms(target, rows, weight):
        target[:, VIS:, :] = mm_nt(rows, G[weight]).astype(BF).reshape(4, TXT, width)

    text_terms(R.pg, R.gut[...], TIN)
    text_terms(R.pf, R.ht[...], TOUT)
    gather(vin, 4)
    gather(vout, 4)

    def terms(target, rows, weight, m):
        part = mm_nt(rows[2 * m * VIS : 2 * (m + 1) * VIS, :], G[weight]).astype(BF)
        target[2 * m : 2 * m + 2, :VIS, :] = part.reshape(2, VIS, width)

    mate_g = remote(R.pg.at[pl.ds(theirs, 2)], R.rg, mate)
    cross_g = remote(R.xsg, R.xrg, across)
    gy_across = remote(R.gy.at[x], R.gy.at[x], across)
    gy_mate = remote(R.ga.at[pair_own], R.ga.at[pair_own], mate)
    gy_passed = remote(R.ga.at[pair_across], R.ga.at[pair_across], mate)
    started.extend([cross_g, gy_across, gy_mate, gy_passed])

    def image_terms(m):
        terms(R.pg, R.guv, VIN, m)
        pl.when(c != m)(mate_g.start)

    def sum_cores(m):
        @pl.when(c == m)
        def _():
            mate_g.wait_recv()
            R.xsg[...] = (R.pg[pair_across].astype(F32) + R.rg[1 - x].astype(F32)).astype(BF)
            cross_g.start()

    def middle_back(m):
        @pl.when(c == m)
        def _():
            cross_g.wait_recv()

            @pl.loop(0, SEQ // 64)
            def _(j):
                rows = pl.ds(pl.multiple_of(j * 64, 64), 64)
                grad_normed = (
                    R.pg[pair_own, rows, :].astype(F32)
                    + R.rg[x, rows, :].astype(F32)
                    + R.xrg[rows, :].astype(F32)
                )
                normed, inverse = normalize(R.y1[rows, :])
                grad = R.dy[rows, :].astype(F32) + normalize_back(grad_normed, normed, inverse)
                R.gy[x, rows, :] = grad.astype(BF)
                R.ga[pair_own, rows, :] = (grad * live_rows(x, j)).astype(BF)

            gy_across.start()
            gy_mate.start()

    def middle_pass(m):
        @pl.when(c == m)
        def _():
            gy_across.wait_recv()

            @pl.loop(0, SEQ // 64)
            def _(j):
                rows = pl.ds(pl.multiple_of(j * 64, 64), 64)
                R.ga[pair_across, rows, :] = (
                    R.gy[1 - x, rows, :].astype(F32) * live_rows(1 - x, j)
                ).astype(BF)

            gy_passed.start()

    def middle_came(m):
        @pl.when(c != m)
        def _():
            gy_mate.wait_recv()
            gy_passed.wait_recv()

    sent(send_x)
    cross_a.wait_send()

    @pl.loop(0, tiles)
    def _(j):
        expert((0, 2), 0, VIS, VIN, VOUT, R.hv, R.guv, j)

    image_terms(0)

    @pl.loop(0, tiles)
    def _(j):
        expert((2, 2), 0, VIS, VIN, VOUT, R.hv, R.guv, j)
        pl.when(j == 0)(functools.partial(sum_cores, 0))

    pass_sum(tout, 1)
    image_terms(1)
    for copy in (to_across, to_mate, passed):
        sent(copy)
    sum_cores(1)
    pass_sum(tin, 1)
    weight_grad(VOUT, R.gzvt, R.hv)
    middle_back(0)
    pass_sum(vout, 0)
    pass_sum(tout, 2)
    weight_grad(VIN, R.n2vt, R.guv)
    pass_sum(vin, 0)
    pass_sum(tin, 2)

    terms(R.pf, R.hv, VOUT, 0)
    middle_pass(0)
    middle_back(1)
    pass_sum(tout, 3)
    terms(R.pf, R.hv, VOUT, 1)
    mate_f = start(R.pf.at[pl.ds(theirs, 2)], R.rf, mate)
    cross_f = remote(R.xsf, R.xrf, across)
    started.append(cross_f)
    pass_sum(tin, 3)
    mate_g.wait_send()
    middle_came(0)

    back_mate = [remote(R.pb.at[theirs + t], R.rb.at[t], mate) for t in range(2)]
    back_cross = [remote(R.xsb.at[t], R.xrb.at[t], across) for t in range(2)]
    started.extend(back_mate + back_cross)

    def attention_back(m):
        pairs = [2 * m, 2 * m + 1]
        grad_contexts = [mm(R.ga[i], R.wo[...]).astype(BF) for i in pairs]
        turned_k = [R.k[i].T for i in pairs]
        grad_q = [[], []]
        grad_k = [jnp.zeros((SEQ, span), F32) for _ in pairs]
        grad_v = [jnp.zeros((SEQ, span), F32) for _ in pairs]
        for h in range(heads):
            for t, i in enumerate(pairs):
                probs = R.probs[i * heads + h]
                grad_probs = mm_nt(only(h, R.v[i]), grad_contexts[t])
                exact = probs.astype(F32)
                inner = jnp.sum(grad_probs * exact, axis=0, keepdims=True)
                grad_scores = (exact * (grad_probs - inner)).astype(BF)
                grad_q[t].append(mm(head_rows(turned_k[t], h), grad_scores))
                grad_k[t] += mm(grad_scores, only(h, R.q[i]))
                grad_v[t] += mm(probs, only(h, grad_contexts[t]))
        for t, i in enumerate(pairs):
            turned_q = jnp.concatenate(grad_q[t], axis=0).T
            joined = jnp.concatenate([turned_q, grad_k[t], grad_v[t]], axis=1).astype(BF)
            R.gqkv[i, :, : 3 * span] = joined
            R.pb[i] = mm_nt(joined, G[ATT][:, : 3 * span]).astype(BF)
            pl.when(c != m)(back_mate[t].start)

    def back_sum(m, t):
        @pl.when(c == m)
        def _():
            back_mate[t].wait_recv()
            R.xsb[t] = (R.pb[2 * m + t].astype(F32) + R.rb[t].astype(F32)).astype(BF)
            back_cross[t].start()

    mate_f.wait_recv()
    R.xsf[...] = (R.pf[pair_across].astype(F32) + R.rf[1 - x].astype(F32)).astype(BF)
    R.fown[...] = (R.pf[pair_own].astype(F32) + R.rf[x].astype(F32)).astype(BF)
    attention_back(0)
    middle_pass(1)
    cross_f.start()
    pass_sum(vout, 1)
    back_sum(0, 0)
    back_sum(0, 1)
    pass_sum(vin, 1)
    middle_came(1)
    pass_sum(vout, 2)
    attention_back(1)
    pass_sum(vin, 2)
    back_sum(1, 0)

    lanes = width // 2

    @pl.loop(0, width // 256)
    def _(j):
        rows = pl.ds(pl.multiple_of(j * 256, 256), 256)
        grad_v = mm(R.n1t[rows, :], R.gqkv[:, :, lanes : 3 * span].reshape(4 * SEQ, span))
        grad_o = mm(R.ct[...], R.ga[:, :, rows].reshape(4 * SEQ, 256)).T
        PART[ATT, rows, lanes:] = jnp.concatenate([grad_v, grad_o], axis=1).astype(BF)

    pass_sum(far, 0)

    cross_f.wait_recv()

    @pl.loop(0, SEQ // 64)
    def _(j):
        rows = pl.ds(pl.multiple_of(j * 64, 64), 64)
        branch = R.fown[rows, :].astype(F32) + R.xrf[rows, :].astype(F32)
        OUT[x, rows, :] = (R.y1[rows, :] + live_rows(x, j) * branch).astype(BF)

    out_across = start(OUT.at[x], OUT.at[x], across)

    @pl.loop(0, width // 256)
    def _(j):
        rows = pl.ds(pl.multiple_of(j * 256, 256), 256)
        grads = mm(R.n1t[rows, :], R.gqkv[:, :, :lanes].reshape(4 * SEQ, lanes))
        PART[ATT, rows, :lanes] = grads.astype(BF)

    pass_sum(near, 0)
    back_sum(1, 1)
    pass_sum(vout, 3)
    pass_sum(vin, 3)

    def input_back(m, t):
        @pl.when(c == m)
        def _():
            back_cross[t].wait_recv()

            @pl.loop(0, SEQ // 64)
            def _(j):
                rows = pl.ds(pl.multiple_of(j * 64, 64), 64)
                grad_normed = R.xsb[t, rows, :].astype(F32) + R.xrb[t, rows, :].astype(F32)
                normed, inverse = normalize(R.x[t, rows, :].astype(F32))
                grad = R.gy[t, rows, :].astype(F32) + normalize_back(grad_normed, normed, inverse)
                high = grad.astype(BF)
                rows = pl.ds(pl.multiple_of(t * SEQ + j * 64, 64), 64)
                R.hv[rows, :] = high
                R.guv[rows, :] = (grad - high.astype(F32)).astype(BF)

    pass_sum(far, 1)
    input_back(0, 0)
    pass_sum(near, 1)
    input_back(0, 1)
    end_sum(tout, tin)
    pass_sum(far, 2)
    pass_sum(near, 2)
    end_sum(vout, vin)

    leaving = []

    def leave(slot, source, target):
        leaving.append(fetch(slot, source, target))

    slots = lax.broadcasted_iota(jnp.int32, (row_count, 2 * SEQ), 1)
    rows = lax.broadcasted_iota(jnp.int32, (row_count, 2 * SEQ), 0)
    turn = slots // SEQ
    back = placed(turn, slots - turn * SEQ, rows, slots >= 0)
    out_across.wait_recv()
    R.out_tokens[...] = mm(back, OUT[...].reshape(2 * SEQ, width)).astype(BF)
    leave(6, R.out_tokens, R.out_tokens_hbm)
    for copy in finals:
        copy.wait_recv()
    finals.clear()
    leave(7, GW.at[pl.ds(1, 4)], R.gw_hbm.at[pl.ds(1, 4)])
    pass_sum(far, 3)
    pass_sum(near, 3)
    input_back(1, 0)
    input_back(1, 1)
    R.grad_tokens[...] = mm(back, R.hv[: 2 * SEQ, :]) + mm(back, R.guv[: 2 * SEQ, :])
    leave(8, R.grad_tokens, R.grad_tokens_hbm)
    end_sum(far, near)

    first_lane = lax.broadcasted_iota(jnp.int32, (own, 128), 1) == 0
    for place in range(2):
        attn = sum(total for k, total in row_sums[place] if k == ATT)
        experts = sum(total for k, total in row_sums[place] if k != ATT)
        R.gs[place] = jnp.where(first_lane, attn, experts)
    peers = [
        start(R.gs.at[place], R.gr.at[slot], device)
        for slot, (place, device) in enumerate(((1, mate), (0, across), (1, diagonal)))
    ]
    for copy in finals + peers:
        copy.wait_recv()
    leave(9, GW.at[pl.ds(0, 1)], R.gw_hbm.at[pl.ds(0, 1)])
    GG[...] = (R.gs[0] + R.gr[1]) + (R.gr[0] + R.gr[2])

    for copy in started:
        copy.wait_send()
    for copy in leaving:
        copy.wait()
    for k in range(5):
        for semaphore in (k, 5 + k):
            pltpu.make_async_remote_copy(
                src_ref=LAND.at[k],
                dst_ref=LAND.at[k],
                send_sem=R.ring_sent.at[semaphore],
                recv_sem=R.ring_came.at[0],
                device_id=ahead,
                device_id_type=MESH,
            ).wait_send()


def finish_kernel(n_results, out, gtok, gw_hbm, gg, gain_attn, gain_ffn, *rest):
    results, scratch = rest[:n_results], rest[n_results:]
    buffers, (out_buffer, gtok_buffer, gw, came, gone) = scratch[:n_results], scratch[n_results:]
    arriving = [
        pltpu.make_async_copy(source, target, came.at[slot])
        for slot, (source, target) in enumerate(((gw_hbm, gw), (out, out_buffer), (gtok, gtok_buffer)))
    ]
    for copy in arriving:
        copy.start()
    width = gw.shape[3]
    own = gw.shape[2]
    span = width // 4
    gain_one, gain_two = column(gain_attn), column(gain_ffn)
    square = unit(own).astype(F32)
    leaving = []

    def leave(slot, source):
        copy = pltpu.make_async_copy(source, results[slot], gone.at[slot])
        copy.start()
        leaving.append(copy)

    def both(part):
        cols = slice(part * span, (part + 1) * span)
        return jnp.concatenate([gw[ATT, core][:, cols] for core in range(2)], axis=1)

    def put(slot, value):
        buffers[slot][...] = value
        leave(slot, buffers[slot])

    put(2, jnp.sum(square * (gg[:, :1] / gain_one), axis=0, keepdims=True))
    put(7, jnp.sum(square * (gg[:, 1:2] / gain_two), axis=0, keepdims=True))
    arriving[0].wait()
    for slot, k, scale in ((8, VIN, gain_two), (9, VOUT, 1.0), (10, TIN, gain_two), (11, TOUT, 1.0)):
        put(slot, jnp.concatenate([gw[k, 0], gw[k, 1]], axis=1) * scale)
    put(3, both(0) * (gain_one * HEAD_DIM**-0.5))
    put(4, both(1) * gain_one)
    put(5, both(2) * gain_one)
    put(6, both(3))
    arriving[1].wait()
    leave(0, out_buffer)
    arriving[2].wait()
    leave(1, gtok_buffer)
    for copy in leaving:
        copy.wait()


def fused_layer(
    tokens,
    caption_lengths,
    gain_attn,
    w_query,
    w_key,
    w_value,
    w_out,
    gain_ffn,
    vis_in,
    vis_out,
    txt_in,
    txt_out,
    cotangent,
):
    n = lax.axis_size("dp") // 2
    own = w_query.shape[0]
    row_count, width = tokens.shape
    span = width // 4
    heads = span // HEAD_DIM
    gain_one, gain_two = gain_attn.reshape(1, own), gain_ffn.reshape(1, own)

    rows = 4 * SEQ
    scratch = dict(
        tokens=pltpu.VMEM((row_count, width), BF),
        cotangent=pltpu.VMEM((row_count, width), BF),
        txt_in=pltpu.VMEM((own, 2 * width), BF),
        txt_out=pltpu.VMEM((own, 2 * width), BF),
        vis_in=pltpu.VMEM((own, 2 * width), BF),
        vis_out=pltpu.VMEM((own, 2 * width), BF),
        out_tokens=pltpu.VMEM((row_count, width), BF),
        grad_tokens=pltpu.VMEM((row_count, width), F32),
        gw=pltpu.VMEM((5, 2, own, width), F32),
        local=pltpu.SemaphoreType.DMA((10,)),
        shard=pltpu.VMEM((5, 2, own, width), BF),
        lens=pltpu.VMEM((2, 8, 128), F32),
        x=pltpu.VMEM((2, SEQ, width), BF),
        dy=pltpu.VMEM((SEQ, width), BF),
        padded_out=pltpu.VMEM((2, SEQ, width), BF),
        gathered=pltpu.VMEM((5, width, width), BF),
        part=pltpu.VMEM((5, width, width), BF),
        land=pltpu.VMEM((5, n - 1, 2 * own, width), BF),
        give=pltpu.VMEM((5, own, width), F32),
        x4=pltpu.VMEM((4, SEQ, width), BF),
        lens4=pltpu.VMEM((4, 8, 128), F32),
        n1=pltpu.VMEM((4, SEQ, width), BF),
        n1t=pltpu.VMEM((width, rows), BF),
        gz=pltpu.VMEM((4, SEQ, width), BF),
        gzvt=pltpu.VMEM((width, 4 * VIS), BF),
        ct=pltpu.VMEM((span, rows), BF),
        fown=pltpu.VMEM((SEQ, width), BF),
        gztt=pltpu.VMEM((width, 4 * TXT), BF),
        wo=pltpu.VMEM((width, span), BF),
        q=pltpu.VMEM((4, SEQ, span), BF),
        k=pltpu.VMEM((4, SEQ, span), BF),
        v=pltpu.VMEM((4, SEQ, span), BF),
        probs=pltpu.VMEM((4 * heads, SEQ, SEQ), BF),
        pa=pltpu.VMEM((4, SEQ, width), BF),
        ra=pltpu.VMEM((2, SEQ, width), BF),
        xs=pltpu.VMEM((SEQ, width), BF),
        xr=pltpu.VMEM((SEQ, width), BF),
        y1=pltpu.VMEM((SEQ, width), F32),
        n2vt=pltpu.VMEM((width, 4 * VIS), BF),
        n2tt=pltpu.VMEM((width, 4 * TXT), BF),
        u=pltpu.VMEM((4 * VIS, 256), F32),
        gh=pltpu.VMEM((4 * VIS, 256), F32),
        hv=pltpu.VMEM((4 * VIS, width), BF),
        guv=pltpu.VMEM((4 * VIS, width), BF),
        ht=pltpu.VMEM((4 * TXT, width), BF),
        gut=pltpu.VMEM((4 * TXT, width), BF),
        pg=pltpu.VMEM((4, SEQ, width), BF),
        rg=pltpu.VMEM((2, SEQ, width), BF),
        gy=pltpu.VMEM((2, SEQ, width), BF),
        xsf=pltpu.VMEM((SEQ, width), BF),
        xrf=pltpu.VMEM((SEQ, width), BF),
        xsb=pltpu.VMEM((2, SEQ, width), BF),
        xrb=pltpu.VMEM((2, SEQ, width), BF),
        gs=pltpu.VMEM((2, own, 128), F32),
        gr=pltpu.VMEM((3, own, 128), F32),
        sent=pltpu.SemaphoreType.DMA((40,)),
        came=pltpu.SemaphoreType.DMA((40,)),
        ring_sent=pltpu.SemaphoreType.DMA((10,)),
        ring_came=pltpu.SemaphoreType.DMA((6 * 2 * (n // 2) * 2,)),
    )
    inputs = dict(
        lengths=caption_lengths,
        tokens_hbm=tokens,
        cotangent_hbm=cotangent,
        gain_attn=gain_one,
        gain_ffn=gain_two,
        w_query=w_query,
        w_key=w_key,
        w_value=w_value,
        w_out=w_out.T,
        vis_in_hbm=vis_in,
        vis_out_hbm=vis_out.T,
        txt_in_hbm=txt_in,
        txt_out_hbm=txt_out.T,
    )
    results = dict(
        out_tokens_hbm=jax.ShapeDtypeStruct((row_count, width), BF),
        grad_tokens_hbm=jax.ShapeDtypeStruct((row_count, width), F32),
        gw_hbm=jax.ShapeDtypeStruct((5, 2, own, width), F32),
        gg=jax.ShapeDtypeStruct((own, 128), F32),
    )
    vmem, hbm = pl.BlockSpec(memory_space=pltpu.VMEM), pl.BlockSpec(memory_space=pl.ANY)
    names = tuple(inputs) + tuple(results) + tuple(scratch)
    out, gtok, gw, gg = pl.pallas_call(
        functools.partial(layer_kernel, n, names),
        out_shape=tuple(results.values()),
        in_specs=[pl.BlockSpec(memory_space=pltpu.SMEM)] + [hbm if k.endswith(HBM) else vmem for k in names[1 : len(inputs)]],
        out_specs=[hbm if k.endswith(HBM) else vmem for k in results],
        scratch_shapes=list(scratch.values()),
        compiler_params=pltpu.CompilerParams(
            collective_id=0, has_side_effects=True, vmem_limit_bytes=60 * 2**20
        ),
    )(*inputs.values())

    shapes = (
        jax.ShapeDtypeStruct((row_count, width), BF),
        jax.ShapeDtypeStruct((row_count, width), F32),
        jax.ShapeDtypeStruct((1, own), F32),
        jax.ShapeDtypeStruct((own, 2 * span), F32),
        jax.ShapeDtypeStruct((own, 2 * span), F32),
        jax.ShapeDtypeStruct((own, 2 * span), F32),
        jax.ShapeDtypeStruct((own, 2 * span), F32),
        jax.ShapeDtypeStruct((1, own), F32),
        jax.ShapeDtypeStruct((own, 2 * width), F32),
        jax.ShapeDtypeStruct((own, 2 * width), F32),
        jax.ShapeDtypeStruct((own, 2 * width), F32),
        jax.ShapeDtypeStruct((own, 2 * width), F32),
    )
    buffers = [pltpu.VMEM(one.shape if slot > 1 else (8, 128), F32) for slot, one in enumerate(shapes)]
    final = pl.pallas_call(
        functools.partial(finish_kernel, len(shapes)),
        out_shape=shapes,
        in_specs=[hbm] * 3 + [vmem] * 3,
        out_specs=[hbm] * len(shapes),
        scratch_shapes=buffers
        + [
            pltpu.VMEM((row_count, width), BF),
            pltpu.VMEM((row_count, width), F32),
            pltpu.VMEM((5, 2, own, width), F32),
            pltpu.SemaphoreType.DMA((3,)),
            pltpu.SemaphoreType.DMA((len(shapes),)),
        ],
        compiler_params=pltpu.CompilerParams(vmem_limit_bytes=60 * 2**20),
    )(out, gtok, gw, gg, gain_one, gain_two)
    final = list(final)
    final[2] = final[2].reshape(own)
    final[7] = final[7].reshape(own)
    for turned in (6, 9, 11):
        final[turned] = final[turned].T
    return tuple(final)


def norm_parts(values):
    center = values - jnp.mean(values, axis=-1, keepdims=True)
    spread = jnp.mean(center * center, axis=-1, keepdims=True)
    inverse = lax.rsqrt(spread + epsilon)
    return (center * inverse, inverse)


def norm_back(grad_out, normed, inverse, gain):
    grad_normed = grad_out * gain
    grad_gain = jnp.sum(grad_out * normed, axis=0)
    inner = (
        grad_normed
        - jnp.mean(grad_normed, axis=-1, keepdims=True)
        - normed * jnp.mean(grad_normed * normed, axis=-1, keepdims=True)
    )
    return (inverse * inner, grad_gain)


def matmul(left, right):
    return jnp.dot(left, right, preferred_element_type=jnp.float32)


def matmul_tn(left, right):
    return lax.dot_general(
        left, right, (((0,), (0,)), ((), ())), preferred_element_type=jnp.float32
    )


def matmul_nt(left, right):
    return lax.dot_general(
        left, right, (((1,), (1,)), ((), ())), preferred_element_type=jnp.float32
    )


def gelu_slope(pre):
    cumulative = 0.5 * (1.0 + lax.erf(pre * inv_root_two))
    density = jnp.exp(-0.5 * pre * pre) * inv_root_tau
    return cumulative + pre * density


def expert_forward(rows, weight_in, weight_out):
    pre = matmul(rows, weight_in)
    hidden = jax.nn.gelu(pre, approximate=False).astype(jnp.bfloat16)
    return (pre, hidden, matmul(hidden, weight_out))


def expert_backward(rows, pre, hidden, grad_out, weight_in, weight_out):
    grad_weight_out = matmul_tn(hidden, grad_out)
    grad_hidden = matmul_nt(grad_out, weight_out)
    grad_pre = (grad_hidden * gelu_slope(pre)).astype(jnp.bfloat16)
    return (matmul_tn(rows, grad_pre), grad_weight_out, matmul_nt(grad_pre, weight_in))


def join_experts(image_rows, text_rows, pair_count, width):
    joined = jnp.concatenate(
        [
            image_rows.reshape(pair_count, PATCHES, width),
            text_rows.reshape(pair_count, CAPTION, width),
        ],
        axis=1,
    )
    return joined.reshape(-1, width)


def plain_layer(
    tokens,
    caption_lengths,
    gain_attn,
    w_query,
    w_key,
    w_value,
    w_out,
    gain_ffn,
    vis_in,
    vis_out,
    txt_in,
    txt_out,
    cotangent,
):
    seq_len = PATCHES + CAPTION
    width = tokens.shape[1]
    pair_count = tokens.shape[0] // seq_len
    half_pairs = pair_count // lax.axis_size("tensor")
    half_rows = half_pairs * seq_len
    row_start = lax.axis_index("tensor") * half_rows
    gain_one, query_w, key_w, value_w, out_w = (
        lax.all_gather(gain_attn, "dp", axis=0, tiled=True),
        lax.all_gather(w_query, "dp", axis=0, tiled=True),
        lax.all_gather(w_key, "dp", axis=0, tiled=True),
        lax.all_gather(w_value, "dp", axis=0, tiled=True),
        lax.all_gather(w_out, "dp", axis=1, tiled=True),
    )
    gain_two, vis_in_w, vis_out_w, txt_in_w, txt_out_w = (
        lax.all_gather(gain_ffn, "dp", axis=0, tiled=True),
        lax.all_gather(vis_in, "dp", axis=0, tiled=True),
        lax.all_gather(vis_out, "dp", axis=1, tiled=True),
        lax.all_gather(txt_in, "dp", axis=0, tiled=True),
        lax.all_gather(txt_out, "dp", axis=1, tiled=True),
    )
    gain_one = gain_one.astype(jnp.float32)
    gain_two = gain_two.astype(jnp.float32)
    head_local = query_w.shape[1] // HEAD_DIM
    score_scale = HEAD_DIM ** (-0.5)
    position = jnp.arange(seq_len, dtype=jnp.int32)
    live = (position[None, :] < PATCHES) | (position[None, :] - PATCHES < caption_lengths[:, None])
    valid_rows = live.astype(jnp.float32)
    mask_col = valid_rows.reshape(-1, 1)
    key_live = valid_rows[:, None, None, :] > 0.5

    def own_rows(values):
        return lax.dynamic_slice_in_dim(values, row_start, half_rows, 0)

    inputs = tokens.astype(jnp.float32)
    normed_one, inverse_one = norm_parts(inputs)
    first_in = (normed_one * gain_one).astype(jnp.bfloat16)

    def project(weight):
        return (
            matmul(first_in, weight)
            .astype(jnp.bfloat16)
            .reshape(pair_count, seq_len, head_local, HEAD_DIM)
        )

    queries = project(query_w)
    keys_all = project(key_w)
    values_all = project(value_w)

    def score_block():
        raw = (
            jnp.einsum("pqhe,pkhe->phqk", queries, keys_all, preferred_element_type=jnp.float32)
            * score_scale
        )
        return jnp.where(key_live, raw, -1e30)

    scores = score_block()
    top = jnp.max(scores, axis=-1, keepdims=True)
    weights = jnp.exp(scores - top)
    total = jnp.sum(weights, axis=-1, keepdims=True)
    probs = (weights / total).astype(jnp.bfloat16)
    log_total = top + jnp.log(total)
    context = jnp.einsum("phqk,pkhe->pqhe", probs, values_all, preferred_element_type=jnp.float32)
    context = context.astype(jnp.bfloat16).reshape(-1, head_local * HEAD_DIM)
    attn_terms = matmul(context, out_w)
    attended_own = lax.psum_scatter(
        attn_terms.astype(jnp.bfloat16), "tensor", scatter_dimension=0, tiled=True
    ).astype(jnp.float32)
    mask_own = own_rows(mask_col)
    middle_own = own_rows(inputs) + mask_own * attended_own
    normed_two, inverse_two = norm_parts(middle_own)
    second_own = (normed_two * gain_two).astype(jnp.bfloat16)
    grid = lax.all_gather(second_own, "tensor", axis=0, tiled=True).reshape(
        pair_count, seq_len, width
    )
    image_rows = grid[:, :PATCHES].reshape(-1, width)
    text_rows = grid[:, PATCHES:].reshape(-1, width)
    image_pre, image_hidden, image_part = expert_forward(image_rows, vis_in_w, vis_out_w)
    text_pre, text_hidden, text_part = expert_forward(text_rows, txt_in_w, txt_out_w)
    image_own, text_own = (
        lax.psum_scatter(
            image_part.astype(jnp.bfloat16), "tensor", scatter_dimension=0, tiled=True
        ).astype(jnp.float32),
        lax.psum_scatter(
            text_part.astype(jnp.bfloat16), "tensor", scatter_dimension=0, tiled=True
        ).astype(jnp.float32),
    )
    branch_own = join_experts(image_own, text_own, half_pairs, width)
    output_own = (middle_own + mask_own * branch_own).astype(jnp.bfloat16)
    upstream = cotangent.astype(jnp.float32)
    grad_branch = (upstream * mask_col).astype(jnp.bfloat16).reshape(pair_count, seq_len, width)
    image_grads = expert_backward(
        image_rows,
        image_pre,
        image_hidden,
        grad_branch[:, :PATCHES].reshape(-1, width),
        vis_in_w,
        vis_out_w,
    )
    text_grads = expert_backward(
        text_rows,
        text_pre,
        text_hidden,
        grad_branch[:, PATCHES:].reshape(-1, width),
        txt_in_w,
        txt_out_w,
    )
    back_image_own, back_text_own = (
        lax.psum_scatter(
            image_grads[2].astype(jnp.bfloat16), "tensor", scatter_dimension=0, tiled=True
        ).astype(jnp.float32),
        lax.psum_scatter(
            text_grads[2].astype(jnp.bfloat16), "tensor", scatter_dimension=0, tiled=True
        ).astype(jnp.float32),
    )
    grad_second_own = join_experts(back_image_own, back_text_own, half_pairs, width)
    grad_norm_own, gain_part = norm_back(grad_second_own, normed_two, inverse_two, gain_two)
    grad_middle_own = own_rows(upstream) + grad_norm_own
    output_wide, grad_middle, gain_parts = (
        lax.all_gather(
            output_own.astype(jnp.float32).astype(jnp.bfloat16), "tensor", axis=0, tiled=True
        ).astype(jnp.float32),
        lax.all_gather(grad_middle_own.astype(jnp.bfloat16), "tensor", axis=0, tiled=True).astype(
            grad_middle_own.dtype
        ),
        lax.all_gather(gain_part.astype(jnp.bfloat16), "tensor", axis=0, tiled=True).astype(
            gain_part.dtype
        ),
    )
    output = output_wide.astype(jnp.bfloat16)
    grad_gain_two = jnp.sum(gain_parts.reshape(-1, width), axis=0)
    grad_attended = (grad_middle * mask_col).astype(jnp.bfloat16)
    grad_out_w = matmul_tn(context, grad_attended)
    grad_context = (
        matmul_nt(grad_attended, out_w)
        .astype(jnp.bfloat16)
        .reshape(pair_count, seq_len, head_local, HEAD_DIM)
    )
    scores_again = score_block()
    probs_exact = jnp.exp(scores_again - log_total)
    grad_probs = jnp.einsum(
        "pqhe,pkhe->phqk", grad_context, values_all, preferred_element_type=jnp.float32
    )
    inner = jnp.sum(grad_probs * probs_exact, axis=-1, keepdims=True)
    grad_scores = (probs_exact * (grad_probs - inner)).astype(jnp.bfloat16)
    grad_values = jnp.einsum(
        "phqk,pqhe->pkhe", probs, grad_context, preferred_element_type=jnp.float32
    )
    grad_values = grad_values.astype(jnp.bfloat16).reshape(-1, head_local * HEAD_DIM)
    grad_queries = (
        jnp.einsum("phqk,pkhe->pqhe", grad_scores, keys_all, preferred_element_type=jnp.float32)
        * score_scale
    )
    grad_queries = grad_queries.astype(jnp.bfloat16).reshape(-1, head_local * HEAD_DIM)
    grad_keys = (
        jnp.einsum("phqk,pqhe->pkhe", grad_scores, queries, preferred_element_type=jnp.float32)
        * score_scale
    )
    grad_keys = grad_keys.astype(jnp.bfloat16).reshape(-1, head_local * HEAD_DIM)
    grad_query_w = matmul_tn(first_in, grad_queries)
    grad_key_w = matmul_tn(first_in, grad_keys)
    grad_value_w = matmul_tn(first_in, grad_values)
    first_part = (
        matmul_nt(grad_queries, query_w)
        + matmul_nt(grad_keys, key_w)
        + matmul_nt(grad_values, value_w)
    )
    grad_first = lax.psum(first_part.astype(jnp.bfloat16), "tensor").astype(jnp.float32)
    grad_norm_one, grad_gain_one = norm_back(grad_first, normed_one, inverse_one, gain_one)
    grad_inputs = grad_middle + grad_norm_one
    attn_sent = (
        lax.psum_scatter(grad_gain_one, "dp", scatter_dimension=0, tiled=True),
        lax.psum_scatter(grad_query_w, "dp", scatter_dimension=0, tiled=True),
        lax.psum_scatter(grad_key_w, "dp", scatter_dimension=0, tiled=True),
        lax.psum_scatter(grad_value_w, "dp", scatter_dimension=0, tiled=True),
        lax.psum_scatter(grad_out_w, "dp", scatter_dimension=1, tiled=True),
    )
    final_expert = (
        lax.psum_scatter(grad_gain_two, "dp", scatter_dimension=0, tiled=True),
        lax.psum_scatter(image_grads[0], "dp", scatter_dimension=0, tiled=True),
        lax.psum_scatter(image_grads[1], "dp", scatter_dimension=1, tiled=True),
        lax.psum_scatter(text_grads[0], "dp", scatter_dimension=0, tiled=True),
        lax.psum_scatter(text_grads[1], "dp", scatter_dimension=1, tiled=True),
    )
    return (
        output,
        grad_inputs,
        attn_sent[0],
        attn_sent[1],
        attn_sent[2],
        attn_sent[3],
        attn_sent[4],
        final_expert[0],
        final_expert[1],
        final_expert[2],
        final_expert[3],
        final_expert[4],
    )


def solution(mesh):
    def local(tokens, lengths, gain, w_query, *rest):
        ring = mesh.shape["dp"] // 2
        fits = (
            mesh.shape["tensor"] == 2
            and ring == 8
            and lengths.shape[0] == 2
            and w_query.shape[0] % 16 == 0
        )
        layer = fused_layer if fits else plain_layer
        return layer(tokens, lengths, gain, w_query, *rest)

    return jax.shard_map(
        local,
        mesh=mesh,
        in_specs=(
            P("dp", None),
            P("dp"),
            P("dp"),
            P("dp", "tensor"),
            P("dp", "tensor"),
            P("dp", "tensor"),
            P("tensor", "dp"),
            P("dp"),
            P("dp", "tensor"),
            P("tensor", "dp"),
            P("dp", "tensor"),
            P("tensor", "dp"),
            P("dp", None),
        ),
        out_specs=(
            P("dp", None),
            P("dp", None),
            P("dp"),
            P("dp", "tensor"),
            P("dp", "tensor"),
            P("dp", "tensor"),
            P("tensor", "dp"),
            P("dp"),
            P("dp", "tensor"),
            P("tensor", "dp"),
            P("dp", "tensor"),
            P("tensor", "dp"),
        ),
        check_vma=False,
    )
```

```python
import functools
import math
import types

import jax
import jax.numpy as jnp
from jax import lax
from jax.experimental import pallas as pl
from jax.experimental.pallas import tpu as pltpu
from jax.sharding import PartitionSpec as P

HEAD_DIM = 64
PATCHES = 197
CAPTION = 40
VIS = 208
TXT = 48
SEQ = VIS + TXT

MESH = pl.DeviceIdType.MESH
HBM = "_hbm"
BF = jnp.bfloat16
F32 = jnp.float32

ATT, TIN, TOUT, VIN, VOUT = range(5)

epsilon = 1e-05
inv_root_two = 1.0 / math.sqrt(2.0)
inv_root_tau = 1.0 / math.sqrt(2.0 * math.pi)


def mm(left, right):
    return jnp.dot(left, right, preferred_element_type=F32)


def mm_nt(left, right):
    return lax.dot_general(left, right, (((1,), (1,)), ((), ())), preferred_element_type=F32)


def mm_tn(left, right):
    return lax.dot_general(left, right, (((0,), (0,)), ((), ())), preferred_element_type=F32)


def normalize(values):
    center = values - jnp.mean(values, axis=-1, keepdims=True)
    spread = jnp.mean(center * center, axis=-1, keepdims=True)
    inverse = lax.rsqrt(spread + epsilon)
    return center * inverse, inverse


def normalize_back(grad_normed, normed, inverse):
    return inverse * (
        grad_normed
        - jnp.mean(grad_normed, axis=-1, keepdims=True)
        - normed * jnp.mean(grad_normed * normed, axis=-1, keepdims=True)
    )


def unit(size):
    rows = lax.broadcasted_iota(jnp.int32, (size, size), 0)
    return (rows == lax.broadcasted_iota(jnp.int32, (size, size), 1)).astype(F32).astype(BF)


def column(ref):
    size = ref.shape[1]
    return jnp.sum(unit(size).astype(F32) * ref[...].astype(F32), axis=1, keepdims=True)


def layer_kernel(n, names, *refs):
    R = types.SimpleNamespace(**dict(zip(names, refs)))
    R.pb, R.pf, R.ga, R.rf, R.rb, R.n2 = R.pg, R.pa, R.x4, R.ra, R.rg, R.n1
    R.gqkv, R.xsg, R.xrg = R.n2, R.xs, R.xr
    S, G, PART, LAND = R.shard, R.gathered, R.part, R.land
    OUT, GW, GG = R.padded_out, R.gw, R.gg
    width = G.shape[2]
    own = width // (2 * n)
    span = width // 4
    heads = span // HEAD_DIM

    x = lax.axis_index("tensor")
    d = lax.axis_index("dp")
    c = lax.rem(d, 2)
    other = 1 - c
    chip = d // 2
    y, z = lax.rem(chip, 2), chip // 2
    r = z + y * (n - 1 - 2 * z)
    half = n // 2

    def chip_at(pos):
        pos = lax.rem(pos + 2 * n, n)
        upper = pos // half
        return 2 * (pos + upper * (n - 1 - 2 * pos)) + upper

    near_mate = d + 1 - 2 * c
    mate, across, diagonal = (near_mate, x), (d, 1 - x), (near_mate, 1 - x)
    ahead = (2 * chip_at(r + 1) + c, x)
    behind = (2 * chip_at(r - 1) + c, x)
    way = (ahead, behind)

    offsets = {hop: 2 * own * chip_at(r + hop) for hop in range(-half, half + 1)}


    my_rows = pl.ds(pl.multiple_of(own * d, 16), own)

    def fetch(slot, source, target):
        copy = pltpu.make_async_copy(source, target, R.local.at[slot])
        copy.start()
        return copy

    fetched = [
        fetch(0, R.tokens_hbm, R.tokens),
        fetch(1, R.txt_in_hbm, R.txt_in),
        fetch(2, R.txt_out_hbm, R.txt_out),
        fetch(3, R.vis_in_hbm, R.vis_in),
        fetch(4, R.vis_out_hbm, R.vis_out),
        fetch(5, R.cotangent_hbm, R.cotangent),
    ]

    barrier = pltpu.get_barrier_semaphore()
    for device in (mate, across, diagonal, ahead, behind):
        pl.semaphore_signal(barrier, inc=1, device_id=device, device_id_type=MESH)

    mine, theirs = pl.multiple_of(2 * c, 2), pl.multiple_of(2 * other, 2)
    pair_own = 2 * c + x
    pair_across = 2 * c + 1 - x

    started = []
    counter = [0]

    def remote(source, target, device):
        index = counter[0]
        counter[0] += 1
        return pltpu.make_async_remote_copy(
            src_ref=source,
            dst_ref=target,
            send_sem=R.sent.at[index],
            recv_sem=R.came.at[index],
            device_id=device,
            device_id_type=MESH,
        )

    def start(source, target, device):
        copy = remote(source, target, device)
        copy.start()
        started.append(copy)
        return copy

    def sent(copy):
        copy.wait_send()
        started[:] = [one for one in started if one is not copy]

    def rows_at(hop):
        return pl.ds(pl.multiple_of(offsets[hop], 16), 2 * own)

    near, far = (ATT, 0, width // 2), (ATT, width // 2, width // 2)
    parts = [near, far] + [(k, 0, width) for k in (TIN, TOUT, VIN, VOUT)]
    tin, tout, vin, vout = parts[2:]
    longest = half

    def hops(part, side):
        return half if (parts.index(part) + side) % 2 == 0 else n - 1 - half

    def ring_index(part, side, s):
        return (parts.index(part) * 2 + side) * longest + s

    def view(ref, part, rows):
        k, first, count = part
        return ref.at[k, rows, pl.ds(first, count)]

    sum_base = len(parts) * 2 * longest

    def gather_copy(part, side, s, pos):
        block = view(G, part, rows_at(pos))
        i = ring_index(part, side, s)
        return pltpu.make_async_remote_copy(
            src_ref=block,
            dst_ref=block,
            send_sem=R.ring_sent.at[part[0]],
            recv_sem=R.ring_came.at[i],
            device_id=way[side],
            device_id_type=MESH,
        )

    def gather(part, s):
        for side in range(2):
            pos = -s if side == 0 else s
            if 0 < s <= hops(part, side):
                gather_copy(part, side, s - 1, pos).wait_recv()
            if s < hops(part, side):
                gather_copy(part, side, s, pos).start()

    def landed(part, side, s):
        k, first, count = part
        return LAND.at[k, side * hops(part, 0) + s, :, pl.ds(first, count)]

    def sum_copy(part, side, s, source):
        i = sum_base + ring_index(part, side, s)
        return pltpu.make_async_remote_copy(
            src_ref=source,
            dst_ref=landed(part, side, s),
            send_sem=R.ring_sent.at[5 + part[0]],
            recv_sem=R.ring_came.at[i],
            device_id=way[side],
            device_id_type=MESH,
        )

    def pass_sum(part, s):
        for side in range(2):
            reach = hops(part, side)
            if s >= reach:
                continue
            pos = reach - s if side == 0 else s - reach
            term = view(PART, part, rows_at(pos))
            if s == 0:
                source = term
            else:
                source = landed(part, side, s - 1)
                sum_copy(part, side, s - 1, source).wait_recv()
                source[...] = (source[...].astype(F32) + term[...].astype(F32)).astype(BF)
            sum_copy(part, side, s, source).start()

    finals = []
    row_sums = [[], []]

    def end_sum(*group):
        for part in group:
            k, first, count = part
            ends = []
            for side in range(2):
                end = landed(part, side, hops(part, side) - 1)
                sum_copy(part, side, hops(part, side) - 1, end).wait_recv()
                ends.append(end)
            cols = slice(first, first + count)
            counted = min(3 * span - first, count) if k == ATT else count

            def total(core):
                rows = pl.ds(pl.multiple_of(own * core, 16), own)
                chip_rows = pl.ds(pl.multiple_of(2 * own * chip + own * core, 16), own)
                block = (
                    ends[0][rows, :].astype(F32)
                    + ends[1][rows, :].astype(F32)
                    + PART[k, chip_rows, cols].astype(F32)
                )
                if k in (ATT, TIN, VIN):
                    weighted = G[k, chip_rows, cols].astype(F32)[:, :counted] * block[:, :counted]
                    total = jnp.sum(weighted, axis=-1, keepdims=True)
                    row_sums[0 if core is c else 1].append((k, total))
                return block

            R.give[k, :, cols] = total(other)
            finals.append(
                start(R.give.at[k, :, pl.ds(first, count)], GW.at[k, c, :, pl.ds(first, count)], mate)
            )
            GW[k, c, :, cols] = total(c)

    def shard_part(k, value):
        for core in range(2):
            S[k, core] = value(core).astype(BF)

    gain_one, gain_two = column(R.gain_attn), column(R.gain_ffn)

    def attention_part(core):
        cols = slice(core * span, (core + 1) * span)
        return jnp.concatenate(
            [
                R.w_query[:, cols].astype(F32) * (gain_one * HEAD_DIM**-0.5),
                R.w_key[:, cols].astype(F32) * gain_one,
                R.w_value[:, cols].astype(F32) * gain_one,
                R.w_out[:, cols].astype(F32),
            ],
            axis=1,
        )

    def half_of(ref, core):
        return ref[:, core * width : (core + 1) * width].astype(F32) * gain_two

    def turned_half(ref, core):
        return ref[:, core * width : (core + 1) * width]

    lengths = R.lengths

    def live(t, slots):
        return (slots < PATCHES) | ((slots >= VIS) & (slots < VIS + lengths[t]))

    def live_rows(t, j, count=64):
        slots = lax.broadcasted_iota(jnp.int32, (count, 1), 0) + j * count
        return live(t, slots).astype(F32)

    row_count = R.tokens.shape[0]

    def placed(t, slots, rows, kept):
        source = t * (PATCHES + CAPTION) + slots - (slots >= VIS).astype(jnp.int32) * (VIS - PATCHES)
        return ((rows == source) & kept).astype(F32).astype(BF)

    def chooser(t, only_live):
        slots = lax.broadcasted_iota(jnp.int32, (SEQ, row_count), 0)
        rows = lax.broadcasted_iota(jnp.int32, (SEQ, row_count), 1)
        filled = (slots < PATCHES) | ((slots >= VIS) & (slots < VIS + CAPTION))
        return placed(t, slots, rows, live(t, slots) if only_live else filled)

    shard_part(ATT, attention_part)
    G[ATT, my_rows, :] = S[ATT, c]
    for t in range(2):
        R.lens[t] = jnp.full((8, 128), lengths[t], jnp.int32).astype(F32)
    pl.semaphore_wait(barrier, 5)
    shard_a = start(S.at[pl.ds(0, 1), other], G.at[pl.ds(0, 1), my_rows, :], mate)
    send_lens = start(R.lens, R.lens4.at[pl.ds(mine, 2)], mate)
    fetched[0].wait()
    for t in range(2):
        R.x4[2 * c + t] = mm(chooser(t, False), R.tokens[...]).astype(BF)
        R.lens4[2 * c + t] = R.lens[t]
    send_x = start(R.x4.at[pl.ds(mine, 2)], R.x4.at[pl.ds(mine, 2)], mate)
    shard_a.wait_recv()
    gather(near, 0)
    gather(far, 0)
    for copy in fetched[1:]:
        copy.wait()

    shard_part(TIN, functools.partial(half_of, R.txt_in))
    shard_part(TOUT, functools.partial(turned_half, R.txt_out))
    shard_part(VIN, functools.partial(half_of, R.vis_in))
    shard_part(VOUT, functools.partial(turned_half, R.vis_out))
    shard_b = start(S.at[pl.ds(1, 4), other], G.at[pl.ds(1, 4), my_rows, :], mate)
    for k in (TIN, TOUT, VIN, VOUT):
        G[k, my_rows, :] = S[k, c]
    gather(near, 1)
    for t in range(2):
        R.gz[2 * c + t] = mm(chooser(t, True), R.cotangent[...]).astype(BF)
        if t == 0:
            gather(far, 1)
    send_gz = start(R.gz.at[pl.ds(mine, 2)], R.gz.at[pl.ds(mine, 2)], mate)
    R.dy[...] = mm(chooser(x, False), R.cotangent[...]).astype(BF)
    for t in range(2):
        R.x[t] = R.x4[2 * c + t]
    shard_b.wait_recv()
    gather(tin, 0)
    gather(near, 2)
    send_x.wait_recv()

    for i in range(4):

        @pl.loop(0, SEQ // 64)
        def _(j, i=i):
            rows = pl.ds(pl.multiple_of(j * 64, 64), 64)
            normed, _ = normalize(R.x4[i, rows, :].astype(F32))
            R.n1[i, rows, :] = normed.astype(BF)

        R.n1t[:, i * SEQ : (i + 1) * SEQ] = R.n1[i].T
        if i == 0:
            gather(far, 2)
        if i == 1:
            gather(tout, 0)
            gather(near, 3)
        if i == 2:
            gather(far, 3)
            gather(vin, 0)
            gather(vout, 0)
    send_gz.wait_recv()
    send_lens.wait_recv()
    gather(near, 4)
    gather(far, 4)

    R.wo[...] = G[ATT][:, 3 * span :]

    @pl.loop(0, 4)
    def _(i):
        projected = mm(R.n1[i], G[ATT][:, : 3 * span]).astype(BF)
        R.q[i] = projected[:, :span]
        R.k[i] = projected[:, span : 2 * span]
        R.v[i] = projected[:, 2 * span :]

    lane = lax.broadcasted_iota(jnp.int32, (1, span), 1) // HEAD_DIM

    def only(head, values):
        return values * (lane == head).astype(F32).astype(BF)

    def head_rows(values, head):
        return values[head * HEAD_DIM : (head + 1) * HEAD_DIM, :]

    order = []
    for j in range(4):
        core = other if j < 2 else c
        turn = 1 - x if j % 2 == 0 else x
        order.append((turn, 2 * core + turn))
    attn_mate = [remote(R.pa.at[i], R.ra.at[turn], mate) for turn, i in order[:2]]
    cross_a = remote(R.xs, R.xr, across)

    for j, (turn, i) in enumerate(order):
        q, k, v = R.q[i], R.k[i], R.v[i]
        turned_v = v.T
        slots = lax.broadcasted_iota(jnp.int32, (SEQ, 1), 0)
        caption = (slots - VIS).astype(F32) < R.lens4[i][:1, :1]
        bias = jnp.where((slots < PATCHES) | ((slots >= VIS) & caption), 0.0, -1e30)
        contexts = []
        for h in range(heads):
            scores = mm_nt(only(h, k), q) + bias
            top = jnp.max(scores, axis=0, keepdims=True)
            weights = jnp.exp(scores - top)
            total = jnp.sum(weights, axis=0, keepdims=True)
            probs = (weights * (1.0 / total)).astype(BF)
            R.probs[i * heads + h] = probs
            contexts.append(mm(head_rows(turned_v, h), probs))
        contexts = jnp.concatenate(contexts, axis=0)
        R.ct[:, pl.ds(pl.multiple_of(i * SEQ, SEQ), SEQ)] = contexts.astype(BF)
        context = contexts.T.astype(BF)
        R.pa[i] = mm_nt(context, R.wo[...]).astype(BF)
        if j < 2:
            attn_mate[j].start()
        if j == 2:
            attn_mate[0].wait_recv()
            R.xs[...] = (R.pa[pair_across].astype(F32) + R.ra[1 - x].astype(F32)).astype(BF)
            cross_a.start()
        if j == 0:
            gather(tin, 1)
        if j == 1:
            gather(tout, 1)
        if j == 3:
            gather(tin, 2)
            gather(tout, 2)

    for copy in attn_mate:
        copy.wait_send()
    attn_mate[1].wait_recv()

    @pl.loop(0, width // 256)
    def _(j):
        cols = pl.ds(pl.multiple_of(j * 256, 256), 256)
        R.gzvt[cols, :] = R.gz[:, :VIS, cols].reshape(4 * VIS, 256).T
        R.gztt[cols, :] = R.gz[:, VIS:, cols].reshape(4 * TXT, 256).T

    gather(vin, 1)
    cross_a.wait_recv()

    @pl.loop(0, SEQ // 64)
    def _(j):
        rows = pl.ds(pl.multiple_of(j * 64, 64), 64)
        attended = (
            R.pa[pair_own, rows, :].astype(F32)
            + R.ra[x, rows, :].astype(F32)
            + R.xr[rows, :].astype(F32)
        )
        middle = R.x[x, rows, :].astype(F32) + live_rows(x, j) * attended
        R.y1[rows, :] = middle
        normed, _ = normalize(middle)
        R.n2[pair_own, rows, :] = normed.astype(BF)

    block = R.n2.at[pair_own]
    to_across = start(block, block, across)
    to_mate = start(block, block, mate)
    gather(vout, 1)
    gather(tin, 3)
    gather(tout, 3)
    to_across.wait_recv()
    block = R.n2.at[pair_across]
    passed = start(block, block, mate)
    gather(vin, 2)
    gather(vout, 2)
    gather(tin, 4)
    gather(tout, 4)
    to_mate.wait_recv()
    passed.wait_recv()

    def expert(pairs, low, high, w_in, w_out, h_ref, gu_ref, j):
        first, count = pairs
        per = high - low
        total_rows = count * per
        cols = pl.ds(pl.multiple_of(j * 256, 256), 256)
        inside = slice(first, first + count)
        R.u[:total_rows, :] = mm(
            R.n2[inside, low:high, :].reshape(total_rows, width), G[w_in, :, cols]
        )
        R.gh[:total_rows, :] = mm(
            R.gz[inside, low:high, :].reshape(total_rows, width), G[w_out, :, cols]
        )
        step = min(total_rows, VIS)

        @pl.loop(0, 2 * (total_rows // step))
        def _(i):
            lanes = lax.rem(i, 2) * 128
            rows = pl.ds(pl.multiple_of(i // 2 * step, 16), step)
            into = pl.ds(pl.multiple_of(first * per + i // 2 * step, 16), step)
            side = pl.ds(pl.multiple_of(lanes, 128), 128)
            pre = R.u[rows, side]
            cumulative = 0.5 * (1.0 + lax.erf(pre * inv_root_two))
            density = jnp.exp(-0.5 * pre * pre) * inv_root_tau
            onto = pl.ds(pl.multiple_of(j * 256 + lanes, 128), 128)
            h_ref[into, onto] = (pre * cumulative).astype(BF)
            gu_ref[into, onto] = (R.gh[rows, side] * (cumulative + pre * density)).astype(BF)

    def weight_grad(k, turned, ref):
        @pl.loop(0, width // 256)
        def _(j):
            cols = pl.ds(pl.multiple_of(j * 256, 256), 256)
            PART[k, :, cols] = mm(turned[...], ref[:, cols]).astype(BF)

    tiles = width // 256

    @pl.loop(0, tiles)
    def _(j):
        expert((0, 4), VIS, SEQ, TIN, TOUT, R.ht, R.gut, j)

    gather(vin, 3)
    weight_grad(TOUT, R.gztt, R.ht)

    @pl.loop(0, width // 256)
    def _(j):
        cols = pl.ds(pl.multiple_of(j * 256, 256), 256)
        R.n2vt[cols, :] = R.n2[:, :VIS, cols].reshape(4 * VIS, 256).T
        R.n2tt[cols, :] = R.n2[:, VIS:, cols].reshape(4 * TXT, 256).T

    gather(vout, 3)
    weight_grad(TIN, R.n2tt, R.gut)
    pass_sum(tout, 0)
    pass_sum(tin, 0)

    def text_terms(target, rows, weight):
        target[:, VIS:, :] = mm_nt(rows, G[weight]).astype(BF).reshape(4, TXT, width)

    text_terms(R.pg, R.gut[...], TIN)
    text_terms(R.pf, R.ht[...], TOUT)
    gather(vin, 4)
    gather(vout, 4)

    def terms(target, rows, weight, m):
        part = mm_nt(rows[2 * m * VIS : 2 * (m + 1) * VIS, :], G[weight]).astype(BF)
        target[2 * m : 2 * m + 2, :VIS, :] = part.reshape(2, VIS, width)

    mate_g = remote(R.pg.at[pl.ds(theirs, 2)], R.rg, mate)
    cross_g = remote(R.xsg, R.xrg, across)
    gy_across = remote(R.gy.at[x], R.gy.at[x], across)
    gy_mate = remote(R.ga.at[pair_own], R.ga.at[pair_own], mate)
    gy_passed = remote(R.ga.at[pair_across], R.ga.at[pair_across], mate)
    started.extend([cross_g, gy_across, gy_mate, gy_passed])

    def image_terms(m):
        terms(R.pg, R.guv, VIN, m)
        pl.when(c != m)(mate_g.start)

    def sum_cores(m):
        @pl.when(c == m)
        def _():
            mate_g.wait_recv()
            R.xsg[...] = (R.pg[pair_across].astype(F32) + R.rg[1 - x].astype(F32)).astype(BF)
            cross_g.start()

    def middle_back(m):
        @pl.when(c == m)
        def _():
            cross_g.wait_recv()

            @pl.loop(0, SEQ // 64)
            def _(j):
                rows = pl.ds(pl.multiple_of(j * 64, 64), 64)
                grad_normed = (
                    R.pg[pair_own, rows, :].astype(F32)
                    + R.rg[x, rows, :].astype(F32)
                    + R.xrg[rows, :].astype(F32)
                )
                normed, inverse = normalize(R.y1[rows, :])
                grad = R.dy[rows, :].astype(F32) + normalize_back(grad_normed, normed, inverse)
                R.gy[x, rows, :] = grad.astype(BF)
                R.ga[pair_own, rows, :] = (grad * live_rows(x, j)).astype(BF)

            gy_across.start()
            gy_mate.start()

    def middle_pass(m):
        @pl.when(c == m)
        def _():
            gy_across.wait_recv()

            @pl.loop(0, SEQ // 64)
            def _(j):
                rows = pl.ds(pl.multiple_of(j * 64, 64), 64)
                R.ga[pair_across, rows, :] = (
                    R.gy[1 - x, rows, :].astype(F32) * live_rows(1 - x, j)
                ).astype(BF)

            gy_passed.start()

    def middle_came(m):
        @pl.when(c != m)
        def _():
            gy_mate.wait_recv()
            gy_passed.wait_recv()

    sent(send_x)
    cross_a.wait_send()

    @pl.loop(0, tiles)
    def _(j):
        expert((0, 2), 0, VIS, VIN, VOUT, R.hv, R.guv, j)

    image_terms(0)

    @pl.loop(0, tiles)
    def _(j):
        expert((2, 2), 0, VIS, VIN, VOUT, R.hv, R.guv, j)
        pl.when(j == 0)(functools.partial(sum_cores, 0))

    pass_sum(tout, 1)
    image_terms(1)
    for copy in (to_across, to_mate, passed):
        sent(copy)
    sum_cores(1)
    pass_sum(tin, 1)
    weight_grad(VOUT, R.gzvt, R.hv)
    middle_back(0)
    pass_sum(vout, 0)
    pass_sum(tout, 2)
    weight_grad(VIN, R.n2vt, R.guv)
    pass_sum(vin, 0)
    pass_sum(tin, 2)

    terms(R.pf, R.hv, VOUT, 0)
    middle_pass(0)
    middle_back(1)
    pass_sum(tout, 3)
    terms(R.pf, R.hv, VOUT, 1)
    mate_f = start(R.pf.at[pl.ds(theirs, 2)], R.rf, mate)
    cross_f = remote(R.xsf, R.xrf, across)
    started.append(cross_f)
    pass_sum(tin, 3)
    mate_g.wait_send()
    middle_came(0)

    back_mate = [remote(R.pb.at[theirs + t], R.rb.at[t], mate) for t in range(2)]
    back_cross = [remote(R.xsb.at[t], R.xrb.at[t], across) for t in range(2)]
    started.extend(back_mate + back_cross)

    def attention_back(m):
        pairs = [2 * m, 2 * m + 1]
        grad_contexts = [mm(R.ga[i], R.wo[...]).astype(BF) for i in pairs]
        turned_k = [R.k[i].T for i in pairs]
        grad_q = [[], []]
        grad_k = [jnp.zeros((SEQ, span), F32) for _ in pairs]
        grad_v = [jnp.zeros((SEQ, span), F32) for _ in pairs]
        for h in range(heads):
            for t, i in enumerate(pairs):
                probs = R.probs[i * heads + h]
                grad_probs = mm_nt(only(h, R.v[i]), grad_contexts[t])
                exact = probs.astype(F32)
                inner = jnp.sum(grad_probs * exact, axis=0, keepdims=True)
                grad_scores = (exact * (grad_probs - inner)).astype(BF)
                grad_q[t].append(mm(head_rows(turned_k[t], h), grad_scores))
                grad_k[t] += mm(grad_scores, only(h, R.q[i]))
                grad_v[t] += mm(probs, only(h, grad_contexts[t]))
        for t, i in enumerate(pairs):
            turned_q = jnp.concatenate(grad_q[t], axis=0).T
            joined = jnp.concatenate([turned_q, grad_k[t], grad_v[t]], axis=1).astype(BF)
            R.gqkv[i, :, : 3 * span] = joined
            R.pb[i] = mm_nt(joined, G[ATT][:, : 3 * span]).astype(BF)
            pl.when(c != m)(back_mate[t].start)

    def back_sum(m, t):
        @pl.when(c == m)
        def _():
            back_mate[t].wait_recv()
            R.xsb[t] = (R.pb[2 * m + t].astype(F32) + R.rb[t].astype(F32)).astype(BF)
            back_cross[t].start()

    mate_f.wait_recv()
    R.xsf[...] = (R.pf[pair_across].astype(F32) + R.rf[1 - x].astype(F32)).astype(BF)
    R.fown[...] = (R.pf[pair_own].astype(F32) + R.rf[x].astype(F32)).astype(BF)
    attention_back(0)
    middle_pass(1)
    cross_f.start()
    pass_sum(vout, 1)
    back_sum(0, 0)
    back_sum(0, 1)
    pass_sum(vin, 1)
    middle_came(1)
    attention_back(1)
    pass_sum(vout, 2)
    pass_sum(vin, 2)
    back_sum(1, 0)

    lanes = width // 2

    @pl.loop(0, width // 256)
    def _(j):
        rows = pl.ds(pl.multiple_of(j * 256, 256), 256)
        grad_v = mm(R.n1t[rows, :], R.gqkv[:, :, lanes : 3 * span].reshape(4 * SEQ, span))
        grad_o = mm(R.ct[...], R.ga[:, :, rows].reshape(4 * SEQ, 256)).T
        PART[ATT, rows, lanes:] = jnp.concatenate([grad_v, grad_o], axis=1).astype(BF)

    pass_sum(far, 0)

    cross_f.wait_recv()

    @pl.loop(0, SEQ // 64)
    def _(j):
        rows = pl.ds(pl.multiple_of(j * 64, 64), 64)
        branch = R.fown[rows, :].astype(F32) + R.xrf[rows, :].astype(F32)
        OUT[x, rows, :] = (R.y1[rows, :] + live_rows(x, j) * branch).astype(BF)

    out_across = start(OUT.at[x], OUT.at[x], across)

    @pl.loop(0, width // 256)
    def _(j):
        rows = pl.ds(pl.multiple_of(j * 256, 256), 256)
        grads = mm(R.n1t[rows, :], R.gqkv[:, :, :lanes].reshape(4 * SEQ, lanes))
        PART[ATT, rows, :lanes] = grads.astype(BF)

    pass_sum(near, 0)
    back_sum(1, 1)
    pass_sum(vout, 3)
    pass_sum(vin, 3)

    def input_back(m, t):
        @pl.when(c == m)
        def _():
            back_cross[t].wait_recv()

            @pl.loop(0, SEQ // 64)
            def _(j):
                rows = pl.ds(pl.multiple_of(j * 64, 64), 64)
                grad_normed = R.xsb[t, rows, :].astype(F32) + R.xrb[t, rows, :].astype(F32)
                normed, inverse = normalize(R.x[t, rows, :].astype(F32))
                grad = R.gy[t, rows, :].astype(F32) + normalize_back(grad_normed, normed, inverse)
                high = grad.astype(BF)
                rows = pl.ds(pl.multiple_of(t * SEQ + j * 64, 64), 64)
                R.hv[rows, :] = high
                R.guv[rows, :] = (grad - high.astype(F32)).astype(BF)

    pass_sum(far, 1)
    input_back(0, 0)
    pass_sum(near, 1)
    input_back(0, 1)
    end_sum(tout, tin)
    pass_sum(far, 2)
    pass_sum(near, 2)
    end_sum(vout, vin)

    leaving = []

    def leave(slot, source, target):
        leaving.append(fetch(slot, source, target))

    slots = lax.broadcasted_iota(jnp.int32, (row_count, 2 * SEQ), 1)
    rows = lax.broadcasted_iota(jnp.int32, (row_count, 2 * SEQ), 0)
    turn = slots // SEQ
    back = placed(turn, slots - turn * SEQ, rows, slots >= 0)
    out_across.wait_recv()
    R.out_tokens[...] = mm(back, OUT[...].reshape(2 * SEQ, width)).astype(BF)
    leave(6, R.out_tokens, R.out_tokens_hbm)
    for copy in finals:
        copy.wait_recv()
    finals.clear()
    leave(7, GW.at[pl.ds(1, 4)], R.gw_hbm.at[pl.ds(1, 4)])
    pass_sum(far, 3)
    pass_sum(near, 3)
    input_back(1, 0)
    input_back(1, 1)
    R.grad_tokens[...] = mm(back, R.hv[: 2 * SEQ, :]) + mm(back, R.guv[: 2 * SEQ, :])
    leave(8, R.grad_tokens, R.grad_tokens_hbm)
    end_sum(far, near)

    first_lane = lax.broadcasted_iota(jnp.int32, (own, 128), 1) == 0
    for place in range(2):
        attn = sum(total for k, total in row_sums[place] if k == ATT)
        experts = sum(total for k, total in row_sums[place] if k != ATT)
        R.gs[place] = jnp.where(first_lane, attn, experts)
    peers = [
        start(R.gs.at[place], R.gr.at[slot], device)
        for slot, (place, device) in enumerate(((1, mate), (0, across), (1, diagonal)))
    ]
    for copy in finals + peers:
        copy.wait_recv()
    leave(9, GW.at[pl.ds(0, 1)], R.gw_hbm.at[pl.ds(0, 1)])
    GG[...] = (R.gs[0] + R.gr[1]) + (R.gr[0] + R.gr[2])

    for copy in started:
        copy.wait_send()
    for copy in leaving:
        copy.wait()
    for k in range(5):
        for semaphore in (k, 5 + k):
            pltpu.make_async_remote_copy(
                src_ref=LAND.at[k],
                dst_ref=LAND.at[k],
                send_sem=R.ring_sent.at[semaphore],
                recv_sem=R.ring_came.at[0],
                device_id=ahead,
                device_id_type=MESH,
            ).wait_send()


def finish_kernel(n_results, out, gtok, gw_hbm, gg, gain_attn, gain_ffn, *rest):
    results, scratch = rest[:n_results], rest[n_results:]
    buffers, (out_buffer, gtok_buffer, gw, came, gone) = scratch[:n_results], scratch[n_results:]
    arriving = [
        pltpu.make_async_copy(source, target, came.at[slot])
        for slot, (source, target) in enumerate(((gw_hbm, gw), (out, out_buffer), (gtok, gtok_buffer)))
    ]
    for copy in arriving:
        copy.start()
    width = gw.shape[3]
    own = gw.shape[2]
    span = width // 4
    gain_one, gain_two = column(gain_attn), column(gain_ffn)
    square = unit(own).astype(F32)
    leaving = []

    def leave(slot, source):
        copy = pltpu.make_async_copy(source, results[slot], gone.at[slot])
        copy.start()
        leaving.append(copy)

    def both(part):
        cols = slice(part * span, (part + 1) * span)
        return jnp.concatenate([gw[ATT, core][:, cols] for core in range(2)], axis=1)

    def put(slot, value):
        buffers[slot][...] = value
        leave(slot, buffers[slot])

    put(2, jnp.sum(square * (gg[:, :1] / gain_one), axis=0, keepdims=True))
    put(7, jnp.sum(square * (gg[:, 1:2] / gain_two), axis=0, keepdims=True))
    arriving[0].wait()
    for slot, k, scale in ((8, VIN, gain_two), (9, VOUT, 1.0), (10, TIN, gain_two), (11, TOUT, 1.0)):
        put(slot, jnp.concatenate([gw[k, 0], gw[k, 1]], axis=1) * scale)
    put(3, both(0) * (gain_one * HEAD_DIM**-0.5))
    put(4, both(1) * gain_one)
    put(5, both(2) * gain_one)
    put(6, both(3))
    arriving[1].wait()
    leave(0, out_buffer)
    arriving[2].wait()
    leave(1, gtok_buffer)
    for copy in leaving:
        copy.wait()


def fused_layer(
    tokens,
    caption_lengths,
    gain_attn,
    w_query,
    w_key,
    w_value,
    w_out,
    gain_ffn,
    vis_in,
    vis_out,
    txt_in,
    txt_out,
    cotangent,
):
    n = lax.axis_size("dp") // 2
    own = w_query.shape[0]
    row_count, width = tokens.shape
    span = width // 4
    heads = span // HEAD_DIM
    gain_one, gain_two = gain_attn.reshape(1, own), gain_ffn.reshape(1, own)

    rows = 4 * SEQ
    scratch = dict(
        tokens=pltpu.VMEM((row_count, width), BF),
        cotangent=pltpu.VMEM((row_count, width), BF),
        txt_in=pltpu.VMEM((own, 2 * width), BF),
        txt_out=pltpu.VMEM((own, 2 * width), BF),
        vis_in=pltpu.VMEM((own, 2 * width), BF),
        vis_out=pltpu.VMEM((own, 2 * width), BF),
        out_tokens=pltpu.VMEM((row_count, width), BF),
        grad_tokens=pltpu.VMEM((row_count, width), F32),
        gw=pltpu.VMEM((5, 2, own, width), F32),
        local=pltpu.SemaphoreType.DMA((10,)),
        shard=pltpu.VMEM((5, 2, own, width), BF),
        lens=pltpu.VMEM((2, 8, 128), F32),
        x=pltpu.VMEM((2, SEQ, width), BF),
        dy=pltpu.VMEM((SEQ, width), BF),
        padded_out=pltpu.VMEM((2, SEQ, width), BF),
        gathered=pltpu.VMEM((5, width, width), BF),
        part=pltpu.VMEM((5, width, width), BF),
        land=pltpu.VMEM((5, n - 1, 2 * own, width), BF),
        give=pltpu.VMEM((5, own, width), F32),
        x4=pltpu.VMEM((4, SEQ, width), BF),
        lens4=pltpu.VMEM((4, 8, 128), F32),
        n1=pltpu.VMEM((4, SEQ, width), BF),
        n1t=pltpu.VMEM((width, rows), BF),
        gz=pltpu.VMEM((4, SEQ, width), BF),
        gzvt=pltpu.VMEM((width, 4 * VIS), BF),
        ct=pltpu.VMEM((span, rows), BF),
        fown=pltpu.VMEM((SEQ, width), BF),
        gztt=pltpu.VMEM((width, 4 * TXT), BF),
        wo=pltpu.VMEM((width, span), BF),
        q=pltpu.VMEM((4, SEQ, span), BF),
        k=pltpu.VMEM((4, SEQ, span), BF),
        v=pltpu.VMEM((4, SEQ, span), BF),
        probs=pltpu.VMEM((4 * heads, SEQ, SEQ), BF),
        pa=pltpu.VMEM((4, SEQ, width), BF),
        ra=pltpu.VMEM((2, SEQ, width), BF),
        xs=pltpu.VMEM((SEQ, width), BF),
        xr=pltpu.VMEM((SEQ, width), BF),
        y1=pltpu.VMEM((SEQ, width), F32),
        n2vt=pltpu.VMEM((width, 4 * VIS), BF),
        n2tt=pltpu.VMEM((width, 4 * TXT), BF),
        u=pltpu.VMEM((4 * VIS, 256), F32),
        gh=pltpu.VMEM((4 * VIS, 256), F32),
        hv=pltpu.VMEM((4 * VIS, width), BF),
        guv=pltpu.VMEM((4 * VIS, width), BF),
        ht=pltpu.VMEM((4 * TXT, width), BF),
        gut=pltpu.VMEM((4 * TXT, width), BF),
        pg=pltpu.VMEM((4, SEQ, width), BF),
        rg=pltpu.VMEM((2, SEQ, width), BF),
        gy=pltpu.VMEM((2, SEQ, width), BF),
        xsf=pltpu.VMEM((SEQ, width), BF),
        xrf=pltpu.VMEM((SEQ, width), BF),
        xsb=pltpu.VMEM((2, SEQ, width), BF),
        xrb=pltpu.VMEM((2, SEQ, width), BF),
        gs=pltpu.VMEM((2, own, 128), F32),
        gr=pltpu.VMEM((3, own, 128), F32),
        sent=pltpu.SemaphoreType.DMA((40,)),
        came=pltpu.SemaphoreType.DMA((40,)),
        ring_sent=pltpu.SemaphoreType.DMA((10,)),
        ring_came=pltpu.SemaphoreType.DMA((6 * 2 * (n // 2) * 2,)),
    )
    inputs = dict(
        lengths=caption_lengths,
        tokens_hbm=tokens,
        cotangent_hbm=cotangent,
        gain_attn=gain_one,
        gain_ffn=gain_two,
        w_query=w_query,
        w_key=w_key,
        w_value=w_value,
        w_out=w_out.T,
        vis_in_hbm=vis_in,
        vis_out_hbm=vis_out.T,
        txt_in_hbm=txt_in,
        txt_out_hbm=txt_out.T,
    )
    results = dict(
        out_tokens_hbm=jax.ShapeDtypeStruct((row_count, width), BF),
        grad_tokens_hbm=jax.ShapeDtypeStruct((row_count, width), F32),
        gw_hbm=jax.ShapeDtypeStruct((5, 2, own, width), F32),
        gg=jax.ShapeDtypeStruct((own, 128), F32),
    )
    vmem, hbm = pl.BlockSpec(memory_space=pltpu.VMEM), pl.BlockSpec(memory_space=pl.ANY)
    names = tuple(inputs) + tuple(results) + tuple(scratch)
    out, gtok, gw, gg = pl.pallas_call(
        functools.partial(layer_kernel, n, names),
        out_shape=tuple(results.values()),
        in_specs=[pl.BlockSpec(memory_space=pltpu.SMEM)] + [hbm if k.endswith(HBM) else vmem for k in names[1 : len(inputs)]],
        out_specs=[hbm if k.endswith(HBM) else vmem for k in results],
        scratch_shapes=list(scratch.values()),
        compiler_params=pltpu.CompilerParams(
            collective_id=0, has_side_effects=True, vmem_limit_bytes=60 * 2**20
        ),
    )(*inputs.values())

    shapes = (
        jax.ShapeDtypeStruct((row_count, width), BF),
        jax.ShapeDtypeStruct((row_count, width), F32),
        jax.ShapeDtypeStruct((1, own), F32),
        jax.ShapeDtypeStruct((own, 2 * span), F32),
        jax.ShapeDtypeStruct((own, 2 * span), F32),
        jax.ShapeDtypeStruct((own, 2 * span), F32),
        jax.ShapeDtypeStruct((own, 2 * span), F32),
        jax.ShapeDtypeStruct((1, own), F32),
        jax.ShapeDtypeStruct((own, 2 * width), F32),
        jax.ShapeDtypeStruct((own, 2 * width), F32),
        jax.ShapeDtypeStruct((own, 2 * width), F32),
        jax.ShapeDtypeStruct((own, 2 * width), F32),
    )
    buffers = [pltpu.VMEM(one.shape if slot > 1 else (8, 128), F32) for slot, one in enumerate(shapes)]
    final = pl.pallas_call(
        functools.partial(finish_kernel, len(shapes)),
        out_shape=shapes,
        in_specs=[hbm] * 3 + [vmem] * 3,
        out_specs=[hbm] * len(shapes),
        scratch_shapes=buffers
        + [
            pltpu.VMEM((row_count, width), BF),
            pltpu.VMEM((row_count, width), F32),
            pltpu.VMEM((5, 2, own, width), F32),
            pltpu.SemaphoreType.DMA((3,)),
            pltpu.SemaphoreType.DMA((len(shapes),)),
        ],
        compiler_params=pltpu.CompilerParams(vmem_limit_bytes=60 * 2**20),
    )(out, gtok, gw, gg, gain_one, gain_two)
    final = list(final)
    final[2] = final[2].reshape(own)
    final[7] = final[7].reshape(own)
    for turned in (6, 9, 11):
        final[turned] = final[turned].T
    return tuple(final)


def norm_parts(values):
    center = values - jnp.mean(values, axis=-1, keepdims=True)
    spread = jnp.mean(center * center, axis=-1, keepdims=True)
    inverse = lax.rsqrt(spread + epsilon)
    return (center * inverse, inverse)


def norm_back(grad_out, normed, inverse, gain):
    grad_normed = grad_out * gain
    grad_gain = jnp.sum(grad_out * normed, axis=0)
    inner = (
        grad_normed
        - jnp.mean(grad_normed, axis=-1, keepdims=True)
        - normed * jnp.mean(grad_normed * normed, axis=-1, keepdims=True)
    )
    return (inverse * inner, grad_gain)


def matmul(left, right):
    return jnp.dot(left, right, preferred_element_type=jnp.float32)


def matmul_tn(left, right):
    return lax.dot_general(
        left, right, (((0,), (0,)), ((), ())), preferred_element_type=jnp.float32
    )


def matmul_nt(left, right):
    return lax.dot_general(
        left, right, (((1,), (1,)), ((), ())), preferred_element_type=jnp.float32
    )


def gelu_slope(pre):
    cumulative = 0.5 * (1.0 + lax.erf(pre * inv_root_two))
    density = jnp.exp(-0.5 * pre * pre) * inv_root_tau
    return cumulative + pre * density


def expert_forward(rows, weight_in, weight_out):
    pre = matmul(rows, weight_in)
    hidden = jax.nn.gelu(pre, approximate=False).astype(jnp.bfloat16)
    return (pre, hidden, matmul(hidden, weight_out))


def expert_backward(rows, pre, hidden, grad_out, weight_in, weight_out):
    grad_weight_out = matmul_tn(hidden, grad_out)
    grad_hidden = matmul_nt(grad_out, weight_out)
    grad_pre = (grad_hidden * gelu_slope(pre)).astype(jnp.bfloat16)
    return (matmul_tn(rows, grad_pre), grad_weight_out, matmul_nt(grad_pre, weight_in))


def join_experts(image_rows, text_rows, pair_count, width):
    joined = jnp.concatenate(
        [
            image_rows.reshape(pair_count, PATCHES, width),
            text_rows.reshape(pair_count, CAPTION, width),
        ],
        axis=1,
    )
    return joined.reshape(-1, width)


def plain_layer(
    tokens,
    caption_lengths,
    gain_attn,
    w_query,
    w_key,
    w_value,
    w_out,
    gain_ffn,
    vis_in,
    vis_out,
    txt_in,
    txt_out,
    cotangent,
):
    seq_len = PATCHES + CAPTION
    width = tokens.shape[1]
    pair_count = tokens.shape[0] // seq_len
    half_pairs = pair_count // lax.axis_size("tensor")
    half_rows = half_pairs * seq_len
    row_start = lax.axis_index("tensor") * half_rows
    gain_one, query_w, key_w, value_w, out_w = (
        lax.all_gather(gain_attn, "dp", axis=0, tiled=True),
        lax.all_gather(w_query, "dp", axis=0, tiled=True),
        lax.all_gather(w_key, "dp", axis=0, tiled=True),
        lax.all_gather(w_value, "dp", axis=0, tiled=True),
        lax.all_gather(w_out, "dp", axis=1, tiled=True),
    )
    gain_two, vis_in_w, vis_out_w, txt_in_w, txt_out_w = (
        lax.all_gather(gain_ffn, "dp", axis=0, tiled=True),
        lax.all_gather(vis_in, "dp", axis=0, tiled=True),
        lax.all_gather(vis_out, "dp", axis=1, tiled=True),
        lax.all_gather(txt_in, "dp", axis=0, tiled=True),
        lax.all_gather(txt_out, "dp", axis=1, tiled=True),
    )
    gain_one = gain_one.astype(jnp.float32)
    gain_two = gain_two.astype(jnp.float32)
    head_local = query_w.shape[1] // HEAD_DIM
    score_scale = HEAD_DIM ** (-0.5)
    position = jnp.arange(seq_len, dtype=jnp.int32)
    live = (position[None, :] < PATCHES) | (position[None, :] - PATCHES < caption_lengths[:, None])
    valid_rows = live.astype(jnp.float32)
    mask_col = valid_rows.reshape(-1, 1)
    key_live = valid_rows[:, None, None, :] > 0.5

    def own_rows(values):
        return lax.dynamic_slice_in_dim(values, row_start, half_rows, 0)

    inputs = tokens.astype(jnp.float32)
    normed_one, inverse_one = norm_parts(inputs)
    first_in = (normed_one * gain_one).astype(jnp.bfloat16)

    def project(weight):
        return (
            matmul(first_in, weight)
            .astype(jnp.bfloat16)
            .reshape(pair_count, seq_len, head_local, HEAD_DIM)
        )

    queries = project(query_w)
    keys_all = project(key_w)
    values_all = project(value_w)

    def score_block():
        raw = (
            jnp.einsum("pqhe,pkhe->phqk", queries, keys_all, preferred_element_type=jnp.float32)
            * score_scale
        )
        return jnp.where(key_live, raw, -1e30)

    scores = score_block()
    top = jnp.max(scores, axis=-1, keepdims=True)
    weights = jnp.exp(scores - top)
    total = jnp.sum(weights, axis=-1, keepdims=True)
    probs = (weights / total).astype(jnp.bfloat16)
    log_total = top + jnp.log(total)
    context = jnp.einsum("phqk,pkhe->pqhe", probs, values_all, preferred_element_type=jnp.float32)
    context = context.astype(jnp.bfloat16).reshape(-1, head_local * HEAD_DIM)
    attn_terms = matmul(context, out_w)
    attended_own = lax.psum_scatter(
        attn_terms.astype(jnp.bfloat16), "tensor", scatter_dimension=0, tiled=True
    ).astype(jnp.float32)
    mask_own = own_rows(mask_col)
    middle_own = own_rows(inputs) + mask_own * attended_own
    normed_two, inverse_two = norm_parts(middle_own)
    second_own = (normed_two * gain_two).astype(jnp.bfloat16)
    grid = lax.all_gather(second_own, "tensor", axis=0, tiled=True).reshape(
        pair_count, seq_len, width
    )
    image_rows = grid[:, :PATCHES].reshape(-1, width)
    text_rows = grid[:, PATCHES:].reshape(-1, width)
    image_pre, image_hidden, image_part = expert_forward(image_rows, vis_in_w, vis_out_w)
    text_pre, text_hidden, text_part = expert_forward(text_rows, txt_in_w, txt_out_w)
    image_own, text_own = (
        lax.psum_scatter(
            image_part.astype(jnp.bfloat16), "tensor", scatter_dimension=0, tiled=True
        ).astype(jnp.float32),
        lax.psum_scatter(
            text_part.astype(jnp.bfloat16), "tensor", scatter_dimension=0, tiled=True
        ).astype(jnp.float32),
    )
    branch_own = join_experts(image_own, text_own, half_pairs, width)
    output_own = (middle_own + mask_own * branch_own).astype(jnp.bfloat16)
    upstream = cotangent.astype(jnp.float32)
    grad_branch = (upstream * mask_col).astype(jnp.bfloat16).reshape(pair_count, seq_len, width)
    image_grads = expert_backward(
        image_rows,
        image_pre,
        image_hidden,
        grad_branch[:, :PATCHES].reshape(-1, width),
        vis_in_w,
        vis_out_w,
    )
    text_grads = expert_backward(
        text_rows,
        text_pre,
        text_hidden,
        grad_branch[:, PATCHES:].reshape(-1, width),
        txt_in_w,
        txt_out_w,
    )
    back_image_own, back_text_own = (
        lax.psum_scatter(
            image_grads[2].astype(jnp.bfloat16), "tensor", scatter_dimension=0, tiled=True
        ).astype(jnp.float32),
        lax.psum_scatter(
            text_grads[2].astype(jnp.bfloat16), "tensor", scatter_dimension=0, tiled=True
        ).astype(jnp.float32),
    )
    grad_second_own = join_experts(back_image_own, back_text_own, half_pairs, width)
    grad_norm_own, gain_part = norm_back(grad_second_own, normed_two, inverse_two, gain_two)
    grad_middle_own = own_rows(upstream) + grad_norm_own
    output_wide, grad_middle, gain_parts = (
        lax.all_gather(
            output_own.astype(jnp.float32).astype(jnp.bfloat16), "tensor", axis=0, tiled=True
        ).astype(jnp.float32),
        lax.all_gather(grad_middle_own.astype(jnp.bfloat16), "tensor", axis=0, tiled=True).astype(
            grad_middle_own.dtype
        ),
        lax.all_gather(gain_part.astype(jnp.bfloat16), "tensor", axis=0, tiled=True).astype(
            gain_part.dtype
        ),
    )
    output = output_wide.astype(jnp.bfloat16)
    grad_gain_two = jnp.sum(gain_parts.reshape(-1, width), axis=0)
    grad_attended = (grad_middle * mask_col).astype(jnp.bfloat16)
    grad_out_w = matmul_tn(context, grad_attended)
    grad_context = (
        matmul_nt(grad_attended, out_w)
        .astype(jnp.bfloat16)
        .reshape(pair_count, seq_len, head_local, HEAD_DIM)
    )
    scores_again = score_block()
    probs_exact = jnp.exp(scores_again - log_total)
    grad_probs = jnp.einsum(
        "pqhe,pkhe->phqk", grad_context, values_all, preferred_element_type=jnp.float32
    )
    inner = jnp.sum(grad_probs * probs_exact, axis=-1, keepdims=True)
    grad_scores = (probs_exact * (grad_probs - inner)).astype(jnp.bfloat16)
    grad_values = jnp.einsum(
        "phqk,pqhe->pkhe", probs, grad_context, preferred_element_type=jnp.float32
    )
    grad_values = grad_values.astype(jnp.bfloat16).reshape(-1, head_local * HEAD_DIM)
    grad_queries = (
        jnp.einsum("phqk,pkhe->pqhe", grad_scores, keys_all, preferred_element_type=jnp.float32)
        * score_scale
    )
    grad_queries = grad_queries.astype(jnp.bfloat16).reshape(-1, head_local * HEAD_DIM)
    grad_keys = (
        jnp.einsum("phqk,pqhe->pkhe", grad_scores, queries, preferred_element_type=jnp.float32)
        * score_scale
    )
    grad_keys = grad_keys.astype(jnp.bfloat16).reshape(-1, head_local * HEAD_DIM)
    grad_query_w = matmul_tn(first_in, grad_queries)
    grad_key_w = matmul_tn(first_in, grad_keys)
    grad_value_w = matmul_tn(first_in, grad_values)
    first_part = (
        matmul_nt(grad_queries, query_w)
        + matmul_nt(grad_keys, key_w)
        + matmul_nt(grad_values, value_w)
    )
    grad_first = lax.psum(first_part.astype(jnp.bfloat16), "tensor").astype(jnp.float32)
    grad_norm_one, grad_gain_one = norm_back(grad_first, normed_one, inverse_one, gain_one)
    grad_inputs = grad_middle + grad_norm_one
    attn_sent = (
        lax.psum_scatter(grad_gain_one, "dp", scatter_dimension=0, tiled=True),
        lax.psum_scatter(grad_query_w, "dp", scatter_dimension=0, tiled=True),
        lax.psum_scatter(grad_key_w, "dp", scatter_dimension=0, tiled=True),
        lax.psum_scatter(grad_value_w, "dp", scatter_dimension=0, tiled=True),
        lax.psum_scatter(grad_out_w, "dp", scatter_dimension=1, tiled=True),
    )
    final_expert = (
        lax.psum_scatter(grad_gain_two, "dp", scatter_dimension=0, tiled=True),
        lax.psum_scatter(image_grads[0], "dp", scatter_dimension=0, tiled=True),
        lax.psum_scatter(image_grads[1], "dp", scatter_dimension=1, tiled=True),
        lax.psum_scatter(text_grads[0], "dp", scatter_dimension=0, tiled=True),
        lax.psum_scatter(text_grads[1], "dp", scatter_dimension=1, tiled=True),
    )
    return (
        output,
        grad_inputs,
        attn_sent[0],
        attn_sent[1],
        attn_sent[2],
        attn_sent[3],
        attn_sent[4],
        final_expert[0],
        final_expert[1],
        final_expert[2],
        final_expert[3],
        final_expert[4],
    )


def solution(mesh):
    def local(tokens, lengths, gain, w_query, *rest):
        ring = mesh.shape["dp"] // 2
        fits = (
            mesh.shape["tensor"] == 2
            and ring == 8
            and lengths.shape[0] == 2
            and w_query.shape[0] % 16 == 0
        )
        layer = fused_layer if fits else plain_layer
        return layer(tokens, lengths, gain, w_query, *rest)

    return jax.shard_map(
        local,
        mesh=mesh,
        in_specs=(
            P("dp", None),
            P("dp"),
            P("dp"),
            P("dp", "tensor"),
            P("dp", "tensor"),
            P("dp", "tensor"),
            P("tensor", "dp"),
            P("dp"),
            P("dp", "tensor"),
            P("tensor", "dp"),
            P("dp", "tensor"),
            P("tensor", "dp"),
            P("dp", None),
        ),
        out_specs=(
            P("dp", None),
            P("dp", None),
            P("dp"),
            P("dp", "tensor"),
            P("dp", "tensor"),
            P("dp", "tensor"),
            P("tensor", "dp"),
            P("dp"),
            P("dp", "tensor"),
            P("tensor", "dp"),
            P("dp", "tensor"),
            P("tensor", "dp"),
        ),
        check_vma=False,
    )
```
